32 devices in a mesh: fsdp: 4 (over z), ctx: 4 (over y, x), tp: 2 (over core).
Axes of the slice: x: 2, y: 2, z: 4, core: 2. Of those that a mesh axis runs over, the one named last changes fastest.
Arguments:
- tokens: bfloat16 [4, 1024, 2048], P('fsdp', 'ctx'), may hold values from -6 to 6
- w_query: bfloat16 [2048, 2048], P('fsdp', 'tp'), may hold values from -0.125 to 0.125
- w_key: bfloat16 [2048, 2048], P('fsdp', 'tp'), may hold values from -0.125 to 0.125
- w_value: bfloat16 [2048, 2048], P('fsdp', 'tp'), may hold values from -0.125 to 0.125
- w_out: bfloat16 [2048, 2048], P('tp', 'fsdp'), may hold values from -4 to 4
- gain_attn: bfloat16 [2048], P('fsdp'), may hold values from 0.5 to 1.5
- gain_query: bfloat16 [128], P('fsdp'), may hold values from 0.5 to 1.5
- gain_key: bfloat16 [128], P('fsdp'), may hold values from 0.5 to 1.5
- gain_moe: bfloat16 [2048], P('fsdp'), may hold values from 0.5 to 1.5
- w_router: bfloat16 [2048, 16], P('fsdp'), may hold values from -0.125 to 0.125
- w_experts: bfloat16 [2048, 3, 16, 1024], P('fsdp', None, None, 'tp')
- routes: int32 [4, 1024, 8], P('fsdp', 'ctx'), may hold values from 0 to 15, all different within a row; in each aligned block of 256 rows (0 to 255, 256 to 511, ..., all dimensions but the last counted through in order) at most 144 rows name the same one
- cotangent: bfloat16 [4, 1024, 2048], P('fsdp', 'ctx'), may hold values from -6 to 6
Outputs:
- layer_out: bfloat16 [4, 1024, 2048], P('fsdp', 'ctx', 'tp')
- tokens_grad: bfloat16 [4, 1024, 2048], P('fsdp', 'ctx')
- dw_query: float32 [2048, 2048], P(('fsdp', 'ctx'), 'tp')
- dw_key: float32 [2048, 2048], P(('fsdp', 'ctx'), 'tp')
- dw_value: float32 [2048, 2048], P(('fsdp', 'ctx'), 'tp')
- dw_out: float32 [2048, 2048], P('tp', ('fsdp', 'ctx'))
- dgain_attn: float32 [2048], P(('fsdp', 'ctx'))
- dgain_query: float32 [128], P(('fsdp', 'ctx'))
- dgain_key: float32 [128], P(('fsdp', 'ctx'))
- dgain_moe: float32 [2048], P(('fsdp', 'ctx'))
- dw_router: float32 [2048, 16], P(('fsdp', 'ctx'))
- dw_experts: float32 [2048, 3, 16, 1024], P(('fsdp', 'ctx'), None, None, 'tp')
The draws below stay inside these ranges and needn't reach their ends.
Inputs may be any that keep to these rules, and one draw needn't show every extreme that they name: `routes`: within each sequence, each aligned block of 256 positions (the positions of one index of ctx) names no expert more than 144 times; some blocks reach 144. The 8 experts of a token are distinct.
All inputs are finite; a program needn't handle non-finite values.
Results may differ from the reference program's by a relative error of at most 0.022.
Values may be sent and summed in bfloat16 or wider, within the bound.
A program may use at most 320 MiB of HBM per device.

```python
import math
import jax
import jax.numpy as jnp
import numpy as np
from jax import lax

D = 2048
H = 16
HD = 128
F = 1024
TOPK = 8
E = 16
LEN = 1024
SEQS = 4
STRETCH = 256
CAP = 512
MOST = 144


def draw_w_experts(key, part):
    normal_draw = jnp.clip(jax.random.normal(key, (D, 3, E, F), jnp.float32), -6.0, 6.0)
    scales = jnp.array([D ** (-0.5), D ** (-0.5), 6.0 * F ** (-0.5)], jnp.float32)
    return (normal_draw * scales[None, :, None, None]).astype(jnp.bfloat16)


def block_levels(key, extent, cuts, low, largest):
    gain, own = 1.0, jax.random.fold_in(key, 6)
    for dim, parts in cuts:
        draws = jnp.exp(jax.random.uniform(jax.random.fold_in(own, dim), (parts,), jnp.float32, low / len(cuts), largest / len(cuts)))
        gain = gain * jnp.repeat(draws, extent[dim] // parts).reshape([-1 if axis == dim else 1 for axis in range(len(extent))])
    return gain


def assign_block(key, own, number, rows, number_of, top, reach, skew):
    sequence = jax.random.permutation(key, number_of)
    crowded, common = load_shares(number_of, rows * top, reach, skew, True), load_shares(number_of, rows * top, reach, skew, False)
    places = jnp.arange(number_of)

    def named(sizes, turn):
        used = int((sizes > 0).sum())
        fixed = max(1, used // 4)
        shifted = fixed + (places - fixed + turn * (used - fixed)) % max(1, number_of - fixed)
        return jnp.zeros((number_of,), jnp.int32).at[sequence[jnp.where(places < fixed, places, shifted)]].set(jnp.asarray(sizes, jnp.int32))

    sizes = jnp.where(number % 4 == 0, named(crowded, number // 4), named(common, number - number // 4 - 1))
    mixed = jax.random.permutation(jax.random.fold_in(own, 3), number_of)
    donor, receiver = mixed[0:number_of // 2 * 2:2], mixed[1:number_of // 2 * 2:2]
    margin = jnp.minimum(sizes[donor] - 1, reach - sizes[receiver]) // 2
    margin = jnp.where((donor == sequence[0]) | (receiver == sequence[0]) | (sizes[receiver] == 0), 0, jnp.maximum(margin, 0))
    shifted = jax.random.randint(jax.random.fold_in(own, 4), (number_of // 2,), 0, 1 << 20) % (margin + 1)
    sizes = sizes.at[donor].add(-shifted).at[receiver].add(shifted)
    items = jnp.searchsorted(jnp.cumsum(sizes), jnp.arange(rows * top), side="right").astype(jnp.int32)
    table = items.reshape(top, rows).T
    table = table[jax.random.permutation(jax.random.fold_in(own, 1), rows)]
    turn = jax.random.randint(jax.random.fold_in(own, 2), (rows, 1), 0, top)
    return jnp.take_along_axis(table, (jnp.arange(top)[None, :] + turn) % top, axis=1)


def load_shares(count, total, reach, slope, full):
    loads = [(1 << 20) // math.isqrt(standing ** slope) + 1 for standing in range(1, count + 1)]
    largest = reach if full else min(reach, max(-(-total // count), total * loads[0] // sum(loads)))
    least = 1 if total - largest >= count - 1 else 0
    given, rest = [largest] + [least] * (count - 1), total - largest - least * (count - 1)
    while rest > 0:
        movable = [i for i in range(1, count) if given[i] < largest] or [i for i in range(1, count) if given[i] < reach]
        pool, budget = sum([loads[i] for i in movable]), rest
        for i in movable:
            extra = min(reach - given[i], max(1, budget * loads[i] // pool), rest)
            given[i] = given[i] + extra
            rest = rest - extra
    return np.array(given)


def scatter_about(stream_key, extent, spread, most, split=(), kind=jnp.bfloat16):
    values = spread * jax.random.normal(stream_key, extent, jnp.float32)
    if split:
        values = values * block_levels(stream_key, extent, split, -0.22, 0.18)
    return jnp.clip(values, -most, most).astype(kind)


def setup_inputs(seed: int = 0) -> dict:
    splits = jax.random.split(jax.random.key(seed), 14)
    tokens = scatter_about(splits[0], (SEQS, LEN, D), 1.0, 6.0, ((0, 4), (1, 4)))
    w_query = scatter_about(splits[1], (D, D), D ** -0.5, 0.125, ((0, 4), (1, 2)))
    w_key = scatter_about(splits[2], (D, D), D ** -0.5, 0.125, ((0, 4), (1, 2)))
    w_value = scatter_about(splits[3], (D, D), D ** -0.5, 0.125, ((0, 4), (1, 2)))
    w_out = scatter_about(splits[4], (D, D), (max(D // LEN, 1)) ** -0.5, 4.0, ((0, 2), (1, 4)))
    gain_attn = jnp.clip(1.0 + 0.1 * jax.random.normal(splits[5], (D,), jnp.float32), 0.5, 1.5).astype(jnp.bfloat16)
    gain_query = jnp.clip(1.0 + 0.1 * jax.random.normal(splits[6], (HD,), jnp.float32), 0.5, 1.5).astype(jnp.bfloat16)
    gain_key = jnp.clip(1.0 + 0.1 * jax.random.normal(splits[7], (HD,), jnp.float32), 0.5, 1.5).astype(jnp.bfloat16)
    gain_moe = jnp.clip(1.0 + 0.1 * jax.random.normal(splits[8], (D,), jnp.float32), 0.5, 1.5).astype(jnp.bfloat16)
    w_router = scatter_about(splits[9], (D, E), D ** -0.5, 0.125, ((0, 4),))
    w_experts = draw_w_experts(jax.random.fold_in(splits[13], 71), 0)
    routes_keys = jax.random.split(jax.random.fold_in(splits[11], 1), SEQS * LEN // STRETCH)
    routes_turns = jax.random.permutation(jax.random.fold_in(splits[11], 3), SEQS * LEN // STRETCH)
    routes = jax.vmap(lambda own, number: assign_block(jax.random.fold_in(splits[11], 2), own, number, STRETCH, E, TOPK, MOST, 2))(routes_keys, routes_turns).reshape((SEQS, LEN, TOPK))
    cotangent = scatter_about(splits[12], (SEQS, LEN, D), 1.0, 6.0, ((0, 4), (1, 4)))
    return dict(tokens=tokens, w_query=w_query, w_key=w_key, w_value=w_value, w_out=w_out, gain_attn=gain_attn, gain_query=gain_query, gain_key=gain_key, gain_moe=gain_moe, w_router=w_router, w_experts=w_experts, routes=routes, cotangent=cotangent)


EPS = 1e-06
ROPE_BASE = 10000.0
HIGH = lax.Precision.HIGHEST

@jax.custom_vjp
def low(v):
    return lax.optimization_barrier(v.astype(jnp.bfloat16)).astype(jnp.float32)

@jax.custom_vjp
def low_back(v):
    return v

def low_keep(v):
    return (low(v), None)

def low_pass(kept, grad):
    return (grad,)

def back_keep(v):
    return (v, None)

def back_low(kept, grad):
    return (low(grad),)
low.defvjp(low_keep, low_pass)
low_back.defvjp(back_keep, back_low)

def matmul(left, right):
    return jnp.matmul(left, right, precision=HIGH)

def rms_scale(values):
    return lax.rsqrt(lax.optimization_barrier(jnp.mean(values * values, -1, keepdims=True)) + EPS)

def head_norm(values, gain_vec):
    return values * rms_scale(values) * gain_vec

def rope_tables(length):
    half_dim = HD // 2
    inv_freq = jnp.exp(jnp.arange(half_dim, dtype=jnp.float32) * (-2.0 * math.log(ROPE_BASE) / HD))
    angles = jnp.arange(length, dtype=jnp.int32).astype(jnp.float32)[:, None] * inv_freq[None, :]
    cos_table = jnp.cos(angles)
    sin_table = jnp.sin(angles)
    return (jnp.concatenate([cos_table, cos_table], -1), jnp.concatenate([sin_table, sin_table], -1))

def rotate(values):
    half_dim = values.shape[-1] // 2
    return jnp.concatenate([-values[..., half_dim:], values[..., :half_dim]], -1)

def apply_rope(values, cos_table, sin_table):
    return values * cos_table + rotate(values) * sin_table

def slot_tables(route_rows):
    flat_routes = route_rows.reshape(-1).astype(jnp.int32)
    onehot = (flat_routes[:, None] == jnp.arange(E, dtype=jnp.int32)[None, :]).astype(jnp.int32)
    earlier = jnp.cumsum(onehot, 0, dtype=jnp.int32) - onehot
    slot_index = lax.optimization_barrier(jnp.sum(earlier * onehot, 1, dtype=jnp.int32))
    kept_mask = slot_index < CAP
    position = jnp.where(kept_mask, flat_routes * CAP + slot_index, E * CAP).astype(jnp.int32)
    token_ids = jnp.arange(LEN * TOPK, dtype=jnp.int32) // TOPK
    owner_rows = jnp.zeros((E * CAP,), jnp.int32).at[position].set(token_ids, mode='drop')
    return (position.reshape(LEN, TOPK), kept_mask.reshape(LEN, TOPK), owner_rows)

def experts_apply(normed_seq, probs_seq, route_rows, position, kept_mask, owner_rows, w_experts):
    onehot = (route_rows[:, :, None] == jnp.arange(E, dtype=jnp.int32)[None, None, :]).astype(jnp.float32)
    gate_weight = lax.optimization_barrier(jnp.sum(onehot * probs_seq[:, None, :], -1)) * kept_mask.astype(jnp.float32)
    gathered = normed_seq[owner_rows].reshape(E, CAP, D)
    gate_act = low_back(jnp.einsum('ecd,def->ecf', gathered, w_experts[:, 0], precision=HIGH))
    up_act = low_back(jnp.einsum('ecd,def->ecf', gathered, w_experts[:, 1], precision=HIGH))
    hidden = low(jax.nn.silu(gate_act) * up_act)
    expert_out = low_back(jnp.einsum('ecf,def->ecd', hidden, w_experts[:, 2], precision=HIGH)).reshape(E * CAP, D)
    picked = expert_out[jnp.minimum(position, E * CAP - 1)]
    return lax.optimization_barrier(jnp.sum(gate_weight[:, :, None] * picked, 1))

def apply_block(weights, pieces):
    w_query, w_key, w_value, w_out, gain_attn, gain_query, gain_key, gain_moe, w_router, w_experts = weights
    hidden_in, route_rows, position, kept_mask, owner_rows = pieces
    group_size = hidden_in.shape[0]
    normed_one = low(hidden_in * rms_scale(hidden_in) * gain_attn)
    query_proj = low_back(matmul(normed_one, w_query))
    key_proj = low_back(matmul(normed_one, w_key))
    value_proj = low_back(matmul(normed_one, w_value))
    head_shape = (group_size, LEN, H, HD)
    cos_table, sin_table = rope_tables(LEN)
    cos_table = cos_table[:, None, :]
    sin_table = sin_table[:, None, :]
    queries = low(apply_rope(head_norm(query_proj.reshape(head_shape), gain_query), cos_table, sin_table))
    keys = low(apply_rope(head_norm(key_proj.reshape(head_shape), gain_key), cos_table, sin_table))
    values = low(value_proj.reshape(head_shape))
    score_scale = 1.0 / math.sqrt(HD)
    scores = low_back(jnp.einsum('gqhd,gkhd->ghqk', queries, keys, precision=HIGH) * score_scale)
    attn_probs = jax.nn.softmax(scores, -1)
    context = jnp.einsum('ghqk,gkhd->gqhd', low(attn_probs), values, precision=HIGH)
    context = low(low_back(context)).reshape(group_size, LEN, D)
    residual = hidden_in + low_back(matmul(context, w_out))
    normed_two = low(residual * rms_scale(residual) * gain_moe)
    router_probs = jax.nn.softmax(low_back(matmul(normed_two, w_router)), -1)
    moe = jax.vmap(experts_apply, in_axes=(0, 0, 0, 0, 0, 0, None))(normed_two, router_probs, route_rows, position, kept_mask, owner_rows, w_experts)
    return residual + moe

def reference(tokens, w_query, w_key, w_value, w_out, gain_attn, gain_query, gain_key, gain_moe, w_router, w_experts, routes, cotangent):
    position, kept_mask, owner_rows = jax.vmap(slot_tables)(routes)
    group_size = math.gcd(SEQS, max(1, 4096 // LEN))
    steps_count = SEQS // group_size

    def regroup(tensor):
        return tensor.reshape((steps_count, group_size) + tensor.shape[1:])

    def forward(hidden_in, *weights):

        def one_block(pieces):
            return apply_block(weights, pieces)
        outputs = lax.map(jax.checkpoint(one_block), (regroup(hidden_in), regroup(routes), regroup(position), regroup(kept_mask), regroup(owner_rows)))
        return outputs.reshape(hidden_in.shape)
    floats = [tensor.astype(jnp.float32) for tensor in (tokens, w_query, w_key, w_value, w_out, gain_attn, gain_query, gain_key, gain_moe, w_router, w_experts)]
    layer_out, pullback = jax.vjp(forward, *floats)
    gradients = pullback(cotangent.astype(jnp.float32))
    return (layer_out.astype(jnp.bfloat16), gradients[0].astype(jnp.bfloat16), gradients[1], gradients[2], gradients[3], gradients[4], gradients[5], gradients[6], gradients[7], gradients[8], gradients[9], gradients[10])
```

```python
import math

import jax
import jax.numpy as jnp
from jax import lax
from jax.sharding import PartitionSpec as P

HD = 128
TOPK = 8
E = 16
CAP = 512


EPS = 1e-06
ROPE_BASE = 10000.0


def prefix(value, axis, join, neutral):
    count, mine = (lax.axis_size(axis), lax.axis_index(axis))
    pieces = lax.all_gather(value, axis)
    running = jnp.full_like(value, 0) + jnp.asarray(neutral, value.dtype)

    def lap(position, running):
        longer = join(running, pieces[position])
        return jnp.where(position < mine, longer, running)

    return lax.fori_loop(0, count - 1, lap, running)


def rms_scale(values):
    return lax.rsqrt(jnp.mean(values * values, -1, keepdims=True) + EPS)


def norm_back(grad_normed, values, inv_rms, gain_vec):
    weighted = grad_normed * gain_vec.astype(jnp.float32)
    inner_sum = jnp.sum(weighted * values, -1, keepdims=True)
    return (
        inv_rms * weighted - values * (inv_rms * inv_rms * inv_rms) * inner_sum / values.shape[-1]
    )


def rope_tables(first, length):
    half_dim = HD // 2
    inv_freq = jnp.exp(jnp.arange(half_dim, dtype=jnp.float32) * (-2.0 * math.log(ROPE_BASE) / HD))
    places = (first + jnp.arange(length, dtype=jnp.int32)).astype(jnp.float32)
    angles = places[:, None] * inv_freq[None, :]
    cos_table = jnp.cos(angles)
    sin_table = jnp.sin(angles)
    cos_full = jnp.concatenate([cos_table, cos_table], -1)[:, None, :]
    sin_full = jnp.concatenate([sin_table, sin_table], -1)[:, None, :]
    return (cos_full, sin_full)


def rotate(values):
    half_dim = values.shape[-1] // 2
    return jnp.concatenate([-values[..., half_dim:], values[..., :half_dim]], -1)


def rotate_back(values):
    half_dim = values.shape[-1] // 2
    return jnp.concatenate([values[..., half_dim:], -values[..., :half_dim]], -1)


def apply_rope(values, cos_full, sin_full):
    return values * cos_full + rotate(values) * sin_full


def rope_back(grads, cos_full, sin_full):
    return grads * cos_full + rotate_back(grads * sin_full)


def add_counts(earlier, later):
    return earlier + later


def general(
    tokens,
    w_query,
    w_key,
    w_value,
    w_out,
    gain_attn,
    gain_query,
    gain_key,
    gain_moe,
    w_router,
    w_experts,
    routes,
    cotangent,
):
    seq_count, block_len, model_width = tokens.shape
    row_count = seq_count * block_len
    (
        full_query,
        full_key,
        full_value,
        full_out,
        router_full,
        attn_gain,
        query_gain,
        key_gain,
        moe_gain,
    ) = (
        lax.all_gather(w_query, "fsdp", axis=0, tiled=True),
        lax.all_gather(w_key, "fsdp", axis=0, tiled=True),
        lax.all_gather(w_value, "fsdp", axis=0, tiled=True),
        lax.all_gather(w_out, "fsdp", axis=1, tiled=True),
        lax.all_gather(w_router, "fsdp", axis=0, tiled=True),
        lax.all_gather(gain_attn, "fsdp", axis=0, tiled=True),
        lax.all_gather(gain_query, "fsdp", axis=0, tiled=True),
        lax.all_gather(gain_key, "fsdp", axis=0, tiled=True),
        lax.all_gather(gain_moe, "fsdp", axis=0, tiled=True),
    )
    local_width = full_query.shape[1]
    head_count = local_width // HD
    head_shape = (seq_count, block_len, head_count, HD)
    token_rows = tokens.reshape(row_count, model_width).astype(jnp.float32)
    inv_one = rms_scale(token_rows)
    normed_one = (token_rows * inv_one * attn_gain.astype(jnp.float32)).astype(jnp.bfloat16)
    query_proj = jnp.dot(normed_one, full_query, preferred_element_type=jnp.float32)
    key_proj = jnp.dot(normed_one, full_key, preferred_element_type=jnp.float32)
    value_proj = jnp.dot(normed_one, full_value, preferred_element_type=jnp.float32)
    cos_full, sin_full = rope_tables(lax.axis_index("ctx") * block_len, block_len)
    query_heads = query_proj.reshape(head_shape)
    key_heads = key_proj.reshape(head_shape)
    query_inv = rms_scale(query_heads)
    key_inv = rms_scale(key_heads)
    queries = apply_rope(
        query_heads * query_inv * query_gain.astype(jnp.float32), cos_full, sin_full
    ).astype(jnp.bfloat16)
    keys_local = apply_rope(
        key_heads * key_inv * key_gain.astype(jnp.float32), cos_full, sin_full
    ).astype(jnp.bfloat16)
    keys_local = keys_local.reshape(seq_count, block_len, local_width)
    values_local = value_proj.astype(jnp.bfloat16).reshape(seq_count, block_len, local_width)
    keys_all, values_all = (
        lax.all_gather(keys_local, "ctx", axis=1, tiled=True),
        lax.all_gather(values_local, "ctx", axis=1, tiled=True),
    )
    seq_len = keys_all.shape[1]
    key_rows = keys_all.reshape(seq_count, seq_len, head_count, HD)
    value_rows = values_all.reshape(seq_count, seq_len, head_count, HD)
    score_scale = 1.0 / math.sqrt(HD)
    scores = (
        jnp.einsum("sqhd,skhd->shqk", queries, key_rows, preferred_element_type=jnp.float32)
        * score_scale
    )
    maximum = jnp.max(scores, -1, keepdims=True)
    exp_scores = jnp.exp(scores - maximum)
    denominator = jnp.sum(exp_scores, -1, keepdims=True)
    attn_probs = exp_scores / denominator
    log_total = maximum + jnp.log(denominator)
    context = jnp.einsum(
        "shqk,skhd->sqhd",
        attn_probs.astype(jnp.bfloat16),
        value_rows,
        preferred_element_type=jnp.float32,
    )
    context = context.astype(jnp.bfloat16).reshape(row_count, local_width)
    attn_part = jnp.dot(context, full_out, preferred_element_type=jnp.float32)
    residual = token_rows + lax.psum(attn_part, "tp")
    inv_two = rms_scale(residual)
    normed_two = (residual * inv_two * moe_gain.astype(jnp.float32)).astype(jnp.bfloat16)
    logits = jnp.dot(normed_two, router_full, preferred_element_type=jnp.float32)
    router_probs = jax.nn.softmax(logits, -1)
    pair_count = block_len * TOPK
    route_rows = routes.reshape(seq_count, pair_count)
    expert_ids = jnp.arange(E, dtype=jnp.int32)
    onehot = (route_rows[:, :, None] == expert_ids[None, None, :]).astype(jnp.int32)
    counts = jnp.sum(onehot, 1, dtype=jnp.int32)
    offsets = prefix(counts, "ctx", add_counts, jnp.zeros_like(counts))
    earlier = jnp.cumsum(onehot, 1, dtype=jnp.int32) - onehot
    local_rank = jnp.sum(earlier * onehot, 2, dtype=jnp.int32)
    slot_base = jnp.sum(onehot * offsets[:, None, :], 2, dtype=jnp.int32)
    kept_mask = (slot_base + local_rank < CAP).astype(jnp.float32).reshape(row_count, TOPK)
    block_most = pair_count * 9 // (8 * E)
    expert_span = seq_count * block_most
    seq_ids = jnp.arange(seq_count, dtype=jnp.int32)[:, None]
    buffer_row = (route_rows * expert_span + seq_ids * block_most + local_rank).reshape(
        row_count * TOPK
    )
    token_ids = (
        seq_ids * block_len + jnp.arange(pair_count, dtype=jnp.int32)[None, :] // TOPK
    ).reshape(row_count * TOPK)
    owner_rows = jnp.zeros((E * expert_span,), jnp.int32).at[buffer_row].set(token_ids)
    onehot_f = onehot.astype(jnp.float32).reshape(row_count, TOPK, E)
    gate_weight = jnp.sum(onehot_f * router_probs[:, None, :], 2) * kept_mask
    slot_weight = (
        jnp.zeros((E * expert_span,), jnp.float32)
        .at[buffer_row]
        .set(gate_weight.reshape(row_count * TOPK))
    )
    expert_rows = normed_two[owner_rows].reshape(E, expert_span, model_width)
    cotan_rows = cotangent.reshape(row_count, model_width)
    grad_expert = (slot_weight[:, None] * cotan_rows[owner_rows].astype(jnp.float32)).astype(
        jnp.bfloat16
    )
    grad_expert = grad_expert.reshape(E, expert_span, model_width)
    ffn_local = w_experts.shape[3]
    fsdp_count = lax.axis_size("fsdp")
    ctx_count = lax.axis_size("ctx")
    group_count = fsdp_count * ctx_count
    sharing = group_count // E
    padded_span = -(-expert_span // sharing) * sharing
    part_span = padded_span // sharing
    target_experts = (
        jnp.arange(fsdp_count, dtype=jnp.int32) * ctx_count + lax.axis_index("ctx")
    ) // sharing
    selected = jnp.take(w_experts, target_experts, axis=2)
    owned = lax.all_to_all(selected, "fsdp", split_axis=2, concat_axis=0, tiled=True)[:, :, 0]
    send_rows = expert_rows.reshape(group_count, part_span, model_width)
    send_grads = grad_expert.reshape(group_count, part_span, model_width)
    recv_rows, recv_grads = (
        lax.all_to_all(send_rows, ("fsdp", "ctx"), split_axis=0, concat_axis=0, tiled=True),
        lax.all_to_all(send_grads, ("fsdp", "ctx"), split_axis=0, concat_axis=0, tiled=True),
    )
    rows_flat = recv_rows.reshape(group_count * part_span, model_width)
    grads_flat = recv_grads.reshape(group_count * part_span, model_width)
    gate_act = jnp.dot(rows_flat, owned[:, 0], preferred_element_type=jnp.float32)
    up_act = jnp.dot(rows_flat, owned[:, 1], preferred_element_type=jnp.float32)
    sigmoid_gate = jax.nn.sigmoid(gate_act)
    silu_gate = gate_act * sigmoid_gate
    hidden = (silu_gate * up_act).astype(jnp.bfloat16)
    produced = jnp.einsum("mf,df->md", hidden, owned[:, 2], preferred_element_type=jnp.float32)
    grad_hidden = jnp.dot(grads_flat, owned[:, 2], preferred_element_type=jnp.float32)
    grad_gate = (
        grad_hidden * up_act * sigmoid_gate * (1.0 + gate_act * (1.0 - sigmoid_gate))
    ).astype(jnp.bfloat16)
    grad_up = (grad_hidden * silu_gate).astype(jnp.bfloat16)
    rows_grad = jnp.einsum("mf,df->md", grad_gate, owned[:, 0], preferred_element_type=jnp.float32)
    rows_grad = rows_grad + jnp.einsum(
        "mf,df->md", grad_up, owned[:, 1], preferred_element_type=jnp.float32
    )
    back_out, back_rows = (
        lax.all_to_all(
            produced.reshape(group_count, part_span, model_width).astype(jnp.bfloat16),
            ("fsdp", "ctx"),
            split_axis=0,
            concat_axis=0,
            tiled=True,
        ).astype(jnp.float32),
        lax.all_to_all(
            rows_grad.reshape(group_count, part_span, model_width).astype(jnp.bfloat16),
            ("fsdp", "ctx"),
            split_axis=0,
            concat_axis=0,
            tiled=True,
        ).astype(jnp.float32),
    )
    expert_out = back_out.reshape(E, padded_span, model_width)
    grad_rows = back_rows.reshape(E, padded_span, model_width)
    gate_term = jnp.einsum("md,mf->df", rows_flat, grad_gate, preferred_element_type=jnp.float32)
    up_term = jnp.einsum("md,mf->df", rows_flat, grad_up, preferred_element_type=jnp.float32)
    down_term = jnp.einsum("md,mf->df", grads_flat, hidden, preferred_element_type=jnp.float32)
    owner_terms = jnp.stack([gate_term, up_term, down_term], 1)[:, :, None, :]
    relaid = lax.all_to_all(
        owner_terms.astype(jnp.bfloat16), ("fsdp", "ctx"), split_axis=0, concat_axis=2, tiled=True
    ).astype(owner_terms.dtype)
    dw_experts = jnp.sum(relaid.reshape(relaid.shape[0], 3, E, sharing, ffn_local), 3)
    picked = expert_out.reshape(E * expert_span, model_width)[buffer_row].reshape(
        row_count, TOPK, model_width
    )
    moe_part = jnp.sum(gate_weight[:, :, None] * picked, 1)
    cotan_float = cotan_rows.astype(jnp.float32)
    grad_gate_part = jnp.sum(picked * cotan_float[:, None, :], 2)
    moe_shard = lax.psum_scatter(
        moe_part.astype(jnp.bfloat16), "tp", scatter_dimension=1, tiled=True
    ).astype(jnp.float32)
    piece_width = moe_shard.shape[1]
    residual_shard = lax.dynamic_slice_in_dim(
        residual, lax.axis_index("tp") * piece_width, piece_width, 1
    )
    layer_out = (
        (residual_shard + moe_shard).astype(jnp.bfloat16).reshape(seq_count, block_len, piece_width)
    )
    grad_normed_part = jnp.sum(
        grad_rows.reshape(E * expert_span, model_width)[buffer_row].reshape(
            row_count, TOPK, model_width
        ),
        1,
    )
    grad_normed_sum, grad_gate_sum = (
        lax.psum(grad_normed_part.astype(jnp.bfloat16), "tp").astype(jnp.float32),
        lax.psum(grad_gate_part.astype(jnp.bfloat16), "tp").astype(jnp.float32),
    )
    grad_pick = grad_gate_sum * kept_mask
    grad_router_probs = jnp.sum(onehot_f * grad_pick[:, :, None], 1)
    grad_logits = router_probs * (
        grad_router_probs - jnp.sum(router_probs * grad_router_probs, -1, keepdims=True)
    )
    grad_logits = grad_logits.astype(jnp.bfloat16)
    grad_router_w = jnp.einsum(
        "nd,ne->de", normed_two, grad_logits, preferred_element_type=jnp.float32
    )
    grad_normed_two = grad_normed_sum + jnp.einsum(
        "ne,de->nd", grad_logits, router_full, preferred_element_type=jnp.float32
    )
    grad_moe_gain = jnp.sum(grad_normed_two * residual * inv_two, 0)
    grad_residual = cotan_float + norm_back(grad_normed_two, residual, inv_two, moe_gain)
    grad_attn = grad_residual.astype(jnp.bfloat16)
    grad_w_out = jnp.einsum("nl,nd->ld", context, grad_attn, preferred_element_type=jnp.float32)
    grad_context = jnp.einsum("nd,ld->nl", grad_attn, full_out, preferred_element_type=jnp.float32)
    grad_context = grad_context.astype(jnp.bfloat16).reshape(head_shape)
    scores = (
        jnp.einsum("sqhd,skhd->shqk", queries, key_rows, preferred_element_type=jnp.float32)
        * score_scale
    )
    attn_probs = jnp.exp(scores - log_total)
    grad_probs = jnp.einsum(
        "sqhd,skhd->shqk", grad_context, value_rows, preferred_element_type=jnp.float32
    )
    grad_scores = attn_probs * (grad_probs - jnp.sum(attn_probs * grad_probs, -1, keepdims=True))
    grad_scores = grad_scores.astype(jnp.bfloat16)
    grad_queries = (
        jnp.einsum("shqk,skhd->sqhd", grad_scores, key_rows, preferred_element_type=jnp.float32)
        * score_scale
    )
    grad_keys_all = (
        jnp.einsum("shqk,sqhd->skhd", grad_scores, queries, preferred_element_type=jnp.float32)
        * score_scale
    )
    grad_values_all = jnp.einsum(
        "shqk,sqhd->skhd",
        attn_probs.astype(jnp.bfloat16),
        grad_context,
        preferred_element_type=jnp.float32,
    )
    grad_keys_own, grad_values_own = (
        lax.psum_scatter(
            grad_keys_all.reshape(seq_count, seq_len, local_width).astype(jnp.bfloat16),
            "ctx",
            scatter_dimension=1,
            tiled=True,
        ).astype(jnp.float32),
        lax.psum_scatter(
            grad_values_all.reshape(seq_count, seq_len, local_width).astype(jnp.bfloat16),
            "ctx",
            scatter_dimension=1,
            tiled=True,
        ).astype(jnp.float32),
    )
    grad_qnormed = rope_back(grad_queries, cos_full, sin_full)
    grad_knormed = rope_back(grad_keys_own.reshape(head_shape), cos_full, sin_full)
    grad_qgain = jnp.sum(grad_qnormed * query_heads * query_inv, (0, 1, 2))
    grad_kgain = jnp.sum(grad_knormed * key_heads * key_inv, (0, 1, 2))
    grad_qproj = (
        norm_back(grad_qnormed, query_heads, query_inv, query_gain)
        .astype(jnp.bfloat16)
        .reshape(row_count, local_width)
    )
    grad_kproj = (
        norm_back(grad_knormed, key_heads, key_inv, key_gain)
        .astype(jnp.bfloat16)
        .reshape(row_count, local_width)
    )
    grad_vproj = grad_values_own.astype(jnp.bfloat16).reshape(row_count, local_width)
    grad_wq = jnp.einsum("nd,nl->dl", normed_one, grad_qproj, preferred_element_type=jnp.float32)
    grad_wk = jnp.einsum("nd,nl->dl", normed_one, grad_kproj, preferred_element_type=jnp.float32)
    grad_wv = jnp.einsum("nd,nl->dl", normed_one, grad_vproj, preferred_element_type=jnp.float32)
    grad_normed_one = jnp.einsum(
        "nl,dl->nd", grad_qproj, full_query, preferred_element_type=jnp.float32
    )
    grad_normed_one = grad_normed_one + jnp.einsum(
        "nl,dl->nd", grad_kproj, full_key, preferred_element_type=jnp.float32
    )
    grad_normed_one = grad_normed_one + jnp.einsum(
        "nl,dl->nd", grad_vproj, full_value, preferred_element_type=jnp.float32
    )
    grad_normed_one, grad_qgain, grad_kgain = (
        lax.psum(grad_normed_one.astype(jnp.bfloat16), "tp").astype(jnp.float32),
        lax.psum(grad_qgain.astype(jnp.bfloat16), "tp").astype(jnp.float32),
        lax.psum(grad_kgain.astype(jnp.bfloat16), "tp").astype(jnp.float32),
    )
    grad_attn_gain = jnp.sum(grad_normed_one * token_rows * inv_one, 0)
    tokens_grad = grad_residual + norm_back(grad_normed_one, token_rows, inv_one, attn_gain)
    tokens_grad = tokens_grad.astype(jnp.bfloat16).reshape(seq_count, block_len, model_width)
    dw_query, dw_key, dw_value, dw_out, dw_router, dgain_attn, dgain_query, dgain_key, dgain_moe = (
        lax.psum_scatter(grad_wq, ("fsdp", "ctx"), scatter_dimension=0, tiled=True),
        lax.psum_scatter(grad_wk, ("fsdp", "ctx"), scatter_dimension=0, tiled=True),
        lax.psum_scatter(grad_wv, ("fsdp", "ctx"), scatter_dimension=0, tiled=True),
        lax.psum_scatter(grad_w_out, ("fsdp", "ctx"), scatter_dimension=1, tiled=True),
        lax.psum_scatter(grad_router_w, ("fsdp", "ctx"), scatter_dimension=0, tiled=True),
        lax.psum_scatter(grad_attn_gain, ("fsdp", "ctx"), scatter_dimension=0, tiled=True),
        lax.psum_scatter(grad_qgain, ("fsdp", "ctx"), scatter_dimension=0, tiled=True),
        lax.psum_scatter(grad_kgain, ("fsdp", "ctx"), scatter_dimension=0, tiled=True),
        lax.psum_scatter(grad_moe_gain, ("fsdp", "ctx"), scatter_dimension=0, tiled=True),
    )
    return (
        layer_out,
        tokens_grad,
        dw_query,
        dw_key,
        dw_value,
        dw_out,
        dgain_attn,
        dgain_query,
        dgain_key,
        dgain_moe,
        dw_router,
        dw_experts,
    )


def swap(value):
    return lax.ppermute(value, "tp", [(0, 1), (1, 0)])


def exchange(value, axes):
    return lax.all_to_all(value, axes, split_axis=0, concat_axis=0, tiled=True)


def spread(value, axes):
    count = lax.axis_size(axes)
    return exchange(jnp.broadcast_to(value[None], (count,) + value.shape), axes)


def dot(left, right):
    return jnp.dot(left, right, preferred_element_type=jnp.float32)


def dot_nt(left, right):
    return lax.dot_general(left, right, (((1,), (1,)), ((), ())), preferred_element_type=jnp.float32)


def dot_tn(left, right):
    return lax.dot_general(left, right, (((0,), (0,)), ((), ())), preferred_element_type=jnp.float32)


def two_parts(values):
    high = values.astype(jnp.bfloat16)
    low = (values - high.astype(jnp.float32)).astype(jnp.bfloat16)
    return (high, low)


def by_core(mine, other, core):
    return jnp.where(core == 0, jnp.stack([mine, other]), jnp.stack([other, mine]))


def half_rows_sum(partial):
    received = swap(partial[1].astype(jnp.bfloat16))
    summed = (partial[0] + received.astype(jnp.float32)).astype(jnp.bfloat16)
    pieces = exchange(summed, "ctx")
    return jnp.sum(pieces.astype(jnp.float32), 0)


def all_rows(half):
    mine = spread(half, "ctx")
    return jnp.stack([mine, swap(mine)])


def one_chip(
    tokens,
    w_query,
    w_key,
    w_value,
    w_out,
    gain_attn,
    gain_query,
    gain_key,
    gain_moe,
    w_router,
    w_experts,
    routes,
    cotangent,
):
    z, c, t = lax.axis_index("fsdp"), lax.axis_index("ctx"), lax.axis_index("tp")
    nz, nc = lax.axis_size("fsdp"), lax.axis_size("ctx")
    block, width = tokens.shape[1], tokens.shape[2]
    rows = block // 2
    tall = block * nc
    deep = width // nz
    ffn = w_experts.shape[3]
    most = block * TOPK * 9 // (8 * E)
    bf16, f32 = jnp.bfloat16, jnp.float32

    token_half = lax.dynamic_slice_in_dim(tokens[0], t * rows, rows, 0)
    cotan_half = lax.dynamic_slice_in_dim(cotangent[0], t * rows, rows, 0)
    small = jnp.concatenate(
        [gain_attn, gain_moe, w_router.T.reshape(-1), gain_query, gain_key]
    )
    small = lax.all_gather(small, "fsdp", axis=0)
    attn_gain = small[:, :deep].reshape(-1).astype(f32)
    moe_gain = small[:, deep : 2 * deep].reshape(-1).astype(f32)
    router = small[:, 2 * deep : (2 + E) * deep].reshape(nz, E, deep)
    router = router.transpose(0, 2, 1).reshape(width, E)
    part = HD // nz
    query_gain = small[:, (2 + E) * deep : (2 + E) * deep + part].reshape(-1).astype(f32)
    key_gain = small[:, (2 + E) * deep + part :].reshape(-1).astype(f32)
    routes_all = lax.all_gather(routes[0], ("fsdp", "ctx"), axis=0)

    local = w_query.shape[1] // nc
    cols = [lax.dynamic_slice_in_dim(w, c * local, local, 1) for w in (w_query, w_key, w_value)]
    w_qkv = spread(jnp.concatenate(cols, 1), "fsdp").reshape(width, 3 * local)
    w_o = spread(lax.dynamic_slice_in_dim(w_out, c * local, local, 0), "fsdp")
    w_o = w_o.transpose(1, 0, 2).reshape(local, width)

    own = lax.dynamic_slice_in_dim(w_experts, c * nz, nz, 2)
    own = own.transpose(1, 2, 0, 3)
    mats = [exchange(own[k], "fsdp").reshape(width, ffn) for k in range(3)]
    others = [swap(m) for m in mats]
    halves = [mats, others]

    x_rows = all_rows(token_half).reshape(tall, width).astype(f32)
    place = (
        jnp.arange(nc, dtype=jnp.int32)[None, :, None] * block
        + ((jnp.arange(2, dtype=jnp.int32) + t) % 2)[:, None, None] * rows
        + jnp.arange(rows, dtype=jnp.int32)[None, None, :]
    ).reshape(tall)
    half_dim = HD // 2
    inv_freq = jnp.exp(jnp.arange(half_dim, dtype=f32) * (-2.0 * math.log(ROPE_BASE) / HD))
    angles = place.astype(f32)[:, None] * inv_freq[None, :]
    cos_full = jnp.concatenate([jnp.cos(angles)] * 2, -1)[:, None, :]
    sin_full = jnp.concatenate([jnp.sin(angles)] * 2, -1)[:, None, :]
    normed_one = (x_rows * rms_scale(x_rows) * attn_gain).astype(bf16)
    proj = dot(normed_one, w_qkv).reshape(tall, 3, local // HD, HD)
    query_heads, key_heads = proj[:, 0], proj[:, 1]
    values = proj[:, 2].astype(bf16)
    query_inv, key_inv = rms_scale(query_heads), rms_scale(key_heads)
    queries = apply_rope(query_heads * query_inv * query_gain, cos_full, sin_full).astype(bf16)
    keys = apply_rope(key_heads * key_inv * key_gain, cos_full, sin_full).astype(bf16)
    score_scale = 1.0 / math.sqrt(HD)
    scores = jnp.einsum("qhd,khd->hqk", queries, keys, preferred_element_type=f32) * score_scale
    maximum = jnp.max(scores, -1, keepdims=True)
    exp_scores = jnp.exp(scores - maximum)
    denominator = jnp.sum(exp_scores, -1, keepdims=True)
    attn_probs = exp_scores / denominator
    log_total = maximum + jnp.log(denominator)
    context = jnp.einsum("hqk,khd->qhd", attn_probs.astype(bf16), values, preferred_element_type=f32)
    context = context.astype(bf16).reshape(tall, local)
    attn_part = dot(context, w_o).reshape(2, nc, rows, width)
    own_tokens = token_half.astype(f32)
    residual = own_tokens + half_rows_sum(attn_part)
    inv_two = rms_scale(residual)
    normed_two = (residual * inv_two * moe_gain).astype(bf16)
    logits = dot(normed_two, router)
    router_probs = jax.nn.softmax(logits, -1)

    ids = jnp.arange(E, dtype=jnp.int32)
    named_all = jnp.any(routes_all[:, :, :, None] == ids, 2)
    named_all = named_all.reshape(nz, nc, block, E).astype(jnp.int32)
    own_seq = lax.dynamic_index_in_dim(named_all, z, 0, keepdims=False).reshape(tall, E)
    slot = jnp.cumsum(own_seq, 0) - own_seq
    kept_seq = (own_seq * (slot < CAP)).astype(f32)
    kept = lax.dynamic_slice_in_dim(kept_seq, c * block + t * rows, rows, 0)
    gates = router_probs * kept
    line = lax.dynamic_index_in_dim(named_all, c, 1, keepdims=False)
    line = lax.dynamic_slice_in_dim(line, t * 2, 2, 0)
    rank = jnp.cumsum(line, 1) - line
    plane = jnp.arange(nc, dtype=jnp.int32) * nz + z
    line = jnp.take(line, plane, axis=2)
    rank = jnp.take(rank, plane, axis=2)
    order = (jnp.arange(2, dtype=jnp.int32) + t) % 2
    line = jnp.take(line.reshape(2, 2, rows, nc), order, axis=1).reshape(2, block, nc)
    rank = jnp.take(rank.reshape(2, 2, rows, nc), order, axis=1).reshape(2, block, nc)
    pick = (rank[..., None] == jnp.arange(most, dtype=jnp.int32)) & (line[..., None] > 0)
    pick = pick.transpose(0, 2, 3, 1).reshape(2, nc * most, block).astype(bf16)

    def dispatch(half):
        mine = spread(half, "fsdp")
        keep = lax.dynamic_slice_in_dim(mine, t * 2, 2, 0)
        send = lax.dynamic_slice_in_dim(mine, (1 - t) * 2, 2, 0)
        both = jnp.concatenate([keep, swap(send)], 1)
        picked = jnp.einsum("sib,sbw->siw", pick, both, preferred_element_type=f32).astype(bf16)
        picked = picked.reshape(2, nc, most, -1).transpose(1, 0, 2, 3)
        return exchange(picked, "ctx").reshape(nc * 2 * most, -1)

    cot_rows = dispatch(cotan_half)
    high, low = two_parts(gates)
    tail = jnp.zeros((rows, 128 - 2 * E), bf16)
    in_rows = dispatch(jnp.concatenate([normed_two, high, low, tail], 1))
    x_in = in_rows[:, :width]
    mine_id = c * nz + z
    extra = in_rows[:, width : width + 2 * E].astype(f32).reshape(-1, 2, E)
    weight = jnp.sum(jnp.where(ids == mine_id, extra, 0.0), (1, 2))[:, None]

    out_rows = back_rows = 0.0
    pair_grad = 0.0
    updates = []
    for w_gate, w_up, w_down in halves:
        gate_act = dot(x_in, w_gate)
        up_act = dot(x_in, w_up)
        grad_out = dot(cot_rows, w_down)
        sig = jax.nn.sigmoid(gate_act)
        silu = gate_act * sig
        hidden = silu * up_act
        pair_grad = pair_grad + jnp.sum(hidden.astype(bf16).astype(f32) * grad_out, 1, keepdims=True)
        weighted = (weight * hidden).astype(bf16)
        grad_hidden = weight * grad_out
        grad_gate = (grad_hidden * up_act * sig * (1.0 + gate_act * (1.0 - sig))).astype(bf16)
        grad_up = (grad_hidden * silu).astype(bf16)
        out_rows = out_rows + dot_nt(weighted, w_down)
        back_rows = back_rows + dot_nt(grad_gate, w_gate) + dot_nt(grad_up, w_up)
        updates.append((dot_tn(x_in, grad_gate), dot_tn(x_in, grad_up), dot_tn(cot_rows, weighted)))
    own_updates, other_updates = updates
    high, low = two_parts(jnp.where(ids == mine_id, pair_grad, 0.0))
    tail = jnp.zeros((high.shape[0], 128 - 2 * E), bf16)
    reply = jnp.concatenate([out_rows.astype(bf16), back_rows.astype(bf16), high, low, tail], 1)

    def collect(reply):
        reply = exchange(reply.reshape(nc, 2, most, -1), "ctx")
        reply = reply.transpose(1, 0, 2, 3).reshape(2, nc * most, -1)
        dense = jnp.einsum("sib,siw->sbw", pick, reply, preferred_element_type=f32).astype(bf16)
        mine, send = dense[:, :rows], dense[:, rows:]
        stacked = by_core(mine, swap(send), t).reshape(nz, rows, -1)
        return jnp.sum(exchange(stacked, "fsdp").astype(f32), 0)

    dense = collect(reply)
    moe_rows, grad_rows = dense[:, :width], dense[:, width : 2 * width]
    pair_rows = dense[:, 2 * width : 2 * width + E] + dense[:, 2 * width + E : 2 * width + 2 * E]

    dw_experts = []
    for mine, other in zip(own_updates, other_updates):
        total = (mine + swap(other.astype(bf16)).astype(f32)).astype(bf16)
        dw_experts.append(exchange(total.reshape(nz * nc, -1, ffn), ("fsdp", "ctx")))
    dw_experts = jnp.stack(dw_experts, 1).astype(f32)
    dw_experts = dw_experts.reshape(nz, nc, 3, -1, ffn).transpose(3, 2, 1, 0, 4)
    dw_experts = dw_experts.reshape(-1, 3, E, ffn)

    layer = (residual + moe_rows).astype(bf16)
    piece = width // 2
    layer_mine = lax.dynamic_slice_in_dim(layer, t * piece, piece, 1)
    layer_send = lax.dynamic_slice_in_dim(layer, (1 - t) * piece, piece, 1)
    layer_out = by_core(layer_mine, swap(layer_send), t).reshape(1, block, piece)

    grad_router_probs = pair_rows * kept
    grad_logits = router_probs * (
        grad_router_probs - jnp.sum(router_probs * grad_router_probs, -1, keepdims=True)
    )
    grad_logits = grad_logits.astype(bf16)
    dw_router = dot_tn(normed_two, grad_logits)
    grad_normed_two = grad_rows + dot_nt(grad_logits, router)
    dgain_moe = jnp.sum(grad_normed_two * residual * inv_two, 0)
    grad_residual = cotan_half.astype(f32) + norm_back(grad_normed_two, residual, inv_two, moe_gain)
    grad_attn = all_rows(grad_residual.astype(bf16)).reshape(tall, width)

    dw_out = dot_tn(context, grad_attn).astype(bf16)
    grad_context = dot_nt(grad_attn, w_o).astype(bf16).reshape(tall, -1, HD)
    scores = jnp.einsum("qhd,khd->hqk", queries, keys, preferred_element_type=f32) * score_scale
    attn_probs = jnp.exp(scores - log_total)
    grad_probs = jnp.einsum("qhd,khd->hqk", grad_context, values, preferred_element_type=f32)
    grad_scores = attn_probs * (grad_probs - jnp.sum(attn_probs * grad_probs, -1, keepdims=True))
    grad_scores = grad_scores.astype(bf16)
    grad_queries = jnp.einsum("hqk,khd->qhd", grad_scores, keys, preferred_element_type=f32) * score_scale
    grad_keys = jnp.einsum("hqk,qhd->khd", grad_scores, queries, preferred_element_type=f32) * score_scale
    grad_values = jnp.einsum(
        "hqk,qhd->khd", attn_probs.astype(bf16), grad_context, preferred_element_type=f32
    ).astype(bf16)
    grad_qnormed = rope_back(grad_queries, cos_full, sin_full)
    grad_knormed = rope_back(grad_keys, cos_full, sin_full)
    dgain_query = jnp.sum(grad_qnormed * query_heads * query_inv, (0, 1))
    dgain_key = jnp.sum(grad_knormed * key_heads * key_inv, (0, 1))
    grad_qproj = norm_back(grad_qnormed, query_heads, query_inv, query_gain).astype(bf16)
    grad_kproj = norm_back(grad_knormed, key_heads, key_inv, key_gain).astype(bf16)
    grad_proj = jnp.stack([grad_qproj, grad_kproj, grad_values], 1).reshape(tall, 3 * local)
    dw_qkv = dot_tn(normed_one, grad_proj).astype(bf16)
    grad_normed_part = dot_nt(grad_proj, w_qkv).reshape(2, nc, rows, width)
    grad_normed_one = half_rows_sum(grad_normed_part)
    inv_one = rms_scale(own_tokens)
    dgain_attn = jnp.sum(grad_normed_one * own_tokens * inv_one, 0)
    grad_tokens = grad_residual + norm_back(grad_normed_one, own_tokens, inv_one, attn_gain)
    grad_tokens = grad_tokens.astype(bf16)
    tokens_grad = by_core(grad_tokens, swap(grad_tokens), t).reshape(1, block, width)

    chips = nz * nc
    strip = width // chips
    got_qkv = exchange(dw_qkv.reshape(chips, strip, 3 * local), ("fsdp", "ctx"))
    got_qkv = jnp.sum(got_qkv.reshape(nz, nc, strip, 3, local).astype(f32), 0)
    got_qkv = got_qkv.transpose(2, 1, 0, 3).reshape(3, strip, nc * local)
    got_out = exchange(dw_out.reshape(local, chips, strip).transpose(1, 0, 2), ("fsdp", "ctx"))
    got_out = jnp.sum(got_out.reshape(nz, nc, local, strip).astype(f32), 0).reshape(nc * local, strip)

    head_part = HD // chips
    sums = jnp.concatenate(
        [
            dw_router.reshape(chips, strip * E),
            dgain_attn.reshape(chips, strip),
            dgain_moe.reshape(chips, strip),
            dgain_query.reshape(chips, head_part),
            dgain_key.reshape(chips, head_part),
        ],
        1,
    )
    sums = jnp.sum(exchange(sums, ("fsdp", "ctx")), 0)
    sums = sums + swap(sums)
    base = strip * E
    return (
        layer_out,
        tokens_grad,
        got_qkv[0],
        got_qkv[1],
        got_qkv[2],
        got_out,
        sums[base : base + strip],
        sums[base + 2 * strip : base + 2 * strip + head_part],
        sums[base + 2 * strip + head_part :],
        sums[base + strip : base + 2 * strip],
        sums[:base].reshape(strip, E),
        dw_experts,
    )


def solution(mesh):
    chips = mesh.shape["fsdp"] * mesh.shape["ctx"]
    plain = chips == E and mesh.shape["fsdp"] == 4 and mesh.shape["tp"] == 2
    return jax.shard_map(
        one_chip if plain else general,
        mesh=mesh,
        in_specs=(
            P("fsdp", "ctx", None),
            P("fsdp", "tp"),
            P("fsdp", "tp"),
            P("fsdp", "tp"),
            P("tp", "fsdp"),
            P("fsdp"),
            P("fsdp"),
            P("fsdp"),
            P("fsdp"),
            P("fsdp", None),
            P("fsdp", None, None, "tp"),
            P("fsdp", "ctx", None),
            P("fsdp", "ctx", None),
        ),
        out_specs=(
            P("fsdp", "ctx", "tp"),
            P("fsdp", "ctx", None),
            P(("fsdp", "ctx"), "tp"),
            P(("fsdp", "ctx"), "tp"),
            P(("fsdp", "ctx"), "tp"),
            P("tp", ("fsdp", "ctx")),
            P(("fsdp", "ctx")),
            P(("fsdp", "ctx")),
            P(("fsdp", "ctx")),
            P(("fsdp", "ctx")),
            P(("fsdp", "ctx"), None),
            P(("fsdp", "ctx"), None, None, "tp"),
        ),
        check_vma=False,
    )
```

```python
import functools
import math

import jax
import jax.numpy as jnp
from jax import lax
from jax.experimental import pallas as pl
from jax.experimental.pallas import tpu as pltpu
from jax.sharding import PartitionSpec as P

HD = 128
TOPK = 8
E = 16
CAP = 512
MESH = pl.DeviceIdType.MESH


EPS = 1e-06
ROPE_BASE = 10000.0


def prefix(value, axis, join, neutral):
    count, mine = (lax.axis_size(axis), lax.axis_index(axis))
    pieces = lax.all_gather(value, axis)
    running = jnp.full_like(value, 0) + jnp.asarray(neutral, value.dtype)

    def lap(position, running):
        longer = join(running, pieces[position])
        return jnp.where(position < mine, longer, running)

    return lax.fori_loop(0, count - 1, lap, running)


def rms_scale(values):
    return lax.rsqrt(jnp.mean(values * values, -1, keepdims=True) + EPS)


def norm_back(grad_normed, values, inv_rms, gain_vec):
    weighted = grad_normed * gain_vec.astype(jnp.float32)
    inner_sum = jnp.sum(weighted * values, -1, keepdims=True)
    return (
        inv_rms * weighted - values * (inv_rms * inv_rms * inv_rms) * inner_sum / values.shape[-1]
    )


def rope_tables(first, length):
    half_dim = HD // 2
    inv_freq = jnp.exp(jnp.arange(half_dim, dtype=jnp.float32) * (-2.0 * math.log(ROPE_BASE) / HD))
    places = (first + jnp.arange(length, dtype=jnp.int32)).astype(jnp.float32)
    angles = places[:, None] * inv_freq[None, :]
    cos_table = jnp.cos(angles)
    sin_table = jnp.sin(angles)
    cos_full = jnp.concatenate([cos_table, cos_table], -1)[:, None, :]
    sin_full = jnp.concatenate([sin_table, sin_table], -1)[:, None, :]
    return (cos_full, sin_full)


def rotate(values):
    half_dim = values.shape[-1] // 2
    return jnp.concatenate([-values[..., half_dim:], values[..., :half_dim]], -1)


def rotate_back(values):
    half_dim = values.shape[-1] // 2
    return jnp.concatenate([values[..., half_dim:], -values[..., :half_dim]], -1)


def apply_rope(values, cos_full, sin_full):
    return values * cos_full + rotate(values) * sin_full


def rope_back(grads, cos_full, sin_full):
    return grads * cos_full + rotate_back(grads * sin_full)


def add_counts(earlier, later):
    return earlier + later


def general(
    tokens,
    w_query,
    w_key,
    w_value,
    w_out,
    gain_attn,
    gain_query,
    gain_key,
    gain_moe,
    w_router,
    w_experts,
    routes,
    cotangent,
):
    seq_count, block_len, model_width = tokens.shape
    row_count = seq_count * block_len
    (
        full_query,
        full_key,
        full_value,
        full_out,
        router_full,
        attn_gain,
        query_gain,
        key_gain,
        moe_gain,
    ) = (
        lax.all_gather(w_query, "fsdp", axis=0, tiled=True),
        lax.all_gather(w_key, "fsdp", axis=0, tiled=True),
        lax.all_gather(w_value, "fsdp", axis=0, tiled=True),
        lax.all_gather(w_out, "fsdp", axis=1, tiled=True),
        lax.all_gather(w_router, "fsdp", axis=0, tiled=True),
        lax.all_gather(gain_attn, "fsdp", axis=0, tiled=True),
        lax.all_gather(gain_query, "fsdp", axis=0, tiled=True),
        lax.all_gather(gain_key, "fsdp", axis=0, tiled=True),
        lax.all_gather(gain_moe, "fsdp", axis=0, tiled=True),
    )
    local_width = full_query.shape[1]
    head_count = local_width // HD
    head_shape = (seq_count, block_len, head_count, HD)
    token_rows = tokens.reshape(row_count, model_width).astype(jnp.float32)
    inv_one = rms_scale(token_rows)
    normed_one = (token_rows * inv_one * attn_gain.astype(jnp.float32)).astype(jnp.bfloat16)
    query_proj = jnp.dot(normed_one, full_query, preferred_element_type=jnp.float32)
    key_proj = jnp.dot(normed_one, full_key, preferred_element_type=jnp.float32)
    value_proj = jnp.dot(normed_one, full_value, preferred_element_type=jnp.float32)
    cos_full, sin_full = rope_tables(lax.axis_index("ctx") * block_len, block_len)
    query_heads = query_proj.reshape(head_shape)
    key_heads = key_proj.reshape(head_shape)
    query_inv = rms_scale(query_heads)
    key_inv = rms_scale(key_heads)
    queries = apply_rope(
        query_heads * query_inv * query_gain.astype(jnp.float32), cos_full, sin_full
    ).astype(jnp.bfloat16)
    keys_local = apply_rope(
        key_heads * key_inv * key_gain.astype(jnp.float32), cos_full, sin_full
    ).astype(jnp.bfloat16)
    keys_local = keys_local.reshape(seq_count, block_len, local_width)
    values_local = value_proj.astype(jnp.bfloat16).reshape(seq_count, block_len, local_width)
    keys_all, values_all = (
        lax.all_gather(keys_local, "ctx", axis=1, tiled=True),
        lax.all_gather(values_local, "ctx", axis=1, tiled=True),
    )
    seq_len = keys_all.shape[1]
    key_rows = keys_all.reshape(seq_count, seq_len, head_count, HD)
    value_rows = values_all.reshape(seq_count, seq_len, head_count, HD)
    score_scale = 1.0 / math.sqrt(HD)
    scores = (
        jnp.einsum("sqhd,skhd->shqk", queries, key_rows, preferred_element_type=jnp.float32)
        * score_scale
    )
    maximum = jnp.max(scores, -1, keepdims=True)
    exp_scores = jnp.exp(scores - maximum)
    denominator = jnp.sum(exp_scores, -1, keepdims=True)
    attn_probs = exp_scores / denominator
    log_total = maximum + jnp.log(denominator)
    context = jnp.einsum(
        "shqk,skhd->sqhd",
        attn_probs.astype(jnp.bfloat16),
        value_rows,
        preferred_element_type=jnp.float32,
    )
    context = context.astype(jnp.bfloat16).reshape(row_count, local_width)
    attn_part = jnp.dot(context, full_out, preferred_element_type=jnp.float32)
    residual = token_rows + lax.psum(attn_part, "tp")
    inv_two = rms_scale(residual)
    normed_two = (residual * inv_two * moe_gain.astype(jnp.float32)).astype(jnp.bfloat16)
    logits = jnp.dot(normed_two, router_full, preferred_element_type=jnp.float32)
    router_probs = jax.nn.softmax(logits, -1)
    pair_count = block_len * TOPK
    route_rows = routes.reshape(seq_count, pair_count)
    expert_ids = jnp.arange(E, dtype=jnp.int32)
    onehot = (route_rows[:, :, None] == expert_ids[None, None, :]).astype(jnp.int32)
    counts = jnp.sum(onehot, 1, dtype=jnp.int32)
    offsets = prefix(counts, "ctx", add_counts, jnp.zeros_like(counts))
    earlier = jnp.cumsum(onehot, 1, dtype=jnp.int32) - onehot
    local_rank = jnp.sum(earlier * onehot, 2, dtype=jnp.int32)
    slot_base = jnp.sum(onehot * offsets[:, None, :], 2, dtype=jnp.int32)
    kept_mask = (slot_base + local_rank < CAP).astype(jnp.float32).reshape(row_count, TOPK)
    block_most = pair_count * 9 // (8 * E)
    expert_span = seq_count * block_most
    seq_ids = jnp.arange(seq_count, dtype=jnp.int32)[:, None]
    buffer_row = (route_rows * expert_span + seq_ids * block_most + local_rank).reshape(
        row_count * TOPK
    )
    token_ids = (
        seq_ids * block_len + jnp.arange(pair_count, dtype=jnp.int32)[None, :] // TOPK
    ).reshape(row_count * TOPK)
    owner_rows = jnp.zeros((E * expert_span,), jnp.int32).at[buffer_row].set(token_ids)
    onehot_f = onehot.astype(jnp.float32).reshape(row_count, TOPK, E)
    gate_weight = jnp.sum(onehot_f * router_probs[:, None, :], 2) * kept_mask
    slot_weight = (
        jnp.zeros((E * expert_span,), jnp.float32)
        .at[buffer_row]
        .set(gate_weight.reshape(row_count * TOPK))
    )
    expert_rows = normed_two[owner_rows].reshape(E, expert_span, model_width)
    cotan_rows = cotangent.reshape(row_count, model_width)
    grad_expert = (slot_weight[:, None] * cotan_rows[owner_rows].astype(jnp.float32)).astype(
        jnp.bfloat16
    )
    grad_expert = grad_expert.reshape(E, expert_span, model_width)
    ffn_local = w_experts.shape[3]
    fsdp_count = lax.axis_size("fsdp")
    ctx_count = lax.axis_size("ctx")
    group_count = fsdp_count * ctx_count
    sharing = group_count // E
    padded_span = -(-expert_span // sharing) * sharing
    part_span = padded_span // sharing
    target_experts = (
        jnp.arange(fsdp_count, dtype=jnp.int32) * ctx_count + lax.axis_index("ctx")
    ) // sharing
    selected = jnp.take(w_experts, target_experts, axis=2)
    owned = lax.all_to_all(selected, "fsdp", split_axis=2, concat_axis=0, tiled=True)[:, :, 0]
    send_rows = expert_rows.reshape(group_count, part_span, model_width)
    send_grads = grad_expert.reshape(group_count, part_span, model_width)
    recv_rows, recv_grads = (
        lax.all_to_all(send_rows, ("fsdp", "ctx"), split_axis=0, concat_axis=0, tiled=True),
        lax.all_to_all(send_grads, ("fsdp", "ctx"), split_axis=0, concat_axis=0, tiled=True),
    )
    rows_flat = recv_rows.reshape(group_count * part_span, model_width)
    grads_flat = recv_grads.reshape(group_count * part_span, model_width)
    gate_act = jnp.dot(rows_flat, owned[:, 0], preferred_element_type=jnp.float32)
    up_act = jnp.dot(rows_flat, owned[:, 1], preferred_element_type=jnp.float32)
    sigmoid_gate = jax.nn.sigmoid(gate_act)
    silu_gate = gate_act * sigmoid_gate
    hidden = (silu_gate * up_act).astype(jnp.bfloat16)
    produced = jnp.einsum("mf,df->md", hidden, owned[:, 2], preferred_element_type=jnp.float32)
    grad_hidden = jnp.dot(grads_flat, owned[:, 2], preferred_element_type=jnp.float32)
    grad_gate = (
        grad_hidden * up_act * sigmoid_gate * (1.0 + gate_act * (1.0 - sigmoid_gate))
    ).astype(jnp.bfloat16)
    grad_up = (grad_hidden * silu_gate).astype(jnp.bfloat16)
    rows_grad = jnp.einsum("mf,df->md", grad_gate, owned[:, 0], preferred_element_type=jnp.float32)
    rows_grad = rows_grad + jnp.einsum(
        "mf,df->md", grad_up, owned[:, 1], preferred_element_type=jnp.float32
    )
    back_out, back_rows = (
        lax.all_to_all(
            produced.reshape(group_count, part_span, model_width).astype(jnp.bfloat16),
            ("fsdp", "ctx"),
            split_axis=0,
            concat_axis=0,
            tiled=True,
        ).astype(jnp.float32),
        lax.all_to_all(
            rows_grad.reshape(group_count, part_span, model_width).astype(jnp.bfloat16),
            ("fsdp", "ctx"),
            split_axis=0,
            concat_axis=0,
            tiled=True,
        ).astype(jnp.float32),
    )
    expert_out = back_out.reshape(E, padded_span, model_width)
    grad_rows = back_rows.reshape(E, padded_span, model_width)
    gate_term = jnp.einsum("md,mf->df", rows_flat, grad_gate, preferred_element_type=jnp.float32)
    up_term = jnp.einsum("md,mf->df", rows_flat, grad_up, preferred_element_type=jnp.float32)
    down_term = jnp.einsum("md,mf->df", grads_flat, hidden, preferred_element_type=jnp.float32)
    owner_terms = jnp.stack([gate_term, up_term, down_term], 1)[:, :, None, :]
    relaid = lax.all_to_all(
        owner_terms.astype(jnp.bfloat16), ("fsdp", "ctx"), split_axis=0, concat_axis=2, tiled=True
    ).astype(owner_terms.dtype)
    dw_experts = jnp.sum(relaid.reshape(relaid.shape[0], 3, E, sharing, ffn_local), 3)
    picked = expert_out.reshape(E * expert_span, model_width)[buffer_row].reshape(
        row_count, TOPK, model_width
    )
    moe_part = jnp.sum(gate_weight[:, :, None] * picked, 1)
    cotan_float = cotan_rows.astype(jnp.float32)
    grad_gate_part = jnp.sum(picked * cotan_float[:, None, :], 2)
    moe_shard = lax.psum_scatter(
        moe_part.astype(jnp.bfloat16), "tp", scatter_dimension=1, tiled=True
    ).astype(jnp.float32)
    piece_width = moe_shard.shape[1]
    residual_shard = lax.dynamic_slice_in_dim(
        residual, lax.axis_index("tp") * piece_width, piece_width, 1
    )
    layer_out = (
        (residual_shard + moe_shard).astype(jnp.bfloat16).reshape(seq_count, block_len, piece_width)
    )
    grad_normed_part = jnp.sum(
        grad_rows.reshape(E * expert_span, model_width)[buffer_row].reshape(
            row_count, TOPK, model_width
        ),
        1,
    )
    grad_normed_sum, grad_gate_sum = (
        lax.psum(grad_normed_part.astype(jnp.bfloat16), "tp").astype(jnp.float32),
        lax.psum(grad_gate_part.astype(jnp.bfloat16), "tp").astype(jnp.float32),
    )
    grad_pick = grad_gate_sum * kept_mask
    grad_router_probs = jnp.sum(onehot_f * grad_pick[:, :, None], 1)
    grad_logits = router_probs * (
        grad_router_probs - jnp.sum(router_probs * grad_router_probs, -1, keepdims=True)
    )
    grad_logits = grad_logits.astype(jnp.bfloat16)
    grad_router_w = jnp.einsum(
        "nd,ne->de", normed_two, grad_logits, preferred_element_type=jnp.float32
    )
    grad_normed_two = grad_normed_sum + jnp.einsum(
        "ne,de->nd", grad_logits, router_full, preferred_element_type=jnp.float32
    )
    grad_moe_gain = jnp.sum(grad_normed_two * residual * inv_two, 0)
    grad_residual = cotan_float + norm_back(grad_normed_two, residual, inv_two, moe_gain)
    grad_attn = grad_residual.astype(jnp.bfloat16)
    grad_w_out = jnp.einsum("nl,nd->ld", context, grad_attn, preferred_element_type=jnp.float32)
    grad_context = jnp.einsum("nd,ld->nl", grad_attn, full_out, preferred_element_type=jnp.float32)
    grad_context = grad_context.astype(jnp.bfloat16).reshape(head_shape)
    scores = (
        jnp.einsum("sqhd,skhd->shqk", queries, key_rows, preferred_element_type=jnp.float32)
        * score_scale
    )
    attn_probs = jnp.exp(scores - log_total)
    grad_probs = jnp.einsum(
        "sqhd,skhd->shqk", grad_context, value_rows, preferred_element_type=jnp.float32
    )
    grad_scores = attn_probs * (grad_probs - jnp.sum(attn_probs * grad_probs, -1, keepdims=True))
    grad_scores = grad_scores.astype(jnp.bfloat16)
    grad_queries = (
        jnp.einsum("shqk,skhd->sqhd", grad_scores, key_rows, preferred_element_type=jnp.float32)
        * score_scale
    )
    grad_keys_all = (
        jnp.einsum("shqk,sqhd->skhd", grad_scores, queries, preferred_element_type=jnp.float32)
        * score_scale
    )
    grad_values_all = jnp.einsum(
        "shqk,sqhd->skhd",
        attn_probs.astype(jnp.bfloat16),
        grad_context,
        preferred_element_type=jnp.float32,
    )
    grad_keys_own, grad_values_own = (
        lax.psum_scatter(
            grad_keys_all.reshape(seq_count, seq_len, local_width).astype(jnp.bfloat16),
            "ctx",
            scatter_dimension=1,
            tiled=True,
        ).astype(jnp.float32),
        lax.psum_scatter(
            grad_values_all.reshape(seq_count, seq_len, local_width).astype(jnp.bfloat16),
            "ctx",
            scatter_dimension=1,
            tiled=True,
        ).astype(jnp.float32),
    )
    grad_qnormed = rope_back(grad_queries, cos_full, sin_full)
    grad_knormed = rope_back(grad_keys_own.reshape(head_shape), cos_full, sin_full)
    grad_qgain = jnp.sum(grad_qnormed * query_heads * query_inv, (0, 1, 2))
    grad_kgain = jnp.sum(grad_knormed * key_heads * key_inv, (0, 1, 2))
    grad_qproj = (
        norm_back(grad_qnormed, query_heads, query_inv, query_gain)
        .astype(jnp.bfloat16)
        .reshape(row_count, local_width)
    )
    grad_kproj = (
        norm_back(grad_knormed, key_heads, key_inv, key_gain)
        .astype(jnp.bfloat16)
        .reshape(row_count, local_width)
    )
    grad_vproj = grad_values_own.astype(jnp.bfloat16).reshape(row_count, local_width)
    grad_wq = jnp.einsum("nd,nl->dl", normed_one, grad_qproj, preferred_element_type=jnp.float32)
    grad_wk = jnp.einsum("nd,nl->dl", normed_one, grad_kproj, preferred_element_type=jnp.float32)
    grad_wv = jnp.einsum("nd,nl->dl", normed_one, grad_vproj, preferred_element_type=jnp.float32)
    grad_normed_one = jnp.einsum(
        "nl,dl->nd", grad_qproj, full_query, preferred_element_type=jnp.float32
    )
    grad_normed_one = grad_normed_one + jnp.einsum(
        "nl,dl->nd", grad_kproj, full_key, preferred_element_type=jnp.float32
    )
    grad_normed_one = grad_normed_one + jnp.einsum(
        "nl,dl->nd", grad_vproj, full_value, preferred_element_type=jnp.float32
    )
    grad_normed_one, grad_qgain, grad_kgain = (
        lax.psum(grad_normed_one.astype(jnp.bfloat16), "tp").astype(jnp.float32),
        lax.psum(grad_qgain.astype(jnp.bfloat16), "tp").astype(jnp.float32),
        lax.psum(grad_kgain.astype(jnp.bfloat16), "tp").astype(jnp.float32),
    )
    grad_attn_gain = jnp.sum(grad_normed_one * token_rows * inv_one, 0)
    tokens_grad = grad_residual + norm_back(grad_normed_one, token_rows, inv_one, attn_gain)
    tokens_grad = tokens_grad.astype(jnp.bfloat16).reshape(seq_count, block_len, model_width)
    dw_query, dw_key, dw_value, dw_out, dw_router, dgain_attn, dgain_query, dgain_key, dgain_moe = (
        lax.psum_scatter(grad_wq, ("fsdp", "ctx"), scatter_dimension=0, tiled=True),
        lax.psum_scatter(grad_wk, ("fsdp", "ctx"), scatter_dimension=0, tiled=True),
        lax.psum_scatter(grad_wv, ("fsdp", "ctx"), scatter_dimension=0, tiled=True),
        lax.psum_scatter(grad_w_out, ("fsdp", "ctx"), scatter_dimension=1, tiled=True),
        lax.psum_scatter(grad_router_w, ("fsdp", "ctx"), scatter_dimension=0, tiled=True),
        lax.psum_scatter(grad_attn_gain, ("fsdp", "ctx"), scatter_dimension=0, tiled=True),
        lax.psum_scatter(grad_qgain, ("fsdp", "ctx"), scatter_dimension=0, tiled=True),
        lax.psum_scatter(grad_kgain, ("fsdp", "ctx"), scatter_dimension=0, tiled=True),
        lax.psum_scatter(grad_moe_gain, ("fsdp", "ctx"), scatter_dimension=0, tiled=True),
    )
    return (
        layer_out,
        tokens_grad,
        dw_query,
        dw_key,
        dw_value,
        dw_out,
        dgain_attn,
        dgain_query,
        dgain_key,
        dgain_moe,
        dw_router,
        dw_experts,
    )


def swap(value):
    return lax.ppermute(value, "tp", [(0, 1), (1, 0)])


def exchange(value, axes):
    return lax.all_to_all(value, axes, split_axis=0, concat_axis=0, tiled=True)


def spread(value, axes):
    count = lax.axis_size(axes)
    return exchange(jnp.broadcast_to(value[None], (count,) + value.shape), axes)


def dot(left, right):
    return jnp.dot(left, right, preferred_element_type=jnp.float32)


def dot_nt(left, right):
    return lax.dot_general(left, right, (((1,), (1,)), ((), ())), preferred_element_type=jnp.float32)


def dot_tn(left, right):
    return lax.dot_general(left, right, (((0,), (0,)), ((), ())), preferred_element_type=jnp.float32)


def two_parts(values):
    high = values.astype(jnp.bfloat16)
    low = (values - high.astype(jnp.float32)).astype(jnp.bfloat16)
    return (high, low)


def by_core(mine, other, core):
    return jnp.where(core == 0, jnp.stack([mine, other]), jnp.stack([other, mine]))


def remote(src, dst, send, recv, **where):
    return pltpu.make_async_remote_copy(
        src_ref=src, dst_ref=dst, send_sem=send, recv_sem=recv, device_id=where, device_id_type=MESH
    )


def places():
    return lax.axis_index("fsdp"), lax.axis_index("ctx"), lax.axis_index("tp")


def ring(index, step, count):
    return lax.rem(index + step + count, count)


def greet(nz, nc, line):
    z, c, t = places()
    barrier = pltpu.get_barrier_semaphore()

    def tell(**where):
        pl.semaphore_signal(barrier, inc=1, device_id=where, device_id_type=MESH)

    if line:
        for step in range(1, nz):
            tell(fsdp=ring(z, step, nz))
        count = nz - 1
    else:
        pl.when(z > 0)(lambda: tell(fsdp=z - 1))
        pl.when(z < nz - 1)(lambda: tell(fsdp=z + 1))
        count = jnp.where(z > 0, 1, 0) + jnp.where(z < nz - 1, 1, 0)
    for step in range(1, nc):
        tell(ctx=ring(c, step, nc))
    tell(tp=1 - t)
    pl.semaphore_wait(barrier, count + nc)


def line_copies(bufs, send_sem, recv_sem, way, step, shard, target):
    return [
        remote(buf.at[shard], buf.at[shard], send_sem.at[way, step, k], recv_sem.at[way, step, k], fsdp=target)
        for k, buf in enumerate(bufs)
    ]


def line_gather(nz, bufs, send_sem, recv_sem, arrived):
    z = lax.axis_index("fsdp")
    for step in range(nz - 1):

        @pl.when((z < nz - 1) & (z >= step))
        def _():
            for copy in line_copies(bufs, send_sem, recv_sem, 0, step, z - step, z + 1):
                copy.start()

        @pl.when((z > 0) & (z + step < nz))
        def _():
            for copy in line_copies(bufs, send_sem, recv_sem, 1, step, z + step, z - 1):
                copy.start()

        @pl.when(z - 1 >= step)
        def _():
            for copy in line_copies(bufs, send_sem, recv_sem, 0, step, z - 1 - step, z - 1):
                copy.wait_recv()
            arrived(z - 1 - step)

        @pl.when(z + 1 + step < nz)
        def _():
            for copy in line_copies(bufs, send_sem, recv_sem, 1, step, z + 1 + step, z + 1):
                copy.wait_recv()
            arrived(z + 1 + step)

    for step in range(nz - 1):

        @pl.when((z < nz - 1) & (z >= step))
        def _():
            for copy in line_copies(bufs, send_sem, recv_sem, 0, step, z - step, z + 1):
                copy.wait_send()

        @pl.when((z > 0) & (z + step < nz))
        def _():
            for copy in line_copies(bufs, send_sem, recv_sem, 1, step, z + step, z - 1):
                copy.wait_send()


def regroup(shard, t, rows, line, two, keep_sem, give_send, give_recv, start):
    slot = lax.rem(shard, 2)
    band = pl.ds(pl.multiple_of(t * rows, rows), rows)

    def keep():
        pltpu.make_async_copy(line.at[shard], two.at[slot, band], keep_sem.at[slot]).start()

    def give():
        remote(line.at[shard], two.at[slot, band], give_send.at[slot], give_recv.at[slot], tp=1 - t).start()

    pl.when(shard // 2 == t)(keep)
    pl.when(shard // 2 != t)(give)


def load_kernel(
    nz, nc, tok, cot, wq, wk, wv, wo, small,
    x_all, w_qkv, w_o, small_all, cot_line, cot_two, routes_seq,
    own_sem, line_send, line_recv, tok_send, tok_recv, pass_send, pass_recv,
    route_send, route_recv, keep_sem, give_send, give_recv,
):
    z, c, t = places()
    block = tok.shape[0]
    rows = block // 2
    local = w_qkv.shape[2] // 3
    kinds = routes_seq.shape[1]
    first = small.shape[0] - kinds
    half = pl.ds(pl.multiple_of(t * rows, rows), rows)
    column = pl.ds(pl.multiple_of(c * local, local), local)
    own = [
        pltpu.make_async_copy(w.at[:, column], w_qkv.at[z, :, pl.ds(k * local, local)], own_sem.at[k])
        for k, w in enumerate((wq, wk, wv))
    ]
    own += [
        pltpu.make_async_copy(wo.at[column], w_o.at[z], own_sem.at[3]),
        pltpu.make_async_copy(small, small_all.at[z], own_sem.at[4]),
        pltpu.make_async_copy(cot.at[half], cot_line.at[z], own_sem.at[5]),
        pltpu.make_async_copy(tok, x_all.at[pl.ds(pl.multiple_of(c * block, block), block)], own_sem.at[6]),
        pltpu.make_async_copy(small.at[pl.ds(first, kinds)], routes_seq.at[c], own_sem.at[7]),
    ]
    for copy in own:
        copy.start()
    greet(nz, nc, False)

    def band(source, core):
        return x_all.at[pl.ds(pl.multiple_of(source * block + core * rows, rows), rows)]

    def token_copy(step, source, target):
        return remote(tok.at[half], band(source, t), tok_send.at[step], tok_recv.at[step], ctx=target)

    def pass_copy(step, source, core):
        return remote(band(source, core), band(source, core), pass_send.at[step], pass_recv.at[step], tp=1 - t)

    def route_copy(step, source, target):
        return remote(
            small.at[pl.ds(first, kinds)], routes_seq.at[source], route_send.at[step], route_recv.at[step], ctx=target
        )

    for step in range(1, nc):
        token_copy(step - 1, c, ring(c, step, nc)).start()
        route_copy(step - 1, c, ring(c, step, nc)).start()
    for copy in own:
        copy.wait()

    def arrived(shard):
        regroup(shard, t, rows, cot_line, cot_two, keep_sem, give_send, give_recv, True)

    arrived(z)

    def later(shard):
        arrived(shard)

    line_gather(nz, (w_qkv, w_o, small_all, cot_line), line_send, line_recv, later)
    for step in range(1, nc):
        source = ring(c, -step, nc)
        token_copy(step - 1, source, source).wait_recv()
        pass_copy(step - 1, source, t).start()
        route_copy(step - 1, source, source).wait_recv()
    for step in range(1, nc):
        source = ring(c, -step, nc)
        pass_copy(step - 1, source, 1 - t).wait_recv()
        pass_copy(step - 1, source, t).wait_send()
        token_copy(step - 1, c, source).wait_send()
        route_copy(step - 1, c, source).wait_send()
    finish_regroup(t, rows, cot_line, cot_two, keep_sem, give_send, give_recv)


def finish_regroup(t, rows, line, two, keep_sem, give_send, give_recv):
    for slot in range(2):
        wait_two(slot, t, rows, line, two, keep_sem, give_recv)
        band = pl.ds(pl.multiple_of(t * rows, rows), rows)
        remote(line.at[0], two.at[slot, band], give_send.at[slot], give_recv.at[slot], tp=1 - t).wait_send()


def wait_two(slot, t, rows, line, two, keep_sem, give_recv):
    band = pl.ds(pl.multiple_of(t * rows, rows), rows)
    other = pl.ds(pl.multiple_of((1 - t) * rows, rows), rows)
    pltpu.make_async_copy(line.at[0], two.at[slot, band], keep_sem.at[slot]).wait()
    remote(line.at[0], two.at[slot, other], give_recv.at[slot], give_recv.at[slot], tp=1 - t).wait_recv()


def load(tok, cot, wq, wk, wv, wo, small, kinds):
    nz, nc = lax.axis_size("fsdp"), lax.axis_size("ctx")
    block, width = tok.shape
    deep, local = wq.shape[0], wq.shape[1] // nc
    rows = block // 2
    dma = pltpu.SemaphoreType.DMA
    bf16 = jnp.bfloat16
    shapes = [
        (nc * block, width),
        (nz, deep, 3 * local),
        (nz, local, wo.shape[1]),
        (nz,) + small.shape,
        (nz, rows, width),
        (2, block, width),
        (nc, kinds, 128),
    ]
    return pl.pallas_call(
        functools.partial(load_kernel, nz, nc),
        out_shape=[jax.ShapeDtypeStruct(shape, bf16) for shape in shapes],
        in_specs=[pl.BlockSpec(memory_space=pl.ANY)] * 7,
        out_specs=[pl.BlockSpec(memory_space=pltpu.VMEM)] * 7,
        scratch_shapes=[
            dma((8,)),
            dma((2, nz - 1, 4)), dma((2, nz - 1, 4)),
            dma((nc - 1,)), dma((nc - 1,)), dma((nc - 1,)), dma((nc - 1,)), dma((nc - 1,)), dma((nc - 1,)),
            dma((2,)), dma((2,)), dma((2,)),
        ],
        compiler_params=pltpu.CompilerParams(
            collective_id=0, has_side_effects=True, vmem_limit_bytes=40 * 2**20
        ),
    )(tok, cot, wq, wk, wv, wo, small)


def dispatch_kernel(
    nz, nc, part, tok, gain, router, kept, pick, cot_two,
    residual, normed, probs, x_in, g_in, cot_in,
    sib, rs_send, rs_recv, n_line, g_line, n_two, g_two, x_send, g_send, cot_send,
    sib_s, sib_r, rs_s, rs_r, line_send, line_recv, keep_sem, give_send, give_recv,
    gkeep_sem, ggive_send, ggive_recv, x_s, x_r, g_s, g_r, cot_s, cot_r, own_sem,
):
    z, c, t = places()
    f32, bf16 = jnp.float32, jnp.bfloat16
    rows, width = residual.shape
    most = x_in.shape[2]
    greet(nz, nc, False)

    def sib_copy(q):
        return remote(part.at[q, 1 - t], sib.at[q], sib_s.at[q], sib_r.at[q], tp=1 - t)

    def rs_copy(step, source, target):
        return remote(rs_send.at[step], rs_recv.at[step], rs_s.at[step], rs_r.at[step], ctx=target)

    for step in range(1, nc + 1):
        sib_copy(ring(c, step, nc)).start()
    chunk = 16
    for step in range(1, nc):
        q = ring(c, step, nc)
        sib_copy(q).wait_recv()

        @pl.loop(0, rows // chunk)
        def _(k):
            at = pl.ds(pl.multiple_of(k * chunk, chunk), chunk)
            rs_send[step - 1, at, :] = (part[q, t, at, :].astype(f32) + sib[q, at, :].astype(f32)).astype(bf16)

        rs_copy(step - 1, c, q).start()

    def picked(slot, source, out, out_at):
        lanes = out.shape[-1]
        piece = min(lanes, 512)

        @pl.loop(0, lanes // piece)
        def _(k):
            at = pl.ds(pl.multiple_of(k * piece, piece), piece)
            out[out_at, :, at] = jnp.dot(
                pick[slot], source[slot, :, at], preferred_element_type=f32
            ).astype(bf16)

    def send_copy(slot, step, src, dst, send, recv, source, target):
        return remote(
            src.at[slot, pl.ds(pl.multiple_of(target * most, 16), most)],
            dst.at[source, slot],
            send.at[slot, step - 1],
            recv.at[slot, step - 1],
            ctx=target,
        )

    def own_copy(slot, src, dst, k):
        return pltpu.make_async_copy(
            src.at[slot, pl.ds(pl.multiple_of(c * most, 16), most)], dst.at[c, slot], own_sem.at[k, slot]
        )

    for slot in range(2):
        picked(slot, cot_two, cot_send, slot)
        for step in range(1, nc):
            send_copy(slot, step, cot_send, cot_in, cot_s, cot_r, c, ring(c, step, nc)).start()
        own_copy(slot, cot_send, cot_in, 0).start()

    sib_copy(c).wait_recv()
    for step in range(1, nc):
        rs_copy(step - 1, c, c).wait_recv()

    @pl.loop(0, rows // chunk)
    def _(k):
        at = pl.ds(pl.multiple_of(k * chunk, chunk), chunk)
        start = pl.ds(pl.multiple_of(t * rows + k * chunk, chunk), chunk)
        total = part[c, t, at, :].astype(f32) + sib[c, at, :].astype(f32)
        for step in range(nc - 1):
            total = total + rs_recv[step, at, :].astype(f32)
        total = total + tok[start, :].astype(f32)
        residual[at, :] = total
        inv = lax.rsqrt(jnp.mean(total * total, -1, keepdims=True) + EPS)
        row = (total * inv * gain[...]).astype(bf16)
        normed[at, :] = row
        n_line[z, at, :] = row

    logits = lax.dot_general(
        normed[...], router[...], (((1,), (1,)), ((), ())), preferred_element_type=f32
    )
    lane = lax.broadcasted_iota(jnp.int32, logits.shape, 1)
    logits = jnp.where(lane < E, logits, -jnp.inf)
    top = jnp.max(logits, -1, keepdims=True)
    raised = jnp.exp(logits - top)
    prob = raised / jnp.sum(raised, -1, keepdims=True)
    probs[...] = prob
    gates = prob * kept[...]
    high = gates.astype(bf16)
    g_line[z, :, pl.ds(0, 128)] = high
    g_line[z, :, pl.ds(128, 128)] = (gates - high.astype(f32)).astype(bf16)

    def arrived(shard):
        regroup(shard, t, rows, n_line, n_two, keep_sem, give_send, give_recv, True)
        regroup(shard, t, rows, g_line, g_two, gkeep_sem, ggive_send, ggive_recv, True)

    arrived(z)
    line_gather(nz, (n_line, g_line), line_send, line_recv, arrived)
    for slot in range(2):
        wait_two(slot, t, rows, n_line, n_two, keep_sem, give_recv)
        wait_two(slot, t, rows, g_line, g_two, gkeep_sem, ggive_recv)
        picked(slot, n_two, x_send, slot)
        picked(slot, g_two, g_send, slot)
        for step in range(1, nc):
            send_copy(slot, step, x_send, x_in, x_s, x_r, c, ring(c, step, nc)).start()
            send_copy(slot, step, g_send, g_in, g_s, g_r, c, ring(c, step, nc)).start()
        own_copy(slot, x_send, x_in, 1).start()
        own_copy(slot, g_send, g_in, 2).start()

    band = pl.ds(pl.multiple_of(t * rows, rows), rows)
    for slot in range(2):
        remote(n_line.at[0], n_two.at[slot, band], give_send.at[slot], give_recv.at[slot], tp=1 - t).wait_send()
        remote(g_line.at[0], g_two.at[slot, band], ggive_send.at[slot], ggive_recv.at[slot], tp=1 - t).wait_send()
        own_copy(slot, cot_send, cot_in, 0).wait()
        own_copy(slot, x_send, x_in, 1).wait()
        own_copy(slot, g_send, g_in, 2).wait()
        for step in range(1, nc):
            source = ring(c, -step, nc)
            for src, dst, s, r in (
                (cot_send, cot_in, cot_s, cot_r),
                (x_send, x_in, x_s, x_r),
                (g_send, g_in, g_s, g_r),
            ):
                copy = send_copy(slot, step, src, dst, s, r, source, source)
                copy.wait_recv()
                copy.wait_send()
    for step in range(1, nc):
        rs_copy(step - 1, c, c).wait_send()
    for step in range(nc):
        sib_copy(step).wait_send()


def dispatch(part, tok, gain, router, kept, pick, cot_two):
    nz, nc = lax.axis_size("fsdp"), lax.axis_size("ctx")
    rows, width = part.shape[2], part.shape[3]
    block = rows * 2
    most = pick.shape[1] // nc
    dma = pltpu.SemaphoreType.DMA
    bf16, f32 = jnp.bfloat16, jnp.float32
    vmem = pl.BlockSpec(memory_space=pltpu.VMEM)
    hbm = pl.BlockSpec(memory_space=pl.ANY)
    return pl.pallas_call(
        functools.partial(dispatch_kernel, nz, nc),
        out_shape=[
            jax.ShapeDtypeStruct((rows, width), f32),
            jax.ShapeDtypeStruct((rows, width), bf16),
            jax.ShapeDtypeStruct((rows, 128), f32),
            jax.ShapeDtypeStruct((nc, 2, most, width), bf16),
            jax.ShapeDtypeStruct((nc, 2, most, 256), bf16),
            jax.ShapeDtypeStruct((nc, 2, most, width), bf16),
        ],
        in_specs=[vmem] * 7,
        out_specs=[vmem] * 3 + [hbm] * 3,
        scratch_shapes=[
            pltpu.VMEM((nc, rows, width), bf16),
            pltpu.VMEM((nc - 1, rows, width), bf16),
            pltpu.VMEM((nc - 1, rows, width), bf16),
            pltpu.VMEM((nz, rows, width), bf16),
            pltpu.VMEM((nz, rows, 256), bf16),
            pltpu.VMEM((2, block, width), bf16),
            pltpu.VMEM((2, block, 256), bf16),
            pltpu.VMEM((2, nc * most, width), bf16),
            pltpu.VMEM((2, nc * most, 256), bf16),
            pltpu.VMEM((2, nc * most, width), bf16),
            dma((nc,)), dma((nc,)), dma((nc - 1,)), dma((nc - 1,)),
            dma((2, nz - 1, 2)), dma((2, nz - 1, 2)),
            dma((2,)), dma((2,)), dma((2,)), dma((2,)), dma((2,)), dma((2,)),
            dma((2, nc - 1)), dma((2, nc - 1)), dma((2, nc - 1)), dma((2, nc - 1)), dma((2, nc - 1)), dma((2, nc - 1)),
            dma((3, 2)),
        ],
        compiler_params=pltpu.CompilerParams(
            collective_id=1, has_side_effects=True, vmem_limit_bytes=56 * 2**20
        ),
    )(part, tok, gain, router, kept, pick, cot_two)


def half_rows_sum(partial, core):
    mine = lax.dynamic_index_in_dim(partial, core, 1, keepdims=False)
    received = swap(lax.dynamic_index_in_dim(partial, 1 - core, 1, keepdims=False))
    summed = (mine.astype(jnp.float32) + received.astype(jnp.float32)).astype(jnp.bfloat16)
    pieces = exchange(summed, "ctx")
    return jnp.sum(pieces.astype(jnp.float32), 0)


def all_rows(half, core):
    mine = spread(half, "ctx")
    return by_core(mine, swap(mine), core).transpose(1, 0, 2, 3)


def one_chip(
    tokens,
    w_query,
    w_key,
    w_value,
    w_out,
    gain_attn,
    gain_query,
    gain_key,
    gain_moe,
    w_router,
    w_experts,
    routes,
    cotangent,
):
    z, c, t = lax.axis_index("fsdp"), lax.axis_index("ctx"), lax.axis_index("tp")
    nz, nc = lax.axis_size("fsdp"), lax.axis_size("ctx")
    block, width = tokens.shape[1], tokens.shape[2]
    rows = block // 2
    tall = block * nc
    deep = width // nz
    ffn = w_experts.shape[3]
    most = block * TOPK * 9 // (8 * E)
    bf16, f32 = jnp.bfloat16, jnp.float32

    token_half = lax.dynamic_slice_in_dim(tokens[0], t * rows, rows, 0)
    cotan_half = lax.dynamic_slice_in_dim(cotangent[0], t * rows, rows, 0)
    local = w_query.shape[1] // nc
    small = jnp.concatenate([w_router.T.reshape(-1), gain_attn, gain_moe, gain_query, gain_key])
    total = small.shape[0]
    small = jnp.pad(small, (0, -total % 2048))
    kinds = block * TOPK // 128
    small = jnp.concatenate([small, routes.reshape(-1).astype(bf16)]).reshape(-1, 128)
    x_rows, w_qkv, w_o, small, _, cot_two, routes_seq = load(
        tokens[0], cotangent[0], w_query, w_key, w_value, w_out, small, kinds
    )
    w_qkv = w_qkv.reshape(width, 3 * local)
    w_o = w_o.transpose(1, 0, 2).reshape(local, width)
    routes_line = small[:, small.shape[1] - kinds :].reshape(nz, block, TOPK)
    routes_seq = routes_seq.reshape(tall, TOPK)
    small = small.reshape(nz, -1)
    router = small[:, : E * deep].reshape(nz, E, deep).transpose(1, 0, 2).reshape(E, width)
    at = E * deep
    attn_gain = small[:, at : at + deep].reshape(-1).astype(f32)
    moe_gain = small[:, at + deep : at + 2 * deep].reshape(-1).astype(f32)
    at, part = at + 2 * deep, HD // nz
    query_gain = small[:, at : at + part].reshape(-1).astype(f32)
    key_gain = small[:, at + part : at + 2 * part].reshape(-1).astype(f32)

    own = lax.dynamic_slice_in_dim(w_experts, c * nz, nz, 2).transpose(2, 1, 0, 3)
    own, w_qkv = lax.optimization_barrier((own, w_qkv))
    moved = exchange(own, "fsdp").transpose(1, 0, 2, 3)
    mats = [moved[k].reshape(width, ffn) for k in range(3)]
    others = [swap(m) for m in mats]
    halves = [mats, others]

    ids = jnp.arange(E, dtype=jnp.int32)
    own_seq = jnp.any(routes_seq[:, :, None] == ids.astype(bf16), 1).astype(jnp.int32)
    slot = jnp.cumsum(own_seq, 0) - own_seq
    kept_seq = (own_seq * (slot < CAP)).astype(f32)
    kept = lax.dynamic_slice_in_dim(kept_seq, c * block + t * rows, rows, 0)
    line = lax.dynamic_slice_in_dim(routes_line, t * 2, 2, 0)
    plane = (jnp.arange(nc, dtype=jnp.int32) * nz + z).astype(bf16)
    line = jnp.any(line[..., None] == plane, 2).astype(jnp.int32)
    rank = jnp.cumsum(line, 1) - line
    pick = (rank[..., None] == jnp.arange(most, dtype=jnp.int32)) & (line[..., None] > 0)
    pick = pick.transpose(0, 2, 3, 1).reshape(2, nc * most, block).astype(bf16)

    x_rows = x_rows.astype(f32)
    place = jnp.arange(tall, dtype=jnp.int32)
    half_dim = HD // 2
    inv_freq = jnp.exp(jnp.arange(half_dim, dtype=f32) * (-2.0 * math.log(ROPE_BASE) / HD))
    angles = place.astype(f32)[:, None] * inv_freq[None, :]
    cos_full = jnp.concatenate([jnp.cos(angles)] * 2, -1)[:, None, :]
    sin_full = jnp.concatenate([jnp.sin(angles)] * 2, -1)[:, None, :]
    normed_one = (x_rows * rms_scale(x_rows) * attn_gain).astype(bf16)
    proj = dot(normed_one, w_qkv).reshape(tall, 3, local // HD, HD)
    query_heads, key_heads = proj[:, 0], proj[:, 1]
    values = proj[:, 2].astype(bf16)
    query_inv, key_inv = rms_scale(query_heads), rms_scale(key_heads)
    queries = apply_rope(query_heads * query_inv * query_gain, cos_full, sin_full).astype(bf16)
    keys = apply_rope(key_heads * key_inv * key_gain, cos_full, sin_full).astype(bf16)
    score_scale = 1.0 / math.sqrt(HD)
    scores = jnp.einsum("qhd,khd->hqk", queries, keys, preferred_element_type=f32) * score_scale
    maximum = jnp.max(scores, -1, keepdims=True)
    exp_scores = jnp.exp(scores - maximum)
    denominator = jnp.sum(exp_scores, -1, keepdims=True)
    attn_probs = exp_scores / denominator
    log_total = maximum + jnp.log(denominator)
    context = jnp.einsum("hqk,khd->qhd", attn_probs.astype(bf16), values, preferred_element_type=f32)
    context = context.astype(bf16).reshape(tall, local)
    attn_part = dot(context, w_o).astype(bf16).reshape(nc, 2, rows, width)
    kept_wide = jnp.pad(kept, ((0, 0), (0, 128 - E)))
    router_wide = jnp.pad(router, ((0, 128 - E), (0, 0)))
    residual, normed_two, router_probs, x_in, g_in, cot_rows = dispatch(
        attn_part, tokens[0], moe_gain[None], router_wide, kept_wide, pick, cot_two
    )
    router_probs = router_probs[:, :E]
    own_tokens = token_half.astype(f32)
    inv_two = rms_scale(residual)
    x_in = x_in.reshape(nc * 2 * most, width)
    cot_rows = cot_rows.reshape(nc * 2 * most, width)
    g_in = g_in.reshape(nc * 2 * most, 2, 128)[:, :, :E].astype(f32)
    mine_id = c * nz + z
    weight = jnp.sum(jnp.where(ids == mine_id, g_in, 0.0), (1, 2))[:, None]

    out_rows = back_rows = 0.0
    pair_grad = 0.0
    updates = []
    for w_gate, w_up, w_down in halves:
        gate_act = dot(x_in, w_gate)
        up_act = dot(x_in, w_up)
        grad_out = dot(cot_rows, w_down)
        sig = jax.nn.sigmoid(gate_act)
        silu = gate_act * sig
        hidden = silu * up_act
        pair_grad = pair_grad + jnp.sum(hidden.astype(bf16).astype(f32) * grad_out, 1, keepdims=True)
        weighted = (weight * hidden).astype(bf16)
        grad_hidden = weight * grad_out
        grad_gate = (grad_hidden * up_act * sig * (1.0 + gate_act * (1.0 - sig))).astype(bf16)
        grad_up = (grad_hidden * silu).astype(bf16)
        out_rows = out_rows + dot_nt(weighted, w_down)
        back_rows = back_rows + dot_nt(grad_gate, w_gate) + dot_nt(grad_up, w_up)
        updates.append((dot_tn(x_in, grad_gate), dot_tn(x_in, grad_up), dot_tn(cot_rows, weighted)))
    own_updates, other_updates = updates
    high, low = two_parts(jnp.where(ids == mine_id, pair_grad, 0.0))
    tail = jnp.zeros((high.shape[0], 128 - 2 * E), bf16)
    reply = jnp.concatenate([out_rows.astype(bf16), back_rows.astype(bf16), high, low, tail], 1)

    def collect(reply):
        reply = exchange(reply.reshape(nc, 2, most, -1), "ctx")
        reply = reply.transpose(1, 0, 2, 3).reshape(2, nc * most, -1)
        dense = jnp.einsum("sib,siw->sbw", pick, reply, preferred_element_type=f32).astype(bf16)
        mine = lax.dynamic_slice_in_dim(dense, t * rows, rows, 1)
        send = lax.dynamic_slice_in_dim(dense, (1 - t) * rows, rows, 1)
        stacked = by_core(mine, swap(send), t).reshape(nz, rows, -1)
        return jnp.sum(exchange(stacked, "fsdp").astype(f32), 0)

    dense = collect(reply)
    moe_rows, grad_rows = dense[:, :width], dense[:, width : 2 * width]
    pair_rows = dense[:, 2 * width : 2 * width + E] + dense[:, 2 * width + E : 2 * width + 2 * E]

    dw_experts = []
    for mine, other in zip(own_updates, other_updates):
        total = (mine + swap(other.astype(bf16)).astype(f32)).astype(bf16)
        dw_experts.append(exchange(total.reshape(nz * nc, -1, ffn), ("fsdp", "ctx")))
    dw_experts = jnp.stack(dw_experts, 1).astype(f32)
    dw_experts = dw_experts.reshape(nz, nc, 3, -1, ffn).transpose(3, 2, 1, 0, 4)
    dw_experts = dw_experts.reshape(-1, 3, E, ffn)

    layer = (residual + moe_rows).astype(bf16)
    piece = width // 2
    layer_mine = lax.dynamic_slice_in_dim(layer, t * piece, piece, 1)
    layer_send = lax.dynamic_slice_in_dim(layer, (1 - t) * piece, piece, 1)
    layer_out = by_core(layer_mine, swap(layer_send), t).reshape(1, block, piece)

    grad_router_probs = pair_rows * kept
    grad_logits = router_probs * (
        grad_router_probs - jnp.sum(router_probs * grad_router_probs, -1, keepdims=True)
    )
    grad_logits = grad_logits.astype(bf16)
    dw_router = dot_tn(normed_two, grad_logits)
    grad_normed_two = grad_rows + dot(grad_logits, router)
    dgain_moe = jnp.sum(grad_normed_two * residual * inv_two, 0)
    grad_residual = cotan_half.astype(f32) + norm_back(grad_normed_two, residual, inv_two, moe_gain)
    grad_attn = all_rows(grad_residual.astype(bf16), t).reshape(tall, width)

    dw_out = dot_tn(context, grad_attn).astype(bf16)
    grad_context = dot_nt(grad_attn, w_o).astype(bf16).reshape(tall, -1, HD)
    scores = jnp.einsum("qhd,khd->hqk", queries, keys, preferred_element_type=f32) * score_scale
    attn_probs = jnp.exp(scores - log_total)
    grad_probs = jnp.einsum("qhd,khd->hqk", grad_context, values, preferred_element_type=f32)
    grad_scores = attn_probs * (grad_probs - jnp.sum(attn_probs * grad_probs, -1, keepdims=True))
    grad_scores = grad_scores.astype(bf16)
    grad_queries = jnp.einsum("hqk,khd->qhd", grad_scores, keys, preferred_element_type=f32) * score_scale
    grad_keys = jnp.einsum("hqk,qhd->khd", grad_scores, queries, preferred_element_type=f32) * score_scale
    grad_values = jnp.einsum(
        "hqk,qhd->khd", attn_probs.astype(bf16), grad_context, preferred_element_type=f32
    ).astype(bf16)
    grad_qnormed = rope_back(grad_queries, cos_full, sin_full)
    grad_knormed = rope_back(grad_keys, cos_full, sin_full)
    dgain_query = jnp.sum(grad_qnormed * query_heads * query_inv, (0, 1))
    dgain_key = jnp.sum(grad_knormed * key_heads * key_inv, (0, 1))
    grad_qproj = norm_back(grad_qnormed, query_heads, query_inv, query_gain).astype(bf16)
    grad_kproj = norm_back(grad_knormed, key_heads, key_inv, key_gain).astype(bf16)
    grad_proj = jnp.stack([grad_qproj, grad_kproj, grad_values], 1).reshape(tall, 3 * local)
    dw_qkv = dot_tn(normed_one, grad_proj).astype(bf16)
    grad_normed_part = dot_nt(grad_proj, w_qkv).astype(bf16).reshape(nc, 2, rows, width)
    grad_normed_one = half_rows_sum(grad_normed_part, t)
    inv_one = rms_scale(own_tokens)
    dgain_attn = jnp.sum(grad_normed_one * own_tokens * inv_one, 0)
    grad_tokens = grad_residual + norm_back(grad_normed_one, own_tokens, inv_one, attn_gain)
    grad_tokens = grad_tokens.astype(bf16)
    tokens_grad = by_core(grad_tokens, swap(grad_tokens), t).reshape(1, block, width)

    chips = nz * nc
    strip = width // chips
    got_qkv = exchange(dw_qkv.reshape(chips, strip, 3 * local), ("fsdp", "ctx"))
    got_qkv = jnp.sum(got_qkv.reshape(nz, nc, strip, 3, local).astype(f32), 0)
    got_qkv = got_qkv.transpose(2, 1, 0, 3).reshape(3, strip, nc * local)
    got_out = exchange(dw_out.reshape(local, chips, strip).transpose(1, 0, 2), ("fsdp", "ctx"))
    got_out = jnp.sum(got_out.reshape(nz, nc, local, strip).astype(f32), 0).reshape(nc * local, strip)

    head_part = HD // chips
    sums = jnp.concatenate(
        [
            dw_router.reshape(chips, strip * E),
            dgain_attn.reshape(chips, strip),
            dgain_moe.reshape(chips, strip),
            dgain_query.reshape(chips, head_part),
            dgain_key.reshape(chips, head_part),
        ],
        1,
    )
    sums = jnp.sum(exchange(sums, ("fsdp", "ctx")), 0)
    sums = sums + swap(sums)
    base = strip * E
    return (
        layer_out,
        tokens_grad,
        got_qkv[0],
        got_qkv[1],
        got_qkv[2],
        got_out,
        sums[base : base + strip],
        sums[base + 2 * strip : base + 2 * strip + head_part],
        sums[base + 2 * strip + head_part :],
        sums[base + strip : base + 2 * strip],
        sums[:base].reshape(strip, E),
        dw_experts,
    )


def solution(mesh):
    chips = mesh.shape["fsdp"] * mesh.shape["ctx"]
    plain = chips == E and mesh.shape["fsdp"] == 4 and mesh.shape["tp"] == 2
    return jax.shard_map(
        one_chip if plain else general,
        mesh=mesh,
        in_specs=(
            P("fsdp", "ctx", None),
            P("fsdp", "tp"),
            P("fsdp", "tp"),
            P("fsdp", "tp"),
            P("tp", "fsdp"),
            P("fsdp"),
            P("fsdp"),
            P("fsdp"),
            P("fsdp"),
            P("fsdp", None),
            P("fsdp", None, None, "tp"),
            P("fsdp", "ctx", None),
            P("fsdp", "ctx", None),
        ),
        out_specs=(
            P("fsdp", "ctx", "tp"),
            P("fsdp", "ctx", None),
            P(("fsdp", "ctx"), "tp"),
            P(("fsdp", "ctx"), "tp"),
            P(("fsdp", "ctx"), "tp"),
            P("tp", ("fsdp", "ctx")),
            P(("fsdp", "ctx")),
            P(("fsdp", "ctx")),
            P(("fsdp", "ctx")),
            P(("fsdp", "ctx")),
            P(("fsdp", "ctx"), None),
            P(("fsdp", "ctx"), None, None, "tp"),
        ),
        check_vma=False,
    )
```

```python
import functools
import math

import jax
import jax.numpy as jnp
from jax import lax
from jax.experimental import pallas as pl
from jax.experimental.pallas import tpu as pltpu
from jax.sharding import PartitionSpec as P

HD = 128
TOPK = 8
E = 16
CAP = 512
MESH = pl.DeviceIdType.MESH


EPS = 1e-06
ROPE_BASE = 10000.0


def prefix(value, axis, join, neutral):
    count, mine = (lax.axis_size(axis), lax.axis_index(axis))
    pieces = lax.all_gather(value, axis)
    running = jnp.full_like(value, 0) + jnp.asarray(neutral, value.dtype)

    def lap(position, running):
        longer = join(running, pieces[position])
        return jnp.where(position < mine, longer, running)

    return lax.fori_loop(0, count - 1, lap, running)


def rms_scale(values):
    return lax.rsqrt(jnp.mean(values * values, -1, keepdims=True) + EPS)


def norm_back(grad_normed, values, inv_rms, gain_vec):
    weighted = grad_normed * gain_vec.astype(jnp.float32)
    inner_sum = jnp.sum(weighted * values, -1, keepdims=True)
    return (
        inv_rms * weighted - values * (inv_rms * inv_rms * inv_rms) * inner_sum / values.shape[-1]
    )


def rope_tables(first, length):
    half_dim = HD // 2
    inv_freq = jnp.exp(jnp.arange(half_dim, dtype=jnp.float32) * (-2.0 * math.log(ROPE_BASE) / HD))
    places = (first + jnp.arange(length, dtype=jnp.int32)).astype(jnp.float32)
    angles = places[:, None] * inv_freq[None, :]
    cos_table = jnp.cos(angles)
    sin_table = jnp.sin(angles)
    cos_full = jnp.concatenate([cos_table, cos_table], -1)[:, None, :]
    sin_full = jnp.concatenate([sin_table, sin_table], -1)[:, None, :]
    return (cos_full, sin_full)


def rotate(values):
    half_dim = values.shape[-1] // 2
    return jnp.concatenate([-values[..., half_dim:], values[..., :half_dim]], -1)


def rotate_back(values):
    half_dim = values.shape[-1] // 2
    return jnp.concatenate([values[..., half_dim:], -values[..., :half_dim]], -1)


def apply_rope(values, cos_full, sin_full):
    return values * cos_full + rotate(values) * sin_full


def rope_back(grads, cos_full, sin_full):
    return grads * cos_full + rotate_back(grads * sin_full)


def add_counts(earlier, later):
    return earlier + later


def general(
    tokens,
    w_query,
    w_key,
    w_value,
    w_out,
    gain_attn,
    gain_query,
    gain_key,
    gain_moe,
    w_router,
    w_experts,
    routes,
    cotangent,
):
    seq_count, block_len, model_width = tokens.shape
    row_count = seq_count * block_len
    (
        full_query,
        full_key,
        full_value,
        full_out,
        router_full,
        attn_gain,
        query_gain,
        key_gain,
        moe_gain,
    ) = (
        lax.all_gather(w_query, "fsdp", axis=0, tiled=True),
        lax.all_gather(w_key, "fsdp", axis=0, tiled=True),
        lax.all_gather(w_value, "fsdp", axis=0, tiled=True),
        lax.all_gather(w_out, "fsdp", axis=1, tiled=True),
        lax.all_gather(w_router, "fsdp", axis=0, tiled=True),
        lax.all_gather(gain_attn, "fsdp", axis=0, tiled=True),
        lax.all_gather(gain_query, "fsdp", axis=0, tiled=True),
        lax.all_gather(gain_key, "fsdp", axis=0, tiled=True),
        lax.all_gather(gain_moe, "fsdp", axis=0, tiled=True),
    )
    local_width = full_query.shape[1]
    head_count = local_width // HD
    head_shape = (seq_count, block_len, head_count, HD)
    token_rows = tokens.reshape(row_count, model_width).astype(jnp.float32)
    inv_one = rms_scale(token_rows)
    normed_one = (token_rows * inv_one * attn_gain.astype(jnp.float32)).astype(jnp.bfloat16)
    query_proj = jnp.dot(normed_one, full_query, preferred_element_type=jnp.float32)
    key_proj = jnp.dot(normed_one, full_key, preferred_element_type=jnp.float32)
    value_proj = jnp.dot(normed_one, full_value, preferred_element_type=jnp.float32)
    cos_full, sin_full = rope_tables(lax.axis_index("ctx") * block_len, block_len)
    query_heads = query_proj.reshape(head_shape)
    key_heads = key_proj.reshape(head_shape)
    query_inv = rms_scale(query_heads)
    key_inv = rms_scale(key_heads)
    queries = apply_rope(
        query_heads * query_inv * query_gain.astype(jnp.float32), cos_full, sin_full
    ).astype(jnp.bfloat16)
    keys_local = apply_rope(
        key_heads * key_inv * key_gain.astype(jnp.float32), cos_full, sin_full
    ).astype(jnp.bfloat16)
    keys_local = keys_local.reshape(seq_count, block_len, local_width)
    values_local = value_proj.astype(jnp.bfloat16).reshape(seq_count, block_len, local_width)
    keys_all, values_all = (
        lax.all_gather(keys_local, "ctx", axis=1, tiled=True),
        lax.all_gather(values_local, "ctx", axis=1, tiled=True),
    )
    seq_len = keys_all.shape[1]
    key_rows = keys_all.reshape(seq_count, seq_len, head_count, HD)
    value_rows = values_all.reshape(seq_count, seq_len, head_count, HD)
    score_scale = 1.0 / math.sqrt(HD)
    scores = (
        jnp.einsum("sqhd,skhd->shqk", queries, key_rows, preferred_element_type=jnp.float32)
        * score_scale
    )
    maximum = jnp.max(scores, -1, keepdims=True)
    exp_scores = jnp.exp(scores - maximum)
    denominator = jnp.sum(exp_scores, -1, keepdims=True)
    attn_probs = exp_scores / denominator
    log_total = maximum + jnp.log(denominator)
    context = jnp.einsum(
        "shqk,skhd->sqhd",
        attn_probs.astype(jnp.bfloat16),
        value_rows,
        preferred_element_type=jnp.float32,
    )
    context = context.astype(jnp.bfloat16).reshape(row_count, local_width)
    attn_part = jnp.dot(context, full_out, preferred_element_type=jnp.float32)
    residual = token_rows + lax.psum(attn_part, "tp")
    inv_two = rms_scale(residual)
    normed_two = (residual * inv_two * moe_gain.astype(jnp.float32)).astype(jnp.bfloat16)
    logits = jnp.dot(normed_two, router_full, preferred_element_type=jnp.float32)
    router_probs = jax.nn.softmax(logits, -1)
    pair_count = block_len * TOPK
    route_rows = routes.reshape(seq_count, pair_count)
    expert_ids = jnp.arange(E, dtype=jnp.int32)
    onehot = (route_rows[:, :, None] == expert_ids[None, None, :]).astype(jnp.int32)
    counts = jnp.sum(onehot, 1, dtype=jnp.int32)
    offsets = prefix(counts, "ctx", add_counts, jnp.zeros_like(counts))
    earlier = jnp.cumsum(onehot, 1, dtype=jnp.int32) - onehot
    local_rank = jnp.sum(earlier * onehot, 2, dtype=jnp.int32)
    slot_base = jnp.sum(onehot * offsets[:, None, :], 2, dtype=jnp.int32)
    kept_mask = (slot_base + local_rank < CAP).astype(jnp.float32).reshape(row_count, TOPK)
    block_most = pair_count * 9 // (8 * E)
    expert_span = seq_count * block_most
    seq_ids = jnp.arange(seq_count, dtype=jnp.int32)[:, None]
    buffer_row = (route_rows * expert_span + seq_ids * block_most + local_rank).reshape(
        row_count * TOPK
    )
    token_ids = (
        seq_ids * block_len + jnp.arange(pair_count, dtype=jnp.int32)[None, :] // TOPK
    ).reshape(row_count * TOPK)
    owner_rows = jnp.zeros((E * expert_span,), jnp.int32).at[buffer_row].set(token_ids)
    onehot_f = onehot.astype(jnp.float32).reshape(row_count, TOPK, E)
    gate_weight = jnp.sum(onehot_f * router_probs[:, None, :], 2) * kept_mask
    slot_weight = (
        jnp.zeros((E * expert_span,), jnp.float32)
        .at[buffer_row]
        .set(gate_weight.reshape(row_count * TOPK))
    )
    expert_rows = normed_two[owner_rows].reshape(E, expert_span, model_width)
    cotan_rows = cotangent.reshape(row_count, model_width)
    grad_expert = (slot_weight[:, None] * cotan_rows[owner_rows].astype(jnp.float32)).astype(
        jnp.bfloat16
    )
    grad_expert = grad_expert.reshape(E, expert_span, model_width)
    ffn_local = w_experts.shape[3]
    fsdp_count = lax.axis_size("fsdp")
    ctx_count = lax.axis_size("ctx")
    group_count = fsdp_count * ctx_count
    sharing = group_count // E
    padded_span = -(-expert_span // sharing) * sharing
    part_span = padded_span // sharing
    target_experts = (
        jnp.arange(fsdp_count, dtype=jnp.int32) * ctx_count + lax.axis_index("ctx")
    ) // sharing
    selected = jnp.take(w_experts, target_experts, axis=2)
    owned = lax.all_to_all(selected, "fsdp", split_axis=2, concat_axis=0, tiled=True)[:, :, 0]
    send_rows = expert_rows.reshape(group_count, part_span, model_width)
    send_grads = grad_expert.reshape(group_count, part_span, model_width)
    recv_rows, recv_grads = (
        lax.all_to_all(send_rows, ("fsdp", "ctx"), split_axis=0, concat_axis=0, tiled=True),
        lax.all_to_all(send_grads, ("fsdp", "ctx"), split_axis=0, concat_axis=0, tiled=True),
    )
    rows_flat = recv_rows.reshape(group_count * part_span, model_width)
    grads_flat = recv_grads.reshape(group_count * part_span, model_width)
    gate_act = jnp.dot(rows_flat, owned[:, 0], preferred_element_type=jnp.float32)
    up_act = jnp.dot(rows_flat, owned[:, 1], preferred_element_type=jnp.float32)
    sigmoid_gate = jax.nn.sigmoid(gate_act)
    silu_gate = gate_act * sigmoid_gate
    hidden = (silu_gate * up_act).astype(jnp.bfloat16)
    produced = jnp.einsum("mf,df->md", hidden, owned[:, 2], preferred_element_type=jnp.float32)
    grad_hidden = jnp.dot(grads_flat, owned[:, 2], preferred_element_type=jnp.float32)
    grad_gate = (
        grad_hidden * up_act * sigmoid_gate * (1.0 + gate_act * (1.0 - sigmoid_gate))
    ).astype(jnp.bfloat16)
    grad_up = (grad_hidden * silu_gate).astype(jnp.bfloat16)
    rows_grad = jnp.einsum("mf,df->md", grad_gate, owned[:, 0], preferred_element_type=jnp.float32)
    rows_grad = rows_grad + jnp.einsum(
        "mf,df->md", grad_up, owned[:, 1], preferred_element_type=jnp.float32
    )
    back_out, back_rows = (
        lax.all_to_all(
            produced.reshape(group_count, part_span, model_width).astype(jnp.bfloat16),
            ("fsdp", "ctx"),
            split_axis=0,
            concat_axis=0,
            tiled=True,
        ).astype(jnp.float32),
        lax.all_to_all(
            rows_grad.reshape(group_count, part_span, model_width).astype(jnp.bfloat16),
            ("fsdp", "ctx"),
            split_axis=0,
            concat_axis=0,
            tiled=True,
        ).astype(jnp.float32),
    )
    expert_out = back_out.reshape(E, padded_span, model_width)
    grad_rows = back_rows.reshape(E, padded_span, model_width)
    gate_term = jnp.einsum("md,mf->df", rows_flat, grad_gate, preferred_element_type=jnp.float32)
    up_term = jnp.einsum("md,mf->df", rows_flat, grad_up, preferred_element_type=jnp.float32)
    down_term = jnp.einsum("md,mf->df", grads_flat, hidden, preferred_element_type=jnp.float32)
    owner_terms = jnp.stack([gate_term, up_term, down_term], 1)[:, :, None, :]
    relaid = lax.all_to_all(
        owner_terms.astype(jnp.bfloat16), ("fsdp", "ctx"), split_axis=0, concat_axis=2, tiled=True
    ).astype(owner_terms.dtype)
    dw_experts = jnp.sum(relaid.reshape(relaid.shape[0], 3, E, sharing, ffn_local), 3)
    picked = expert_out.reshape(E * expert_span, model_width)[buffer_row].reshape(
        row_count, TOPK, model_width
    )
    moe_part = jnp.sum(gate_weight[:, :, None] * picked, 1)
    cotan_float = cotan_rows.astype(jnp.float32)
    grad_gate_part = jnp.sum(picked * cotan_float[:, None, :], 2)
    moe_shard = lax.psum_scatter(
        moe_part.astype(jnp.bfloat16), "tp", scatter_dimension=1, tiled=True
    ).astype(jnp.float32)
    piece_width = moe_shard.shape[1]
    residual_shard = lax.dynamic_slice_in_dim(
        residual, lax.axis_index("tp") * piece_width, piece_width, 1
    )
    layer_out = (
        (residual_shard + moe_shard).astype(jnp.bfloat16).reshape(seq_count, block_len, piece_width)
    )
    grad_normed_part = jnp.sum(
        grad_rows.reshape(E * expert_span, model_width)[buffer_row].reshape(
            row_count, TOPK, model_width
        ),
        1,
    )
    grad_normed_sum, grad_gate_sum = (
        lax.psum(grad_normed_part.astype(jnp.bfloat16), "tp").astype(jnp.float32),
        lax.psum(grad_gate_part.astype(jnp.bfloat16), "tp").astype(jnp.float32),
    )
    grad_pick = grad_gate_sum * kept_mask
    grad_router_probs = jnp.sum(onehot_f * grad_pick[:, :, None], 1)
    grad_logits = router_probs * (
        grad_router_probs - jnp.sum(router_probs * grad_router_probs, -1, keepdims=True)
    )
    grad_logits = grad_logits.astype(jnp.bfloat16)
    grad_router_w = jnp.einsum(
        "nd,ne->de", normed_two, grad_logits, preferred_element_type=jnp.float32
    )
    grad_normed_two = grad_normed_sum + jnp.einsum(
        "ne,de->nd", grad_logits, router_full, preferred_element_type=jnp.float32
    )
    grad_moe_gain = jnp.sum(grad_normed_two * residual * inv_two, 0)
    grad_residual = cotan_float + norm_back(grad_normed_two, residual, inv_two, moe_gain)
    grad_attn = grad_residual.astype(jnp.bfloat16)
    grad_w_out = jnp.einsum("nl,nd->ld", context, grad_attn, preferred_element_type=jnp.float32)
    grad_context = jnp.einsum("nd,ld->nl", grad_attn, full_out, preferred_element_type=jnp.float32)
    grad_context = grad_context.astype(jnp.bfloat16).reshape(head_shape)
    scores = (
        jnp.einsum("sqhd,skhd->shqk", queries, key_rows, preferred_element_type=jnp.float32)
        * score_scale
    )
    attn_probs = jnp.exp(scores - log_total)
    grad_probs = jnp.einsum(
        "sqhd,skhd->shqk", grad_context, value_rows, preferred_element_type=jnp.float32
    )
    grad_scores = attn_probs * (grad_probs - jnp.sum(attn_probs * grad_probs, -1, keepdims=True))
    grad_scores = grad_scores.astype(jnp.bfloat16)
    grad_queries = (
        jnp.einsum("shqk,skhd->sqhd", grad_scores, key_rows, preferred_element_type=jnp.float32)
        * score_scale
    )
    grad_keys_all = (
        jnp.einsum("shqk,sqhd->skhd", grad_scores, queries, preferred_element_type=jnp.float32)
        * score_scale
    )
    grad_values_all = jnp.einsum(
        "shqk,sqhd->skhd",
        attn_probs.astype(jnp.bfloat16),
        grad_context,
        preferred_element_type=jnp.float32,
    )
    grad_keys_own, grad_values_own = (
        lax.psum_scatter(
            grad_keys_all.reshape(seq_count, seq_len, local_width).astype(jnp.bfloat16),
            "ctx",
            scatter_dimension=1,
            tiled=True,
        ).astype(jnp.float32),
        lax.psum_scatter(
            grad_values_all.reshape(seq_count, seq_len, local_width).astype(jnp.bfloat16),
            "ctx",
            scatter_dimension=1,
            tiled=True,
        ).astype(jnp.float32),
    )
    grad_qnormed = rope_back(grad_queries, cos_full, sin_full)
    grad_knormed = rope_back(grad_keys_own.reshape(head_shape), cos_full, sin_full)
    grad_qgain = jnp.sum(grad_qnormed * query_heads * query_inv, (0, 1, 2))
    grad_kgain = jnp.sum(grad_knormed * key_heads * key_inv, (0, 1, 2))
    grad_qproj = (
        norm_back(grad_qnormed, query_heads, query_inv, query_gain)
        .astype(jnp.bfloat16)
        .reshape(row_count, local_width)
    )
    grad_kproj = (
        norm_back(grad_knormed, key_heads, key_inv, key_gain)
        .astype(jnp.bfloat16)
        .reshape(row_count, local_width)
    )
    grad_vproj = grad_values_own.astype(jnp.bfloat16).reshape(row_count, local_width)
    grad_wq = jnp.einsum("nd,nl->dl", normed_one, grad_qproj, preferred_element_type=jnp.float32)
    grad_wk = jnp.einsum("nd,nl->dl", normed_one, grad_kproj, preferred_element_type=jnp.float32)
    grad_wv = jnp.einsum("nd,nl->dl", normed_one, grad_vproj, preferred_element_type=jnp.float32)
    grad_normed_one = jnp.einsum(
        "nl,dl->nd", grad_qproj, full_query, preferred_element_type=jnp.float32
    )
    grad_normed_one = grad_normed_one + jnp.einsum(
        "nl,dl->nd", grad_kproj, full_key, preferred_element_type=jnp.float32
    )
    grad_normed_one = grad_normed_one + jnp.einsum(
        "nl,dl->nd", grad_vproj, full_value, preferred_element_type=jnp.float32
    )
    grad_normed_one, grad_qgain, grad_kgain = (
        lax.psum(grad_normed_one.astype(jnp.bfloat16), "tp").astype(jnp.float32),
        lax.psum(grad_qgain.astype(jnp.bfloat16), "tp").astype(jnp.float32),
        lax.psum(grad_kgain.astype(jnp.bfloat16), "tp").astype(jnp.float32),
    )
    grad_attn_gain = jnp.sum(grad_normed_one * token_rows * inv_one, 0)
    tokens_grad = grad_residual + norm_back(grad_normed_one, token_rows, inv_one, attn_gain)
    tokens_grad = tokens_grad.astype(jnp.bfloat16).reshape(seq_count, block_len, model_width)
    dw_query, dw_key, dw_value, dw_out, dw_router, dgain_attn, dgain_query, dgain_key, dgain_moe = (
        lax.psum_scatter(grad_wq, ("fsdp", "ctx"), scatter_dimension=0, tiled=True),
        lax.psum_scatter(grad_wk, ("fsdp", "ctx"), scatter_dimension=0, tiled=True),
        lax.psum_scatter(grad_wv, ("fsdp", "ctx"), scatter_dimension=0, tiled=True),
        lax.psum_scatter(grad_w_out, ("fsdp", "ctx"), scatter_dimension=1, tiled=True),
        lax.psum_scatter(grad_router_w, ("fsdp", "ctx"), scatter_dimension=0, tiled=True),
        lax.psum_scatter(grad_attn_gain, ("fsdp", "ctx"), scatter_dimension=0, tiled=True),
        lax.psum_scatter(grad_qgain, ("fsdp", "ctx"), scatter_dimension=0, tiled=True),
        lax.psum_scatter(grad_kgain, ("fsdp", "ctx"), scatter_dimension=0, tiled=True),
        lax.psum_scatter(grad_moe_gain, ("fsdp", "ctx"), scatter_dimension=0, tiled=True),
    )
    return (
        layer_out,
        tokens_grad,
        dw_query,
        dw_key,
        dw_value,
        dw_out,
        dgain_attn,
        dgain_query,
        dgain_key,
        dgain_moe,
        dw_router,
        dw_experts,
    )


def swap(value):
    return lax.ppermute(value, "tp", [(0, 1), (1, 0)])


def exchange(value, axes):
    return lax.all_to_all(value, axes, split_axis=0, concat_axis=0, tiled=True)


def spread(value, axes):
    count = lax.axis_size(axes)
    return exchange(jnp.broadcast_to(value[None], (count,) + value.shape), axes)


def dot(left, right):
    return jnp.dot(left, right, preferred_element_type=jnp.float32)


def dot_nt(left, right):
    return lax.dot_general(left, right, (((1,), (1,)), ((), ())), preferred_element_type=jnp.float32)


def dot_tn(left, right):
    return lax.dot_general(left, right, (((0,), (0,)), ((), ())), preferred_element_type=jnp.float32)


def two_parts(values):
    high = values.astype(jnp.bfloat16)
    low = (values - high.astype(jnp.float32)).astype(jnp.bfloat16)
    return (high, low)


def by_core(mine, other, core):
    return jnp.where(core == 0, jnp.stack([mine, other]), jnp.stack([other, mine]))


def remote(src, dst, send, recv, **where):
    return pltpu.make_async_remote_copy(
        src_ref=src, dst_ref=dst, send_sem=send, recv_sem=recv, device_id=where, device_id_type=MESH
    )


def places():
    return lax.axis_index("fsdp"), lax.axis_index("ctx"), lax.axis_index("tp")


def ring(index, step, count):
    return lax.rem(index + step + count, count)


def greet(nz, nc, line):
    z, c, t = places()
    barrier = pltpu.get_barrier_semaphore()

    def tell(**where):
        pl.semaphore_signal(barrier, inc=1, device_id=where, device_id_type=MESH)

    if line:
        for step in range(1, nz):
            tell(fsdp=ring(z, step, nz))
        count = nz - 1
    else:
        pl.when(z > 0)(lambda: tell(fsdp=z - 1))
        pl.when(z < nz - 1)(lambda: tell(fsdp=z + 1))
        count = jnp.where(z > 0, 1, 0) + jnp.where(z < nz - 1, 1, 0)
    for step in range(1, nc):
        tell(ctx=ring(c, step, nc))
    tell(tp=1 - t)
    pl.semaphore_wait(barrier, count + nc)


def line_copies(bufs, send_sem, recv_sem, way, step, shard, target):
    return [
        remote(buf.at[shard], buf.at[shard], send_sem.at[way, step, k], recv_sem.at[way, step, k], fsdp=target)
        for k, buf in enumerate(bufs)
    ]


def line_gather(nz, bufs, send_sem, recv_sem, arrived, begun=None, near=None):
    z = lax.axis_index("fsdp")
    for step in range(nz - 1):

        @pl.when((z < nz - 1) & (z >= step))
        def _():
            for copy in line_copies(bufs, send_sem, recv_sem, 0, step, z - step, z + 1):
                copy.start()

        @pl.when((z > 0) & (z + step < nz))
        def _():
            for copy in line_copies(bufs, send_sem, recv_sem, 1, step, z + step, z - 1):
                copy.start()

        if step == 0 and begun is not None:
            begun()
        if near is not None:
            near(step)

        @pl.when(z - 1 >= step)
        def _():
            for copy in line_copies(bufs, send_sem, recv_sem, 0, step, z - 1 - step, z - 1):
                copy.wait_recv()
            arrived(z - 1 - step)

        @pl.when(z + 1 + step < nz)
        def _():
            for copy in line_copies(bufs, send_sem, recv_sem, 1, step, z + 1 + step, z + 1):
                copy.wait_recv()
            arrived(z + 1 + step)


def line_sent(nz, bufs, send_sem, recv_sem):
    z = lax.axis_index("fsdp")
    for step in range(nz - 1):

        @pl.when((z < nz - 1) & (z >= step))
        def _():
            for copy in line_copies(bufs, send_sem, recv_sem, 0, step, z - step, z + 1):
                copy.wait_send()

        @pl.when((z > 0) & (z + step < nz))
        def _():
            for copy in line_copies(bufs, send_sem, recv_sem, 1, step, z + step, z - 1):
                copy.wait_send()


def pick_rows(pick, slot, source, out):
    lanes = out.shape[-1]
    piece = min(lanes, 512)

    @pl.loop(0, lanes // piece)
    def _(k):
        at = pl.ds(pl.multiple_of(k * piece, piece), piece)
        out[slot, :, at] = jnp.dot(pick[slot], source[slot, :, at], preferred_element_type=jnp.float32).astype(
            jnp.bfloat16
        )


def plane_copy(most, src, dst, send, recv, slot, step, source, target):
    rows = pl.ds(pl.multiple_of(target * most, 16), most)
    return remote(
        src.at[slot, rows], dst.at[source, slot], send.at[slot, step - 1], recv.at[slot, step - 1], ctx=target
    )


def regroup(shard, t, rows, line, two, keep_sem, give_send, give_recv):
    slot = lax.rem(shard, 2)
    band = pl.ds(pl.multiple_of(t * rows, rows), rows)

    def keep():
        pltpu.make_async_copy(line.at[shard], two.at[slot, band], keep_sem.at[slot]).start()

    def give():
        remote(line.at[shard], two.at[slot, band], give_send.at[slot], give_recv.at[slot], tp=1 - t).start()

    pl.when(shard // 2 == t)(keep)
    pl.when(shard // 2 != t)(give)


def load_kernel(
    nz, nc, tok, cot, wq, wk, wv, wo, small, rank,
    x_all, w_qkv, w_o, small_all, rank_line, rank_seq, pick, cot_in,
    cot_line, cot_two, cot_send,
    own_sem, line_send, line_recv, w_send, w_recv, tok_send, tok_recv, pass_send, pass_recv,
    rank_send, rank_recv, keep_sem, give_send, give_recv, cot_s, cot_r, cot_own,
):
    z, c, t = places()
    block = tok.shape[0]
    rows = block // 2
    local = w_qkv.shape[2] // 3
    most = cot_in.shape[2]
    half = pl.ds(pl.multiple_of(t * rows, rows), rows)
    column = pl.ds(pl.multiple_of(c * local, local), local)
    own = [
        pltpu.make_async_copy(cot.at[half], cot_line.at[z], own_sem.at[5]),
        pltpu.make_async_copy(small, small_all.at[z], own_sem.at[4]),
        pltpu.make_async_copy(rank, rank_line.at[z], own_sem.at[7]),
        pltpu.make_async_copy(rank, rank_seq.at[c], own_sem.at[8]),
    ]
    own += [
        pltpu.make_async_copy(w.at[:, column], w_qkv.at[z, :, pl.ds(k * local, local)], own_sem.at[k])
        for k, w in enumerate((wq, wk, wv))
    ]
    own += [
        pltpu.make_async_copy(wo.at[column], w_o.at[z], own_sem.at[3]),
        pltpu.make_async_copy(tok, x_all.at[pl.ds(pl.multiple_of(c * block, block), block)], own_sem.at[6]),
    ]
    for copy in own:
        copy.start()
    greet(nz, nc, False)

    def band(source, core):
        return x_all.at[pl.ds(pl.multiple_of(source * block + core * rows, rows), rows)]

    def token_copy(step, source, target):
        return remote(tok.at[half], band(source, t), tok_send.at[step], tok_recv.at[step], ctx=target)

    def pass_copy(step, source, core):
        return remote(band(source, core), band(source, core), pass_send.at[step], pass_recv.at[step], tp=1 - t)

    def rank_copy(step, source, target):
        return remote(rank, rank_seq.at[source], rank_send.at[step], rank_recv.at[step], ctx=target)

    for step in range(1, nc):
        token_copy(step - 1, c, ring(c, step, nc)).start()
        rank_copy(step - 1, c, ring(c, step, nc)).start()
    for copy in own:
        copy.wait()

    def arrived(shard):
        regroup(shard, t, rows, cot_line, cot_two, keep_sem, give_send, give_recv)

    arrived(z)
    first = (cot_line, rank_line, small_all)
    line_gather(nz, first, line_send, line_recv, arrived)

    def own_copy(slot):
        return pltpu.make_async_copy(
            cot_send.at[slot, pl.ds(pl.multiple_of(c * most, 16), most)], cot_in.at[c, slot], cot_own.at[slot]
        )

    def send_cotangent():
        number = lax.broadcasted_iota(jnp.int32, (most, block), 0).astype(jnp.float32)
        for slot in range(2):
            for q in range(nc):
                row = rank_line[2 * t + slot, pl.ds(q * nz + z, 1), :]
                hit = jnp.where(number == row, 1.0, 0.0)
                pick[slot, pl.ds(q * most, most), :] = hit.astype(jnp.bfloat16)
        for slot in range(2):
            wait_two(slot, t, rows, cot_line, cot_two, keep_sem, give_recv)
            pick_rows(pick, slot, cot_two, cot_send)
            for step in range(1, nc):
                plane_copy(most, cot_send, cot_in, cot_s, cot_r, slot, step, c, ring(c, step, nc)).start()
            own_copy(slot).start()

    def ignore(shard):
        pass

    line_gather(nz, (w_qkv, w_o), w_send, w_recv, ignore, send_cotangent)
    for step in range(1, nc):
        source = ring(c, -step, nc)
        token_copy(step - 1, source, source).wait_recv()
        pass_copy(step - 1, source, t).start()
        rank_copy(step - 1, source, source).wait_recv()
    for step in range(1, nc):
        source = ring(c, -step, nc)
        pass_copy(step - 1, source, 1 - t).wait_recv()
        pass_copy(step - 1, source, t).wait_send()
        token_copy(step - 1, c, source).wait_send()
        rank_copy(step - 1, c, source).wait_send()
        for slot in range(2):
            copy = plane_copy(most, cot_send, cot_in, cot_s, cot_r, slot, step, source, source)
            copy.wait_recv()
            copy.wait_send()
    line_sent(nz, first, line_send, line_recv)
    line_sent(nz, (w_qkv, w_o), w_send, w_recv)
    for slot in range(2):
        own_copy(slot).wait()
        wait_given(slot, t, rows, cot_line, cot_two, give_send, give_recv)


def wait_given(slot, t, rows, line, two, give_send, give_recv):
    band = pl.ds(pl.multiple_of(t * rows, rows), rows)
    remote(line.at[0], two.at[slot, band], give_send.at[slot], give_recv.at[slot], tp=1 - t).wait_send()


def wait_two(slot, t, rows, line, two, keep_sem, give_recv):
    band = pl.ds(pl.multiple_of(t * rows, rows), rows)
    other = pl.ds(pl.multiple_of((1 - t) * rows, rows), rows)
    pltpu.make_async_copy(line.at[0], two.at[slot, band], keep_sem.at[slot]).wait()
    remote(line.at[0], two.at[slot, other], give_recv.at[slot], give_recv.at[slot], tp=1 - t).wait_recv()


def load(tok, cot, wq, wk, wv, wo, small, rank, most):
    nz, nc = lax.axis_size("fsdp"), lax.axis_size("ctx")
    block, width = tok.shape
    deep, local = wq.shape[0], wq.shape[1] // nc
    rows = block // 2
    dma = pltpu.SemaphoreType.DMA
    bf16, f32 = jnp.bfloat16, jnp.float32
    shapes = [
        ((nc * block, width), bf16),
        ((nz, deep, 3 * local), bf16),
        ((nz, local, wo.shape[1]), bf16),
        ((nz,) + small.shape, bf16),
        ((nz,) + rank.shape, f32),
        ((nc,) + rank.shape, f32),
        ((2, nc * most, block), bf16),
        ((nc, 2, most, width), bf16),
    ]
    hbm = pl.BlockSpec(memory_space=pl.ANY)
    return pl.pallas_call(
        functools.partial(load_kernel, nz, nc),
        out_shape=[jax.ShapeDtypeStruct(shape, kind) for shape, kind in shapes],
        in_specs=[hbm] * 8,
        out_specs=[pl.BlockSpec(memory_space=pltpu.VMEM)] * 7 + [hbm],
        scratch_shapes=[
            pltpu.VMEM((nz, rows, width), bf16),
            pltpu.VMEM((2, block, width), bf16),
            pltpu.VMEM((2, nc * most, width), bf16),
            dma((9,)),
            dma((2, nz - 1, 3)), dma((2, nz - 1, 3)), dma((2, nz - 1, 2)), dma((2, nz - 1, 2)),
            dma((nc - 1,)), dma((nc - 1,)), dma((nc - 1,)), dma((nc - 1,)), dma((nc - 1,)), dma((nc - 1,)),
            dma((2,)), dma((2,)), dma((2,)), dma((2, nc - 1)), dma((2, nc - 1)), dma((2,)),
        ],
        compiler_params=pltpu.CompilerParams(
            collective_id=0, has_side_effects=True, vmem_limit_bytes=48 * 2**20
        ),
    )(tok, cot, wq, wk, wv, wo, small, rank)


def dispatch_kernel(
    nz, nc, part, tok, gain, router, kept, pick,
    residual, normed, probs, x_in, g_in,
    sib, rs_send, rs_recv, n_line, g_line, n_two, g_two, x_send, g_send,
    sib_s, sib_r, rs_s, rs_r, line_send, line_recv, keep_sem, give_send, give_recv,
    gkeep_sem, ggive_send, ggive_recv, x_s, x_r, g_s, g_r, own_sem,
):
    z, c, t = places()
    f32, bf16 = jnp.float32, jnp.bfloat16
    rows, width = residual.shape
    most = x_in.shape[2]
    greet(nz, nc, False)

    def sib_copy(q):
        return remote(part.at[q, 1 - t], sib.at[q], sib_s.at[q], sib_r.at[q], tp=1 - t)

    def rs_copy(step, source, target):
        return remote(rs_send.at[step], rs_recv.at[step], rs_s.at[step], rs_r.at[step], ctx=target)

    for step in range(1, nc + 1):
        sib_copy(ring(c, step, nc)).start()
    chunk = 16
    for step in range(1, nc):
        q = ring(c, step, nc)
        sib_copy(q).wait_recv()

        @pl.loop(0, rows // chunk)
        def _(k):
            at = pl.ds(pl.multiple_of(k * chunk, chunk), chunk)
            rs_send[step - 1, at, :] = (part[q, t, at, :].astype(f32) + sib[q, at, :].astype(f32)).astype(bf16)

        rs_copy(step - 1, c, q).start()

    def own_copy(slot, src, dst, k):
        return pltpu.make_async_copy(
            src.at[slot, pl.ds(pl.multiple_of(c * most, 16), most)], dst.at[c, slot], own_sem.at[k, slot]
        )

    sib_copy(c).wait_recv()
    for step in range(1, nc):
        rs_copy(step - 1, c, c).wait_recv()

    @pl.loop(0, rows // chunk)
    def _(k):
        at = pl.ds(pl.multiple_of(k * chunk, chunk), chunk)
        start = pl.ds(pl.multiple_of(t * rows + k * chunk, chunk), chunk)
        total = part[c, t, at, :].astype(f32) + sib[c, at, :].astype(f32)
        for step in range(nc - 1):
            total = total + rs_recv[step, at, :].astype(f32)
        total = total + tok[start, :].astype(f32)
        residual[at, :] = total
        inv = lax.rsqrt(jnp.mean(total * total, -1, keepdims=True) + EPS)
        row = (total * inv * gain[...]).astype(bf16)
        normed[at, :] = row
        n_line[z, at, :] = row

    logits = lax.dot_general(
        normed[...], router[...], (((1,), (1,)), ((), ())), preferred_element_type=f32
    )
    lane = lax.broadcasted_iota(jnp.int32, logits.shape, 1)
    logits = jnp.where(lane < E, logits, -jnp.inf)
    top = jnp.max(logits, -1, keepdims=True)
    raised = jnp.exp(logits - top)
    prob = raised / jnp.sum(raised, -1, keepdims=True)
    probs[...] = prob
    gates = prob * kept[...]
    high = gates.astype(bf16)
    g_line[z, :, pl.ds(0, 128)] = high
    g_line[z, :, pl.ds(128, 128)] = (gates - high.astype(f32)).astype(bf16)

    def arrived(shard):
        regroup(shard, t, rows, n_line, n_two, keep_sem, give_send, give_recv)
        regroup(shard, t, rows, g_line, g_two, gkeep_sem, ggive_send, ggive_recv)

    arrived(z)
    sent = ((x_send, x_in, x_s, x_r), (g_send, g_in, g_s, g_r))

    def near(distance):
        above, below = z + distance, z - distance
        is_above = (above < nz) & (above // 2 == t)
        is_below = (below >= 0) & (below // 2 == t)
        slot = lax.rem(jnp.where(is_above, above, below + 2), 2)

        @pl.when(is_above | is_below)
        def _():
            wait_two(slot, t, rows, n_line, n_two, keep_sem, give_recv)
            wait_two(slot, t, rows, g_line, g_two, gkeep_sem, ggive_recv)
            pick_rows(pick, slot, n_two, x_send)
            pick_rows(pick, slot, g_two, g_send)
            for k, (src, dst, s, r) in enumerate(sent):
                for step in range(1, nc):
                    plane_copy(most, src, dst, s, r, slot, step, c, ring(c, step, nc)).start()
                own_copy(slot, src, dst, k).start()

    line_gather(nz, (n_line, g_line), line_send, line_recv, arrived, None, near)
    near(nz - 1)
    line_sent(nz, (n_line, g_line), line_send, line_recv)
    for slot in range(2):
        wait_given(slot, t, rows, n_line, n_two, give_send, give_recv)
        wait_given(slot, t, rows, g_line, g_two, ggive_send, ggive_recv)
        for k, (src, dst, s, r) in enumerate(sent):
            own_copy(slot, src, dst, k).wait()
            for step in range(1, nc):
                source = ring(c, -step, nc)
                copy = plane_copy(most, src, dst, s, r, slot, step, source, source)
                copy.wait_recv()
                copy.wait_send()
    for step in range(1, nc):
        rs_copy(step - 1, c, c).wait_send()
    for step in range(nc):
        sib_copy(step).wait_send()


def dispatch(part, tok, gain, router, kept, pick):
    nz, nc = lax.axis_size("fsdp"), lax.axis_size("ctx")
    rows, width = part.shape[2], part.shape[3]
    block = rows * 2
    most = pick.shape[1] // nc
    dma = pltpu.SemaphoreType.DMA
    bf16, f32 = jnp.bfloat16, jnp.float32
    vmem = pl.BlockSpec(memory_space=pltpu.VMEM)
    hbm = pl.BlockSpec(memory_space=pl.ANY)
    return pl.pallas_call(
        functools.partial(dispatch_kernel, nz, nc),
        out_shape=[
            jax.ShapeDtypeStruct((rows, width), f32),
            jax.ShapeDtypeStruct((rows, width), bf16),
            jax.ShapeDtypeStruct((rows, 128), f32),
            jax.ShapeDtypeStruct((nc, 2, most, width), bf16),
            jax.ShapeDtypeStruct((nc, 2, most, 256), bf16),
        ],
        in_specs=[vmem] * 6,
        out_specs=[vmem] * 3 + [hbm] * 2,
        scratch_shapes=[
            pltpu.VMEM((nc, rows, width), bf16),
            pltpu.VMEM((nc - 1, rows, width), bf16),
            pltpu.VMEM((nc - 1, rows, width), bf16),
            pltpu.VMEM((nz, rows, width), bf16),
            pltpu.VMEM((nz, rows, 256), bf16),
            pltpu.VMEM((2, block, width), bf16),
            pltpu.VMEM((2, block, 256), bf16),
            pltpu.VMEM((2, nc * most, width), bf16),
            pltpu.VMEM((2, nc * most, 256), bf16),
            dma((nc,)), dma((nc,)), dma((nc - 1,)), dma((nc - 1,)),
            dma((2, nz - 1, 2)), dma((2, nz - 1, 2)),
            dma((2,)), dma((2,)), dma((2,)), dma((2,)), dma((2,)), dma((2,)),
            dma((2, nc - 1)), dma((2, nc - 1)), dma((2, nc - 1)), dma((2, nc - 1)),
            dma((2, 2)),
        ],
        compiler_params=pltpu.CompilerParams(
            collective_id=1, has_side_effects=True, vmem_limit_bytes=56 * 2**20
        ),
    )(part, tok, gain, router, kept, pick)


def experts_kernel(
    x_hbm, cot_hbm, weight, own_hbm, other_hbm, y, r, pair, own_grad, other_grad,
    x, cot, w, gate, up, out_grad, hid, gg, gu, stage, sem, stage_sem,
):
    f32, bf16 = jnp.float32, jnp.bfloat16
    width, tall = x.shape[1], x.shape[0]
    nz, deep, ffn = w.shape[1], w.shape[3], w.shape[4]
    span = 256
    copies = [
        pltpu.make_async_copy(cot_hbm, cot, sem.at[0]),
        pltpu.make_async_copy(own_hbm, w.at[0], sem.at[1]),
        pltpu.make_async_copy(x_hbm, x, sem.at[2]),
        pltpu.make_async_copy(other_hbm, w.at[1], sem.at[3]),
    ]
    for copy in copies:
        copy.start()
    for copy in copies:
        copy.wait()
    pair[...] = jnp.zeros_like(pair)
    per = ffn // span

    @pl.loop(0, 2 * per)
    def _(n):
        half, at = n // per, pl.ds(pl.multiple_of(lax.rem(n, per) * span, span), span)
        full = pl.ds(pl.multiple_of(n * span, span), span)

        def times(rows, k):
            return jnp.dot(rows[...], w[half, :, k, :, at].reshape(width, span), preferred_element_type=f32)

        out_grad[...] = times(cot, 2)
        gate[...] = times(x, 0)
        up[...] = times(x, 1)
        chunk = 48

        @pl.loop(0, tall // chunk)
        def _(m):
            rows = pl.ds(pl.multiple_of(m * chunk, chunk), chunk)
            g, u, o, k = gate[rows, :], up[rows, :], out_grad[rows, :], weight[rows, :]
            sig = 1.0 / (1.0 + jnp.exp(-g))
            silu = g * sig
            hidden = silu * u
            pair[rows, :] += jnp.sum(hidden.astype(bf16).astype(f32) * o, 1, keepdims=True)
            hid[rows, full] = (k * hidden).astype(bf16)
            o = k * o
            gg[rows, full] = (o * u * sig * (1.0 + g * (1.0 - sig))).astype(bf16)
            gu[rows, full] = (o * silu).astype(bf16)

    per_deep = deep // span

    @pl.loop(0, width // span)
    def _(n):
        zone, at = n // per_deep, pl.ds(pl.multiple_of(lax.rem(n, per_deep) * span, span), span)
        full = pl.ds(pl.multiple_of(n * span, span), span)

        def back(rows, k):
            total = 0.0
            for half in range(2):
                total = total + lax.dot_general(
                    rows[:, pl.ds(half * ffn, ffn)], w[half, zone, k, at, :], (((1,), (1,)), ((), ())),
                    preferred_element_type=f32,
                )
            return total

        y[:, full] = back(hid, 2).astype(bf16)
        r[:, full] = (back(gg, 0) + back(gu, 1)).astype(bf16)

    strip = stage.shape[4]
    count = span // strip

    def flush(n, half):
        slot = lax.rem(n, 2)
        out = (own_grad, other_grad)[half]
        return pltpu.make_async_copy(
            stage.at[slot, half], out.at[pl.ds(pl.multiple_of(n * count, count), count)], stage_sem.at[slot, half]
        )

    @pl.loop(0, width // span)
    def _(n):
        full = pl.ds(pl.multiple_of(n * span, span), span)
        slot = lax.rem(n, 2)

        @pl.when(n >= 2)
        def _():
            for half in range(2):
                flush(n - 2, half).wait()

        for k, (rows, grads) in enumerate(((x, gg), (x, gu), (cot, hid))):
            value = lax.dot_general(
                rows[:, full], grads[...], (((0,), (0,)), ((), ())), preferred_element_type=f32
            ).astype(bf16)
            for half in range(2):
                for i in range(count):
                    stage[slot, half, i, k] = value[i * strip : (i + 1) * strip, half * ffn : (half + 1) * ffn]
        for half in range(2):
            flush(n, half).start()

    for n in (width // span - 2, width // span - 1):
        for half in range(2):
            flush(n, half).wait()


def experts(x, cot, weight, own, other, strip):
    bf16, f32 = jnp.bfloat16, jnp.float32
    tall, width = x.shape
    ffn = own.shape[3]
    vmem = pl.BlockSpec(memory_space=pltpu.VMEM)
    hbm = pl.BlockSpec(memory_space=pl.ANY)
    grads = jax.ShapeDtypeStruct((width // strip, 3, strip, ffn), bf16)
    dma = pltpu.SemaphoreType.DMA
    return pl.pallas_call(
        experts_kernel,
        out_shape=[
            jax.ShapeDtypeStruct((tall, width), bf16),
            jax.ShapeDtypeStruct((tall, width), bf16),
            jax.ShapeDtypeStruct((tall, 1), f32),
            grads,
            grads,
        ],
        in_specs=[hbm, hbm, vmem, hbm, hbm],
        out_specs=[vmem, vmem, vmem, hbm, hbm],
        scratch_shapes=[
            pltpu.VMEM((tall, width), bf16),
            pltpu.VMEM((tall, width), bf16),
            pltpu.VMEM((2,) + own.shape, bf16),
            pltpu.VMEM((tall, 256), f32),
            pltpu.VMEM((tall, 256), f32),
            pltpu.VMEM((tall, 256), f32),
            pltpu.VMEM((tall, 2 * ffn), bf16),
            pltpu.VMEM((tall, 2 * ffn), bf16),
            pltpu.VMEM((tall, 2 * ffn), bf16),
            pltpu.VMEM((2, 2, 256 // strip, 3, strip, ffn), bf16),
            dma((4,)),
            dma((2, 2)),
        ],
        compiler_params=pltpu.CompilerParams(vmem_limit_bytes=60 * 2**20),
    )(x, cot, weight, own, other)


def collector(nz, nc, pick_t, items, sems):
    z, c, t = places()
    to_s, to_r, own_sem, sib_s, sib_r, line_s, line_r, keep_sem = sems
    rows = items[0][2].shape[1]
    mine_at = pl.ds(pl.multiple_of(t * rows, rows), rows)
    give_at = pl.ds(pl.multiple_of((1 - t) * rows, rows), rows)
    count = len(items)

    def to_copy(slot, k, step, source, target):
        src, got = items[k][:2]
        return remote(
            src.at[target, slot], got.at[slot, source], to_s.at[k, slot, step - 1], to_r.at[k, slot, step - 1], ctx=target
        )

    def own_copy(slot, k):
        src, got = items[k][:2]
        return pltpu.make_async_copy(src.at[c, slot], got.at[slot, c], own_sem.at[k, slot])

    def sib_copy(slot, k):
        give, sib = items[k][3:5]
        return remote(give.at[slot], sib.at[slot], sib_s.at[k, slot], sib_r.at[k, slot], tp=1 - t)

    def line_copy(slot, k, half, source, target):
        src = items[k][2 if half == 0 else 4]
        return remote(src.at[slot], items[k][5].at[source], line_s.at[k, half, slot], line_r.at[k, source], fsdp=target)

    def keep_copy(slot, k, half):
        src = items[k][2 if half == 0 else 4]
        return pltpu.make_async_copy(src.at[slot], items[k][5].at[z], keep_sem.at[k])

    def goal(slot, half):
        return 2 * (t if half == 0 else 1 - t) + slot

    def forward(slot, k, half):
        target = goal(slot, half)
        pl.when(target != z)(lambda: line_copy(slot, k, half, z, target).start())
        pl.when(target == z)(lambda: keep_copy(slot, k, half).start())

    def begin(slot):
        for k in range(count):
            for step in range(1, nc):
                to_copy(slot, k, step, c, ring(c, step, nc)).start()
            own_copy(slot, k).start()

    def scatter(slot, k):
        got, mine, give = items[k][1:4]
        lanes = mine.shape[-1]
        span = min(lanes, 512)
        tall = got.shape[1] * got.shape[2]

        @pl.loop(0, lanes // span)
        def _(n):
            at = pl.ds(pl.multiple_of(n * span, span), span)
            pairs = got[slot, :, :, at].reshape(tall, span)
            for picks, out in ((mine_at, mine), (give_at, give)):
                out[slot, :, at] = jnp.dot(
                    pick_t[slot, picks, :], pairs, preferred_element_type=jnp.float32
                ).astype(jnp.bfloat16)

    def process(slot):
        for k in range(count):
            own_copy(slot, k).wait()
            for step in range(1, nc):
                source = ring(c, -step, nc)
                to_copy(slot, k, step, source, c).wait_recv()
            scatter(slot, k)
            sib_copy(slot, k).start()
            forward(slot, k, 0)
        for k in range(count):
            sib_copy(slot, k).wait_recv()
            forward(slot, k, 1)

    def join():
        for k in range(count):
            keep_copy(0, k, 0).wait()
            for step in range(1, nz):
                line_copy(0, k, 0, ring(z, -step, nz), z).wait_recv()

    def done():
        for slot in range(2):
            for k in range(count):
                for step in range(1, nc):
                    to_copy(slot, k, step, c, ring(c, step, nc)).wait_send()
                sib_copy(slot, k).wait_send()
                for half in range(2):
                    pl.when(goal(slot, half) != z)(
                        lambda: line_copy(slot, k, half, z, goal(slot, half)).wait_send()
                    )

    return begin, process, join, done


def collector_scratch(nz, nc, most, rows, widths):
    dma = pltpu.SemaphoreType.DMA
    bf16 = jnp.bfloat16
    count = len(widths)
    bufs = []
    for w in widths:
        bufs += [pltpu.VMEM((2, nc, most, w), bf16)]
        bufs += [pltpu.VMEM((2, rows, w), bf16)] * 3
        bufs += [pltpu.VMEM((nz, rows, w), bf16)]
    sems = [
        dma((count, 2, nc - 1)), dma((count, 2, nc - 1)), dma((count, 2)), dma((count, 2)), dma((count, 2)),
        dma((count, 2, 2)), dma((count, nz)), dma((count,)),
    ]
    return bufs, sems


def return_kernel(
    nz, nc, r, g, pick_t, residual, probs, kept, router, gain, cot,
    logits_grad, gain_grad, residual_grad, attn_grad, *scratch,
):
    z, c, t = places()
    f32, bf16 = jnp.float32, jnp.bfloat16
    rows, width = residual.shape
    r_line, g_line = scratch[4], scratch[9]
    row_s, row_r, pass_s, pass_r = scratch[18:]
    items = ((r,) + scratch[:5], (g,) + scratch[5:10])
    begin, process, join, done = collector(nz, nc, pick_t, items, scratch[10:18])
    greet(nz, nc, True)
    for slot in range(2):
        begin(slot)
    for slot in range(2):
        process(slot)
    join()
    pairs = jnp.zeros((rows, 128), f32)
    for source in range(nz):
        pairs = pairs + g_line[source, :, 0:128].astype(f32) + g_line[source, :, 128:256].astype(f32)
    pairs = pairs * kept[...]
    prob = probs[...]
    grad_logits = (prob * (pairs - jnp.sum(prob * pairs, -1, keepdims=True))).astype(bf16)
    logits_grad[...] = grad_logits
    gain_grad[...] = jnp.zeros_like(gain_grad)
    chunk = 16

    @pl.loop(0, rows // chunk)
    def _(k):
        at = pl.ds(pl.multiple_of(k * chunk, chunk), chunk)
        full = pl.ds(pl.multiple_of(t * rows + k * chunk, chunk), chunk)
        res = residual[at, :]
        grad = r_line[0, at, :].astype(f32)
        for source in range(1, nz):
            grad = grad + r_line[source, at, :].astype(f32)
        grad = grad + jnp.dot(logits_grad[at, :], router[...], preferred_element_type=f32)
        inv = lax.rsqrt(jnp.mean(res * res, -1, keepdims=True) + EPS)
        gain_grad[...] += jnp.sum((grad * res * inv).reshape(chunk // 8, 8, width), 0)
        weighted = grad * gain[...]
        inner = jnp.sum(weighted * res, -1, keepdims=True)
        out = cot[full, :].astype(f32) + inv * weighted - res * (inv * inv * inv) * inner / width
        residual_grad[at, :] = out
        attn_grad[c, t, at, :] = out.astype(bf16)

    def row_copy(step, source, target):
        return remote(attn_grad.at[source, t], attn_grad.at[source, t], row_s.at[step], row_r.at[step], ctx=target)

    def pass_copy(step, source, core):
        return remote(attn_grad.at[source, core], attn_grad.at[source, core], pass_s.at[step], pass_r.at[step], tp=1 - t)

    for step in range(1, nc):
        row_copy(step, c, ring(c, step, nc)).start()
    pass_copy(0, c, t).start()
    for step in range(1, nc):
        source = ring(c, -step, nc)
        row_copy(step, source, source).wait_recv()
        pass_copy(step, source, t).start()
    for step in range(nc):
        source = ring(c, -step, nc)
        pass_copy(step, source, 1 - t).wait_recv()
        pass_copy(step, source, t).wait_send()
        if step:
            row_copy(step, c, source).wait_send()
    done()


def give_back(r, g, pick_t, residual, probs, kept, router, gain, cot):
    nz, nc = lax.axis_size("fsdp"), lax.axis_size("ctx")
    rows, width = residual.shape
    dma = pltpu.SemaphoreType.DMA
    bf16, f32 = jnp.bfloat16, jnp.float32
    vmem = pl.BlockSpec(memory_space=pltpu.VMEM)
    hbm = pl.BlockSpec(memory_space=pl.ANY)
    bufs, sems = collector_scratch(nz, nc, r.shape[2], rows, (width, 256))
    return pl.pallas_call(
        functools.partial(return_kernel, nz, nc),
        out_shape=[
            jax.ShapeDtypeStruct((rows, 128), bf16),
            jax.ShapeDtypeStruct((8, width), f32),
            jax.ShapeDtypeStruct((rows, width), f32),
            jax.ShapeDtypeStruct((nc, 2, rows, width), bf16),
        ],
        in_specs=[hbm] * 2 + [vmem] * 7,
        out_specs=[vmem] * 4,
        scratch_shapes=bufs + sems + [dma((nc,)), dma((nc,)), dma((nc,)), dma((nc,))],
        compiler_params=pltpu.CompilerParams(
            collective_id=2, has_side_effects=True, vmem_limit_bytes=56 * 2**20
        ),
    )(r, g, pick_t, residual, probs, kept, router, gain, cot)


def final_kernel(
    nz, nc, part, tok, gain, residual_grad, dw, dwo, small, y, pick_t, residual,
    tokens_grad, dw_out, dwo_out, small_out, layer,
    sib, rs_send, rs_recv, tok_grad, gain_acc, dw_up, dw_down, dwo_up, dwo_down, dw_to, dwo_to,
    dw_next, dwo_next, small_line, small_plane, small_sib, small_a, small_b,
    sib_s, sib_r, rs_s, rs_r, line_s, line_r, to_s, to_r, tg_s, tg_r, sm_s, sm_r, sp_s, sp_r, ss_s, ss_r,
    layer_send, lay_s, lay_r, *scratch,
):
    z, c, t = places()
    f32, bf16 = jnp.float32, jnp.bfloat16
    rows, width = residual_grad.shape
    piece = width // 2
    chunk = 16
    y_line = scratch[4]
    begin, process, join, done = collector(nz, nc, pick_t, ((y,) + scratch[:5],), scratch[5:])
    greet(nz, nc, True)

    bufs = ((dw, dw_up, dw_down), (dwo, dwo_up, dwo_down))
    outs = (dw_next, dwo_next)

    def hop(way, step, k, target):
        src = outs[k].at[way, step]
        return remote(src, bufs[k][1 + way].at[step], line_s.at[way, step, k], line_r.at[way, step, k], fsdp=target)

    def add_to(k, way, step, shard, joined):
        own, out = bufs[k][0], outs[k]
        got = bufs[k][1 + way]
        height = own.shape[2]
        tile = 32

        @pl.loop(0, nc * (height // tile))
        def _(n):
            q, at = n // (height // tile), pl.ds(pl.multiple_of(lax.rem(n, height // tile) * tile, tile), tile)
            value = own[shard, q, at, :]
            if joined:
                value = (value.astype(f32) + got[step, q, at, :].astype(f32)).astype(bf16)
            out[way, step, q, at, :] = value

    def line_step(step):
        for way in range(2):
            shard = nz - 1 - step if way == 0 else step
            ahead = z + 1 if way == 0 else z - 1
            behind = z - 1 if way == 0 else z + 1
            first = z == 0 if way == 0 else z == nz - 1
            sends = shard > z if way == 0 else shard < z
            gets = (z > 0) & (shard >= z) if way == 0 else (z < nz - 1) & (shard <= z)

            @pl.when(gets)
            def _():
                for k in range(2):
                    hop(way, step, k, behind).wait_recv()

            @pl.when(sends & jnp.logical_not(first))
            def _():
                for k in range(2):
                    add_to(k, way, step, shard, True)
                    hop(way, step, k, ahead).start()

    def line_begin():
        for way in range(2):
            first = z == 0 if way == 0 else z == nz - 1

            @pl.when(first)
            def _():
                for step in range(nz - 1):
                    shard = nz - 1 - step if way == 0 else step
                    for k in range(2):
                        add_to(k, way, step, shard, False)
                        hop(way, step, k, z + 1 if way == 0 else z - 1).start()

    def sib_copy(q):
        return remote(part.at[q, 1 - t], sib.at[q], sib_s.at[q], sib_r.at[q], tp=1 - t)

    def rs_copy(step, target):
        return remote(rs_send.at[step], rs_recv.at[step], rs_s.at[step], rs_r.at[step], ctx=target)

    for step in range(1, nc + 1):
        sib_copy(ring(c, step, nc)).start()
    line_begin()
    for step in range(1, nc):
        q = ring(c, step, nc)
        sib_copy(q).wait_recv()

        @pl.loop(0, rows // chunk)
        def _(k):
            at = pl.ds(pl.multiple_of(k * chunk, chunk), chunk)
            rs_send[step - 1, at, :] = (part[q, t, at, :].astype(f32) + sib[q, at, :].astype(f32)).astype(bf16)

        rs_copy(step - 1, q).start()
    sib_copy(c).wait_recv()
    begin(0)
    line_step(0)
    begin(1)
    for step in range(1, nc):
        rs_copy(step - 1, c).wait_recv()
    gain_acc[...] = jnp.zeros_like(gain_acc)

    @pl.loop(0, rows // chunk)
    def _(k):
        at = pl.ds(pl.multiple_of(k * chunk, chunk), chunk)
        full = pl.ds(pl.multiple_of(t * rows + k * chunk, chunk), chunk)
        grad = part[c, t, at, :].astype(f32) + sib[c, at, :].astype(f32)
        for step in range(nc - 1):
            grad = grad + rs_recv[step, at, :].astype(f32)
        x = tok[full, :].astype(f32)
        inv = lax.rsqrt(jnp.mean(x * x, -1, keepdims=True) + EPS)
        gain_acc[...] += jnp.sum((grad * x * inv).reshape(chunk // 8, 8, width), 0)
        weighted = grad * gain[...]
        inner = jnp.sum(weighted * x, -1, keepdims=True)
        out = residual_grad[at, :] + inv * weighted - x * (inv * inv * inv) * inner / width
        tok_grad[at, :] = out.astype(bf16)
        tokens_grad[full, :] = out.astype(bf16)

    def grad_copy(core):
        return remote(
            tok_grad, tokens_grad.at[pl.ds(pl.multiple_of(core * rows, rows), rows)], tg_s, tg_r, tp=1 - t
        )

    grad_copy(t).start()

    small_a[...] = small[...]
    total = jnp.sum(gain_acc[...], 0, keepdims=True)
    for strip in range(nz * nc):
        small_a[strip // nc, strip % nc, pl.ds(17, 1), :] = total[:, strip * 128 : (strip + 1) * 128]

    def small_copy(step, shard, target):
        return remote(small_a.at[shard], small_line.at[step], sm_s.at[step], sm_r.at[step], fsdp=target)

    def plane_copy(step, shard, target):
        return remote(small_b.at[shard], small_plane.at[step], sp_s.at[step], sp_r.at[step], ctx=target)

    for step in range(1, nz):
        small_copy(step - 1, ring(z, step, nz), ring(z, step, nz)).start()
    line_step(1)
    process(0)
    line_step(2)
    for step in range(1, nz):
        small_copy(step - 1, z, z).wait_recv()
    value = small_a[z]
    for step in range(nz - 1):
        value = value + small_line[step]
    small_b[...] = value
    for step in range(1, nc):
        plane_copy(step - 1, ring(c, step, nc), ring(c, step, nc)).start()

    def close(k, out, to):
        own, up, down = bufs[k]
        height = own.shape[2]
        tile = 32

        @pl.loop(0, nc * (height // tile))
        def _(n):
            q, at = n // (height // tile), pl.ds(pl.multiple_of(lax.rem(n, height // tile) * tile, tile), tile)
            base = own[z, q, at, :].astype(f32)
            above = up[jnp.minimum(nz - 1 - z, nz - 2), q, at, :].astype(f32)
            below = down[jnp.minimum(z, nz - 2), q, at, :].astype(f32)
            base = base + jnp.where(z > 0, above, 0.0) + jnp.where(z < nz - 1, below, 0.0)
            to[q, at, :] = base.astype(bf16)

    close(0, dw_out, dw_to)
    close(1, dwo_out, dwo_to)

    def to_copy(k, step, source, target):
        src, dst = ((dw_to, dw_out), (dwo_to, dwo_out))[k]
        return remote(src.at[target], dst.at[source], to_s.at[k, step], to_r.at[k, step], ctx=target)

    for step in range(1, nc):
        for k in range(2):
            to_copy(k, step - 1, c, ring(c, step, nc)).start()
    def layer_copy(core):
        return remote(
            layer_send.at[:, pl.ds(pl.multiple_of((1 - t) * piece, piece), piece)],
            layer.at[pl.ds(pl.multiple_of(core * rows, rows), rows)],
            lay_s, lay_r, tp=1 - t,
        )

    process(1)
    join()

    @pl.loop(0, rows // chunk)
    def _(k):
        at = pl.ds(pl.multiple_of(k * chunk, chunk), chunk)
        full = pl.ds(pl.multiple_of(t * rows + k * chunk, chunk), chunk)
        total = residual[at, :]
        for source in range(nz):
            total = total + y_line[source, at, :].astype(f32)
        layer_send[at, :] = total.astype(bf16)
        layer[full, :] = layer_send[at, pl.ds(pl.multiple_of(t * piece, piece), piece)]

    layer_copy(t).start()
    dw_out[c, :, :] = dw_to[c, :, :]
    dwo_out[c, :, :] = dwo_to[c, :, :]
    for step in range(1, nc):
        plane_copy(step - 1, c, c).wait_recv()
    value = small_b[c]
    for step in range(nc - 1):
        value = value + small_plane[step]
    small_out[...] = value
    final = remote(small_out, small_sib, ss_s, ss_r, tp=1 - t)
    final.start()
    final.wait()
    small_out[...] = value + small_sib[...]
    for step in range(1, nc):
        source = ring(c, -step, nc)
        for k in range(2):
            src, dst = ((dw_to, dw_out), (dwo_to, dwo_out))[k]
            remote(
                src.at[c], dst.at[source], to_s.at[k, step - 1], to_r.at[k, step - 1], ctx=source
            ).wait_recv()
    grad_copy(1 - t).wait_recv()
    grad_copy(t).wait_send()
    layer_copy(1 - t).wait_recv()
    layer_copy(t).wait_send()
    done()
    for step in range(1, nc):
        for k in range(2):
            to_copy(k, step - 1, c, ring(c, step, nc)).wait_send()
        plane_copy(step - 1, ring(c, step, nc), ring(c, step, nc)).wait_send()
        rs_copy(step - 1, c).wait_send()
    for step in range(1, nz):
        small_copy(step - 1, ring(z, step, nz), ring(z, step, nz)).wait_send()
    for q in range(nc):
        sib_copy(q).wait_send()
    for step in range(nz - 1):
        for way in range(2):
            shard = nz - 1 - step if way == 0 else step
            ahead = z + 1 if way == 0 else z - 1
            sends = shard > z if way == 0 else shard < z

            @pl.when(sends)
            def _():
                for k in range(2):
                    hop(way, step, k, ahead).wait_send()


def finish(part, tok, gain, residual_grad, dw, dwo, small, y, pick_t, residual):
    nz, nc = lax.axis_size("fsdp"), lax.axis_size("ctx")
    rows, width = residual_grad.shape
    dma = pltpu.SemaphoreType.DMA
    bf16, f32 = jnp.bfloat16, jnp.float32
    vmem = pl.BlockSpec(memory_space=pltpu.VMEM)
    one, two = dw.shape[1:], dwo.shape[1:]
    bufs, sems = collector_scratch(nz, nc, y.shape[2], rows, (width,))
    tiny = small.shape[2:]
    return pl.pallas_call(
        functools.partial(final_kernel, nz, nc),
        out_shape=[
            jax.ShapeDtypeStruct((2 * rows, width), bf16),
            jax.ShapeDtypeStruct(one, bf16),
            jax.ShapeDtypeStruct(two, bf16),
            jax.ShapeDtypeStruct(tiny, f32),
            jax.ShapeDtypeStruct((2 * rows, width // 2), bf16),
        ],
        in_specs=[vmem] * 7 + [pl.BlockSpec(memory_space=pl.ANY)] + [vmem] * 2,
        out_specs=[vmem] * 5,
        scratch_shapes=[
            pltpu.VMEM((nc, rows, width), bf16),
            pltpu.VMEM((nc - 1, rows, width), bf16),
            pltpu.VMEM((nc - 1, rows, width), bf16),
            pltpu.VMEM((rows, width), bf16),
            pltpu.VMEM((8, width), f32),
            pltpu.VMEM((nz - 1,) + one, bf16),
            pltpu.VMEM((nz - 1,) + one, bf16),
            pltpu.VMEM((nz - 1,) + two, bf16),
            pltpu.VMEM((nz - 1,) + two, bf16),
            pltpu.VMEM(one, bf16),
            pltpu.VMEM(two, bf16),
            pltpu.VMEM((2, nz - 1) + one, bf16),
            pltpu.VMEM((2, nz - 1) + two, bf16),
            pltpu.VMEM((nz - 1,) + small.shape[1:], f32),
            pltpu.VMEM((nc - 1,) + tiny, f32),
            pltpu.VMEM(tiny, f32),
            pltpu.VMEM(small.shape, f32),
            pltpu.VMEM(small.shape[1:], f32),
            dma((nc,)), dma((nc,)), dma((nc - 1,)), dma((nc - 1,)),
            dma((2, nz - 1, 2)), dma((2, nz - 1, 2)),
            dma((2, nc - 1)), dma((2, nc - 1)), dma, dma,
            dma((nz - 1,)), dma((nz - 1,)), dma((nc - 1,)), dma((nc - 1,)), dma, dma,
            pltpu.VMEM((rows, width), bf16), dma, dma,
        ] + bufs + sems,
        compiler_params=pltpu.CompilerParams(
            collective_id=3, has_side_effects=True, vmem_limit_bytes=60 * 2**20
        ),
    )(part, tok, gain, residual_grad, dw, dwo, small, y, pick_t, residual)


def one_chip(
    tokens,
    w_query,
    w_key,
    w_value,
    w_out,
    gain_attn,
    gain_query,
    gain_key,
    gain_moe,
    w_router,
    w_experts,
    routes,
    cotangent,
):
    z, c, t = lax.axis_index("fsdp"), lax.axis_index("ctx"), lax.axis_index("tp")
    nz, nc = lax.axis_size("fsdp"), lax.axis_size("ctx")
    block, width = tokens.shape[1], tokens.shape[2]
    rows = block // 2
    tall = block * nc
    deep = width // nz
    ffn = w_experts.shape[3]
    most = block * TOPK * 9 // (8 * E)
    bf16, f32 = jnp.bfloat16, jnp.float32

    token_half = lax.dynamic_slice_in_dim(tokens[0], t * rows, rows, 0)
    cotan_half = lax.dynamic_slice_in_dim(cotangent[0], t * rows, rows, 0)
    local = w_query.shape[1] // nc
    small = jnp.concatenate([w_router.T.reshape(-1), gain_attn, gain_moe, gain_query, gain_key])
    total = small.shape[0]
    small = jnp.pad(small, (0, -total % 2048))
    small = small.reshape(-1, 128)
    ids = jnp.arange(E, dtype=jnp.int32)
    named = jnp.any(routes[0][:, :, None] == ids, 1)
    below = jnp.tril(jnp.ones((block, block), bf16), -1)
    rank = jnp.where(named, dot(below, named.astype(bf16)), -1.0).T
    x_rows, w_qkv, w_o, small, _, rank_seq, pick, cot_rows = load(
        tokens[0], cotangent[0], w_query, w_key, w_value, w_out, small, rank, most
    )
    w_qkv = w_qkv.reshape(width, 3 * local)
    w_o = w_o.transpose(1, 0, 2).reshape(local, width)
    small = small.reshape(nz, -1)
    router = small[:, : E * deep].reshape(nz, E, deep).transpose(1, 0, 2).reshape(E, width)
    at = E * deep
    attn_gain = small[:, at : at + deep].reshape(-1).astype(f32)
    moe_gain = small[:, at + deep : at + 2 * deep].reshape(-1).astype(f32)
    at, part = at + 2 * deep, HD // nz
    query_gain = small[:, at : at + part].reshape(-1).astype(f32)
    key_gain = small[:, at + part : at + 2 * part].reshape(-1).astype(f32)

    own = lax.dynamic_slice_in_dim(w_experts, c * nz, nz, 2).transpose(2, 1, 0, 3)
    own, w_qkv = lax.optimization_barrier((own, w_qkv))
    own = exchange(own, "fsdp")

    counts = jnp.sum((rank_seq >= 0).astype(f32), 2)
    earlier = jnp.sum(jnp.where(jnp.arange(nc)[:, None] < c, counts, 0.0), 0)
    kept = ((rank >= 0) & (rank + earlier[:, None] < CAP)).astype(f32).T
    kept = lax.dynamic_slice_in_dim(kept, t * rows, rows, 0)

    x_rows = x_rows.astype(f32)
    place = jnp.arange(tall, dtype=jnp.int32)
    half_dim = HD // 2
    inv_freq = jnp.exp(jnp.arange(half_dim, dtype=f32) * (-2.0 * math.log(ROPE_BASE) / HD))
    angles = place.astype(f32)[:, None] * inv_freq[None, :]
    cos_full = jnp.concatenate([jnp.cos(angles)] * 2, -1)[:, None, :]
    sin_full = jnp.concatenate([jnp.sin(angles)] * 2, -1)[:, None, :]
    normed_one = (x_rows * rms_scale(x_rows) * attn_gain).astype(bf16)
    proj = dot(normed_one, w_qkv).reshape(tall, 3, local // HD, HD)
    query_heads, key_heads = proj[:, 0], proj[:, 1]
    values = proj[:, 2].astype(bf16)
    query_inv, key_inv = rms_scale(query_heads), rms_scale(key_heads)
    queries = apply_rope(query_heads * query_inv * query_gain, cos_full, sin_full).astype(bf16)
    keys = apply_rope(key_heads * key_inv * key_gain, cos_full, sin_full).astype(bf16)
    score_scale = 1.0 / math.sqrt(HD)
    scores = jnp.einsum("qhd,khd->hqk", queries, keys, preferred_element_type=f32) * score_scale
    maximum = jnp.max(scores, -1, keepdims=True)
    exp_scores = jnp.exp(scores - maximum)
    denominator = jnp.sum(exp_scores, -1, keepdims=True)
    attn_probs = exp_scores / denominator
    log_total = maximum + jnp.log(denominator)
    context = jnp.einsum("hqk,khd->qhd", attn_probs.astype(bf16), values, preferred_element_type=f32)
    context = context.astype(bf16).reshape(tall, local)
    attn_part = dot(context, w_o).astype(bf16).reshape(nc, 2, rows, width)
    kept_wide = jnp.pad(kept, ((0, 0), (0, 128 - E)))
    router_wide = jnp.pad(router, ((0, 128 - E), (0, 0)))
    residual, normed_two, router_probs, x_in, g_in = dispatch(
        attn_part, tokens[0], moe_gain[None], router_wide, kept_wide, pick
    )
    own, x_in = lax.optimization_barrier((own, x_in))
    other = swap(own)
    x_in = x_in.reshape(nc * 2 * most, width)
    cot_rows = cot_rows.reshape(nc * 2 * most, width)
    g_in = g_in.reshape(nc * 2 * most, 2, 128)[:, :, :E].astype(f32)
    mine_id = c * nz + z
    weight = jnp.sum(jnp.where(ids == mine_id, g_in, 0.0), (1, 2))[:, None]

    chips = nz * nc
    strip = width // chips
    out_rows, back_rows, pair_grad, own_grad, other_grad = experts(x_in, cot_rows, weight, own, other, strip)
    dw_experts = (own_grad.astype(f32) + swap(other_grad).astype(f32)).astype(bf16)
    dw_gate = exchange(dw_experts[:, :1], ("fsdp", "ctx"))
    high, low = two_parts(jnp.where(jnp.arange(128) == mine_id, pair_grad, 0.0))
    shape = (nc, 2, most, -1)
    pick_t = pick.transpose(0, 2, 1)
    grad_logits, dgain_moe, grad_residual, grad_attn = give_back(
        back_rows.reshape(shape),
        jnp.concatenate([high, low], 1).reshape(shape),
        pick_t,
        residual,
        router_probs,
        kept_wide,
        router_wide,
        moe_gain[None],
        cotangent[0],
    )

    dw_router = dot_tn(normed_two, grad_logits[:, :E])
    dgain_moe = jnp.sum(dgain_moe, 0)
    dw_rest, grad_attn = lax.optimization_barrier((dw_experts[:, 1:], grad_attn))
    dw_rest = exchange(dw_rest, ("fsdp", "ctx"))
    grad_attn = grad_attn.reshape(tall, width)

    dw_out = dot_tn(context, grad_attn).astype(bf16)
    grad_context = dot_nt(grad_attn, w_o).astype(bf16).reshape(tall, -1, HD)
    scores = jnp.einsum("qhd,khd->hqk", queries, keys, preferred_element_type=f32) * score_scale
    attn_probs = jnp.exp(scores - log_total)
    grad_probs = jnp.einsum("qhd,khd->hqk", grad_context, values, preferred_element_type=f32)
    grad_scores = attn_probs * (grad_probs - jnp.sum(attn_probs * grad_probs, -1, keepdims=True))
    grad_scores = grad_scores.astype(bf16)
    grad_queries = jnp.einsum("hqk,khd->qhd", grad_scores, keys, preferred_element_type=f32) * score_scale
    grad_keys = jnp.einsum("hqk,qhd->khd", grad_scores, queries, preferred_element_type=f32) * score_scale
    grad_values = jnp.einsum(
        "hqk,qhd->khd", attn_probs.astype(bf16), grad_context, preferred_element_type=f32
    ).astype(bf16)
    grad_qnormed = rope_back(grad_queries, cos_full, sin_full)
    grad_knormed = rope_back(grad_keys, cos_full, sin_full)
    dgain_query = jnp.sum(grad_qnormed * query_heads * query_inv, (0, 1))
    dgain_key = jnp.sum(grad_knormed * key_heads * key_inv, (0, 1))
    grad_qproj = norm_back(grad_qnormed, query_heads, query_inv, query_gain).astype(bf16)
    grad_kproj = norm_back(grad_knormed, key_heads, key_inv, key_gain).astype(bf16)
    grad_proj = jnp.stack([grad_qproj, grad_kproj, grad_values], 1).reshape(tall, 3 * local)
    dw_qkv = dot_tn(normed_one, grad_proj).astype(bf16)
    grad_normed_part = dot_nt(grad_proj, w_qkv).astype(bf16).reshape(nc, 2, rows, width)
    head_part = HD // chips
    heads = [dgain_query.reshape(chips, 1, head_part), dgain_key.reshape(chips, 1, head_part)]
    heads = jnp.pad(jnp.concatenate(heads, 2), ((0, 0), (0, 0), (0, strip - 2 * head_part)))
    sums = jnp.concatenate(
        [
            dw_router.reshape(chips, E, strip),
            dgain_moe.reshape(chips, 1, strip),
            jnp.zeros((chips, 1, strip), f32),
            heads,
            jnp.zeros((chips, 24 - E - 3, strip), f32),
        ],
        1,
    ).reshape(nz, nc, 24, strip)
    dw_experts = jnp.concatenate([dw_gate, dw_rest], 1).reshape(nz, nc, 3, strip, ffn).transpose(3, 2, 1, 0, 4)
    dw_experts = dw_experts.reshape(strip, 3, E, ffn).astype(f32)
    tokens_grad, got_qkv, got_out, sums, layer_out = finish(
        grad_normed_part,
        tokens[0],
        attn_gain[None],
        grad_residual,
        dw_qkv.reshape(nz, nc, strip, 3 * local),
        dw_out.reshape(local, nz, nc, strip).transpose(1, 2, 0, 3),
        sums,
        out_rows.reshape(shape),
        pick_t,
        residual,
    )
    got_qkv = got_qkv.astype(f32).reshape(nc, strip, 3, local)
    got_qkv = got_qkv.transpose(2, 1, 0, 3).reshape(3, strip, nc * local)
    return (
        layer_out[None],
        tokens_grad[None],
        got_qkv[0],
        got_qkv[1],
        got_qkv[2],
        got_out.astype(f32).reshape(nc * local, strip),
        sums[E + 1],
        sums[E + 2, :head_part],
        sums[E + 2, head_part : 2 * head_part],
        sums[E],
        sums[:E].reshape(strip, E),
        dw_experts,
    )


def solution(mesh):
    chips = mesh.shape["fsdp"] * mesh.shape["ctx"]
    plain = chips == E and mesh.shape["fsdp"] == 4 and mesh.shape["tp"] == 2
    return jax.shard_map(
        one_chip if plain else general,
        mesh=mesh,
        in_specs=(
            P("fsdp", "ctx", None),
            P("fsdp", "tp"),
            P("fsdp", "tp"),
            P("fsdp", "tp"),
            P("tp", "fsdp"),
            P("fsdp"),
            P("fsdp"),
            P("fsdp"),
            P("fsdp"),
            P("fsdp", None),
            P("fsdp", None, None, "tp"),
            P("fsdp", "ctx", None),
            P("fsdp", "ctx", None),
        ),
        out_specs=(
            P("fsdp", "ctx", "tp"),
            P("fsdp", "ctx", None),
            P(("fsdp", "ctx"), "tp"),
            P(("fsdp", "ctx"), "tp"),
            P(("fsdp", "ctx"), "tp"),
            P("tp", ("fsdp", "ctx")),
            P(("fsdp", "ctx")),
            P(("fsdp", "ctx")),
            P(("fsdp", "ctx")),
            P(("fsdp", "ctx")),
            P(("fsdp", "ctx"), None),
            P(("fsdp", "ctx"), None, None, "tp"),
        ),
        check_vma=False,
    )
```

```python
import functools
import math

import jax
import jax.numpy as jnp
from jax import lax
from jax.experimental import pallas as pl
from jax.experimental.pallas import tpu as pltpu
from jax.sharding import PartitionSpec as P

HD = 128
TOPK = 8
E = 16
CAP = 512
MESH = pl.DeviceIdType.MESH


EPS = 1e-06
ROPE_BASE = 10000.0


def prefix(value, axis, join, neutral):
    count, mine = (lax.axis_size(axis), lax.axis_index(axis))
    pieces = lax.all_gather(value, axis)
    running = jnp.full_like(value, 0) + jnp.asarray(neutral, value.dtype)

    def lap(position, running):
        longer = join(running, pieces[position])
        return jnp.where(position < mine, longer, running)

    return lax.fori_loop(0, count - 1, lap, running)


def rms_scale(values):
    return lax.rsqrt(jnp.mean(values * values, -1, keepdims=True) + EPS)


def norm_back(grad_normed, values, inv_rms, gain_vec):
    weighted = grad_normed * gain_vec.astype(jnp.float32)
    inner_sum = jnp.sum(weighted * values, -1, keepdims=True)
    return (
        inv_rms * weighted - values * (inv_rms * inv_rms * inv_rms) * inner_sum / values.shape[-1]
    )


def rope_tables(first, length):
    half_dim = HD // 2
    inv_freq = jnp.exp(jnp.arange(half_dim, dtype=jnp.float32) * (-2.0 * math.log(ROPE_BASE) / HD))
    places = (first + jnp.arange(length, dtype=jnp.int32)).astype(jnp.float32)
    angles = places[:, None] * inv_freq[None, :]
    cos_table = jnp.cos(angles)
    sin_table = jnp.sin(angles)
    cos_full = jnp.concatenate([cos_table, cos_table], -1)[:, None, :]
    sin_full = jnp.concatenate([sin_table, sin_table], -1)[:, None, :]
    return (cos_full, sin_full)


def rotate(values):
    half_dim = values.shape[-1] // 2
    return jnp.concatenate([-values[..., half_dim:], values[..., :half_dim]], -1)


def rotate_back(values):
    half_dim = values.shape[-1] // 2
    return jnp.concatenate([values[..., half_dim:], -values[..., :half_dim]], -1)


def apply_rope(values, cos_full, sin_full):
    return values * cos_full + rotate(values) * sin_full


def rope_back(grads, cos_full, sin_full):
    return grads * cos_full + rotate_back(grads * sin_full)


def add_counts(earlier, later):
    return earlier + later


def general(
    tokens,
    w_query,
    w_key,
    w_value,
    w_out,
    gain_attn,
    gain_query,
    gain_key,
    gain_moe,
    w_router,
    w_experts,
    routes,
    cotangent,
):
    seq_count, block_len, model_width = tokens.shape
    row_count = seq_count * block_len
    (
        full_query,
        full_key,
        full_value,
        full_out,
        router_full,
        attn_gain,
        query_gain,
        key_gain,
        moe_gain,
    ) = (
        lax.all_gather(w_query, "fsdp", axis=0, tiled=True),
        lax.all_gather(w_key, "fsdp", axis=0, tiled=True),
        lax.all_gather(w_value, "fsdp", axis=0, tiled=True),
        lax.all_gather(w_out, "fsdp", axis=1, tiled=True),
        lax.all_gather(w_router, "fsdp", axis=0, tiled=True),
        lax.all_gather(gain_attn, "fsdp", axis=0, tiled=True),
        lax.all_gather(gain_query, "fsdp", axis=0, tiled=True),
        lax.all_gather(gain_key, "fsdp", axis=0, tiled=True),
        lax.all_gather(gain_moe, "fsdp", axis=0, tiled=True),
    )
    local_width = full_query.shape[1]
    head_count = local_width // HD
    head_shape = (seq_count, block_len, head_count, HD)
    token_rows = tokens.reshape(row_count, model_width).astype(jnp.float32)
    inv_one = rms_scale(token_rows)
    normed_one = (token_rows * inv_one * attn_gain.astype(jnp.float32)).astype(jnp.bfloat16)
    query_proj = jnp.dot(normed_one, full_query, preferred_element_type=jnp.float32)
    key_proj = jnp.dot(normed_one, full_key, preferred_element_type=jnp.float32)
    value_proj = jnp.dot(normed_one, full_value, preferred_element_type=jnp.float32)
    cos_full, sin_full = rope_tables(lax.axis_index("ctx") * block_len, block_len)
    query_heads = query_proj.reshape(head_shape)
    key_heads = key_proj.reshape(head_shape)
    query_inv = rms_scale(query_heads)
    key_inv = rms_scale(key_heads)
    queries = apply_rope(
        query_heads * query_inv * query_gain.astype(jnp.float32), cos_full, sin_full
    ).astype(jnp.bfloat16)
    keys_local = apply_rope(
        key_heads * key_inv * key_gain.astype(jnp.float32), cos_full, sin_full
    ).astype(jnp.bfloat16)
    keys_local = keys_local.reshape(seq_count, block_len, local_width)
    values_local = value_proj.astype(jnp.bfloat16).reshape(seq_count, block_len, local_width)
    keys_all, values_all = (
        lax.all_gather(keys_local, "ctx", axis=1, tiled=True),
        lax.all_gather(values_local, "ctx", axis=1, tiled=True),
    )
    seq_len = keys_all.shape[1]
    key_rows = keys_all.reshape(seq_count, seq_len, head_count, HD)
    value_rows = values_all.reshape(seq_count, seq_len, head_count, HD)
    score_scale = 1.0 / math.sqrt(HD)
    scores = (
        jnp.einsum("sqhd,skhd->shqk", queries, key_rows, preferred_element_type=jnp.float32)
        * score_scale
    )
    maximum = jnp.max(scores, -1, keepdims=True)
    exp_scores = jnp.exp(scores - maximum)
    denominator = jnp.sum(exp_scores, -1, keepdims=True)
    attn_probs = exp_scores / denominator
    log_total = maximum + jnp.log(denominator)
    context = jnp.einsum(
        "shqk,skhd->sqhd",
        attn_probs.astype(jnp.bfloat16),
        value_rows,
        preferred_element_type=jnp.float32,
    )
    context = context.astype(jnp.bfloat16).reshape(row_count, local_width)
    attn_part = jnp.dot(context, full_out, preferred_element_type=jnp.float32)
    residual = token_rows + lax.psum(attn_part, "tp")
    inv_two = rms_scale(residual)
    normed_two = (residual * inv_two * moe_gain.astype(jnp.float32)).astype(jnp.bfloat16)
    logits = jnp.dot(normed_two, router_full, preferred_element_type=jnp.float32)
    router_probs = jax.nn.softmax(logits, -1)
    pair_count = block_len * TOPK
    route_rows = routes.reshape(seq_count, pair_count)
    expert_ids = jnp.arange(E, dtype=jnp.int32)
    onehot = (route_rows[:, :, None] == expert_ids[None, None, :]).astype(jnp.int32)
    counts = jnp.sum(onehot, 1, dtype=jnp.int32)
    offsets = prefix(counts, "ctx", add_counts, jnp.zeros_like(counts))
    earlier = jnp.cumsum(onehot, 1, dtype=jnp.int32) - onehot
    local_rank = jnp.sum(earlier * onehot, 2, dtype=jnp.int32)
    slot_base = jnp.sum(onehot * offsets[:, None, :], 2, dtype=jnp.int32)
    kept_mask = (slot_base + local_rank < CAP).astype(jnp.float32).reshape(row_count, TOPK)
    block_most = pair_count * 9 // (8 * E)
    expert_span = seq_count * block_most
    seq_ids = jnp.arange(seq_count, dtype=jnp.int32)[:, None]
    buffer_row = (route_rows * expert_span + seq_ids * block_most + local_rank).reshape(
        row_count * TOPK
    )
    token_ids = (
        seq_ids * block_len + jnp.arange(pair_count, dtype=jnp.int32)[None, :] // TOPK
    ).reshape(row_count * TOPK)
    owner_rows = jnp.zeros((E * expert_span,), jnp.int32).at[buffer_row].set(token_ids)
    onehot_f = onehot.astype(jnp.float32).reshape(row_count, TOPK, E)
    gate_weight = jnp.sum(onehot_f * router_probs[:, None, :], 2) * kept_mask
    slot_weight = (
        jnp.zeros((E * expert_span,), jnp.float32)
        .at[buffer_row]
        .set(gate_weight.reshape(row_count * TOPK))
    )
    expert_rows = normed_two[owner_rows].reshape(E, expert_span, model_width)
    cotan_rows = cotangent.reshape(row_count, model_width)
    grad_expert = (slot_weight[:, None] * cotan_rows[owner_rows].astype(jnp.float32)).astype(
        jnp.bfloat16
    )
    grad_expert = grad_expert.reshape(E, expert_span, model_width)
    ffn_local = w_experts.shape[3]
    fsdp_count = lax.axis_size("fsdp")
    ctx_count = lax.axis_size("ctx")
    group_count = fsdp_count * ctx_count
    sharing = group_count // E
    padded_span = -(-expert_span // sharing) * sharing
    part_span = padded_span // sharing
    target_experts = (
        jnp.arange(fsdp_count, dtype=jnp.int32) * ctx_count + lax.axis_index("ctx")
    ) // sharing
    selected = jnp.take(w_experts, target_experts, axis=2)
    owned = lax.all_to_all(selected, "fsdp", split_axis=2, concat_axis=0, tiled=True)[:, :, 0]
    send_rows = expert_rows.reshape(group_count, part_span, model_width)
    send_grads = grad_expert.reshape(group_count, part_span, model_width)
    recv_rows, recv_grads = (
        lax.all_to_all(send_rows, ("fsdp", "ctx"), split_axis=0, concat_axis=0, tiled=True),
        lax.all_to_all(send_grads, ("fsdp", "ctx"), split_axis=0, concat_axis=0, tiled=True),
    )
    rows_flat = recv_rows.reshape(group_count * part_span, model_width)
    grads_flat = recv_grads.reshape(group_count * part_span, model_width)
    gate_act = jnp.dot(rows_flat, owned[:, 0], preferred_element_type=jnp.float32)
    up_act = jnp.dot(rows_flat, owned[:, 1], preferred_element_type=jnp.float32)
    sigmoid_gate = jax.nn.sigmoid(gate_act)
    silu_gate = gate_act * sigmoid_gate
    hidden = (silu_gate * up_act).astype(jnp.bfloat16)
    produced = jnp.einsum("mf,df->md", hidden, owned[:, 2], preferred_element_type=jnp.float32)
    grad_hidden = jnp.dot(grads_flat, owned[:, 2], preferred_element_type=jnp.float32)
    grad_gate = (
        grad_hidden * up_act * sigmoid_gate * (1.0 + gate_act * (1.0 - sigmoid_gate))
    ).astype(jnp.bfloat16)
    grad_up = (grad_hidden * silu_gate).astype(jnp.bfloat16)
    rows_grad = jnp.einsum("mf,df->md", grad_gate, owned[:, 0], preferred_element_type=jnp.float32)
    rows_grad = rows_grad + jnp.einsum(
        "mf,df->md", grad_up, owned[:, 1], preferred_element_type=jnp.float32
    )
    back_out, back_rows = (
        lax.all_to_all(
            produced.reshape(group_count, part_span, model_width).astype(jnp.bfloat16),
            ("fsdp", "ctx"),
            split_axis=0,
            concat_axis=0,
            tiled=True,
        ).astype(jnp.float32),
        lax.all_to_all(
            rows_grad.reshape(group_count, part_span, model_width).astype(jnp.bfloat16),
            ("fsdp", "ctx"),
            split_axis=0,
            concat_axis=0,
            tiled=True,
        ).astype(jnp.float32),
    )
    expert_out = back_out.reshape(E, padded_span, model_width)
    grad_rows = back_rows.reshape(E, padded_span, model_width)
    gate_term = jnp.einsum("md,mf->df", rows_flat, grad_gate, preferred_element_type=jnp.float32)
    up_term = jnp.einsum("md,mf->df", rows_flat, grad_up, preferred_element_type=jnp.float32)
    down_term = jnp.einsum("md,mf->df", grads_flat, hidden, preferred_element_type=jnp.float32)
    owner_terms = jnp.stack([gate_term, up_term, down_term], 1)[:, :, None, :]
    relaid = lax.all_to_all(
        owner_terms.astype(jnp.bfloat16), ("fsdp", "ctx"), split_axis=0, concat_axis=2, tiled=True
    ).astype(owner_terms.dtype)
    dw_experts = jnp.sum(relaid.reshape(relaid.shape[0], 3, E, sharing, ffn_local), 3)
    picked = expert_out.reshape(E * expert_span, model_width)[buffer_row].reshape(
        row_count, TOPK, model_width
    )
    moe_part = jnp.sum(gate_weight[:, :, None] * picked, 1)
    cotan_float = cotan_rows.astype(jnp.float32)
    grad_gate_part = jnp.sum(picked * cotan_float[:, None, :], 2)
    moe_shard = lax.psum_scatter(
        moe_part.astype(jnp.bfloat16), "tp", scatter_dimension=1, tiled=True
    ).astype(jnp.float32)
    piece_width = moe_shard.shape[1]
    residual_shard = lax.dynamic_slice_in_dim(
        residual, lax.axis_index("tp") * piece_width, piece_width, 1
    )
    layer_out = (
        (residual_shard + moe_shard).astype(jnp.bfloat16).reshape(seq_count, block_len, piece_width)
    )
    grad_normed_part = jnp.sum(
        grad_rows.reshape(E * expert_span, model_width)[buffer_row].reshape(
            row_count, TOPK, model_width
        ),
        1,
    )
    grad_normed_sum, grad_gate_sum = (
        lax.psum(grad_normed_part.astype(jnp.bfloat16), "tp").astype(jnp.float32),
        lax.psum(grad_gate_part.astype(jnp.bfloat16), "tp").astype(jnp.float32),
    )
    grad_pick = grad_gate_sum * kept_mask
    grad_router_probs = jnp.sum(onehot_f * grad_pick[:, :, None], 1)
    grad_logits = router_probs * (
        grad_router_probs - jnp.sum(router_probs * grad_router_probs, -1, keepdims=True)
    )
    grad_logits = grad_logits.astype(jnp.bfloat16)
    grad_router_w = jnp.einsum(
        "nd,ne->de", normed_two, grad_logits, preferred_element_type=jnp.float32
    )
    grad_normed_two = grad_normed_sum + jnp.einsum(
        "ne,de->nd", grad_logits, router_full, preferred_element_type=jnp.float32
    )
    grad_moe_gain = jnp.sum(grad_normed_two * residual * inv_two, 0)
    grad_residual = cotan_float + norm_back(grad_normed_two, residual, inv_two, moe_gain)
    grad_attn = grad_residual.astype(jnp.bfloat16)
    grad_w_out = jnp.einsum("nl,nd->ld", context, grad_attn, preferred_element_type=jnp.float32)
    grad_context = jnp.einsum("nd,ld->nl", grad_attn, full_out, preferred_element_type=jnp.float32)
    grad_context = grad_context.astype(jnp.bfloat16).reshape(head_shape)
    scores = (
        jnp.einsum("sqhd,skhd->shqk", queries, key_rows, preferred_element_type=jnp.float32)
        * score_scale
    )
    attn_probs = jnp.exp(scores - log_total)
    grad_probs = jnp.einsum(
        "sqhd,skhd->shqk", grad_context, value_rows, preferred_element_type=jnp.float32
    )
    grad_scores = attn_probs * (grad_probs - jnp.sum(attn_probs * grad_probs, -1, keepdims=True))
    grad_scores = grad_scores.astype(jnp.bfloat16)
    grad_queries = (
        jnp.einsum("shqk,skhd->sqhd", grad_scores, key_rows, preferred_element_type=jnp.float32)
        * score_scale
    )
    grad_keys_all = (
        jnp.einsum("shqk,sqhd->skhd", grad_scores, queries, preferred_element_type=jnp.float32)
        * score_scale
    )
    grad_values_all = jnp.einsum(
        "shqk,sqhd->skhd",
        attn_probs.astype(jnp.bfloat16),
        grad_context,
        preferred_element_type=jnp.float32,
    )
    grad_keys_own, grad_values_own = (
        lax.psum_scatter(
            grad_keys_all.reshape(seq_count, seq_len, local_width).astype(jnp.bfloat16),
            "ctx",
            scatter_dimension=1,
            tiled=True,
        ).astype(jnp.float32),
        lax.psum_scatter(
            grad_values_all.reshape(seq_count, seq_len, local_width).astype(jnp.bfloat16),
            "ctx",
            scatter_dimension=1,
            tiled=True,
        ).astype(jnp.float32),
    )
    grad_qnormed = rope_back(grad_queries, cos_full, sin_full)
    grad_knormed = rope_back(grad_keys_own.reshape(head_shape), cos_full, sin_full)
    grad_qgain = jnp.sum(grad_qnormed * query_heads * query_inv, (0, 1, 2))
    grad_kgain = jnp.sum(grad_knormed * key_heads * key_inv, (0, 1, 2))
    grad_qproj = (
        norm_back(grad_qnormed, query_heads, query_inv, query_gain)
        .astype(jnp.bfloat16)
        .reshape(row_count, local_width)
    )
    grad_kproj = (
        norm_back(grad_knormed, key_heads, key_inv, key_gain)
        .astype(jnp.bfloat16)
        .reshape(row_count, local_width)
    )
    grad_vproj = grad_values_own.astype(jnp.bfloat16).reshape(row_count, local_width)
    grad_wq = jnp.einsum("nd,nl->dl", normed_one, grad_qproj, preferred_element_type=jnp.float32)
    grad_wk = jnp.einsum("nd,nl->dl", normed_one, grad_kproj, preferred_element_type=jnp.float32)
    grad_wv = jnp.einsum("nd,nl->dl", normed_one, grad_vproj, preferred_element_type=jnp.float32)
    grad_normed_one = jnp.einsum(
        "nl,dl->nd", grad_qproj, full_query, preferred_element_type=jnp.float32
    )
    grad_normed_one = grad_normed_one + jnp.einsum(
        "nl,dl->nd", grad_kproj, full_key, preferred_element_type=jnp.float32
    )
    grad_normed_one = grad_normed_one + jnp.einsum(
        "nl,dl->nd", grad_vproj, full_value, preferred_element_type=jnp.float32
    )
    grad_normed_one, grad_qgain, grad_kgain = (
        lax.psum(grad_normed_one.astype(jnp.bfloat16), "tp").astype(jnp.float32),
        lax.psum(grad_qgain.astype(jnp.bfloat16), "tp").astype(jnp.float32),
        lax.psum(grad_kgain.astype(jnp.bfloat16), "tp").astype(jnp.float32),
    )
    grad_attn_gain = jnp.sum(grad_normed_one * token_rows * inv_one, 0)
    tokens_grad = grad_residual + norm_back(grad_normed_one, token_rows, inv_one, attn_gain)
    tokens_grad = tokens_grad.astype(jnp.bfloat16).reshape(seq_count, block_len, model_width)
    dw_query, dw_key, dw_value, dw_out, dw_router, dgain_attn, dgain_query, dgain_key, dgain_moe = (
        lax.psum_scatter(grad_wq, ("fsdp", "ctx"), scatter_dimension=0, tiled=True),
        lax.psum_scatter(grad_wk, ("fsdp", "ctx"), scatter_dimension=0, tiled=True),
        lax.psum_scatter(grad_wv, ("fsdp", "ctx"), scatter_dimension=0, tiled=True),
        lax.psum_scatter(grad_w_out, ("fsdp", "ctx"), scatter_dimension=1, tiled=True),
        lax.psum_scatter(grad_router_w, ("fsdp", "ctx"), scatter_dimension=0, tiled=True),
        lax.psum_scatter(grad_attn_gain, ("fsdp", "ctx"), scatter_dimension=0, tiled=True),
        lax.psum_scatter(grad_qgain, ("fsdp", "ctx"), scatter_dimension=0, tiled=True),
        lax.psum_scatter(grad_kgain, ("fsdp", "ctx"), scatter_dimension=0, tiled=True),
        lax.psum_scatter(grad_moe_gain, ("fsdp", "ctx"), scatter_dimension=0, tiled=True),
    )
    return (
        layer_out,
        tokens_grad,
        dw_query,
        dw_key,
        dw_value,
        dw_out,
        dgain_attn,
        dgain_query,
        dgain_key,
        dgain_moe,
        dw_router,
        dw_experts,
    )


def swap(value):
    return lax.ppermute(value, "tp", [(0, 1), (1, 0)])


def exchange(value, axes):
    return lax.all_to_all(value, axes, split_axis=0, concat_axis=0, tiled=True)


def spread(value, axes):
    count = lax.axis_size(axes)
    return exchange(jnp.broadcast_to(value[None], (count,) + value.shape), axes)


def dot(left, right):
    return jnp.dot(left, right, preferred_element_type=jnp.float32)


def dot_nt(left, right):
    return lax.dot_general(left, right, (((1,), (1,)), ((), ())), preferred_element_type=jnp.float32)


def dot_tn(left, right):
    return lax.dot_general(left, right, (((0,), (0,)), ((), ())), preferred_element_type=jnp.float32)


def two_parts(values):
    high = values.astype(jnp.bfloat16)
    low = (values - high.astype(jnp.float32)).astype(jnp.bfloat16)
    return (high, low)


def by_core(mine, other, core):
    return jnp.where(core == 0, jnp.stack([mine, other]), jnp.stack([other, mine]))


def remote(src, dst, send, recv, **where):
    return pltpu.make_async_remote_copy(
        src_ref=src, dst_ref=dst, send_sem=send, recv_sem=recv, device_id=where, device_id_type=MESH
    )


def places():
    return lax.axis_index("fsdp"), lax.axis_index("ctx"), lax.axis_index("tp")


def ring(index, step, count):
    return lax.rem(index + step + count, count)


def greet(nz, nc, line, far=False):
    z, c, t = places()
    barrier = pltpu.get_barrier_semaphore()

    def tell(**where):
        pl.semaphore_signal(barrier, inc=1, device_id=where, device_id_type=MESH)

    if line:
        for step in range(1, nz):
            tell(fsdp=ring(z, step, nz))
        count = nz - 1
    else:
        pl.when(z > 0)(lambda: tell(fsdp=z - 1))
        pl.when(z < nz - 1)(lambda: tell(fsdp=z + 1))
        count = jnp.where(z > 0, 1, 0) + jnp.where(z < nz - 1, 1, 0)
    for step in range(1, nc):
        tell(ctx=ring(c, step, nc))
        if far:
            for hop in range(1, nz):
                tell(fsdp=ring(z, hop, nz), ctx=ring(c, step, nc))
    if far:
        count = count + (nz - 1) * (nc - 1)
    tell(tp=1 - t)
    pl.semaphore_wait(barrier, count + nc)


def line_copies(bufs, send_sem, recv_sem, way, step, shard, target):
    return [
        remote(buf.at[shard], buf.at[shard], send_sem.at[way, step, k], recv_sem.at[way, step, k], fsdp=target)
        for k, buf in enumerate(bufs)
    ]


def line_gather(nz, bufs, send_sem, recv_sem, arrived, begun=None, near=None):
    z = lax.axis_index("fsdp")
    for step in range(nz - 1):

        @pl.when((z < nz - 1) & (z >= step))
        def _():
            for copy in line_copies(bufs, send_sem, recv_sem, 0, step, z - step, z + 1):
                copy.start()

        @pl.when((z > 0) & (z + step < nz))
        def _():
            for copy in line_copies(bufs, send_sem, recv_sem, 1, step, z + step, z - 1):
                copy.start()

        if step == 0 and begun is not None:
            begun()
        if near is not None:
            near(step)

        @pl.when(z - 1 >= step)
        def _():
            for copy in line_copies(bufs, send_sem, recv_sem, 0, step, z - 1 - step, z - 1):
                copy.wait_recv()
            arrived(z - 1 - step)

        @pl.when(z + 1 + step < nz)
        def _():
            for copy in line_copies(bufs, send_sem, recv_sem, 1, step, z + 1 + step, z + 1):
                copy.wait_recv()
            arrived(z + 1 + step)


def line_sent(nz, bufs, send_sem, recv_sem):
    z = lax.axis_index("fsdp")
    for step in range(nz - 1):

        @pl.when((z < nz - 1) & (z >= step))
        def _():
            for copy in line_copies(bufs, send_sem, recv_sem, 0, step, z - step, z + 1):
                copy.wait_send()

        @pl.when((z > 0) & (z + step < nz))
        def _():
            for copy in line_copies(bufs, send_sem, recv_sem, 1, step, z + step, z - 1):
                copy.wait_send()


def pick_rows(pick, slot, source, out):
    lanes = out.shape[-1]
    piece = min(lanes, 512)

    @pl.loop(0, lanes // piece)
    def _(k):
        at = pl.ds(pl.multiple_of(k * piece, piece), piece)
        out[slot, :, at] = jnp.dot(pick[slot], source[slot, :, at], preferred_element_type=jnp.float32).astype(
            jnp.bfloat16
        )


def plane_copy(most, src, dst, send, recv, slot, step, source, target):
    rows = pl.ds(pl.multiple_of(target * most, 16), most)
    return remote(
        src.at[slot, rows], dst.at[source, slot], send.at[slot, step - 1], recv.at[slot, step - 1], ctx=target
    )


def regroup(shard, t, rows, line, two, keep_sem, give_send, give_recv):
    slot = lax.rem(shard, 2)
    band = pl.ds(pl.multiple_of(t * rows, rows), rows)

    def keep():
        pltpu.make_async_copy(line.at[shard], two.at[slot, band], keep_sem.at[slot]).start()

    def give():
        remote(line.at[shard], two.at[slot, band], give_send.at[slot], give_recv.at[slot], tp=1 - t).start()

    pl.when(shard // 2 == t)(keep)
    pl.when(shard // 2 != t)(give)


def load_kernel(
    nz, nc, tok, cot, wq, wk, wv, wo, small, rank,
    x_all, w_qkv, w_o, small_all, rank_line, rank_seq, pick, cot_in,
    cot_line, cot_two, cot_send,
    own_sem, line_send, line_recv, w_send, w_recv, tok_send, tok_recv, pass_send, pass_recv,
    rank_send, rank_recv, keep_sem, give_send, give_recv, cot_s, cot_r, cot_own,
):
    z, c, t = places()
    block = tok.shape[0]
    rows = block // 2
    local = w_qkv.shape[2] // 3
    most = cot_in.shape[2]
    half = pl.ds(pl.multiple_of(t * rows, rows), rows)
    column = pl.ds(pl.multiple_of(c * local, local), local)
    own = [
        pltpu.make_async_copy(cot.at[half], cot_line.at[z], own_sem.at[5]),
        pltpu.make_async_copy(small, small_all.at[z], own_sem.at[4]),
        pltpu.make_async_copy(rank, rank_line.at[z], own_sem.at[7]),
        pltpu.make_async_copy(rank, rank_seq.at[c], own_sem.at[8]),
    ]
    own += [
        pltpu.make_async_copy(w.at[:, column], w_qkv.at[z, :, pl.ds(k * local, local)], own_sem.at[k])
        for k, w in enumerate((wq, wk, wv))
    ]
    own += [
        pltpu.make_async_copy(wo.at[column], w_o.at[z], own_sem.at[3]),
        pltpu.make_async_copy(tok, x_all.at[pl.ds(pl.multiple_of(c * block, block), block)], own_sem.at[6]),
    ]
    for copy in own:
        copy.start()
    greet(nz, nc, False)

    def band(source, core):
        return x_all.at[pl.ds(pl.multiple_of(source * block + core * rows, rows), rows)]

    def token_copy(step, source, target):
        return remote(tok.at[half], band(source, t), tok_send.at[step], tok_recv.at[step], ctx=target)

    def pass_copy(step, source, core):
        return remote(band(source, core), band(source, core), pass_send.at[step], pass_recv.at[step], tp=1 - t)

    def rank_copy(step, source, target):
        return remote(rank, rank_seq.at[source], rank_send.at[step], rank_recv.at[step], ctx=target)

    for step in range(1, nc):
        token_copy(step - 1, c, ring(c, step, nc)).start()
        rank_copy(step - 1, c, ring(c, step, nc)).start()
    for copy in own:
        copy.wait()

    def arrived(shard):
        regroup(shard, t, rows, cot_line, cot_two, keep_sem, give_send, give_recv)

    arrived(z)
    first = (cot_line, rank_line, small_all)
    line_gather(nz, first, line_send, line_recv, arrived)

    def own_copy(slot):
        return pltpu.make_async_copy(
            cot_send.at[slot, pl.ds(pl.multiple_of(c * most, 16), most)], cot_in.at[c, slot], cot_own.at[slot]
        )

    def send_cotangent():
        number = lax.broadcasted_iota(jnp.int32, (most, block), 0).astype(jnp.float32)
        for slot in range(2):
            for q in range(nc):
                row = rank_line[2 * t + slot, pl.ds(q * nz + z, 1), :]
                hit = jnp.where(number == row, 1.0, 0.0)
                pick[slot, pl.ds(q * most, most), :] = hit.astype(jnp.bfloat16)
        for slot in range(2):
            wait_two(slot, t, rows, cot_line, cot_two, keep_sem, give_recv)
            pick_rows(pick, slot, cot_two, cot_send)
            for step in range(1, nc):
                plane_copy(most, cot_send, cot_in, cot_s, cot_r, slot, step, c, ring(c, step, nc)).start()
            own_copy(slot).start()

    def ignore(shard):
        pass

    line_gather(nz, (w_qkv, w_o), w_send, w_recv, ignore, send_cotangent)
    for step in range(1, nc):
        source = ring(c, -step, nc)
        token_copy(step - 1, source, source).wait_recv()
        pass_copy(step - 1, source, t).start()
        rank_copy(step - 1, source, source).wait_recv()
    for step in range(1, nc):
        source = ring(c, -step, nc)
        pass_copy(step - 1, source, 1 - t).wait_recv()
        pass_copy(step - 1, source, t).wait_send()
        token_copy(step - 1, c, source).wait_send()
        rank_copy(step - 1, c, source).wait_send()
        for slot in range(2):
            copy = plane_copy(most, cot_send, cot_in, cot_s, cot_r, slot, step, source, source)
            copy.wait_recv()
            copy.wait_send()
    line_sent(nz, first, line_send, line_recv)
    line_sent(nz, (w_qkv, w_o), w_send, w_recv)
    for slot in range(2):
        own_copy(slot).wait()
        wait_given(slot, t, rows, cot_line, cot_two, give_send, give_recv)


def wait_given(slot, t, rows, line, two, give_send, give_recv):
    band = pl.ds(pl.multiple_of(t * rows, rows), rows)
    remote(line.at[0], two.at[slot, band], give_send.at[slot], give_recv.at[slot], tp=1 - t).wait_send()


def wait_two(slot, t, rows, line, two, keep_sem, give_recv):
    band = pl.ds(pl.multiple_of(t * rows, rows), rows)
    other = pl.ds(pl.multiple_of((1 - t) * rows, rows), rows)
    pltpu.make_async_copy(line.at[0], two.at[slot, band], keep_sem.at[slot]).wait()
    remote(line.at[0], two.at[slot, other], give_recv.at[slot], give_recv.at[slot], tp=1 - t).wait_recv()


def load(tok, cot, wq, wk, wv, wo, small, rank, most):
    nz, nc = lax.axis_size("fsdp"), lax.axis_size("ctx")
    block, width = tok.shape
    deep, local = wq.shape[0], wq.shape[1] // nc
    rows = block // 2
    dma = pltpu.SemaphoreType.DMA
    bf16, f32 = jnp.bfloat16, jnp.float32
    shapes = [
        ((nc * block, width), bf16),
        ((nz, deep, 3 * local), bf16),
        ((nz, local, wo.shape[1]), bf16),
        ((nz,) + small.shape, bf16),
        ((nz,) + rank.shape, f32),
        ((nc,) + rank.shape, f32),
        ((2, nc * most, block), bf16),
        ((nc, 2, most, width), bf16),
    ]
    hbm = pl.BlockSpec(memory_space=pl.ANY)
    return pl.pallas_call(
        functools.partial(load_kernel, nz, nc),
        out_shape=[jax.ShapeDtypeStruct(shape, kind) for shape, kind in shapes],
        in_specs=[hbm] * 8,
        out_specs=[pl.BlockSpec(memory_space=pltpu.VMEM)] * 7 + [hbm],
        scratch_shapes=[
            pltpu.VMEM((nz, rows, width), bf16),
            pltpu.VMEM((2, block, width), bf16),
            pltpu.VMEM((2, nc * most, width), bf16),
            dma((9,)),
            dma((2, nz - 1, 3)), dma((2, nz - 1, 3)), dma((2, nz - 1, 2)), dma((2, nz - 1, 2)),
            dma((nc - 1,)), dma((nc - 1,)), dma((nc - 1,)), dma((nc - 1,)), dma((nc - 1,)), dma((nc - 1,)),
            dma((2,)), dma((2,)), dma((2,)), dma((2, nc - 1)), dma((2, nc - 1)), dma((2,)),
        ],
        compiler_params=pltpu.CompilerParams(
            collective_id=0, has_side_effects=True, vmem_limit_bytes=48 * 2**20
        ),
    )(tok, cot, wq, wk, wv, wo, small, rank)


def dispatch_kernel(
    nz, nc, part, tok, gain, router, kept, pick, third,
    residual, normed, probs, x_in, g_in, third_got,
    sib, rs_send, rs_recv, n_line, g_line, n_two, g_two, x_send, g_send,
    sib_s, sib_r, rs_s, rs_r, line_send, line_recv, keep_sem, give_send, give_recv,
    gkeep_sem, ggive_send, ggive_recv, x_s, x_r, g_s, g_r, own_sem,
    third_s, third_r, third_own,
):
    z, c, t = places()
    f32, bf16 = jnp.float32, jnp.bfloat16
    rows, width = residual.shape
    most = x_in.shape[2]
    greet(nz, nc, True)
    keep_third = pltpu.make_async_copy(third.at[z], third_got.at[z], third_own)
    keep_third.start()

    def third_copy(step, source, target):
        return remote(third.at[target], third_got.at[source], third_s.at[step], third_r.at[step], fsdp=target)

    def sib_copy(q):
        return remote(part.at[q, 1 - t], sib.at[q], sib_s.at[q], sib_r.at[q], tp=1 - t)

    def rs_copy(step, source, target):
        return remote(rs_send.at[step], rs_recv.at[step], rs_s.at[step], rs_r.at[step], ctx=target)

    for step in range(1, nc + 1):
        sib_copy(ring(c, step, nc)).start()
    chunk = 16
    for step in range(1, nc):
        q = ring(c, step, nc)
        sib_copy(q).wait_recv()

        @pl.loop(0, rows // chunk)
        def _(k):
            at = pl.ds(pl.multiple_of(k * chunk, chunk), chunk)
            rs_send[step - 1, at, :] = (part[q, t, at, :].astype(f32) + sib[q, at, :].astype(f32)).astype(bf16)

        rs_copy(step - 1, c, q).start()

    def own_copy(slot, src, dst, k):
        return pltpu.make_async_copy(
            src.at[slot, pl.ds(pl.multiple_of(c * most, 16), most)], dst.at[c, slot], own_sem.at[k, slot]
        )

    sib_copy(c).wait_recv()
    for step in range(1, nc):
        rs_copy(step - 1, c, c).wait_recv()

    @pl.loop(0, rows // chunk)
    def _(k):
        at = pl.ds(pl.multiple_of(k * chunk, chunk), chunk)
        start = pl.ds(pl.multiple_of(t * rows + k * chunk, chunk), chunk)
        total = part[c, t, at, :].astype(f32) + sib[c, at, :].astype(f32)
        for step in range(nc - 1):
            total = total + rs_recv[step, at, :].astype(f32)
        total = total + tok[start, :].astype(f32)
        residual[at, :] = total
        inv = lax.rsqrt(jnp.mean(total * total, -1, keepdims=True) + EPS)
        row = (total * inv * gain[...]).astype(bf16)
        normed[at, :] = row
        n_line[z, at, :] = row

    logits = lax.dot_general(
        normed[...], router[...], (((1,), (1,)), ((), ())), preferred_element_type=f32
    )
    lane = lax.broadcasted_iota(jnp.int32, logits.shape, 1)
    logits = jnp.where(lane < E, logits, -jnp.inf)
    top = jnp.max(logits, -1, keepdims=True)
    raised = jnp.exp(logits - top)
    prob = raised / jnp.sum(raised, -1, keepdims=True)
    probs[...] = prob
    gates = prob * kept[...]
    high = gates.astype(bf16)
    g_line[z, :, pl.ds(0, 128)] = high
    g_line[z, :, pl.ds(128, 128)] = (gates - high.astype(f32)).astype(bf16)

    def arrived(shard):
        regroup(shard, t, rows, n_line, n_two, keep_sem, give_send, give_recv)
        regroup(shard, t, rows, g_line, g_two, gkeep_sem, ggive_send, ggive_recv)

    arrived(z)
    sent = ((x_send, x_in, x_s, x_r), (g_send, g_in, g_s, g_r))

    def near(distance):
        above, below = z + distance, z - distance
        is_above = (above < nz) & (above // 2 == t)
        is_below = (below >= 0) & (below // 2 == t)
        slot = lax.rem(jnp.where(is_above, above, below + 2), 2)

        @pl.when(is_above | is_below)
        def _():
            wait_two(slot, t, rows, n_line, n_two, keep_sem, give_recv)
            wait_two(slot, t, rows, g_line, g_two, gkeep_sem, ggive_recv)
            pick_rows(pick, slot, n_two, x_send)
            pick_rows(pick, slot, g_two, g_send)
            for k, (src, dst, s, r) in enumerate(sent):
                for step in range(1, nc):
                    plane_copy(most, src, dst, s, r, slot, step, c, ring(c, step, nc)).start()
                own_copy(slot, src, dst, k).start()

    line_gather(nz, (n_line, g_line), line_send, line_recv, arrived, None, near)
    near(nz - 1)
    for step in range(1, nz):
        third_copy(step - 1, z, ring(z, step, nz)).start()
    line_sent(nz, (n_line, g_line), line_send, line_recv)
    for slot in range(2):
        wait_given(slot, t, rows, n_line, n_two, give_send, give_recv)
        wait_given(slot, t, rows, g_line, g_two, ggive_send, ggive_recv)
        for k, (src, dst, s, r) in enumerate(sent):
            own_copy(slot, src, dst, k).wait()
            for step in range(1, nc):
                source = ring(c, -step, nc)
                copy = plane_copy(most, src, dst, s, r, slot, step, source, source)
                copy.wait_recv()
                copy.wait_send()
    for step in range(1, nc):
        rs_copy(step - 1, c, c).wait_send()
    for step in range(nc):
        sib_copy(step).wait_send()
    for step in range(1, nz):
        source = ring(z, -step, nz)
        third_copy(step - 1, source, source).wait_recv()
        third_copy(step - 1, source, source).wait_send()
    keep_third.wait()


def dispatch(part, tok, gain, router, kept, pick, third):
    nz, nc = lax.axis_size("fsdp"), lax.axis_size("ctx")
    rows, width = part.shape[2], part.shape[3]
    block = rows * 2
    most = pick.shape[1] // nc
    dma = pltpu.SemaphoreType.DMA
    bf16, f32 = jnp.bfloat16, jnp.float32
    vmem = pl.BlockSpec(memory_space=pltpu.VMEM)
    hbm = pl.BlockSpec(memory_space=pl.ANY)
    return pl.pallas_call(
        functools.partial(dispatch_kernel, nz, nc),
        out_shape=[
            jax.ShapeDtypeStruct((rows, width), f32),
            jax.ShapeDtypeStruct((rows, width), bf16),
            jax.ShapeDtypeStruct((rows, 128), f32),
            jax.ShapeDtypeStruct((nc, 2, most, width), bf16),
            jax.ShapeDtypeStruct((nc, 2, most, 256), bf16),
            jax.ShapeDtypeStruct(third.shape, bf16),
        ],
        in_specs=[vmem] * 6 + [hbm],
        out_specs=[vmem] * 3 + [hbm] * 3,
        scratch_shapes=[
            pltpu.VMEM((nc, rows, width), bf16),
            pltpu.VMEM((nc - 1, rows, width), bf16),
            pltpu.VMEM((nc - 1, rows, width), bf16),
            pltpu.VMEM((nz, rows, width), bf16),
            pltpu.VMEM((nz, rows, 256), bf16),
            pltpu.VMEM((2, block, width), bf16),
            pltpu.VMEM((2, block, 256), bf16),
            pltpu.VMEM((2, nc * most, width), bf16),
            pltpu.VMEM((2, nc * most, 256), bf16),
            dma((nc,)), dma((nc,)), dma((nc - 1,)), dma((nc - 1,)),
            dma((2, nz - 1, 2)), dma((2, nz - 1, 2)),
            dma((2,)), dma((2,)), dma((2,)), dma((2,)), dma((2,)), dma((2,)),
            dma((2, nc - 1)), dma((2, nc - 1)), dma((2, nc - 1)), dma((2, nc - 1)),
            dma((2, 2)),
            dma((nz - 1,)), dma((nz - 1,)), dma,
        ],
        compiler_params=pltpu.CompilerParams(
            collective_id=1, has_side_effects=True, vmem_limit_bytes=56 * 2**20
        ),
    )(part, tok, gain, router, kept, pick, third)


def experts_kernel(
    nz, nc, x_hbm, cot_hbm, gates, pair_hbm, third_hbm, y, r, pair_out, own_grad, other_grad,
    x, cot, w, weight, pair, gate, up, out_grad, hid, gg, gu, stage,
    sem, swap_s, swap_r, stage_sem, give_sem, got_sem,
):
    z, c, t = places()
    f32, bf16 = jnp.float32, jnp.bfloat16
    width, tall = x.shape[1], x.shape[0]
    deep, ffn = w.shape[3], w.shape[4]
    span = 256
    chunk = 48
    copies = [
        pltpu.make_async_copy(cot_hbm, cot, sem.at[0]),
        pltpu.make_async_copy(pair_hbm, w.at[0, :, pl.ds(0, 2)], sem.at[1]),
        pltpu.make_async_copy(x_hbm, x, sem.at[2]),
        pltpu.make_async_copy(third_hbm, w.at[0, :, 2], sem.at[3]),
    ]
    for copy in copies:
        copy.start()
    barrier = pltpu.get_barrier_semaphore()
    pl.semaphore_signal(barrier, inc=1, device_id=dict(tp=1 - t), device_id_type=MESH)
    pl.semaphore_wait(barrier, 1)
    swaps = [
        remote(pair_hbm, w.at[1, :, pl.ds(0, 2)], swap_s.at[0], swap_r.at[0], tp=1 - t),
        remote(third_hbm, w.at[1, :, 2], swap_s.at[1], swap_r.at[1], tp=1 - t),
    ]
    for copy in swaps:
        copy.start()
    pair[...] = jnp.zeros_like(pair)
    lane = lax.broadcasted_iota(jnp.int32, (chunk, 256), 1)
    mine = c * nz + z

    @pl.loop(0, tall // chunk)
    def _(m):
        rows = pl.ds(pl.multiple_of(m * chunk, chunk), chunk)
        value = gates[rows, :].astype(f32)
        value = jnp.where((lane == mine) | (lane == mine + 128), value, 0.0)
        weight[rows, :] = jnp.sum(value, 1, keepdims=True)

    for copy in copies:
        copy.wait()
    per = ffn // span

    def forward(n):
        half, at = n // per, pl.ds(pl.multiple_of(lax.rem(n, per) * span, span), span)
        full = pl.ds(pl.multiple_of(n * span, span), span)

        def times(rows, k):
            return jnp.dot(rows[...], w[half, :, k, :, at].reshape(width, span), preferred_element_type=f32)

        out_grad[...] = times(cot, 1)
        gate[...] = times(x, 0)
        up[...] = times(x, 2)

        @pl.loop(0, tall // chunk)
        def _(m):
            rows = pl.ds(pl.multiple_of(m * chunk, chunk), chunk)
            g, u, o, k = gate[rows, :], up[rows, :], out_grad[rows, :], weight[rows, :]
            sig = 1.0 / (1.0 + jnp.exp(-g))
            silu = g * sig
            hidden = silu * u
            pair[rows, :] += jnp.sum(hidden.astype(bf16).astype(f32) * o, 1, keepdims=True)
            hid[rows, full] = (k * hidden).astype(bf16)
            o = k * o
            gg[rows, full] = (o * u * sig * (1.0 + g * (1.0 - sig))).astype(bf16)
            gu[rows, full] = (o * silu).astype(bf16)

    pl.loop(0, per)(forward)
    for copy in swaps:
        copy.wait_recv()
    pl.loop(per, 2 * per)(forward)

    @pl.loop(0, tall // chunk)
    def _(m):
        rows = pl.ds(pl.multiple_of(m * chunk, chunk), chunk)
        value = pair[rows, :]
        high = value.astype(bf16).astype(f32)
        out = jnp.where(lane == mine, high, jnp.where(lane == mine + 128, value - high, 0.0))
        pair_out[rows, :] = out.astype(bf16)

    per_deep = deep // span

    @pl.loop(0, width // span)
    def _(n):
        zone, at = n // per_deep, pl.ds(pl.multiple_of(lax.rem(n, per_deep) * span, span), span)
        full = pl.ds(pl.multiple_of(n * span, span), span)

        def back(rows, k):
            total = 0.0
            for half in range(2):
                total = total + lax.dot_general(
                    rows[:, pl.ds(half * ffn, ffn)], w[half, zone, k, at, :], (((1,), (1,)), ((), ())),
                    preferred_element_type=f32,
                )
            return total

        y[:, full] = back(hid, 1).astype(bf16)
        r[:, full] = (back(gg, 0) + back(gu, 2)).astype(bf16)

    strip = stage.shape[4]
    count = span // strip

    def flush(n):
        slot = lax.rem(n, 2)
        at = pl.ds(pl.multiple_of(n * count, count), count)
        return (
            pltpu.make_async_copy(stage.at[slot, 0], own_grad.at[at], stage_sem.at[slot]),
            remote(stage.at[slot, 1], other_grad.at[at], give_sem.at[slot], got_sem, tp=1 - t),
        )

    def flushed(n):
        keep, give = flush(n)
        keep.wait()
        give.wait_send()

    @pl.loop(0, width // span)
    def _(n):
        full = pl.ds(pl.multiple_of(n * span, span), span)
        slot = lax.rem(n, 2)

        @pl.when(n >= 2)
        def _():
            flushed(n - 2)

        for k, (rows, grads) in enumerate(((x, gg), (x, gu), (cot, hid))):
            value = lax.dot_general(
                rows[:, full], grads[...], (((0,), (0,)), ((), ())), preferred_element_type=f32
            ).astype(bf16)
            for half in range(2):
                for i in range(count):
                    stage[slot, half, i, k] = value[i * strip : (i + 1) * strip, half * ffn : (half + 1) * ffn]
        for copy in flush(n):
            copy.start()

    flushed(width // span - 2)
    flushed(width // span - 1)
    remote(other_grad, other_grad, got_sem, got_sem, tp=1 - t).wait_recv()
    for copy in swaps:
        copy.wait_send()


def experts(x, cot, gates, pair, third, strip):
    bf16, f32 = jnp.bfloat16, jnp.float32
    nz, nc = lax.axis_size("fsdp"), lax.axis_size("ctx")
    tall, width = x.shape
    deep, ffn = third.shape[1:]
    vmem = pl.BlockSpec(memory_space=pltpu.VMEM)
    hbm = pl.BlockSpec(memory_space=pl.ANY)
    grads = jax.ShapeDtypeStruct((width // strip, 3, strip, ffn), bf16)
    dma = pltpu.SemaphoreType.DMA
    return pl.pallas_call(
        functools.partial(experts_kernel, nz, nc),
        out_shape=[
            jax.ShapeDtypeStruct((tall, width), bf16),
            jax.ShapeDtypeStruct((tall, width), bf16),
            jax.ShapeDtypeStruct((tall, 256), bf16),
            grads,
            grads,
        ],
        in_specs=[hbm, hbm, vmem, hbm, hbm],
        out_specs=[vmem, vmem, vmem, hbm, hbm],
        scratch_shapes=[
            pltpu.VMEM((tall, width), bf16),
            pltpu.VMEM((tall, width), bf16),
            pltpu.VMEM((2, nz, 3, deep, ffn), bf16),
            pltpu.VMEM((tall, 1), f32),
            pltpu.VMEM((tall, 1), f32),
            pltpu.VMEM((tall, 256), f32),
            pltpu.VMEM((tall, 256), f32),
            pltpu.VMEM((tall, 256), f32),
            pltpu.VMEM((tall, 2 * ffn), bf16),
            pltpu.VMEM((tall, 2 * ffn), bf16),
            pltpu.VMEM((tall, 2 * ffn), bf16),
            pltpu.VMEM((2, 2, 256 // strip, 3, strip, ffn), bf16),
            dma((4,)), dma((2,)), dma((2,)), dma((2,)), dma((2,)), dma,
        ],
        compiler_params=pltpu.CompilerParams(
            collective_id=4, has_side_effects=True, vmem_limit_bytes=60 * 2**20
        ),
    )(x, cot, gates, pair, third)


def select_kernel(nz, src, pair, third):
    c = lax.axis_index("ctx")
    tile = 16
    count = src.shape[2]
    row = lax.broadcasted_iota(jnp.int32, (nz * tile, tile * count), 0)
    column = lax.broadcasted_iota(jnp.int32, (nz * tile, tile * count), 1)
    hit = column == lax.rem(row, tile) * count + c * nz + row // tile
    hit = jnp.where(hit, 1.0, 0.0).astype(jnp.bfloat16)
    for n in range(src.shape[0] // tile):
        at = pl.ds(n * tile, tile)
        for k in range(3):
            value = src[n * tile : (n + 1) * tile, k].reshape(tile * count, -1)
            value = jnp.dot(hit, value, preferred_element_type=jnp.float32).astype(jnp.bfloat16)
            value = value.reshape(nz, tile, -1)
            if k == 1:
                third[:, at, :] = value
            else:
                pair[:, k // 2, at, :] = value


def select(w_experts, nz):
    deep, kinds, count, ffn = w_experts.shape
    band = 64
    bf16 = jnp.bfloat16
    return pl.pallas_call(
        functools.partial(select_kernel, nz),
        grid=(deep // band,),
        out_shape=[
            jax.ShapeDtypeStruct((nz, 2, deep, ffn), bf16),
            jax.ShapeDtypeStruct((nz, deep, ffn), bf16),
        ],
        in_specs=[pl.BlockSpec((band, kinds, count, ffn), lambda i: (i, 0, 0, 0))],
        out_specs=[
            pl.BlockSpec((nz, 2, band, ffn), lambda i: (0, 0, i, 0)),
            pl.BlockSpec((nz, band, ffn), lambda i: (0, i, 0)),
        ],
        compiler_params=pltpu.CompilerParams(vmem_limit_bytes=40 * 2**20),
    )(w_experts)


def place_kernel(nz, nc, gate, rest, out):
    tile = gate.shape[2]
    count = nz * nc
    row = lax.broadcasted_iota(jnp.int32, (tile * count, tile * count), 0)
    column = lax.broadcasted_iota(jnp.int32, (tile * count, tile * count), 1)
    expert = lax.rem(row, count)
    hit = column == (lax.rem(expert, nz) * nc + expert // nz) * tile + row // count
    hit = jnp.where(hit, 1.0, 0.0).astype(jnp.bfloat16)
    for k in range(3):
        early = gate.shape[1]
        value = (gate[:, k] if k < early else rest[:, k - early]).reshape(count * tile, -1)
        value = jnp.dot(hit, value, preferred_element_type=jnp.float32)
        out[:, k] = value.reshape(tile, count, -1)


def lay_out(gate, rest, nz, nc):
    count, _, strip, ffn = gate.shape
    tile = 16
    return pl.pallas_call(
        functools.partial(place_kernel, nz, nc),
        grid=(strip // tile,),
        out_shape=jax.ShapeDtypeStruct((strip, 3, count, ffn), jnp.float32),
        in_specs=[
            pl.BlockSpec((count, src.shape[1], tile, ffn), lambda i: (0, 0, i, 0))
            for src in (gate, rest)
        ],
        out_specs=pl.BlockSpec((tile, 3, count, ffn), lambda i: (i, 0, 0, 0)),
        compiler_params=pltpu.CompilerParams(vmem_limit_bytes=40 * 2**20),
    )(gate, rest)


def collector(nz, nc, pick_t, items, sems):
    z, c, t = places()
    to_s, to_r, own_sem, sib_s, sib_r, line_s, line_r, keep_sem = sems
    rows = items[0][2].shape[1]
    mine_at = pl.ds(pl.multiple_of(t * rows, rows), rows)
    give_at = pl.ds(pl.multiple_of((1 - t) * rows, rows), rows)
    count = len(items)

    def lanes(turn, k):
        wide = items[k][2].shape[-1] // 2
        return pl.ds(turn * wide, wide)

    def to_copy(turn, k, step, source, target):
        src, got = items[k][:2]
        at = lanes(turn, k)
        return remote(
            src.at[target, :, :, at], got.at[source, :, :, at], to_s.at[k, turn, step - 1], to_r.at[k, turn, step - 1],
            ctx=target,
        )

    def own_copy(turn, k):
        src, got = items[k][:2]
        at = lanes(turn, k)
        return pltpu.make_async_copy(src.at[c, :, :, at], got.at[c, :, :, at], own_sem.at[k, turn])

    def sib_copy(turn, k):
        give, sib = items[k][3:5]
        at = lanes(turn, k)
        return remote(give.at[:, :, at], sib.at[:, :, at], sib_s.at[k, turn], sib_r.at[k, turn], tp=1 - t)

    def line_copy(turn, slot, k, half, source, target):
        src = items[k][2 if half == 0 else 4]
        at = lanes(turn, k)
        return remote(
            src.at[slot, :, at], items[k][5].at[source, :, at],
            line_s.at[k, turn, 2 * half + slot], line_r.at[k, turn, source], fsdp=target,
        )

    def keep_copy(turn, slot, k, half):
        src = items[k][2 if half == 0 else 4]
        at = lanes(turn, k)
        return pltpu.make_async_copy(src.at[slot, :, at], items[k][5].at[z, :, at], keep_sem.at[k, turn])

    def goal(slot, half):
        return 2 * (t if half == 0 else 1 - t) + slot

    def forward(turn, k, half):
        for slot in range(2):
            target = goal(slot, half)
            pl.when(target != z)(lambda: line_copy(turn, slot, k, half, z, target).start())
            pl.when(target == z)(lambda: keep_copy(turn, slot, k, half).start())

    def begin(turn):
        for k in range(count):
            for step in range(1, nc):
                to_copy(turn, k, step, c, ring(c, step, nc)).start()
            own_copy(turn, k).start()

    def scatter(turn, slot, k):
        got, mine, give = items[k][1:4]
        wide = mine.shape[-1] // 2
        span = min(wide, 512)
        tall = got.shape[0] * got.shape[2]

        @pl.loop(0, wide // span)
        def _(n):
            at = pl.ds(pl.multiple_of(turn * wide + n * span, span), span)
            pairs = got[:, slot, :, at].reshape(tall, span)
            for picks, out in ((mine_at, mine), (give_at, give)):
                out[slot, :, at] = jnp.dot(
                    pick_t[slot, picks, :], pairs, preferred_element_type=jnp.float32
                ).astype(jnp.bfloat16)

    def process(turn):
        for k in range(count):
            own_copy(turn, k).wait()
            for step in range(1, nc):
                source = ring(c, -step, nc)
                to_copy(turn, k, step, source, c).wait_recv()
            for slot in range(2):
                scatter(turn, slot, k)
            sib_copy(turn, k).start()
            forward(turn, k, 0)
        for k in range(count):
            sib_copy(turn, k).wait_recv()
            forward(turn, k, 1)

    def join():
        for turn in range(2):
            for k in range(count):
                keep_copy(turn, 0, k, 0).wait()
                for step in range(1, nz):
                    line_copy(turn, 0, k, 0, ring(z, -step, nz), z).wait_recv()

    def done():
        for turn in range(2):
            for k in range(count):
                for step in range(1, nc):
                    to_copy(turn, k, step, c, ring(c, step, nc)).wait_send()
                sib_copy(turn, k).wait_send()
                for half in range(2):
                    for slot in range(2):
                        pl.when(goal(slot, half) != z)(
                            lambda: line_copy(turn, slot, k, half, z, goal(slot, half)).wait_send()
                        )

    return begin, process, join, done


def collector_scratch(nz, nc, most, rows, widths):
    dma = pltpu.SemaphoreType.DMA
    bf16 = jnp.bfloat16
    count = len(widths)
    bufs = []
    for w in widths:
        bufs += [pltpu.VMEM((nc, 2, most, w), bf16)]
        bufs += [pltpu.VMEM((2, rows, w), bf16)] * 3
        bufs += [pltpu.VMEM((nz, rows, w), bf16)]
    sems = [
        dma((count, 2, nc - 1)), dma((count, 2, nc - 1)), dma((count, 2)), dma((count, 2)), dma((count, 2)),
        dma((count, 2, 4)), dma((count, 2, nz)), dma((count, 2)),
    ]
    return bufs, sems


def return_kernel(
    nz, nc, r, g, early, pick_t, residual, probs, kept, router, gain, cot,
    logits_grad, gain_grad, residual_grad, attn_grad, early_got, *scratch,
):
    z, c, t = places()
    f32, bf16 = jnp.float32, jnp.bfloat16
    rows, width = residual.shape
    r_line, g_line = scratch[4], scratch[9]
    row_s, row_r, pass_s, pass_r, early_s, early_r, early_own = scratch[18:]
    items = ((r,) + scratch[:5], (g,) + scratch[5:10])
    begin, process, join, done = collector(nz, nc, pick_t, items, scratch[10:18])
    here = z * nc + c
    keep_early = pltpu.make_async_copy(early.at[here], early_got.at[here], early_own)
    keep_early.start()
    greet(nz, nc, True, True)
    chips = nz * nc
    steps = [(i, j) for i in range(nz) for j in range(nc) if i or j]

    def early_copy(n, source, target, fsdp, ctx):
        return remote(early.at[target], early_got.at[source], early_s.at[n], early_r.at[n], fsdp=fsdp, ctx=ctx)

    begin(0)
    for n, (i, j) in enumerate(steps):
        zz, cc = ring(z, i, nz), ring(c, j, nc)
        early_copy(n, here, zz * nc + cc, zz, cc).start()
    begin(1)
    for turn in range(2):
        process(turn)
    join()
    pairs = jnp.zeros((rows, 128), f32)
    for source in range(nz):
        pairs = pairs + g_line[source, :, 0:128].astype(f32) + g_line[source, :, 128:256].astype(f32)
    pairs = pairs * kept[...]
    prob = probs[...]
    grad_logits = (prob * (pairs - jnp.sum(prob * pairs, -1, keepdims=True))).astype(bf16)
    logits_grad[...] = grad_logits
    gain_grad[...] = jnp.zeros_like(gain_grad)
    chunk = 16

    @pl.loop(0, rows // chunk)
    def _(k):
        at = pl.ds(pl.multiple_of(k * chunk, chunk), chunk)
        full = pl.ds(pl.multiple_of(t * rows + k * chunk, chunk), chunk)
        res = residual[at, :]
        grad = r_line[0, at, :].astype(f32)
        for source in range(1, nz):
            grad = grad + r_line[source, at, :].astype(f32)
        grad = grad + jnp.dot(logits_grad[at, :], router[...], preferred_element_type=f32)
        inv = lax.rsqrt(jnp.mean(res * res, -1, keepdims=True) + EPS)
        gain_grad[...] += jnp.sum((grad * res * inv).reshape(chunk // 8, 8, width), 0)
        weighted = grad * gain[...]
        inner = jnp.sum(weighted * res, -1, keepdims=True)
        out = cot[full, :].astype(f32) + inv * weighted - res * (inv * inv * inv) * inner / width
        residual_grad[at, :] = out
        attn_grad[c, t, at, :] = out.astype(bf16)

    def row_copy(step, source, target):
        return remote(attn_grad.at[source, t], attn_grad.at[source, t], row_s.at[step], row_r.at[step], ctx=target)

    def pass_copy(step, source, core):
        return remote(attn_grad.at[source, core], attn_grad.at[source, core], pass_s.at[step], pass_r.at[step], tp=1 - t)

    for step in range(1, nc):
        row_copy(step, c, ring(c, step, nc)).start()
    pass_copy(0, c, t).start()
    for step in range(1, nc):
        source = ring(c, -step, nc)
        row_copy(step, source, source).wait_recv()
        pass_copy(step, source, t).start()
    for step in range(nc):
        source = ring(c, -step, nc)
        pass_copy(step, source, 1 - t).wait_recv()
        pass_copy(step, source, t).wait_send()
        if step:
            row_copy(step, c, source).wait_send()
    done()
    for n, (i, j) in enumerate(steps):
        zz, cc = ring(z, -i, nz), ring(c, -j, nc)
        copy = early_copy(n, zz * nc + cc, zz * nc + cc, zz, cc)
        copy.wait_recv()
        copy.wait_send()
    keep_early.wait()


def give_back(r, g, early, pick_t, residual, probs, kept, router, gain, cot):
    nz, nc = lax.axis_size("fsdp"), lax.axis_size("ctx")
    rows, width = residual.shape
    dma = pltpu.SemaphoreType.DMA
    bf16, f32 = jnp.bfloat16, jnp.float32
    vmem = pl.BlockSpec(memory_space=pltpu.VMEM)
    hbm = pl.BlockSpec(memory_space=pl.ANY)
    bufs, sems = collector_scratch(nz, nc, r.shape[2], rows, (width, 256))
    return pl.pallas_call(
        functools.partial(return_kernel, nz, nc),
        out_shape=[
            jax.ShapeDtypeStruct((rows, 128), bf16),
            jax.ShapeDtypeStruct((8, width), f32),
            jax.ShapeDtypeStruct((rows, width), f32),
            jax.ShapeDtypeStruct((nc, 2, rows, width), bf16),
            jax.ShapeDtypeStruct(early.shape, bf16),
        ],
        in_specs=[hbm] * 3 + [vmem] * 7,
        out_specs=[vmem] * 4 + [hbm],
        scratch_shapes=bufs
        + sems
        + [dma((nc,)), dma((nc,)), dma((nc,)), dma((nc,))]
        + [dma((nz * nc - 1,)), dma((nz * nc - 1,)), dma],
        compiler_params=pltpu.CompilerParams(
            collective_id=2, has_side_effects=True, vmem_limit_bytes=56 * 2**20
        ),
    )(r, g, early, pick_t, residual, probs, kept, router, gain, cot)


def final_kernel(
    nz, nc, part, tok, gain, residual_grad, dw, dwo, small, y, pick_t, residual,
    tokens_grad, dw_out, dwo_out, small_out, layer,
    sib, rs_send, rs_recv, tok_grad, gain_acc, dw_up, dw_down, dwo_up, dwo_down, dw_to, dwo_to,
    dw_next, dwo_next, small_line, small_plane, small_sib, small_a, small_b,
    sib_s, sib_r, rs_s, rs_r, line_s, line_r, to_s, to_r, tg_s, tg_r, sm_s, sm_r, sp_s, sp_r, ss_s, ss_r,
    layer_send, lay_s, lay_r, *scratch,
):
    z, c, t = places()
    f32, bf16 = jnp.float32, jnp.bfloat16
    rows, width = residual_grad.shape
    piece = width // 2
    chunk = 16
    y_line = scratch[4]
    begin, process, join, done = collector(nz, nc, pick_t, ((y,) + scratch[:5],), scratch[5:])
    greet(nz, nc, True)

    bufs = ((dw, dw_up, dw_down), (dwo, dwo_up, dwo_down))
    outs = (dw_next, dwo_next)

    def hop(way, step, k, target):
        src = outs[k].at[way, step]
        return remote(src, bufs[k][1 + way].at[step], line_s.at[way, step, k], line_r.at[way, step, k], fsdp=target)

    def add_to(k, way, step, shard, joined):
        own, out = bufs[k][0], outs[k]
        got = bufs[k][1 + way]
        height = own.shape[2]
        tile = 32

        @pl.loop(0, nc * (height // tile))
        def _(n):
            q, at = n // (height // tile), pl.ds(pl.multiple_of(lax.rem(n, height // tile) * tile, tile), tile)
            value = own[shard, q, at, :]
            if joined:
                value = (value.astype(f32) + got[step, q, at, :].astype(f32)).astype(bf16)
            out[way, step, q, at, :] = value

    def line_one(step, way):
        shard = nz - 1 - step if way == 0 else step
        ahead = z + 1 if way == 0 else z - 1
        behind = z - 1 if way == 0 else z + 1
        first = z == 0 if way == 0 else z == nz - 1
        sends = shard > z if way == 0 else shard < z
        gets = (z > 0) & (shard >= z) if way == 0 else (z < nz - 1) & (shard <= z)

        @pl.when(gets)
        def _():
            for k in range(2):
                hop(way, step, k, behind).wait_recv()

        @pl.when(sends & jnp.logical_not(first))
        def _():
            for k in range(2):
                add_to(k, way, step, shard, True)
                hop(way, step, k, ahead).start()

    def line_step(step):
        @pl.when(2 * z < nz)
        def _():
            line_one(step, 0)
            line_one(step, 1)

        @pl.when(2 * z >= nz)
        def _():
            line_one(step, 1)
            line_one(step, 0)

    def line_begin():
        for way in range(2):
            first = z == 0 if way == 0 else z == nz - 1

            @pl.when(first)
            def _():
                for step in range(nz - 1):
                    shard = nz - 1 - step if way == 0 else step
                    for k in range(2):
                        add_to(k, way, step, shard, False)
                        hop(way, step, k, z + 1 if way == 0 else z - 1).start()

    def sib_copy(q):
        return remote(part.at[q, 1 - t], sib.at[q], sib_s.at[q], sib_r.at[q], tp=1 - t)

    def rs_copy(step, target):
        return remote(rs_send.at[step], rs_recv.at[step], rs_s.at[step], rs_r.at[step], ctx=target)

    for step in range(1, nc + 1):
        sib_copy(ring(c, step, nc)).start()
    line_begin()
    for step in range(1, nc):
        q = ring(c, step, nc)
        sib_copy(q).wait_recv()

        @pl.loop(0, rows // chunk)
        def _(k):
            at = pl.ds(pl.multiple_of(k * chunk, chunk), chunk)
            rs_send[step - 1, at, :] = (part[q, t, at, :].astype(f32) + sib[q, at, :].astype(f32)).astype(bf16)

        rs_copy(step - 1, q).start()
    sib_copy(c).wait_recv()
    begin(0)
    line_step(0)
    begin(1)
    for step in range(1, nc):
        rs_copy(step - 1, c).wait_recv()
    gain_acc[...] = jnp.zeros_like(gain_acc)

    @pl.loop(0, rows // chunk)
    def _(k):
        at = pl.ds(pl.multiple_of(k * chunk, chunk), chunk)
        full = pl.ds(pl.multiple_of(t * rows + k * chunk, chunk), chunk)
        grad = part[c, t, at, :].astype(f32) + sib[c, at, :].astype(f32)
        for step in range(nc - 1):
            grad = grad + rs_recv[step, at, :].astype(f32)
        x = tok[full, :].astype(f32)
        inv = lax.rsqrt(jnp.mean(x * x, -1, keepdims=True) + EPS)
        gain_acc[...] += jnp.sum((grad * x * inv).reshape(chunk // 8, 8, width), 0)
        weighted = grad * gain[...]
        inner = jnp.sum(weighted * x, -1, keepdims=True)
        out = residual_grad[at, :] + inv * weighted - x * (inv * inv * inv) * inner / width
        tok_grad[at, :] = out.astype(bf16)
        tokens_grad[full, :] = out.astype(bf16)

    def grad_copy(core):
        return remote(
            tok_grad, tokens_grad.at[pl.ds(pl.multiple_of(core * rows, rows), rows)], tg_s, tg_r, tp=1 - t
        )

    grad_copy(t).start()

    small_a[...] = small[...]
    total = jnp.sum(gain_acc[...], 0, keepdims=True)
    for strip in range(nz * nc):
        small_a[strip // nc, strip % nc, pl.ds(17, 1), :] = total[:, strip * 128 : (strip + 1) * 128]

    def small_copy(step, shard, target):
        return remote(small_a.at[shard], small_line.at[step], sm_s.at[step], sm_r.at[step], fsdp=target)

    def plane_copy(step, shard, target):
        return remote(small_b.at[shard], small_plane.at[step], sp_s.at[step], sp_r.at[step], ctx=target)

    for step in range(1, nz):
        small_copy(step - 1, ring(z, step, nz), ring(z, step, nz)).start()
    line_step(1)
    process(0)
    line_step(2)
    process(1)
    for step in range(1, nz):
        small_copy(step - 1, z, z).wait_recv()
    value = small_a[z]
    for step in range(nz - 1):
        value = value + small_line[step]
    small_b[...] = value
    for step in range(1, nc):
        plane_copy(step - 1, ring(c, step, nc), ring(c, step, nc)).start()

    def close(k, out, to):
        own, up, down = bufs[k]
        height = own.shape[2]
        tile = 32

        @pl.loop(0, nc * (height // tile))
        def _(n):
            q, at = n // (height // tile), pl.ds(pl.multiple_of(lax.rem(n, height // tile) * tile, tile), tile)
            base = own[z, q, at, :].astype(f32)
            above = up[jnp.minimum(nz - 1 - z, nz - 2), q, at, :].astype(f32)
            below = down[jnp.minimum(z, nz - 2), q, at, :].astype(f32)
            base = base + jnp.where(z > 0, above, 0.0) + jnp.where(z < nz - 1, below, 0.0)
            to[q, at, :] = base.astype(bf16)

    close(0, dw_out, dw_to)
    close(1, dwo_out, dwo_to)

    def to_copy(k, step, source, target):
        src, dst = ((dw_to, dw_out), (dwo_to, dwo_out))[k]
        return remote(src.at[target], dst.at[source], to_s.at[k, step], to_r.at[k, step], ctx=target)

    for step in range(1, nc):
        for k in range(2):
            to_copy(k, step - 1, c, ring(c, step, nc)).start()
    def layer_copy(core):
        return remote(
            layer_send.at[:, pl.ds(pl.multiple_of((1 - t) * piece, piece), piece)],
            layer.at[pl.ds(pl.multiple_of(core * rows, rows), rows)],
            lay_s, lay_r, tp=1 - t,
        )

    join()

    @pl.loop(0, rows // chunk)
    def _(k):
        at = pl.ds(pl.multiple_of(k * chunk, chunk), chunk)
        full = pl.ds(pl.multiple_of(t * rows + k * chunk, chunk), chunk)
        total = residual[at, :]
        for source in range(nz):
            total = total + y_line[source, at, :].astype(f32)
        layer_send[at, :] = total.astype(bf16)
        layer[full, :] = layer_send[at, pl.ds(pl.multiple_of(t * piece, piece), piece)]

    layer_copy(t).start()
    dw_out[c, :, :] = dw_to[c, :, :]
    dwo_out[c, :, :] = dwo_to[c, :, :]
    for step in range(1, nc):
        plane_copy(step - 1, c, c).wait_recv()
    value = small_b[c]
    for step in range(nc - 1):
        value = value + small_plane[step]
    small_out[...] = value
    final = remote(small_out, small_sib, ss_s, ss_r, tp=1 - t)
    final.start()
    final.wait()
    small_out[...] = value + small_sib[...]
    for step in range(1, nc):
        source = ring(c, -step, nc)
        for k in range(2):
            src, dst = ((dw_to, dw_out), (dwo_to, dwo_out))[k]
            remote(
                src.at[c], dst.at[source], to_s.at[k, step - 1], to_r.at[k, step - 1], ctx=source
            ).wait_recv()
    grad_copy(1 - t).wait_recv()
    grad_copy(t).wait_send()
    layer_copy(1 - t).wait_recv()
    layer_copy(t).wait_send()
    done()
    for step in range(1, nc):
        for k in range(2):
            to_copy(k, step - 1, c, ring(c, step, nc)).wait_send()
        plane_copy(step - 1, ring(c, step, nc), ring(c, step, nc)).wait_send()
        rs_copy(step - 1, c).wait_send()
    for step in range(1, nz):
        small_copy(step - 1, ring(z, step, nz), ring(z, step, nz)).wait_send()
    for q in range(nc):
        sib_copy(q).wait_send()
    for step in range(nz - 1):
        for way in range(2):
            shard = nz - 1 - step if way == 0 else step
            ahead = z + 1 if way == 0 else z - 1
            sends = shard > z if way == 0 else shard < z

            @pl.when(sends)
            def _():
                for k in range(2):
                    hop(way, step, k, ahead).wait_send()


def finish(part, tok, gain, residual_grad, dw, dwo, small, y, pick_t, residual):
    nz, nc = lax.axis_size("fsdp"), lax.axis_size("ctx")
    rows, width = residual_grad.shape
    dma = pltpu.SemaphoreType.DMA
    bf16, f32 = jnp.bfloat16, jnp.float32
    vmem = pl.BlockSpec(memory_space=pltpu.VMEM)
    one, two = dw.shape[1:], dwo.shape[1:]
    bufs, sems = collector_scratch(nz, nc, y.shape[2], rows, (width,))
    tiny = small.shape[2:]
    return pl.pallas_call(
        functools.partial(final_kernel, nz, nc),
        out_shape=[
            jax.ShapeDtypeStruct((2 * rows, width), bf16),
            jax.ShapeDtypeStruct(one, bf16),
            jax.ShapeDtypeStruct(two, bf16),
            jax.ShapeDtypeStruct(tiny, f32),
            jax.ShapeDtypeStruct((2 * rows, width // 2), bf16),
        ],
        in_specs=[vmem] * 7 + [pl.BlockSpec(memory_space=pl.ANY)] + [vmem] * 2,
        out_specs=[vmem] * 5,
        scratch_shapes=[
            pltpu.VMEM((nc, rows, width), bf16),
            pltpu.VMEM((nc - 1, rows, width), bf16),
            pltpu.VMEM((nc - 1, rows, width), bf16),
            pltpu.VMEM((rows, width), bf16),
            pltpu.VMEM((8, width), f32),
            pltpu.VMEM((nz - 1,) + one, bf16),
            pltpu.VMEM((nz - 1,) + one, bf16),
            pltpu.VMEM((nz - 1,) + two, bf16),
            pltpu.VMEM((nz - 1,) + two, bf16),
            pltpu.VMEM(one, bf16),
            pltpu.VMEM(two, bf16),
            pltpu.VMEM((2, nz - 1) + one, bf16),
            pltpu.VMEM((2, nz - 1) + two, bf16),
            pltpu.VMEM((nz - 1,) + small.shape[1:], f32),
            pltpu.VMEM((nc - 1,) + tiny, f32),
            pltpu.VMEM(tiny, f32),
            pltpu.VMEM(small.shape, f32),
            pltpu.VMEM(small.shape[1:], f32),
            dma((nc,)), dma((nc,)), dma((nc - 1,)), dma((nc - 1,)),
            dma((2, nz - 1, 2)), dma((2, nz - 1, 2)),
            dma((2, nc - 1)), dma((2, nc - 1)), dma, dma,
            dma((nz - 1,)), dma((nz - 1,)), dma((nc - 1,)), dma((nc - 1,)), dma, dma,
            pltpu.VMEM((rows, width), bf16), dma, dma,
        ] + bufs + sems,
        compiler_params=pltpu.CompilerParams(
            collective_id=3, has_side_effects=True, vmem_limit_bytes=60 * 2**20
        ),
    )(part, tok, gain, residual_grad, dw, dwo, small, y, pick_t, residual)


def one_chip(
    tokens,
    w_query,
    w_key,
    w_value,
    w_out,
    gain_attn,
    gain_query,
    gain_key,
    gain_moe,
    w_router,
    w_experts,
    routes,
    cotangent,
):
    z, c, t = lax.axis_index("fsdp"), lax.axis_index("ctx"), lax.axis_index("tp")
    nz, nc = lax.axis_size("fsdp"), lax.axis_size("ctx")
    block, width = tokens.shape[1], tokens.shape[2]
    rows = block // 2
    tall = block * nc
    deep = width // nz
    ffn = w_experts.shape[3]
    most = block * TOPK * 9 // (8 * E)
    bf16, f32 = jnp.bfloat16, jnp.float32

    token_half = lax.dynamic_slice_in_dim(tokens[0], t * rows, rows, 0)
    cotan_half = lax.dynamic_slice_in_dim(cotangent[0], t * rows, rows, 0)
    local = w_query.shape[1] // nc
    small = jnp.concatenate([w_router.T.reshape(-1), gain_attn, gain_moe, gain_query, gain_key])
    total = small.shape[0]
    small = jnp.pad(small, (0, -total % 2048))
    small = small.reshape(-1, 128)
    ids = jnp.arange(E, dtype=jnp.int32)
    named = jnp.any(routes[0][:, :, None] == ids, 1)
    below = jnp.tril(jnp.ones((block, block), bf16), -1)
    rank = jnp.where(named, dot(below, named.astype(bf16)), -1.0).T
    x_rows, w_qkv, w_o, small, _, rank_seq, pick, cot_rows = load(
        tokens[0], cotangent[0], w_query, w_key, w_value, w_out, small, rank, most
    )
    w_qkv = w_qkv.reshape(width, 3 * local)
    w_o = w_o.transpose(1, 0, 2).reshape(local, width)
    small = small.reshape(nz, -1)
    router = small[:, : E * deep].reshape(nz, E, deep).transpose(1, 0, 2).reshape(E, width)
    at = E * deep
    attn_gain = small[:, at : at + deep].reshape(-1).astype(f32)
    moe_gain = small[:, at + deep : at + 2 * deep].reshape(-1).astype(f32)
    at, part = at + 2 * deep, HD // nz
    query_gain = small[:, at : at + part].reshape(-1).astype(f32)
    key_gain = small[:, at + part : at + 2 * part].reshape(-1).astype(f32)

    w_experts, w_qkv = lax.optimization_barrier((w_experts, w_qkv))
    pair, third = select(w_experts, nz)
    pair = exchange(pair, "fsdp")

    counts = jnp.sum((rank_seq >= 0).astype(f32), 2)
    earlier = jnp.sum(jnp.where(jnp.arange(nc)[:, None] < c, counts, 0.0), 0)
    kept = ((rank >= 0) & (rank + earlier[:, None] < CAP)).astype(f32).T
    kept = lax.dynamic_slice_in_dim(kept, t * rows, rows, 0)

    x_rows = x_rows.astype(f32)
    place = jnp.arange(tall, dtype=jnp.int32)
    half_dim = HD // 2
    inv_freq = jnp.exp(jnp.arange(half_dim, dtype=f32) * (-2.0 * math.log(ROPE_BASE) / HD))
    angles = place.astype(f32)[:, None] * inv_freq[None, :]
    cos_full = jnp.concatenate([jnp.cos(angles)] * 2, -1)[:, None, :]
    sin_full = jnp.concatenate([jnp.sin(angles)] * 2, -1)[:, None, :]
    normed_one = (x_rows * rms_scale(x_rows) * attn_gain).astype(bf16)
    proj = dot(normed_one, w_qkv).reshape(tall, 3, local // HD, HD)
    query_heads, key_heads = proj[:, 0], proj[:, 1]
    values = proj[:, 2].astype(bf16)
    query_inv, key_inv = rms_scale(query_heads), rms_scale(key_heads)
    queries = apply_rope(query_heads * query_inv * query_gain, cos_full, sin_full).astype(bf16)
    keys = apply_rope(key_heads * key_inv * key_gain, cos_full, sin_full).astype(bf16)
    score_scale = 1.0 / math.sqrt(HD)
    scores = jnp.einsum("qhd,khd->hqk", queries, keys, preferred_element_type=f32) * score_scale
    maximum = jnp.max(scores, -1, keepdims=True)
    exp_scores = jnp.exp(scores - maximum)
    denominator = jnp.sum(exp_scores, -1, keepdims=True)
    attn_probs = exp_scores / denominator
    log_total = maximum + jnp.log(denominator)
    context = jnp.einsum("hqk,khd->qhd", attn_probs.astype(bf16), values, preferred_element_type=f32)
    context = context.astype(bf16).reshape(tall, local)
    attn_part = dot(context, w_o).astype(bf16).reshape(nc, 2, rows, width)
    kept_wide = jnp.pad(kept, ((0, 0), (0, 128 - E)))
    router_wide = jnp.pad(router, ((0, 128 - E), (0, 0)))
    residual, normed_two, router_probs, x_in, g_in, third = dispatch(
        attn_part, tokens[0], moe_gain[None], router_wide, kept_wide, pick, third
    )
    pair, x_in = lax.optimization_barrier((pair, x_in))
    x_in = x_in.reshape(nc * 2 * most, width)
    cot_rows = cot_rows.reshape(nc * 2 * most, width)
    chips = nz * nc
    strip = width // chips
    out_rows, back_rows, pair_rows, own_grad, other_grad = experts(
        x_in, cot_rows, g_in.reshape(nc * 2 * most, -1), pair, third, strip
    )
    early = 1
    dw_gate = (own_grad[:, :early].astype(f32) + other_grad[:, :early].astype(f32)).astype(bf16)
    shape = (nc, 2, most, -1)
    pick_t = pick.transpose(0, 2, 1)
    grad_logits, dgain_moe, grad_residual, grad_attn, dw_gate = give_back(
        back_rows.reshape(shape),
        pair_rows.reshape(shape),
        dw_gate,
        pick_t,
        residual,
        router_probs,
        kept_wide,
        router_wide,
        moe_gain[None],
        cotangent[0],
    )

    dw_router = dot_tn(normed_two, grad_logits[:, :E])
    dgain_moe = jnp.sum(dgain_moe, 0)
    dw_rest = (own_grad[:, early:].astype(f32) + other_grad[:, early:].astype(f32)).astype(bf16)
    dw_rest, grad_attn = lax.optimization_barrier((dw_rest, grad_attn))
    dw_rest = exchange(dw_rest, ("fsdp", "ctx"))
    grad_attn = grad_attn.reshape(tall, width)

    dw_out = dot_tn(context, grad_attn).astype(bf16)
    grad_context = dot_nt(grad_attn, w_o).astype(bf16).reshape(tall, -1, HD)
    scores = jnp.einsum("qhd,khd->hqk", queries, keys, preferred_element_type=f32) * score_scale
    attn_probs = jnp.exp(scores - log_total)
    grad_probs = jnp.einsum("qhd,khd->hqk", grad_context, values, preferred_element_type=f32)
    grad_scores = attn_probs * (grad_probs - jnp.sum(attn_probs * grad_probs, -1, keepdims=True))
    grad_scores = grad_scores.astype(bf16)
    grad_queries = jnp.einsum("hqk,khd->qhd", grad_scores, keys, preferred_element_type=f32) * score_scale
    grad_keys = jnp.einsum("hqk,qhd->khd", grad_scores, queries, preferred_element_type=f32) * score_scale
    grad_values = jnp.einsum(
        "hqk,qhd->khd", attn_probs.astype(bf16), grad_context, preferred_element_type=f32
    ).astype(bf16)
    grad_qnormed = rope_back(grad_queries, cos_full, sin_full)
    grad_knormed = rope_back(grad_keys, cos_full, sin_full)
    dgain_query = jnp.sum(grad_qnormed * query_heads * query_inv, (0, 1))
    dgain_key = jnp.sum(grad_knormed * key_heads * key_inv, (0, 1))
    grad_qproj = norm_back(grad_qnormed, query_heads, query_inv, query_gain).astype(bf16)
    grad_kproj = norm_back(grad_knormed, key_heads, key_inv, key_gain).astype(bf16)
    grad_proj = jnp.stack([grad_qproj, grad_kproj, grad_values], 1).reshape(tall, 3 * local)
    dw_qkv = dot_tn(normed_one, grad_proj).astype(bf16)
    grad_normed_part = dot_nt(grad_proj, w_qkv).astype(bf16).reshape(nc, 2, rows, width)
    head_part = HD // chips
    heads = [dgain_query.reshape(chips, 1, head_part), dgain_key.reshape(chips, 1, head_part)]
    heads = jnp.pad(jnp.concatenate(heads, 2), ((0, 0), (0, 0), (0, strip - 2 * head_part)))
    sums = jnp.concatenate(
        [
            dw_router.reshape(chips, E, strip),
            dgain_moe.reshape(chips, 1, strip),
            jnp.zeros((chips, 1, strip), f32),
            heads,
            jnp.zeros((chips, 24 - E - 3, strip), f32),
        ],
        1,
    ).reshape(nz, nc, 24, strip)
    tokens_grad, got_qkv, got_out, sums, layer_out = finish(
        grad_normed_part,
        tokens[0],
        attn_gain[None],
        grad_residual,
        dw_qkv.reshape(nz, nc, strip, 3 * local),
        dw_out.reshape(local, nz, nc, strip).transpose(1, 2, 0, 3),
        sums,
        out_rows.reshape(shape),
        pick_t,
        residual,
    )
    dw_experts = lay_out(dw_gate, dw_rest, nz, nc)
    got_qkv = got_qkv.astype(f32).reshape(nc, strip, 3, local)
    got_qkv = got_qkv.transpose(2, 1, 0, 3).reshape(3, strip, nc * local)
    return (
        layer_out[None],
        tokens_grad[None],
        got_qkv[0],
        got_qkv[1],
        got_qkv[2],
        got_out.astype(f32).reshape(nc * local, strip),
        sums[E + 1],
        sums[E + 2, :head_part],
        sums[E + 2, head_part : 2 * head_part],
        sums[E],
        sums[:E].reshape(strip, E),
        dw_experts,
    )


def solution(mesh):
    chips = mesh.shape["fsdp"] * mesh.shape["ctx"]
    plain = chips == E and mesh.shape["fsdp"] == 4 and mesh.shape["tp"] == 2
    return jax.shard_map(
        one_chip if plain else general,
        mesh=mesh,
        in_specs=(
            P("fsdp", "ctx", None),
            P("fsdp", "tp"),
            P("fsdp", "tp"),
            P("fsdp", "tp"),
            P("tp", "fsdp"),
            P("fsdp"),
            P("fsdp"),
            P("fsdp"),
            P("fsdp"),
            P("fsdp", None),
            P("fsdp", None, None, "tp"),
            P("fsdp", "ctx", None),
            P("fsdp", "ctx", None),
        ),
        out_specs=(
            P("fsdp", "ctx", "tp"),
            P("fsdp", "ctx", None),
            P(("fsdp", "ctx"), "tp"),
            P(("fsdp", "ctx"), "tp"),
            P(("fsdp", "ctx"), "tp"),
            P("tp", ("fsdp", "ctx")),
            P(("fsdp", "ctx")),
            P(("fsdp", "ctx")),
            P(("fsdp", "ctx")),
            P(("fsdp", "ctx")),
            P(("fsdp", "ctx"), None),
            P(("fsdp", "ctx"), None, None, "tp"),
        ),
        check_vma=False,
    )
```

```python
import functools
import math

import jax
import jax.numpy as jnp
from jax import lax
from jax.experimental import pallas as pl
from jax.experimental.pallas import tpu as pltpu
from jax.sharding import PartitionSpec as P

HD = 128
TOPK = 8
E = 16
CAP = 512
MESH = pl.DeviceIdType.MESH


EPS = 1e-06
ROPE_BASE = 10000.0


def prefix(value, axis, join, neutral):
    count, mine = (lax.axis_size(axis), lax.axis_index(axis))
    pieces = lax.all_gather(value, axis)
    running = jnp.full_like(value, 0) + jnp.asarray(neutral, value.dtype)

    def lap(position, running):
        longer = join(running, pieces[position])
        return jnp.where(position < mine, longer, running)

    return lax.fori_loop(0, count - 1, lap, running)


def rms_scale(values):
    return lax.rsqrt(jnp.mean(values * values, -1, keepdims=True) + EPS)


def norm_back(grad_normed, values, inv_rms, gain_vec):
    weighted = grad_normed * gain_vec.astype(jnp.float32)
    inner_sum = jnp.sum(weighted * values, -1, keepdims=True)
    return (
        inv_rms * weighted - values * (inv_rms * inv_rms * inv_rms) * inner_sum / values.shape[-1]
    )


def rope_tables(first, length):
    half_dim = HD // 2
    inv_freq = jnp.exp(jnp.arange(half_dim, dtype=jnp.float32) * (-2.0 * math.log(ROPE_BASE) / HD))
    places = (first + jnp.arange(length, dtype=jnp.int32)).astype(jnp.float32)
    angles = places[:, None] * inv_freq[None, :]
    cos_table = jnp.cos(angles)
    sin_table = jnp.sin(angles)
    cos_full = jnp.concatenate([cos_table, cos_table], -1)[:, None, :]
    sin_full = jnp.concatenate([sin_table, sin_table], -1)[:, None, :]
    return (cos_full, sin_full)


def rotate(values):
    half_dim = values.shape[-1] // 2
    return jnp.concatenate([-values[..., half_dim:], values[..., :half_dim]], -1)


def rotate_back(values):
    half_dim = values.shape[-1] // 2
    return jnp.concatenate([values[..., half_dim:], -values[..., :half_dim]], -1)


def apply_rope(values, cos_full, sin_full):
    return values * cos_full + rotate(values) * sin_full


def rope_back(grads, cos_full, sin_full):
    return grads * cos_full + rotate_back(grads * sin_full)


def add_counts(earlier, later):
    return earlier + later


def general(
    tokens,
    w_query,
    w_key,
    w_value,
    w_out,
    gain_attn,
    gain_query,
    gain_key,
    gain_moe,
    w_router,
    w_experts,
    routes,
    cotangent,
):
    seq_count, block_len, model_width = tokens.shape
    row_count = seq_count * block_len
    (
        full_query,
        full_key,
        full_value,
        full_out,
        router_full,
        attn_gain,
        query_gain,
        key_gain,
        moe_gain,
    ) = (
        lax.all_gather(w_query, "fsdp", axis=0, tiled=True),
        lax.all_gather(w_key, "fsdp", axis=0, tiled=True),
        lax.all_gather(w_value, "fsdp", axis=0, tiled=True),
        lax.all_gather(w_out, "fsdp", axis=1, tiled=True),
        lax.all_gather(w_router, "fsdp", axis=0, tiled=True),
        lax.all_gather(gain_attn, "fsdp", axis=0, tiled=True),
        lax.all_gather(gain_query, "fsdp", axis=0, tiled=True),
        lax.all_gather(gain_key, "fsdp", axis=0, tiled=True),
        lax.all_gather(gain_moe, "fsdp", axis=0, tiled=True),
    )
    local_width = full_query.shape[1]
    head_count = local_width // HD
    head_shape = (seq_count, block_len, head_count, HD)
    token_rows = tokens.reshape(row_count, model_width).astype(jnp.float32)
    inv_one = rms_scale(token_rows)
    normed_one = (token_rows * inv_one * attn_gain.astype(jnp.float32)).astype(jnp.bfloat16)
    query_proj = jnp.dot(normed_one, full_query, preferred_element_type=jnp.float32)
    key_proj = jnp.dot(normed_one, full_key, preferred_element_type=jnp.float32)
    value_proj = jnp.dot(normed_one, full_value, preferred_element_type=jnp.float32)
    cos_full, sin_full = rope_tables(lax.axis_index("ctx") * block_len, block_len)
    query_heads = query_proj.reshape(head_shape)
    key_heads = key_proj.reshape(head_shape)
    query_inv = rms_scale(query_heads)
    key_inv = rms_scale(key_heads)
    queries = apply_rope(
        query_heads * query_inv * query_gain.astype(jnp.float32), cos_full, sin_full
    ).astype(jnp.bfloat16)
    keys_local = apply_rope(
        key_heads * key_inv * key_gain.astype(jnp.float32), cos_full, sin_full
    ).astype(jnp.bfloat16)
    keys_local = keys_local.reshape(seq_count, block_len, local_width)
    values_local = value_proj.astype(jnp.bfloat16).reshape(seq_count, block_len, local_width)
    keys_all, values_all = (
        lax.all_gather(keys_local, "ctx", axis=1, tiled=True),
        lax.all_gather(values_local, "ctx", axis=1, tiled=True),
    )
    seq_len = keys_all.shape[1]
    key_rows = keys_all.reshape(seq_count, seq_len, head_count, HD)
    value_rows = values_all.reshape(seq_count, seq_len, head_count, HD)
    score_scale = 1.0 / math.sqrt(HD)
    scores = (
        jnp.einsum("sqhd,skhd->shqk", queries, key_rows, preferred_element_type=jnp.float32)
        * score_scale
    )
    maximum = jnp.max(scores, -1, keepdims=True)
    exp_scores = jnp.exp(scores - maximum)
    denominator = jnp.sum(exp_scores, -1, keepdims=True)
    attn_probs = exp_scores / denominator
    log_total = maximum + jnp.log(denominator)
    context = jnp.einsum(
        "shqk,skhd->sqhd",
        attn_probs.astype(jnp.bfloat16),
        value_rows,
        preferred_element_type=jnp.float32,
    )
    context = context.astype(jnp.bfloat16).reshape(row_count, local_width)
    attn_part = jnp.dot(context, full_out, preferred_element_type=jnp.float32)
    residual = token_rows + lax.psum(attn_part, "tp")
    inv_two = rms_scale(residual)
    normed_two = (residual * inv_two * moe_gain.astype(jnp.float32)).astype(jnp.bfloat16)
    logits = jnp.dot(normed_two, router_full, preferred_element_type=jnp.float32)
    router_probs = jax.nn.softmax(logits, -1)
    pair_count = block_len * TOPK
    route_rows = routes.reshape(seq_count, pair_count)
    expert_ids = jnp.arange(E, dtype=jnp.int32)
    onehot = (route_rows[:, :, None] == expert_ids[None, None, :]).astype(jnp.int32)
    counts = jnp.sum(onehot, 1, dtype=jnp.int32)
    offsets = prefix(counts, "ctx", add_counts, jnp.zeros_like(counts))
    earlier = jnp.cumsum(onehot, 1, dtype=jnp.int32) - onehot
    local_rank = jnp.sum(earlier * onehot, 2, dtype=jnp.int32)
    slot_base = jnp.sum(onehot * offsets[:, None, :], 2, dtype=jnp.int32)
    kept_mask = (slot_base + local_rank < CAP).astype(jnp.float32).reshape(row_count, TOPK)
    block_most = pair_count * 9 // (8 * E)
    expert_span = seq_count * block_most
    seq_ids = jnp.arange(seq_count, dtype=jnp.int32)[:, None]
    buffer_row = (route_rows * expert_span + seq_ids * block_most + local_rank).reshape(
        row_count * TOPK
    )
    token_ids = (
        seq_ids * block_len + jnp.arange(pair_count, dtype=jnp.int32)[None, :] // TOPK
    ).reshape(row_count * TOPK)
    owner_rows = jnp.zeros((E * expert_span,), jnp.int32).at[buffer_row].set(token_ids)
    onehot_f = onehot.astype(jnp.float32).reshape(row_count, TOPK, E)
    gate_weight = jnp.sum(onehot_f * router_probs[:, None, :], 2) * kept_mask
    slot_weight = (
        jnp.zeros((E * expert_span,), jnp.float32)
        .at[buffer_row]
        .set(gate_weight.reshape(row_count * TOPK))
    )
    expert_rows = normed_two[owner_rows].reshape(E, expert_span, model_width)
    cotan_rows = cotangent.reshape(row_count, model_width)
    grad_expert = (slot_weight[:, None] * cotan_rows[owner_rows].astype(jnp.float32)).astype(
        jnp.bfloat16
    )
    grad_expert = grad_expert.reshape(E, expert_span, model_width)
    ffn_local = w_experts.shape[3]
    fsdp_count = lax.axis_size("fsdp")
    ctx_count = lax.axis_size("ctx")
    group_count = fsdp_count * ctx_count
    sharing = group_count // E
    padded_span = -(-expert_span // sharing) * sharing
    part_span = padded_span // sharing
    target_experts = (
        jnp.arange(fsdp_count, dtype=jnp.int32) * ctx_count + lax.axis_index("ctx")
    ) // sharing
    selected = jnp.take(w_experts, target_experts, axis=2)
    owned = lax.all_to_all(selected, "fsdp", split_axis=2, concat_axis=0, tiled=True)[:, :, 0]
    send_rows = expert_rows.reshape(group_count, part_span, model_width)
    send_grads = grad_expert.reshape(group_count, part_span, model_width)
    recv_rows, recv_grads = (
        lax.all_to_all(send_rows, ("fsdp", "ctx"), split_axis=0, concat_axis=0, tiled=True),
        lax.all_to_all(send_grads, ("fsdp", "ctx"), split_axis=0, concat_axis=0, tiled=True),
    )
    rows_flat = recv_rows.reshape(group_count * part_span, model_width)
    grads_flat = recv_grads.reshape(group_count * part_span, model_width)
    gate_act = jnp.dot(rows_flat, owned[:, 0], preferred_element_type=jnp.float32)
    up_act = jnp.dot(rows_flat, owned[:, 1], preferred_element_type=jnp.float32)
    sigmoid_gate = jax.nn.sigmoid(gate_act)
    silu_gate = gate_act * sigmoid_gate
    hidden = (silu_gate * up_act).astype(jnp.bfloat16)
    produced = jnp.einsum("mf,df->md", hidden, owned[:, 2], preferred_element_type=jnp.float32)
    grad_hidden = jnp.dot(grads_flat, owned[:, 2], preferred_element_type=jnp.float32)
    grad_gate = (
        grad_hidden * up_act * sigmoid_gate * (1.0 + gate_act * (1.0 - sigmoid_gate))
    ).astype(jnp.bfloat16)
    grad_up = (grad_hidden * silu_gate).astype(jnp.bfloat16)
    rows_grad = jnp.einsum("mf,df->md", grad_gate, owned[:, 0], preferred_element_type=jnp.float32)
    rows_grad = rows_grad + jnp.einsum(
        "mf,df->md", grad_up, owned[:, 1], preferred_element_type=jnp.float32
    )
    back_out, back_rows = (
        lax.all_to_all(
            produced.reshape(group_count, part_span, model_width).astype(jnp.bfloat16),
            ("fsdp", "ctx"),
            split_axis=0,
            concat_axis=0,
            tiled=True,
        ).astype(jnp.float32),
        lax.all_to_all(
            rows_grad.reshape(group_count, part_span, model_width).astype(jnp.bfloat16),
            ("fsdp", "ctx"),
            split_axis=0,
            concat_axis=0,
            tiled=True,
        ).astype(jnp.float32),
    )
    expert_out = back_out.reshape(E, padded_span, model_width)
    grad_rows = back_rows.reshape(E, padded_span, model_width)
    gate_term = jnp.einsum("md,mf->df", rows_flat, grad_gate, preferred_element_type=jnp.float32)
    up_term = jnp.einsum("md,mf->df", rows_flat, grad_up, preferred_element_type=jnp.float32)
    down_term = jnp.einsum("md,mf->df", grads_flat, hidden, preferred_element_type=jnp.float32)
    owner_terms = jnp.stack([gate_term, up_term, down_term], 1)[:, :, None, :]
    relaid = lax.all_to_all(
        owner_terms.astype(jnp.bfloat16), ("fsdp", "ctx"), split_axis=0, concat_axis=2, tiled=True
    ).astype(owner_terms.dtype)
    dw_experts = jnp.sum(relaid.reshape(relaid.shape[0], 3, E, sharing, ffn_local), 3)
    picked = expert_out.reshape(E * expert_span, model_width)[buffer_row].reshape(
        row_count, TOPK, model_width
    )
    moe_part = jnp.sum(gate_weight[:, :, None] * picked, 1)
    cotan_float = cotan_rows.astype(jnp.float32)
    grad_gate_part = jnp.sum(picked * cotan_float[:, None, :], 2)
    moe_shard = lax.psum_scatter(
        moe_part.astype(jnp.bfloat16), "tp", scatter_dimension=1, tiled=True
    ).astype(jnp.float32)
    piece_width = moe_shard.shape[1]
    residual_shard = lax.dynamic_slice_in_dim(
        residual, lax.axis_index("tp") * piece_width, piece_width, 1
    )
    layer_out = (
        (residual_shard + moe_shard).astype(jnp.bfloat16).reshape(seq_count, block_len, piece_width)
    )
    grad_normed_part = jnp.sum(
        grad_rows.reshape(E * expert_span, model_width)[buffer_row].reshape(
            row_count, TOPK, model_width
        ),
        1,
    )
    grad_normed_sum, grad_gate_sum = (
        lax.psum(grad_normed_part.astype(jnp.bfloat16), "tp").astype(jnp.float32),
        lax.psum(grad_gate_part.astype(jnp.bfloat16), "tp").astype(jnp.float32),
    )
    grad_pick = grad_gate_sum * kept_mask
    grad_router_probs = jnp.sum(onehot_f * grad_pick[:, :, None], 1)
    grad_logits = router_probs * (
        grad_router_probs - jnp.sum(router_probs * grad_router_probs, -1, keepdims=True)
    )
    grad_logits = grad_logits.astype(jnp.bfloat16)
    grad_router_w = jnp.einsum(
        "nd,ne->de", normed_two, grad_logits, preferred_element_type=jnp.float32
    )
    grad_normed_two = grad_normed_sum + jnp.einsum(
        "ne,de->nd", grad_logits, router_full, preferred_element_type=jnp.float32
    )
    grad_moe_gain = jnp.sum(grad_normed_two * residual * inv_two, 0)
    grad_residual = cotan_float + norm_back(grad_normed_two, residual, inv_two, moe_gain)
    grad_attn = grad_residual.astype(jnp.bfloat16)
    grad_w_out = jnp.einsum("nl,nd->ld", context, grad_attn, preferred_element_type=jnp.float32)
    grad_context = jnp.einsum("nd,ld->nl", grad_attn, full_out, preferred_element_type=jnp.float32)
    grad_context = grad_context.astype(jnp.bfloat16).reshape(head_shape)
    scores = (
        jnp.einsum("sqhd,skhd->shqk", queries, key_rows, preferred_element_type=jnp.float32)
        * score_scale
    )
    attn_probs = jnp.exp(scores - log_total)
    grad_probs = jnp.einsum(
        "sqhd,skhd->shqk", grad_context, value_rows, preferred_element_type=jnp.float32
    )
    grad_scores = attn_probs * (grad_probs - jnp.sum(attn_probs * grad_probs, -1, keepdims=True))
    grad_scores = grad_scores.astype(jnp.bfloat16)
    grad_queries = (
        jnp.einsum("shqk,skhd->sqhd", grad_scores, key_rows, preferred_element_type=jnp.float32)
        * score_scale
    )
    grad_keys_all = (
        jnp.einsum("shqk,sqhd->skhd", grad_scores, queries, preferred_element_type=jnp.float32)
        * score_scale
    )
    grad_values_all = jnp.einsum(
        "shqk,sqhd->skhd",
        attn_probs.astype(jnp.bfloat16),
        grad_context,
        preferred_element_type=jnp.float32,
    )
    grad_keys_own, grad_values_own = (
        lax.psum_scatter(
            grad_keys_all.reshape(seq_count, seq_len, local_width).astype(jnp.bfloat16),
            "ctx",
            scatter_dimension=1,
            tiled=True,
        ).astype(jnp.float32),
        lax.psum_scatter(
            grad_values_all.reshape(seq_count, seq_len, local_width).astype(jnp.bfloat16),
            "ctx",
            scatter_dimension=1,
            tiled=True,
        ).astype(jnp.float32),
    )
    grad_qnormed = rope_back(grad_queries, cos_full, sin_full)
    grad_knormed = rope_back(grad_keys_own.reshape(head_shape), cos_full, sin_full)
    grad_qgain = jnp.sum(grad_qnormed * query_heads * query_inv, (0, 1, 2))
    grad_kgain = jnp.sum(grad_knormed * key_heads * key_inv, (0, 1, 2))
    grad_qproj = (
        norm_back(grad_qnormed, query_heads, query_inv, query_gain)
        .astype(jnp.bfloat16)
        .reshape(row_count, local_width)
    )
    grad_kproj = (
        norm_back(grad_knormed, key_heads, key_inv, key_gain)
        .astype(jnp.bfloat16)
        .reshape(row_count, local_width)
    )
    grad_vproj = grad_values_own.astype(jnp.bfloat16).reshape(row_count, local_width)
    grad_wq = jnp.einsum("nd,nl->dl", normed_one, grad_qproj, preferred_element_type=jnp.float32)
    grad_wk = jnp.einsum("nd,nl->dl", normed_one, grad_kproj, preferred_element_type=jnp.float32)
    grad_wv = jnp.einsum("nd,nl->dl", normed_one, grad_vproj, preferred_element_type=jnp.float32)
    grad_normed_one = jnp.einsum(
        "nl,dl->nd", grad_qproj, full_query, preferred_element_type=jnp.float32
    )
    grad_normed_one = grad_normed_one + jnp.einsum(
        "nl,dl->nd", grad_kproj, full_key, preferred_element_type=jnp.float32
    )
    grad_normed_one = grad_normed_one + jnp.einsum(
        "nl,dl->nd", grad_vproj, full_value, preferred_element_type=jnp.float32
    )
    grad_normed_one, grad_qgain, grad_kgain = (
        lax.psum(grad_normed_one.astype(jnp.bfloat16), "tp").astype(jnp.float32),
        lax.psum(grad_qgain.astype(jnp.bfloat16), "tp").astype(jnp.float32),
        lax.psum(grad_kgain.astype(jnp.bfloat16), "tp").astype(jnp.float32),
    )
    grad_attn_gain = jnp.sum(grad_normed_one * token_rows * inv_one, 0)
    tokens_grad = grad_residual + norm_back(grad_normed_one, token_rows, inv_one, attn_gain)
    tokens_grad = tokens_grad.astype(jnp.bfloat16).reshape(seq_count, block_len, model_width)
    dw_query, dw_key, dw_value, dw_out, dw_router, dgain_attn, dgain_query, dgain_key, dgain_moe = (
        lax.psum_scatter(grad_wq, ("fsdp", "ctx"), scatter_dimension=0, tiled=True),
        lax.psum_scatter(grad_wk, ("fsdp", "ctx"), scatter_dimension=0, tiled=True),
        lax.psum_scatter(grad_wv, ("fsdp", "ctx"), scatter_dimension=0, tiled=True),
        lax.psum_scatter(grad_w_out, ("fsdp", "ctx"), scatter_dimension=1, tiled=True),
        lax.psum_scatter(grad_router_w, ("fsdp", "ctx"), scatter_dimension=0, tiled=True),
        lax.psum_scatter(grad_attn_gain, ("fsdp", "ctx"), scatter_dimension=0, tiled=True),
        lax.psum_scatter(grad_qgain, ("fsdp", "ctx"), scatter_dimension=0, tiled=True),
        lax.psum_scatter(grad_kgain, ("fsdp", "ctx"), scatter_dimension=0, tiled=True),
        lax.psum_scatter(grad_moe_gain, ("fsdp", "ctx"), scatter_dimension=0, tiled=True),
    )
    return (
        layer_out,
        tokens_grad,
        dw_query,
        dw_key,
        dw_value,
        dw_out,
        dgain_attn,
        dgain_query,
        dgain_key,
        dgain_moe,
        dw_router,
        dw_experts,
    )


def swap(value):
    return lax.ppermute(value, "tp", [(0, 1), (1, 0)])


def exchange(value, axes):
    return lax.all_to_all(value, axes, split_axis=0, concat_axis=0, tiled=True)


def spread(value, axes):
    count = lax.axis_size(axes)
    return exchange(jnp.broadcast_to(value[None], (count,) + value.shape), axes)


def dot(left, right):
    return jnp.dot(left, right, preferred_element_type=jnp.float32)


def dot_nt(left, right):
    return lax.dot_general(left, right, (((1,), (1,)), ((), ())), preferred_element_type=jnp.float32)


def dot_tn(left, right):
    return lax.dot_general(left, right, (((0,), (0,)), ((), ())), preferred_element_type=jnp.float32)


def two_parts(values):
    high = values.astype(jnp.bfloat16)
    low = (values - high.astype(jnp.float32)).astype(jnp.bfloat16)
    return (high, low)


def by_core(mine, other, core):
    return jnp.where(core == 0, jnp.stack([mine, other]), jnp.stack([other, mine]))


def remote(src, dst, send, recv, **where):
    return pltpu.make_async_remote_copy(
        src_ref=src, dst_ref=dst, send_sem=send, recv_sem=recv, device_id=where, device_id_type=MESH
    )


def places():
    return lax.axis_index("fsdp"), lax.axis_index("ctx"), lax.axis_index("tp")


def ring(index, step, count):
    return lax.rem(index + step + count, count)


def greet(nz, nc, line, far=False):
    z, c, t = places()
    barrier = pltpu.get_barrier_semaphore()

    def tell(**where):
        pl.semaphore_signal(barrier, inc=1, device_id=where, device_id_type=MESH)

    if line:
        for step in range(1, nz):
            tell(fsdp=ring(z, step, nz))
        count = nz - 1
    else:
        pl.when(z > 0)(lambda: tell(fsdp=z - 1))
        pl.when(z < nz - 1)(lambda: tell(fsdp=z + 1))
        count = jnp.where(z > 0, 1, 0) + jnp.where(z < nz - 1, 1, 0)
    for step in range(1, nc):
        tell(ctx=ring(c, step, nc))
        if far:
            for hop in range(1, nz):
                tell(fsdp=ring(z, hop, nz), ctx=ring(c, step, nc))
    if far:
        count = count + (nz - 1) * (nc - 1)
    tell(tp=1 - t)
    pl.semaphore_wait(barrier, count + nc)


def line_copies(bufs, send_sem, recv_sem, way, step, shard, target):
    return [
        remote(buf.at[shard], buf.at[shard], send_sem.at[way, step, k], recv_sem.at[way, step, k], fsdp=target)
        for k, buf in enumerate(bufs)
    ]


def line_gather(nz, bufs, send_sem, recv_sem, arrived, begun=None, near=None):
    z = lax.axis_index("fsdp")
    for step in range(nz - 1):

        @pl.when((z < nz - 1) & (z >= step))
        def _():
            for copy in line_copies(bufs, send_sem, recv_sem, 0, step, z - step, z + 1):
                copy.start()

        @pl.when((z > 0) & (z + step < nz))
        def _():
            for copy in line_copies(bufs, send_sem, recv_sem, 1, step, z + step, z - 1):
                copy.start()

        if step == 0 and begun is not None:
            begun()
        if near is not None:
            near(step)

        @pl.when(z - 1 >= step)
        def _():
            for copy in line_copies(bufs, send_sem, recv_sem, 0, step, z - 1 - step, z - 1):
                copy.wait_recv()
            arrived(z - 1 - step)

        @pl.when(z + 1 + step < nz)
        def _():
            for copy in line_copies(bufs, send_sem, recv_sem, 1, step, z + 1 + step, z + 1):
                copy.wait_recv()
            arrived(z + 1 + step)


def line_sent(nz, bufs, send_sem, recv_sem):
    z = lax.axis_index("fsdp")
    for step in range(nz - 1):

        @pl.when((z < nz - 1) & (z >= step))
        def _():
            for copy in line_copies(bufs, send_sem, recv_sem, 0, step, z - step, z + 1):
                copy.wait_send()

        @pl.when((z > 0) & (z + step < nz))
        def _():
            for copy in line_copies(bufs, send_sem, recv_sem, 1, step, z + step, z - 1):
                copy.wait_send()


def pick_rows(pick, slot, source, out):
    lanes = out.shape[-1]
    piece = min(lanes, 512)

    @pl.loop(0, lanes // piece)
    def _(k):
        at = pl.ds(pl.multiple_of(k * piece, piece), piece)
        out[slot, :, at] = jnp.dot(pick[slot], source[slot, :, at], preferred_element_type=jnp.float32).astype(
            jnp.bfloat16
        )


def plane_copy(most, src, dst, send, recv, slot, step, source, target):
    rows = pl.ds(pl.multiple_of(target * most, 16), most)
    return remote(
        src.at[slot, rows], dst.at[source, slot], send.at[slot, step - 1], recv.at[slot, step - 1], ctx=target
    )


def regroup(shard, t, rows, line, two, keep_sem, give_send, give_recv):
    slot = lax.rem(shard, 2)
    band = pl.ds(pl.multiple_of(t * rows, rows), rows)

    def keep():
        pltpu.make_async_copy(line.at[shard], two.at[slot, band], keep_sem.at[slot]).start()

    def give():
        remote(line.at[shard], two.at[slot, band], give_send.at[slot], give_recv.at[slot], tp=1 - t).start()

    pl.when(shard // 2 == t)(keep)
    pl.when(shard // 2 != t)(give)


def selector(nz, src, pair, third, held, pair_out, third_out, in_sem, pair_sem, third_sem):
    c = lax.axis_index("ctx")
    tile = 16
    count = src.shape[2]
    height = held.shape[1]
    bands = src.shape[0] // height

    def take(b):
        slot = lax.rem(b, 2)
        return pltpu.make_async_copy(
            src.at[pl.ds(pl.multiple_of(b * height, height), height)], held.at[slot], in_sem.at[slot]
        )

    def put(b):
        slot = lax.rem(b, 2)
        at = pl.ds(pl.multiple_of(b * height, height), height)
        return (
            pltpu.make_async_copy(pair_out.at[slot], pair.at[:, :, at], pair_sem.at[slot]),
            pltpu.make_async_copy(third_out.at[slot], third.at[:, at], third_sem.at[slot]),
        )

    def pick_band(b):
        slot = lax.rem(b, 2)
        take(b).wait()
        pl.when(b + 1 < bands)(lambda: take(b + 1).start())

        @pl.when(b >= 2)
        def _():
            for copy in put(b - 2):
                copy.wait()

        row = lax.broadcasted_iota(jnp.int32, (nz * tile, tile * count), 0)
        column = lax.broadcasted_iota(jnp.int32, (nz * tile, tile * count), 1)
        hit = column == lax.rem(row, tile) * count + c * nz + row // tile
        hit = jnp.where(hit, 1.0, 0.0).astype(jnp.bfloat16)
        for n in range(height // tile):
            at = pl.ds(n * tile, tile)
            for k in range(3):
                value = held[slot, n * tile : (n + 1) * tile, k].reshape(tile * count, -1)
                value = jnp.dot(hit, value, preferred_element_type=jnp.float32).astype(jnp.bfloat16)
                value = value.reshape(nz, tile, -1)
                if k == 1:
                    third_out[slot, :, at, :] = value
                else:
                    pair_out[slot, :, k // 2, at, :] = value
        for copy in put(b):
            copy.start()

    def close():
        for b in (bands - 2, bands - 1):
            for copy in put(b):
                copy.wait()

    pick_band.close = close
    return take, pick_band, bands


def load_kernel(
    nz, nc, tok, cot, wq, wk, wv, wo, small, rank, w_experts,
    x_all, w_qkv, w_o, small_all, rank_line, rank_seq, pick, cot_in, pair, third,
    cot_line, cot_two, cot_send,
    own_sem, line_send, line_recv, w_send, w_recv, tok_send, tok_recv, pass_send, pass_recv,
    rank_send, rank_recv, keep_sem, give_send, give_recv, cot_s, cot_r, cot_own,
    sel_in, sel_pair, sel_third, sel_s, sel_p, sel_t,
):
    z, c, t = places()
    block = tok.shape[0]
    rows = block // 2
    local = w_qkv.shape[2] // 3
    most = cot_in.shape[2]
    half = pl.ds(pl.multiple_of(t * rows, rows), rows)
    column = pl.ds(pl.multiple_of(c * local, local), local)
    own = [
        pltpu.make_async_copy(cot.at[half], cot_line.at[z], own_sem.at[5]),
        pltpu.make_async_copy(small, small_all.at[z], own_sem.at[4]),
        pltpu.make_async_copy(rank, rank_line.at[z], own_sem.at[7]),
        pltpu.make_async_copy(rank, rank_seq.at[c], own_sem.at[8]),
    ]
    own += [
        pltpu.make_async_copy(w.at[:, column], w_qkv.at[z, :, pl.ds(k * local, local)], own_sem.at[k])
        for k, w in enumerate((wq, wk, wv))
    ]
    own += [
        pltpu.make_async_copy(wo.at[column], w_o.at[z], own_sem.at[3]),
        pltpu.make_async_copy(tok, x_all.at[pl.ds(pl.multiple_of(c * block, block), block)], own_sem.at[6]),
    ]
    for copy in own:
        copy.start()
    take, pick_band, bands = selector(nz, w_experts, pair, third, sel_in, sel_pair, sel_third, sel_s, sel_p, sel_t)
    take(0).start()
    greet(nz, nc, False)

    def band(source, core):
        return x_all.at[pl.ds(pl.multiple_of(source * block + core * rows, rows), rows)]

    def token_copy(step, source, target):
        return remote(tok.at[half], band(source, t), tok_send.at[step], tok_recv.at[step], ctx=target)

    def pass_copy(step, source, core):
        return remote(band(source, core), band(source, core), pass_send.at[step], pass_recv.at[step], tp=1 - t)

    def rank_copy(step, source, target):
        return remote(rank, rank_seq.at[source], rank_send.at[step], rank_recv.at[step], ctx=target)

    for step in range(1, nc):
        token_copy(step - 1, c, ring(c, step, nc)).start()
        rank_copy(step - 1, c, ring(c, step, nc)).start()
    for copy in own:
        copy.wait()

    def arrived(shard):
        regroup(shard, t, rows, cot_line, cot_two, keep_sem, give_send, give_recv)

    arrived(z)
    first = (cot_line, rank_line, small_all)
    line_gather(nz, first, line_send, line_recv, arrived)

    def own_copy(slot):
        return pltpu.make_async_copy(
            cot_send.at[slot, pl.ds(pl.multiple_of(c * most, 16), most)], cot_in.at[c, slot], cot_own.at[slot]
        )

    def send_cotangent():
        number = lax.broadcasted_iota(jnp.int32, (most, block), 0).astype(jnp.float32)
        for slot in range(2):
            for q in range(nc):
                row = rank_line[2 * t + slot, pl.ds(q * nz + z, 1), :]
                hit = jnp.where(number == row, 1.0, 0.0)
                pick[slot, pl.ds(q * most, most), :] = hit.astype(jnp.bfloat16)
        for slot in range(2):
            wait_two(slot, t, rows, cot_line, cot_two, keep_sem, give_recv)
            pick_rows(pick, slot, cot_two, cot_send)
            for step in range(1, nc):
                plane_copy(most, cot_send, cot_in, cot_s, cot_r, slot, step, c, ring(c, step, nc)).start()
            own_copy(slot).start()

    def ignore(shard):
        pass

    def select_some(step):
        pl.loop(bands * (0, 1, 3)[step] // 4, bands * (1, 3, 4)[step] // 4)(pick_band)

    line_gather(nz, (w_qkv, w_o), w_send, w_recv, ignore, send_cotangent, select_some)
    pick_band.close()
    for step in range(1, nc):
        source = ring(c, -step, nc)
        token_copy(step - 1, source, source).wait_recv()
        pass_copy(step - 1, source, t).start()
        rank_copy(step - 1, source, source).wait_recv()
    for step in range(1, nc):
        source = ring(c, -step, nc)
        pass_copy(step - 1, source, 1 - t).wait_recv()
        pass_copy(step - 1, source, t).wait_send()
        token_copy(step - 1, c, source).wait_send()
        rank_copy(step - 1, c, source).wait_send()
        for slot in range(2):
            copy = plane_copy(most, cot_send, cot_in, cot_s, cot_r, slot, step, source, source)
            copy.wait_recv()
            copy.wait_send()
    line_sent(nz, first, line_send, line_recv)
    line_sent(nz, (w_qkv, w_o), w_send, w_recv)
    for slot in range(2):
        own_copy(slot).wait()
        wait_given(slot, t, rows, cot_line, cot_two, give_send, give_recv)


def wait_given(slot, t, rows, line, two, give_send, give_recv):
    band = pl.ds(pl.multiple_of(t * rows, rows), rows)
    remote(line.at[0], two.at[slot, band], give_send.at[slot], give_recv.at[slot], tp=1 - t).wait_send()


def wait_two(slot, t, rows, line, two, keep_sem, give_recv):
    band = pl.ds(pl.multiple_of(t * rows, rows), rows)
    other = pl.ds(pl.multiple_of((1 - t) * rows, rows), rows)
    pltpu.make_async_copy(line.at[0], two.at[slot, band], keep_sem.at[slot]).wait()
    remote(line.at[0], two.at[slot, other], give_recv.at[slot], give_recv.at[slot], tp=1 - t).wait_recv()


def load(tok, cot, wq, wk, wv, wo, small, rank, w_experts, most):
    nz, nc = lax.axis_size("fsdp"), lax.axis_size("ctx")
    block, width = tok.shape
    deep, local = wq.shape[0], wq.shape[1] // nc
    rows = block // 2
    count, ffn = w_experts.shape[2:]
    dma = pltpu.SemaphoreType.DMA
    bf16, f32 = jnp.bfloat16, jnp.float32
    shapes = [
        ((nc * block, width), bf16),
        ((nz, deep, 3 * local), bf16),
        ((nz, local, wo.shape[1]), bf16),
        ((nz,) + small.shape, bf16),
        ((nz,) + rank.shape, f32),
        ((nc,) + rank.shape, f32),
        ((2, nc * most, block), bf16),
        ((nc, 2, most, width), bf16),
        ((nz, 2, deep, ffn), bf16),
        ((nz, deep, ffn), bf16),
    ]
    hbm = pl.BlockSpec(memory_space=pl.ANY)
    height = 32
    return pl.pallas_call(
        functools.partial(load_kernel, nz, nc),
        out_shape=[jax.ShapeDtypeStruct(shape, kind) for shape, kind in shapes],
        in_specs=[hbm] * 9,
        out_specs=[pl.BlockSpec(memory_space=pltpu.VMEM)] * 7 + [hbm] * 3,
        scratch_shapes=[
            pltpu.VMEM((nz, rows, width), bf16),
            pltpu.VMEM((2, block, width), bf16),
            pltpu.VMEM((2, nc * most, width), bf16),
            dma((9,)),
            dma((2, nz - 1, 3)), dma((2, nz - 1, 3)), dma((2, nz - 1, 2)), dma((2, nz - 1, 2)),
            dma((nc - 1,)), dma((nc - 1,)), dma((nc - 1,)), dma((nc - 1,)), dma((nc - 1,)), dma((nc - 1,)),
            dma((2,)), dma((2,)), dma((2,)), dma((2, nc - 1)), dma((2, nc - 1)), dma((2,)),
            pltpu.VMEM((2, height, 3, count, ffn), bf16),
            pltpu.VMEM((2, nz, 2, height, ffn), bf16),
            pltpu.VMEM((2, nz, height, ffn), bf16),
            dma((2,)), dma((2,)), dma((2,)),
        ],
        compiler_params=pltpu.CompilerParams(
            collective_id=0, has_side_effects=True, vmem_limit_bytes=48 * 2**20
        ),
    )(tok, cot, wq, wk, wv, wo, small, rank, w_experts)


def dispatch_kernel(
    nz, nc, part, tok, gain, router, kept, pick, third,
    residual, normed, probs, x_in, g_in, third_got,
    sib, rs_send, rs_recv, n_line, g_line, n_two, g_two, x_send, g_send,
    sib_s, sib_r, rs_s, rs_r, line_send, line_recv, keep_sem, give_send, give_recv,
    gkeep_sem, ggive_send, ggive_recv, x_s, x_r, g_s, g_r, own_sem,
    third_s, third_r, third_own,
):
    z, c, t = places()
    f32, bf16 = jnp.float32, jnp.bfloat16
    rows, width = residual.shape
    most = x_in.shape[2]
    greet(nz, nc, True)
    keep_third = pltpu.make_async_copy(third.at[z], third_got.at[z], third_own)
    keep_third.start()

    def third_copy(step, source, target):
        return remote(third.at[target], third_got.at[source], third_s.at[step], third_r.at[step], fsdp=target)

    def sib_copy(q):
        return remote(part.at[q, 1 - t], sib.at[q], sib_s.at[q], sib_r.at[q], tp=1 - t)

    def rs_copy(step, source, target):
        return remote(rs_send.at[step], rs_recv.at[step], rs_s.at[step], rs_r.at[step], ctx=target)

    for step in range(1, nc + 1):
        sib_copy(ring(c, step, nc)).start()
    chunk = 16
    for step in range(1, nc):
        q = ring(c, step, nc)
        sib_copy(q).wait_recv()

        @pl.loop(0, rows // chunk)
        def _(k):
            at = pl.ds(pl.multiple_of(k * chunk, chunk), chunk)
            rs_send[step - 1, at, :] = (part[q, t, at, :].astype(f32) + sib[q, at, :].astype(f32)).astype(bf16)

        rs_copy(step - 1, c, q).start()

    def own_copy(slot, src, dst, k):
        return pltpu.make_async_copy(
            src.at[slot, pl.ds(pl.multiple_of(c * most, 16), most)], dst.at[c, slot], own_sem.at[k, slot]
        )

    sib_copy(c).wait_recv()
    for step in range(1, nc):
        rs_copy(step - 1, c, c).wait_recv()

    @pl.loop(0, rows // chunk)
    def _(k):
        at = pl.ds(pl.multiple_of(k * chunk, chunk), chunk)
        start = pl.ds(pl.multiple_of(t * rows + k * chunk, chunk), chunk)
        total = part[c, t, at, :].astype(f32) + sib[c, at, :].astype(f32)
        for step in range(nc - 1):
            total = total + rs_recv[step, at, :].astype(f32)
        total = total + tok[start, :].astype(f32)
        residual[at, :] = total
        inv = lax.rsqrt(jnp.mean(total * total, -1, keepdims=True) + EPS)
        row = (total * inv * gain[...]).astype(bf16)
        normed[at, :] = row
        n_line[z, at, :] = row

    logits = lax.dot_general(
        normed[...], router[...], (((1,), (1,)), ((), ())), preferred_element_type=f32
    )
    lane = lax.broadcasted_iota(jnp.int32, logits.shape, 1)
    logits = jnp.where(lane < E, logits, -jnp.inf)
    top = jnp.max(logits, -1, keepdims=True)
    raised = jnp.exp(logits - top)
    prob = raised / jnp.sum(raised, -1, keepdims=True)
    probs[...] = prob
    gates = prob * kept[...]
    high = gates.astype(bf16)
    g_line[z, :, pl.ds(0, 128)] = high
    g_line[z, :, pl.ds(128, 128)] = (gates - high.astype(f32)).astype(bf16)

    def arrived(shard):
        regroup(shard, t, rows, n_line, n_two, keep_sem, give_send, give_recv)
        regroup(shard, t, rows, g_line, g_two, gkeep_sem, ggive_send, ggive_recv)

    arrived(z)
    sent = ((x_send, x_in, x_s, x_r), (g_send, g_in, g_s, g_r))

    def near(distance):
        above, below = z + distance, z - distance
        is_above = (above < nz) & (above // 2 == t)
        is_below = (below >= 0) & (below // 2 == t)
        slot = lax.rem(jnp.where(is_above, above, below + 2), 2)

        @pl.when(is_above | is_below)
        def _():
            wait_two(slot, t, rows, n_line, n_two, keep_sem, give_recv)
            wait_two(slot, t, rows, g_line, g_two, gkeep_sem, ggive_recv)
            pick_rows(pick, slot, n_two, x_send)
            pick_rows(pick, slot, g_two, g_send)
            for k, (src, dst, s, r) in enumerate(sent):
                for step in range(1, nc):
                    plane_copy(most, src, dst, s, r, slot, step, c, ring(c, step, nc)).start()
                own_copy(slot, src, dst, k).start()

    line_gather(nz, (n_line, g_line), line_send, line_recv, arrived, None, near)
    near(nz - 1)
    for step in range(1, nz):
        third_copy(step - 1, z, ring(z, step, nz)).start()
    line_sent(nz, (n_line, g_line), line_send, line_recv)
    for slot in range(2):
        wait_given(slot, t, rows, n_line, n_two, give_send, give_recv)
        wait_given(slot, t, rows, g_line, g_two, ggive_send, ggive_recv)
        for k, (src, dst, s, r) in enumerate(sent):
            own_copy(slot, src, dst, k).wait()
            for step in range(1, nc):
                source = ring(c, -step, nc)
                copy = plane_copy(most, src, dst, s, r, slot, step, source, source)
                copy.wait_recv()
                copy.wait_send()
    for step in range(1, nc):
        rs_copy(step - 1, c, c).wait_send()
    for step in range(nc):
        sib_copy(step).wait_send()
    for step in range(1, nz):
        source = ring(z, -step, nz)
        third_copy(step - 1, source, source).wait_recv()
        third_copy(step - 1, source, source).wait_send()
    keep_third.wait()


def dispatch(part, tok, gain, router, kept, pick, third):
    nz, nc = lax.axis_size("fsdp"), lax.axis_size("ctx")
    rows, width = part.shape[2], part.shape[3]
    block = rows * 2
    most = pick.shape[1] // nc
    dma = pltpu.SemaphoreType.DMA
    bf16, f32 = jnp.bfloat16, jnp.float32
    vmem = pl.BlockSpec(memory_space=pltpu.VMEM)
    hbm = pl.BlockSpec(memory_space=pl.ANY)
    return pl.pallas_call(
        functools.partial(dispatch_kernel, nz, nc),
        out_shape=[
            jax.ShapeDtypeStruct((rows, width), f32),
            jax.ShapeDtypeStruct((rows, width), bf16),
            jax.ShapeDtypeStruct((rows, 128), f32),
            jax.ShapeDtypeStruct((nc, 2, most, width), bf16),
            jax.ShapeDtypeStruct((nc, 2, most, 256), bf16),
            jax.ShapeDtypeStruct(third.shape, bf16),
        ],
        in_specs=[vmem] * 6 + [hbm],
        out_specs=[vmem] * 3 + [hbm] * 3,
        scratch_shapes=[
            pltpu.VMEM((nc, rows, width), bf16),
            pltpu.VMEM((nc - 1, rows, width), bf16),
            pltpu.VMEM((nc - 1, rows, width), bf16),
            pltpu.VMEM((nz, rows, width), bf16),
            pltpu.VMEM((nz, rows, 256), bf16),
            pltpu.VMEM((2, block, width), bf16),
            pltpu.VMEM((2, block, 256), bf16),
            pltpu.VMEM((2, nc * most, width), bf16),
            pltpu.VMEM((2, nc * most, 256), bf16),
            dma((nc,)), dma((nc,)), dma((nc - 1,)), dma((nc - 1,)),
            dma((2, nz - 1, 2)), dma((2, nz - 1, 2)),
            dma((2,)), dma((2,)), dma((2,)), dma((2,)), dma((2,)), dma((2,)),
            dma((2, nc - 1)), dma((2, nc - 1)), dma((2, nc - 1)), dma((2, nc - 1)),
            dma((2, 2)),
            dma((nz - 1,)), dma((nz - 1,)), dma,
        ],
        compiler_params=pltpu.CompilerParams(
            collective_id=1, has_side_effects=True, vmem_limit_bytes=56 * 2**20
        ),
    )(part, tok, gain, router, kept, pick, third)


def experts_kernel(
    nz, nc, x_hbm, cot_hbm, gates, pair_hbm, third_hbm, y, r, pair_out, hid, gg, gu,
    x, cot, w, weight, pair, gate, up, out_grad,
    sem, swap_s, swap_r,
):
    z, c, t = places()
    f32, bf16 = jnp.float32, jnp.bfloat16
    width, tall = x.shape[1], x.shape[0]
    deep, ffn = w.shape[3], w.shape[4]
    span = 256
    chunk = 48
    copies = [
        pltpu.make_async_copy(cot_hbm, cot, sem.at[0]),
        pltpu.make_async_copy(pair_hbm, w.at[0, :, pl.ds(0, 2)], sem.at[1]),
        pltpu.make_async_copy(x_hbm, x, sem.at[2]),
        pltpu.make_async_copy(third_hbm, w.at[0, :, 2], sem.at[3]),
    ]
    for copy in copies:
        copy.start()
    barrier = pltpu.get_barrier_semaphore()
    pl.semaphore_signal(barrier, inc=1, device_id=dict(tp=1 - t), device_id_type=MESH)
    pl.semaphore_wait(barrier, 1)
    swaps = [
        remote(pair_hbm, w.at[1, :, pl.ds(0, 2)], swap_s.at[0], swap_r.at[0], tp=1 - t),
        remote(third_hbm, w.at[1, :, 2], swap_s.at[1], swap_r.at[1], tp=1 - t),
    ]
    for copy in swaps:
        copy.start()
    pair[...] = jnp.zeros_like(pair)
    lane = lax.broadcasted_iota(jnp.int32, (chunk, 256), 1)
    mine = c * nz + z

    @pl.loop(0, tall // chunk)
    def _(m):
        rows = pl.ds(pl.multiple_of(m * chunk, chunk), chunk)
        value = gates[rows, :].astype(f32)
        value = jnp.where((lane == mine) | (lane == mine + 128), value, 0.0)
        weight[rows, :] = jnp.sum(value, 1, keepdims=True)

    for copy in copies:
        copy.wait()
    per = ffn // span

    def forward(n):
        half, at = n // per, pl.ds(pl.multiple_of(lax.rem(n, per) * span, span), span)
        full = pl.ds(pl.multiple_of(n * span, span), span)

        def times(rows, k):
            return jnp.dot(rows[...], w[half, :, k, :, at].reshape(width, span), preferred_element_type=f32)

        out_grad[...] = times(cot, 1)
        gate[...] = times(x, 0)
        up[...] = times(x, 2)

        @pl.loop(0, tall // chunk)
        def _(m):
            rows = pl.ds(pl.multiple_of(m * chunk, chunk), chunk)
            g, u, o, k = gate[rows, :], up[rows, :], out_grad[rows, :], weight[rows, :]
            sig = 1.0 / (1.0 + jnp.exp(-g))
            silu = g * sig
            hidden = silu * u
            pair[rows, :] += jnp.sum(hidden.astype(bf16).astype(f32) * o, 1, keepdims=True)
            hid[rows, full] = (k * hidden).astype(bf16)
            o = k * o
            gg[rows, full] = (o * u * sig * (1.0 + g * (1.0 - sig))).astype(bf16)
            gu[rows, full] = (o * silu).astype(bf16)

    pl.loop(0, per)(forward)
    for copy in swaps:
        copy.wait_recv()
    pl.loop(per, 2 * per)(forward)

    @pl.loop(0, tall // chunk)
    def _(m):
        rows = pl.ds(pl.multiple_of(m * chunk, chunk), chunk)
        value = pair[rows, :]
        high = value.astype(bf16).astype(f32)
        out = jnp.where(lane == mine, high, jnp.where(lane == mine + 128, value - high, 0.0))
        pair_out[rows, :] = out.astype(bf16)

    per_deep = deep // span

    @pl.loop(0, width // span)
    def _(n):
        zone, at = n // per_deep, pl.ds(pl.multiple_of(lax.rem(n, per_deep) * span, span), span)
        full = pl.ds(pl.multiple_of(n * span, span), span)

        def back(rows, k):
            total = 0.0
            for half in range(2):
                total = total + lax.dot_general(
                    rows[:, pl.ds(half * ffn, ffn)], w[half, zone, k, at, :], (((1,), (1,)), ((), ())),
                    preferred_element_type=f32,
                )
            return total

        y[:, full] = back(hid, 1).astype(bf16)
        r[:, full] = (back(gg, 0) + back(gu, 2)).astype(bf16)

    for copy in swaps:
        copy.wait_send()


def experts(x, cot, gates, pair, third):
    bf16, f32 = jnp.bfloat16, jnp.float32
    nz, nc = lax.axis_size("fsdp"), lax.axis_size("ctx")
    tall, width = x.shape
    deep, ffn = third.shape[1:]
    vmem = pl.BlockSpec(memory_space=pltpu.VMEM)
    hbm = pl.BlockSpec(memory_space=pl.ANY)
    inner = jax.ShapeDtypeStruct((tall, 2 * ffn), bf16)
    dma = pltpu.SemaphoreType.DMA
    return pl.pallas_call(
        functools.partial(experts_kernel, nz, nc),
        out_shape=[
            jax.ShapeDtypeStruct((tall, width), bf16),
            jax.ShapeDtypeStruct((tall, width), bf16),
            jax.ShapeDtypeStruct((tall, 256), bf16),
            inner,
            inner,
            inner,
        ],
        in_specs=[hbm, hbm, vmem, hbm, hbm],
        out_specs=[vmem] * 6,
        scratch_shapes=[
            pltpu.VMEM((tall, width), bf16),
            pltpu.VMEM((tall, width), bf16),
            pltpu.VMEM((2, nz, 3, deep, ffn), bf16),
            pltpu.VMEM((tall, 1), f32),
            pltpu.VMEM((tall, 1), f32),
            pltpu.VMEM((tall, 256), f32),
            pltpu.VMEM((tall, 256), f32),
            pltpu.VMEM((tall, 256), f32),
            dma((4,)), dma((2,)), dma((2,)),
        ],
        compiler_params=pltpu.CompilerParams(
            collective_id=4, has_side_effects=True, vmem_limit_bytes=60 * 2**20
        ),
    )(x, cot, gates, pair, third)


def place_kernel(nz, nc, gate, rest, out):
    tile = gate.shape[2]
    count = nz * nc
    row = lax.broadcasted_iota(jnp.int32, (tile * count, tile * count), 0)
    column = lax.broadcasted_iota(jnp.int32, (tile * count, tile * count), 1)
    expert = lax.rem(row, count)
    hit = column == (lax.rem(expert, nz) * nc + expert // nz) * tile + row // count
    hit = jnp.where(hit, 1.0, 0.0).astype(jnp.bfloat16)
    for k in range(3):
        early = gate.shape[1]
        value = (gate[:, k] if k < early else rest[:, k - early]).reshape(count * tile, -1)
        value = jnp.dot(hit, value, preferred_element_type=jnp.float32)
        out[:, k] = value.reshape(tile, count, -1)


def lay_out(gate, rest, nz, nc):
    count, _, strip, ffn = gate.shape
    tile = 16
    return pl.pallas_call(
        functools.partial(place_kernel, nz, nc),
        grid=(strip // tile,),
        out_shape=jax.ShapeDtypeStruct((strip, 3, count, ffn), jnp.float32),
        in_specs=[
            pl.BlockSpec((count, src.shape[1], tile, ffn), lambda i: (0, 0, i, 0))
            for src in (gate, rest)
        ],
        out_specs=pl.BlockSpec((tile, 3, count, ffn), lambda i: (i, 0, 0, 0)),
        compiler_params=pltpu.CompilerParams(vmem_limit_bytes=40 * 2**20),
    )(gate, rest)


def collector(nz, nc, pick_t, items, sems):
    z, c, t = places()
    to_s, to_r, own_sem, sib_s, sib_r, line_s, line_r, keep_sem = sems
    rows = items[0][2].shape[1]
    mine_at = pl.ds(pl.multiple_of(t * rows, rows), rows)
    give_at = pl.ds(pl.multiple_of((1 - t) * rows, rows), rows)
    count = len(items)

    def lanes(turn, k):
        wide = items[k][2].shape[-1] // 2
        return pl.ds(turn * wide, wide)

    def to_copy(turn, k, step, source, target):
        src, got = items[k][:2]
        at = lanes(turn, k)
        return remote(
            src.at[target, :, :, at], got.at[source, :, :, at], to_s.at[k, turn, step - 1], to_r.at[k, turn, step - 1],
            ctx=target,
        )

    def own_copy(turn, k):
        src, got = items[k][:2]
        at = lanes(turn, k)
        return pltpu.make_async_copy(src.at[c, :, :, at], got.at[c, :, :, at], own_sem.at[k, turn])

    def sib_copy(turn, k):
        give, sib = items[k][3:5]
        at = lanes(turn, k)
        return remote(give.at[:, :, at], sib.at[:, :, at], sib_s.at[k, turn], sib_r.at[k, turn], tp=1 - t)

    def line_copy(turn, slot, k, half, source, target):
        src = items[k][2 if half == 0 else 4]
        at = lanes(turn, k)
        return remote(
            src.at[slot, :, at], items[k][5].at[source, :, at],
            line_s.at[k, turn, 2 * half + slot], line_r.at[k, turn, source], fsdp=target,
        )

    def keep_copy(turn, slot, k, half):
        src = items[k][2 if half == 0 else 4]
        at = lanes(turn, k)
        return pltpu.make_async_copy(src.at[slot, :, at], items[k][5].at[z, :, at], keep_sem.at[k, turn])

    def goal(slot, half):
        return 2 * (t if half == 0 else 1 - t) + slot

    def forward(turn, k, half):
        for slot in range(2):
            target = goal(slot, half)
            pl.when(target != z)(lambda: line_copy(turn, slot, k, half, z, target).start())
            pl.when(target == z)(lambda: keep_copy(turn, slot, k, half).start())

    def begin(turn):
        for k in range(count):
            for step in range(1, nc):
                to_copy(turn, k, step, c, ring(c, step, nc)).start()
            own_copy(turn, k).start()

    def scatter(turn, slot, k):
        got, mine, give = items[k][1:4]
        wide = mine.shape[-1] // 2
        span = min(wide, 512)
        tall = got.shape[0] * got.shape[2]

        @pl.loop(0, wide // span)
        def _(n):
            at = pl.ds(pl.multiple_of(turn * wide + n * span, span), span)
            pairs = got[:, slot, :, at].reshape(tall, span)
            for picks, out in ((mine_at, mine), (give_at, give)):
                out[slot, :, at] = jnp.dot(
                    pick_t[slot, picks, :], pairs, preferred_element_type=jnp.float32
                ).astype(jnp.bfloat16)

    def process(turn):
        for k in range(count):
            own_copy(turn, k).wait()
            for step in range(1, nc):
                source = ring(c, -step, nc)
                to_copy(turn, k, step, source, c).wait_recv()
            for slot in range(2):
                scatter(turn, slot, k)
            sib_copy(turn, k).start()
            forward(turn, k, 0)
        for k in range(count):
            sib_copy(turn, k).wait_recv()
            forward(turn, k, 1)

    def join():
        for turn in range(2):
            for k in range(count):
                keep_copy(turn, 0, k, 0).wait()
                for step in range(1, nz):
                    line_copy(turn, 0, k, 0, ring(z, -step, nz), z).wait_recv()

    def done():
        for turn in range(2):
            for k in range(count):
                for step in range(1, nc):
                    to_copy(turn, k, step, c, ring(c, step, nc)).wait_send()
                sib_copy(turn, k).wait_send()
                for half in range(2):
                    for slot in range(2):
                        pl.when(goal(slot, half) != z)(
                            lambda: line_copy(turn, slot, k, half, z, goal(slot, half)).wait_send()
                        )

    return begin, process, join, done


def collector_scratch(nz, nc, most, rows, widths):
    dma = pltpu.SemaphoreType.DMA
    bf16 = jnp.bfloat16
    count = len(widths)
    bufs = []
    for w in widths:
        bufs += [pltpu.VMEM((nc, 2, most, w), bf16)]
        bufs += [pltpu.VMEM((2, rows, w), bf16)] * 3
        bufs += [pltpu.VMEM((nz, rows, w), bf16)]
    sems = [
        dma((count, 2, nc - 1)), dma((count, 2, nc - 1)), dma((count, 2)), dma((count, 2)), dma((count, 2)),
        dma((count, 2, 4)), dma((count, 2, nz)), dma((count, 2)),
    ]
    return bufs, sems


def return_kernel(
    nz, nc, r, g, x_hbm, cot_hbm, hid_hbm, gg_hbm, gu_hbm, pick_t, residual, probs, kept, router, gain, cot,
    logits_grad, gain_grad, residual_grad, attn_grad, early_got, own_grad, other_grad,
    x, cot_rows, hid, gg, gu, stage, early, early_sib,
    load_sem, keep_sem, give_sem, got_sem, first_s, first_r, *scratch,
):
    z, c, t = places()
    f32, bf16 = jnp.float32, jnp.bfloat16
    rows, width = residual.shape
    r_line, g_line = scratch[4], scratch[9]
    row_s, row_r, pass_s, pass_r, early_s, early_r, early_own = scratch[18:]
    items = ((r,) + scratch[:5], (g,) + scratch[5:10])
    begin, process, join, done = collector(nz, nc, pick_t, items, scratch[10:18])
    here = z * nc + c
    keep_early = pltpu.make_async_copy(early.at[here], early_got.at[here], early_own)
    loads = [
        pltpu.make_async_copy(src, dst, load_sem.at[k])
        for k, (src, dst) in enumerate(
            ((x_hbm, x), (gg_hbm, gg), (gu_hbm, gu), (cot_hbm, cot_rows), (hid_hbm, hid))
        )
    ]
    for copy in loads:
        copy.start()
    greet(nz, nc, True, True)
    chips = nz * nc
    steps = [(i, j) for i in range(nz) for j in range(nc) if i or j]

    def early_copy(n, source, target, fsdp, ctx):
        return remote(early.at[target], early_got.at[source], early_s.at[n], early_r.at[n], fsdp=fsdp, ctx=ctx)

    begin(0)
    begin(1)
    for copy in loads:
        copy.wait()

    span = 256
    ffn = stage.shape[5]
    strip = stage.shape[4]
    per = span // strip
    bands = width // span

    def flush(n):
        slot = lax.rem(n, 2)
        at = pl.ds(pl.multiple_of(n * per, per), per)
        return (
            pltpu.make_async_copy(stage.at[slot, 0, :, pl.ds(1, 2)], own_grad.at[at], keep_sem.at[slot]),
            remote(stage.at[slot, 1, :, pl.ds(1, 2)], other_grad.at[at], give_sem.at[slot], got_sem, tp=1 - t),
            remote(stage.at[slot, 1, :, 0], early_sib.at[at], first_s.at[slot], first_r, tp=1 - t),
        )

    def flushed(n):
        keep, give, first = flush(n)
        keep.wait()
        give.wait_send()
        first.wait_send()

    @pl.loop(0, bands)
    def _(n):
        full = pl.ds(pl.multiple_of(n * span, span), span)
        slot = lax.rem(n, 2)
        pl.when(n >= 2)(lambda: flushed(n - 2))
        for k, (rows_in, grads) in enumerate(((x, gg), (x, gu), (cot_rows, hid))):
            value = lax.dot_general(
                rows_in[:, full], grads[...], (((0,), (0,)), ((), ())), preferred_element_type=f32
            ).astype(bf16)
            for i in range(per):
                piece = value[i * strip : (i + 1) * strip]
                if k == 0:
                    early[n * per + i] = piece[:, :ffn]
                else:
                    stage[slot, 0, i, k] = piece[:, :ffn]
                stage[slot, 1, i, k] = piece[:, ffn:]
        for copy in flush(n):
            copy.start()

    flushed(bands - 2)
    flushed(bands - 1)
    remote(early_sib, early_sib, first_r, first_r, tp=1 - t).wait_recv()

    @pl.loop(0, chips)
    def _(n):
        early[n] = (early[n].astype(f32) + early_sib[n].astype(f32)).astype(bf16)

    keep_early.start()
    for n, (i, j) in enumerate(steps):
        zz, cc = ring(z, i, nz), ring(c, j, nc)
        early_copy(n, here, zz * nc + cc, zz, cc).start()
    for turn in range(2):
        process(turn)
    join()
    pairs = jnp.zeros((rows, 128), f32)
    for source in range(nz):
        pairs = pairs + g_line[source, :, 0:128].astype(f32) + g_line[source, :, 128:256].astype(f32)
    pairs = pairs * kept[...]
    prob = probs[...]
    grad_logits = (prob * (pairs - jnp.sum(prob * pairs, -1, keepdims=True))).astype(bf16)
    logits_grad[...] = grad_logits
    gain_grad[...] = jnp.zeros_like(gain_grad)
    chunk = 16

    @pl.loop(0, rows // chunk)
    def _(k):
        at = pl.ds(pl.multiple_of(k * chunk, chunk), chunk)
        full = pl.ds(pl.multiple_of(t * rows + k * chunk, chunk), chunk)
        res = residual[at, :]
        grad = r_line[0, at, :].astype(f32)
        for source in range(1, nz):
            grad = grad + r_line[source, at, :].astype(f32)
        grad = grad + jnp.dot(logits_grad[at, :], router[...], preferred_element_type=f32)
        inv = lax.rsqrt(jnp.mean(res * res, -1, keepdims=True) + EPS)
        gain_grad[...] += jnp.sum((grad * res * inv).reshape(chunk // 8, 8, width), 0)
        weighted = grad * gain[...]
        inner = jnp.sum(weighted * res, -1, keepdims=True)
        out = cot[full, :].astype(f32) + inv * weighted - res * (inv * inv * inv) * inner / width
        residual_grad[at, :] = out
        attn_grad[c, t, at, :] = out.astype(bf16)

    def row_copy(step, source, target):
        return remote(attn_grad.at[source, t], attn_grad.at[source, t], row_s.at[step], row_r.at[step], ctx=target)

    def pass_copy(step, source, core):
        return remote(attn_grad.at[source, core], attn_grad.at[source, core], pass_s.at[step], pass_r.at[step], tp=1 - t)

    for step in range(1, nc):
        row_copy(step, c, ring(c, step, nc)).start()
    pass_copy(0, c, t).start()
    for step in range(1, nc):
        source = ring(c, -step, nc)
        row_copy(step, source, source).wait_recv()
        pass_copy(step, source, t).start()
    for step in range(nc):
        source = ring(c, -step, nc)
        pass_copy(step, source, 1 - t).wait_recv()
        pass_copy(step, source, t).wait_send()
        if step:
            row_copy(step, c, source).wait_send()
    done()
    for n, (i, j) in enumerate(steps):
        zz, cc = ring(z, -i, nz), ring(c, -j, nc)
        copy = early_copy(n, zz * nc + cc, zz * nc + cc, zz, cc)
        copy.wait_recv()
        copy.wait_send()
    keep_early.wait()
    remote(other_grad, other_grad, got_sem, got_sem, tp=1 - t).wait_recv()


def give_back(r, g, x, cot_rows, hid, gg, gu, pick_t, residual, probs, kept, router, gain, cot):
    nz, nc = lax.axis_size("fsdp"), lax.axis_size("ctx")
    rows, width = residual.shape
    dma = pltpu.SemaphoreType.DMA
    bf16, f32 = jnp.bfloat16, jnp.float32
    vmem = pl.BlockSpec(memory_space=pltpu.VMEM)
    hbm = pl.BlockSpec(memory_space=pl.ANY)
    bufs, sems = collector_scratch(nz, nc, r.shape[2], rows, (width, 256))
    chips = nz * nc
    strip, ffn = width // chips, hid.shape[1] // 2
    tall = x.shape[0]
    return pl.pallas_call(
        functools.partial(return_kernel, nz, nc),
        out_shape=[
            jax.ShapeDtypeStruct((rows, 128), bf16),
            jax.ShapeDtypeStruct((8, width), f32),
            jax.ShapeDtypeStruct((rows, width), f32),
            jax.ShapeDtypeStruct((nc, 2, rows, width), bf16),
            jax.ShapeDtypeStruct((chips, strip, ffn), bf16),
            jax.ShapeDtypeStruct((chips, 2, strip, ffn), bf16),
            jax.ShapeDtypeStruct((chips, 2, strip, ffn), bf16),
        ],
        in_specs=[hbm] * 7 + [vmem] * 7,
        out_specs=[vmem] * 4 + [hbm] * 3,
        scratch_shapes=[
            pltpu.VMEM((tall, width), bf16),
            pltpu.VMEM((tall, width), bf16),
            pltpu.VMEM((tall, 2 * ffn), bf16),
            pltpu.VMEM((tall, 2 * ffn), bf16),
            pltpu.VMEM((tall, 2 * ffn), bf16),
            pltpu.VMEM((2, 2, 256 // strip, 3, strip, ffn), bf16),
            pltpu.VMEM((chips, strip, ffn), bf16),
            pltpu.VMEM((chips, strip, ffn), bf16),
            dma((5,)), dma((2,)), dma((2,)), dma, dma((2,)), dma,
        ]
        + bufs
        + sems
        + [dma((nc,)), dma((nc,)), dma((nc,)), dma((nc,))]
        + [dma((nz * nc - 1,)), dma((nz * nc - 1,)), dma],
        compiler_params=pltpu.CompilerParams(
            collective_id=2, has_side_effects=True, vmem_limit_bytes=60 * 2**20
        ),
    )(r, g, x, cot_rows, hid, gg, gu, pick_t, residual, probs, kept, router, gain, cot)


def final_kernel(
    nz, nc, part, tok, gain, residual_grad, dw, dwo, small, y, pick_t, residual,
    tokens_grad, dw_out, dwo_out, small_out, layer,
    sib, rs_send, rs_recv, tok_grad, gain_acc, dw_up, dw_down, dwo_up, dwo_down, dw_to, dwo_to,
    dw_next, dwo_next, small_line, small_plane, small_sib, small_a, small_b,
    sib_s, sib_r, rs_s, rs_r, line_s, line_r, to_s, to_r, tg_s, tg_r, sm_s, sm_r, sp_s, sp_r, ss_s, ss_r,
    layer_send, lay_s, lay_r, *scratch,
):
    z, c, t = places()
    f32, bf16 = jnp.float32, jnp.bfloat16
    rows, width = residual_grad.shape
    piece = width // 2
    chunk = 16
    y_line = scratch[4]
    begin, process, join, done = collector(nz, nc, pick_t, ((y,) + scratch[:5],), scratch[5:])
    greet(nz, nc, True)

    bufs = ((dw, dw_up, dw_down), (dwo, dwo_up, dwo_down))
    outs = (dw_next, dwo_next)

    def hop(way, step, k, target):
        src = outs[k].at[way, step]
        return remote(src, bufs[k][1 + way].at[step], line_s.at[way, step, k], line_r.at[way, step, k], fsdp=target)

    def add_to(k, way, step, shard, joined):
        own, out = bufs[k][0], outs[k]
        got = bufs[k][1 + way]
        height = own.shape[2]
        tile = 32

        @pl.loop(0, nc * (height // tile))
        def _(n):
            q, at = n // (height // tile), pl.ds(pl.multiple_of(lax.rem(n, height // tile) * tile, tile), tile)
            value = own[shard, q, at, :]
            if joined:
                value = (value.astype(f32) + got[step, q, at, :].astype(f32)).astype(bf16)
            out[way, step, q, at, :] = value

    def line_one(step, way):
        shard = nz - 1 - step if way == 0 else step
        ahead = z + 1 if way == 0 else z - 1
        behind = z - 1 if way == 0 else z + 1
        first = z == 0 if way == 0 else z == nz - 1
        sends = shard > z if way == 0 else shard < z
        gets = (z > 0) & (shard >= z) if way == 0 else (z < nz - 1) & (shard <= z)

        @pl.when(gets)
        def _():
            for k in range(2):
                hop(way, step, k, behind).wait_recv()

        @pl.when(sends & jnp.logical_not(first))
        def _():
            for k in range(2):
                add_to(k, way, step, shard, True)
                hop(way, step, k, ahead).start()

    def line_step(step):
        @pl.when(2 * z < nz)
        def _():
            line_one(step, 0)
            line_one(step, 1)

        @pl.when(2 * z >= nz)
        def _():
            line_one(step, 1)
            line_one(step, 0)

    def line_begin():
        for way in range(2):
            first = z == 0 if way == 0 else z == nz - 1

            @pl.when(first)
            def _():
                for step in range(nz - 1):
                    shard = nz - 1 - step if way == 0 else step
                    for k in range(2):
                        add_to(k, way, step, shard, False)
                        hop(way, step, k, z + 1 if way == 0 else z - 1).start()

    def sib_copy(q):
        return remote(part.at[q, 1 - t], sib.at[q], sib_s.at[q], sib_r.at[q], tp=1 - t)

    def rs_copy(step, target):
        return remote(rs_send.at[step], rs_recv.at[step], rs_s.at[step], rs_r.at[step], ctx=target)

    for step in range(1, nc + 1):
        sib_copy(ring(c, step, nc)).start()
    line_begin()
    for step in range(1, nc):
        q = ring(c, step, nc)
        sib_copy(q).wait_recv()

        @pl.loop(0, rows // chunk)
        def _(k):
            at = pl.ds(pl.multiple_of(k * chunk, chunk), chunk)
            rs_send[step - 1, at, :] = (part[q, t, at, :].astype(f32) + sib[q, at, :].astype(f32)).astype(bf16)

        rs_copy(step - 1, q).start()
    sib_copy(c).wait_recv()
    begin(0)
    line_step(0)
    begin(1)
    for step in range(1, nc):
        rs_copy(step - 1, c).wait_recv()
    gain_acc[...] = jnp.zeros_like(gain_acc)

    @pl.loop(0, rows // chunk)
    def _(k):
        at = pl.ds(pl.multiple_of(k * chunk, chunk), chunk)
        full = pl.ds(pl.multiple_of(t * rows + k * chunk, chunk), chunk)
        grad = part[c, t, at, :].astype(f32) + sib[c, at, :].astype(f32)
        for step in range(nc - 1):
            grad = grad + rs_recv[step, at, :].astype(f32)
        x = tok[full, :].astype(f32)
        inv = lax.rsqrt(jnp.mean(x * x, -1, keepdims=True) + EPS)
        gain_acc[...] += jnp.sum((grad * x * inv).reshape(chunk // 8, 8, width), 0)
        weighted = grad * gain[...]
        inner = jnp.sum(weighted * x, -1, keepdims=True)
        out = residual_grad[at, :] + inv * weighted - x * (inv * inv * inv) * inner / width
        tok_grad[at, :] = out.astype(bf16)
        tokens_grad[full, :] = out.astype(bf16)

    def grad_copy(core):
        return remote(
            tok_grad, tokens_grad.at[pl.ds(pl.multiple_of(core * rows, rows), rows)], tg_s, tg_r, tp=1 - t
        )

    grad_copy(t).start()

    small_a[...] = small[...]
    total = jnp.sum(gain_acc[...], 0, keepdims=True)
    for strip in range(nz * nc):
        small_a[strip // nc, strip % nc, pl.ds(17, 1), :] = total[:, strip * 128 : (strip + 1) * 128]

    def small_copy(step, shard, target):
        return remote(small_a.at[shard], small_line.at[step], sm_s.at[step], sm_r.at[step], fsdp=target)

    def plane_copy(step, shard, target):
        return remote(small_b.at[shard], small_plane.at[step], sp_s.at[step], sp_r.at[step], ctx=target)

    for step in range(1, nz):
        small_copy(step - 1, ring(z, step, nz), ring(z, step, nz)).start()
    line_step(1)
    process(0)
    line_step(2)
    process(1)
    for step in range(1, nz):
        small_copy(step - 1, z, z).wait_recv()
    value = small_a[z]
    for step in range(nz - 1):
        value = value + small_line[step]
    small_b[...] = value
    for step in range(1, nc):
        plane_copy(step - 1, ring(c, step, nc), ring(c, step, nc)).start()

    def close(k, out, to):
        own, up, down = bufs[k]
        height = own.shape[2]
        tile = 32

        @pl.loop(0, nc * (height // tile))
        def _(n):
            q, at = n // (height // tile), pl.ds(pl.multiple_of(lax.rem(n, height // tile) * tile, tile), tile)
            base = own[z, q, at, :].astype(f32)
            above = up[jnp.minimum(nz - 1 - z, nz - 2), q, at, :].astype(f32)
            below = down[jnp.minimum(z, nz - 2), q, at, :].astype(f32)
            base = base + jnp.where(z > 0, above, 0.0) + jnp.where(z < nz - 1, below, 0.0)
            to[q, at, :] = base.astype(bf16)

    close(0, dw_out, dw_to)
    close(1, dwo_out, dwo_to)

    def to_copy(k, step, source, target):
        src, dst = ((dw_to, dw_out), (dwo_to, dwo_out))[k]
        return remote(src.at[target], dst.at[source], to_s.at[k, step], to_r.at[k, step], ctx=target)

    for step in range(1, nc):
        for k in range(2):
            to_copy(k, step - 1, c, ring(c, step, nc)).start()
    def layer_copy(core):
        return remote(
            layer_send.at[:, pl.ds(pl.multiple_of((1 - t) * piece, piece), piece)],
            layer.at[pl.ds(pl.multiple_of(core * rows, rows), rows)],
            lay_s, lay_r, tp=1 - t,
        )

    join()

    @pl.loop(0, rows // chunk)
    def _(k):
        at = pl.ds(pl.multiple_of(k * chunk, chunk), chunk)
        full = pl.ds(pl.multiple_of(t * rows + k * chunk, chunk), chunk)
        total = residual[at, :]
        for source in range(nz):
            total = total + y_line[source, at, :].astype(f32)
        layer_send[at, :] = total.astype(bf16)
        layer[full, :] = layer_send[at, pl.ds(pl.multiple_of(t * piece, piece), piece)]

    layer_copy(t).start()
    dw_out[c, :, :] = dw_to[c, :, :]
    dwo_out[c, :, :] = dwo_to[c, :, :]
    for step in range(1, nc):
        plane_copy(step - 1, c, c).wait_recv()
    value = small_b[c]
    for step in range(nc - 1):
        value = value + small_plane[step]
    small_out[...] = value
    final = remote(small_out, small_sib, ss_s, ss_r, tp=1 - t)
    final.start()
    final.wait()
    small_out[...] = value + small_sib[...]
    for step in range(1, nc):
        source = ring(c, -step, nc)
        for k in range(2):
            src, dst = ((dw_to, dw_out), (dwo_to, dwo_out))[k]
            remote(
                src.at[c], dst.at[source], to_s.at[k, step - 1], to_r.at[k, step - 1], ctx=source
            ).wait_recv()
    grad_copy(1 - t).wait_recv()
    grad_copy(t).wait_send()
    layer_copy(1 - t).wait_recv()
    layer_copy(t).wait_send()
    done()
    for step in range(1, nc):
        for k in range(2):
            to_copy(k, step - 1, c, ring(c, step, nc)).wait_send()
        plane_copy(step - 1, ring(c, step, nc), ring(c, step, nc)).wait_send()
        rs_copy(step - 1, c).wait_send()
    for step in range(1, nz):
        small_copy(step - 1, ring(z, step, nz), ring(z, step, nz)).wait_send()
    for q in range(nc):
        sib_copy(q).wait_send()
    for step in range(nz - 1):
        for way in range(2):
            shard = nz - 1 - step if way == 0 else step
            ahead = z + 1 if way == 0 else z - 1
            sends = shard > z if way == 0 else shard < z

            @pl.when(sends)
            def _():
                for k in range(2):
                    hop(way, step, k, ahead).wait_send()


def finish(part, tok, gain, residual_grad, dw, dwo, small, y, pick_t, residual):
    nz, nc = lax.axis_size("fsdp"), lax.axis_size("ctx")
    rows, width = residual_grad.shape
    dma = pltpu.SemaphoreType.DMA
    bf16, f32 = jnp.bfloat16, jnp.float32
    vmem = pl.BlockSpec(memory_space=pltpu.VMEM)
    one, two = dw.shape[1:], dwo.shape[1:]
    bufs, sems = collector_scratch(nz, nc, y.shape[2], rows, (width,))
    tiny = small.shape[2:]
    return pl.pallas_call(
        functools.partial(final_kernel, nz, nc),
        out_shape=[
            jax.ShapeDtypeStruct((2 * rows, width), bf16),
            jax.ShapeDtypeStruct(one, bf16),
            jax.ShapeDtypeStruct(two, bf16),
            jax.ShapeDtypeStruct(tiny, f32),
            jax.ShapeDtypeStruct((2 * rows, width // 2), bf16),
        ],
        in_specs=[vmem] * 7 + [pl.BlockSpec(memory_space=pl.ANY)] + [vmem] * 2,
        out_specs=[vmem] * 5,
        scratch_shapes=[
            pltpu.VMEM((nc, rows, width), bf16),
            pltpu.VMEM((nc - 1, rows, width), bf16),
            pltpu.VMEM((nc - 1, rows, width), bf16),
            pltpu.VMEM((rows, width), bf16),
            pltpu.VMEM((8, width), f32),
            pltpu.VMEM((nz - 1,) + one, bf16),
            pltpu.VMEM((nz - 1,) + one, bf16),
            pltpu.VMEM((nz - 1,) + two, bf16),
            pltpu.VMEM((nz - 1,) + two, bf16),
            pltpu.VMEM(one, bf16),
            pltpu.VMEM(two, bf16),
            pltpu.VMEM((2, nz - 1) + one, bf16),
            pltpu.VMEM((2, nz - 1) + two, bf16),
            pltpu.VMEM((nz - 1,) + small.shape[1:], f32),
            pltpu.VMEM((nc - 1,) + tiny, f32),
            pltpu.VMEM(tiny, f32),
            pltpu.VMEM(small.shape, f32),
            pltpu.VMEM(small.shape[1:], f32),
            dma((nc,)), dma((nc,)), dma((nc - 1,)), dma((nc - 1,)),
            dma((2, nz - 1, 2)), dma((2, nz - 1, 2)),
            dma((2, nc - 1)), dma((2, nc - 1)), dma, dma,
            dma((nz - 1,)), dma((nz - 1,)), dma((nc - 1,)), dma((nc - 1,)), dma, dma,
            pltpu.VMEM((rows, width), bf16), dma, dma,
        ] + bufs + sems,
        compiler_params=pltpu.CompilerParams(
            collective_id=3, has_side_effects=True, vmem_limit_bytes=60 * 2**20
        ),
    )(part, tok, gain, residual_grad, dw, dwo, small, y, pick_t, residual)


def one_chip(
    tokens,
    w_query,
    w_key,
    w_value,
    w_out,
    gain_attn,
    gain_query,
    gain_key,
    gain_moe,
    w_router,
    w_experts,
    routes,
    cotangent,
):
    z, c, t = lax.axis_index("fsdp"), lax.axis_index("ctx"), lax.axis_index("tp")
    nz, nc = lax.axis_size("fsdp"), lax.axis_size("ctx")
    block, width = tokens.shape[1], tokens.shape[2]
    rows = block // 2
    tall = block * nc
    deep = width // nz
    ffn = w_experts.shape[3]
    most = block * TOPK * 9 // (8 * E)
    bf16, f32 = jnp.bfloat16, jnp.float32

    token_half = lax.dynamic_slice_in_dim(tokens[0], t * rows, rows, 0)
    cotan_half = lax.dynamic_slice_in_dim(cotangent[0], t * rows, rows, 0)
    local = w_query.shape[1] // nc
    small = jnp.concatenate([w_router.T.reshape(-1), gain_attn, gain_moe, gain_query, gain_key])
    total = small.shape[0]
    small = jnp.pad(small, (0, -total % 2048))
    small = small.reshape(-1, 128)
    ids = jnp.arange(E, dtype=jnp.int32)
    named = jnp.any(routes[0][:, :, None] == ids, 1)
    below = jnp.tril(jnp.ones((block, block), bf16), -1)
    rank = jnp.where(named, dot(below, named.astype(bf16)), -1.0).T
    x_rows, w_qkv, w_o, small, _, rank_seq, pick, cot_rows, pair, third = load(
        tokens[0], cotangent[0], w_query, w_key, w_value, w_out, small, rank, w_experts, most
    )
    w_qkv = w_qkv.reshape(width, 3 * local)
    w_o = w_o.transpose(1, 0, 2).reshape(local, width)
    small = small.reshape(nz, -1)
    router = small[:, : E * deep].reshape(nz, E, deep).transpose(1, 0, 2).reshape(E, width)
    at = E * deep
    attn_gain = small[:, at : at + deep].reshape(-1).astype(f32)
    moe_gain = small[:, at + deep : at + 2 * deep].reshape(-1).astype(f32)
    at, part = at + 2 * deep, HD // nz
    query_gain = small[:, at : at + part].reshape(-1).astype(f32)
    key_gain = small[:, at + part : at + 2 * part].reshape(-1).astype(f32)

    pair = exchange(pair, "fsdp")

    counts = jnp.sum((rank_seq >= 0).astype(f32), 2)
    earlier = jnp.sum(jnp.where(jnp.arange(nc)[:, None] < c, counts, 0.0), 0)
    kept = ((rank >= 0) & (rank + earlier[:, None] < CAP)).astype(f32).T
    kept = lax.dynamic_slice_in_dim(kept, t * rows, rows, 0)

    x_rows = x_rows.astype(f32)
    place = jnp.arange(tall, dtype=jnp.int32)
    half_dim = HD // 2
    inv_freq = jnp.exp(jnp.arange(half_dim, dtype=f32) * (-2.0 * math.log(ROPE_BASE) / HD))
    angles = place.astype(f32)[:, None] * inv_freq[None, :]
    cos_full = jnp.concatenate([jnp.cos(angles)] * 2, -1)[:, None, :]
    sin_full = jnp.concatenate([jnp.sin(angles)] * 2, -1)[:, None, :]
    normed_one = (x_rows * rms_scale(x_rows) * attn_gain).astype(bf16)
    proj = dot(normed_one, w_qkv).reshape(tall, 3, local // HD, HD)
    query_heads, key_heads = proj[:, 0], proj[:, 1]
    values = proj[:, 2].astype(bf16)
    query_inv, key_inv = rms_scale(query_heads), rms_scale(key_heads)
    queries = apply_rope(query_heads * query_inv * query_gain, cos_full, sin_full).astype(bf16)
    keys = apply_rope(key_heads * key_inv * key_gain, cos_full, sin_full).astype(bf16)
    score_scale = 1.0 / math.sqrt(HD)
    scores = jnp.einsum("qhd,khd->hqk", queries, keys, preferred_element_type=f32) * score_scale
    maximum = jnp.max(scores, -1, keepdims=True)
    exp_scores = jnp.exp(scores - maximum)
    denominator = jnp.sum(exp_scores, -1, keepdims=True)
    attn_probs = exp_scores / denominator
    log_total = maximum + jnp.log(denominator)
    context = jnp.einsum("hqk,khd->qhd", attn_probs.astype(bf16), values, preferred_element_type=f32)
    context = context.astype(bf16).reshape(tall, local)
    attn_part = dot(context, w_o).astype(bf16).reshape(nc, 2, rows, width)
    kept_wide = jnp.pad(kept, ((0, 0), (0, 128 - E)))
    router_wide = jnp.pad(router, ((0, 128 - E), (0, 0)))
    residual, normed_two, router_probs, x_in, g_in, third = dispatch(
        attn_part, tokens[0], moe_gain[None], router_wide, kept_wide, pick, third
    )
    pair, x_in = lax.optimization_barrier((pair, x_in))
    x_in = x_in.reshape(nc * 2 * most, width)
    cot_rows = cot_rows.reshape(nc * 2 * most, width)
    chips = nz * nc
    strip = width // chips
    out_rows, back_rows, pair_rows, hid, gg, gu = experts(
        x_in, cot_rows, g_in.reshape(nc * 2 * most, -1), pair, third
    )
    shape = (nc, 2, most, -1)
    pick_t = pick.transpose(0, 2, 1)
    grad_logits, dgain_moe, grad_residual, grad_attn, dw_gate, own_grad, other_grad = give_back(
        back_rows.reshape(shape),
        pair_rows.reshape(shape),
        x_in,
        cot_rows,
        hid,
        gg,
        gu,
        pick_t,
        residual,
        router_probs,
        kept_wide,
        router_wide,
        moe_gain[None],
        cotangent[0],
    )

    dw_router = dot_tn(normed_two, grad_logits[:, :E])
    dgain_moe = jnp.sum(dgain_moe, 0)
    dw_rest = (own_grad.astype(f32) + other_grad.astype(f32)).astype(bf16)
    dw_rest, grad_attn = lax.optimization_barrier((dw_rest, grad_attn))
    dw_rest = exchange(dw_rest, ("fsdp", "ctx"))
    grad_attn = grad_attn.reshape(tall, width)

    dw_out = dot_tn(context, grad_attn).astype(bf16)
    grad_context = dot_nt(grad_attn, w_o).astype(bf16).reshape(tall, -1, HD)
    scores = jnp.einsum("qhd,khd->hqk", queries, keys, preferred_element_type=f32) * score_scale
    attn_probs = jnp.exp(scores - log_total)
    grad_probs = jnp.einsum("qhd,khd->hqk", grad_context, values, preferred_element_type=f32)
    grad_scores = attn_probs * (grad_probs - jnp.sum(attn_probs * grad_probs, -1, keepdims=True))
    grad_scores = grad_scores.astype(bf16)
    grad_queries = jnp.einsum("hqk,khd->qhd", grad_scores, keys, preferred_element_type=f32) * score_scale
    grad_keys = jnp.einsum("hqk,qhd->khd", grad_scores, queries, preferred_element_type=f32) * score_scale
    grad_values = jnp.einsum(
        "hqk,qhd->khd", attn_probs.astype(bf16), grad_context, preferred_element_type=f32
    ).astype(bf16)
    grad_qnormed = rope_back(grad_queries, cos_full, sin_full)
    grad_knormed = rope_back(grad_keys, cos_full, sin_full)
    dgain_query = jnp.sum(grad_qnormed * query_heads * query_inv, (0, 1))
    dgain_key = jnp.sum(grad_knormed * key_heads * key_inv, (0, 1))
    grad_qproj = norm_back(grad_qnormed, query_heads, query_inv, query_gain).astype(bf16)
    grad_kproj = norm_back(grad_knormed, key_heads, key_inv, key_gain).astype(bf16)
    grad_proj = jnp.stack([grad_qproj, grad_kproj, grad_values], 1).reshape(tall, 3 * local)
    dw_qkv = dot_tn(normed_one, grad_proj).astype(bf16)
    grad_normed_part = dot_nt(grad_proj, w_qkv).astype(bf16).reshape(nc, 2, rows, width)
    head_part = HD // chips
    heads = [dgain_query.reshape(chips, 1, head_part), dgain_key.reshape(chips, 1, head_part)]
    heads = jnp.pad(jnp.concatenate(heads, 2), ((0, 0), (0, 0), (0, strip - 2 * head_part)))
    sums = jnp.concatenate(
        [
            dw_router.reshape(chips, E, strip),
            dgain_moe.reshape(chips, 1, strip),
            jnp.zeros((chips, 1, strip), f32),
            heads,
            jnp.zeros((chips, 24 - E - 3, strip), f32),
        ],
        1,
    ).reshape(nz, nc, 24, strip)
    tokens_grad, got_qkv, got_out, sums, layer_out = finish(
        grad_normed_part,
        tokens[0],
        attn_gain[None],
        grad_residual,
        dw_qkv.reshape(nz, nc, strip, 3 * local),
        dw_out.reshape(local, nz, nc, strip).transpose(1, 2, 0, 3),
        sums,
        out_rows.reshape(shape),
        pick_t,
        residual,
    )
    dw_experts = lay_out(dw_gate[:, None], dw_rest, nz, nc)
    got_qkv = got_qkv.astype(f32).reshape(nc, strip, 3, local)
    got_qkv = got_qkv.transpose(2, 1, 0, 3).reshape(3, strip, nc * local)
    return (
        layer_out[None],
        tokens_grad[None],
        got_qkv[0],
        got_qkv[1],
        got_qkv[2],
        got_out.astype(f32).reshape(nc * local, strip),
        sums[E + 1],
        sums[E + 2, :head_part],
        sums[E + 2, head_part : 2 * head_part],
        sums[E],
        sums[:E].reshape(strip, E),
        dw_experts,
    )


def solution(mesh):
    chips = mesh.shape["fsdp"] * mesh.shape["ctx"]
    plain = chips == E and mesh.shape["fsdp"] == 4 and mesh.shape["tp"] == 2
    return jax.shard_map(
        one_chip if plain else general,
        mesh=mesh,
        in_specs=(
            P("fsdp", "ctx", None),
            P("fsdp", "tp"),
            P("fsdp", "tp"),
            P("fsdp", "tp"),
            P("tp", "fsdp"),
            P("fsdp"),
            P("fsdp"),
            P("fsdp"),
            P("fsdp"),
            P("fsdp", None),
            P("fsdp", None, None, "tp"),
            P("fsdp", "ctx", None),
            P("fsdp", "ctx", None),
        ),
        out_specs=(
            P("fsdp", "ctx", "tp"),
            P("fsdp", "ctx", None),
            P(("fsdp", "ctx"), "tp"),
            P(("fsdp", "ctx"), "tp"),
            P(("fsdp", "ctx"), "tp"),
            P("tp", ("fsdp", "ctx")),
            P(("fsdp", "ctx")),
            P(("fsdp", "ctx")),
            P(("fsdp", "ctx")),
            P(("fsdp", "ctx")),
            P(("fsdp", "ctx"), None),
            P(("fsdp", "ctx"), None, None, "tp"),
        ),
        check_vma=False,
    )
```

```python
import functools
import math

import jax
import jax.numpy as jnp
from jax import lax
from jax.experimental import pallas as pl
from jax.experimental.pallas import tpu as pltpu
from jax.sharding import PartitionSpec as P

HD = 128
TOPK = 8
E = 16
CAP = 512
MESH = pl.DeviceIdType.MESH


EPS = 1e-06
ROPE_BASE = 10000.0


def prefix(value, axis, join, neutral):
    count, mine = (lax.axis_size(axis), lax.axis_index(axis))
    pieces = lax.all_gather(value, axis)
    running = jnp.full_like(value, 0) + jnp.asarray(neutral, value.dtype)

    def lap(position, running):
        longer = join(running, pieces[position])
        return jnp.where(position < mine, longer, running)

    return lax.fori_loop(0, count - 1, lap, running)


def rms_scale(values):
    return lax.rsqrt(jnp.mean(values * values, -1, keepdims=True) + EPS)


def norm_back(grad_normed, values, inv_rms, gain_vec):
    weighted = grad_normed * gain_vec.astype(jnp.float32)
    inner_sum = jnp.sum(weighted * values, -1, keepdims=True)
    return (
        inv_rms * weighted - values * (inv_rms * inv_rms * inv_rms) * inner_sum / values.shape[-1]
    )


def rope_tables(first, length):
    half_dim = HD // 2
    inv_freq = jnp.exp(jnp.arange(half_dim, dtype=jnp.float32) * (-2.0 * math.log(ROPE_BASE) / HD))
    places = (first + jnp.arange(length, dtype=jnp.int32)).astype(jnp.float32)
    angles = places[:, None] * inv_freq[None, :]
    cos_table = jnp.cos(angles)
    sin_table = jnp.sin(angles)
    cos_full = jnp.concatenate([cos_table, cos_table], -1)[:, None, :]
    sin_full = jnp.concatenate([sin_table, sin_table], -1)[:, None, :]
    return (cos_full, sin_full)


def rotate(values):
    half_dim = values.shape[-1] // 2
    return jnp.concatenate([-values[..., half_dim:], values[..., :half_dim]], -1)


def rotate_back(values):
    half_dim = values.shape[-1] // 2
    return jnp.concatenate([values[..., half_dim:], -values[..., :half_dim]], -1)


def apply_rope(values, cos_full, sin_full):
    return values * cos_full + rotate(values) * sin_full


def rope_back(grads, cos_full, sin_full):
    return grads * cos_full + rotate_back(grads * sin_full)


def add_counts(earlier, later):
    return earlier + later


def general(
    tokens,
    w_query,
    w_key,
    w_value,
    w_out,
    gain_attn,
    gain_query,
    gain_key,
    gain_moe,
    w_router,
    w_experts,
    routes,
    cotangent,
):
    seq_count, block_len, model_width = tokens.shape
    row_count = seq_count * block_len
    (
        full_query,
        full_key,
        full_value,
        full_out,
        router_full,
        attn_gain,
        query_gain,
        key_gain,
        moe_gain,
    ) = (
        lax.all_gather(w_query, "fsdp", axis=0, tiled=True),
        lax.all_gather(w_key, "fsdp", axis=0, tiled=True),
        lax.all_gather(w_value, "fsdp", axis=0, tiled=True),
        lax.all_gather(w_out, "fsdp", axis=1, tiled=True),
        lax.all_gather(w_router, "fsdp", axis=0, tiled=True),
        lax.all_gather(gain_attn, "fsdp", axis=0, tiled=True),
        lax.all_gather(gain_query, "fsdp", axis=0, tiled=True),
        lax.all_gather(gain_key, "fsdp", axis=0, tiled=True),
        lax.all_gather(gain_moe, "fsdp", axis=0, tiled=True),
    )
    local_width = full_query.shape[1]
    head_count = local_width // HD
    head_shape = (seq_count, block_len, head_count, HD)
    token_rows = tokens.reshape(row_count, model_width).astype(jnp.float32)
    inv_one = rms_scale(token_rows)
    normed_one = (token_rows * inv_one * attn_gain.astype(jnp.float32)).astype(jnp.bfloat16)
    query_proj = jnp.dot(normed_one, full_query, preferred_element_type=jnp.float32)
    key_proj = jnp.dot(normed_one, full_key, preferred_element_type=jnp.float32)
    value_proj = jnp.dot(normed_one, full_value, preferred_element_type=jnp.float32)
    cos_full, sin_full = rope_tables(lax.axis_index("ctx") * block_len, block_len)
    query_heads = query_proj.reshape(head_shape)
    key_heads = key_proj.reshape(head_shape)
    query_inv = rms_scale(query_heads)
    key_inv = rms_scale(key_heads)
    queries = apply_rope(
        query_heads * query_inv * query_gain.astype(jnp.float32), cos_full, sin_full
    ).astype(jnp.bfloat16)
    keys_local = apply_rope(
        key_heads * key_inv * key_gain.astype(jnp.float32), cos_full, sin_full
    ).astype(jnp.bfloat16)
    keys_local = keys_local.reshape(seq_count, block_len, local_width)
    values_local = value_proj.astype(jnp.bfloat16).reshape(seq_count, block_len, local_width)
    keys_all, values_all = (
        lax.all_gather(keys_local, "ctx", axis=1, tiled=True),
        lax.all_gather(values_local, "ctx", axis=1, tiled=True),
    )
    seq_len = keys_all.shape[1]
    key_rows = keys_all.reshape(seq_count, seq_len, head_count, HD)
    value_rows = values_all.reshape(seq_count, seq_len, head_count, HD)
    score_scale = 1.0 / math.sqrt(HD)
    scores = (
        jnp.einsum("sqhd,skhd->shqk", queries, key_rows, preferred_element_type=jnp.float32)
        * score_scale
    )
    maximum = jnp.max(scores, -1, keepdims=True)
    exp_scores = jnp.exp(scores - maximum)
    denominator = jnp.sum(exp_scores, -1, keepdims=True)
    attn_probs = exp_scores / denominator
    log_total = maximum + jnp.log(denominator)
    context = jnp.einsum(
        "shqk,skhd->sqhd",
        attn_probs.astype(jnp.bfloat16),
        value_rows,
        preferred_element_type=jnp.float32,
    )
    context = context.astype(jnp.bfloat16).reshape(row_count, local_width)
    attn_part = jnp.dot(context, full_out, preferred_element_type=jnp.float32)
    residual = token_rows + lax.psum(attn_part, "tp")
    inv_two = rms_scale(residual)
    normed_two = (residual * inv_two * moe_gain.astype(jnp.float32)).astype(jnp.bfloat16)
    logits = jnp.dot(normed_two, router_full, preferred_element_type=jnp.float32)
    router_probs = jax.nn.softmax(logits, -1)
    pair_count = block_len * TOPK
    route_rows = routes.reshape(seq_count, pair_count)
    expert_ids = jnp.arange(E, dtype=jnp.int32)
    onehot = (route_rows[:, :, None] == expert_ids[None, None, :]).astype(jnp.int32)
    counts = jnp.sum(onehot, 1, dtype=jnp.int32)
    offsets = prefix(counts, "ctx", add_counts, jnp.zeros_like(counts))
    earlier = jnp.cumsum(onehot, 1, dtype=jnp.int32) - onehot
    local_rank = jnp.sum(earlier * onehot, 2, dtype=jnp.int32)
    slot_base = jnp.sum(onehot * offsets[:, None, :], 2, dtype=jnp.int32)
    kept_mask = (slot_base + local_rank < CAP).astype(jnp.float32).reshape(row_count, TOPK)
    block_most = pair_count * 9 // (8 * E)
    expert_span = seq_count * block_most
    seq_ids = jnp.arange(seq_count, dtype=jnp.int32)[:, None]
    buffer_row = (route_rows * expert_span + seq_ids * block_most + local_rank).reshape(
        row_count * TOPK
    )
    token_ids = (
        seq_ids * block_len + jnp.arange(pair_count, dtype=jnp.int32)[None, :] // TOPK
    ).reshape(row_count * TOPK)
    owner_rows = jnp.zeros((E * expert_span,), jnp.int32).at[buffer_row].set(token_ids)
    onehot_f = onehot.astype(jnp.float32).reshape(row_count, TOPK, E)
    gate_weight = jnp.sum(onehot_f * router_probs[:, None, :], 2) * kept_mask
    slot_weight = (
        jnp.zeros((E * expert_span,), jnp.float32)
        .at[buffer_row]
        .set(gate_weight.reshape(row_count * TOPK))
    )
    expert_rows = normed_two[owner_rows].reshape(E, expert_span, model_width)
    cotan_rows = cotangent.reshape(row_count, model_width)
    grad_expert = (slot_weight[:, None] * cotan_rows[owner_rows].astype(jnp.float32)).astype(
        jnp.bfloat16
    )
    grad_expert = grad_expert.reshape(E, expert_span, model_width)
    ffn_local = w_experts.shape[3]
    fsdp_count = lax.axis_size("fsdp")
    ctx_count = lax.axis_size("ctx")
    group_count = fsdp_count * ctx_count
    sharing = group_count // E
    padded_span = -(-expert_span // sharing) * sharing
    part_span = padded_span // sharing
    target_experts = (
        jnp.arange(fsdp_count, dtype=jnp.int32) * ctx_count + lax.axis_index("ctx")
    ) // sharing
    selected = jnp.take(w_experts, target_experts, axis=2)
    owned = lax.all_to_all(selected, "fsdp", split_axis=2, concat_axis=0, tiled=True)[:, :, 0]
    send_rows = expert_rows.reshape(group_count, part_span, model_width)
    send_grads = grad_expert.reshape(group_count, part_span, model_width)
    recv_rows, recv_grads = (
        lax.all_to_all(send_rows, ("fsdp", "ctx"), split_axis=0, concat_axis=0, tiled=True),
        lax.all_to_all(send_grads, ("fsdp", "ctx"), split_axis=0, concat_axis=0, tiled=True),
    )
    rows_flat = recv_rows.reshape(group_count * part_span, model_width)
    grads_flat = recv_grads.reshape(group_count * part_span, model_width)
    gate_act = jnp.dot(rows_flat, owned[:, 0], preferred_element_type=jnp.float32)
    up_act = jnp.dot(rows_flat, owned[:, 1], preferred_element_type=jnp.float32)
    sigmoid_gate = jax.nn.sigmoid(gate_act)
    silu_gate = gate_act * sigmoid_gate
    hidden = (silu_gate * up_act).astype(jnp.bfloat16)
    produced = jnp.einsum("mf,df->md", hidden, owned[:, 2], preferred_element_type=jnp.float32)
    grad_hidden = jnp.dot(grads_flat, owned[:, 2], preferred_element_type=jnp.float32)
    grad_gate = (
        grad_hidden * up_act * sigmoid_gate * (1.0 + gate_act * (1.0 - sigmoid_gate))
    ).astype(jnp.bfloat16)
    grad_up = (grad_hidden * silu_gate).astype(jnp.bfloat16)
    rows_grad = jnp.einsum("mf,df->md", grad_gate, owned[:, 0], preferred_element_type=jnp.float32)
    rows_grad = rows_grad + jnp.einsum(
        "mf,df->md", grad_up, owned[:, 1], preferred_element_type=jnp.float32
    )
    back_out, back_rows = (
        lax.all_to_all(
            produced.reshape(group_count, part_span, model_width).astype(jnp.bfloat16),
            ("fsdp", "ctx"),
            split_axis=0,
            concat_axis=0,
            tiled=True,
        ).astype(jnp.float32),
        lax.all_to_all(
            rows_grad.reshape(group_count, part_span, model_width).astype(jnp.bfloat16),
            ("fsdp", "ctx"),
            split_axis=0,
            concat_axis=0,
            tiled=True,
        ).astype(jnp.float32),
    )
    expert_out = back_out.reshape(E, padded_span, model_width)
    grad_rows = back_rows.reshape(E, padded_span, model_width)
    gate_term = jnp.einsum("md,mf->df", rows_flat, grad_gate, preferred_element_type=jnp.float32)
    up_term = jnp.einsum("md,mf->df", rows_flat, grad_up, preferred_element_type=jnp.float32)
    down_term = jnp.einsum("md,mf->df", grads_flat, hidden, preferred_element_type=jnp.float32)
    owner_terms = jnp.stack([gate_term, up_term, down_term], 1)[:, :, None, :]
    relaid = lax.all_to_all(
        owner_terms.astype(jnp.bfloat16), ("fsdp", "ctx"), split_axis=0, concat_axis=2, tiled=True
    ).astype(owner_terms.dtype)
    dw_experts = jnp.sum(relaid.reshape(relaid.shape[0], 3, E, sharing, ffn_local), 3)
    picked = expert_out.reshape(E * expert_span, model_width)[buffer_row].reshape(
        row_count, TOPK, model_width
    )
    moe_part = jnp.sum(gate_weight[:, :, None] * picked, 1)
    cotan_float = cotan_rows.astype(jnp.float32)
    grad_gate_part = jnp.sum(picked * cotan_float[:, None, :], 2)
    moe_shard = lax.psum_scatter(
        moe_part.astype(jnp.bfloat16), "tp", scatter_dimension=1, tiled=True
    ).astype(jnp.float32)
    piece_width = moe_shard.shape[1]
    residual_shard = lax.dynamic_slice_in_dim(
        residual, lax.axis_index("tp") * piece_width, piece_width, 1
    )
    layer_out = (
        (residual_shard + moe_shard).astype(jnp.bfloat16).reshape(seq_count, block_len, piece_width)
    )
    grad_normed_part = jnp.sum(
        grad_rows.reshape(E * expert_span, model_width)[buffer_row].reshape(
            row_count, TOPK, model_width
        ),
        1,
    )
    grad_normed_sum, grad_gate_sum = (
        lax.psum(grad_normed_part.astype(jnp.bfloat16), "tp").astype(jnp.float32),
        lax.psum(grad_gate_part.astype(jnp.bfloat16), "tp").astype(jnp.float32),
    )
    grad_pick = grad_gate_sum * kept_mask
    grad_router_probs = jnp.sum(onehot_f * grad_pick[:, :, None], 1)
    grad_logits = router_probs * (
        grad_router_probs - jnp.sum(router_probs * grad_router_probs, -1, keepdims=True)
    )
    grad_logits = grad_logits.astype(jnp.bfloat16)
    grad_router_w = jnp.einsum(
        "nd,ne->de", normed_two, grad_logits, preferred_element_type=jnp.float32
    )
    grad_normed_two = grad_normed_sum + jnp.einsum(
        "ne,de->nd", grad_logits, router_full, preferred_element_type=jnp.float32
    )
    grad_moe_gain = jnp.sum(grad_normed_two * residual * inv_two, 0)
    grad_residual = cotan_float + norm_back(grad_normed_two, residual, inv_two, moe_gain)
    grad_attn = grad_residual.astype(jnp.bfloat16)
    grad_w_out = jnp.einsum("nl,nd->ld", context, grad_attn, preferred_element_type=jnp.float32)
    grad_context = jnp.einsum("nd,ld->nl", grad_attn, full_out, preferred_element_type=jnp.float32)
    grad_context = grad_context.astype(jnp.bfloat16).reshape(head_shape)
    scores = (
        jnp.einsum("sqhd,skhd->shqk", queries, key_rows, preferred_element_type=jnp.float32)
        * score_scale
    )
    attn_probs = jnp.exp(scores - log_total)
    grad_probs = jnp.einsum(
        "sqhd,skhd->shqk", grad_context, value_rows, preferred_element_type=jnp.float32
    )
    grad_scores = attn_probs * (grad_probs - jnp.sum(attn_probs * grad_probs, -1, keepdims=True))
    grad_scores = grad_scores.astype(jnp.bfloat16)
    grad_queries = (
        jnp.einsum("shqk,skhd->sqhd", grad_scores, key_rows, preferred_element_type=jnp.float32)
        * score_scale
    )
    grad_keys_all = (
        jnp.einsum("shqk,sqhd->skhd", grad_scores, queries, preferred_element_type=jnp.float32)
        * score_scale
    )
    grad_values_all = jnp.einsum(
        "shqk,sqhd->skhd",
        attn_probs.astype(jnp.bfloat16),
        grad_context,
        preferred_element_type=jnp.float32,
    )
    grad_keys_own, grad_values_own = (
        lax.psum_scatter(
            grad_keys_all.reshape(seq_count, seq_len, local_width).astype(jnp.bfloat16),
            "ctx",
            scatter_dimension=1,
            tiled=True,
        ).astype(jnp.float32),
        lax.psum_scatter(
            grad_values_all.reshape(seq_count, seq_len, local_width).astype(jnp.bfloat16),
            "ctx",
            scatter_dimension=1,
            tiled=True,
        ).astype(jnp.float32),
    )
    grad_qnormed = rope_back(grad_queries, cos_full, sin_full)
    grad_knormed = rope_back(grad_keys_own.reshape(head_shape), cos_full, sin_full)
    grad_qgain = jnp.sum(grad_qnormed * query_heads * query_inv, (0, 1, 2))
    grad_kgain = jnp.sum(grad_knormed * key_heads * key_inv, (0, 1, 2))
    grad_qproj = (
        norm_back(grad_qnormed, query_heads, query_inv, query_gain)
        .astype(jnp.bfloat16)
        .reshape(row_count, local_width)
    )
    grad_kproj = (
        norm_back(grad_knormed, key_heads, key_inv, key_gain)
        .astype(jnp.bfloat16)
        .reshape(row_count, local_width)
    )
    grad_vproj = grad_values_own.astype(jnp.bfloat16).reshape(row_count, local_width)
    grad_wq = jnp.einsum("nd,nl->dl", normed_one, grad_qproj, preferred_element_type=jnp.float32)
    grad_wk = jnp.einsum("nd,nl->dl", normed_one, grad_kproj, preferred_element_type=jnp.float32)
    grad_wv = jnp.einsum("nd,nl->dl", normed_one, grad_vproj, preferred_element_type=jnp.float32)
    grad_normed_one = jnp.einsum(
        "nl,dl->nd", grad_qproj, full_query, preferred_element_type=jnp.float32
    )
    grad_normed_one = grad_normed_one + jnp.einsum(
        "nl,dl->nd", grad_kproj, full_key, preferred_element_type=jnp.float32
    )
    grad_normed_one = grad_normed_one + jnp.einsum(
        "nl,dl->nd", grad_vproj, full_value, preferred_element_type=jnp.float32
    )
    grad_normed_one, grad_qgain, grad_kgain = (
        lax.psum(grad_normed_one.astype(jnp.bfloat16), "tp").astype(jnp.float32),
        lax.psum(grad_qgain.astype(jnp.bfloat16), "tp").astype(jnp.float32),
        lax.psum(grad_kgain.astype(jnp.bfloat16), "tp").astype(jnp.float32),
    )
    grad_attn_gain = jnp.sum(grad_normed_one * token_rows * inv_one, 0)
    tokens_grad = grad_residual + norm_back(grad_normed_one, token_rows, inv_one, attn_gain)
    tokens_grad = tokens_grad.astype(jnp.bfloat16).reshape(seq_count, block_len, model_width)
    dw_query, dw_key, dw_value, dw_out, dw_router, dgain_attn, dgain_query, dgain_key, dgain_moe = (
        lax.psum_scatter(grad_wq, ("fsdp", "ctx"), scatter_dimension=0, tiled=True),
        lax.psum_scatter(grad_wk, ("fsdp", "ctx"), scatter_dimension=0, tiled=True),
        lax.psum_scatter(grad_wv, ("fsdp", "ctx"), scatter_dimension=0, tiled=True),
        lax.psum_scatter(grad_w_out, ("fsdp", "ctx"), scatter_dimension=1, tiled=True),
        lax.psum_scatter(grad_router_w, ("fsdp", "ctx"), scatter_dimension=0, tiled=True),
        lax.psum_scatter(grad_attn_gain, ("fsdp", "ctx"), scatter_dimension=0, tiled=True),
        lax.psum_scatter(grad_qgain, ("fsdp", "ctx"), scatter_dimension=0, tiled=True),
        lax.psum_scatter(grad_kgain, ("fsdp", "ctx"), scatter_dimension=0, tiled=True),
        lax.psum_scatter(grad_moe_gain, ("fsdp", "ctx"), scatter_dimension=0, tiled=True),
    )
    return (
        layer_out,
        tokens_grad,
        dw_query,
        dw_key,
        dw_value,
        dw_out,
        dgain_attn,
        dgain_query,
        dgain_key,
        dgain_moe,
        dw_router,
        dw_experts,
    )


def swap(value):
    return lax.ppermute(value, "tp", [(0, 1), (1, 0)])


def exchange(value, axes):
    return lax.all_to_all(value, axes, split_axis=0, concat_axis=0, tiled=True)


def spread(value, axes):
    count = lax.axis_size(axes)
    return exchange(jnp.broadcast_to(value[None], (count,) + value.shape), axes)


def dot(left, right):
    return jnp.dot(left, right, preferred_element_type=jnp.float32)


def dot_nt(left, right):
    return lax.dot_general(left, right, (((1,), (1,)), ((), ())), preferred_element_type=jnp.float32)


def dot_tn(left, right):
    return lax.dot_general(left, right, (((0,), (0,)), ((), ())), preferred_element_type=jnp.float32)


def two_parts(values):
    high = values.astype(jnp.bfloat16)
    low = (values - high.astype(jnp.float32)).astype(jnp.bfloat16)
    return (high, low)


def by_core(mine, other, core):
    return jnp.where(core == 0, jnp.stack([mine, other]), jnp.stack([other, mine]))


def remote(src, dst, send, recv, **where):
    return pltpu.make_async_remote_copy(
        src_ref=src, dst_ref=dst, send_sem=send, recv_sem=recv, device_id=where, device_id_type=MESH
    )


def places():
    return lax.axis_index("fsdp"), lax.axis_index("ctx"), lax.axis_index("tp")


def ring(index, step, count):
    return lax.rem(index + step + count, count)


def greet(nz, nc, line, far=False):
    z, c, t = places()
    barrier = pltpu.get_barrier_semaphore()

    def tell(**where):
        pl.semaphore_signal(barrier, inc=1, device_id=where, device_id_type=MESH)

    if line:
        for step in range(1, nz):
            tell(fsdp=ring(z, step, nz))
        count = nz - 1
    else:
        pl.when(z > 0)(lambda: tell(fsdp=z - 1))
        pl.when(z < nz - 1)(lambda: tell(fsdp=z + 1))
        count = jnp.where(z > 0, 1, 0) + jnp.where(z < nz - 1, 1, 0)
    for step in range(1, nc):
        tell(ctx=ring(c, step, nc))
        if far:
            for hop in range(1, nz):
                tell(fsdp=ring(z, hop, nz), ctx=ring(c, step, nc))
    if far:
        count = count + (nz - 1) * (nc - 1)
    tell(tp=1 - t)
    pl.semaphore_wait(barrier, count + nc)


def line_copies(bufs, send_sem, recv_sem, way, step, shard, target):
    return [
        remote(buf.at[shard], buf.at[shard], send_sem.at[way, step, k], recv_sem.at[way, step, k], fsdp=target)
        for k, buf in enumerate(bufs)
    ]


def line_gather(nz, bufs, send_sem, recv_sem, arrived, begun=None, near=None):
    z = lax.axis_index("fsdp")
    for step in range(nz - 1):

        @pl.when((z < nz - 1) & (z >= step))
        def _():
            for copy in line_copies(bufs, send_sem, recv_sem, 0, step, z - step, z + 1):
                copy.start()

        @pl.when((z > 0) & (z + step < nz))
        def _():
            for copy in line_copies(bufs, send_sem, recv_sem, 1, step, z + step, z - 1):
                copy.start()

        if step == 0 and begun is not None:
            begun()
        if near is not None:
            near(step)

        @pl.when(z - 1 >= step)
        def _():
            for copy in line_copies(bufs, send_sem, recv_sem, 0, step, z - 1 - step, z - 1):
                copy.wait_recv()
            arrived(z - 1 - step)

        @pl.when(z + 1 + step < nz)
        def _():
            for copy in line_copies(bufs, send_sem, recv_sem, 1, step, z + 1 + step, z + 1):
                copy.wait_recv()
            arrived(z + 1 + step)


def line_sent(nz, bufs, send_sem, recv_sem):
    z = lax.axis_index("fsdp")
    for step in range(nz - 1):

        @pl.when((z < nz - 1) & (z >= step))
        def _():
            for copy in line_copies(bufs, send_sem, recv_sem, 0, step, z - step, z + 1):
                copy.wait_send()

        @pl.when((z > 0) & (z + step < nz))
        def _():
            for copy in line_copies(bufs, send_sem, recv_sem, 1, step, z + step, z - 1):
                copy.wait_send()


def pick_rows(pick, slot, source, out):
    lanes = out.shape[-1]
    piece = min(lanes, 512)

    @pl.loop(0, lanes // piece)
    def _(k):
        at = pl.ds(pl.multiple_of(k * piece, piece), piece)
        out[slot, :, at] = jnp.dot(pick[slot], source[slot, :, at], preferred_element_type=jnp.float32).astype(
            jnp.bfloat16
        )


def plane_copy(most, src, dst, send, recv, slot, step, source, target):
    rows = pl.ds(pl.multiple_of(target * most, 16), most)
    return remote(
        src.at[slot, rows], dst.at[source, slot], send.at[slot, step - 1], recv.at[slot, step - 1], ctx=target
    )


def regroup(shard, t, rows, line, two, keep_sem, give_send, give_recv):
    slot = lax.rem(shard, 2)
    band = pl.ds(pl.multiple_of(t * rows, rows), rows)

    def keep():
        pltpu.make_async_copy(line.at[shard], two.at[slot, band], keep_sem.at[slot]).start()

    def give():
        remote(line.at[shard], two.at[slot, band], give_send.at[slot], give_recv.at[slot], tp=1 - t).start()

    pl.when(shard // 2 == t)(keep)
    pl.when(shard // 2 != t)(give)


def selector(nz, src, pair, third, held, pair_out, third_out, in_sem, pair_sem, third_sem):
    c = lax.axis_index("ctx")
    tile = 16
    count = src.shape[2]
    height = held.shape[1]
    bands = src.shape[0] // height

    def take(b):
        slot = lax.rem(b, 2)
        return pltpu.make_async_copy(
            src.at[pl.ds(pl.multiple_of(b * height, height), height)], held.at[slot], in_sem.at[slot]
        )

    def put(b):
        slot = lax.rem(b, 2)
        at = pl.ds(pl.multiple_of(b * height, height), height)
        return (
            pltpu.make_async_copy(pair_out.at[slot], pair.at[:, :, at], pair_sem.at[slot]),
            pltpu.make_async_copy(third_out.at[slot], third.at[:, at], third_sem.at[slot]),
        )

    def pick_band(b):
        slot = lax.rem(b, 2)
        take(b).wait()
        pl.when(b + 1 < bands)(lambda: take(b + 1).start())

        @pl.when(b >= 2)
        def _():
            for copy in put(b - 2):
                copy.wait()

        row = lax.broadcasted_iota(jnp.int32, (nz * tile, tile * count), 0)
        column = lax.broadcasted_iota(jnp.int32, (nz * tile, tile * count), 1)
        hit = column == lax.rem(row, tile) * count + c * nz + row // tile
        hit = jnp.where(hit, 1.0, 0.0).astype(jnp.bfloat16)
        for n in range(height // tile):
            at = pl.ds(n * tile, tile)
            for k in range(3):
                value = held[slot, n * tile : (n + 1) * tile, k].reshape(tile * count, -1)
                value = jnp.dot(hit, value, preferred_element_type=jnp.float32).astype(jnp.bfloat16)
                value = value.reshape(nz, tile, -1)
                if k == 1:
                    third_out[slot, :, at, :] = value
                else:
                    pair_out[slot, :, k // 2, at, :] = value
        for copy in put(b):
            copy.start()

    def close():
        for b in (bands - 2, bands - 1):
            for copy in put(b):
                copy.wait()

    pick_band.close = close
    return take, pick_band, bands


def load_kernel(
    nz, nc, tok, cot, wq, wk, wv, wo, small, rank, w_experts,
    x_all, w_qkv, w_o, small_all, rank_line, rank_seq, pick, cot_in, pair, third,
    cot_line, cot_two, cot_send,
    own_sem, line_send, line_recv, w_send, w_recv, tok_send, tok_recv, pass_send, pass_recv,
    rank_send, rank_recv, keep_sem, give_send, give_recv, cot_s, cot_r, cot_own,
    sel_in, sel_pair, sel_third, sel_s, sel_p, sel_t,
):
    z, c, t = places()
    block = tok.shape[0]
    rows = block // 2
    local = w_qkv.shape[2] // 3
    most = cot_in.shape[2]
    half = pl.ds(pl.multiple_of(t * rows, rows), rows)
    column = pl.ds(pl.multiple_of(c * local, local), local)
    own = [
        pltpu.make_async_copy(cot.at[half], cot_line.at[z], own_sem.at[5]),
        pltpu.make_async_copy(small, small_all.at[z], own_sem.at[4]),
        pltpu.make_async_copy(rank, rank_line.at[z], own_sem.at[7]),
        pltpu.make_async_copy(rank, rank_seq.at[c], own_sem.at[8]),
    ]
    own += [
        pltpu.make_async_copy(w.at[:, column], w_qkv.at[z, :, pl.ds(k * local, local)], own_sem.at[k])
        for k, w in enumerate((wq, wk, wv))
    ]
    own += [
        pltpu.make_async_copy(wo.at[column], w_o.at[z], own_sem.at[3]),
        pltpu.make_async_copy(tok, x_all.at[pl.ds(pl.multiple_of(c * block, block), block)], own_sem.at[6]),
    ]
    for copy in own:
        copy.start()
    take, pick_band, bands = selector(nz, w_experts, pair, third, sel_in, sel_pair, sel_third, sel_s, sel_p, sel_t)
    take(0).start()
    greet(nz, nc, False)

    def band(source, core):
        return x_all.at[pl.ds(pl.multiple_of(source * block + core * rows, rows), rows)]

    def token_copy(step, source, target):
        return remote(tok.at[half], band(source, t), tok_send.at[step], tok_recv.at[step], ctx=target)

    def pass_copy(step, source, core):
        return remote(band(source, core), band(source, core), pass_send.at[step], pass_recv.at[step], tp=1 - t)

    def rank_copy(step, source, target):
        return remote(rank, rank_seq.at[source], rank_send.at[step], rank_recv.at[step], ctx=target)

    for step in range(1, nc):
        token_copy(step - 1, c, ring(c, step, nc)).start()
        rank_copy(step - 1, c, ring(c, step, nc)).start()
    for copy in own:
        copy.wait()

    def arrived(shard):
        regroup(shard, t, rows, cot_line, cot_two, keep_sem, give_send, give_recv)

    arrived(z)
    first = (cot_line, rank_line, small_all)
    line_gather(nz, first, line_send, line_recv, arrived)

    def own_copy(slot):
        return pltpu.make_async_copy(
            cot_send.at[slot, pl.ds(pl.multiple_of(c * most, 16), most)], cot_in.at[c, slot], cot_own.at[slot]
        )

    def send_cotangent():
        number = lax.broadcasted_iota(jnp.int32, (most, block), 0).astype(jnp.float32)
        for slot in range(2):
            for q in range(nc):
                row = rank_line[2 * t + slot, pl.ds(q * nz + z, 1), :]
                hit = jnp.where(number == row, 1.0, 0.0)
                pick[slot, pl.ds(q * most, most), :] = hit.astype(jnp.bfloat16)
        for slot in range(2):
            wait_two(slot, t, rows, cot_line, cot_two, keep_sem, give_recv)
            pick_rows(pick, slot, cot_two, cot_send)
            for step in range(1, nc):
                plane_copy(most, cot_send, cot_in, cot_s, cot_r, slot, step, c, ring(c, step, nc)).start()
            own_copy(slot).start()

    def ignore(shard):
        pass

    def select_some(step):
        pl.loop(bands * (0, 1, 3)[step] // 4, bands * (1, 3, 4)[step] // 4)(pick_band)

    line_gather(nz, (w_qkv, w_o), w_send, w_recv, ignore, send_cotangent, select_some)
    pick_band.close()
    for step in range(1, nc):
        source = ring(c, -step, nc)
        token_copy(step - 1, source, source).wait_recv()
        pass_copy(step - 1, source, t).start()
        rank_copy(step - 1, source, source).wait_recv()
    for step in range(1, nc):
        source = ring(c, -step, nc)
        pass_copy(step - 1, source, 1 - t).wait_recv()
        pass_copy(step - 1, source, t).wait_send()
        token_copy(step - 1, c, source).wait_send()
        rank_copy(step - 1, c, source).wait_send()
        for slot in range(2):
            copy = plane_copy(most, cot_send, cot_in, cot_s, cot_r, slot, step, source, source)
            copy.wait_recv()
            copy.wait_send()
    line_sent(nz, first, line_send, line_recv)
    line_sent(nz, (w_qkv, w_o), w_send, w_recv)
    for slot in range(2):
        own_copy(slot).wait()
        wait_given(slot, t, rows, cot_line, cot_two, give_send, give_recv)


def wait_given(slot, t, rows, line, two, give_send, give_recv):
    band = pl.ds(pl.multiple_of(t * rows, rows), rows)
    remote(line.at[0], two.at[slot, band], give_send.at[slot], give_recv.at[slot], tp=1 - t).wait_send()


def wait_two(slot, t, rows, line, two, keep_sem, give_recv):
    band = pl.ds(pl.multiple_of(t * rows, rows), rows)
    other = pl.ds(pl.multiple_of((1 - t) * rows, rows), rows)
    pltpu.make_async_copy(line.at[0], two.at[slot, band], keep_sem.at[slot]).wait()
    remote(line.at[0], two.at[slot, other], give_recv.at[slot], give_recv.at[slot], tp=1 - t).wait_recv()


def load(tok, cot, wq, wk, wv, wo, small, rank, w_experts, most):
    nz, nc = lax.axis_size("fsdp"), lax.axis_size("ctx")
    block, width = tok.shape
    deep, local = wq.shape[0], wq.shape[1] // nc
    rows = block // 2
    count, ffn = w_experts.shape[2:]
    dma = pltpu.SemaphoreType.DMA
    bf16, f32 = jnp.bfloat16, jnp.float32
    shapes = [
        ((nc * block, width), bf16),
        ((nz, deep, 3 * local), bf16),
        ((nz, local, wo.shape[1]), bf16),
        ((nz,) + small.shape, bf16),
        ((nz,) + rank.shape, f32),
        ((nc,) + rank.shape, f32),
        ((2, nc * most, block), bf16),
        ((nc, 2, most, width), bf16),
        ((nz, 2, deep, ffn), bf16),
        ((nz, deep, ffn), bf16),
    ]
    hbm = pl.BlockSpec(memory_space=pl.ANY)
    height = 32
    return pl.pallas_call(
        functools.partial(load_kernel, nz, nc),
        out_shape=[jax.ShapeDtypeStruct(shape, kind) for shape, kind in shapes],
        in_specs=[hbm] * 9,
        out_specs=[pl.BlockSpec(memory_space=pltpu.VMEM)] * 7 + [hbm] * 3,
        scratch_shapes=[
            pltpu.VMEM((nz, rows, width), bf16),
            pltpu.VMEM((2, block, width), bf16),
            pltpu.VMEM((2, nc * most, width), bf16),
            dma((9,)),
            dma((2, nz - 1, 3)), dma((2, nz - 1, 3)), dma((2, nz - 1, 2)), dma((2, nz - 1, 2)),
            dma((nc - 1,)), dma((nc - 1,)), dma((nc - 1,)), dma((nc - 1,)), dma((nc - 1,)), dma((nc - 1,)),
            dma((2,)), dma((2,)), dma((2,)), dma((2, nc - 1)), dma((2, nc - 1)), dma((2,)),
            pltpu.VMEM((2, height, 3, count, ffn), bf16),
            pltpu.VMEM((2, nz, 2, height, ffn), bf16),
            pltpu.VMEM((2, nz, height, ffn), bf16),
            dma((2,)), dma((2,)), dma((2,)),
        ],
        compiler_params=pltpu.CompilerParams(
            collective_id=0, has_side_effects=True, vmem_limit_bytes=48 * 2**20
        ),
    )(tok, cot, wq, wk, wv, wo, small, rank, w_experts)


def dispatch_kernel(
    nz, nc, part, tok, gain, router, kept, pick, third,
    residual, normed, probs, x_in, g_in, third_got,
    sib, rs_send, rs_recv, n_line, g_line, n_two, g_two, x_send, g_send,
    sib_s, sib_r, rs_s, rs_r, line_send, line_recv, keep_sem, give_send, give_recv,
    gkeep_sem, ggive_send, ggive_recv, x_s, x_r, g_s, g_r, own_sem,
    third_s, third_r, third_own,
):
    z, c, t = places()
    f32, bf16 = jnp.float32, jnp.bfloat16
    rows, width = residual.shape
    most = x_in.shape[2]
    greet(nz, nc, True)
    keep_third = pltpu.make_async_copy(third.at[z], third_got.at[z], third_own)
    keep_third.start()

    def third_copy(step, source, target):
        return remote(third.at[target], third_got.at[source], third_s.at[step], third_r.at[step], fsdp=target)

    def sib_copy(q):
        return remote(part.at[q, 1 - t], sib.at[q], sib_s.at[q], sib_r.at[q], tp=1 - t)

    def rs_copy(step, source, target):
        return remote(rs_send.at[step], rs_recv.at[step], rs_s.at[step], rs_r.at[step], ctx=target)

    for step in range(1, nc + 1):
        sib_copy(ring(c, step, nc)).start()
    chunk = 16
    for step in range(1, nc):
        q = ring(c, step, nc)
        sib_copy(q).wait_recv()

        @pl.loop(0, rows // chunk)
        def _(k):
            at = pl.ds(pl.multiple_of(k * chunk, chunk), chunk)
            rs_send[step - 1, at, :] = (part[q, t, at, :].astype(f32) + sib[q, at, :].astype(f32)).astype(bf16)

        rs_copy(step - 1, c, q).start()

    def own_copy(slot, src, dst, k):
        return pltpu.make_async_copy(
            src.at[slot, pl.ds(pl.multiple_of(c * most, 16), most)], dst.at[c, slot], own_sem.at[k, slot]
        )

    sib_copy(c).wait_recv()
    for step in range(1, nc):
        rs_copy(step - 1, c, c).wait_recv()

    @pl.loop(0, rows // chunk)
    def _(k):
        at = pl.ds(pl.multiple_of(k * chunk, chunk), chunk)
        start = pl.ds(pl.multiple_of(t * rows + k * chunk, chunk), chunk)
        total = part[c, t, at, :].astype(f32) + sib[c, at, :].astype(f32)
        for step in range(nc - 1):
            total = total + rs_recv[step, at, :].astype(f32)
        total = total + tok[start, :].astype(f32)
        residual[at, :] = total
        inv = lax.rsqrt(jnp.mean(total * total, -1, keepdims=True) + EPS)
        row = (total * inv * gain[...]).astype(bf16)
        normed[at, :] = row
        n_line[z, at, :] = row

    logits = lax.dot_general(
        normed[...], router[...], (((1,), (1,)), ((), ())), preferred_element_type=f32
    )
    lane = lax.broadcasted_iota(jnp.int32, logits.shape, 1)
    logits = jnp.where(lane < E, logits, -jnp.inf)
    top = jnp.max(logits, -1, keepdims=True)
    raised = jnp.exp(logits - top)
    prob = raised / jnp.sum(raised, -1, keepdims=True)
    probs[...] = prob
    gates = prob * kept[...]
    high = gates.astype(bf16)
    g_line[z, :, pl.ds(0, 128)] = high
    g_line[z, :, pl.ds(128, 128)] = (gates - high.astype(f32)).astype(bf16)

    def arrived(shard):
        regroup(shard, t, rows, n_line, n_two, keep_sem, give_send, give_recv)
        regroup(shard, t, rows, g_line, g_two, gkeep_sem, ggive_send, ggive_recv)

    arrived(z)
    sent = ((x_send, x_in, x_s, x_r), (g_send, g_in, g_s, g_r))

    def near(distance):
        above, below = z + distance, z - distance
        is_above = (above < nz) & (above // 2 == t)
        is_below = (below >= 0) & (below // 2 == t)
        slot = lax.rem(jnp.where(is_above, above, below + 2), 2)

        @pl.when(is_above | is_below)
        def _():
            wait_two(slot, t, rows, n_line, n_two, keep_sem, give_recv)
            wait_two(slot, t, rows, g_line, g_two, gkeep_sem, ggive_recv)
            pick_rows(pick, slot, n_two, x_send)
            pick_rows(pick, slot, g_two, g_send)
            for k, (src, dst, s, r) in enumerate(sent):
                for step in range(1, nc):
                    plane_copy(most, src, dst, s, r, slot, step, c, ring(c, step, nc)).start()
                own_copy(slot, src, dst, k).start()

    line_gather(nz, (n_line, g_line), line_send, line_recv, arrived, None, near)
    near(nz - 1)
    for step in range(1, nz):
        third_copy(step - 1, z, ring(z, step, nz)).start()
    line_sent(nz, (n_line, g_line), line_send, line_recv)
    for slot in range(2):
        wait_given(slot, t, rows, n_line, n_two, give_send, give_recv)
        wait_given(slot, t, rows, g_line, g_two, ggive_send, ggive_recv)
        for k, (src, dst, s, r) in enumerate(sent):
            own_copy(slot, src, dst, k).wait()
            for step in range(1, nc):
                source = ring(c, -step, nc)
                copy = plane_copy(most, src, dst, s, r, slot, step, source, source)
                copy.wait_recv()
                copy.wait_send()
    for step in range(1, nc):
        rs_copy(step - 1, c, c).wait_send()
    for step in range(nc):
        sib_copy(step).wait_send()
    for step in range(1, nz):
        source = ring(z, -step, nz)
        third_copy(step - 1, source, source).wait_recv()
        third_copy(step - 1, source, source).wait_send()
    keep_third.wait()


def dispatch(part, tok, gain, router, kept, pick, third):
    nz, nc = lax.axis_size("fsdp"), lax.axis_size("ctx")
    rows, width = part.shape[2], part.shape[3]
    block = rows * 2
    most = pick.shape[1] // nc
    dma = pltpu.SemaphoreType.DMA
    bf16, f32 = jnp.bfloat16, jnp.float32
    vmem = pl.BlockSpec(memory_space=pltpu.VMEM)
    hbm = pl.BlockSpec(memory_space=pl.ANY)
    return pl.pallas_call(
        functools.partial(dispatch_kernel, nz, nc),
        out_shape=[
            jax.ShapeDtypeStruct((rows, width), f32),
            jax.ShapeDtypeStruct((rows, width), bf16),
            jax.ShapeDtypeStruct((rows, 128), f32),
            jax.ShapeDtypeStruct((nc, 2, most, width), bf16),
            jax.ShapeDtypeStruct((nc, 2, most, 256), bf16),
            jax.ShapeDtypeStruct(third.shape, bf16),
        ],
        in_specs=[vmem] * 6 + [hbm],
        out_specs=[vmem] * 3 + [hbm] * 3,
        scratch_shapes=[
            pltpu.VMEM((nc, rows, width), bf16),
            pltpu.VMEM((nc - 1, rows, width), bf16),
            pltpu.VMEM((nc - 1, rows, width), bf16),
            pltpu.VMEM((nz, rows, width), bf16),
            pltpu.VMEM((nz, rows, 256), bf16),
            pltpu.VMEM((2, block, width), bf16),
            pltpu.VMEM((2, block, 256), bf16),
            pltpu.VMEM((2, nc * most, width), bf16),
            pltpu.VMEM((2, nc * most, 256), bf16),
            dma((nc,)), dma((nc,)), dma((nc - 1,)), dma((nc - 1,)),
            dma((2, nz - 1, 2)), dma((2, nz - 1, 2)),
            dma((2,)), dma((2,)), dma((2,)), dma((2,)), dma((2,)), dma((2,)),
            dma((2, nc - 1)), dma((2, nc - 1)), dma((2, nc - 1)), dma((2, nc - 1)),
            dma((2, 2)),
            dma((nz - 1,)), dma((nz - 1,)), dma,
        ],
        compiler_params=pltpu.CompilerParams(
            collective_id=1, has_side_effects=True, vmem_limit_bytes=56 * 2**20
        ),
    )(part, tok, gain, router, kept, pick, third)


def experts_kernel(
    nz, nc, x_hbm, cot_hbm, gates, pair_hbm, third_hbm, y_hbm, r_hbm, pair_out, hid_hbm, gg_hbm, gu_hbm,
    x, cot, w, weight, pair, gate, up, out_grad, y, r, hid, gg, gu,
    sem, swap_s, swap_r, out_sem, inner_sem,
):
    z, c, t = places()
    f32, bf16 = jnp.float32, jnp.bfloat16
    width, tall = x.shape[1], x.shape[0]
    deep, ffn = w.shape[3], w.shape[4]
    span = 256
    chunk = 288
    copies = [
        pltpu.make_async_copy(cot_hbm, cot, sem.at[0]),
        pltpu.make_async_copy(pair_hbm, w.at[0, :, pl.ds(0, 2)], sem.at[1]),
        pltpu.make_async_copy(x_hbm, x, sem.at[2]),
        pltpu.make_async_copy(third_hbm, w.at[0, :, 2], sem.at[3]),
    ]
    for copy in copies:
        copy.start()
    barrier = pltpu.get_barrier_semaphore()
    pl.semaphore_signal(barrier, inc=1, device_id=dict(tp=1 - t), device_id_type=MESH)
    pl.semaphore_wait(barrier, 1)
    swaps = [
        remote(pair_hbm, w.at[1, :, pl.ds(0, 2)], swap_s.at[0], swap_r.at[0], tp=1 - t),
        remote(third_hbm, w.at[1, :, 2], swap_s.at[1], swap_r.at[1], tp=1 - t),
    ]
    for copy in swaps:
        copy.start()
    pair[...] = jnp.zeros_like(pair)
    lane = lax.broadcasted_iota(jnp.int32, (chunk, 256), 1)
    mine = c * nz + z

    @pl.loop(0, tall // chunk)
    def _(m):
        rows = pl.ds(pl.multiple_of(m * chunk, chunk), chunk)
        value = gates[rows, :].astype(f32)
        value = jnp.where((lane == mine) | (lane == mine + 128), value, 0.0)
        weight[rows, :] = jnp.sum(value, 1, keepdims=True)

    for copy in copies[:2]:
        copy.wait()
    per = ffn // span

    def forward(n):
        half, at = n // per, pl.ds(pl.multiple_of(lax.rem(n, per) * span, span), span)
        full = pl.ds(pl.multiple_of(n * span, span), span)

        def times(rows, k):
            return jnp.dot(rows[...], w[half, :, k, :, at].reshape(width, span), preferred_element_type=f32)

        out_grad[...] = times(cot, 1)

        @pl.when(n == 0)
        def _():
            for copy in copies[2:]:
                copy.wait()

        gate[...] = times(x, 0)
        up[...] = times(x, 2)

        @pl.loop(0, tall // chunk)
        def _(m):
            rows = pl.ds(pl.multiple_of(m * chunk, chunk), chunk)
            g, u, o, k = gate[rows, :], up[rows, :], out_grad[rows, :], weight[rows, :]
            sig = 1.0 / (1.0 + jnp.exp(-g))
            silu = g * sig
            hidden = silu * u
            pair[rows, :] += jnp.sum(hidden.astype(bf16).astype(f32) * o, 1, keepdims=True)
            hid[rows, full] = (k * hidden).astype(bf16)
            o = k * o
            gg[rows, full] = (o * u * sig * (1.0 + g * (1.0 - sig))).astype(bf16)
            gu[rows, full] = (o * silu).astype(bf16)

    pl.loop(0, per)(forward)
    for copy in swaps:
        copy.wait_recv()
    pl.loop(per, 2 * per)(forward)

    @pl.loop(0, tall // chunk)
    def _(m):
        rows = pl.ds(pl.multiple_of(m * chunk, chunk), chunk)
        value = pair[rows, :]
        high = value.astype(bf16).astype(f32)
        out = jnp.where(lane == mine, high, jnp.where(lane == mine + 128, value - high, 0.0))
        pair_out[rows, :] = out.astype(bf16)

    inner = [
        pltpu.make_async_copy(src, dst, inner_sem.at[k])
        for k, (src, dst) in enumerate(((hid, hid_hbm), (gg, gg_hbm), (gu, gu_hbm)))
    ]
    for copy in inner:
        copy.start()
    per_deep = deep // span

    def leave(n):
        full = pl.ds(pl.multiple_of(n * span, span), span)
        return (
            pltpu.make_async_copy(y.at[:, full], y_hbm.at[:, full], out_sem.at[0, n]),
            pltpu.make_async_copy(r.at[:, full], r_hbm.at[:, full], out_sem.at[1, n]),
        )

    @pl.loop(0, width // span)
    def _(n):
        zone, at = n // per_deep, pl.ds(pl.multiple_of(lax.rem(n, per_deep) * span, span), span)
        full = pl.ds(pl.multiple_of(n * span, span), span)

        def back(rows, k):
            total = 0.0
            for half in range(2):
                total = total + lax.dot_general(
                    rows[:, pl.ds(half * ffn, ffn)], w[half, zone, k, at, :], (((1,), (1,)), ((), ())),
                    preferred_element_type=f32,
                )
            return total

        y[:, full] = back(hid, 1).astype(bf16)
        r[:, full] = (back(gg, 0) + back(gu, 2)).astype(bf16)
        for copy in leave(n):
            copy.start()

    for n in range(width // span):
        for copy in leave(n):
            copy.wait()
    for copy in inner:
        copy.wait()
    for copy in swaps:
        copy.wait_send()


def experts(x, cot, gates, pair, third):
    bf16, f32 = jnp.bfloat16, jnp.float32
    nz, nc = lax.axis_size("fsdp"), lax.axis_size("ctx")
    tall, width = x.shape
    deep, ffn = third.shape[1:]
    vmem = pl.BlockSpec(memory_space=pltpu.VMEM)
    hbm = pl.BlockSpec(memory_space=pl.ANY)
    inner = jax.ShapeDtypeStruct((tall, 2 * ffn), bf16)
    dma = pltpu.SemaphoreType.DMA
    return pl.pallas_call(
        functools.partial(experts_kernel, nz, nc),
        out_shape=[
            jax.ShapeDtypeStruct((tall, width), bf16),
            jax.ShapeDtypeStruct((tall, width), bf16),
            jax.ShapeDtypeStruct((tall, 256), bf16),
            inner,
            inner,
            inner,
        ],
        in_specs=[hbm, hbm, vmem, hbm, hbm],
        out_specs=[hbm, hbm, vmem, hbm, hbm, hbm],
        scratch_shapes=[
            pltpu.VMEM((tall, width), bf16),
            pltpu.VMEM((tall, width), bf16),
            pltpu.VMEM((2, nz, 3, deep, ffn), bf16),
            pltpu.VMEM((tall, 1), f32),
            pltpu.VMEM((tall, 1), f32),
            pltpu.VMEM((tall, 256), f32),
            pltpu.VMEM((tall, 256), f32),
            pltpu.VMEM((tall, 256), f32),
            pltpu.VMEM((tall, width), bf16),
            pltpu.VMEM((tall, width), bf16),
            pltpu.VMEM((tall, 2 * ffn), bf16),
            pltpu.VMEM((tall, 2 * ffn), bf16),
            pltpu.VMEM((tall, 2 * ffn), bf16),
            dma((4,)), dma((2,)), dma((2,)), dma((2, width // 256)), dma((3,)),
        ],
        compiler_params=pltpu.CompilerParams(
            collective_id=4, has_side_effects=True, vmem_limit_bytes=60 * 2**20
        ),
    )(x, cot, gates, pair, third)


def place_kernel(nz, nc, gate, rest, out):
    tile = gate.shape[2]
    count = nz * nc
    row = lax.broadcasted_iota(jnp.int32, (tile * count, tile * count), 0)
    column = lax.broadcasted_iota(jnp.int32, (tile * count, tile * count), 1)
    expert = lax.rem(row, count)
    hit = column == (lax.rem(expert, nz) * nc + expert // nz) * tile + row // count
    hit = jnp.where(hit, 1.0, 0.0).astype(jnp.bfloat16)
    for k in range(3):
        early = gate.shape[1]
        value = (gate[:, k] if k < early else rest[:, k - early]).reshape(count * tile, -1)
        value = jnp.dot(hit, value, preferred_element_type=jnp.float32)
        out[:, k] = value.reshape(tile, count, -1)


def lay_out(gate, rest, nz, nc):
    count, _, strip, ffn = gate.shape
    tile = 16
    return pl.pallas_call(
        functools.partial(place_kernel, nz, nc),
        grid=(strip // tile,),
        out_shape=jax.ShapeDtypeStruct((strip, 3, count, ffn), jnp.float32),
        in_specs=[
            pl.BlockSpec((count, src.shape[1], tile, ffn), lambda i: (0, 0, i, 0))
            for src in (gate, rest)
        ],
        out_specs=pl.BlockSpec((tile, 3, count, ffn), lambda i: (i, 0, 0, 0)),
        compiler_params=pltpu.CompilerParams(vmem_limit_bytes=40 * 2**20),
    )(gate, rest)


def collector(nz, nc, pick_t, items, sems):
    z, c, t = places()
    to_s, to_r, own_sem, sib_s, sib_r, line_s, line_r, keep_sem = sems
    rows = items[0][2].shape[1]
    mine_at = pl.ds(pl.multiple_of(t * rows, rows), rows)
    give_at = pl.ds(pl.multiple_of((1 - t) * rows, rows), rows)
    count = len(items)

    def lanes(turn, k):
        wide = items[k][2].shape[-1] // 2
        return pl.ds(turn * wide, wide)

    def to_copy(turn, k, step, source, target):
        src, got = items[k][:2]
        at = lanes(turn, k)
        return remote(
            src.at[target, :, :, at], got.at[source, :, :, at], to_s.at[k, turn, step - 1], to_r.at[k, turn, step - 1],
            ctx=target,
        )

    def own_copy(turn, k):
        src, got = items[k][:2]
        at = lanes(turn, k)
        return pltpu.make_async_copy(src.at[c, :, :, at], got.at[c, :, :, at], own_sem.at[k, turn])

    def sib_copy(turn, k):
        give, sib = items[k][3:5]
        at = lanes(turn, k)
        return remote(give.at[:, :, at], sib.at[:, :, at], sib_s.at[k, turn], sib_r.at[k, turn], tp=1 - t)

    def line_copy(turn, slot, k, half, source, target):
        src = items[k][2 if half == 0 else 4]
        at = lanes(turn, k)
        return remote(
            src.at[slot, :, at], items[k][5].at[source, :, at],
            line_s.at[k, turn, 2 * half + slot], line_r.at[k, turn, source], fsdp=target,
        )

    def keep_copy(turn, slot, k, half):
        src = items[k][2 if half == 0 else 4]
        at = lanes(turn, k)
        return pltpu.make_async_copy(src.at[slot, :, at], items[k][5].at[z, :, at], keep_sem.at[k, turn])

    def goal(slot, half):
        return 2 * (t if half == 0 else 1 - t) + slot

    def forward(turn, k, half):
        for slot in range(2):
            target = goal(slot, half)
            pl.when(target != z)(lambda: line_copy(turn, slot, k, half, z, target).start())
            pl.when(target == z)(lambda: keep_copy(turn, slot, k, half).start())

    def begin(turn):
        for k in range(count):
            for step in range(1, nc):
                to_copy(turn, k, step, c, ring(c, step, nc)).start()
            own_copy(turn, k).start()

    def scatter(turn, slot, k):
        got, mine, give = items[k][1:4]
        wide = mine.shape[-1] // 2
        span = min(wide, 512)
        tall = got.shape[0] * got.shape[2]

        @pl.loop(0, wide // span)
        def _(n):
            at = pl.ds(pl.multiple_of(turn * wide + n * span, span), span)
            pairs = got[:, slot, :, at].reshape(tall, span)
            for picks, out in ((mine_at, mine), (give_at, give)):
                out[slot, :, at] = jnp.dot(
                    pick_t[slot, picks, :], pairs, preferred_element_type=jnp.float32
                ).astype(jnp.bfloat16)

    def process(turn):
        for k in range(count):
            own_copy(turn, k).wait()
            for step in range(1, nc):
                source = ring(c, -step, nc)
                to_copy(turn, k, step, source, c).wait_recv()
            for slot in range(2):
                scatter(turn, slot, k)
            sib_copy(turn, k).start()
            forward(turn, k, 0)
        for k in range(count):
            sib_copy(turn, k).wait_recv()
            forward(turn, k, 1)

    def join():
        for turn in range(2):
            for k in range(count):
                keep_copy(turn, 0, k, 0).wait()
                for step in range(1, nz):
                    line_copy(turn, 0, k, 0, ring(z, -step, nz), z).wait_recv()

    def done():
        for turn in range(2):
            for k in range(count):
                for step in range(1, nc):
                    to_copy(turn, k, step, c, ring(c, step, nc)).wait_send()
                sib_copy(turn, k).wait_send()
                for half in range(2):
                    for slot in range(2):
                        pl.when(goal(slot, half) != z)(
                            lambda: line_copy(turn, slot, k, half, z, goal(slot, half)).wait_send()
                        )

    return begin, process, join, done


def collector_scratch(nz, nc, most, rows, widths):
    dma = pltpu.SemaphoreType.DMA
    bf16 = jnp.bfloat16
    count = len(widths)
    bufs = []
    for w in widths:
        bufs += [pltpu.VMEM((nc, 2, most, w), bf16)]
        bufs += [pltpu.VMEM((2, rows, w), bf16)] * 3
        bufs += [pltpu.VMEM((nz, rows, w), bf16)]
    sems = [
        dma((count, 2, nc - 1)), dma((count, 2, nc - 1)), dma((count, 2)), dma((count, 2)), dma((count, 2)),
        dma((count, 2, 4)), dma((count, 2, nz)), dma((count, 2)),
    ]
    return bufs, sems


def return_kernel(
    nz, nc, r, g, x_hbm, cot_hbm, hid_hbm, gg_hbm, gu_hbm, pick_t, residual, probs, kept, router, gain, cot,
    logits_grad, gain_grad, residual_grad, attn_grad, early_got, own_grad, other_grad,
    x, cot_rows, hid, gg, gu, stage, early, early_sib,
    load_sem, keep_sem, give_sem, got_sem, first_s, first_r, *scratch,
):
    z, c, t = places()
    f32, bf16 = jnp.float32, jnp.bfloat16
    rows, width = residual.shape
    r_line, g_line = scratch[4], scratch[9]
    row_s, row_r, pass_s, pass_r, early_s, early_r, early_own = scratch[18:]
    items = ((r,) + scratch[:5], (g,) + scratch[5:10])
    begin, process, join, done = collector(nz, nc, pick_t, items, scratch[10:18])
    here = z * nc + c
    keep_early = pltpu.make_async_copy(early.at[here], early_got.at[here], early_own)
    loads = [
        pltpu.make_async_copy(src, dst, load_sem.at[k])
        for k, (src, dst) in enumerate(
            ((x_hbm, x), (gg_hbm, gg), (gu_hbm, gu), (cot_hbm, cot_rows), (hid_hbm, hid))
        )
    ]
    for copy in loads:
        copy.start()
    greet(nz, nc, True, True)
    chips = nz * nc
    steps = [(i, j) for i in range(nz) for j in range(nc) if i or j]

    def early_copy(n, source, target, fsdp, ctx):
        return remote(early.at[target], early_got.at[source], early_s.at[n], early_r.at[n], fsdp=fsdp, ctx=ctx)

    begin(0)
    begin(1)
    for copy in loads:
        copy.wait()

    span = 256
    ffn = stage.shape[5]
    strip = stage.shape[4]
    per = span // strip
    bands = width // span

    def flush(n):
        slot = lax.rem(n, 2)
        at = pl.ds(pl.multiple_of(n * per, per), per)
        return (
            pltpu.make_async_copy(stage.at[slot, 0, :, pl.ds(1, 2)], own_grad.at[at], keep_sem.at[slot]),
            remote(stage.at[slot, 1, :, pl.ds(1, 2)], other_grad.at[at], give_sem.at[slot], got_sem, tp=1 - t),
            remote(stage.at[slot, 1, :, 0], early_sib.at[at], first_s.at[slot], first_r, tp=1 - t),
        )

    def flushed(n):
        keep, give, first = flush(n)
        keep.wait()
        give.wait_send()
        first.wait_send()

    @pl.loop(0, bands)
    def _(n):
        full = pl.ds(pl.multiple_of(n * span, span), span)
        slot = lax.rem(n, 2)
        pl.when(n >= 2)(lambda: flushed(n - 2))
        for k, (rows_in, grads) in enumerate(((x, gg), (x, gu), (cot_rows, hid))):
            value = lax.dot_general(
                rows_in[:, full], grads[...], (((0,), (0,)), ((), ())), preferred_element_type=f32
            ).astype(bf16)
            for i in range(per):
                piece = value[i * strip : (i + 1) * strip]
                if k == 0:
                    early[n * per + i] = piece[:, :ffn]
                else:
                    stage[slot, 0, i, k] = piece[:, :ffn]
                stage[slot, 1, i, k] = piece[:, ffn:]
        for copy in flush(n):
            copy.start()

    flushed(bands - 2)
    flushed(bands - 1)
    remote(early_sib, early_sib, first_r, first_r, tp=1 - t).wait_recv()

    @pl.loop(0, chips)
    def _(n):
        early[n] = (early[n].astype(f32) + early_sib[n].astype(f32)).astype(bf16)

    for turn in range(2):
        process(turn)
    join()
    pairs = jnp.zeros((rows, 128), f32)
    for source in range(nz):
        pairs = pairs + g_line[source, :, 0:128].astype(f32) + g_line[source, :, 128:256].astype(f32)
    pairs = pairs * kept[...]
    prob = probs[...]
    grad_logits = (prob * (pairs - jnp.sum(prob * pairs, -1, keepdims=True))).astype(bf16)
    logits_grad[...] = grad_logits
    gain_grad[...] = jnp.zeros_like(gain_grad)
    chunk = 16

    @pl.loop(0, rows // chunk)
    def _(k):
        at = pl.ds(pl.multiple_of(k * chunk, chunk), chunk)
        full = pl.ds(pl.multiple_of(t * rows + k * chunk, chunk), chunk)
        res = residual[at, :]
        grad = r_line[0, at, :].astype(f32)
        for source in range(1, nz):
            grad = grad + r_line[source, at, :].astype(f32)
        grad = grad + jnp.dot(logits_grad[at, :], router[...], preferred_element_type=f32)
        inv = lax.rsqrt(jnp.mean(res * res, -1, keepdims=True) + EPS)
        gain_grad[...] += jnp.sum((grad * res * inv).reshape(chunk // 8, 8, width), 0)
        weighted = grad * gain[...]
        inner = jnp.sum(weighted * res, -1, keepdims=True)
        out = cot[full, :].astype(f32) + inv * weighted - res * (inv * inv * inv) * inner / width
        residual_grad[at, :] = out
        attn_grad[c, t, at, :] = out.astype(bf16)

    def row_copy(step, source, target):
        return remote(attn_grad.at[source, t], attn_grad.at[source, t], row_s.at[step], row_r.at[step], ctx=target)

    def pass_copy(step, source, core):
        return remote(attn_grad.at[source, core], attn_grad.at[source, core], pass_s.at[step], pass_r.at[step], tp=1 - t)

    for step in range(1, nc):
        row_copy(step, c, ring(c, step, nc)).start()
    pass_copy(0, c, t).start()
    keep_early.start()
    for n, (i, j) in enumerate(steps):
        zz, cc = ring(z, i, nz), ring(c, j, nc)
        early_copy(n, here, zz * nc + cc, zz, cc).start()
    for step in range(1, nc):
        source = ring(c, -step, nc)
        row_copy(step, source, source).wait_recv()
        pass_copy(step, source, t).start()
    for step in range(nc):
        source = ring(c, -step, nc)
        pass_copy(step, source, 1 - t).wait_recv()
        pass_copy(step, source, t).wait_send()
        if step:
            row_copy(step, c, source).wait_send()
    done()
    for n, (i, j) in enumerate(steps):
        zz, cc = ring(z, -i, nz), ring(c, -j, nc)
        copy = early_copy(n, zz * nc + cc, zz * nc + cc, zz, cc)
        copy.wait_recv()
        copy.wait_send()
    keep_early.wait()
    remote(other_grad, other_grad, got_sem, got_sem, tp=1 - t).wait_recv()


def give_back(r, g, x, cot_rows, hid, gg, gu, pick_t, residual, probs, kept, router, gain, cot):
    nz, nc = lax.axis_size("fsdp"), lax.axis_size("ctx")
    rows, width = residual.shape
    dma = pltpu.SemaphoreType.DMA
    bf16, f32 = jnp.bfloat16, jnp.float32
    vmem = pl.BlockSpec(memory_space=pltpu.VMEM)
    hbm = pl.BlockSpec(memory_space=pl.ANY)
    bufs, sems = collector_scratch(nz, nc, r.shape[2], rows, (width, 256))
    chips = nz * nc
    strip, ffn = width // chips, hid.shape[1] // 2
    tall = x.shape[0]
    return pl.pallas_call(
        functools.partial(return_kernel, nz, nc),
        out_shape=[
            jax.ShapeDtypeStruct((rows, 128), bf16),
            jax.ShapeDtypeStruct((8, width), f32),
            jax.ShapeDtypeStruct((rows, width), f32),
            jax.ShapeDtypeStruct((nc, 2, rows, width), bf16),
            jax.ShapeDtypeStruct((chips, strip, ffn), bf16),
            jax.ShapeDtypeStruct((chips, 2, strip, ffn), bf16),
            jax.ShapeDtypeStruct((chips, 2, strip, ffn), bf16),
        ],
        in_specs=[hbm] * 7 + [vmem] * 7,
        out_specs=[vmem] * 4 + [hbm] * 3,
        scratch_shapes=[
            pltpu.VMEM((tall, width), bf16),
            pltpu.VMEM((tall, width), bf16),
            pltpu.VMEM((tall, 2 * ffn), bf16),
            pltpu.VMEM((tall, 2 * ffn), bf16),
            pltpu.VMEM((tall, 2 * ffn), bf16),
            pltpu.VMEM((2, 2, 256 // strip, 3, strip, ffn), bf16),
            pltpu.VMEM((chips, strip, ffn), bf16),
            pltpu.VMEM((chips, strip, ffn), bf16),
            dma((5,)), dma((2,)), dma((2,)), dma, dma((2,)), dma,
        ]
        + bufs
        + sems
        + [dma((nc,)), dma((nc,)), dma((nc,)), dma((nc,))]
        + [dma((nz * nc - 1,)), dma((nz * nc - 1,)), dma],
        compiler_params=pltpu.CompilerParams(
            collective_id=2, has_side_effects=True, vmem_limit_bytes=60 * 2**20
        ),
    )(r, g, x, cot_rows, hid, gg, gu, pick_t, residual, probs, kept, router, gain, cot)


def final_kernel(
    nz, nc, part, tok, gain, residual_grad, dw, dwo, small, y, pick_t, residual,
    tokens_grad, dw_out, dwo_out, small_out, layer,
    sib, rs_send, rs_recv, tok_grad, gain_acc, dw_up, dw_down, dwo_up, dwo_down, dw_to, dwo_to,
    dw_next, dwo_next, small_line, small_plane, small_sib, small_a, small_b,
    sib_s, sib_r, rs_s, rs_r, line_s, line_r, to_s, to_r, tg_s, tg_r, sm_s, sm_r, sp_s, sp_r, ss_s, ss_r,
    layer_send, lay_s, lay_r, *scratch,
):
    z, c, t = places()
    f32, bf16 = jnp.float32, jnp.bfloat16
    rows, width = residual_grad.shape
    piece = width // 2
    chunk = 16
    y_line = scratch[4]
    begin, process, join, done = collector(nz, nc, pick_t, ((y,) + scratch[:5],), scratch[5:])
    greet(nz, nc, True)

    bufs = ((dw, dw_up, dw_down), (dwo, dwo_up, dwo_down))
    outs = (dw_next, dwo_next)

    def hop(way, step, k, target):
        src = outs[k].at[way, step]
        return remote(src, bufs[k][1 + way].at[step], line_s.at[way, step, k], line_r.at[way, step, k], fsdp=target)

    def add_to(k, way, step, shard, joined):
        own, out = bufs[k][0], outs[k]
        got = bufs[k][1 + way]
        height = own.shape[2]
        tile = 32

        @pl.loop(0, nc * (height // tile))
        def _(n):
            q, at = n // (height // tile), pl.ds(pl.multiple_of(lax.rem(n, height // tile) * tile, tile), tile)
            value = own[shard, q, at, :]
            if joined:
                value = (value.astype(f32) + got[step, q, at, :].astype(f32)).astype(bf16)
            out[way, step, q, at, :] = value

    def line_one(step, way):
        shard = nz - 1 - step if way == 0 else step
        ahead = z + 1 if way == 0 else z - 1
        behind = z - 1 if way == 0 else z + 1
        first = z == 0 if way == 0 else z == nz - 1
        sends = shard > z if way == 0 else shard < z
        gets = (z > 0) & (shard >= z) if way == 0 else (z < nz - 1) & (shard <= z)

        @pl.when(gets)
        def _():
            for k in range(2):
                hop(way, step, k, behind).wait_recv()

        @pl.when(sends & jnp.logical_not(first))
        def _():
            for k in range(2):
                add_to(k, way, step, shard, True)
                hop(way, step, k, ahead).start()

    def line_step(step):
        @pl.when(2 * z < nz)
        def _():
            line_one(step, 0)
            line_one(step, 1)

        @pl.when(2 * z >= nz)
        def _():
            line_one(step, 1)
            line_one(step, 0)

    def line_begin():
        for way in range(2):
            first = z == 0 if way == 0 else z == nz - 1

            @pl.when(first)
            def _():
                for step in range(nz - 1):
                    shard = nz - 1 - step if way == 0 else step
                    for k in range(2):
                        add_to(k, way, step, shard, False)
                        hop(way, step, k, z + 1 if way == 0 else z - 1).start()

    def sib_copy(q):
        return remote(part.at[q, 1 - t], sib.at[q], sib_s.at[q], sib_r.at[q], tp=1 - t)

    def rs_copy(step, target):
        return remote(rs_send.at[step], rs_recv.at[step], rs_s.at[step], rs_r.at[step], ctx=target)

    for step in range(1, nc + 1):
        sib_copy(ring(c, step, nc)).start()
    line_begin()
    for step in range(1, nc):
        q = ring(c, step, nc)
        sib_copy(q).wait_recv()

        @pl.loop(0, rows // chunk)
        def _(k):
            at = pl.ds(pl.multiple_of(k * chunk, chunk), chunk)
            rs_send[step - 1, at, :] = (part[q, t, at, :].astype(f32) + sib[q, at, :].astype(f32)).astype(bf16)

        rs_copy(step - 1, q).start()
    sib_copy(c).wait_recv()
    begin(0)
    line_step(0)
    begin(1)
    for step in range(1, nc):
        rs_copy(step - 1, c).wait_recv()
    gain_acc[...] = jnp.zeros_like(gain_acc)

    @pl.loop(0, rows // chunk)
    def _(k):
        at = pl.ds(pl.multiple_of(k * chunk, chunk), chunk)
        full = pl.ds(pl.multiple_of(t * rows + k * chunk, chunk), chunk)
        grad = part[c, t, at, :].astype(f32) + sib[c, at, :].astype(f32)
        for step in range(nc - 1):
            grad = grad + rs_recv[step, at, :].astype(f32)
        x = tok[full, :].astype(f32)
        inv = lax.rsqrt(jnp.mean(x * x, -1, keepdims=True) + EPS)
        gain_acc[...] += jnp.sum((grad * x * inv).reshape(chunk // 8, 8, width), 0)
        weighted = grad * gain[...]
        inner = jnp.sum(weighted * x, -1, keepdims=True)
        out = residual_grad[at, :] + inv * weighted - x * (inv * inv * inv) * inner / width
        tok_grad[at, :] = out.astype(bf16)
        tokens_grad[full, :] = out.astype(bf16)

    def grad_copy(core):
        return remote(
            tok_grad, tokens_grad.at[pl.ds(pl.multiple_of(core * rows, rows), rows)], tg_s, tg_r, tp=1 - t
        )

    grad_copy(t).start()

    small_a[...] = small[...]
    total = jnp.sum(gain_acc[...], 0, keepdims=True)
    for strip in range(nz * nc):
        small_a[strip // nc, strip % nc, pl.ds(17, 1), :] = total[:, strip * 128 : (strip + 1) * 128]

    def small_copy(step, shard, target):
        return remote(small_a.at[shard], small_line.at[step], sm_s.at[step], sm_r.at[step], fsdp=target)

    def plane_copy(step, shard, target):
        return remote(small_b.at[shard], small_plane.at[step], sp_s.at[step], sp_r.at[step], ctx=target)

    for step in range(1, nz):
        small_copy(step - 1, ring(z, step, nz), ring(z, step, nz)).start()
    line_step(1)
    process(0)
    line_step(2)
    process(1)
    for step in range(1, nz):
        small_copy(step - 1, z, z).wait_recv()
    value = small_a[z]
    for step in range(nz - 1):
        value = value + small_line[step]
    small_b[...] = value
    for step in range(1, nc):
        plane_copy(step - 1, ring(c, step, nc), ring(c, step, nc)).start()

    def close(k, out, to):
        own, up, down = bufs[k]
        height = own.shape[2]
        tile = 32

        @pl.loop(0, nc * (height // tile))
        def _(n):
            q, at = n // (height // tile), pl.ds(pl.multiple_of(lax.rem(n, height // tile) * tile, tile), tile)
            base = own[z, q, at, :].astype(f32)
            above = up[jnp.minimum(nz - 1 - z, nz - 2), q, at, :].astype(f32)
            below = down[jnp.minimum(z, nz - 2), q, at, :].astype(f32)
            base = base + jnp.where(z > 0, above, 0.0) + jnp.where(z < nz - 1, below, 0.0)
            to[q, at, :] = base.astype(bf16)

    close(0, dw_out, dw_to)
    close(1, dwo_out, dwo_to)

    def to_copy(k, step, source, target):
        src, dst = ((dw_to, dw_out), (dwo_to, dwo_out))[k]
        return remote(src.at[target], dst.at[source], to_s.at[k, step], to_r.at[k, step], ctx=target)

    for step in range(1, nc):
        for k in range(2):
            to_copy(k, step - 1, c, ring(c, step, nc)).start()
    def layer_copy(core):
        return remote(
            layer_send.at[:, pl.ds(pl.multiple_of((1 - t) * piece, piece), piece)],
            layer.at[pl.ds(pl.multiple_of(core * rows, rows), rows)],
            lay_s, lay_r, tp=1 - t,
        )

    join()

    @pl.loop(0, rows // chunk)
    def _(k):
        at = pl.ds(pl.multiple_of(k * chunk, chunk), chunk)
        full = pl.ds(pl.multiple_of(t * rows + k * chunk, chunk), chunk)
        total = residual[at, :]
        for source in range(nz):
            total = total + y_line[source, at, :].astype(f32)
        layer_send[at, :] = total.astype(bf16)
        layer[full, :] = layer_send[at, pl.ds(pl.multiple_of(t * piece, piece), piece)]

    layer_copy(t).start()
    dw_out[c, :, :] = dw_to[c, :, :]
    dwo_out[c, :, :] = dwo_to[c, :, :]
    for step in range(1, nc):
        plane_copy(step - 1, c, c).wait_recv()
    value = small_b[c]
    for step in range(nc - 1):
        value = value + small_plane[step]
    small_out[...] = value
    final = remote(small_out, small_sib, ss_s, ss_r, tp=1 - t)
    final.start()
    final.wait()
    small_out[...] = value + small_sib[...]
    for step in range(1, nc):
        source = ring(c, -step, nc)
        for k in range(2):
            src, dst = ((dw_to, dw_out), (dwo_to, dwo_out))[k]
            remote(
                src.at[c], dst.at[source], to_s.at[k, step - 1], to_r.at[k, step - 1], ctx=source
            ).wait_recv()
    grad_copy(1 - t).wait_recv()
    grad_copy(t).wait_send()
    layer_copy(1 - t).wait_recv()
    layer_copy(t).wait_send()
    done()
    for step in range(1, nc):
        for k in range(2):
            to_copy(k, step - 1, c, ring(c, step, nc)).wait_send()
        plane_copy(step - 1, ring(c, step, nc), ring(c, step, nc)).wait_send()
        rs_copy(step - 1, c).wait_send()
    for step in range(1, nz):
        small_copy(step - 1, ring(z, step, nz), ring(z, step, nz)).wait_send()
    for q in range(nc):
        sib_copy(q).wait_send()
    for step in range(nz - 1):
        for way in range(2):
            shard = nz - 1 - step if way == 0 else step
            ahead = z + 1 if way == 0 else z - 1
            sends = shard > z if way == 0 else shard < z

            @pl.when(sends)
            def _():
                for k in range(2):
                    hop(way, step, k, ahead).wait_send()


def finish(part, tok, gain, residual_grad, dw, dwo, small, y, pick_t, residual):
    nz, nc = lax.axis_size("fsdp"), lax.axis_size("ctx")
    rows, width = residual_grad.shape
    dma = pltpu.SemaphoreType.DMA
    bf16, f32 = jnp.bfloat16, jnp.float32
    vmem = pl.BlockSpec(memory_space=pltpu.VMEM)
    one, two = dw.shape[1:], dwo.shape[1:]
    bufs, sems = collector_scratch(nz, nc, y.shape[2], rows, (width,))
    tiny = small.shape[2:]
    return pl.pallas_call(
        functools.partial(final_kernel, nz, nc),
        out_shape=[
            jax.ShapeDtypeStruct((2 * rows, width), bf16),
            jax.ShapeDtypeStruct(one, bf16),
            jax.ShapeDtypeStruct(two, bf16),
            jax.ShapeDtypeStruct(tiny, f32),
            jax.ShapeDtypeStruct((2 * rows, width // 2), bf16),
        ],
        in_specs=[vmem] * 7 + [pl.BlockSpec(memory_space=pl.ANY)] + [vmem] * 2,
        out_specs=[vmem] * 5,
        scratch_shapes=[
            pltpu.VMEM((nc, rows, width), bf16),
            pltpu.VMEM((nc - 1, rows, width), bf16),
            pltpu.VMEM((nc - 1, rows, width), bf16),
            pltpu.VMEM((rows, width), bf16),
            pltpu.VMEM((8, width), f32),
            pltpu.VMEM((nz - 1,) + one, bf16),
            pltpu.VMEM((nz - 1,) + one, bf16),
            pltpu.VMEM((nz - 1,) + two, bf16),
            pltpu.VMEM((nz - 1,) + two, bf16),
            pltpu.VMEM(one, bf16),
            pltpu.VMEM(two, bf16),
            pltpu.VMEM((2, nz - 1) + one, bf16),
            pltpu.VMEM((2, nz - 1) + two, bf16),
            pltpu.VMEM((nz - 1,) + small.shape[1:], f32),
            pltpu.VMEM((nc - 1,) + tiny, f32),
            pltpu.VMEM(tiny, f32),
            pltpu.VMEM(small.shape, f32),
            pltpu.VMEM(small.shape[1:], f32),
            dma((nc,)), dma((nc,)), dma((nc - 1,)), dma((nc - 1,)),
            dma((2, nz - 1, 2)), dma((2, nz - 1, 2)),
            dma((2, nc - 1)), dma((2, nc - 1)), dma, dma,
            dma((nz - 1,)), dma((nz - 1,)), dma((nc - 1,)), dma((nc - 1,)), dma, dma,
            pltpu.VMEM((rows, width), bf16), dma, dma,
        ] + bufs + sems,
        compiler_params=pltpu.CompilerParams(
            collective_id=3, has_side_effects=True, vmem_limit_bytes=60 * 2**20
        ),
    )(part, tok, gain, residual_grad, dw, dwo, small, y, pick_t, residual)


def one_chip(
    tokens,
    w_query,
    w_key,
    w_value,
    w_out,
    gain_attn,
    gain_query,
    gain_key,
    gain_moe,
    w_router,
    w_experts,
    routes,
    cotangent,
):
    z, c, t = lax.axis_index("fsdp"), lax.axis_index("ctx"), lax.axis_index("tp")
    nz, nc = lax.axis_size("fsdp"), lax.axis_size("ctx")
    block, width = tokens.shape[1], tokens.shape[2]
    rows = block // 2
    tall = block * nc
    deep = width // nz
    ffn = w_experts.shape[3]
    most = block * TOPK * 9 // (8 * E)
    bf16, f32 = jnp.bfloat16, jnp.float32

    token_half = lax.dynamic_slice_in_dim(tokens[0], t * rows, rows, 0)
    cotan_half = lax.dynamic_slice_in_dim(cotangent[0], t * rows, rows, 0)
    local = w_query.shape[1] // nc
    small = jnp.concatenate([w_router.T.reshape(-1), gain_attn, gain_moe, gain_query, gain_key])
    total = small.shape[0]
    small = jnp.pad(small, (0, -total % 2048))
    small = small.reshape(-1, 128)
    ids = jnp.arange(E, dtype=jnp.int32)
    named = jnp.any(routes[0][:, :, None] == ids, 1)
    below = jnp.tril(jnp.ones((block, block), bf16), -1)
    rank = jnp.where(named, dot(below, named.astype(bf16)), -1.0).T
    x_rows, w_qkv, w_o, small, _, rank_seq, pick, cot_rows, pair, third = load(
        tokens[0], cotangent[0], w_query, w_key, w_value, w_out, small, rank, w_experts, most
    )
    w_qkv = w_qkv.reshape(width, 3 * local)
    w_o = w_o.transpose(1, 0, 2).reshape(local, width)
    small = small.reshape(nz, -1)
    router = small[:, : E * deep].reshape(nz, E, deep).transpose(1, 0, 2).reshape(E, width)
    at = E * deep
    attn_gain = small[:, at : at + deep].reshape(-1).astype(f32)
    moe_gain = small[:, at + deep : at + 2 * deep].reshape(-1).astype(f32)
    at, part = at + 2 * deep, HD // nz
    query_gain = small[:, at : at + part].reshape(-1).astype(f32)
    key_gain = small[:, at + part : at + 2 * part].reshape(-1).astype(f32)

    pair = exchange(pair, "fsdp")

    counts = jnp.sum((rank_seq >= 0).astype(f32), 2)
    earlier = jnp.sum(jnp.where(jnp.arange(nc)[:, None] < c, counts, 0.0), 0)
    kept = ((rank >= 0) & (rank + earlier[:, None] < CAP)).astype(f32).T
    kept = lax.dynamic_slice_in_dim(kept, t * rows, rows, 0)

    x_rows = x_rows.astype(f32)
    place = jnp.arange(tall, dtype=jnp.int32)
    half_dim = HD // 2
    inv_freq = jnp.exp(jnp.arange(half_dim, dtype=f32) * (-2.0 * math.log(ROPE_BASE) / HD))
    angles = place.astype(f32)[:, None] * inv_freq[None, :]
    cos_full = jnp.concatenate([jnp.cos(angles)] * 2, -1)[:, None, :]
    sin_full = jnp.concatenate([jnp.sin(angles)] * 2, -1)[:, None, :]
    normed_one = (x_rows * rms_scale(x_rows) * attn_gain).astype(bf16)
    proj = dot(normed_one, w_qkv).reshape(tall, 3, local // HD, HD)
    query_heads, key_heads = proj[:, 0], proj[:, 1]
    values = proj[:, 2].astype(bf16)
    query_inv, key_inv = rms_scale(query_heads), rms_scale(key_heads)
    queries = apply_rope(query_heads * query_inv * query_gain, cos_full, sin_full).astype(bf16)
    keys = apply_rope(key_heads * key_inv * key_gain, cos_full, sin_full).astype(bf16)
    score_scale = 1.0 / math.sqrt(HD)
    scores = jnp.einsum("qhd,khd->hqk", queries, keys, preferred_element_type=f32) * score_scale
    maximum = jnp.max(scores, -1, keepdims=True)
    exp_scores = jnp.exp(scores - maximum)
    denominator = jnp.sum(exp_scores, -1, keepdims=True)
    attn_probs = exp_scores / denominator
    log_total = maximum + jnp.log(denominator)
    context = jnp.einsum("hqk,khd->qhd", attn_probs.astype(bf16), values, preferred_element_type=f32)
    context = context.astype(bf16).reshape(tall, local)
    attn_part = dot(context, w_o).astype(bf16).reshape(nc, 2, rows, width)
    kept_wide = jnp.pad(kept, ((0, 0), (0, 128 - E)))
    router_wide = jnp.pad(router, ((0, 128 - E), (0, 0)))
    residual, normed_two, router_probs, x_in, g_in, third = dispatch(
        attn_part, tokens[0], moe_gain[None], router_wide, kept_wide, pick, third
    )
    pair, x_in = lax.optimization_barrier((pair, x_in))
    x_in = x_in.reshape(nc * 2 * most, width)
    cot_rows = cot_rows.reshape(nc * 2 * most, width)
    chips = nz * nc
    strip = width // chips
    out_rows, back_rows, pair_rows, hid, gg, gu = experts(
        x_in, cot_rows, g_in.reshape(nc * 2 * most, -1), pair, third
    )
    shape = (nc, 2, most, -1)
    pick_t = pick.transpose(0, 2, 1)
    grad_logits, dgain_moe, grad_residual, grad_attn, dw_gate, own_grad, other_grad = give_back(
        back_rows.reshape(shape),
        pair_rows.reshape(shape),
        x_in,
        cot_rows,
        hid,
        gg,
        gu,
        pick_t,
        residual,
        router_probs,
        kept_wide,
        router_wide,
        moe_gain[None],
        cotangent[0],
    )

    dw_router = dot_tn(normed_two, grad_logits[:, :E])
    dgain_moe = jnp.sum(dgain_moe, 0)
    dw_rest = (own_grad.astype(f32) + other_grad.astype(f32)).astype(bf16)
    dw_rest, grad_attn = lax.optimization_barrier((dw_rest, grad_attn))
    dw_rest = exchange(dw_rest, ("fsdp", "ctx"))
    grad_attn = grad_attn.reshape(tall, width)

    dw_out = dot_tn(context, grad_attn).astype(bf16)
    grad_context = dot_nt(grad_attn, w_o).astype(bf16).reshape(tall, -1, HD)
    scores = jnp.einsum("qhd,khd->hqk", queries, keys, preferred_element_type=f32) * score_scale
    attn_probs = jnp.exp(scores - log_total)
    grad_probs = jnp.einsum("qhd,khd->hqk", grad_context, values, preferred_element_type=f32)
    grad_scores = attn_probs * (grad_probs - jnp.sum(attn_probs * grad_probs, -1, keepdims=True))
    grad_scores = grad_scores.astype(bf16)
    grad_queries = jnp.einsum("hqk,khd->qhd", grad_scores, keys, preferred_element_type=f32) * score_scale
    grad_keys = jnp.einsum("hqk,qhd->khd", grad_scores, queries, preferred_element_type=f32) * score_scale
    grad_values = jnp.einsum(
        "hqk,qhd->khd", attn_probs.astype(bf16), grad_context, preferred_element_type=f32
    ).astype(bf16)
    grad_qnormed = rope_back(grad_queries, cos_full, sin_full)
    grad_knormed = rope_back(grad_keys, cos_full, sin_full)
    dgain_query = jnp.sum(grad_qnormed * query_heads * query_inv, (0, 1))
    dgain_key = jnp.sum(grad_knormed * key_heads * key_inv, (0, 1))
    grad_qproj = norm_back(grad_qnormed, query_heads, query_inv, query_gain).astype(bf16)
    grad_kproj = norm_back(grad_knormed, key_heads, key_inv, key_gain).astype(bf16)
    grad_proj = jnp.stack([grad_qproj, grad_kproj, grad_values], 1).reshape(tall, 3 * local)
    dw_qkv = dot_tn(normed_one, grad_proj).astype(bf16)
    grad_normed_part = dot_nt(grad_proj, w_qkv).astype(bf16).reshape(nc, 2, rows, width)
    head_part = HD // chips
    heads = [dgain_query.reshape(chips, 1, head_part), dgain_key.reshape(chips, 1, head_part)]
    heads = jnp.pad(jnp.concatenate(heads, 2), ((0, 0), (0, 0), (0, strip - 2 * head_part)))
    sums = jnp.concatenate(
        [
            dw_router.reshape(chips, E, strip),
            dgain_moe.reshape(chips, 1, strip),
            jnp.zeros((chips, 1, strip), f32),
            heads,
            jnp.zeros((chips, 24 - E - 3, strip), f32),
        ],
        1,
    ).reshape(nz, nc, 24, strip)
    tokens_grad, got_qkv, got_out, sums, layer_out = finish(
        grad_normed_part,
        tokens[0],
        attn_gain[None],
        grad_residual,
        dw_qkv.reshape(nz, nc, strip, 3 * local),
        dw_out.reshape(local, nz, nc, strip).transpose(1, 2, 0, 3),
        sums,
        out_rows.reshape(shape),
        pick_t,
        residual,
    )
    dw_experts = lay_out(dw_gate[:, None], dw_rest, nz, nc)
    got_qkv = got_qkv.astype(f32).reshape(nc, strip, 3, local)
    got_qkv = got_qkv.transpose(2, 1, 0, 3).reshape(3, strip, nc * local)
    return (
        layer_out[None],
        tokens_grad[None],
        got_qkv[0],
        got_qkv[1],
        got_qkv[2],
        got_out.astype(f32).reshape(nc * local, strip),
        sums[E + 1],
        sums[E + 2, :head_part],
        sums[E + 2, head_part : 2 * head_part],
        sums[E],
        sums[:E].reshape(strip, E),
        dw_experts,
    )


def solution(mesh):
    chips = mesh.shape["fsdp"] * mesh.shape["ctx"]
    plain = chips == E and mesh.shape["fsdp"] == 4 and mesh.shape["tp"] == 2
    return jax.shard_map(
        one_chip if plain else general,
        mesh=mesh,
        in_specs=(
            P("fsdp", "ctx", None),
            P("fsdp", "tp"),
            P("fsdp", "tp"),
            P("fsdp", "tp"),
            P("tp", "fsdp"),
            P("fsdp"),
            P("fsdp"),
            P("fsdp"),
            P("fsdp"),
            P("fsdp", None),
            P("fsdp", None, None, "tp"),
            P("fsdp", "ctx", None),
            P("fsdp", "ctx", None),
        ),
        out_specs=(
            P("fsdp", "ctx", "tp"),
            P("fsdp", "ctx", None),
            P(("fsdp", "ctx"), "tp"),
            P(("fsdp", "ctx"), "tp"),
            P(("fsdp", "ctx"), "tp"),
            P("tp", ("fsdp", "ctx")),
            P(("fsdp", "ctx")),
            P(("fsdp", "ctx")),
            P(("fsdp", "ctx")),
            P(("fsdp", "ctx")),
            P(("fsdp", "ctx"), None),
            P(("fsdp", "ctx"), None, None, "tp"),
        ),
        check_vma=False,
    )
```

```python
import functools
import math

import jax
import jax.numpy as jnp
from jax import lax
from jax.experimental import pallas as pl
from jax.experimental.pallas import tpu as pltpu
from jax.sharding import PartitionSpec as P

HD = 128
TOPK = 8
E = 16
CAP = 512
MESH = pl.DeviceIdType.MESH


EPS = 1e-06
ROPE_BASE = 10000.0


def prefix(value, axis, join, neutral):
    count, mine = (lax.axis_size(axis), lax.axis_index(axis))
    pieces = lax.all_gather(value, axis)
    running = jnp.full_like(value, 0) + jnp.asarray(neutral, value.dtype)

    def lap(position, running):
        longer = join(running, pieces[position])
        return jnp.where(position < mine, longer, running)

    return lax.fori_loop(0, count - 1, lap, running)


def rms_scale(values):
    return lax.rsqrt(jnp.mean(values * values, -1, keepdims=True) + EPS)


def norm_back(grad_normed, values, inv_rms, gain_vec):
    weighted = grad_normed * gain_vec.astype(jnp.float32)
    inner_sum = jnp.sum(weighted * values, -1, keepdims=True)
    return (
        inv_rms * weighted - values * (inv_rms * inv_rms * inv_rms) * inner_sum / values.shape[-1]
    )


def rope_tables(first, length):
    half_dim = HD // 2
    inv_freq = jnp.exp(jnp.arange(half_dim, dtype=jnp.float32) * (-2.0 * math.log(ROPE_BASE) / HD))
    places = (first + jnp.arange(length, dtype=jnp.int32)).astype(jnp.float32)
    angles = places[:, None] * inv_freq[None, :]
    cos_table = jnp.cos(angles)
    sin_table = jnp.sin(angles)
    cos_full = jnp.concatenate([cos_table, cos_table], -1)[:, None, :]
    sin_full = jnp.concatenate([sin_table, sin_table], -1)[:, None, :]
    return (cos_full, sin_full)


def rotate(values):
    half_dim = values.shape[-1] // 2
    return jnp.concatenate([-values[..., half_dim:], values[..., :half_dim]], -1)


def rotate_back(values):
    half_dim = values.shape[-1] // 2
    return jnp.concatenate([values[..., half_dim:], -values[..., :half_dim]], -1)


def apply_rope(values, cos_full, sin_full):
    return values * cos_full + rotate(values) * sin_full


def rope_back(grads, cos_full, sin_full):
    return grads * cos_full + rotate_back(grads * sin_full)


def add_counts(earlier, later):
    return earlier + later


def general(
    tokens,
    w_query,
    w_key,
    w_value,
    w_out,
    gain_attn,
    gain_query,
    gain_key,
    gain_moe,
    w_router,
    w_experts,
    routes,
    cotangent,
):
    seq_count, block_len, model_width = tokens.shape
    row_count = seq_count * block_len
    (
        full_query,
        full_key,
        full_value,
        full_out,
        router_full,
        attn_gain,
        query_gain,
        key_gain,
        moe_gain,
    ) = (
        lax.all_gather(w_query, "fsdp", axis=0, tiled=True),
        lax.all_gather(w_key, "fsdp", axis=0, tiled=True),
        lax.all_gather(w_value, "fsdp", axis=0, tiled=True),
        lax.all_gather(w_out, "fsdp", axis=1, tiled=True),
        lax.all_gather(w_router, "fsdp", axis=0, tiled=True),
        lax.all_gather(gain_attn, "fsdp", axis=0, tiled=True),
        lax.all_gather(gain_query, "fsdp", axis=0, tiled=True),
        lax.all_gather(gain_key, "fsdp", axis=0, tiled=True),
        lax.all_gather(gain_moe, "fsdp", axis=0, tiled=True),
    )
    local_width = full_query.shape[1]
    head_count = local_width // HD
    head_shape = (seq_count, block_len, head_count, HD)
    token_rows = tokens.reshape(row_count, model_width).astype(jnp.float32)
    inv_one = rms_scale(token_rows)
    normed_one = (token_rows * inv_one * attn_gain.astype(jnp.float32)).astype(jnp.bfloat16)
    query_proj = jnp.dot(normed_one, full_query, preferred_element_type=jnp.float32)
    key_proj = jnp.dot(normed_one, full_key, preferred_element_type=jnp.float32)
    value_proj = jnp.dot(normed_one, full_value, preferred_element_type=jnp.float32)
    cos_full, sin_full = rope_tables(lax.axis_index("ctx") * block_len, block_len)
    query_heads = query_proj.reshape(head_shape)
    key_heads = key_proj.reshape(head_shape)
    query_inv = rms_scale(query_heads)
    key_inv = rms_scale(key_heads)
    queries = apply_rope(
        query_heads * query_inv * query_gain.astype(jnp.float32), cos_full, sin_full
    ).astype(jnp.bfloat16)
    keys_local = apply_rope(
        key_heads * key_inv * key_gain.astype(jnp.float32), cos_full, sin_full
    ).astype(jnp.bfloat16)
    keys_local = keys_local.reshape(seq_count, block_len, local_width)
    values_local = value_proj.astype(jnp.bfloat16).reshape(seq_count, block_len, local_width)
    keys_all, values_all = (
        lax.all_gather(keys_local, "ctx", axis=1, tiled=True),
        lax.all_gather(values_local, "ctx", axis=1, tiled=True),
    )
    seq_len = keys_all.shape[1]
    key_rows = keys_all.reshape(seq_count, seq_len, head_count, HD)
    value_rows = values_all.reshape(seq_count, seq_len, head_count, HD)
    score_scale = 1.0 / math.sqrt(HD)
    scores = (
        jnp.einsum("sqhd,skhd->shqk", queries, key_rows, preferred_element_type=jnp.float32)
        * score_scale
    )
    maximum = jnp.max(scores, -1, keepdims=True)
    exp_scores = jnp.exp(scores - maximum)
    denominator = jnp.sum(exp_scores, -1, keepdims=True)
    attn_probs = exp_scores / denominator
    log_total = maximum + jnp.log(denominator)
    context = jnp.einsum(
        "shqk,skhd->sqhd",
        attn_probs.astype(jnp.bfloat16),
        value_rows,
        preferred_element_type=jnp.float32,
    )
    context = context.astype(jnp.bfloat16).reshape(row_count, local_width)
    attn_part = jnp.dot(context, full_out, preferred_element_type=jnp.float32)
    residual = token_rows + lax.psum(attn_part, "tp")
    inv_two = rms_scale(residual)
    normed_two = (residual * inv_two * moe_gain.astype(jnp.float32)).astype(jnp.bfloat16)
    logits = jnp.dot(normed_two, router_full, preferred_element_type=jnp.float32)
    router_probs = jax.nn.softmax(logits, -1)
    pair_count = block_len * TOPK
    route_rows = routes.reshape(seq_count, pair_count)
    expert_ids = jnp.arange(E, dtype=jnp.int32)
    onehot = (route_rows[:, :, None] == expert_ids[None, None, :]).astype(jnp.int32)
    counts = jnp.sum(onehot, 1, dtype=jnp.int32)
    offsets = prefix(counts, "ctx", add_counts, jnp.zeros_like(counts))
    earlier = jnp.cumsum(onehot, 1, dtype=jnp.int32) - onehot
    local_rank = jnp.sum(earlier * onehot, 2, dtype=jnp.int32)
    slot_base = jnp.sum(onehot * offsets[:, None, :], 2, dtype=jnp.int32)
    kept_mask = (slot_base + local_rank < CAP).astype(jnp.float32).reshape(row_count, TOPK)
    block_most = pair_count * 9 // (8 * E)
    expert_span = seq_count * block_most
    seq_ids = jnp.arange(seq_count, dtype=jnp.int32)[:, None]
    buffer_row = (route_rows * expert_span + seq_ids * block_most + local_rank).reshape(
        row_count * TOPK
    )
    token_ids = (
        seq_ids * block_len + jnp.arange(pair_count, dtype=jnp.int32)[None, :] // TOPK
    ).reshape(row_count * TOPK)
    owner_rows = jnp.zeros((E * expert_span,), jnp.int32).at[buffer_row].set(token_ids)
    onehot_f = onehot.astype(jnp.float32).reshape(row_count, TOPK, E)
    gate_weight = jnp.sum(onehot_f * router_probs[:, None, :], 2) * kept_mask
    slot_weight = (
        jnp.zeros((E * expert_span,), jnp.float32)
        .at[buffer_row]
        .set(gate_weight.reshape(row_count * TOPK))
    )
    expert_rows = normed_two[owner_rows].reshape(E, expert_span, model_width)
    cotan_rows = cotangent.reshape(row_count, model_width)
    grad_expert = (slot_weight[:, None] * cotan_rows[owner_rows].astype(jnp.float32)).astype(
        jnp.bfloat16
    )
    grad_expert = grad_expert.reshape(E, expert_span, model_width)
    ffn_local = w_experts.shape[3]
    fsdp_count = lax.axis_size("fsdp")
    ctx_count = lax.axis_size("ctx")
    group_count = fsdp_count * ctx_count
    sharing = group_count // E
    padded_span = -(-expert_span // sharing) * sharing
    part_span = padded_span // sharing
    target_experts = (
        jnp.arange(fsdp_count, dtype=jnp.int32) * ctx_count + lax.axis_index("ctx")
    ) // sharing
    selected = jnp.take(w_experts, target_experts, axis=2)
    owned = lax.all_to_all(selected, "fsdp", split_axis=2, concat_axis=0, tiled=True)[:, :, 0]
    send_rows = expert_rows.reshape(group_count, part_span, model_width)
    send_grads = grad_expert.reshape(group_count, part_span, model_width)
    recv_rows, recv_grads = (
        lax.all_to_all(send_rows, ("fsdp", "ctx"), split_axis=0, concat_axis=0, tiled=True),
        lax.all_to_all(send_grads, ("fsdp", "ctx"), split_axis=0, concat_axis=0, tiled=True),
    )
    rows_flat = recv_rows.reshape(group_count * part_span, model_width)
    grads_flat = recv_grads.reshape(group_count * part_span, model_width)
    gate_act = jnp.dot(rows_flat, owned[:, 0], preferred_element_type=jnp.float32)
    up_act = jnp.dot(rows_flat, owned[:, 1], preferred_element_type=jnp.float32)
    sigmoid_gate = jax.nn.sigmoid(gate_act)
    silu_gate = gate_act * sigmoid_gate
    hidden = (silu_gate * up_act).astype(jnp.bfloat16)
    produced = jnp.einsum("mf,df->md", hidden, owned[:, 2], preferred_element_type=jnp.float32)
    grad_hidden = jnp.dot(grads_flat, owned[:, 2], preferred_element_type=jnp.float32)
    grad_gate = (
        grad_hidden * up_act * sigmoid_gate * (1.0 + gate_act * (1.0 - sigmoid_gate))
    ).astype(jnp.bfloat16)
    grad_up = (grad_hidden * silu_gate).astype(jnp.bfloat16)
    rows_grad = jnp.einsum("mf,df->md", grad_gate, owned[:, 0], preferred_element_type=jnp.float32)
    rows_grad = rows_grad + jnp.einsum(
        "mf,df->md", grad_up, owned[:, 1], preferred_element_type=jnp.float32
    )
    back_out, back_rows = (
        lax.all_to_all(
            produced.reshape(group_count, part_span, model_width).astype(jnp.bfloat16),
            ("fsdp", "ctx"),
            split_axis=0,
            concat_axis=0,
            tiled=True,
        ).astype(jnp.float32),
        lax.all_to_all(
            rows_grad.reshape(group_count, part_span, model_width).astype(jnp.bfloat16),
            ("fsdp", "ctx"),
            split_axis=0,
            concat_axis=0,
            tiled=True,
        ).astype(jnp.float32),
    )
    expert_out = back_out.reshape(E, padded_span, model_width)
    grad_rows = back_rows.reshape(E, padded_span, model_width)
    gate_term = jnp.einsum("md,mf->df", rows_flat, grad_gate, preferred_element_type=jnp.float32)
    up_term = jnp.einsum("md,mf->df", rows_flat, grad_up, preferred_element_type=jnp.float32)
    down_term = jnp.einsum("md,mf->df", grads_flat, hidden, preferred_element_type=jnp.float32)
    owner_terms = jnp.stack([gate_term, up_term, down_term], 1)[:, :, None, :]
    relaid = lax.all_to_all(
        owner_terms.astype(jnp.bfloat16), ("fsdp", "ctx"), split_axis=0, concat_axis=2, tiled=True
    ).astype(owner_terms.dtype)
    dw_experts = jnp.sum(relaid.reshape(relaid.shape[0], 3, E, sharing, ffn_local), 3)
    picked = expert_out.reshape(E * expert_span, model_width)[buffer_row].reshape(
        row_count, TOPK, model_width
    )
    moe_part = jnp.sum(gate_weight[:, :, None] * picked, 1)
    cotan_float = cotan_rows.astype(jnp.float32)
    grad_gate_part = jnp.sum(picked * cotan_float[:, None, :], 2)
    moe_shard = lax.psum_scatter(
        moe_part.astype(jnp.bfloat16), "tp", scatter_dimension=1, tiled=True
    ).astype(jnp.float32)
    piece_width = moe_shard.shape[1]
    residual_shard = lax.dynamic_slice_in_dim(
        residual, lax.axis_index("tp") * piece_width, piece_width, 1
    )
    layer_out = (
        (residual_shard + moe_shard).astype(jnp.bfloat16).reshape(seq_count, block_len, piece_width)
    )
    grad_normed_part = jnp.sum(
        grad_rows.reshape(E * expert_span, model_width)[buffer_row].reshape(
            row_count, TOPK, model_width
        ),
        1,
    )
    grad_normed_sum, grad_gate_sum = (
        lax.psum(grad_normed_part.astype(jnp.bfloat16), "tp").astype(jnp.float32),
        lax.psum(grad_gate_part.astype(jnp.bfloat16), "tp").astype(jnp.float32),
    )
    grad_pick = grad_gate_sum * kept_mask
    grad_router_probs = jnp.sum(onehot_f * grad_pick[:, :, None], 1)
    grad_logits = router_probs * (
        grad_router_probs - jnp.sum(router_probs * grad_router_probs, -1, keepdims=True)
    )
    grad_logits = grad_logits.astype(jnp.bfloat16)
    grad_router_w = jnp.einsum(
        "nd,ne->de", normed_two, grad_logits, preferred_element_type=jnp.float32
    )
    grad_normed_two = grad_normed_sum + jnp.einsum(
        "ne,de->nd", grad_logits, router_full, preferred_element_type=jnp.float32
    )
    grad_moe_gain = jnp.sum(grad_normed_two * residual * inv_two, 0)
    grad_residual = cotan_float + norm_back(grad_normed_two, residual, inv_two, moe_gain)
    grad_attn = grad_residual.astype(jnp.bfloat16)
    grad_w_out = jnp.einsum("nl,nd->ld", context, grad_attn, preferred_element_type=jnp.float32)
    grad_context = jnp.einsum("nd,ld->nl", grad_attn, full_out, preferred_element_type=jnp.float32)
    grad_context = grad_context.astype(jnp.bfloat16).reshape(head_shape)
    scores = (
        jnp.einsum("sqhd,skhd->shqk", queries, key_rows, preferred_element_type=jnp.float32)
        * score_scale
    )
    attn_probs = jnp.exp(scores - log_total)
    grad_probs = jnp.einsum(
        "sqhd,skhd->shqk", grad_context, value_rows, preferred_element_type=jnp.float32
    )
    grad_scores = attn_probs * (grad_probs - jnp.sum(attn_probs * grad_probs, -1, keepdims=True))
    grad_scores = grad_scores.astype(jnp.bfloat16)
    grad_queries = (
        jnp.einsum("shqk,skhd->sqhd", grad_scores, key_rows, preferred_element_type=jnp.float32)
        * score_scale
    )
    grad_keys_all = (
        jnp.einsum("shqk,sqhd->skhd", grad_scores, queries, preferred_element_type=jnp.float32)
        * score_scale
    )
    grad_values_all = jnp.einsum(
        "shqk,sqhd->skhd",
        attn_probs.astype(jnp.bfloat16),
        grad_context,
        preferred_element_type=jnp.float32,
    )
    grad_keys_own, grad_values_own = (
        lax.psum_scatter(
            grad_keys_all.reshape(seq_count, seq_len, local_width).astype(jnp.bfloat16),
            "ctx",
            scatter_dimension=1,
            tiled=True,
        ).astype(jnp.float32),
        lax.psum_scatter(
            grad_values_all.reshape(seq_count, seq_len, local_width).astype(jnp.bfloat16),
            "ctx",
            scatter_dimension=1,
            tiled=True,
        ).astype(jnp.float32),
    )
    grad_qnormed = rope_back(grad_queries, cos_full, sin_full)
    grad_knormed = rope_back(grad_keys_own.reshape(head_shape), cos_full, sin_full)
    grad_qgain = jnp.sum(grad_qnormed * query_heads * query_inv, (0, 1, 2))
    grad_kgain = jnp.sum(grad_knormed * key_heads * key_inv, (0, 1, 2))
    grad_qproj = (
        norm_back(grad_qnormed, query_heads, query_inv, query_gain)
        .astype(jnp.bfloat16)
        .reshape(row_count, local_width)
    )
    grad_kproj = (
        norm_back(grad_knormed, key_heads, key_inv, key_gain)
        .astype(jnp.bfloat16)
        .reshape(row_count, local_width)
    )
    grad_vproj = grad_values_own.astype(jnp.bfloat16).reshape(row_count, local_width)
    grad_wq = jnp.einsum("nd,nl->dl", normed_one, grad_qproj, preferred_element_type=jnp.float32)
    grad_wk = jnp.einsum("nd,nl->dl", normed_one, grad_kproj, preferred_element_type=jnp.float32)
    grad_wv = jnp.einsum("nd,nl->dl", normed_one, grad_vproj, preferred_element_type=jnp.float32)
    grad_normed_one = jnp.einsum(
        "nl,dl->nd", grad_qproj, full_query, preferred_element_type=jnp.float32
    )
    grad_normed_one = grad_normed_one + jnp.einsum(
        "nl,dl->nd", grad_kproj, full_key, preferred_element_type=jnp.float32
    )
    grad_normed_one = grad_normed_one + jnp.einsum(
        "nl,dl->nd", grad_vproj, full_value, preferred_element_type=jnp.float32
    )
    grad_normed_one, grad_qgain, grad_kgain = (
        lax.psum(grad_normed_one.astype(jnp.bfloat16), "tp").astype(jnp.float32),
        lax.psum(grad_qgain.astype(jnp.bfloat16), "tp").astype(jnp.float32),
        lax.psum(grad_kgain.astype(jnp.bfloat16), "tp").astype(jnp.float32),
    )
    grad_attn_gain = jnp.sum(grad_normed_one * token_rows * inv_one, 0)
    tokens_grad = grad_residual + norm_back(grad_normed_one, token_rows, inv_one, attn_gain)
    tokens_grad = tokens_grad.astype(jnp.bfloat16).reshape(seq_count, block_len, model_width)
    dw_query, dw_key, dw_value, dw_out, dw_router, dgain_attn, dgain_query, dgain_key, dgain_moe = (
        lax.psum_scatter(grad_wq, ("fsdp", "ctx"), scatter_dimension=0, tiled=True),
        lax.psum_scatter(grad_wk, ("fsdp", "ctx"), scatter_dimension=0, tiled=True),
        lax.psum_scatter(grad_wv, ("fsdp", "ctx"), scatter_dimension=0, tiled=True),
        lax.psum_scatter(grad_w_out, ("fsdp", "ctx"), scatter_dimension=1, tiled=True),
        lax.psum_scatter(grad_router_w, ("fsdp", "ctx"), scatter_dimension=0, tiled=True),
        lax.psum_scatter(grad_attn_gain, ("fsdp", "ctx"), scatter_dimension=0, tiled=True),
        lax.psum_scatter(grad_qgain, ("fsdp", "ctx"), scatter_dimension=0, tiled=True),
        lax.psum_scatter(grad_kgain, ("fsdp", "ctx"), scatter_dimension=0, tiled=True),
        lax.psum_scatter(grad_moe_gain, ("fsdp", "ctx"), scatter_dimension=0, tiled=True),
    )
    return (
        layer_out,
        tokens_grad,
        dw_query,
        dw_key,
        dw_value,
        dw_out,
        dgain_attn,
        dgain_query,
        dgain_key,
        dgain_moe,
        dw_router,
        dw_experts,
    )


def swap(value):
    return lax.ppermute(value, "tp", [(0, 1), (1, 0)])


def exchange(value, axes):
    return lax.all_to_all(value, axes, split_axis=0, concat_axis=0, tiled=True)


def spread(value, axes):
    count = lax.axis_size(axes)
    return exchange(jnp.broadcast_to(value[None], (count,) + value.shape), axes)


def dot(left, right):
    return jnp.dot(left, right, preferred_element_type=jnp.float32)


def dot_nt(left, right):
    return lax.dot_general(left, right, (((1,), (1,)), ((), ())), preferred_element_type=jnp.float32)


def dot_tn(left, right):
    return lax.dot_general(left, right, (((0,), (0,)), ((), ())), preferred_element_type=jnp.float32)


def two_parts(values):
    high = values.astype(jnp.bfloat16)
    low = (values - high.astype(jnp.float32)).astype(jnp.bfloat16)
    return (high, low)


def by_core(mine, other, core):
    return jnp.where(core == 0, jnp.stack([mine, other]), jnp.stack([other, mine]))


def remote(src, dst, send, recv, **where):
    return pltpu.make_async_remote_copy(
        src_ref=src, dst_ref=dst, send_sem=send, recv_sem=recv, device_id=where, device_id_type=MESH
    )


def places():
    return lax.axis_index("fsdp"), lax.axis_index("ctx"), lax.axis_index("tp")


def ring(index, step, count):
    return lax.rem(index + step + count, count)


def greet(nz, nc, line, far=False):
    z, c, t = places()
    barrier = pltpu.get_barrier_semaphore()

    def tell(**where):
        pl.semaphore_signal(barrier, inc=1, device_id=where, device_id_type=MESH)

    if line:
        for step in range(1, nz):
            tell(fsdp=ring(z, step, nz))
        count = nz - 1
    else:
        pl.when(z > 0)(lambda: tell(fsdp=z - 1))
        pl.when(z < nz - 1)(lambda: tell(fsdp=z + 1))
        count = jnp.where(z > 0, 1, 0) + jnp.where(z < nz - 1, 1, 0)
    for step in range(1, nc):
        tell(ctx=ring(c, step, nc))
        if far:
            for hop in range(1, nz):
                tell(fsdp=ring(z, hop, nz), ctx=ring(c, step, nc))
    if far:
        count = count + (nz - 1) * (nc - 1)
    tell(tp=1 - t)
    pl.semaphore_wait(barrier, count + nc)


def line_copies(bufs, send_sem, recv_sem, way, step, shard, target):
    return [
        remote(buf.at[shard], buf.at[shard], send_sem.at[way, step, k], recv_sem.at[way, step, k], fsdp=target)
        for k, buf in enumerate(bufs)
    ]


def line_gather(nz, bufs, send_sem, recv_sem, arrived, begun=None, near=None):
    z = lax.axis_index("fsdp")
    for step in range(nz - 1):

        @pl.when((z < nz - 1) & (z >= step))
        def _():
            for copy in line_copies(bufs, send_sem, recv_sem, 0, step, z - step, z + 1):
                copy.start()

        @pl.when((z > 0) & (z + step < nz))
        def _():
            for copy in line_copies(bufs, send_sem, recv_sem, 1, step, z + step, z - 1):
                copy.start()

        if step == 0 and begun is not None:
            begun()
        if near is not None:
            near(step)

        @pl.when(z - 1 >= step)
        def _():
            for copy in line_copies(bufs, send_sem, recv_sem, 0, step, z - 1 - step, z - 1):
                copy.wait_recv()
            arrived(z - 1 - step)

        @pl.when(z + 1 + step < nz)
        def _():
            for copy in line_copies(bufs, send_sem, recv_sem, 1, step, z + 1 + step, z + 1):
                copy.wait_recv()
            arrived(z + 1 + step)


def line_sent(nz, bufs, send_sem, recv_sem):
    z = lax.axis_index("fsdp")
    for step in range(nz - 1):

        @pl.when((z < nz - 1) & (z >= step))
        def _():
            for copy in line_copies(bufs, send_sem, recv_sem, 0, step, z - step, z + 1):
                copy.wait_send()

        @pl.when((z > 0) & (z + step < nz))
        def _():
            for copy in line_copies(bufs, send_sem, recv_sem, 1, step, z + step, z - 1):
                copy.wait_send()


def pick_rows(pick, slot, source, out):
    lanes = out.shape[-1]
    piece = min(lanes, 512)

    @pl.loop(0, lanes // piece)
    def _(k):
        at = pl.ds(pl.multiple_of(k * piece, piece), piece)
        out[slot, :, at] = jnp.dot(pick[slot], source[slot, :, at], preferred_element_type=jnp.float32).astype(
            jnp.bfloat16
        )


def plane_copy(most, src, dst, send, recv, slot, step, source, target):
    rows = pl.ds(pl.multiple_of(target * most, 16), most)
    return remote(
        src.at[slot, rows], dst.at[source, slot], send.at[slot, step - 1], recv.at[slot, step - 1], ctx=target
    )


def regroup(shard, t, rows, line, two, keep_sem, give_send, give_recv):
    slot = lax.rem(shard, 2)
    band = pl.ds(pl.multiple_of(t * rows, rows), rows)

    def keep():
        pltpu.make_async_copy(line.at[shard], two.at[slot, band], keep_sem.at[slot]).start()

    def give():
        remote(line.at[shard], two.at[slot, band], give_send.at[slot], give_recv.at[slot], tp=1 - t).start()

    pl.when(shard // 2 == t)(keep)
    pl.when(shard // 2 != t)(give)


def selector(nz, src, pair, third, held, pair_out, third_out, in_sem, pair_sem, third_sem):
    c = lax.axis_index("ctx")
    tile = 16
    count = src.shape[2]
    height = held.shape[1]
    bands = src.shape[0] // height

    def take(b):
        slot = lax.rem(b, 2)
        return pltpu.make_async_copy(
            src.at[pl.ds(pl.multiple_of(b * height, height), height)], held.at[slot], in_sem.at[slot]
        )

    def put(b):
        slot = lax.rem(b, 2)
        at = pl.ds(pl.multiple_of(b * height, height), height)
        return (
            pltpu.make_async_copy(pair_out.at[slot], pair.at[:, :, at], pair_sem.at[slot]),
            pltpu.make_async_copy(third_out.at[slot], third.at[:, at], third_sem.at[slot]),
        )

    def pick_band(b):
        slot = lax.rem(b, 2)
        take(b).wait()
        pl.when(b + 1 < bands)(lambda: take(b + 1).start())

        @pl.when(b >= 2)
        def _():
            for copy in put(b - 2):
                copy.wait()

        row = lax.broadcasted_iota(jnp.int32, (nz * tile, tile * count), 0)
        column = lax.broadcasted_iota(jnp.int32, (nz * tile, tile * count), 1)
        hit = column == lax.rem(row, tile) * count + c * nz + row // tile
        hit = jnp.where(hit, 1.0, 0.0).astype(jnp.bfloat16)
        for n in range(height // tile):
            at = pl.ds(n * tile, tile)
            for k in range(3):
                value = held[slot, n * tile : (n + 1) * tile, k].reshape(tile * count, -1)
                value = jnp.dot(hit, value, preferred_element_type=jnp.float32).astype(jnp.bfloat16)
                value = value.reshape(nz, tile, -1)
                if k == 1:
                    third_out[slot, :, at, :] = value
                else:
                    pair_out[slot, :, k // 2, at, :] = value
        for copy in put(b):
            copy.start()

    def close():
        for b in (bands - 2, bands - 1):
            for copy in put(b):
                copy.wait()

    pick_band.close = close
    return take, pick_band, bands


def load_kernel(
    nz, nc, tok, cot, wq, wk, wv, wo, small, rank, w_experts,
    x_all, w_qkv, w_o, small_all, rank_line, rank_seq, pick, cot_in, pair, third, middle,
    cot_line, cot_two, cot_send,
    own_sem, line_send, line_recv, w_send, w_recv, tok_send, tok_recv, pass_send, pass_recv,
    rank_send, rank_recv, keep_sem, give_send, give_recv, cot_s, cot_r, cot_own,
    sel_in, sel_pair, sel_third, sel_s, sel_p, sel_t, mid_s, mid_r,
):
    z, c, t = places()
    block = tok.shape[0]
    rows = block // 2
    local = w_qkv.shape[2] // 3
    most = cot_in.shape[2]
    half = pl.ds(pl.multiple_of(t * rows, rows), rows)
    column = pl.ds(pl.multiple_of(c * local, local), local)
    own = [
        pltpu.make_async_copy(cot.at[half], cot_line.at[z], own_sem.at[5]),
        pltpu.make_async_copy(small, small_all.at[z], own_sem.at[4]),
        pltpu.make_async_copy(rank, rank_line.at[z], own_sem.at[7]),
        pltpu.make_async_copy(rank, rank_seq.at[c], own_sem.at[8]),
    ]
    own += [
        pltpu.make_async_copy(w.at[:, column], w_qkv.at[z, :, pl.ds(k * local, local)], own_sem.at[k])
        for k, w in enumerate((wq, wk, wv))
    ]
    own += [
        pltpu.make_async_copy(wo.at[column], w_o.at[z], own_sem.at[3]),
        pltpu.make_async_copy(tok, x_all.at[pl.ds(pl.multiple_of(c * block, block), block)], own_sem.at[6]),
    ]
    for copy in own:
        copy.start()
    take, pick_band, bands = selector(nz, w_experts, pair, third, sel_in, sel_pair, sel_third, sel_s, sel_p, sel_t)
    take(0).start()
    greet(nz, nc, False)

    def band(source, core):
        return x_all.at[pl.ds(pl.multiple_of(source * block + core * rows, rows), rows)]

    def token_copy(step, source, target):
        return remote(tok.at[half], band(source, t), tok_send.at[step], tok_recv.at[step], ctx=target)

    def pass_copy(step, source, core):
        return remote(band(source, core), band(source, core), pass_send.at[step], pass_recv.at[step], tp=1 - t)

    def rank_copy(step, source, target):
        return remote(rank, rank_seq.at[source], rank_send.at[step], rank_recv.at[step], ctx=target)

    for step in range(1, nc):
        token_copy(step - 1, c, ring(c, step, nc)).start()
        rank_copy(step - 1, c, ring(c, step, nc)).start()
    for copy in own:
        copy.wait()

    def arrived(shard):
        regroup(shard, t, rows, cot_line, cot_two, keep_sem, give_send, give_recv)

    arrived(z)
    first = (cot_line, rank_line, small_all)
    line_gather(nz, first, line_send, line_recv, arrived)

    def own_copy(slot):
        return pltpu.make_async_copy(
            cot_send.at[slot, pl.ds(pl.multiple_of(c * most, 16), most)], cot_in.at[c, slot], cot_own.at[slot]
        )

    def send_cotangent():
        number = lax.broadcasted_iota(jnp.int32, (most, block), 0).astype(jnp.float32)
        for slot in range(2):
            for q in range(nc):
                row = rank_line[2 * t + slot, pl.ds(q * nz + z, 1), :]
                hit = jnp.where(number == row, 1.0, 0.0)
                pick[slot, pl.ds(q * most, most), :] = hit.astype(jnp.bfloat16)
        for slot in range(2):
            wait_two(slot, t, rows, cot_line, cot_two, keep_sem, give_recv)
            pick_rows(pick, slot, cot_two, cot_send)
            for step in range(1, nc):
                plane_copy(most, cot_send, cot_in, cot_s, cot_r, slot, step, c, ring(c, step, nc)).start()
            own_copy(slot).start()

    def ignore(shard):
        pass

    partner = nz - 1 - z
    centre = (z == nz // 2 - 1) | (z == nz // 2)
    middle_copy = remote(third.at[partner], middle, mid_s, mid_r, fsdp=partner)

    def select_some(step):
        pl.loop(bands * (0, 1, 3)[step] // 4, bands * (1, 3, 4)[step] // 4)(pick_band)
        if step == 2:
            pick_band.close()
            pl.when(centre)(lambda: middle_copy.start())

    line_gather(nz, (w_qkv, w_o), w_send, w_recv, ignore, send_cotangent, select_some)
    for step in range(1, nc):
        source = ring(c, -step, nc)
        token_copy(step - 1, source, source).wait_recv()
        pass_copy(step - 1, source, t).start()
        rank_copy(step - 1, source, source).wait_recv()
    for step in range(1, nc):
        source = ring(c, -step, nc)
        pass_copy(step - 1, source, 1 - t).wait_recv()
        pass_copy(step - 1, source, t).wait_send()
        token_copy(step - 1, c, source).wait_send()
        rank_copy(step - 1, c, source).wait_send()
        for slot in range(2):
            copy = plane_copy(most, cot_send, cot_in, cot_s, cot_r, slot, step, source, source)
            copy.wait_recv()
            copy.wait_send()
    line_sent(nz, first, line_send, line_recv)
    line_sent(nz, (w_qkv, w_o), w_send, w_recv)
    for slot in range(2):
        own_copy(slot).wait()
        wait_given(slot, t, rows, cot_line, cot_two, give_send, give_recv)

    @pl.when(centre)
    def _():
        middle_copy.wait_recv()
        middle_copy.wait_send()


def wait_given(slot, t, rows, line, two, give_send, give_recv):
    band = pl.ds(pl.multiple_of(t * rows, rows), rows)
    remote(line.at[0], two.at[slot, band], give_send.at[slot], give_recv.at[slot], tp=1 - t).wait_send()


def wait_two(slot, t, rows, line, two, keep_sem, give_recv):
    band = pl.ds(pl.multiple_of(t * rows, rows), rows)
    other = pl.ds(pl.multiple_of((1 - t) * rows, rows), rows)
    pltpu.make_async_copy(line.at[0], two.at[slot, band], keep_sem.at[slot]).wait()
    remote(line.at[0], two.at[slot, other], give_recv.at[slot], give_recv.at[slot], tp=1 - t).wait_recv()


def load(tok, cot, wq, wk, wv, wo, small, rank, w_experts, most):
    nz, nc = lax.axis_size("fsdp"), lax.axis_size("ctx")
    block, width = tok.shape
    deep, local = wq.shape[0], wq.shape[1] // nc
    rows = block // 2
    count, ffn = w_experts.shape[2:]
    dma = pltpu.SemaphoreType.DMA
    bf16, f32 = jnp.bfloat16, jnp.float32
    shapes = [
        ((nc * block, width), bf16),
        ((nz, deep, 3 * local), bf16),
        ((nz, local, wo.shape[1]), bf16),
        ((nz,) + small.shape, bf16),
        ((nz,) + rank.shape, f32),
        ((nc,) + rank.shape, f32),
        ((2, nc * most, block), bf16),
        ((nc, 2, most, width), bf16),
        ((nz, 2, deep, ffn), bf16),
        ((nz, deep, ffn), bf16),
        ((deep, ffn), bf16),
    ]
    hbm = pl.BlockSpec(memory_space=pl.ANY)
    height = 32
    return pl.pallas_call(
        functools.partial(load_kernel, nz, nc),
        out_shape=[jax.ShapeDtypeStruct(shape, kind) for shape, kind in shapes],
        in_specs=[hbm] * 9,
        out_specs=[pl.BlockSpec(memory_space=pltpu.VMEM)] * 7 + [hbm] * 4,
        scratch_shapes=[
            pltpu.VMEM((nz, rows, width), bf16),
            pltpu.VMEM((2, block, width), bf16),
            pltpu.VMEM((2, nc * most, width), bf16),
            dma((9,)),
            dma((2, nz - 1, 3)), dma((2, nz - 1, 3)), dma((2, nz - 1, 2)), dma((2, nz - 1, 2)),
            dma((nc - 1,)), dma((nc - 1,)), dma((nc - 1,)), dma((nc - 1,)), dma((nc - 1,)), dma((nc - 1,)),
            dma((2,)), dma((2,)), dma((2,)), dma((2, nc - 1)), dma((2, nc - 1)), dma((2,)),
            pltpu.VMEM((2, height, 3, count, ffn), bf16),
            pltpu.VMEM((2, nz, 2, height, ffn), bf16),
            pltpu.VMEM((2, nz, height, ffn), bf16),
            dma((2,)), dma((2,)), dma((2,)), dma, dma,
        ],
        compiler_params=pltpu.CompilerParams(
            collective_id=0, has_side_effects=True, vmem_limit_bytes=48 * 2**20
        ),
    )(tok, cot, wq, wk, wv, wo, small, rank, w_experts)


def dispatch_kernel(
    nz, nc, part, tok, gain, router, kept, pick, third, middle,
    residual, normed, probs, x_in, g_in, third_got,
    sib, rs_send, rs_recv, n_line, g_line, n_two, g_two, x_send, g_send,
    sib_s, sib_r, rs_s, rs_r, line_send, line_recv, keep_sem, give_send, give_recv,
    gkeep_sem, ggive_send, ggive_recv, x_s, x_r, g_s, g_r, own_sem,
    third_s, third_r, third_own, mid_own,
):
    z, c, t = places()
    f32, bf16 = jnp.float32, jnp.bfloat16
    rows, width = residual.shape
    most = x_in.shape[2]
    greet(nz, nc, True)
    keep_third = pltpu.make_async_copy(third.at[z], third_got.at[z], third_own)
    keep_third.start()
    partner = nz - 1 - z
    centre = (z == nz // 2 - 1) | (z == nz // 2)
    keep_middle = pltpu.make_async_copy(middle, third_got.at[partner], mid_own)
    pl.when(centre)(lambda: keep_middle.start())

    def still(other):
        return jnp.logical_not(centre & (other == partner))

    def third_copy(step, source, target):
        return remote(third.at[target], third_got.at[source], third_s.at[step], third_r.at[step], fsdp=target)

    def sib_copy(q):
        return remote(part.at[q, 1 - t], sib.at[q], sib_s.at[q], sib_r.at[q], tp=1 - t)

    def rs_copy(step, source, target):
        return remote(rs_send.at[step], rs_recv.at[step], rs_s.at[step], rs_r.at[step], ctx=target)

    for step in range(1, nc + 1):
        sib_copy(ring(c, step, nc)).start()
    chunk = 16
    for step in range(1, nc):
        q = ring(c, step, nc)
        sib_copy(q).wait_recv()

        @pl.loop(0, rows // chunk)
        def _(k):
            at = pl.ds(pl.multiple_of(k * chunk, chunk), chunk)
            rs_send[step - 1, at, :] = (part[q, t, at, :].astype(f32) + sib[q, at, :].astype(f32)).astype(bf16)

        rs_copy(step - 1, c, q).start()

    def own_copy(slot, src, dst, k):
        return pltpu.make_async_copy(
            src.at[slot, pl.ds(pl.multiple_of(c * most, 16), most)], dst.at[c, slot], own_sem.at[k, slot]
        )

    sib_copy(c).wait_recv()
    for step in range(1, nc):
        rs_copy(step - 1, c, c).wait_recv()

    @pl.loop(0, rows // chunk)
    def _(k):
        at = pl.ds(pl.multiple_of(k * chunk, chunk), chunk)
        start = pl.ds(pl.multiple_of(t * rows + k * chunk, chunk), chunk)
        total = part[c, t, at, :].astype(f32) + sib[c, at, :].astype(f32)
        for step in range(nc - 1):
            total = total + rs_recv[step, at, :].astype(f32)
        total = total + tok[start, :].astype(f32)
        residual[at, :] = total
        inv = lax.rsqrt(jnp.mean(total * total, -1, keepdims=True) + EPS)
        row = (total * inv * gain[...]).astype(bf16)
        normed[at, :] = row
        n_line[z, at, :] = row

    logits = lax.dot_general(
        normed[...], router[...], (((1,), (1,)), ((), ())), preferred_element_type=f32
    )
    lane = lax.broadcasted_iota(jnp.int32, logits.shape, 1)
    logits = jnp.where(lane < E, logits, -jnp.inf)
    top = jnp.max(logits, -1, keepdims=True)
    raised = jnp.exp(logits - top)
    prob = raised / jnp.sum(raised, -1, keepdims=True)
    probs[...] = prob
    gates = prob * kept[...]
    high = gates.astype(bf16)
    g_line[z, :, pl.ds(0, 128)] = high
    g_line[z, :, pl.ds(128, 128)] = (gates - high.astype(f32)).astype(bf16)

    def arrived(shard):
        regroup(shard, t, rows, n_line, n_two, keep_sem, give_send, give_recv)
        regroup(shard, t, rows, g_line, g_two, gkeep_sem, ggive_send, ggive_recv)

    arrived(z)
    sent = ((x_send, x_in, x_s, x_r), (g_send, g_in, g_s, g_r))

    def near(distance):
        above, below = z + distance, z - distance
        is_above = (above < nz) & (above // 2 == t)
        is_below = (below >= 0) & (below // 2 == t)
        slot = lax.rem(jnp.where(is_above, above, below + 2), 2)

        @pl.when(is_above | is_below)
        def _():
            wait_two(slot, t, rows, n_line, n_two, keep_sem, give_recv)
            wait_two(slot, t, rows, g_line, g_two, gkeep_sem, ggive_recv)
            pick_rows(pick, slot, n_two, x_send)
            pick_rows(pick, slot, g_two, g_send)
            for k, (src, dst, s, r) in enumerate(sent):
                for step in range(1, nc):
                    plane_copy(most, src, dst, s, r, slot, step, c, ring(c, step, nc)).start()
                own_copy(slot, src, dst, k).start()

    line_gather(nz, (n_line, g_line), line_send, line_recv, arrived, None, near)
    near(nz - 1)
    for step in range(1, nz):
        pl.when(still(ring(z, step, nz)))(lambda: third_copy(step - 1, z, ring(z, step, nz)).start())
    line_sent(nz, (n_line, g_line), line_send, line_recv)
    for slot in range(2):
        wait_given(slot, t, rows, n_line, n_two, give_send, give_recv)
        wait_given(slot, t, rows, g_line, g_two, ggive_send, ggive_recv)
        for k, (src, dst, s, r) in enumerate(sent):
            own_copy(slot, src, dst, k).wait()
            for step in range(1, nc):
                source = ring(c, -step, nc)
                copy = plane_copy(most, src, dst, s, r, slot, step, source, source)
                copy.wait_recv()
                copy.wait_send()
    for step in range(1, nc):
        rs_copy(step - 1, c, c).wait_send()
    for step in range(nc):
        sib_copy(step).wait_send()
    for step in range(1, nz):
        source = ring(z, -step, nz)
        pl.when(still(source))(lambda: third_copy(step - 1, source, source).wait_recv())
        pl.when(still(ring(z, step, nz)))(lambda: third_copy(step - 1, source, source).wait_send())
    keep_third.wait()
    pl.when(centre)(lambda: keep_middle.wait())


def dispatch(part, tok, gain, router, kept, pick, third, middle):
    nz, nc = lax.axis_size("fsdp"), lax.axis_size("ctx")
    rows, width = part.shape[2], part.shape[3]
    block = rows * 2
    most = pick.shape[1] // nc
    dma = pltpu.SemaphoreType.DMA
    bf16, f32 = jnp.bfloat16, jnp.float32
    vmem = pl.BlockSpec(memory_space=pltpu.VMEM)
    hbm = pl.BlockSpec(memory_space=pl.ANY)
    return pl.pallas_call(
        functools.partial(dispatch_kernel, nz, nc),
        out_shape=[
            jax.ShapeDtypeStruct((rows, width), f32),
            jax.ShapeDtypeStruct((rows, width), bf16),
            jax.ShapeDtypeStruct((rows, 128), f32),
            jax.ShapeDtypeStruct((nc, 2, most, width), bf16),
            jax.ShapeDtypeStruct((nc, 2, most, 256), bf16),
            jax.ShapeDtypeStruct(third.shape, bf16),
        ],
        in_specs=[vmem] * 6 + [hbm] * 2,
        out_specs=[vmem] * 3 + [hbm] * 3,
        scratch_shapes=[
            pltpu.VMEM((nc, rows, width), bf16),
            pltpu.VMEM((nc - 1, rows, width), bf16),
            pltpu.VMEM((nc - 1, rows, width), bf16),
            pltpu.VMEM((nz, rows, width), bf16),
            pltpu.VMEM((nz, rows, 256), bf16),
            pltpu.VMEM((2, block, width), bf16),
            pltpu.VMEM((2, block, 256), bf16),
            pltpu.VMEM((2, nc * most, width), bf16),
            pltpu.VMEM((2, nc * most, 256), bf16),
            dma((nc,)), dma((nc,)), dma((nc - 1,)), dma((nc - 1,)),
            dma((2, nz - 1, 2)), dma((2, nz - 1, 2)),
            dma((2,)), dma((2,)), dma((2,)), dma((2,)), dma((2,)), dma((2,)),
            dma((2, nc - 1)), dma((2, nc - 1)), dma((2, nc - 1)), dma((2, nc - 1)),
            dma((2, 2)),
            dma((nz - 1,)), dma((nz - 1,)), dma, dma,
        ],
        compiler_params=pltpu.CompilerParams(
            collective_id=1, has_side_effects=True, vmem_limit_bytes=56 * 2**20
        ),
    )(part, tok, gain, router, kept, pick, third, middle)


def experts_kernel(
    nz, nc, x_hbm, cot_hbm, gates, pair_hbm, third_hbm, y_hbm, r_hbm, pair_out, hid_hbm, gg_hbm, gu_hbm,
    x, cot, w, weight, pair, gate, up, out_grad, y, r, hid, gg, gu,
    sem, swap_s, swap_r, out_sem, inner_sem,
):
    z, c, t = places()
    f32, bf16 = jnp.float32, jnp.bfloat16
    width, tall = x.shape[1], x.shape[0]
    deep, ffn = w.shape[3], w.shape[4]
    span = 256
    chunk = 288
    copies = [
        pltpu.make_async_copy(cot_hbm, cot, sem.at[0]),
        pltpu.make_async_copy(pair_hbm, w.at[0, :, pl.ds(0, 2)], sem.at[1]),
        pltpu.make_async_copy(x_hbm, x, sem.at[2]),
        pltpu.make_async_copy(third_hbm, w.at[0, :, 2], sem.at[3]),
    ]
    for copy in copies:
        copy.start()
    barrier = pltpu.get_barrier_semaphore()
    pl.semaphore_signal(barrier, inc=1, device_id=dict(tp=1 - t), device_id_type=MESH)
    pl.semaphore_wait(barrier, 1)
    swaps = [
        remote(pair_hbm, w.at[1, :, pl.ds(0, 2)], swap_s.at[0], swap_r.at[0], tp=1 - t),
        remote(third_hbm, w.at[1, :, 2], swap_s.at[1], swap_r.at[1], tp=1 - t),
    ]
    for copy in swaps:
        copy.start()
    pair[...] = jnp.zeros_like(pair)
    lane = lax.broadcasted_iota(jnp.int32, (chunk, 256), 1)
    mine = c * nz + z

    @pl.loop(0, tall // chunk)
    def _(m):
        rows = pl.ds(pl.multiple_of(m * chunk, chunk), chunk)
        value = gates[rows, :].astype(f32)
        value = jnp.where((lane == mine) | (lane == mine + 128), value, 0.0)
        weight[rows, :] = jnp.sum(value, 1, keepdims=True)

    for copy in copies[:2]:
        copy.wait()
    per = ffn // span

    def forward(n):
        half, at = n // per, pl.ds(pl.multiple_of(lax.rem(n, per) * span, span), span)
        full = pl.ds(pl.multiple_of(n * span, span), span)

        def times(rows, k):
            return jnp.dot(rows[...], w[half, :, k, :, at].reshape(width, span), preferred_element_type=f32)

        out_grad[...] = times(cot, 1)

        @pl.when(n == 0)
        def _():
            for copy in copies[2:]:
                copy.wait()

        gate[...] = times(x, 0)
        up[...] = times(x, 2)

        @pl.loop(0, tall // chunk)
        def _(m):
            rows = pl.ds(pl.multiple_of(m * chunk, chunk), chunk)
            g, u, o, k = gate[rows, :], up[rows, :], out_grad[rows, :], weight[rows, :]
            sig = 1.0 / (1.0 + jnp.exp(-g))
            silu = g * sig
            hidden = silu * u
            pair[rows, :] += jnp.sum(hidden.astype(bf16).astype(f32) * o, 1, keepdims=True)
            hid[rows, full] = (k * hidden).astype(bf16)
            o = k * o
            gg[rows, full] = (o * u * sig * (1.0 + g * (1.0 - sig))).astype(bf16)
            gu[rows, full] = (o * silu).astype(bf16)

    pl.loop(0, per)(forward)
    for copy in swaps:
        copy.wait_recv()
    pl.loop(per, 2 * per)(forward)

    @pl.loop(0, tall // chunk)
    def _(m):
        rows = pl.ds(pl.multiple_of(m * chunk, chunk), chunk)
        value = pair[rows, :]
        high = value.astype(bf16).astype(f32)
        out = jnp.where(lane == mine, high, jnp.where(lane == mine + 128, value - high, 0.0))
        pair_out[rows, :] = out.astype(bf16)

    inner = [
        pltpu.make_async_copy(src, dst, inner_sem.at[k])
        for k, (src, dst) in enumerate(((hid, hid_hbm), (gg, gg_hbm), (gu, gu_hbm)))
    ]
    for copy in inner:
        copy.start()
    per_deep = deep // span

    def leave(n):
        full = pl.ds(pl.multiple_of(n * span, span), span)
        return (
            pltpu.make_async_copy(y.at[:, full], y_hbm.at[:, full], out_sem.at[0, n]),
            pltpu.make_async_copy(r.at[:, full], r_hbm.at[:, full], out_sem.at[1, n]),
        )

    @pl.loop(0, width // span)
    def _(n):
        zone, at = n // per_deep, pl.ds(pl.multiple_of(lax.rem(n, per_deep) * span, span), span)
        full = pl.ds(pl.multiple_of(n * span, span), span)

        def back(rows, k):
            total = 0.0
            for half in range(2):
                total = total + lax.dot_general(
                    rows[:, pl.ds(half * ffn, ffn)], w[half, zone, k, at, :], (((1,), (1,)), ((), ())),
                    preferred_element_type=f32,
                )
            return total

        y[:, full] = back(hid, 1).astype(bf16)
        r[:, full] = (back(gg, 0) + back(gu, 2)).astype(bf16)
        for copy in leave(n):
            copy.start()

    for n in range(width // span):
        for copy in leave(n):
            copy.wait()
    for copy in inner:
        copy.wait()
    for copy in swaps:
        copy.wait_send()


def experts(x, cot, gates, pair, third):
    bf16, f32 = jnp.bfloat16, jnp.float32
    nz, nc = lax.axis_size("fsdp"), lax.axis_size("ctx")
    tall, width = x.shape
    deep, ffn = third.shape[1:]
    vmem = pl.BlockSpec(memory_space=pltpu.VMEM)
    hbm = pl.BlockSpec(memory_space=pl.ANY)
    inner = jax.ShapeDtypeStruct((tall, 2 * ffn), bf16)
    dma = pltpu.SemaphoreType.DMA
    return pl.pallas_call(
        functools.partial(experts_kernel, nz, nc),
        out_shape=[
            jax.ShapeDtypeStruct((tall, width), bf16),
            jax.ShapeDtypeStruct((tall, width), bf16),
            jax.ShapeDtypeStruct((tall, 256), bf16),
            inner,
            inner,
            inner,
        ],
        in_specs=[hbm, hbm, vmem, hbm, hbm],
        out_specs=[hbm, hbm, vmem, hbm, hbm, hbm],
        scratch_shapes=[
            pltpu.VMEM((tall, width), bf16),
            pltpu.VMEM((tall, width), bf16),
            pltpu.VMEM((2, nz, 3, deep, ffn), bf16),
            pltpu.VMEM((tall, 1), f32),
            pltpu.VMEM((tall, 1), f32),
            pltpu.VMEM((tall, 256), f32),
            pltpu.VMEM((tall, 256), f32),
            pltpu.VMEM((tall, 256), f32),
            pltpu.VMEM((tall, width), bf16),
            pltpu.VMEM((tall, width), bf16),
            pltpu.VMEM((tall, 2 * ffn), bf16),
            pltpu.VMEM((tall, 2 * ffn), bf16),
            pltpu.VMEM((tall, 2 * ffn), bf16),
            dma((4,)), dma((2,)), dma((2,)), dma((2, width // 256)), dma((3,)),
        ],
        compiler_params=pltpu.CompilerParams(
            collective_id=4, has_side_effects=True, vmem_limit_bytes=60 * 2**20
        ),
    )(x, cot, gates, pair, third)


def place_kernel(nz, nc, gate, rest, out):
    tile = rest.shape[1]
    count = nz * nc
    row = lax.broadcasted_iota(jnp.int32, (tile * count, tile * count), 0)
    column = lax.broadcasted_iota(jnp.int32, (tile * count, tile * count), 1)
    expert = lax.rem(row, count)
    hit = column == (lax.rem(expert, nz) * nc + expert // nz) * tile + row // count
    hit = jnp.where(hit, 1.0, 0.0).astype(jnp.bfloat16)
    for k in range(3):
        value = (gate[k] if k < 2 else rest[...]).reshape(count * tile, -1)
        value = jnp.dot(hit, value, preferred_element_type=jnp.float32)
        out[:, k] = value.reshape(tile, count, -1)


def lay_out(gate, rest, nz, nc):
    count, strip, ffn = rest.shape
    tile = 16
    return pl.pallas_call(
        functools.partial(place_kernel, nz, nc),
        grid=(strip // tile,),
        out_shape=jax.ShapeDtypeStruct((strip, 3, count, ffn), jnp.float32),
        in_specs=[
            pl.BlockSpec((2, count, tile, ffn), lambda i: (0, 0, i, 0)),
            pl.BlockSpec((count, tile, ffn), lambda i: (0, i, 0)),
        ],
        out_specs=pl.BlockSpec((tile, 3, count, ffn), lambda i: (i, 0, 0, 0)),
        compiler_params=pltpu.CompilerParams(vmem_limit_bytes=40 * 2**20),
    )(gate, rest)


def collector(nz, nc, pick_t, items, sems):
    z, c, t = places()
    to_s, to_r, own_sem, sib_s, sib_r, line_s, line_r, keep_sem = sems
    rows = items[0][2].shape[1]
    mine_at = pl.ds(pl.multiple_of(t * rows, rows), rows)
    give_at = pl.ds(pl.multiple_of((1 - t) * rows, rows), rows)
    count = len(items)

    def lanes(turn, k):
        wide = items[k][2].shape[-1] // 2
        return pl.ds(turn * wide, wide)

    def to_copy(turn, k, step, source, target):
        src, got = items[k][:2]
        at = lanes(turn, k)
        return remote(
            src.at[target, :, :, at], got.at[source, :, :, at], to_s.at[k, turn, step - 1], to_r.at[k, turn, step - 1],
            ctx=target,
        )

    def own_copy(turn, k):
        src, got = items[k][:2]
        at = lanes(turn, k)
        return pltpu.make_async_copy(src.at[c, :, :, at], got.at[c, :, :, at], own_sem.at[k, turn])

    def sib_copy(turn, k):
        give, sib = items[k][3:5]
        at = lanes(turn, k)
        return remote(give.at[:, :, at], sib.at[:, :, at], sib_s.at[k, turn], sib_r.at[k, turn], tp=1 - t)

    def line_copy(turn, slot, k, half, source, target):
        src = items[k][2 if half == 0 else 4]
        at = lanes(turn, k)
        return remote(
            src.at[slot, :, at], items[k][5].at[source, :, at],
            line_s.at[k, turn, 2 * half + slot], line_r.at[k, turn, source], fsdp=target,
        )

    def keep_copy(turn, slot, k, half):
        src = items[k][2 if half == 0 else 4]
        at = lanes(turn, k)
        return pltpu.make_async_copy(src.at[slot, :, at], items[k][5].at[z, :, at], keep_sem.at[k, turn])

    def goal(slot, half):
        return 2 * (t if half == 0 else 1 - t) + slot

    def forward(turn, k, half):
        for slot in range(2):
            target = goal(slot, half)
            pl.when(target != z)(lambda: line_copy(turn, slot, k, half, z, target).start())
            pl.when(target == z)(lambda: keep_copy(turn, slot, k, half).start())

    def begin(turn):
        for k in range(count):
            for step in range(1, nc):
                to_copy(turn, k, step, c, ring(c, step, nc)).start()
            own_copy(turn, k).start()

    def scatter(turn, slot, k):
        got, mine, give = items[k][1:4]
        wide = mine.shape[-1] // 2
        span = min(wide, 512)
        tall = got.shape[0] * got.shape[2]

        @pl.loop(0, wide // span)
        def _(n):
            at = pl.ds(pl.multiple_of(turn * wide + n * span, span), span)
            pairs = got[:, slot, :, at].reshape(tall, span)
            for picks, out in ((mine_at, mine), (give_at, give)):
                out[slot, :, at] = jnp.dot(
                    pick_t[slot, picks, :], pairs, preferred_element_type=jnp.float32
                ).astype(jnp.bfloat16)

    def process(turn):
        for k in range(count):
            own_copy(turn, k).wait()
            for step in range(1, nc):
                source = ring(c, -step, nc)
                to_copy(turn, k, step, source, c).wait_recv()
            for slot in range(2):
                scatter(turn, slot, k)
            sib_copy(turn, k).start()
            forward(turn, k, 0)
        for k in range(count):
            sib_copy(turn, k).wait_recv()
            forward(turn, k, 1)

    def join():
        for turn in range(2):
            for k in range(count):
                keep_copy(turn, 0, k, 0).wait()
                for step in range(1, nz):
                    line_copy(turn, 0, k, 0, ring(z, -step, nz), z).wait_recv()

    def done():
        for turn in range(2):
            for k in range(count):
                for step in range(1, nc):
                    to_copy(turn, k, step, c, ring(c, step, nc)).wait_send()
                sib_copy(turn, k).wait_send()
                for half in range(2):
                    for slot in range(2):
                        pl.when(goal(slot, half) != z)(
                            lambda: line_copy(turn, slot, k, half, z, goal(slot, half)).wait_send()
                        )

    return begin, process, join, done


def collector_scratch(nz, nc, most, rows, widths):
    dma = pltpu.SemaphoreType.DMA
    bf16 = jnp.bfloat16
    count = len(widths)
    bufs = []
    for w in widths:
        bufs += [pltpu.VMEM((nc, 2, most, w), bf16)]
        bufs += [pltpu.VMEM((2, rows, w), bf16)] * 3
        bufs += [pltpu.VMEM((nz, rows, w), bf16)]
    sems = [
        dma((count, 2, nc - 1)), dma((count, 2, nc - 1)), dma((count, 2)), dma((count, 2)), dma((count, 2)),
        dma((count, 2, 4)), dma((count, 2, nz)), dma((count, 2)),
    ]
    return bufs, sems


def return_kernel(
    nz, nc, r, g, x_hbm, cot_hbm, hid_hbm, gg_hbm, gu_hbm, pick_t, residual, probs, kept, router, gain, cot,
    logits_grad, gain_grad, residual_grad, attn_grad, early_got, own_grad, other_grad,
    x, cot_rows, hid, gg, gu, stage, early, early_sib,
    load_sem, keep_sem, give_sem, got_sem, *scratch,
):
    z, c, t = places()
    f32, bf16 = jnp.float32, jnp.bfloat16
    rows, width = residual.shape
    r_line, g_line = scratch[4], scratch[9]
    row_s, row_r, pass_s, pass_r, early_s, early_r, early_own = scratch[18:]
    items = ((r,) + scratch[:5], (g,) + scratch[5:10])
    begin, process, join, done = collector(nz, nc, pick_t, items, scratch[10:18])
    here = z * nc + c
    def keep_early(kind):
        return pltpu.make_async_copy(early.at[kind, here], early_got.at[kind, here], early_own.at[kind])

    loads = [
        pltpu.make_async_copy(src, dst, load_sem.at[k])
        for k, (src, dst) in enumerate(
            ((x_hbm, x), (gg_hbm, gg), (gu_hbm, gu), (cot_hbm, cot_rows), (hid_hbm, hid))
        )
    ]
    for copy in loads:
        copy.start()
    greet(nz, nc, True, True)
    chips = nz * nc
    steps = [(i, j) for i in range(nz) for j in range(nc) if i or j]

    def early_copy(kind, n, source, target, fsdp, ctx):
        return remote(
            early.at[kind, target], early_got.at[kind, source], early_s.at[kind, n], early_r.at[kind, n],
            fsdp=fsdp, ctx=ctx,
        )

    def send_early(kind):
        keep_early(kind).start()
        for n, (i, j) in enumerate(steps):
            zz, cc = ring(z, i, nz), ring(c, j, nc)
            early_copy(kind, n, here, zz * nc + cc, zz, cc).start()

    begin(0)
    begin(1)

    span = 256
    strip, ffn = stage.shape[3], stage.shape[4]
    per = span // strip
    bands = width // span

    def gradients(kind, rows_in, grads):
        last = kind == 2

        def flush(n):
            slot = lax.rem(n, 2)
            at = pl.ds(pl.multiple_of(n * per, per), per)
            target = other_grad.at[at] if last else early_sib.at[kind, at]
            give = remote(stage.at[slot, 1], target, give_sem.at[slot], got_sem.at[kind], tp=1 - t)
            if not last:
                return (give,)
            return (give, pltpu.make_async_copy(stage.at[slot, 0], own_grad.at[at], keep_sem.at[slot]))

        def flushed(n):
            copies = flush(n)
            copies[0].wait_send()
            for copy in copies[1:]:
                copy.wait()

        @pl.loop(0, bands)
        def _(n):
            full = pl.ds(pl.multiple_of(n * span, span), span)
            slot = lax.rem(n, 2)
            pl.when(n >= 2)(lambda: flushed(n - 2))
            value = lax.dot_general(
                rows_in[:, full], grads[...], (((0,), (0,)), ((), ())), preferred_element_type=f32
            ).astype(bf16)
            for i in range(per):
                piece = value[i * strip : (i + 1) * strip]
                if last:
                    stage[slot, 0, i] = piece[:, :ffn]
                else:
                    early[kind, n * per + i] = piece[:, :ffn]
                stage[slot, 1, i] = piece[:, ffn:]
            for copy in flush(n):
                copy.start()

        flushed(bands - 2)
        flushed(bands - 1)
        if not last:
            remote(early_sib.at[kind], early_sib.at[kind], got_sem.at[kind], got_sem.at[kind], tp=1 - t).wait_recv()

            @pl.loop(0, chips)
            def _(n):
                early[kind, n] = (early[kind, n].astype(f32) + early_sib[kind, n].astype(f32)).astype(bf16)

    loads[0].wait()
    loads[1].wait()
    gradients(0, x, gg)
    send_early(0)
    for copy in loads[2:]:
        copy.wait()
    gradients(1, x, gu)
    gradients(2, cot_rows, hid)
    for turn in range(2):
        process(turn)
    join()
    pairs = jnp.zeros((rows, 128), f32)
    for source in range(nz):
        pairs = pairs + g_line[source, :, 0:128].astype(f32) + g_line[source, :, 128:256].astype(f32)
    pairs = pairs * kept[...]
    prob = probs[...]
    grad_logits = (prob * (pairs - jnp.sum(prob * pairs, -1, keepdims=True))).astype(bf16)
    logits_grad[...] = grad_logits
    gain_grad[...] = jnp.zeros_like(gain_grad)
    chunk = 16

    @pl.loop(0, rows // chunk)
    def _(k):
        at = pl.ds(pl.multiple_of(k * chunk, chunk), chunk)
        full = pl.ds(pl.multiple_of(t * rows + k * chunk, chunk), chunk)
        res = residual[at, :]
        grad = r_line[0, at, :].astype(f32)
        for source in range(1, nz):
            grad = grad + r_line[source, at, :].astype(f32)
        grad = grad + jnp.dot(logits_grad[at, :], router[...], preferred_element_type=f32)
        inv = lax.rsqrt(jnp.mean(res * res, -1, keepdims=True) + EPS)
        gain_grad[...] += jnp.sum((grad * res * inv).reshape(chunk // 8, 8, width), 0)
        weighted = grad * gain[...]
        inner = jnp.sum(weighted * res, -1, keepdims=True)
        out = cot[full, :].astype(f32) + inv * weighted - res * (inv * inv * inv) * inner / width
        residual_grad[at, :] = out
        attn_grad[c, t, at, :] = out.astype(bf16)

    def row_copy(step, source, target):
        return remote(attn_grad.at[source, t], attn_grad.at[source, t], row_s.at[step], row_r.at[step], ctx=target)

    def pass_copy(step, source, core):
        return remote(attn_grad.at[source, core], attn_grad.at[source, core], pass_s.at[step], pass_r.at[step], tp=1 - t)

    for step in range(1, nc):
        row_copy(step, c, ring(c, step, nc)).start()
    pass_copy(0, c, t).start()
    send_early(1)
    for step in range(1, nc):
        source = ring(c, -step, nc)
        row_copy(step, source, source).wait_recv()
        pass_copy(step, source, t).start()
    for step in range(nc):
        source = ring(c, -step, nc)
        pass_copy(step, source, 1 - t).wait_recv()
        pass_copy(step, source, t).wait_send()
        if step:
            row_copy(step, c, source).wait_send()
    done()
    for kind in range(2):
        for n, (i, j) in enumerate(steps):
            zz, cc = ring(z, -i, nz), ring(c, -j, nc)
            copy = early_copy(kind, n, zz * nc + cc, zz * nc + cc, zz, cc)
            copy.wait_recv()
            copy.wait_send()
        keep_early(kind).wait()
    remote(other_grad, other_grad, got_sem.at[2], got_sem.at[2], tp=1 - t).wait_recv()


def give_back(r, g, x, cot_rows, hid, gg, gu, pick_t, residual, probs, kept, router, gain, cot):
    nz, nc = lax.axis_size("fsdp"), lax.axis_size("ctx")
    rows, width = residual.shape
    dma = pltpu.SemaphoreType.DMA
    bf16, f32 = jnp.bfloat16, jnp.float32
    vmem = pl.BlockSpec(memory_space=pltpu.VMEM)
    hbm = pl.BlockSpec(memory_space=pl.ANY)
    bufs, sems = collector_scratch(nz, nc, r.shape[2], rows, (width, 256))
    chips = nz * nc
    strip, ffn = width // chips, hid.shape[1] // 2
    tall = x.shape[0]
    return pl.pallas_call(
        functools.partial(return_kernel, nz, nc),
        out_shape=[
            jax.ShapeDtypeStruct((rows, 128), bf16),
            jax.ShapeDtypeStruct((8, width), f32),
            jax.ShapeDtypeStruct((rows, width), f32),
            jax.ShapeDtypeStruct((nc, 2, rows, width), bf16),
            jax.ShapeDtypeStruct((2, chips, strip, ffn), bf16),
            jax.ShapeDtypeStruct((chips, strip, ffn), bf16),
            jax.ShapeDtypeStruct((chips, strip, ffn), bf16),
        ],
        in_specs=[hbm] * 7 + [vmem] * 7,
        out_specs=[vmem] * 4 + [hbm] * 3,
        scratch_shapes=[
            pltpu.VMEM((tall, width), bf16),
            pltpu.VMEM((tall, width), bf16),
            pltpu.VMEM((tall, 2 * ffn), bf16),
            pltpu.VMEM((tall, 2 * ffn), bf16),
            pltpu.VMEM((tall, 2 * ffn), bf16),
            pltpu.VMEM((2, 2, 256 // strip, strip, ffn), bf16),
            pltpu.VMEM((2, chips, strip, ffn), bf16),
            pltpu.VMEM((2, chips, strip, ffn), bf16),
            dma((5,)), dma((2,)), dma((2,)), dma((3,)),
        ]
        + bufs
        + sems
        + [dma((nc,)), dma((nc,)), dma((nc,)), dma((nc,))]
        + [dma((2, nz * nc - 1)), dma((2, nz * nc - 1)), dma((2,))],
        compiler_params=pltpu.CompilerParams(
            collective_id=2, has_side_effects=True, vmem_limit_bytes=60 * 2**20
        ),
    )(r, g, x, cot_rows, hid, gg, gu, pick_t, residual, probs, kept, router, gain, cot)


def final_kernel(
    nz, nc, part, tok, gain, residual_grad, dw, dwo, small, y, pick_t, residual,
    tokens_grad, dw_out, dwo_out, small_out, layer,
    sib, rs_send, rs_recv, tok_grad, gain_acc, dw_up, dw_down, dwo_up, dwo_down, dw_to, dwo_to,
    dw_next, dwo_next, small_line, small_plane, small_sib, small_a, small_b,
    sib_s, sib_r, rs_s, rs_r, line_s, line_r, to_s, to_r, tg_s, tg_r, sm_s, sm_r, sp_s, sp_r, ss_s, ss_r,
    layer_send, lay_s, lay_r, *scratch,
):
    z, c, t = places()
    f32, bf16 = jnp.float32, jnp.bfloat16
    rows, width = residual_grad.shape
    piece = width // 2
    chunk = 16
    y_line = scratch[4]
    begin, process, join, done = collector(nz, nc, pick_t, ((y,) + scratch[:5],), scratch[5:])
    greet(nz, nc, True)

    bufs = ((dw, dw_up, dw_down), (dwo, dwo_up, dwo_down))
    outs = (dw_next, dwo_next)

    def hop(way, step, k, target):
        src = outs[k].at[way, step]
        return remote(src, bufs[k][1 + way].at[step], line_s.at[way, step, k], line_r.at[way, step, k], fsdp=target)

    def add_to(k, way, step, shard, joined):
        own, out = bufs[k][0], outs[k]
        got = bufs[k][1 + way]
        height = own.shape[2]
        tile = 32

        @pl.loop(0, nc * (height // tile))
        def _(n):
            q, at = n // (height // tile), pl.ds(pl.multiple_of(lax.rem(n, height // tile) * tile, tile), tile)
            value = own[shard, q, at, :]
            if joined:
                value = (value.astype(f32) + got[step, q, at, :].astype(f32)).astype(bf16)
            out[way, step, q, at, :] = value

    def line_one(step, way):
        shard = nz - 1 - step if way == 0 else step
        ahead = z + 1 if way == 0 else z - 1
        behind = z - 1 if way == 0 else z + 1
        first = z == 0 if way == 0 else z == nz - 1
        sends = shard > z if way == 0 else shard < z
        gets = (z > 0) & (shard >= z) if way == 0 else (z < nz - 1) & (shard <= z)

        @pl.when(gets)
        def _():
            for k in range(2):
                hop(way, step, k, behind).wait_recv()

        @pl.when(sends & jnp.logical_not(first))
        def _():
            for k in range(2):
                add_to(k, way, step, shard, True)
                hop(way, step, k, ahead).start()

    def line_step(step):
        @pl.when(2 * z < nz)
        def _():
            line_one(step, 0)
            line_one(step, 1)

        @pl.when(2 * z >= nz)
        def _():
            line_one(step, 1)
            line_one(step, 0)

    def line_begin():
        for way in range(2):
            first = z == 0 if way == 0 else z == nz - 1

            @pl.when(first)
            def _():
                for step in range(nz - 1):
                    shard = nz - 1 - step if way == 0 else step
                    for k in range(2):
                        add_to(k, way, step, shard, False)
                        hop(way, step, k, z + 1 if way == 0 else z - 1).start()

    def sib_copy(q):
        return remote(part.at[q, 1 - t], sib.at[q], sib_s.at[q], sib_r.at[q], tp=1 - t)

    def rs_copy(step, target):
        return remote(rs_send.at[step], rs_recv.at[step], rs_s.at[step], rs_r.at[step], ctx=target)

    for step in range(1, nc + 1):
        sib_copy(ring(c, step, nc)).start()
    line_begin()
    for step in range(1, nc):
        q = ring(c, step, nc)
        sib_copy(q).wait_recv()

        @pl.loop(0, rows // chunk)
        def _(k):
            at = pl.ds(pl.multiple_of(k * chunk, chunk), chunk)
            rs_send[step - 1, at, :] = (part[q, t, at, :].astype(f32) + sib[q, at, :].astype(f32)).astype(bf16)

        rs_copy(step - 1, q).start()
    sib_copy(c).wait_recv()
    begin(0)
    line_step(0)
    begin(1)
    for step in range(1, nc):
        rs_copy(step - 1, c).wait_recv()
    gain_acc[...] = jnp.zeros_like(gain_acc)

    @pl.loop(0, rows // chunk)
    def _(k):
        at = pl.ds(pl.multiple_of(k * chunk, chunk), chunk)
        full = pl.ds(pl.multiple_of(t * rows + k * chunk, chunk), chunk)
        grad = part[c, t, at, :].astype(f32) + sib[c, at, :].astype(f32)
        for step in range(nc - 1):
            grad = grad + rs_recv[step, at, :].astype(f32)
        x = tok[full, :].astype(f32)
        inv = lax.rsqrt(jnp.mean(x * x, -1, keepdims=True) + EPS)
        gain_acc[...] += jnp.sum((grad * x * inv).reshape(chunk // 8, 8, width), 0)
        weighted = grad * gain[...]
        inner = jnp.sum(weighted * x, -1, keepdims=True)
        out = residual_grad[at, :] + inv * weighted - x * (inv * inv * inv) * inner / width
        tok_grad[at, :] = out.astype(bf16)
        tokens_grad[full, :] = out.astype(bf16)

    def grad_copy(core):
        return remote(
            tok_grad, tokens_grad.at[pl.ds(pl.multiple_of(core * rows, rows), rows)], tg_s, tg_r, tp=1 - t
        )

    grad_copy(t).start()

    small_a[...] = small[...]
    total = jnp.sum(gain_acc[...], 0, keepdims=True)
    for strip in range(nz * nc):
        small_a[strip // nc, strip % nc, pl.ds(17, 1), :] = total[:, strip * 128 : (strip + 1) * 128]

    def small_copy(step, shard, target):
        return remote(small_a.at[shard], small_line.at[step], sm_s.at[step], sm_r.at[step], fsdp=target)

    def plane_copy(step, shard, target):
        return remote(small_b.at[shard], small_plane.at[step], sp_s.at[step], sp_r.at[step], ctx=target)

    for step in range(1, nz):
        small_copy(step - 1, ring(z, step, nz), ring(z, step, nz)).start()
    line_step(1)
    process(0)
    line_step(2)
    process(1)
    for step in range(1, nz):
        small_copy(step - 1, z, z).wait_recv()
    value = small_a[z]
    for step in range(nz - 1):
        value = value + small_line[step]
    small_b[...] = value
    for step in range(1, nc):
        plane_copy(step - 1, ring(c, step, nc), ring(c, step, nc)).start()

    def close(k, out, to):
        own, up, down = bufs[k]
        height = own.shape[2]
        tile = 32

        @pl.loop(0, nc * (height // tile))
        def _(n):
            q, at = n // (height // tile), pl.ds(pl.multiple_of(lax.rem(n, height // tile) * tile, tile), tile)
            base = own[z, q, at, :].astype(f32)
            above = up[jnp.minimum(nz - 1 - z, nz - 2), q, at, :].astype(f32)
            below = down[jnp.minimum(z, nz - 2), q, at, :].astype(f32)
            base = base + jnp.where(z > 0, above, 0.0) + jnp.where(z < nz - 1, below, 0.0)
            to[q, at, :] = base.astype(bf16)

    close(0, dw_out, dw_to)
    close(1, dwo_out, dwo_to)

    def to_copy(k, step, source, target):
        src, dst = ((dw_to, dw_out), (dwo_to, dwo_out))[k]
        return remote(src.at[target], dst.at[source], to_s.at[k, step], to_r.at[k, step], ctx=target)

    for step in range(1, nc):
        for k in range(2):
            to_copy(k, step - 1, c, ring(c, step, nc)).start()
    def layer_copy(core):
        return remote(
            layer_send.at[:, pl.ds(pl.multiple_of((1 - t) * piece, piece), piece)],
            layer.at[pl.ds(pl.multiple_of(core * rows, rows), rows)],
            lay_s, lay_r, tp=1 - t,
        )

    join()

    @pl.loop(0, rows // chunk)
    def _(k):
        at = pl.ds(pl.multiple_of(k * chunk, chunk), chunk)
        full = pl.ds(pl.multiple_of(t * rows + k * chunk, chunk), chunk)
        total = residual[at, :]
        for source in range(nz):
            total = total + y_line[source, at, :].astype(f32)
        layer_send[at, :] = total.astype(bf16)
        layer[full, :] = layer_send[at, pl.ds(pl.multiple_of(t * piece, piece), piece)]

    layer_copy(t).start()
    dw_out[c, :, :] = dw_to[c, :, :]
    dwo_out[c, :, :] = dwo_to[c, :, :]
    for step in range(1, nc):
        plane_copy(step - 1, c, c).wait_recv()
    value = small_b[c]
    for step in range(nc - 1):
        value = value + small_plane[step]
    small_out[...] = value
    final = remote(small_out, small_sib, ss_s, ss_r, tp=1 - t)
    final.start()
    final.wait()
    small_out[...] = value + small_sib[...]
    for step in range(1, nc):
        source = ring(c, -step, nc)
        for k in range(2):
            src, dst = ((dw_to, dw_out), (dwo_to, dwo_out))[k]
            remote(
                src.at[c], dst.at[source], to_s.at[k, step - 1], to_r.at[k, step - 1], ctx=source
            ).wait_recv()
    grad_copy(1 - t).wait_recv()
    grad_copy(t).wait_send()
    layer_copy(1 - t).wait_recv()
    layer_copy(t).wait_send()
    done()
    for step in range(1, nc):
        for k in range(2):
            to_copy(k, step - 1, c, ring(c, step, nc)).wait_send()
        plane_copy(step - 1, ring(c, step, nc), ring(c, step, nc)).wait_send()
        rs_copy(step - 1, c).wait_send()
    for step in range(1, nz):
        small_copy(step - 1, ring(z, step, nz), ring(z, step, nz)).wait_send()
    for q in range(nc):
        sib_copy(q).wait_send()
    for step in range(nz - 1):
        for way in range(2):
            shard = nz - 1 - step if way == 0 else step
            ahead = z + 1 if way == 0 else z - 1
            sends = shard > z if way == 0 else shard < z

            @pl.when(sends)
            def _():
                for k in range(2):
                    hop(way, step, k, ahead).wait_send()


def finish(part, tok, gain, residual_grad, dw, dwo, small, y, pick_t, residual):
    nz, nc = lax.axis_size("fsdp"), lax.axis_size("ctx")
    rows, width = residual_grad.shape
    dma = pltpu.SemaphoreType.DMA
    bf16, f32 = jnp.bfloat16, jnp.float32
    vmem = pl.BlockSpec(memory_space=pltpu.VMEM)
    one, two = dw.shape[1:], dwo.shape[1:]
    bufs, sems = collector_scratch(nz, nc, y.shape[2], rows, (width,))
    tiny = small.shape[2:]
    return pl.pallas_call(
        functools.partial(final_kernel, nz, nc),
        out_shape=[
            jax.ShapeDtypeStruct((2 * rows, width), bf16),
            jax.ShapeDtypeStruct(one, bf16),
            jax.ShapeDtypeStruct(two, bf16),
            jax.ShapeDtypeStruct(tiny, f32),
            jax.ShapeDtypeStruct((2 * rows, width // 2), bf16),
        ],
        in_specs=[vmem] * 7 + [pl.BlockSpec(memory_space=pl.ANY)] + [vmem] * 2,
        out_specs=[vmem] * 5,
        scratch_shapes=[
            pltpu.VMEM((nc, rows, width), bf16),
            pltpu.VMEM((nc - 1, rows, width), bf16),
            pltpu.VMEM((nc - 1, rows, width), bf16),
            pltpu.VMEM((rows, width), bf16),
            pltpu.VMEM((8, width), f32),
            pltpu.VMEM((nz - 1,) + one, bf16),
            pltpu.VMEM((nz - 1,) + one, bf16),
            pltpu.VMEM((nz - 1,) + two, bf16),
            pltpu.VMEM((nz - 1,) + two, bf16),
            pltpu.VMEM(one, bf16),
            pltpu.VMEM(two, bf16),
            pltpu.VMEM((2, nz - 1) + one, bf16),
            pltpu.VMEM((2, nz - 1) + two, bf16),
            pltpu.VMEM((nz - 1,) + small.shape[1:], f32),
            pltpu.VMEM((nc - 1,) + tiny, f32),
            pltpu.VMEM(tiny, f32),
            pltpu.VMEM(small.shape, f32),
            pltpu.VMEM(small.shape[1:], f32),
            dma((nc,)), dma((nc,)), dma((nc - 1,)), dma((nc - 1,)),
            dma((2, nz - 1, 2)), dma((2, nz - 1, 2)),
            dma((2, nc - 1)), dma((2, nc - 1)), dma, dma,
            dma((nz - 1,)), dma((nz - 1,)), dma((nc - 1,)), dma((nc - 1,)), dma, dma,
            pltpu.VMEM((rows, width), bf16), dma, dma,
        ] + bufs + sems,
        compiler_params=pltpu.CompilerParams(
            collective_id=3, has_side_effects=True, vmem_limit_bytes=60 * 2**20
        ),
    )(part, tok, gain, residual_grad, dw, dwo, small, y, pick_t, residual)


def attention_kernel(
    scale, x, gain, w_qkv, tables, gains, w_o,
    normed, proj, queries, keys, values, context, part,
):
    f32, bf16 = jnp.float32, jnp.bfloat16
    tall, local = queries.shape
    width = x.shape[1]
    heads = local // HD
    small, chunk, span = 32, 256, 256

    @pl.loop(0, tall // small)
    def _(n):
        rows = pl.ds(pl.multiple_of(n * small, small), small)
        value = x[rows, :].astype(f32)
        inv = lax.rsqrt(jnp.mean(value * value, -1, keepdims=True) + EPS)
        normed[rows, :] = (value * inv * gain[...]).astype(bf16)

    @pl.loop(0, 3 * local // span)
    def _(n):
        at = pl.ds(pl.multiple_of(n * span, span), span)
        proj[:, at] = jnp.dot(normed[...], w_qkv[:, at], preferred_element_type=f32)

    @pl.loop(0, tall // chunk)
    def _(n):
        rows = pl.ds(pl.multiple_of(n * chunk, chunk), chunk)
        cos, sin = tables[rows, pl.ds(0, HD)], tables[rows, pl.ds(HD, HD)]
        for head in range(heads):
            at = pl.ds(head * HD, HD)
            for kind, out in enumerate((queries, keys)):
                value = proj[rows, pl.ds(kind * local + head * HD, HD)]
                inv = lax.rsqrt(jnp.mean(value * value, -1, keepdims=True) + EPS)
                value = value * inv * gains[pl.ds(kind, 1), :]
                out[rows, at] = (value * cos - pltpu.roll(value, HD // 2, 1) * sin).astype(bf16)
        values[rows, :] = proj[rows, pl.ds(2 * local, local)].astype(bf16)

    @pl.loop(0, tall // chunk)
    def _(n):
        rows = pl.ds(pl.multiple_of(n * chunk, chunk), chunk)
        for head in range(heads):
            at = pl.ds(head * HD, HD)
            scores = lax.dot_general(
                queries[rows, at], keys[:, at], (((1,), (1,)), ((), ())), preferred_element_type=f32
            ) * scale
            raised = jnp.exp(scores - jnp.max(scores, -1, keepdims=True))
            probs = (raised / jnp.sum(raised, -1, keepdims=True)).astype(bf16)
            context[rows, at] = jnp.dot(probs, values[:, at], preferred_element_type=f32).astype(bf16)

    @pl.loop(0, width // span)
    def _(n):
        at = pl.ds(pl.multiple_of(n * span, span), span)
        part[:, at] = jnp.dot(context[...], w_o[:, at], preferred_element_type=f32).astype(bf16)


def attention(x, gain, w_qkv, tables, gains, w_o):
    bf16, f32 = jnp.bfloat16, jnp.float32
    tall, width = x.shape
    local = w_o.shape[0]
    vmem = pl.BlockSpec(memory_space=pltpu.VMEM)
    shapes = [
        ((tall, width), bf16),
        ((tall, 3 * local), f32),
        ((tall, local), bf16),
        ((tall, local), bf16),
        ((tall, local), bf16),
        ((tall, local), bf16),
        ((tall, width), bf16),
    ]
    return pl.pallas_call(
        functools.partial(attention_kernel, 1.0 / math.sqrt(HD)),
        out_shape=[jax.ShapeDtypeStruct(shape, kind) for shape, kind in shapes],
        in_specs=[vmem] * 6,
        out_specs=[vmem] * 7,
        compiler_params=pltpu.CompilerParams(vmem_limit_bytes=56 * 2**20),
    )(x, gain, w_qkv, tables, gains, w_o)


def attention_back_kernel(
    scale, *refs,
):
    sources, refs = refs[:11], refs[11:]
    part, dw, dwo, q_sum, k_sum = refs[:5]
    held, refs = refs[5:16], refs[16:]
    grad_ctx, gq, gk, gv, grads, sem = refs
    grad_attn, w_o, queries, keys, values, proj, tables, gains, context, normed, w_qkv = held
    f32, bf16 = jnp.float32, jnp.bfloat16
    tall, local = queries.shape
    heads = local // HD
    width = grad_attn.shape[1]
    copies = [pltpu.make_async_copy(src, dst, sem.at[k]) for k, (src, dst) in enumerate(zip(sources, held))]
    for copy in copies:
        copy.start()
    for copy in copies[:5]:
        copy.wait()

    def nt(left, right):
        return lax.dot_general(left, right, (((1,), (1,)), ((), ())), preferred_element_type=f32)

    def tn(left, right):
        return lax.dot_general(left, right, (((0,), (0,)), ((), ())), preferred_element_type=f32)

    grad_ctx[...] = nt(grad_attn[...], w_o[...]).astype(bf16)
    gk[...] = jnp.zeros_like(gk)
    gv[...] = jnp.zeros_like(gv)
    q_sum[...] = jnp.zeros_like(q_sum)
    k_sum[...] = jnp.zeros_like(k_sum)
    chunk = 256

    @pl.loop(0, tall // chunk)
    def _(n):
        rows = pl.ds(pl.multiple_of(n * chunk, chunk), chunk)
        for head in range(heads):
            at = pl.ds(head * HD, HD)
            q, k, v, g = queries[rows, at], keys[:, at], values[:, at], grad_ctx[rows, at]
            scores = nt(q, k) * scale
            raised = jnp.exp(scores - jnp.max(scores, -1, keepdims=True))
            probs = raised / jnp.sum(raised, -1, keepdims=True)
            grad_probs = nt(g, v)
            inner = jnp.sum(probs * grad_probs, -1, keepdims=True)
            grad_scores = (probs * (grad_probs - inner)).astype(bf16)
            gq[rows, at] = jnp.dot(grad_scores, k, preferred_element_type=f32) * scale
            gk[:, at] += tn(grad_scores, q)
            gv[:, at] += tn(probs.astype(bf16), g)

    for copy in copies[5:8]:
        copy.wait()

    @pl.loop(0, tall // chunk)
    def _(n):
        rows = pl.ds(pl.multiple_of(n * chunk, chunk), chunk)
        cos, sin = tables[rows, pl.ds(0, HD)], tables[rows, pl.ds(HD, HD)]
        for head in range(heads):
            for kind, total in enumerate((q_sum, k_sum)):
                at = pl.ds(head * HD, HD)
                column = pl.ds(kind * local + head * HD, HD)
                grad = gq[rows, at] if kind == 0 else gk[rows, at] * scale
                grad = grad * cos + pltpu.roll(grad, HD // 2, 1) * sin
                value = proj[rows, column]
                inv = lax.rsqrt(jnp.mean(value * value, -1, keepdims=True) + EPS)
                total[...] += jnp.sum((grad * value * inv).reshape(chunk // 8, 8, HD), 0)
                weighted = grad * gains[pl.ds(kind, 1), :]
                inner = jnp.sum(weighted * value, -1, keepdims=True)
                out = inv * weighted - value * (inv * inv * inv) * inner / HD
                grads[rows, column] = out.astype(bf16)
        grads[rows, pl.ds(2 * local, local)] = gv[rows, :].astype(bf16)

    for copy in copies[8:]:
        copy.wait()
    span = 256
    strip = dwo.shape[2]

    @pl.loop(0, width // span)
    def _(n):
        full = pl.ds(pl.multiple_of(n * span, span), span)
        dw[full, :] = tn(normed[:, full], grads[...]).astype(bf16)
        part[:, full] = nt(grads[...], w_qkv[full, :]).astype(bf16)
        value = tn(context[...], grad_attn[:, full]).astype(bf16)
        for i in range(span // strip):
            dwo[n * (span // strip) + i] = value[:, i * strip : (i + 1) * strip]


def attention_back(grad_attn, w_o, queries, keys, values, proj, tables, gains, context, normed, w_qkv, strip):
    bf16, f32 = jnp.bfloat16, jnp.float32
    tall, width = grad_attn.shape
    local = queries.shape[1]
    vmem = pl.BlockSpec(memory_space=pltpu.VMEM)
    sources = (grad_attn, w_o, queries, keys, values, proj, tables, gains, context, normed, w_qkv)
    return pl.pallas_call(
        functools.partial(attention_back_kernel, 1.0 / math.sqrt(HD)),
        out_shape=[
            jax.ShapeDtypeStruct((tall, width), bf16),
            jax.ShapeDtypeStruct((width, 3 * local), bf16),
            jax.ShapeDtypeStruct((width // strip, local, strip), bf16),
            jax.ShapeDtypeStruct((8, HD), f32),
            jax.ShapeDtypeStruct((8, HD), f32),
        ],
        in_specs=[pl.BlockSpec(memory_space=pl.ANY)] * len(sources),
        out_specs=[vmem] * 5,
        scratch_shapes=[pltpu.VMEM(source.shape, source.dtype) for source in sources]
        + [
            pltpu.VMEM((tall, local), bf16),
            pltpu.VMEM((tall, local), f32),
            pltpu.VMEM((tall, local), f32),
            pltpu.VMEM((tall, local), f32),
            pltpu.VMEM((tall, 3 * local), bf16),
            pltpu.SemaphoreType.DMA((len(sources),)),
        ],
        compiler_params=pltpu.CompilerParams(vmem_limit_bytes=60 * 2**20),
    )(*sources)


def one_chip(
    tokens,
    w_query,
    w_key,
    w_value,
    w_out,
    gain_attn,
    gain_query,
    gain_key,
    gain_moe,
    w_router,
    w_experts,
    routes,
    cotangent,
):
    z, c, t = lax.axis_index("fsdp"), lax.axis_index("ctx"), lax.axis_index("tp")
    nz, nc = lax.axis_size("fsdp"), lax.axis_size("ctx")
    block, width = tokens.shape[1], tokens.shape[2]
    rows = block // 2
    tall = block * nc
    deep = width // nz
    ffn = w_experts.shape[3]
    most = block * TOPK * 9 // (8 * E)
    bf16, f32 = jnp.bfloat16, jnp.float32

    token_half = lax.dynamic_slice_in_dim(tokens[0], t * rows, rows, 0)
    cotan_half = lax.dynamic_slice_in_dim(cotangent[0], t * rows, rows, 0)
    local = w_query.shape[1] // nc
    small = jnp.concatenate([w_router.T.reshape(-1), gain_attn, gain_moe, gain_query, gain_key])
    total = small.shape[0]
    small = jnp.pad(small, (0, -total % 2048))
    small = small.reshape(-1, 128)
    ids = jnp.arange(E, dtype=jnp.int32)
    named = jnp.any(routes[0][:, :, None] == ids, 1)
    below = jnp.tril(jnp.ones((block, block), bf16), -1)
    rank = jnp.where(named, dot(below, named.astype(bf16)), -1.0).T
    x_rows, w_qkv, w_o, small, _, rank_seq, pick, cot_rows, pair, third, middle = load(
        tokens[0], cotangent[0], w_query, w_key, w_value, w_out, small, rank, w_experts, most
    )
    w_qkv = w_qkv.reshape(width, 3 * local)
    w_o = w_o.transpose(1, 0, 2).reshape(local, width)
    small = small.reshape(nz, -1)
    router = small[:, : E * deep].reshape(nz, E, deep).transpose(1, 0, 2).reshape(E, width)
    at = E * deep
    attn_gain = small[:, at : at + deep].reshape(-1).astype(f32)
    moe_gain = small[:, at + deep : at + 2 * deep].reshape(-1).astype(f32)
    at, part = at + 2 * deep, HD // nz
    query_gain = small[:, at : at + part].reshape(-1).astype(f32)
    key_gain = small[:, at + part : at + 2 * part].reshape(-1).astype(f32)

    pair = exchange(pair, "fsdp")

    counts = jnp.sum((rank_seq >= 0).astype(f32), 2)
    earlier = jnp.sum(jnp.where(jnp.arange(nc)[:, None] < c, counts, 0.0), 0)
    kept = ((rank >= 0) & (rank + earlier[:, None] < CAP)).astype(f32).T
    kept = lax.dynamic_slice_in_dim(kept, t * rows, rows, 0)

    half_dim = HD // 2
    inv_freq = jnp.exp(jnp.arange(half_dim, dtype=f32) * (-2.0 * math.log(ROPE_BASE) / HD))
    angles = jnp.arange(tall, dtype=jnp.int32).astype(f32)[:, None] * inv_freq[None, :]
    cosines, sines = jnp.cos(angles), jnp.sin(angles)
    tables = jnp.concatenate([cosines, cosines, sines, -sines], 1)
    gains = jnp.pad(jnp.stack([query_gain, key_gain]), ((0, 6), (0, 0)))
    normed_one, proj, queries, keys, values, context, attn_part = attention(
        x_rows, attn_gain[None], w_qkv, tables, gains, w_o
    )
    attn_part = attn_part.reshape(nc, 2, rows, width)
    kept_wide = jnp.pad(kept, ((0, 0), (0, 128 - E)))
    router_wide = jnp.pad(router, ((0, 128 - E), (0, 0)))
    residual, normed_two, router_probs, x_in, g_in, third = dispatch(
        attn_part, tokens[0], moe_gain[None], router_wide, kept_wide, pick, third, middle
    )
    pair, x_in = lax.optimization_barrier((pair, x_in))
    x_in = x_in.reshape(nc * 2 * most, width)
    cot_rows = cot_rows.reshape(nc * 2 * most, width)
    chips = nz * nc
    strip = width // chips
    out_rows, back_rows, pair_rows, hid, gg, gu = experts(
        x_in, cot_rows, g_in.reshape(nc * 2 * most, -1), pair, third
    )
    shape = (nc, 2, most, -1)
    pick_t = pick.transpose(0, 2, 1)
    grad_logits, dgain_moe, grad_residual, grad_attn, dw_gate, own_grad, other_grad = give_back(
        back_rows.reshape(shape),
        pair_rows.reshape(shape),
        x_in,
        cot_rows,
        hid,
        gg,
        gu,
        pick_t,
        residual,
        router_probs,
        kept_wide,
        router_wide,
        moe_gain[None],
        cotangent[0],
    )

    dw_router = dot_tn(normed_two, grad_logits[:, :E])
    dgain_moe = jnp.sum(dgain_moe, 0)
    dw_rest = (own_grad.astype(f32) + other_grad.astype(f32)).astype(bf16)
    dw_rest, grad_attn = lax.optimization_barrier((dw_rest, grad_attn))
    dw_rest = exchange(dw_rest, ("fsdp", "ctx"))
    grad_attn = grad_attn.reshape(tall, width)

    grad_normed_part, dw_qkv, dw_out, dgain_query, dgain_key = attention_back(
        grad_attn,
        w_o,
        queries,
        keys,
        values,
        proj,
        tables,
        gains,
        context,
        normed_one,
        w_qkv,
        strip,
    )
    dgain_query, dgain_key = jnp.sum(dgain_query, 0), jnp.sum(dgain_key, 0)
    grad_normed_part = grad_normed_part.reshape(nc, 2, rows, width)
    head_part = HD // chips
    heads = [dgain_query.reshape(chips, 1, head_part), dgain_key.reshape(chips, 1, head_part)]
    heads = jnp.pad(jnp.concatenate(heads, 2), ((0, 0), (0, 0), (0, strip - 2 * head_part)))
    sums = jnp.concatenate(
        [
            dw_router.reshape(chips, E, strip),
            dgain_moe.reshape(chips, 1, strip),
            jnp.zeros((chips, 1, strip), f32),
            heads,
            jnp.zeros((chips, 24 - E - 3, strip), f32),
        ],
        1,
    ).reshape(nz, nc, 24, strip)
    tokens_grad, got_qkv, got_out, sums, layer_out = finish(
        grad_normed_part,
        tokens[0],
        attn_gain[None],
        grad_residual,
        dw_qkv.reshape(nz, nc, strip, 3 * local),
        dw_out.reshape(nz, nc, local, strip),
        sums,
        out_rows.reshape(shape),
        pick_t,
        residual,
    )
    dw_experts = lay_out(dw_gate, dw_rest, nz, nc)
    got_qkv = got_qkv.astype(f32).reshape(nc, strip, 3, local)
    got_qkv = got_qkv.transpose(2, 1, 0, 3).reshape(3, strip, nc * local)
    return (
        layer_out[None],
        tokens_grad[None],
        got_qkv[0],
        got_qkv[1],
        got_qkv[2],
        got_out.astype(f32).reshape(nc * local, strip),
        sums[E + 1],
        sums[E + 2, :head_part],
        sums[E + 2, head_part : 2 * head_part],
        sums[E],
        sums[:E].reshape(strip, E),
        dw_experts,
    )


def solution(mesh):
    chips = mesh.shape["fsdp"] * mesh.shape["ctx"]
    plain = chips == E and mesh.shape["fsdp"] == 4 and mesh.shape["tp"] == 2
    return jax.shard_map(
        one_chip if plain else general,
        mesh=mesh,
        in_specs=(
            P("fsdp", "ctx", None),
            P("fsdp", "tp"),
            P("fsdp", "tp"),
            P("fsdp", "tp"),
            P("tp", "fsdp"),
            P("fsdp"),
            P("fsdp"),
            P("fsdp"),
            P("fsdp"),
            P("fsdp", None),
            P("fsdp", None, None, "tp"),
            P("fsdp", "ctx", None),
            P("fsdp", "ctx", None),
        ),
        out_specs=(
            P("fsdp", "ctx", "tp"),
            P("fsdp", "ctx", None),
            P(("fsdp", "ctx"), "tp"),
            P(("fsdp", "ctx"), "tp"),
            P(("fsdp", "ctx"), "tp"),
            P("tp", ("fsdp", "ctx")),
            P(("fsdp", "ctx")),
            P(("fsdp", "ctx")),
            P(("fsdp", "ctx")),
            P(("fsdp", "ctx")),
            P(("fsdp", "ctx"), None),
            P(("fsdp", "ctx"), None, None, "tp"),
        ),
        check_vma=False,
    )
```

```python
import functools
import math

import jax
import jax.numpy as jnp
from jax import lax
from jax.experimental import pallas as pl
from jax.experimental.pallas import tpu as pltpu
from jax.sharding import PartitionSpec as P

HD = 128
TOPK = 8
E = 16
CAP = 512
MESH = pl.DeviceIdType.MESH


EPS = 1e-06
ROPE_BASE = 10000.0


def prefix(value, axis, join, neutral):
    count, mine = (lax.axis_size(axis), lax.axis_index(axis))
    pieces = lax.all_gather(value, axis)
    running = jnp.full_like(value, 0) + jnp.asarray(neutral, value.dtype)

    def lap(position, running):
        longer = join(running, pieces[position])
        return jnp.where(position < mine, longer, running)

    return lax.fori_loop(0, count - 1, lap, running)


def rms_scale(values):
    return lax.rsqrt(jnp.mean(values * values, -1, keepdims=True) + EPS)


def norm_back(grad_normed, values, inv_rms, gain_vec):
    weighted = grad_normed * gain_vec.astype(jnp.float32)
    inner_sum = jnp.sum(weighted * values, -1, keepdims=True)
    return (
        inv_rms * weighted - values * (inv_rms * inv_rms * inv_rms) * inner_sum / values.shape[-1]
    )


def rope_tables(first, length):
    half_dim = HD // 2
    inv_freq = jnp.exp(jnp.arange(half_dim, dtype=jnp.float32) * (-2.0 * math.log(ROPE_BASE) / HD))
    places = (first + jnp.arange(length, dtype=jnp.int32)).astype(jnp.float32)
    angles = places[:, None] * inv_freq[None, :]
    cos_table = jnp.cos(angles)
    sin_table = jnp.sin(angles)
    cos_full = jnp.concatenate([cos_table, cos_table], -1)[:, None, :]
    sin_full = jnp.concatenate([sin_table, sin_table], -1)[:, None, :]
    return (cos_full, sin_full)


def rotate(values):
    half_dim = values.shape[-1] // 2
    return jnp.concatenate([-values[..., half_dim:], values[..., :half_dim]], -1)


def rotate_back(values):
    half_dim = values.shape[-1] // 2
    return jnp.concatenate([values[..., half_dim:], -values[..., :half_dim]], -1)


def apply_rope(values, cos_full, sin_full):
    return values * cos_full + rotate(values) * sin_full


def rope_back(grads, cos_full, sin_full):
    return grads * cos_full + rotate_back(grads * sin_full)


def add_counts(earlier, later):
    return earlier + later


def general(
    tokens,
    w_query,
    w_key,
    w_value,
    w_out,
    gain_attn,
    gain_query,
    gain_key,
    gain_moe,
    w_router,
    w_experts,
    routes,
    cotangent,
):
    seq_count, block_len, model_width = tokens.shape
    row_count = seq_count * block_len
    (
        full_query,
        full_key,
        full_value,
        full_out,
        router_full,
        attn_gain,
        query_gain,
        key_gain,
        moe_gain,
    ) = (
        lax.all_gather(w_query, "fsdp", axis=0, tiled=True),
        lax.all_gather(w_key, "fsdp", axis=0, tiled=True),
        lax.all_gather(w_value, "fsdp", axis=0, tiled=True),
        lax.all_gather(w_out, "fsdp", axis=1, tiled=True),
        lax.all_gather(w_router, "fsdp", axis=0, tiled=True),
        lax.all_gather(gain_attn, "fsdp", axis=0, tiled=True),
        lax.all_gather(gain_query, "fsdp", axis=0, tiled=True),
        lax.all_gather(gain_key, "fsdp", axis=0, tiled=True),
        lax.all_gather(gain_moe, "fsdp", axis=0, tiled=True),
    )
    local_width = full_query.shape[1]
    head_count = local_width // HD
    head_shape = (seq_count, block_len, head_count, HD)
    token_rows = tokens.reshape(row_count, model_width).astype(jnp.float32)
    inv_one = rms_scale(token_rows)
    normed_one = (token_rows * inv_one * attn_gain.astype(jnp.float32)).astype(jnp.bfloat16)
    query_proj = jnp.dot(normed_one, full_query, preferred_element_type=jnp.float32)
    key_proj = jnp.dot(normed_one, full_key, preferred_element_type=jnp.float32)
    value_proj = jnp.dot(normed_one, full_value, preferred_element_type=jnp.float32)
    cos_full, sin_full = rope_tables(lax.axis_index("ctx") * block_len, block_len)
    query_heads = query_proj.reshape(head_shape)
    key_heads = key_proj.reshape(head_shape)
    query_inv = rms_scale(query_heads)
    key_inv = rms_scale(key_heads)
    queries = apply_rope(
        query_heads * query_inv * query_gain.astype(jnp.float32), cos_full, sin_full
    ).astype(jnp.bfloat16)
    keys_local = apply_rope(
        key_heads * key_inv * key_gain.astype(jnp.float32), cos_full, sin_full
    ).astype(jnp.bfloat16)
    keys_local = keys_local.reshape(seq_count, block_len, local_width)
    values_local = value_proj.astype(jnp.bfloat16).reshape(seq_count, block_len, local_width)
    keys_all, values_all = (
        lax.all_gather(keys_local, "ctx", axis=1, tiled=True),
        lax.all_gather(values_local, "ctx", axis=1, tiled=True),
    )
    seq_len = keys_all.shape[1]
    key_rows = keys_all.reshape(seq_count, seq_len, head_count, HD)
    value_rows = values_all.reshape(seq_count, seq_len, head_count, HD)
    score_scale = 1.0 / math.sqrt(HD)
    scores = (
        jnp.einsum("sqhd,skhd->shqk", queries, key_rows, preferred_element_type=jnp.float32)
        * score_scale
    )
    maximum = jnp.max(scores, -1, keepdims=True)
    exp_scores = jnp.exp(scores - maximum)
    denominator = jnp.sum(exp_scores, -1, keepdims=True)
    attn_probs = exp_scores / denominator
    log_total = maximum + jnp.log(denominator)
    context = jnp.einsum(
        "shqk,skhd->sqhd",
        attn_probs.astype(jnp.bfloat16),
        value_rows,
        preferred_element_type=jnp.float32,
    )
    context = context.astype(jnp.bfloat16).reshape(row_count, local_width)
    attn_part = jnp.dot(context, full_out, preferred_element_type=jnp.float32)
    residual = token_rows + lax.psum(attn_part, "tp")
    inv_two = rms_scale(residual)
    normed_two = (residual * inv_two * moe_gain.astype(jnp.float32)).astype(jnp.bfloat16)
    logits = jnp.dot(normed_two, router_full, preferred_element_type=jnp.float32)
    router_probs = jax.nn.softmax(logits, -1)
    pair_count = block_len * TOPK
    route_rows = routes.reshape(seq_count, pair_count)
    expert_ids = jnp.arange(E, dtype=jnp.int32)
    onehot = (route_rows[:, :, None] == expert_ids[None, None, :]).astype(jnp.int32)
    counts = jnp.sum(onehot, 1, dtype=jnp.int32)
    offsets = prefix(counts, "ctx", add_counts, jnp.zeros_like(counts))
    earlier = jnp.cumsum(onehot, 1, dtype=jnp.int32) - onehot
    local_rank = jnp.sum(earlier * onehot, 2, dtype=jnp.int32)
    slot_base = jnp.sum(onehot * offsets[:, None, :], 2, dtype=jnp.int32)
    kept_mask = (slot_base + local_rank < CAP).astype(jnp.float32).reshape(row_count, TOPK)
    block_most = pair_count * 9 // (8 * E)
    expert_span = seq_count * block_most
    seq_ids = jnp.arange(seq_count, dtype=jnp.int32)[:, None]
    buffer_row = (route_rows * expert_span + seq_ids * block_most + local_rank).reshape(
        row_count * TOPK
    )
    token_ids = (
        seq_ids * block_len + jnp.arange(pair_count, dtype=jnp.int32)[None, :] // TOPK
    ).reshape(row_count * TOPK)
    owner_rows = jnp.zeros((E * expert_span,), jnp.int32).at[buffer_row].set(token_ids)
    onehot_f = onehot.astype(jnp.float32).reshape(row_count, TOPK, E)
    gate_weight = jnp.sum(onehot_f * router_probs[:, None, :], 2) * kept_mask
    slot_weight = (
        jnp.zeros((E * expert_span,), jnp.float32)
        .at[buffer_row]
        .set(gate_weight.reshape(row_count * TOPK))
    )
    expert_rows = normed_two[owner_rows].reshape(E, expert_span, model_width)
    cotan_rows = cotangent.reshape(row_count, model_width)
    grad_expert = (slot_weight[:, None] * cotan_rows[owner_rows].astype(jnp.float32)).astype(
        jnp.bfloat16
    )
    grad_expert = grad_expert.reshape(E, expert_span, model_width)
    ffn_local = w_experts.shape[3]
    fsdp_count = lax.axis_size("fsdp")
    ctx_count = lax.axis_size("ctx")
    group_count = fsdp_count * ctx_count
    sharing = group_count // E
    padded_span = -(-expert_span // sharing) * sharing
    part_span = padded_span // sharing
    target_experts = (
        jnp.arange(fsdp_count, dtype=jnp.int32) * ctx_count + lax.axis_index("ctx")
    ) // sharing
    selected = jnp.take(w_experts, target_experts, axis=2)
    owned = lax.all_to_all(selected, "fsdp", split_axis=2, concat_axis=0, tiled=True)[:, :, 0]
    send_rows = expert_rows.reshape(group_count, part_span, model_width)
    send_grads = grad_expert.reshape(group_count, part_span, model_width)
    recv_rows, recv_grads = (
        lax.all_to_all(send_rows, ("fsdp", "ctx"), split_axis=0, concat_axis=0, tiled=True),
        lax.all_to_all(send_grads, ("fsdp", "ctx"), split_axis=0, concat_axis=0, tiled=True),
    )
    rows_flat = recv_rows.reshape(group_count * part_span, model_width)
    grads_flat = recv_grads.reshape(group_count * part_span, model_width)
    gate_act = jnp.dot(rows_flat, owned[:, 0], preferred_element_type=jnp.float32)
    up_act = jnp.dot(rows_flat, owned[:, 1], preferred_element_type=jnp.float32)
    sigmoid_gate = jax.nn.sigmoid(gate_act)
    silu_gate = gate_act * sigmoid_gate
    hidden = (silu_gate * up_act).astype(jnp.bfloat16)
    produced = jnp.einsum("mf,df->md", hidden, owned[:, 2], preferred_element_type=jnp.float32)
    grad_hidden = jnp.dot(grads_flat, owned[:, 2], preferred_element_type=jnp.float32)
    grad_gate = (
        grad_hidden * up_act * sigmoid_gate * (1.0 + gate_act * (1.0 - sigmoid_gate))
    ).astype(jnp.bfloat16)
    grad_up = (grad_hidden * silu_gate).astype(jnp.bfloat16)
    rows_grad = jnp.einsum("mf,df->md", grad_gate, owned[:, 0], preferred_element_type=jnp.float32)
    rows_grad = rows_grad + jnp.einsum(
        "mf,df->md", grad_up, owned[:, 1], preferred_element_type=jnp.float32
    )
    back_out, back_rows = (
        lax.all_to_all(
            produced.reshape(group_count, part_span, model_width).astype(jnp.bfloat16),
            ("fsdp", "ctx"),
            split_axis=0,
            concat_axis=0,
            tiled=True,
        ).astype(jnp.float32),
        lax.all_to_all(
            rows_grad.reshape(group_count, part_span, model_width).astype(jnp.bfloat16),
            ("fsdp", "ctx"),
            split_axis=0,
            concat_axis=0,
            tiled=True,
        ).astype(jnp.float32),
    )
    expert_out = back_out.reshape(E, padded_span, model_width)
    grad_rows = back_rows.reshape(E, padded_span, model_width)
    gate_term = jnp.einsum("md,mf->df", rows_flat, grad_gate, preferred_element_type=jnp.float32)
    up_term = jnp.einsum("md,mf->df", rows_flat, grad_up, preferred_element_type=jnp.float32)
    down_term = jnp.einsum("md,mf->df", grads_flat, hidden, preferred_element_type=jnp.float32)
    owner_terms = jnp.stack([gate_term, up_term, down_term], 1)[:, :, None, :]
    relaid = lax.all_to_all(
        owner_terms.astype(jnp.bfloat16), ("fsdp", "ctx"), split_axis=0, concat_axis=2, tiled=True
    ).astype(owner_terms.dtype)
    dw_experts = jnp.sum(relaid.reshape(relaid.shape[0], 3, E, sharing, ffn_local), 3)
    picked = expert_out.reshape(E * expert_span, model_width)[buffer_row].reshape(
        row_count, TOPK, model_width
    )
    moe_part = jnp.sum(gate_weight[:, :, None] * picked, 1)
    cotan_float = cotan_rows.astype(jnp.float32)
    grad_gate_part = jnp.sum(picked * cotan_float[:, None, :], 2)
    moe_shard = lax.psum_scatter(
        moe_part.astype(jnp.bfloat16), "tp", scatter_dimension=1, tiled=True
    ).astype(jnp.float32)
    piece_width = moe_shard.shape[1]
    residual_shard = lax.dynamic_slice_in_dim(
        residual, lax.axis_index("tp") * piece_width, piece_width, 1
    )
    layer_out = (
        (residual_shard + moe_shard).astype(jnp.bfloat16).reshape(seq_count, block_len, piece_width)
    )
    grad_normed_part = jnp.sum(
        grad_rows.reshape(E * expert_span, model_width)[buffer_row].reshape(
            row_count, TOPK, model_width
        ),
        1,
    )
    grad_normed_sum, grad_gate_sum = (
        lax.psum(grad_normed_part.astype(jnp.bfloat16), "tp").astype(jnp.float32),
        lax.psum(grad_gate_part.astype(jnp.bfloat16), "tp").astype(jnp.float32),
    )
    grad_pick = grad_gate_sum * kept_mask
    grad_router_probs = jnp.sum(onehot_f * grad_pick[:, :, None], 1)
    grad_logits = router_probs * (
        grad_router_probs - jnp.sum(router_probs * grad_router_probs, -1, keepdims=True)
    )
    grad_logits = grad_logits.astype(jnp.bfloat16)
    grad_router_w = jnp.einsum(
        "nd,ne->de", normed_two, grad_logits, preferred_element_type=jnp.float32
    )
    grad_normed_two = grad_normed_sum + jnp.einsum(
        "ne,de->nd", grad_logits, router_full, preferred_element_type=jnp.float32
    )
    grad_moe_gain = jnp.sum(grad_normed_two * residual * inv_two, 0)
    grad_residual = cotan_float + norm_back(grad_normed_two, residual, inv_two, moe_gain)
    grad_attn = grad_residual.astype(jnp.bfloat16)
    grad_w_out = jnp.einsum("nl,nd->ld", context, grad_attn, preferred_element_type=jnp.float32)
    grad_context = jnp.einsum("nd,ld->nl", grad_attn, full_out, preferred_element_type=jnp.float32)
    grad_context = grad_context.astype(jnp.bfloat16).reshape(head_shape)
    scores = (
        jnp.einsum("sqhd,skhd->shqk", queries, key_rows, preferred_element_type=jnp.float32)
        * score_scale
    )
    attn_probs = jnp.exp(scores - log_total)
    grad_probs = jnp.einsum(
        "sqhd,skhd->shqk", grad_context, value_rows, preferred_element_type=jnp.float32
    )
    grad_scores = attn_probs * (grad_probs - jnp.sum(attn_probs * grad_probs, -1, keepdims=True))
    grad_scores = grad_scores.astype(jnp.bfloat16)
    grad_queries = (
        jnp.einsum("shqk,skhd->sqhd", grad_scores, key_rows, preferred_element_type=jnp.float32)
        * score_scale
    )
    grad_keys_all = (
        jnp.einsum("shqk,sqhd->skhd", grad_scores, queries, preferred_element_type=jnp.float32)
        * score_scale
    )
    grad_values_all = jnp.einsum(
        "shqk,sqhd->skhd",
        attn_probs.astype(jnp.bfloat16),
        grad_context,
        preferred_element_type=jnp.float32,
    )
    grad_keys_own, grad_values_own = (
        lax.psum_scatter(
            grad_keys_all.reshape(seq_count, seq_len, local_width).astype(jnp.bfloat16),
            "ctx",
            scatter_dimension=1,
            tiled=True,
        ).astype(jnp.float32),
        lax.psum_scatter(
            grad_values_all.reshape(seq_count, seq_len, local_width).astype(jnp.bfloat16),
            "ctx",
            scatter_dimension=1,
            tiled=True,
        ).astype(jnp.float32),
    )
    grad_qnormed = rope_back(grad_queries, cos_full, sin_full)
    grad_knormed = rope_back(grad_keys_own.reshape(head_shape), cos_full, sin_full)
    grad_qgain = jnp.sum(grad_qnormed * query_heads * query_inv, (0, 1, 2))
    grad_kgain = jnp.sum(grad_knormed * key_heads * key_inv, (0, 1, 2))
    grad_qproj = (
        norm_back(grad_qnormed, query_heads, query_inv, query_gain)
        .astype(jnp.bfloat16)
        .reshape(row_count, local_width)
    )
    grad_kproj = (
        norm_back(grad_knormed, key_heads, key_inv, key_gain)
        .astype(jnp.bfloat16)
        .reshape(row_count, local_width)
    )
    grad_vproj = grad_values_own.astype(jnp.bfloat16).reshape(row_count, local_width)
    grad_wq = jnp.einsum("nd,nl->dl", normed_one, grad_qproj, preferred_element_type=jnp.float32)
    grad_wk = jnp.einsum("nd,nl->dl", normed_one, grad_kproj, preferred_element_type=jnp.float32)
    grad_wv = jnp.einsum("nd,nl->dl", normed_one, grad_vproj, preferred_element_type=jnp.float32)
    grad_normed_one = jnp.einsum(
        "nl,dl->nd", grad_qproj, full_query, preferred_element_type=jnp.float32
    )
    grad_normed_one = grad_normed_one + jnp.einsum(
        "nl,dl->nd", grad_kproj, full_key, preferred_element_type=jnp.float32
    )
    grad_normed_one = grad_normed_one + jnp.einsum(
        "nl,dl->nd", grad_vproj, full_value, preferred_element_type=jnp.float32
    )
    grad_normed_one, grad_qgain, grad_kgain = (
        lax.psum(grad_normed_one.astype(jnp.bfloat16), "tp").astype(jnp.float32),
        lax.psum(grad_qgain.astype(jnp.bfloat16), "tp").astype(jnp.float32),
        lax.psum(grad_kgain.astype(jnp.bfloat16), "tp").astype(jnp.float32),
    )
    grad_attn_gain = jnp.sum(grad_normed_one * token_rows * inv_one, 0)
    tokens_grad = grad_residual + norm_back(grad_normed_one, token_rows, inv_one, attn_gain)
    tokens_grad = tokens_grad.astype(jnp.bfloat16).reshape(seq_count, block_len, model_width)
    dw_query, dw_key, dw_value, dw_out, dw_router, dgain_attn, dgain_query, dgain_key, dgain_moe = (
        lax.psum_scatter(grad_wq, ("fsdp", "ctx"), scatter_dimension=0, tiled=True),
        lax.psum_scatter(grad_wk, ("fsdp", "ctx"), scatter_dimension=0, tiled=True),
        lax.psum_scatter(grad_wv, ("fsdp", "ctx"), scatter_dimension=0, tiled=True),
        lax.psum_scatter(grad_w_out, ("fsdp", "ctx"), scatter_dimension=1, tiled=True),
        lax.psum_scatter(grad_router_w, ("fsdp", "ctx"), scatter_dimension=0, tiled=True),
        lax.psum_scatter(grad_attn_gain, ("fsdp", "ctx"), scatter_dimension=0, tiled=True),
        lax.psum_scatter(grad_qgain, ("fsdp", "ctx"), scatter_dimension=0, tiled=True),
        lax.psum_scatter(grad_kgain, ("fsdp", "ctx"), scatter_dimension=0, tiled=True),
        lax.psum_scatter(grad_moe_gain, ("fsdp", "ctx"), scatter_dimension=0, tiled=True),
    )
    return (
        layer_out,
        tokens_grad,
        dw_query,
        dw_key,
        dw_value,
        dw_out,
        dgain_attn,
        dgain_query,
        dgain_key,
        dgain_moe,
        dw_router,
        dw_experts,
    )


def swap(value):
    return lax.ppermute(value, "tp", [(0, 1), (1, 0)])


def exchange(value, axes):
    return lax.all_to_all(value, axes, split_axis=0, concat_axis=0, tiled=True)


def spread(value, axes):
    count = lax.axis_size(axes)
    return exchange(jnp.broadcast_to(value[None], (count,) + value.shape), axes)


def dot(left, right):
    return jnp.dot(left, right, preferred_element_type=jnp.float32)


def dot_nt(left, right):
    return lax.dot_general(left, right, (((1,), (1,)), ((), ())), preferred_element_type=jnp.float32)


def dot_tn(left, right):
    return lax.dot_general(left, right, (((0,), (0,)), ((), ())), preferred_element_type=jnp.float32)


def two_parts(values):
    high = values.astype(jnp.bfloat16)
    low = (values - high.astype(jnp.float32)).astype(jnp.bfloat16)
    return (high, low)


def by_core(mine, other, core):
    return jnp.where(core == 0, jnp.stack([mine, other]), jnp.stack([other, mine]))


def remote(src, dst, send, recv, **where):
    return pltpu.make_async_remote_copy(
        src_ref=src, dst_ref=dst, send_sem=send, recv_sem=recv, device_id=where, device_id_type=MESH
    )


def places():
    return lax.axis_index("fsdp"), lax.axis_index("ctx"), lax.axis_index("tp")


def ring(index, step, count):
    return lax.rem(index + step + count, count)


def greet(nz, nc, line, far=False):
    z, c, t = places()
    barrier = pltpu.get_barrier_semaphore()

    def tell(**where):
        pl.semaphore_signal(barrier, inc=1, device_id=where, device_id_type=MESH)

    if line:
        for step in range(1, nz):
            tell(fsdp=ring(z, step, nz))
        count = nz - 1
    else:
        pl.when(z > 0)(lambda: tell(fsdp=z - 1))
        pl.when(z < nz - 1)(lambda: tell(fsdp=z + 1))
        count = jnp.where(z > 0, 1, 0) + jnp.where(z < nz - 1, 1, 0)
    for step in range(1, nc):
        tell(ctx=ring(c, step, nc))
        if far:
            for hop in range(1, nz):
                tell(fsdp=ring(z, hop, nz), ctx=ring(c, step, nc))
    if far:
        count = count + (nz - 1) * (nc - 1)
    tell(tp=1 - t)
    pl.semaphore_wait(barrier, count + nc)


def line_copies(bufs, send_sem, recv_sem, way, step, shard, target):
    return [
        remote(buf.at[shard], buf.at[shard], send_sem.at[way, step, k], recv_sem.at[way, step, k], fsdp=target)
        for k, buf in enumerate(bufs)
    ]


def line_gather(nz, bufs, send_sem, recv_sem, arrived, begun=None, near=None):
    z = lax.axis_index("fsdp")
    for step in range(nz - 1):

        @pl.when((z < nz - 1) & (z >= step))
        def _():
            for copy in line_copies(bufs, send_sem, recv_sem, 0, step, z - step, z + 1):
                copy.start()

        @pl.when((z > 0) & (z + step < nz))
        def _():
            for copy in line_copies(bufs, send_sem, recv_sem, 1, step, z + step, z - 1):
                copy.start()

        if step == 0 and begun is not None:
            begun()
        if near is not None:
            near(step)

        @pl.when(z - 1 >= step)
        def _():
            for copy in line_copies(bufs, send_sem, recv_sem, 0, step, z - 1 - step, z - 1):
                copy.wait_recv()
            arrived(z - 1 - step)

        @pl.when(z + 1 + step < nz)
        def _():
            for copy in line_copies(bufs, send_sem, recv_sem, 1, step, z + 1 + step, z + 1):
                copy.wait_recv()
            arrived(z + 1 + step)


def line_sent(nz, bufs, send_sem, recv_sem):
    z = lax.axis_index("fsdp")
    for step in range(nz - 1):

        @pl.when((z < nz - 1) & (z >= step))
        def _():
            for copy in line_copies(bufs, send_sem, recv_sem, 0, step, z - step, z + 1):
                copy.wait_send()

        @pl.when((z > 0) & (z + step < nz))
        def _():
            for copy in line_copies(bufs, send_sem, recv_sem, 1, step, z + step, z - 1):
                copy.wait_send()


def pick_rows(pick, slot, source, out):
    lanes = out.shape[-1]
    piece = min(lanes, 512)

    @pl.loop(0, lanes // piece)
    def _(k):
        at = pl.ds(pl.multiple_of(k * piece, piece), piece)
        out[slot, :, at] = jnp.dot(pick[slot], source[slot, :, at], preferred_element_type=jnp.float32).astype(
            jnp.bfloat16
        )


def plane_copy(most, src, dst, send, recv, slot, step, source, target):
    rows = pl.ds(pl.multiple_of(target * most, 16), most)
    return remote(
        src.at[slot, rows], dst.at[source, slot], send.at[slot, step - 1], recv.at[slot, step - 1], ctx=target
    )


def regroup(shard, t, rows, line, two, keep_sem, give_send, give_recv):
    slot = lax.rem(shard, 2)
    band = pl.ds(pl.multiple_of(t * rows, rows), rows)

    def keep():
        pltpu.make_async_copy(line.at[shard], two.at[slot, band], keep_sem.at[slot]).start()

    def give():
        remote(line.at[shard], two.at[slot, band], give_send.at[slot], give_recv.at[slot], tp=1 - t).start()

    pl.when(shard // 2 == t)(keep)
    pl.when(shard // 2 != t)(give)


def selector(nz, src, pair, third, held, pair_out, third_out, in_sem, pair_sem, third_sem):
    c = lax.axis_index("ctx")
    tile = 16
    count = src.shape[2]
    height = held.shape[1]
    bands = src.shape[0] // height

    def take(b):
        slot = lax.rem(b, 2)
        return pltpu.make_async_copy(
            src.at[pl.ds(pl.multiple_of(b * height, height), height)], held.at[slot], in_sem.at[slot]
        )

    def put(b):
        slot = lax.rem(b, 2)
        at = pl.ds(pl.multiple_of(b * height, height), height)
        return (
            pltpu.make_async_copy(pair_out.at[slot], pair.at[:, :, at], pair_sem.at[slot]),
            pltpu.make_async_copy(third_out.at[slot], third.at[:, at], third_sem.at[slot]),
        )

    def pick_band(b):
        slot = lax.rem(b, 2)
        take(b).wait()
        pl.when(b + 1 < bands)(lambda: take(b + 1).start())

        @pl.when(b >= 2)
        def _():
            for copy in put(b - 2):
                copy.wait()

        row = lax.broadcasted_iota(jnp.int32, (nz * tile, tile * count), 0)
        column = lax.broadcasted_iota(jnp.int32, (nz * tile, tile * count), 1)
        hit = column == lax.rem(row, tile) * count + c * nz + row // tile
        hit = jnp.where(hit, 1.0, 0.0).astype(jnp.bfloat16)
        for n in range(height // tile):
            at = pl.ds(n * tile, tile)
            for k in range(3):
                value = held[slot, n * tile : (n + 1) * tile, k].reshape(tile * count, -1)
                value = jnp.dot(hit, value, preferred_element_type=jnp.float32).astype(jnp.bfloat16)
                value = value.reshape(nz, tile, -1)
                if k == 1:
                    third_out[slot, :, at, :] = value
                else:
                    pair_out[slot, :, k // 2, at, :] = value
        for copy in put(b):
            copy.start()

    def close():
        for b in (bands - 2, bands - 1):
            for copy in put(b):
                copy.wait()

    pick_band.close = close
    return take, pick_band, bands


def load_kernel(
    nz, nc, tok, cot, wq, wk, wv, wo, small, rank, w_experts,
    x_all, w_qkv, w_o, small_all, rank_line, rank_seq, pick, cot_in, pair, third, middle,
    cot_line, cot_two, cot_send,
    own_sem, line_send, line_recv, w_send, w_recv, tok_send, tok_recv, pass_send, pass_recv,
    rank_send, rank_recv, keep_sem, give_send, give_recv, cot_s, cot_r, cot_own,
    sel_in, sel_pair, sel_third, sel_s, sel_p, sel_t, mid_s, mid_r,
):
    z, c, t = places()
    block = tok.shape[0]
    rows = block // 2
    local = w_qkv.shape[2] // 3
    most = cot_in.shape[2]
    half = pl.ds(pl.multiple_of(t * rows, rows), rows)
    column = pl.ds(pl.multiple_of(c * local, local), local)
    own = [
        pltpu.make_async_copy(cot.at[half], cot_line.at[z], own_sem.at[5]),
        pltpu.make_async_copy(small, small_all.at[z], own_sem.at[4]),
        pltpu.make_async_copy(rank, rank_line.at[z], own_sem.at[7]),
        pltpu.make_async_copy(rank, rank_seq.at[c], own_sem.at[8]),
    ]
    own += [
        pltpu.make_async_copy(w.at[:, column], w_qkv.at[z, :, pl.ds(k * local, local)], own_sem.at[k])
        for k, w in enumerate((wq, wk, wv))
    ]
    own += [
        pltpu.make_async_copy(wo.at[column], w_o.at[z], own_sem.at[3]),
        pltpu.make_async_copy(tok, x_all.at[pl.ds(pl.multiple_of(c * block, block), block)], own_sem.at[6]),
    ]
    for copy in own:
        copy.start()
    take, pick_band, bands = selector(nz, w_experts, pair, third, sel_in, sel_pair, sel_third, sel_s, sel_p, sel_t)
    take(0).start()
    greet(nz, nc, False)

    def band(source, core):
        return x_all.at[pl.ds(pl.multiple_of(source * block + core * rows, rows), rows)]

    def token_copy(step, source, target):
        return remote(tok.at[half], band(source, t), tok_send.at[step], tok_recv.at[step], ctx=target)

    def pass_copy(step, source, core):
        return remote(band(source, core), band(source, core), pass_send.at[step], pass_recv.at[step], tp=1 - t)

    def rank_copy(step, source, target):
        return remote(rank, rank_seq.at[source], rank_send.at[step], rank_recv.at[step], ctx=target)

    for step in range(1, nc):
        token_copy(step - 1, c, ring(c, step, nc)).start()
        rank_copy(step - 1, c, ring(c, step, nc)).start()
    for copy in own:
        copy.wait()

    def arrived(shard):
        regroup(shard, t, rows, cot_line, cot_two, keep_sem, give_send, give_recv)

    arrived(z)
    first = (cot_line, rank_line, small_all)
    line_gather(nz, first, line_send, line_recv, arrived)

    def own_copy(slot):
        return pltpu.make_async_copy(
            cot_send.at[slot, pl.ds(pl.multiple_of(c * most, 16), most)], cot_in.at[c, slot], cot_own.at[slot]
        )

    def send_cotangent():
        number = lax.broadcasted_iota(jnp.int32, (most, block), 0).astype(jnp.float32)
        for slot in range(2):
            for q in range(nc):
                row = rank_line[2 * t + slot, pl.ds(q * nz + z, 1), :]
                hit = jnp.where(number == row, 1.0, 0.0)
                pick[slot, pl.ds(q * most, most), :] = hit.astype(jnp.bfloat16)
        for slot in range(2):
            wait_two(slot, t, rows, cot_line, cot_two, keep_sem, give_recv)
            pick_rows(pick, slot, cot_two, cot_send)
            for step in range(1, nc):
                plane_copy(most, cot_send, cot_in, cot_s, cot_r, slot, step, c, ring(c, step, nc)).start()
            own_copy(slot).start()

    def ignore(shard):
        pass

    partner = nz - 1 - z
    centre = (z == nz // 2 - 1) | (z == nz // 2)
    middle_copy = remote(third.at[partner], middle, mid_s, mid_r, fsdp=partner)

    def select_some(step):
        pl.loop(bands * (0, 1, 3)[step] // 4, bands * (1, 3, 4)[step] // 4)(pick_band)
        if step == 2:
            pick_band.close()
            pl.when(centre)(lambda: middle_copy.start())

    line_gather(nz, (w_qkv, w_o), w_send, w_recv, ignore, send_cotangent, select_some)
    for step in range(1, nc):
        source = ring(c, -step, nc)
        token_copy(step - 1, source, source).wait_recv()
        pass_copy(step - 1, source, t).start()
        rank_copy(step - 1, source, source).wait_recv()
    for step in range(1, nc):
        source = ring(c, -step, nc)
        pass_copy(step - 1, source, 1 - t).wait_recv()
        pass_copy(step - 1, source, t).wait_send()
        token_copy(step - 1, c, source).wait_send()
        rank_copy(step - 1, c, source).wait_send()
        for slot in range(2):
            copy = plane_copy(most, cot_send, cot_in, cot_s, cot_r, slot, step, source, source)
            copy.wait_recv()
            copy.wait_send()
    line_sent(nz, first, line_send, line_recv)
    line_sent(nz, (w_qkv, w_o), w_send, w_recv)
    for slot in range(2):
        own_copy(slot).wait()
        wait_given(slot, t, rows, cot_line, cot_two, give_send, give_recv)

    @pl.when(centre)
    def _():
        middle_copy.wait_recv()
        middle_copy.wait_send()


def wait_given(slot, t, rows, line, two, give_send, give_recv):
    band = pl.ds(pl.multiple_of(t * rows, rows), rows)
    remote(line.at[0], two.at[slot, band], give_send.at[slot], give_recv.at[slot], tp=1 - t).wait_send()


def wait_two(slot, t, rows, line, two, keep_sem, give_recv):
    band = pl.ds(pl.multiple_of(t * rows, rows), rows)
    other = pl.ds(pl.multiple_of((1 - t) * rows, rows), rows)
    pltpu.make_async_copy(line.at[0], two.at[slot, band], keep_sem.at[slot]).wait()
    remote(line.at[0], two.at[slot, other], give_recv.at[slot], give_recv.at[slot], tp=1 - t).wait_recv()


def load(tok, cot, wq, wk, wv, wo, small, rank, w_experts, most):
    nz, nc = lax.axis_size("fsdp"), lax.axis_size("ctx")
    block, width = tok.shape
    deep, local = wq.shape[0], wq.shape[1] // nc
    rows = block // 2
    count, ffn = w_experts.shape[2:]
    dma = pltpu.SemaphoreType.DMA
    bf16, f32 = jnp.bfloat16, jnp.float32
    shapes = [
        ((nc * block, width), bf16),
        ((nz, deep, 3 * local), bf16),
        ((nz, local, wo.shape[1]), bf16),
        ((nz,) + small.shape, bf16),
        ((nz,) + rank.shape, f32),
        ((nc,) + rank.shape, f32),
        ((2, nc * most, block), bf16),
        ((nc, 2, most, width), bf16),
        ((nz, 2, deep, ffn), bf16),
        ((nz, deep, ffn), bf16),
        ((deep, ffn), bf16),
    ]
    hbm = pl.BlockSpec(memory_space=pl.ANY)
    height = 32
    return pl.pallas_call(
        functools.partial(load_kernel, nz, nc),
        out_shape=[jax.ShapeDtypeStruct(shape, kind) for shape, kind in shapes],
        in_specs=[hbm] * 9,
        out_specs=[pl.BlockSpec(memory_space=pltpu.VMEM)] * 7 + [hbm] * 4,
        scratch_shapes=[
            pltpu.VMEM((nz, rows, width), bf16),
            pltpu.VMEM((2, block, width), bf16),
            pltpu.VMEM((2, nc * most, width), bf16),
            dma((9,)),
            dma((2, nz - 1, 3)), dma((2, nz - 1, 3)), dma((2, nz - 1, 2)), dma((2, nz - 1, 2)),
            dma((nc - 1,)), dma((nc - 1,)), dma((nc - 1,)), dma((nc - 1,)), dma((nc - 1,)), dma((nc - 1,)),
            dma((2,)), dma((2,)), dma((2,)), dma((2, nc - 1)), dma((2, nc - 1)), dma((2,)),
            pltpu.VMEM((2, height, 3, count, ffn), bf16),
            pltpu.VMEM((2, nz, 2, height, ffn), bf16),
            pltpu.VMEM((2, nz, height, ffn), bf16),
            dma((2,)), dma((2,)), dma((2,)), dma, dma,
        ],
        compiler_params=pltpu.CompilerParams(
            collective_id=0, has_side_effects=True, vmem_limit_bytes=60 * 2**20
        ),
    )(tok, cot, wq, wk, wv, wo, small, rank, w_experts)


def dispatch_kernel(
    nz, nc, part, tok, gain, router, kept, pick, third, middle,
    residual, normed, probs, x_in, g_in, third_got,
    sib, rs_send, rs_recv, n_line, g_line, n_two, g_two, x_send, g_send,
    sib_s, sib_r, rs_s, rs_r, line_send, line_recv, keep_sem, give_send, give_recv,
    gkeep_sem, ggive_send, ggive_recv, x_s, x_r, g_s, g_r, own_sem,
    third_s, third_r, third_own, mid_own,
):
    z, c, t = places()
    f32, bf16 = jnp.float32, jnp.bfloat16
    rows, width = residual.shape
    most = x_in.shape[2]
    greet(nz, nc, True)
    keep_third = pltpu.make_async_copy(third.at[z], third_got.at[z], third_own)
    keep_third.start()
    partner = nz - 1 - z
    centre = (z == nz // 2 - 1) | (z == nz // 2)
    keep_middle = pltpu.make_async_copy(middle, third_got.at[partner], mid_own)
    pl.when(centre)(lambda: keep_middle.start())

    def still(other):
        return jnp.logical_not(centre & (other == partner))

    def third_copy(step, source, target):
        return remote(third.at[target], third_got.at[source], third_s.at[step], third_r.at[step], fsdp=target)

    def sib_copy(q):
        return remote(part.at[q, 1 - t], sib.at[q], sib_s.at[q], sib_r.at[q], tp=1 - t)

    def rs_copy(step, source, target):
        return remote(rs_send.at[step], rs_recv.at[step], rs_s.at[step], rs_r.at[step], ctx=target)

    for step in range(1, nc + 1):
        sib_copy(ring(c, step, nc)).start()
    chunk = 16
    for step in range(1, nc):
        q = ring(c, step, nc)
        sib_copy(q).wait_recv()

        @pl.loop(0, rows // chunk)
        def _(k):
            at = pl.ds(pl.multiple_of(k * chunk, chunk), chunk)
            rs_send[step - 1, at, :] = (part[q, t, at, :].astype(f32) + sib[q, at, :].astype(f32)).astype(bf16)

        rs_copy(step - 1, c, q).start()

    def own_copy(slot, src, dst, k):
        return pltpu.make_async_copy(
            src.at[slot, pl.ds(pl.multiple_of(c * most, 16), most)], dst.at[c, slot], own_sem.at[k, slot]
        )

    sib_copy(c).wait_recv()
    for step in range(1, nc):
        rs_copy(step - 1, c, c).wait_recv()

    @pl.loop(0, rows // chunk)
    def _(k):
        at = pl.ds(pl.multiple_of(k * chunk, chunk), chunk)
        start = pl.ds(pl.multiple_of(t * rows + k * chunk, chunk), chunk)
        total = part[c, t, at, :].astype(f32) + sib[c, at, :].astype(f32)
        for step in range(nc - 1):
            total = total + rs_recv[step, at, :].astype(f32)
        total = total + tok[start, :].astype(f32)
        residual[at, :] = total
        inv = lax.rsqrt(jnp.mean(total * total, -1, keepdims=True) + EPS)
        row = (total * inv * gain[...]).astype(bf16)
        normed[at, :] = row
        n_line[z, at, :] = row

    logits = lax.dot_general(
        normed[...], router[...], (((1,), (1,)), ((), ())), preferred_element_type=f32
    )
    lane = lax.broadcasted_iota(jnp.int32, logits.shape, 1)
    logits = jnp.where(lane < E, logits, -jnp.inf)
    top = jnp.max(logits, -1, keepdims=True)
    raised = jnp.exp(logits - top)
    prob = raised / jnp.sum(raised, -1, keepdims=True)
    probs[...] = prob
    gates = prob * kept[...]
    high = gates.astype(bf16)
    g_line[z, :, pl.ds(0, 128)] = high
    g_line[z, :, pl.ds(128, 128)] = (gates - high.astype(f32)).astype(bf16)

    def arrived(shard):
        regroup(shard, t, rows, n_line, n_two, keep_sem, give_send, give_recv)
        regroup(shard, t, rows, g_line, g_two, gkeep_sem, ggive_send, ggive_recv)

    arrived(z)
    sent = ((x_send, x_in, x_s, x_r), (g_send, g_in, g_s, g_r))

    def near(distance):
        above, below = z + distance, z - distance
        is_above = (above < nz) & (above // 2 == t)
        is_below = (below >= 0) & (below // 2 == t)
        slot = lax.rem(jnp.where(is_above, above, below + 2), 2)

        @pl.when(is_above | is_below)
        def _():
            wait_two(slot, t, rows, n_line, n_two, keep_sem, give_recv)
            wait_two(slot, t, rows, g_line, g_two, gkeep_sem, ggive_recv)
            pick_rows(pick, slot, n_two, x_send)
            pick_rows(pick, slot, g_two, g_send)
            for k, (src, dst, s, r) in enumerate(sent):
                for step in range(1, nc):
                    plane_copy(most, src, dst, s, r, slot, step, c, ring(c, step, nc)).start()
                own_copy(slot, src, dst, k).start()

    line_gather(nz, (n_line, g_line), line_send, line_recv, arrived, None, near)
    near(nz - 1)
    for step in range(1, nz):
        pl.when(still(ring(z, step, nz)))(lambda: third_copy(step - 1, z, ring(z, step, nz)).start())
    line_sent(nz, (n_line, g_line), line_send, line_recv)
    for slot in range(2):
        wait_given(slot, t, rows, n_line, n_two, give_send, give_recv)
        wait_given(slot, t, rows, g_line, g_two, ggive_send, ggive_recv)
        for k, (src, dst, s, r) in enumerate(sent):
            own_copy(slot, src, dst, k).wait()
            for step in range(1, nc):
                source = ring(c, -step, nc)
                copy = plane_copy(most, src, dst, s, r, slot, step, source, source)
                copy.wait_recv()
                copy.wait_send()
    for step in range(1, nc):
        rs_copy(step - 1, c, c).wait_send()
    for step in range(nc):
        sib_copy(step).wait_send()
    for step in range(1, nz):
        source = ring(z, -step, nz)
        pl.when(still(source))(lambda: third_copy(step - 1, source, source).wait_recv())
        pl.when(still(ring(z, step, nz)))(lambda: third_copy(step - 1, source, source).wait_send())
    keep_third.wait()
    pl.when(centre)(lambda: keep_middle.wait())


def dispatch(part, tok, gain, router, kept, pick, third, middle):
    nz, nc = lax.axis_size("fsdp"), lax.axis_size("ctx")
    rows, width = part.shape[2], part.shape[3]
    block = rows * 2
    most = pick.shape[1] // nc
    dma = pltpu.SemaphoreType.DMA
    bf16, f32 = jnp.bfloat16, jnp.float32
    vmem = pl.BlockSpec(memory_space=pltpu.VMEM)
    hbm = pl.BlockSpec(memory_space=pl.ANY)
    return pl.pallas_call(
        functools.partial(dispatch_kernel, nz, nc),
        out_shape=[
            jax.ShapeDtypeStruct((rows, width), f32),
            jax.ShapeDtypeStruct((rows, width), bf16),
            jax.ShapeDtypeStruct((rows, 128), f32),
            jax.ShapeDtypeStruct((nc, 2, most, width), bf16),
            jax.ShapeDtypeStruct((nc, 2, most, 256), bf16),
            jax.ShapeDtypeStruct(third.shape, bf16),
        ],
        in_specs=[vmem] * 6 + [hbm] * 2,
        out_specs=[vmem] * 3 + [hbm] * 3,
        scratch_shapes=[
            pltpu.VMEM((nc, rows, width), bf16),
            pltpu.VMEM((nc - 1, rows, width), bf16),
            pltpu.VMEM((nc - 1, rows, width), bf16),
            pltpu.VMEM((nz, rows, width), bf16),
            pltpu.VMEM((nz, rows, 256), bf16),
            pltpu.VMEM((2, block, width), bf16),
            pltpu.VMEM((2, block, 256), bf16),
            pltpu.VMEM((2, nc * most, width), bf16),
            pltpu.VMEM((2, nc * most, 256), bf16),
            dma((nc,)), dma((nc,)), dma((nc - 1,)), dma((nc - 1,)),
            dma((2, nz - 1, 2)), dma((2, nz - 1, 2)),
            dma((2,)), dma((2,)), dma((2,)), dma((2,)), dma((2,)), dma((2,)),
            dma((2, nc - 1)), dma((2, nc - 1)), dma((2, nc - 1)), dma((2, nc - 1)),
            dma((2, 2)),
            dma((nz - 1,)), dma((nz - 1,)), dma, dma,
        ],
        compiler_params=pltpu.CompilerParams(
            collective_id=1, has_side_effects=True, vmem_limit_bytes=56 * 2**20
        ),
    )(part, tok, gain, router, kept, pick, third, middle)


def experts_kernel(
    nz, nc, x_hbm, cot_hbm, gates, pair_hbm, third_hbm, y_hbm, r_hbm, pair_out, hid_hbm, gg_hbm, gu_hbm,
    x, cot, w, weight, pair, gate, up, out_grad, y, r, hid, gg, gu,
    sem, swap_s, swap_r, out_sem, inner_sem,
):
    z, c, t = places()
    f32, bf16 = jnp.float32, jnp.bfloat16
    width, tall = x.shape[1], x.shape[0]
    deep, ffn = w.shape[3], w.shape[4]
    span = 256
    chunk = 288
    copies = [
        pltpu.make_async_copy(cot_hbm, cot, sem.at[0]),
        pltpu.make_async_copy(pair_hbm, w.at[0, :, pl.ds(0, 2)], sem.at[1]),
        pltpu.make_async_copy(x_hbm, x, sem.at[2]),
        pltpu.make_async_copy(third_hbm, w.at[0, :, 2], sem.at[3]),
    ]
    for copy in copies:
        copy.start()
    barrier = pltpu.get_barrier_semaphore()
    pl.semaphore_signal(barrier, inc=1, device_id=dict(tp=1 - t), device_id_type=MESH)
    pl.semaphore_wait(barrier, 1)
    swaps = [
        remote(pair_hbm, w.at[1, :, pl.ds(0, 2)], swap_s.at[0], swap_r.at[0], tp=1 - t),
        remote(third_hbm, w.at[1, :, 2], swap_s.at[1], swap_r.at[1], tp=1 - t),
    ]
    for copy in swaps:
        copy.start()
    pair[...] = jnp.zeros_like(pair)
    lane = lax.broadcasted_iota(jnp.int32, (chunk, 256), 1)
    mine = c * nz + z

    @pl.loop(0, tall // chunk)
    def _(m):
        rows = pl.ds(pl.multiple_of(m * chunk, chunk), chunk)
        value = gates[rows, :].astype(f32)
        value = jnp.where((lane == mine) | (lane == mine + 128), value, 0.0)
        weight[rows, :] = jnp.sum(value, 1, keepdims=True)

    for copy in copies[:2]:
        copy.wait()
    per = ffn // span

    def forward(n):
        half, at = n // per, pl.ds(pl.multiple_of(lax.rem(n, per) * span, span), span)
        full = pl.ds(pl.multiple_of(n * span, span), span)

        def times(rows, k):
            return jnp.dot(rows[...], w[half, :, k, :, at].reshape(width, span), preferred_element_type=f32)

        out_grad[...] = times(cot, 1)

        @pl.when(n == 0)
        def _():
            for copy in copies[2:]:
                copy.wait()

        gate[...] = times(x, 0)
        up[...] = times(x, 2)

        @pl.loop(0, tall // chunk)
        def _(m):
            rows = pl.ds(pl.multiple_of(m * chunk, chunk), chunk)
            g, u, o, k = gate[rows, :], up[rows, :], out_grad[rows, :], weight[rows, :]
            sig = 1.0 / (1.0 + jnp.exp(-g))
            silu = g * sig
            hidden = silu * u
            pair[rows, :] += jnp.sum(hidden.astype(bf16).astype(f32) * o, 1, keepdims=True)
            hid[rows, full] = (k * hidden).astype(bf16)
            o = k * o
            gg[rows, full] = (o * u * sig * (1.0 + g * (1.0 - sig))).astype(bf16)
            gu[rows, full] = (o * silu).astype(bf16)

    pl.loop(0, per)(forward)
    for copy in swaps:
        copy.wait_recv()
    pl.loop(per, 2 * per)(forward)

    @pl.loop(0, tall // chunk)
    def _(m):
        rows = pl.ds(pl.multiple_of(m * chunk, chunk), chunk)
        value = pair[rows, :]
        high = value.astype(bf16).astype(f32)
        out = jnp.where(lane == mine, high, jnp.where(lane == mine + 128, value - high, 0.0))
        pair_out[rows, :] = out.astype(bf16)

    inner = [
        pltpu.make_async_copy(src, dst, inner_sem.at[k])
        for k, (src, dst) in enumerate(((hid, hid_hbm), (gg, gg_hbm), (gu, gu_hbm)))
    ]
    for copy in inner:
        copy.start()
    per_deep = deep // span

    def leave(n):
        full = pl.ds(pl.multiple_of(n * span, span), span)
        return (
            pltpu.make_async_copy(y.at[:, full], y_hbm.at[:, full], out_sem.at[0, n]),
            pltpu.make_async_copy(r.at[:, full], r_hbm.at[:, full], out_sem.at[1, n]),
        )

    @pl.loop(0, width // span)
    def _(n):
        zone, at = n // per_deep, pl.ds(pl.multiple_of(lax.rem(n, per_deep) * span, span), span)
        full = pl.ds(pl.multiple_of(n * span, span), span)

        def back(rows, k):
            total = 0.0
            for half in range(2):
                total = total + lax.dot_general(
                    rows[:, pl.ds(half * ffn, ffn)], w[half, zone, k, at, :], (((1,), (1,)), ((), ())),
                    preferred_element_type=f32,
                )
            return total

        y[:, full] = back(hid, 1).astype(bf16)
        r[:, full] = (back(gg, 0) + back(gu, 2)).astype(bf16)
        for copy in leave(n):
            copy.start()

    for n in range(width // span):
        for copy in leave(n):
            copy.wait()
    for copy in inner:
        copy.wait()
    for copy in swaps:
        copy.wait_send()


def experts(x, cot, gates, pair, third):
    bf16, f32 = jnp.bfloat16, jnp.float32
    nz, nc = lax.axis_size("fsdp"), lax.axis_size("ctx")
    tall, width = x.shape
    deep, ffn = third.shape[1:]
    vmem = pl.BlockSpec(memory_space=pltpu.VMEM)
    hbm = pl.BlockSpec(memory_space=pl.ANY)
    inner = jax.ShapeDtypeStruct((tall, 2 * ffn), bf16)
    dma = pltpu.SemaphoreType.DMA
    return pl.pallas_call(
        functools.partial(experts_kernel, nz, nc),
        out_shape=[
            jax.ShapeDtypeStruct((tall, width), bf16),
            jax.ShapeDtypeStruct((tall, width), bf16),
            jax.ShapeDtypeStruct((tall, 256), bf16),
            inner,
            inner,
            inner,
        ],
        in_specs=[hbm, hbm, vmem, hbm, hbm],
        out_specs=[hbm, hbm, vmem, hbm, hbm, hbm],
        scratch_shapes=[
            pltpu.VMEM((tall, width), bf16),
            pltpu.VMEM((tall, width), bf16),
            pltpu.VMEM((2, nz, 3, deep, ffn), bf16),
            pltpu.VMEM((tall, 1), f32),
            pltpu.VMEM((tall, 1), f32),
            pltpu.VMEM((tall, 256), f32),
            pltpu.VMEM((tall, 256), f32),
            pltpu.VMEM((tall, 256), f32),
            pltpu.VMEM((tall, width), bf16),
            pltpu.VMEM((tall, width), bf16),
            pltpu.VMEM((tall, 2 * ffn), bf16),
            pltpu.VMEM((tall, 2 * ffn), bf16),
            pltpu.VMEM((tall, 2 * ffn), bf16),
            dma((4,)), dma((2,)), dma((2,)), dma((2, width // 256)), dma((3,)),
        ],
        compiler_params=pltpu.CompilerParams(
            collective_id=4, has_side_effects=True, vmem_limit_bytes=60 * 2**20
        ),
    )(x, cot, gates, pair, third)


def place_kernel(nz, nc, gate, rest, out):
    tile = rest.shape[1]
    count = nz * nc
    row = lax.broadcasted_iota(jnp.int32, (tile * count, tile * count), 0)
    column = lax.broadcasted_iota(jnp.int32, (tile * count, tile * count), 1)
    expert = lax.rem(row, count)
    hit = column == (lax.rem(expert, nz) * nc + expert // nz) * tile + row // count
    hit = jnp.where(hit, 1.0, 0.0).astype(jnp.bfloat16)
    for k in range(3):
        value = (gate[k] if k < 2 else rest[...]).reshape(count * tile, -1)
        value = jnp.dot(hit, value, preferred_element_type=jnp.float32)
        out[:, k] = value.reshape(tile, count, -1)


def lay_out(gate, rest, nz, nc):
    count, strip, ffn = rest.shape
    tile = 16
    return pl.pallas_call(
        functools.partial(place_kernel, nz, nc),
        grid=(strip // tile,),
        out_shape=jax.ShapeDtypeStruct((strip, 3, count, ffn), jnp.float32),
        in_specs=[
            pl.BlockSpec((2, count, tile, ffn), lambda i: (0, 0, i, 0)),
            pl.BlockSpec((count, tile, ffn), lambda i: (0, i, 0)),
        ],
        out_specs=pl.BlockSpec((tile, 3, count, ffn), lambda i: (i, 0, 0, 0)),
        compiler_params=pltpu.CompilerParams(vmem_limit_bytes=40 * 2**20),
    )(gate, rest)


def collector(nz, nc, pick_t, items, sems):
    z, c, t = places()
    to_s, to_r, own_sem, sib_s, sib_r, line_s, line_r, keep_sem = sems
    rows = items[0][2].shape[1]
    mine_at = pl.ds(pl.multiple_of(t * rows, rows), rows)
    give_at = pl.ds(pl.multiple_of((1 - t) * rows, rows), rows)
    count = len(items)

    def lanes(turn, k):
        wide = items[k][2].shape[-1] // 2
        return pl.ds(turn * wide, wide)

    def to_copy(turn, k, step, source, target):
        src, got = items[k][:2]
        at = lanes(turn, k)
        return remote(
            src.at[target, :, :, at], got.at[source, :, :, at], to_s.at[k, turn, step - 1], to_r.at[k, turn, step - 1],
            ctx=target,
        )

    def own_copy(turn, k):
        src, got = items[k][:2]
        at = lanes(turn, k)
        return pltpu.make_async_copy(src.at[c, :, :, at], got.at[c, :, :, at], own_sem.at[k, turn])

    def sib_copy(turn, k):
        give, sib = items[k][3:5]
        at = lanes(turn, k)
        return remote(give.at[:, :, at], sib.at[:, :, at], sib_s.at[k, turn], sib_r.at[k, turn], tp=1 - t)

    def line_copy(turn, slot, k, half, source, target):
        src = items[k][2 if half == 0 else 4]
        at = lanes(turn, k)
        return remote(
            src.at[slot, :, at], items[k][5].at[source, :, at],
            line_s.at[k, turn, 2 * half + slot], line_r.at[k, turn, source], fsdp=target,
        )

    def keep_copy(turn, slot, k, half):
        src = items[k][2 if half == 0 else 4]
        at = lanes(turn, k)
        return pltpu.make_async_copy(src.at[slot, :, at], items[k][5].at[z, :, at], keep_sem.at[k, turn])

    def goal(slot, half):
        return 2 * (t if half == 0 else 1 - t) + slot

    def forward(turn, k, half):
        for slot in range(2):
            target = goal(slot, half)
            pl.when(target != z)(lambda: line_copy(turn, slot, k, half, z, target).start())
            pl.when(target == z)(lambda: keep_copy(turn, slot, k, half).start())

    def begin(turn):
        for k in range(count):
            for step in range(1, nc):
                to_copy(turn, k, step, c, ring(c, step, nc)).start()
            own_copy(turn, k).start()

    def scatter(turn, slot, k):
        got, mine, give = items[k][1:4]
        wide = mine.shape[-1] // 2
        span = min(wide, 512)
        tall = got.shape[0] * got.shape[2]

        @pl.loop(0, wide // span)
        def _(n):
            at = pl.ds(pl.multiple_of(turn * wide + n * span, span), span)
            pairs = got[:, slot, :, at].reshape(tall, span)
            for picks, out in ((mine_at, mine), (give_at, give)):
                out[slot, :, at] = jnp.dot(
                    pick_t[slot, picks, :], pairs, preferred_element_type=jnp.float32
                ).astype(jnp.bfloat16)

    def process(turn):
        for k in range(count):
            own_copy(turn, k).wait()
            for step in range(1, nc):
                source = ring(c, -step, nc)
                to_copy(turn, k, step, source, c).wait_recv()
            for slot in range(2):
                scatter(turn, slot, k)
            sib_copy(turn, k).start()
            forward(turn, k, 0)
        for k in range(count):
            sib_copy(turn, k).wait_recv()
            forward(turn, k, 1)

    def join():
        for turn in range(2):
            for k in range(count):
                keep_copy(turn, 0, k, 0).wait()
                for step in range(1, nz):
                    line_copy(turn, 0, k, 0, ring(z, -step, nz), z).wait_recv()

    def done():
        for turn in range(2):
            for k in range(count):
                for step in range(1, nc):
                    to_copy(turn, k, step, c, ring(c, step, nc)).wait_send()
                sib_copy(turn, k).wait_send()
                for half in range(2):
                    for slot in range(2):
                        pl.when(goal(slot, half) != z)(
                            lambda: line_copy(turn, slot, k, half, z, goal(slot, half)).wait_send()
                        )

    return begin, process, join, done


def collector_scratch(nz, nc, most, rows, widths):
    dma = pltpu.SemaphoreType.DMA
    bf16 = jnp.bfloat16
    count = len(widths)
    bufs = []
    for w in widths:
        bufs += [pltpu.VMEM((nc, 2, most, w), bf16)]
        bufs += [pltpu.VMEM((2, rows, w), bf16)] * 3
        bufs += [pltpu.VMEM((nz, rows, w), bf16)]
    sems = [
        dma((count, 2, nc - 1)), dma((count, 2, nc - 1)), dma((count, 2)), dma((count, 2)), dma((count, 2)),
        dma((count, 2, 4)), dma((count, 2, nz)), dma((count, 2)),
    ]
    return bufs, sems


def return_kernel(
    nz, nc, r, g, x_hbm, cot_hbm, hid_hbm, gg_hbm, gu_hbm, pick_t, residual, probs, kept, router, gain, cot,
    logits_grad, gain_grad, residual_grad, attn_grad, early_got, rest,
    x, cot_rows, hid, gg, gu, stage, early, early_sib,
    load_sem, keep_sem, give_sem, got_sem, *scratch,
):
    z, c, t = places()
    f32, bf16 = jnp.float32, jnp.bfloat16
    rows, width = residual.shape
    r_line, g_line = scratch[4], scratch[9]
    row_s, row_r, pass_s, pass_r, early_s, early_r, early_own = scratch[18:]
    items = ((r,) + scratch[:5], (g,) + scratch[5:10])
    begin, process, join, done = collector(nz, nc, pick_t, items, scratch[10:18])
    here = z * nc + c
    def keep_early(kind):
        return pltpu.make_async_copy(early.at[kind, here], early_got.at[kind, here], early_own.at[kind])

    loads = [
        pltpu.make_async_copy(src, dst, load_sem.at[k])
        for k, (src, dst) in enumerate(
            ((x_hbm, x), (gg_hbm, gg), (gu_hbm, gu), (cot_hbm, cot_rows), (hid_hbm, hid))
        )
    ]
    for copy in loads:
        copy.start()
    greet(nz, nc, True, True)
    chips = nz * nc
    steps = [(i, j) for i in range(nz) for j in range(nc) if i or j]

    def early_copy(kind, n, source, target, fsdp, ctx):
        return remote(
            early.at[kind, target], early_got.at[kind, source], early_s.at[kind, n], early_r.at[kind, n],
            fsdp=fsdp, ctx=ctx,
        )

    def send_early(kind):
        keep_early(kind).start()
        for n, (i, j) in enumerate(steps):
            zz, cc = ring(z, i, nz), ring(c, j, nc)
            early_copy(kind, n, here, zz * nc + cc, zz, cc).start()

    begin(0)
    begin(1)

    span = 256
    strip, ffn = stage.shape[2], stage.shape[3]
    per = span // strip
    bands = width // span

    def gradients(kind, rows_in, grads):
        def flush(n):
            slot = lax.rem(n, 2)
            at = pl.ds(pl.multiple_of(n * per, per), per)
            return remote(stage.at[slot], early_sib.at[kind, at], give_sem.at[slot], got_sem.at[kind], tp=1 - t)

        @pl.loop(0, bands)
        def _(n):
            full = pl.ds(pl.multiple_of(n * span, span), span)
            slot = lax.rem(n, 2)
            pl.when(n >= 2)(lambda: flush(n - 2).wait_send())
            value = lax.dot_general(
                rows_in[:, full], grads[...], (((0,), (0,)), ((), ())), preferred_element_type=f32
            ).astype(bf16)
            for i in range(per):
                piece = value[i * strip : (i + 1) * strip]
                early[kind, n * per + i] = piece[:, :ffn]
                stage[slot, i] = piece[:, ffn:]
            flush(n).start()

        flush(bands - 2).wait_send()
        flush(bands - 1).wait_send()
        remote(early_sib.at[kind], early_sib.at[kind], got_sem.at[kind], got_sem.at[kind], tp=1 - t).wait_recv()

        @pl.loop(0, chips)
        def _(n):
            early[kind, n] = (early[kind, n].astype(f32) + early_sib[kind, n].astype(f32)).astype(bf16)

    loads[0].wait()
    loads[1].wait()
    gradients(0, x, gg)
    send_early(0)
    for copy in loads[2:]:
        copy.wait()
    gradients(1, x, gu)
    gradients(2, cot_rows, hid)
    keep_rest = pltpu.make_async_copy(early.at[2], rest, keep_sem)
    keep_rest.start()
    for turn in range(2):
        process(turn)
    join()
    pairs = jnp.zeros((rows, 128), f32)
    for source in range(nz):
        pairs = pairs + g_line[source, :, 0:128].astype(f32) + g_line[source, :, 128:256].astype(f32)
    pairs = pairs * kept[...]
    prob = probs[...]
    grad_logits = (prob * (pairs - jnp.sum(prob * pairs, -1, keepdims=True))).astype(bf16)
    logits_grad[...] = grad_logits
    gain_grad[...] = jnp.zeros_like(gain_grad)
    chunk = 16

    @pl.loop(0, rows // chunk)
    def _(k):
        at = pl.ds(pl.multiple_of(k * chunk, chunk), chunk)
        full = pl.ds(pl.multiple_of(t * rows + k * chunk, chunk), chunk)
        res = residual[at, :]
        grad = r_line[0, at, :].astype(f32)
        for source in range(1, nz):
            grad = grad + r_line[source, at, :].astype(f32)
        grad = grad + jnp.dot(logits_grad[at, :], router[...], preferred_element_type=f32)
        inv = lax.rsqrt(jnp.mean(res * res, -1, keepdims=True) + EPS)
        gain_grad[...] += jnp.sum((grad * res * inv).reshape(chunk // 8, 8, width), 0)
        weighted = grad * gain[...]
        inner = jnp.sum(weighted * res, -1, keepdims=True)
        out = cot[full, :].astype(f32) + inv * weighted - res * (inv * inv * inv) * inner / width
        residual_grad[at, :] = out
        attn_grad[c, t, at, :] = out.astype(bf16)

    def row_copy(step, source, target):
        return remote(attn_grad.at[source, t], attn_grad.at[source, t], row_s.at[step], row_r.at[step], ctx=target)

    def pass_copy(step, source, core):
        return remote(attn_grad.at[source, core], attn_grad.at[source, core], pass_s.at[step], pass_r.at[step], tp=1 - t)

    for step in range(1, nc):
        row_copy(step, c, ring(c, step, nc)).start()
    pass_copy(0, c, t).start()
    send_early(1)
    for step in range(1, nc):
        source = ring(c, -step, nc)
        row_copy(step, source, source).wait_recv()
        pass_copy(step, source, t).start()
    for step in range(nc):
        source = ring(c, -step, nc)
        pass_copy(step, source, 1 - t).wait_recv()
        pass_copy(step, source, t).wait_send()
        if step:
            row_copy(step, c, source).wait_send()
    done()
    for kind in range(2):
        for n, (i, j) in enumerate(steps):
            zz, cc = ring(z, -i, nz), ring(c, -j, nc)
            copy = early_copy(kind, n, zz * nc + cc, zz * nc + cc, zz, cc)
            copy.wait_recv()
            copy.wait_send()
        keep_early(kind).wait()
    keep_rest.wait()


def give_back(r, g, x, cot_rows, hid, gg, gu, pick_t, residual, probs, kept, router, gain, cot):
    nz, nc = lax.axis_size("fsdp"), lax.axis_size("ctx")
    rows, width = residual.shape
    dma = pltpu.SemaphoreType.DMA
    bf16, f32 = jnp.bfloat16, jnp.float32
    vmem = pl.BlockSpec(memory_space=pltpu.VMEM)
    hbm = pl.BlockSpec(memory_space=pl.ANY)
    bufs, sems = collector_scratch(nz, nc, r.shape[2], rows, (width, 256))
    chips = nz * nc
    strip, ffn = width // chips, hid.shape[1] // 2
    tall = x.shape[0]
    return pl.pallas_call(
        functools.partial(return_kernel, nz, nc),
        out_shape=[
            jax.ShapeDtypeStruct((rows, 128), bf16),
            jax.ShapeDtypeStruct((8, width), f32),
            jax.ShapeDtypeStruct((rows, width), f32),
            jax.ShapeDtypeStruct((nc, 2, rows, width), bf16),
            jax.ShapeDtypeStruct((2, chips, strip, ffn), bf16),
            jax.ShapeDtypeStruct((chips, strip, ffn), bf16),
        ],
        in_specs=[hbm] * 7 + [vmem] * 7,
        out_specs=[vmem] * 4 + [hbm] * 2,
        scratch_shapes=[
            pltpu.VMEM((tall, width), bf16),
            pltpu.VMEM((tall, width), bf16),
            pltpu.VMEM((tall, 2 * ffn), bf16),
            pltpu.VMEM((tall, 2 * ffn), bf16),
            pltpu.VMEM((tall, 2 * ffn), bf16),
            pltpu.VMEM((2, 256 // strip, strip, ffn), bf16),
            pltpu.VMEM((3, chips, strip, ffn), bf16),
            pltpu.VMEM((3, chips, strip, ffn), bf16),
            dma((5,)), dma, dma((2,)), dma((3,)),
        ]
        + bufs
        + sems
        + [dma((nc,)), dma((nc,)), dma((nc,)), dma((nc,))]
        + [dma((2, nz * nc - 1)), dma((2, nz * nc - 1)), dma((2,))],
        compiler_params=pltpu.CompilerParams(
            collective_id=2, has_side_effects=True, vmem_limit_bytes=60 * 2**20
        ),
    )(r, g, x, cot_rows, hid, gg, gu, pick_t, residual, probs, kept, router, gain, cot)


def final_kernel(
    nz, nc, part, tok, gain, residual_grad, dw, dwo, small, y, pick_t, residual,
    tokens_grad, q_out, k_out, v_out, o_out, small_out, layer,
    dw_out, dwo_out, sib, rs_send, rs_recv, tok_grad, gain_acc, dw_up, dw_down, dwo_up, dwo_down, dw_to, dwo_to,
    dw_next, dwo_next, small_line, small_plane, small_sib, small_a, small_b,
    sib_s, sib_r, rs_s, rs_r, line_s, line_r, to_s, to_r, tg_s, tg_r, sm_s, sm_r, sp_s, sp_r, ss_s, ss_r,
    layer_send, lay_s, lay_r, *scratch,
):
    z, c, t = places()
    f32, bf16 = jnp.float32, jnp.bfloat16
    rows, width = residual_grad.shape
    piece = width // 2
    chunk = 16
    y_line = scratch[4]
    begin, process, join, done = collector(nz, nc, pick_t, ((y,) + scratch[:5],), scratch[5:])
    greet(nz, nc, True)

    bufs = ((dw, dw_up, dw_down), (dwo, dwo_up, dwo_down))
    outs = (dw_next, dwo_next)

    def hop(way, step, k, target):
        src = outs[k].at[way, step]
        return remote(src, bufs[k][1 + way].at[step], line_s.at[way, step, k], line_r.at[way, step, k], fsdp=target)

    def add_to(k, way, step, shard, joined):
        own, out = bufs[k][0], outs[k]
        got = bufs[k][1 + way]
        height = own.shape[2]
        tile = 32

        @pl.loop(0, nc * (height // tile))
        def _(n):
            q, at = n // (height // tile), pl.ds(pl.multiple_of(lax.rem(n, height // tile) * tile, tile), tile)
            value = own[shard, q, at, :]
            if joined:
                value = (value.astype(f32) + got[step, q, at, :].astype(f32)).astype(bf16)
            out[way, step, q, at, :] = value

    def line_one(step, way):
        shard = nz - 1 - step if way == 0 else step
        ahead = z + 1 if way == 0 else z - 1
        behind = z - 1 if way == 0 else z + 1
        first = z == 0 if way == 0 else z == nz - 1
        sends = shard > z if way == 0 else shard < z
        gets = (z > 0) & (shard >= z) if way == 0 else (z < nz - 1) & (shard <= z)

        @pl.when(gets)
        def _():
            for k in range(2):
                hop(way, step, k, behind).wait_recv()

        @pl.when(sends & jnp.logical_not(first))
        def _():
            for k in range(2):
                add_to(k, way, step, shard, True)
                hop(way, step, k, ahead).start()

    def line_step(step):
        @pl.when(2 * z < nz)
        def _():
            line_one(step, 0)
            line_one(step, 1)

        @pl.when(2 * z >= nz)
        def _():
            line_one(step, 1)
            line_one(step, 0)

    def line_begin():
        for way in range(2):
            first = z == 0 if way == 0 else z == nz - 1

            @pl.when(first)
            def _():
                for step in range(nz - 1):
                    shard = nz - 1 - step if way == 0 else step
                    for k in range(2):
                        add_to(k, way, step, shard, False)
                        hop(way, step, k, z + 1 if way == 0 else z - 1).start()

    def sib_copy(q):
        return remote(part.at[q, 1 - t], sib.at[q], sib_s.at[q], sib_r.at[q], tp=1 - t)

    def rs_copy(step, target):
        return remote(rs_send.at[step], rs_recv.at[step], rs_s.at[step], rs_r.at[step], ctx=target)

    for step in range(1, nc + 1):
        sib_copy(ring(c, step, nc)).start()
    line_begin()
    for step in range(1, nc):
        q = ring(c, step, nc)
        sib_copy(q).wait_recv()

        @pl.loop(0, rows // chunk)
        def _(k):
            at = pl.ds(pl.multiple_of(k * chunk, chunk), chunk)
            rs_send[step - 1, at, :] = (part[q, t, at, :].astype(f32) + sib[q, at, :].astype(f32)).astype(bf16)

        rs_copy(step - 1, q).start()
    sib_copy(c).wait_recv()
    begin(0)
    line_step(0)
    begin(1)
    for step in range(1, nc):
        rs_copy(step - 1, c).wait_recv()
    gain_acc[...] = jnp.zeros_like(gain_acc)

    @pl.loop(0, rows // chunk)
    def _(k):
        at = pl.ds(pl.multiple_of(k * chunk, chunk), chunk)
        full = pl.ds(pl.multiple_of(t * rows + k * chunk, chunk), chunk)
        grad = part[c, t, at, :].astype(f32) + sib[c, at, :].astype(f32)
        for step in range(nc - 1):
            grad = grad + rs_recv[step, at, :].astype(f32)
        x = tok[full, :].astype(f32)
        inv = lax.rsqrt(jnp.mean(x * x, -1, keepdims=True) + EPS)
        gain_acc[...] += jnp.sum((grad * x * inv).reshape(chunk // 8, 8, width), 0)
        weighted = grad * gain[...]
        inner = jnp.sum(weighted * x, -1, keepdims=True)
        out = residual_grad[at, :] + inv * weighted - x * (inv * inv * inv) * inner / width
        tok_grad[at, :] = out.astype(bf16)
        tokens_grad[full, :] = out.astype(bf16)

    def grad_copy(core):
        return remote(
            tok_grad, tokens_grad.at[pl.ds(pl.multiple_of(core * rows, rows), rows)], tg_s, tg_r, tp=1 - t
        )

    grad_copy(t).start()

    small_a[...] = small[...]
    total = jnp.sum(gain_acc[...], 0, keepdims=True)
    for strip in range(nz * nc):
        small_a[strip // nc, strip % nc, pl.ds(17, 1), :] = total[:, strip * 128 : (strip + 1) * 128]

    def small_copy(step, shard, target):
        return remote(small_a.at[shard], small_line.at[step], sm_s.at[step], sm_r.at[step], fsdp=target)

    def plane_copy(step, shard, target):
        return remote(small_b.at[shard], small_plane.at[step], sp_s.at[step], sp_r.at[step], ctx=target)

    for step in range(1, nz):
        small_copy(step - 1, ring(z, step, nz), ring(z, step, nz)).start()
    line_step(1)
    process(0)
    line_step(2)
    process(1)
    for step in range(1, nz):
        small_copy(step - 1, z, z).wait_recv()
    value = small_a[z]
    for step in range(nz - 1):
        value = value + small_line[step]
    small_b[...] = value
    for step in range(1, nc):
        plane_copy(step - 1, ring(c, step, nc), ring(c, step, nc)).start()

    def close(k, out, to):
        own, up, down = bufs[k]
        height = own.shape[2]
        tile = 32

        @pl.loop(0, nc * (height // tile))
        def _(n):
            q, at = n // (height // tile), pl.ds(pl.multiple_of(lax.rem(n, height // tile) * tile, tile), tile)
            base = own[z, q, at, :].astype(f32)
            above = up[jnp.minimum(nz - 1 - z, nz - 2), q, at, :].astype(f32)
            below = down[jnp.minimum(z, nz - 2), q, at, :].astype(f32)
            base = base + jnp.where(z > 0, above, 0.0) + jnp.where(z < nz - 1, below, 0.0)
            to[q, at, :] = base.astype(bf16)

    close(0, dw_out, dw_to)
    close(1, dwo_out, dwo_to)

    def to_copy(k, step, source, target):
        src, dst = ((dw_to, dw_out), (dwo_to, dwo_out))[k]
        return remote(src.at[target], dst.at[source], to_s.at[k, step], to_r.at[k, step], ctx=target)

    for step in range(1, nc):
        for k in range(2):
            to_copy(k, step - 1, c, ring(c, step, nc)).start()
    def layer_copy(core):
        return remote(
            layer_send.at[:, pl.ds(pl.multiple_of((1 - t) * piece, piece), piece)],
            layer.at[pl.ds(pl.multiple_of(core * rows, rows), rows)],
            lay_s, lay_r, tp=1 - t,
        )

    join()

    @pl.loop(0, rows // chunk)
    def _(k):
        at = pl.ds(pl.multiple_of(k * chunk, chunk), chunk)
        full = pl.ds(pl.multiple_of(t * rows + k * chunk, chunk), chunk)
        total = residual[at, :]
        for source in range(nz):
            total = total + y_line[source, at, :].astype(f32)
        layer_send[at, :] = total.astype(bf16)
        layer[full, :] = layer_send[at, pl.ds(pl.multiple_of(t * piece, piece), piece)]

    layer_copy(t).start()
    dw_out[c, :, :] = dw_to[c, :, :]
    dwo_out[c, :, :] = dwo_to[c, :, :]
    for step in range(1, nc):
        plane_copy(step - 1, c, c).wait_recv()
    value = small_b[c]
    for step in range(nc - 1):
        value = value + small_plane[step]
    small_out[...] = value
    final = remote(small_out, small_sib, ss_s, ss_r, tp=1 - t)
    final.start()
    final.wait()
    small_out[...] = value + small_sib[...]
    for step in range(1, nc):
        source = ring(c, -step, nc)
        for k in range(2):
            src, dst = ((dw_to, dw_out), (dwo_to, dwo_out))[k]
            remote(
                src.at[c], dst.at[source], to_s.at[k, step - 1], to_r.at[k, step - 1], ctx=source
            ).wait_recv()
    local = o_out.shape[0] // nc
    for source in range(nc):
        at = slice(source * local, (source + 1) * local)
        for k, out in enumerate((q_out, k_out, v_out)):
            out[:, at] = dw_out[source, :, k * local : (k + 1) * local].astype(f32)
        o_out[at, :] = dwo_out[source].astype(f32)
    grad_copy(1 - t).wait_recv()
    grad_copy(t).wait_send()
    layer_copy(1 - t).wait_recv()
    layer_copy(t).wait_send()
    done()
    for step in range(1, nc):
        for k in range(2):
            to_copy(k, step - 1, c, ring(c, step, nc)).wait_send()
        plane_copy(step - 1, ring(c, step, nc), ring(c, step, nc)).wait_send()
        rs_copy(step - 1, c).wait_send()
    for step in range(1, nz):
        small_copy(step - 1, ring(z, step, nz), ring(z, step, nz)).wait_send()
    for q in range(nc):
        sib_copy(q).wait_send()
    for step in range(nz - 1):
        for way in range(2):
            shard = nz - 1 - step if way == 0 else step
            ahead = z + 1 if way == 0 else z - 1
            sends = shard > z if way == 0 else shard < z

            @pl.when(sends)
            def _():
                for k in range(2):
                    hop(way, step, k, ahead).wait_send()


def finish(part, tok, gain, residual_grad, dw, dwo, small, y, pick_t, residual):
    nz, nc = lax.axis_size("fsdp"), lax.axis_size("ctx")
    rows, width = residual_grad.shape
    dma = pltpu.SemaphoreType.DMA
    bf16, f32 = jnp.bfloat16, jnp.float32
    vmem = pl.BlockSpec(memory_space=pltpu.VMEM)
    one, two = dw.shape[1:], dwo.shape[1:]
    bufs, sems = collector_scratch(nz, nc, y.shape[2], rows, (width,))
    tiny = small.shape[2:]
    return pl.pallas_call(
        functools.partial(final_kernel, nz, nc),
        out_shape=[
            jax.ShapeDtypeStruct((2 * rows, width), bf16),
            jax.ShapeDtypeStruct((one[1], nc * two[1]), f32),
            jax.ShapeDtypeStruct((one[1], nc * two[1]), f32),
            jax.ShapeDtypeStruct((one[1], nc * two[1]), f32),
            jax.ShapeDtypeStruct((nc * two[1], two[2]), f32),
            jax.ShapeDtypeStruct(tiny, f32),
            jax.ShapeDtypeStruct((2 * rows, width // 2), bf16),
        ],
        in_specs=[vmem] * 7 + [pl.BlockSpec(memory_space=pl.ANY)] + [vmem] * 2,
        out_specs=[vmem] * 7,
        scratch_shapes=[
            pltpu.VMEM(one, bf16),
            pltpu.VMEM(two, bf16),
            pltpu.VMEM((nc, rows, width), bf16),
            pltpu.VMEM((nc - 1, rows, width), bf16),
            pltpu.VMEM((nc - 1, rows, width), bf16),
            pltpu.VMEM((rows, width), bf16),
            pltpu.VMEM((8, width), f32),
            pltpu.VMEM((nz - 1,) + one, bf16),
            pltpu.VMEM((nz - 1,) + one, bf16),
            pltpu.VMEM((nz - 1,) + two, bf16),
            pltpu.VMEM((nz - 1,) + two, bf16),
            pltpu.VMEM(one, bf16),
            pltpu.VMEM(two, bf16),
            pltpu.VMEM((2, nz - 1) + one, bf16),
            pltpu.VMEM((2, nz - 1) + two, bf16),
            pltpu.VMEM((nz - 1,) + small.shape[1:], f32),
            pltpu.VMEM((nc - 1,) + tiny, f32),
            pltpu.VMEM(tiny, f32),
            pltpu.VMEM(small.shape, f32),
            pltpu.VMEM(small.shape[1:], f32),
            dma((nc,)), dma((nc,)), dma((nc - 1,)), dma((nc - 1,)),
            dma((2, nz - 1, 2)), dma((2, nz - 1, 2)),
            dma((2, nc - 1)), dma((2, nc - 1)), dma, dma,
            dma((nz - 1,)), dma((nz - 1,)), dma((nc - 1,)), dma((nc - 1,)), dma, dma,
            pltpu.VMEM((rows, width), bf16), dma, dma,
        ] + bufs + sems,
        compiler_params=pltpu.CompilerParams(
            collective_id=3, has_side_effects=True, vmem_limit_bytes=60 * 2**20
        ),
    )(part, tok, gain, residual_grad, dw, dwo, small, y, pick_t, residual)


def attention_kernel(
    scale, x, gain, w_qkv, tables, gains, w_o,
    normed, proj, queries, keys, values, context, part,
):
    f32, bf16 = jnp.float32, jnp.bfloat16
    tall, local = queries.shape
    width = x.shape[1]
    heads = local // HD
    small, chunk, span = 32, 256, 256

    @pl.loop(0, tall // small)
    def _(n):
        rows = pl.ds(pl.multiple_of(n * small, small), small)
        value = x[rows, :].astype(f32)
        inv = lax.rsqrt(jnp.mean(value * value, -1, keepdims=True) + EPS)
        normed[rows, :] = (value * inv * gain[...]).astype(bf16)

    @pl.loop(0, 3 * local // span)
    def _(n):
        at = pl.ds(pl.multiple_of(n * span, span), span)
        proj[:, at] = jnp.dot(normed[...], w_qkv[:, at], preferred_element_type=f32)

    @pl.loop(0, tall // chunk)
    def _(n):
        rows = pl.ds(pl.multiple_of(n * chunk, chunk), chunk)
        cos, sin = tables[rows, pl.ds(0, HD)], tables[rows, pl.ds(HD, HD)]
        for head in range(heads):
            at = pl.ds(head * HD, HD)
            for kind, out in enumerate((queries, keys)):
                value = proj[rows, pl.ds(kind * local + head * HD, HD)]
                inv = lax.rsqrt(jnp.mean(value * value, -1, keepdims=True) + EPS)
                value = value * inv * gains[pl.ds(kind, 1), :]
                out[rows, at] = (value * cos - pltpu.roll(value, HD // 2, 1) * sin).astype(bf16)
        values[rows, :] = proj[rows, pl.ds(2 * local, local)].astype(bf16)

    @pl.loop(0, tall // chunk)
    def _(n):
        rows = pl.ds(pl.multiple_of(n * chunk, chunk), chunk)
        for head in range(heads):
            at = pl.ds(head * HD, HD)
            scores = lax.dot_general(
                queries[rows, at], keys[:, at], (((1,), (1,)), ((), ())), preferred_element_type=f32
            ) * scale
            raised = jnp.exp(scores - jnp.max(scores, -1, keepdims=True))
            probs = (raised / jnp.sum(raised, -1, keepdims=True)).astype(bf16)
            context[rows, at] = jnp.dot(probs, values[:, at], preferred_element_type=f32).astype(bf16)

    @pl.loop(0, width // span)
    def _(n):
        at = pl.ds(pl.multiple_of(n * span, span), span)
        part[:, at] = jnp.dot(context[...], w_o[:, at], preferred_element_type=f32).astype(bf16)


def attention(x, gain, w_qkv, tables, gains, w_o):
    bf16, f32 = jnp.bfloat16, jnp.float32
    tall, width = x.shape
    local = w_o.shape[0]
    vmem = pl.BlockSpec(memory_space=pltpu.VMEM)
    shapes = [
        ((tall, width), bf16),
        ((tall, 3 * local), f32),
        ((tall, local), bf16),
        ((tall, local), bf16),
        ((tall, local), bf16),
        ((tall, local), bf16),
        ((tall, width), bf16),
    ]
    return pl.pallas_call(
        functools.partial(attention_kernel, 1.0 / math.sqrt(HD)),
        out_shape=[jax.ShapeDtypeStruct(shape, kind) for shape, kind in shapes],
        in_specs=[vmem] * 6,
        out_specs=[vmem] * 7,
        compiler_params=pltpu.CompilerParams(vmem_limit_bytes=56 * 2**20),
    )(x, gain, w_qkv, tables, gains, w_o)


def attention_back_kernel(
    scale, *refs,
):
    sources, refs = refs[:11], refs[11:]
    part, dw, dwo, q_sum, k_sum = refs[:5]
    held, refs = refs[5:16], refs[16:]
    grad_ctx, gq, gk, gv, grads, sem = refs
    grad_attn, w_o, queries, keys, values, proj, tables, gains, context, normed, w_qkv = held
    f32, bf16 = jnp.float32, jnp.bfloat16
    tall, local = queries.shape
    heads = local // HD
    width = grad_attn.shape[1]
    copies = [pltpu.make_async_copy(src, dst, sem.at[k]) for k, (src, dst) in enumerate(zip(sources, held))]
    for copy in copies:
        copy.start()
    for copy in copies[:5]:
        copy.wait()

    def nt(left, right):
        return lax.dot_general(left, right, (((1,), (1,)), ((), ())), preferred_element_type=f32)

    def tn(left, right):
        return lax.dot_general(left, right, (((0,), (0,)), ((), ())), preferred_element_type=f32)

    grad_ctx[...] = nt(grad_attn[...], w_o[...]).astype(bf16)
    gk[...] = jnp.zeros_like(gk)
    gv[...] = jnp.zeros_like(gv)
    q_sum[...] = jnp.zeros_like(q_sum)
    k_sum[...] = jnp.zeros_like(k_sum)
    chunk = 256

    @pl.loop(0, tall // chunk)
    def _(n):
        rows = pl.ds(pl.multiple_of(n * chunk, chunk), chunk)
        for head in range(heads):
            at = pl.ds(head * HD, HD)
            q, k, v, g = queries[rows, at], keys[:, at], values[:, at], grad_ctx[rows, at]
            scores = nt(q, k) * scale
            raised = jnp.exp(scores - jnp.max(scores, -1, keepdims=True))
            probs = raised / jnp.sum(raised, -1, keepdims=True)
            grad_probs = nt(g, v)
            inner = jnp.sum(probs * grad_probs, -1, keepdims=True)
            grad_scores = (probs * (grad_probs - inner)).astype(bf16)
            gq[rows, at] = jnp.dot(grad_scores, k, preferred_element_type=f32) * scale
            gk[:, at] += tn(grad_scores, q)
            gv[:, at] += tn(probs.astype(bf16), g)

    for copy in copies[5:8]:
        copy.wait()

    @pl.loop(0, tall // chunk)
    def _(n):
        rows = pl.ds(pl.multiple_of(n * chunk, chunk), chunk)
        cos, sin = tables[rows, pl.ds(0, HD)], tables[rows, pl.ds(HD, HD)]
        for head in range(heads):
            for kind, total in enumerate((q_sum, k_sum)):
                at = pl.ds(head * HD, HD)
                column = pl.ds(kind * local + head * HD, HD)
                grad = gq[rows, at] if kind == 0 else gk[rows, at] * scale
                grad = grad * cos + pltpu.roll(grad, HD // 2, 1) * sin
                value = proj[rows, column]
                inv = lax.rsqrt(jnp.mean(value * value, -1, keepdims=True) + EPS)
                total[...] += jnp.sum((grad * value * inv).reshape(chunk // 8, 8, HD), 0)
                weighted = grad * gains[pl.ds(kind, 1), :]
                inner = jnp.sum(weighted * value, -1, keepdims=True)
                out = inv * weighted - value * (inv * inv * inv) * inner / HD
                grads[rows, column] = out.astype(bf16)
        grads[rows, pl.ds(2 * local, local)] = gv[rows, :].astype(bf16)

    for copy in copies[8:]:
        copy.wait()
    span = 256
    strip = dwo.shape[2]

    @pl.loop(0, width // span)
    def _(n):
        full = pl.ds(pl.multiple_of(n * span, span), span)
        dw[full, :] = tn(normed[:, full], grads[...]).astype(bf16)
        part[:, full] = nt(grads[...], w_qkv[full, :]).astype(bf16)
        value = tn(context[...], grad_attn[:, full]).astype(bf16)
        for i in range(span // strip):
            dwo[n * (span // strip) + i] = value[:, i * strip : (i + 1) * strip]


def attention_back(grad_attn, w_o, queries, keys, values, proj, tables, gains, context, normed, w_qkv, strip):
    bf16, f32 = jnp.bfloat16, jnp.float32
    tall, width = grad_attn.shape
    local = queries.shape[1]
    vmem = pl.BlockSpec(memory_space=pltpu.VMEM)
    sources = (grad_attn, w_o, queries, keys, values, proj, tables, gains, context, normed, w_qkv)
    return pl.pallas_call(
        functools.partial(attention_back_kernel, 1.0 / math.sqrt(HD)),
        out_shape=[
            jax.ShapeDtypeStruct((tall, width), bf16),
            jax.ShapeDtypeStruct((width, 3 * local), bf16),
            jax.ShapeDtypeStruct((width // strip, local, strip), bf16),
            jax.ShapeDtypeStruct((8, HD), f32),
            jax.ShapeDtypeStruct((8, HD), f32),
        ],
        in_specs=[pl.BlockSpec(memory_space=pl.ANY)] * len(sources),
        out_specs=[vmem] * 5,
        scratch_shapes=[pltpu.VMEM(source.shape, source.dtype) for source in sources]
        + [
            pltpu.VMEM((tall, local), bf16),
            pltpu.VMEM((tall, local), f32),
            pltpu.VMEM((tall, local), f32),
            pltpu.VMEM((tall, local), f32),
            pltpu.VMEM((tall, 3 * local), bf16),
            pltpu.SemaphoreType.DMA((len(sources),)),
        ],
        compiler_params=pltpu.CompilerParams(vmem_limit_bytes=60 * 2**20),
    )(*sources)


def one_chip(
    tokens,
    w_query,
    w_key,
    w_value,
    w_out,
    gain_attn,
    gain_query,
    gain_key,
    gain_moe,
    w_router,
    w_experts,
    routes,
    cotangent,
):
    z, c, t = lax.axis_index("fsdp"), lax.axis_index("ctx"), lax.axis_index("tp")
    nz, nc = lax.axis_size("fsdp"), lax.axis_size("ctx")
    block, width = tokens.shape[1], tokens.shape[2]
    rows = block // 2
    tall = block * nc
    deep = width // nz
    ffn = w_experts.shape[3]
    most = block * TOPK * 9 // (8 * E)
    bf16, f32 = jnp.bfloat16, jnp.float32

    token_half = lax.dynamic_slice_in_dim(tokens[0], t * rows, rows, 0)
    cotan_half = lax.dynamic_slice_in_dim(cotangent[0], t * rows, rows, 0)
    local = w_query.shape[1] // nc
    small = jnp.concatenate([w_router.T.reshape(-1), gain_attn, gain_moe, gain_query, gain_key])
    total = small.shape[0]
    small = jnp.pad(small, (0, -total % 2048))
    small = small.reshape(-1, 128)
    ids = jnp.arange(E, dtype=jnp.int32)
    named = jnp.any(routes[0][:, :, None] == ids, 1)
    below = jnp.tril(jnp.ones((block, block), bf16), -1)
    rank = jnp.where(named, dot(below, named.astype(bf16)), -1.0).T
    x_rows, w_qkv, w_o, small, _, rank_seq, pick, cot_rows, pair, third, middle = load(
        tokens[0], cotangent[0], w_query, w_key, w_value, w_out, small, rank, w_experts, most
    )
    w_qkv = w_qkv.reshape(width, 3 * local)
    w_o = w_o.transpose(1, 0, 2).reshape(local, width)
    small = small.reshape(nz, -1)
    router = small[:, : E * deep].reshape(nz, E, deep).transpose(1, 0, 2).reshape(E, width)
    at = E * deep
    attn_gain = small[:, at : at + deep].reshape(-1).astype(f32)
    moe_gain = small[:, at + deep : at + 2 * deep].reshape(-1).astype(f32)
    at, part = at + 2 * deep, HD // nz
    query_gain = small[:, at : at + part].reshape(-1).astype(f32)
    key_gain = small[:, at + part : at + 2 * part].reshape(-1).astype(f32)

    pair = exchange(pair, "fsdp")

    counts = jnp.sum((rank_seq >= 0).astype(f32), 2)
    earlier = jnp.sum(jnp.where(jnp.arange(nc)[:, None] < c, counts, 0.0), 0)
    kept = ((rank >= 0) & (rank + earlier[:, None] < CAP)).astype(f32).T
    kept = lax.dynamic_slice_in_dim(kept, t * rows, rows, 0)

    half_dim = HD // 2
    inv_freq = jnp.exp(jnp.arange(half_dim, dtype=f32) * (-2.0 * math.log(ROPE_BASE) / HD))
    angles = jnp.arange(tall, dtype=jnp.int32).astype(f32)[:, None] * inv_freq[None, :]
    cosines, sines = jnp.cos(angles), jnp.sin(angles)
    tables = jnp.concatenate([cosines, cosines, sines, -sines], 1)
    gains = jnp.pad(jnp.stack([query_gain, key_gain]), ((0, 6), (0, 0)))
    normed_one, proj, queries, keys, values, context, attn_part = attention(
        x_rows, attn_gain[None], w_qkv, tables, gains, w_o
    )
    attn_part = attn_part.reshape(nc, 2, rows, width)
    kept_wide = jnp.pad(kept, ((0, 0), (0, 128 - E)))
    router_wide = jnp.pad(router, ((0, 128 - E), (0, 0)))
    residual, normed_two, router_probs, x_in, g_in, third = dispatch(
        attn_part, tokens[0], moe_gain[None], router_wide, kept_wide, pick, third, middle
    )
    pair, x_in = lax.optimization_barrier((pair, x_in))
    x_in = x_in.reshape(nc * 2 * most, width)
    cot_rows = cot_rows.reshape(nc * 2 * most, width)
    chips = nz * nc
    strip = width // chips
    out_rows, back_rows, pair_rows, hid, gg, gu = experts(
        x_in, cot_rows, g_in.reshape(nc * 2 * most, -1), pair, third
    )
    shape = (nc, 2, most, -1)
    pick_t = pick.transpose(0, 2, 1)
    grad_logits, dgain_moe, grad_residual, grad_attn, dw_gate, dw_rest = give_back(
        back_rows.reshape(shape),
        pair_rows.reshape(shape),
        x_in,
        cot_rows,
        hid,
        gg,
        gu,
        pick_t,
        residual,
        router_probs,
        kept_wide,
        router_wide,
        moe_gain[None],
        cotangent[0],
    )

    dw_router = dot_tn(normed_two, grad_logits[:, :E])
    dgain_moe = jnp.sum(dgain_moe, 0)
    dw_rest, grad_attn = lax.optimization_barrier((dw_rest, grad_attn))
    dw_rest = exchange(dw_rest, ("fsdp", "ctx"))
    grad_attn = grad_attn.reshape(tall, width)

    grad_normed_part, dw_qkv, dw_out, dgain_query, dgain_key = attention_back(
        grad_attn,
        w_o,
        queries,
        keys,
        values,
        proj,
        tables,
        gains,
        context,
        normed_one,
        w_qkv,
        strip,
    )
    dgain_query, dgain_key = jnp.sum(dgain_query, 0), jnp.sum(dgain_key, 0)
    grad_normed_part = grad_normed_part.reshape(nc, 2, rows, width)
    head_part = HD // chips
    heads = [dgain_query.reshape(chips, 1, head_part), dgain_key.reshape(chips, 1, head_part)]
    heads = jnp.pad(jnp.concatenate(heads, 2), ((0, 0), (0, 0), (0, strip - 2 * head_part)))
    sums = jnp.concatenate(
        [
            dw_router.reshape(chips, E, strip),
            dgain_moe.reshape(chips, 1, strip),
            jnp.zeros((chips, 1, strip), f32),
            heads,
            jnp.zeros((chips, 24 - E - 3, strip), f32),
        ],
        1,
    ).reshape(nz, nc, 24, strip)
    tokens_grad, dw_query, dw_key, dw_value, dw_out, sums, layer_out = finish(
        grad_normed_part,
        tokens[0],
        attn_gain[None],
        grad_residual,
        dw_qkv.reshape(nz, nc, strip, 3 * local),
        dw_out.reshape(nz, nc, local, strip),
        sums,
        out_rows.reshape(shape),
        pick_t,
        residual,
    )
    dw_experts = lay_out(dw_gate, dw_rest, nz, nc)
    return (
        layer_out[None],
        tokens_grad[None],
        dw_query,
        dw_key,
        dw_value,
        dw_out,
        sums[E + 1],
        sums[E + 2, :head_part],
        sums[E + 2, head_part : 2 * head_part],
        sums[E],
        sums[:E].reshape(strip, E),
        dw_experts,
    )


def solution(mesh):
    chips = mesh.shape["fsdp"] * mesh.shape["ctx"]
    plain = chips == E and mesh.shape["fsdp"] == 4 and mesh.shape["tp"] == 2
    return jax.shard_map(
        one_chip if plain else general,
        mesh=mesh,
        in_specs=(
            P("fsdp", "ctx", None),
            P("fsdp", "tp"),
            P("fsdp", "tp"),
            P("fsdp", "tp"),
            P("tp", "fsdp"),
            P("fsdp"),
            P("fsdp"),
            P("fsdp"),
            P("fsdp"),
            P("fsdp", None),
            P("fsdp", None, None, "tp"),
            P("fsdp", "ctx", None),
            P("fsdp", "ctx", None),
        ),
        out_specs=(
            P("fsdp", "ctx", "tp"),
            P("fsdp", "ctx", None),
            P(("fsdp", "ctx"), "tp"),
            P(("fsdp", "ctx"), "tp"),
            P(("fsdp", "ctx"), "tp"),
            P("tp", ("fsdp", "ctx")),
            P(("fsdp", "ctx")),
            P(("fsdp", "ctx")),
            P(("fsdp", "ctx")),
            P(("fsdp", "ctx")),
            P(("fsdp", "ctx"), None),
            P(("fsdp", "ctx"), None, None, "tp"),
        ),
        check_vma=False,
    )
```

```python
import functools
import math

import jax
import jax.numpy as jnp
from jax import lax
from jax.experimental import pallas as pl
from jax.experimental.pallas import tpu as pltpu
from jax.sharding import PartitionSpec as P

HD = 128
TOPK = 8
E = 16
CAP = 512
MESH = pl.DeviceIdType.MESH


EPS = 1e-06
ROPE_BASE = 10000.0


def prefix(value, axis, join, neutral):
    count, mine = (lax.axis_size(axis), lax.axis_index(axis))
    pieces = lax.all_gather(value, axis)
    running = jnp.full_like(value, 0) + jnp.asarray(neutral, value.dtype)

    def lap(position, running):
        longer = join(running, pieces[position])
        return jnp.where(position < mine, longer, running)

    return lax.fori_loop(0, count - 1, lap, running)


def rms_scale(values):
    return lax.rsqrt(jnp.mean(values * values, -1, keepdims=True) + EPS)


def norm_back(grad_normed, values, inv_rms, gain_vec):
    weighted = grad_normed * gain_vec.astype(jnp.float32)
    inner_sum = jnp.sum(weighted * values, -1, keepdims=True)
    return (
        inv_rms * weighted - values * (inv_rms * inv_rms * inv_rms) * inner_sum / values.shape[-1]
    )


def rope_tables(first, length):
    half_dim = HD // 2
    inv_freq = jnp.exp(jnp.arange(half_dim, dtype=jnp.float32) * (-2.0 * math.log(ROPE_BASE) / HD))
    places = (first + jnp.arange(length, dtype=jnp.int32)).astype(jnp.float32)
    angles = places[:, None] * inv_freq[None, :]
    cos_table = jnp.cos(angles)
    sin_table = jnp.sin(angles)
    cos_full = jnp.concatenate([cos_table, cos_table], -1)[:, None, :]
    sin_full = jnp.concatenate([sin_table, sin_table], -1)[:, None, :]
    return (cos_full, sin_full)


def rotate(values):
    half_dim = values.shape[-1] // 2
    return jnp.concatenate([-values[..., half_dim:], values[..., :half_dim]], -1)


def rotate_back(values):
    half_dim = values.shape[-1] // 2
    return jnp.concatenate([values[..., half_dim:], -values[..., :half_dim]], -1)


def apply_rope(values, cos_full, sin_full):
    return values * cos_full + rotate(values) * sin_full


def rope_back(grads, cos_full, sin_full):
    return grads * cos_full + rotate_back(grads * sin_full)


def add_counts(earlier, later):
    return earlier + later


def general(
    tokens,
    w_query,
    w_key,
    w_value,
    w_out,
    gain_attn,
    gain_query,
    gain_key,
    gain_moe,
    w_router,
    w_experts,
    routes,
    cotangent,
):
    seq_count, block_len, model_width = tokens.shape
    row_count = seq_count * block_len
    (
        full_query,
        full_key,
        full_value,
        full_out,
        router_full,
        attn_gain,
        query_gain,
        key_gain,
        moe_gain,
    ) = (
        lax.all_gather(w_query, "fsdp", axis=0, tiled=True),
        lax.all_gather(w_key, "fsdp", axis=0, tiled=True),
        lax.all_gather(w_value, "fsdp", axis=0, tiled=True),
        lax.all_gather(w_out, "fsdp", axis=1, tiled=True),
        lax.all_gather(w_router, "fsdp", axis=0, tiled=True),
        lax.all_gather(gain_attn, "fsdp", axis=0, tiled=True),
        lax.all_gather(gain_query, "fsdp", axis=0, tiled=True),
        lax.all_gather(gain_key, "fsdp", axis=0, tiled=True),
        lax.all_gather(gain_moe, "fsdp", axis=0, tiled=True),
    )
    local_width = full_query.shape[1]
    head_count = local_width // HD
    head_shape = (seq_count, block_len, head_count, HD)
    token_rows = tokens.reshape(row_count, model_width).astype(jnp.float32)
    inv_one = rms_scale(token_rows)
    normed_one = (token_rows * inv_one * attn_gain.astype(jnp.float32)).astype(jnp.bfloat16)
    query_proj = jnp.dot(normed_one, full_query, preferred_element_type=jnp.float32)
    key_proj = jnp.dot(normed_one, full_key, preferred_element_type=jnp.float32)
    value_proj = jnp.dot(normed_one, full_value, preferred_element_type=jnp.float32)
    cos_full, sin_full = rope_tables(lax.axis_index("ctx") * block_len, block_len)
    query_heads = query_proj.reshape(head_shape)
    key_heads = key_proj.reshape(head_shape)
    query_inv = rms_scale(query_heads)
    key_inv = rms_scale(key_heads)
    queries = apply_rope(
        query_heads * query_inv * query_gain.astype(jnp.float32), cos_full, sin_full
    ).astype(jnp.bfloat16)
    keys_local = apply_rope(
        key_heads * key_inv * key_gain.astype(jnp.float32), cos_full, sin_full
    ).astype(jnp.bfloat16)
    keys_local = keys_local.reshape(seq_count, block_len, local_width)
    values_local = value_proj.astype(jnp.bfloat16).reshape(seq_count, block_len, local_width)
    keys_all, values_all = (
        lax.all_gather(keys_local, "ctx", axis=1, tiled=True),
        lax.all_gather(values_local, "ctx", axis=1, tiled=True),
    )
    seq_len = keys_all.shape[1]
    key_rows = keys_all.reshape(seq_count, seq_len, head_count, HD)
    value_rows = values_all.reshape(seq_count, seq_len, head_count, HD)
    score_scale = 1.0 / math.sqrt(HD)
    scores = (
        jnp.einsum("sqhd,skhd->shqk", queries, key_rows, preferred_element_type=jnp.float32)
        * score_scale
    )
    maximum = jnp.max(scores, -1, keepdims=True)
    exp_scores = jnp.exp(scores - maximum)
    denominator = jnp.sum(exp_scores, -1, keepdims=True)
    attn_probs = exp_scores / denominator
    log_total = maximum + jnp.log(denominator)
    context = jnp.einsum(
        "shqk,skhd->sqhd",
        attn_probs.astype(jnp.bfloat16),
        value_rows,
        preferred_element_type=jnp.float32,
    )
    context = context.astype(jnp.bfloat16).reshape(row_count, local_width)
    attn_part = jnp.dot(context, full_out, preferred_element_type=jnp.float32)
    residual = token_rows + lax.psum(attn_part, "tp")
    inv_two = rms_scale(residual)
    normed_two = (residual * inv_two * moe_gain.astype(jnp.float32)).astype(jnp.bfloat16)
    logits = jnp.dot(normed_two, router_full, preferred_element_type=jnp.float32)
    router_probs = jax.nn.softmax(logits, -1)
    pair_count = block_len * TOPK
    route_rows = routes.reshape(seq_count, pair_count)
    expert_ids = jnp.arange(E, dtype=jnp.int32)
    onehot = (route_rows[:, :, None] == expert_ids[None, None, :]).astype(jnp.int32)
    counts = jnp.sum(onehot, 1, dtype=jnp.int32)
    offsets = prefix(counts, "ctx", add_counts, jnp.zeros_like(counts))
    earlier = jnp.cumsum(onehot, 1, dtype=jnp.int32) - onehot
    local_rank = jnp.sum(earlier * onehot, 2, dtype=jnp.int32)
    slot_base = jnp.sum(onehot * offsets[:, None, :], 2, dtype=jnp.int32)
    kept_mask = (slot_base + local_rank < CAP).astype(jnp.float32).reshape(row_count, TOPK)
    block_most = pair_count * 9 // (8 * E)
    expert_span = seq_count * block_most
    seq_ids = jnp.arange(seq_count, dtype=jnp.int32)[:, None]
    buffer_row = (route_rows * expert_span + seq_ids * block_most + local_rank).reshape(
        row_count * TOPK
    )
    token_ids = (
        seq_ids * block_len + jnp.arange(pair_count, dtype=jnp.int32)[None, :] // TOPK
    ).reshape(row_count * TOPK)
    owner_rows = jnp.zeros((E * expert_span,), jnp.int32).at[buffer_row].set(token_ids)
    onehot_f = onehot.astype(jnp.float32).reshape(row_count, TOPK, E)
    gate_weight = jnp.sum(onehot_f * router_probs[:, None, :], 2) * kept_mask
    slot_weight = (
        jnp.zeros((E * expert_span,), jnp.float32)
        .at[buffer_row]
        .set(gate_weight.reshape(row_count * TOPK))
    )
    expert_rows = normed_two[owner_rows].reshape(E, expert_span, model_width)
    cotan_rows = cotangent.reshape(row_count, model_width)
    grad_expert = (slot_weight[:, None] * cotan_rows[owner_rows].astype(jnp.float32)).astype(
        jnp.bfloat16
    )
    grad_expert = grad_expert.reshape(E, expert_span, model_width)
    ffn_local = w_experts.shape[3]
    fsdp_count = lax.axis_size("fsdp")
    ctx_count = lax.axis_size("ctx")
    group_count = fsdp_count * ctx_count
    sharing = group_count // E
    padded_span = -(-expert_span // sharing) * sharing
    part_span = padded_span // sharing
    target_experts = (
        jnp.arange(fsdp_count, dtype=jnp.int32) * ctx_count + lax.axis_index("ctx")
    ) // sharing
    selected = jnp.take(w_experts, target_experts, axis=2)
    owned = lax.all_to_all(selected, "fsdp", split_axis=2, concat_axis=0, tiled=True)[:, :, 0]
    send_rows = expert_rows.reshape(group_count, part_span, model_width)
    send_grads = grad_expert.reshape(group_count, part_span, model_width)
    recv_rows, recv_grads = (
        lax.all_to_all(send_rows, ("fsdp", "ctx"), split_axis=0, concat_axis=0, tiled=True),
        lax.all_to_all(send_grads, ("fsdp", "ctx"), split_axis=0, concat_axis=0, tiled=True),
    )
    rows_flat = recv_rows.reshape(group_count * part_span, model_width)
    grads_flat = recv_grads.reshape(group_count * part_span, model_width)
    gate_act = jnp.dot(rows_flat, owned[:, 0], preferred_element_type=jnp.float32)
    up_act = jnp.dot(rows_flat, owned[:, 1], preferred_element_type=jnp.float32)
    sigmoid_gate = jax.nn.sigmoid(gate_act)
    silu_gate = gate_act * sigmoid_gate
    hidden = (silu_gate * up_act).astype(jnp.bfloat16)
    produced = jnp.einsum("mf,df->md", hidden, owned[:, 2], preferred_element_type=jnp.float32)
    grad_hidden = jnp.dot(grads_flat, owned[:, 2], preferred_element_type=jnp.float32)
    grad_gate = (
        grad_hidden * up_act * sigmoid_gate * (1.0 + gate_act * (1.0 - sigmoid_gate))
    ).astype(jnp.bfloat16)
    grad_up = (grad_hidden * silu_gate).astype(jnp.bfloat16)
    rows_grad = jnp.einsum("mf,df->md", grad_gate, owned[:, 0], preferred_element_type=jnp.float32)
    rows_grad = rows_grad + jnp.einsum(
        "mf,df->md", grad_up, owned[:, 1], preferred_element_type=jnp.float32
    )
    back_out, back_rows = (
        lax.all_to_all(
            produced.reshape(group_count, part_span, model_width).astype(jnp.bfloat16),
            ("fsdp", "ctx"),
            split_axis=0,
            concat_axis=0,
            tiled=True,
        ).astype(jnp.float32),
        lax.all_to_all(
            rows_grad.reshape(group_count, part_span, model_width).astype(jnp.bfloat16),
            ("fsdp", "ctx"),
            split_axis=0,
            concat_axis=0,
            tiled=True,
        ).astype(jnp.float32),
    )
    expert_out = back_out.reshape(E, padded_span, model_width)
    grad_rows = back_rows.reshape(E, padded_span, model_width)
    gate_term = jnp.einsum("md,mf->df", rows_flat, grad_gate, preferred_element_type=jnp.float32)
    up_term = jnp.einsum("md,mf->df", rows_flat, grad_up, preferred_element_type=jnp.float32)
    down_term = jnp.einsum("md,mf->df", grads_flat, hidden, preferred_element_type=jnp.float32)
    owner_terms = jnp.stack([gate_term, up_term, down_term], 1)[:, :, None, :]
    relaid = lax.all_to_all(
        owner_terms.astype(jnp.bfloat16), ("fsdp", "ctx"), split_axis=0, concat_axis=2, tiled=True
    ).astype(owner_terms.dtype)
    dw_experts = jnp.sum(relaid.reshape(relaid.shape[0], 3, E, sharing, ffn_local), 3)
    picked = expert_out.reshape(E * expert_span, model_width)[buffer_row].reshape(
        row_count, TOPK, model_width
    )
    moe_part = jnp.sum(gate_weight[:, :, None] * picked, 1)
    cotan_float = cotan_rows.astype(jnp.float32)
    grad_gate_part = jnp.sum(picked * cotan_float[:, None, :], 2)
    moe_shard = lax.psum_scatter(
        moe_part.astype(jnp.bfloat16), "tp", scatter_dimension=1, tiled=True
    ).astype(jnp.float32)
    piece_width = moe_shard.shape[1]
    residual_shard = lax.dynamic_slice_in_dim(
        residual, lax.axis_index("tp") * piece_width, piece_width, 1
    )
    layer_out = (
        (residual_shard + moe_shard).astype(jnp.bfloat16).reshape(seq_count, block_len, piece_width)
    )
    grad_normed_part = jnp.sum(
        grad_rows.reshape(E * expert_span, model_width)[buffer_row].reshape(
            row_count, TOPK, model_width
        ),
        1,
    )
    grad_normed_sum, grad_gate_sum = (
        lax.psum(grad_normed_part.astype(jnp.bfloat16), "tp").astype(jnp.float32),
        lax.psum(grad_gate_part.astype(jnp.bfloat16), "tp").astype(jnp.float32),
    )
    grad_pick = grad_gate_sum * kept_mask
    grad_router_probs = jnp.sum(onehot_f * grad_pick[:, :, None], 1)
    grad_logits = router_probs * (
        grad_router_probs - jnp.sum(router_probs * grad_router_probs, -1, keepdims=True)
    )
    grad_logits = grad_logits.astype(jnp.bfloat16)
    grad_router_w = jnp.einsum(
        "nd,ne->de", normed_two, grad_logits, preferred_element_type=jnp.float32
    )
    grad_normed_two = grad_normed_sum + jnp.einsum(
        "ne,de->nd", grad_logits, router_full, preferred_element_type=jnp.float32
    )
    grad_moe_gain = jnp.sum(grad_normed_two * residual * inv_two, 0)
    grad_residual = cotan_float + norm_back(grad_normed_two, residual, inv_two, moe_gain)
    grad_attn = grad_residual.astype(jnp.bfloat16)
    grad_w_out = jnp.einsum("nl,nd->ld", context, grad_attn, preferred_element_type=jnp.float32)
    grad_context = jnp.einsum("nd,ld->nl", grad_attn, full_out, preferred_element_type=jnp.float32)
    grad_context = grad_context.astype(jnp.bfloat16).reshape(head_shape)
    scores = (
        jnp.einsum("sqhd,skhd->shqk", queries, key_rows, preferred_element_type=jnp.float32)
        * score_scale
    )
    attn_probs = jnp.exp(scores - log_total)
    grad_probs = jnp.einsum(
        "sqhd,skhd->shqk", grad_context, value_rows, preferred_element_type=jnp.float32
    )
    grad_scores = attn_probs * (grad_probs - jnp.sum(attn_probs * grad_probs, -1, keepdims=True))
    grad_scores = grad_scores.astype(jnp.bfloat16)
    grad_queries = (
        jnp.einsum("shqk,skhd->sqhd", grad_scores, key_rows, preferred_element_type=jnp.float32)
        * score_scale
    )
    grad_keys_all = (
        jnp.einsum("shqk,sqhd->skhd", grad_scores, queries, preferred_element_type=jnp.float32)
        * score_scale
    )
    grad_values_all = jnp.einsum(
        "shqk,sqhd->skhd",
        attn_probs.astype(jnp.bfloat16),
        grad_context,
        preferred_element_type=jnp.float32,
    )
    grad_keys_own, grad_values_own = (
        lax.psum_scatter(
            grad_keys_all.reshape(seq_count, seq_len, local_width).astype(jnp.bfloat16),
            "ctx",
            scatter_dimension=1,
            tiled=True,
        ).astype(jnp.float32),
        lax.psum_scatter(
            grad_values_all.reshape(seq_count, seq_len, local_width).astype(jnp.bfloat16),
            "ctx",
            scatter_dimension=1,
            tiled=True,
        ).astype(jnp.float32),
    )
    grad_qnormed = rope_back(grad_queries, cos_full, sin_full)
    grad_knormed = rope_back(grad_keys_own.reshape(head_shape), cos_full, sin_full)
    grad_qgain = jnp.sum(grad_qnormed * query_heads * query_inv, (0, 1, 2))
    grad_kgain = jnp.sum(grad_knormed * key_heads * key_inv, (0, 1, 2))
    grad_qproj = (
        norm_back(grad_qnormed, query_heads, query_inv, query_gain)
        .astype(jnp.bfloat16)
        .reshape(row_count, local_width)
    )
    grad_kproj = (
        norm_back(grad_knormed, key_heads, key_inv, key_gain)
        .astype(jnp.bfloat16)
        .reshape(row_count, local_width)
    )
    grad_vproj = grad_values_own.astype(jnp.bfloat16).reshape(row_count, local_width)
    grad_wq = jnp.einsum("nd,nl->dl", normed_one, grad_qproj, preferred_element_type=jnp.float32)
    grad_wk = jnp.einsum("nd,nl->dl", normed_one, grad_kproj, preferred_element_type=jnp.float32)
    grad_wv = jnp.einsum("nd,nl->dl", normed_one, grad_vproj, preferred_element_type=jnp.float32)
    grad_normed_one = jnp.einsum(
        "nl,dl->nd", grad_qproj, full_query, preferred_element_type=jnp.float32
    )
    grad_normed_one = grad_normed_one + jnp.einsum(
        "nl,dl->nd", grad_kproj, full_key, preferred_element_type=jnp.float32
    )
    grad_normed_one = grad_normed_one + jnp.einsum(
        "nl,dl->nd", grad_vproj, full_value, preferred_element_type=jnp.float32
    )
    grad_normed_one, grad_qgain, grad_kgain = (
        lax.psum(grad_normed_one.astype(jnp.bfloat16), "tp").astype(jnp.float32),
        lax.psum(grad_qgain.astype(jnp.bfloat16), "tp").astype(jnp.float32),
        lax.psum(grad_kgain.astype(jnp.bfloat16), "tp").astype(jnp.float32),
    )
    grad_attn_gain = jnp.sum(grad_normed_one * token_rows * inv_one, 0)
    tokens_grad = grad_residual + norm_back(grad_normed_one, token_rows, inv_one, attn_gain)
    tokens_grad = tokens_grad.astype(jnp.bfloat16).reshape(seq_count, block_len, model_width)
    dw_query, dw_key, dw_value, dw_out, dw_router, dgain_attn, dgain_query, dgain_key, dgain_moe = (
        lax.psum_scatter(grad_wq, ("fsdp", "ctx"), scatter_dimension=0, tiled=True),
        lax.psum_scatter(grad_wk, ("fsdp", "ctx"), scatter_dimension=0, tiled=True),
        lax.psum_scatter(grad_wv, ("fsdp", "ctx"), scatter_dimension=0, tiled=True),
        lax.psum_scatter(grad_w_out, ("fsdp", "ctx"), scatter_dimension=1, tiled=True),
        lax.psum_scatter(grad_router_w, ("fsdp", "ctx"), scatter_dimension=0, tiled=True),
        lax.psum_scatter(grad_attn_gain, ("fsdp", "ctx"), scatter_dimension=0, tiled=True),
        lax.psum_scatter(grad_qgain, ("fsdp", "ctx"), scatter_dimension=0, tiled=True),
        lax.psum_scatter(grad_kgain, ("fsdp", "ctx"), scatter_dimension=0, tiled=True),
        lax.psum_scatter(grad_moe_gain, ("fsdp", "ctx"), scatter_dimension=0, tiled=True),
    )
    return (
        layer_out,
        tokens_grad,
        dw_query,
        dw_key,
        dw_value,
        dw_out,
        dgain_attn,
        dgain_query,
        dgain_key,
        dgain_moe,
        dw_router,
        dw_experts,
    )


def swap(value):
    return lax.ppermute(value, "tp", [(0, 1), (1, 0)])


def exchange(value, axes):
    return lax.all_to_all(value, axes, split_axis=0, concat_axis=0, tiled=True)


def spread(value, axes):
    count = lax.axis_size(axes)
    return exchange(jnp.broadcast_to(value[None], (count,) + value.shape), axes)


def dot(left, right):
    return jnp.dot(left, right, preferred_element_type=jnp.float32)


def dot_nt(left, right):
    return lax.dot_general(left, right, (((1,), (1,)), ((), ())), preferred_element_type=jnp.float32)


def dot_tn(left, right):
    return lax.dot_general(left, right, (((0,), (0,)), ((), ())), preferred_element_type=jnp.float32)


def two_parts(values):
    high = values.astype(jnp.bfloat16)
    low = (values - high.astype(jnp.float32)).astype(jnp.bfloat16)
    return (high, low)


def by_core(mine, other, core):
    return jnp.where(core == 0, jnp.stack([mine, other]), jnp.stack([other, mine]))


def remote(src, dst, send, recv, **where):
    return pltpu.make_async_remote_copy(
        src_ref=src, dst_ref=dst, send_sem=send, recv_sem=recv, device_id=where, device_id_type=MESH
    )


def places():
    return lax.axis_index("fsdp"), lax.axis_index("ctx"), lax.axis_index("tp")


def ring(index, step, count):
    return lax.rem(index + step + count, count)


def greet(nz, nc, line, far=False):
    z, c, t = places()
    barrier = pltpu.get_barrier_semaphore()

    def tell(**where):
        pl.semaphore_signal(barrier, inc=1, device_id=where, device_id_type=MESH)

    if line:
        for step in range(1, nz):
            tell(fsdp=ring(z, step, nz))
        count = nz - 1
    else:
        pl.when(z > 0)(lambda: tell(fsdp=z - 1))
        pl.when(z < nz - 1)(lambda: tell(fsdp=z + 1))
        count = jnp.where(z > 0, 1, 0) + jnp.where(z < nz - 1, 1, 0)
    for step in range(1, nc):
        tell(ctx=ring(c, step, nc))
        if far:
            for hop in range(1, nz):
                tell(fsdp=ring(z, hop, nz), ctx=ring(c, step, nc))
    if far:
        count = count + (nz - 1) * (nc - 1)
    tell(tp=1 - t)
    pl.semaphore_wait(barrier, count + nc)


def line_copies(bufs, send_sem, recv_sem, way, step, shard, target):
    return [
        remote(buf.at[shard], buf.at[shard], send_sem.at[way, step, k], recv_sem.at[way, step, k], fsdp=target)
        for k, buf in enumerate(bufs)
    ]


def line_gather(nz, bufs, send_sem, recv_sem, arrived, begun=None, near=None):
    z = lax.axis_index("fsdp")
    for step in range(nz - 1):

        @pl.when((z < nz - 1) & (z >= step))
        def _():
            for copy in line_copies(bufs, send_sem, recv_sem, 0, step, z - step, z + 1):
                copy.start()

        @pl.when((z > 0) & (z + step < nz))
        def _():
            for copy in line_copies(bufs, send_sem, recv_sem, 1, step, z + step, z - 1):
                copy.start()

        if step == 0 and begun is not None:
            begun()
        if near is not None:
            near(step)

        @pl.when(z - 1 >= step)
        def _():
            for copy in line_copies(bufs, send_sem, recv_sem, 0, step, z - 1 - step, z - 1):
                copy.wait_recv()
            arrived(z - 1 - step)

        @pl.when(z + 1 + step < nz)
        def _():
            for copy in line_copies(bufs, send_sem, recv_sem, 1, step, z + 1 + step, z + 1):
                copy.wait_recv()
            arrived(z + 1 + step)


def line_sent(nz, bufs, send_sem, recv_sem):
    z = lax.axis_index("fsdp")
    for step in range(nz - 1):

        @pl.when((z < nz - 1) & (z >= step))
        def _():
            for copy in line_copies(bufs, send_sem, recv_sem, 0, step, z - step, z + 1):
                copy.wait_send()

        @pl.when((z > 0) & (z + step < nz))
        def _():
            for copy in line_copies(bufs, send_sem, recv_sem, 1, step, z + step, z - 1):
                copy.wait_send()


def pick_rows(pick, slot, source, out):
    lanes = out.shape[-1]
    piece = min(lanes, 512)

    @pl.loop(0, lanes // piece)
    def _(k):
        at = pl.ds(pl.multiple_of(k * piece, piece), piece)
        out[slot, :, at] = jnp.dot(pick[slot], source[slot, :, at], preferred_element_type=jnp.float32).astype(
            jnp.bfloat16
        )


def plane_copy(most, src, dst, send, recv, slot, step, source, target):
    rows = pl.ds(pl.multiple_of(target * most, 16), most)
    return remote(
        src.at[slot, rows], dst.at[source, slot], send.at[slot, step - 1], recv.at[slot, step - 1], ctx=target
    )


def regroup(shard, t, rows, line, two, keep_sem, give_send, give_recv):
    slot = lax.rem(shard, 2)
    band = pl.ds(pl.multiple_of(t * rows, rows), rows)

    def keep():
        pltpu.make_async_copy(line.at[shard], two.at[slot, band], keep_sem.at[slot]).start()

    def give():
        remote(line.at[shard], two.at[slot, band], give_send.at[slot], give_recv.at[slot], tp=1 - t).start()

    pl.when(shard // 2 == t)(keep)
    pl.when(shard // 2 != t)(give)


def selector(nz, src, pair, third, held, pair_out, third_out, in_sem, pair_sem, third_sem):
    c = lax.axis_index("ctx")
    tile = 16
    count = src.shape[2]
    height = held.shape[1]
    bands = src.shape[0] // height

    def take(b):
        slot = lax.rem(b, 2)
        return pltpu.make_async_copy(
            src.at[pl.ds(pl.multiple_of(b * height, height), height)], held.at[slot], in_sem.at[slot]
        )

    def put(b):
        slot = lax.rem(b, 2)
        at = pl.ds(pl.multiple_of(b * height, height), height)
        return (
            pltpu.make_async_copy(pair_out.at[slot], pair.at[:, at], pair_sem.at[slot]),
            pltpu.make_async_copy(third_out.at[slot], third.at[:, :, at], third_sem.at[slot]),
        )

    def pick_band(b):
        slot = lax.rem(b, 2)
        take(b).wait()
        pl.when(b + 1 < bands)(lambda: take(b + 1).start())

        @pl.when(b >= 2)
        def _():
            for copy in put(b - 2):
                copy.wait()

        row = lax.broadcasted_iota(jnp.int32, (nz * tile, tile * count), 0)
        column = lax.broadcasted_iota(jnp.int32, (nz * tile, tile * count), 1)
        hit = column == lax.rem(row, tile) * count + c * nz + row // tile
        hit = jnp.where(hit, 1.0, 0.0).astype(jnp.bfloat16)
        for n in range(height // tile):
            at = pl.ds(n * tile, tile)
            for k in range(3):
                value = held[slot, n * tile : (n + 1) * tile, k].reshape(tile * count, -1)
                value = jnp.dot(hit, value, preferred_element_type=jnp.float32).astype(jnp.bfloat16)
                value = value.reshape(nz, tile, -1)
                if k == 2:
                    pair_out[slot, :, at, :] = value
                else:
                    third_out[slot, k, :, at, :] = value
        for copy in put(b):
            copy.start()

    def close():
        for b in (bands - 2, bands - 1):
            for copy in put(b):
                copy.wait()

    pick_band.close = close
    return take, pick_band, bands


def load_kernel(
    nz, nc, tok, cot, wq, wk, wv, wo, small, rank, w_experts,
    x_all, w_qkv, w_o, small_all, rank_line, rank_seq, pick, cot_in, pair, third, middle,
    cot_line, cot_two, cot_send,
    own_sem, line_send, line_recv, w_send, w_recv, tok_send, tok_recv, pass_send, pass_recv,
    rank_send, rank_recv, keep_sem, give_send, give_recv, cot_s, cot_r, cot_own,
    sel_in, sel_pair, sel_third, sel_s, sel_p, sel_t, mid_s, mid_r,
):
    z, c, t = places()
    block = tok.shape[0]
    rows = block // 2
    local = w_qkv.shape[2] // 3
    most = cot_in.shape[2]
    half = pl.ds(pl.multiple_of(t * rows, rows), rows)
    column = pl.ds(pl.multiple_of(c * local, local), local)
    own = [
        pltpu.make_async_copy(cot.at[half], cot_line.at[z], own_sem.at[5]),
        pltpu.make_async_copy(small, small_all.at[z], own_sem.at[4]),
        pltpu.make_async_copy(rank, rank_line.at[z], own_sem.at[7]),
        pltpu.make_async_copy(rank, rank_seq.at[c], own_sem.at[8]),
    ]
    own += [
        pltpu.make_async_copy(w.at[:, column], w_qkv.at[z, :, pl.ds(k * local, local)], own_sem.at[k])
        for k, w in enumerate((wq, wk, wv))
    ]
    own += [
        pltpu.make_async_copy(wo.at[column], w_o.at[z], own_sem.at[3]),
        pltpu.make_async_copy(tok, x_all.at[pl.ds(pl.multiple_of(c * block, block), block)], own_sem.at[6]),
    ]
    for copy in own:
        copy.start()
    take, pick_band, bands = selector(nz, w_experts, pair, third, sel_in, sel_pair, sel_third, sel_s, sel_p, sel_t)
    take(0).start()
    greet(nz, nc, False)

    def band(source, core):
        return x_all.at[pl.ds(pl.multiple_of(source * block + core * rows, rows), rows)]

    def token_copy(step, source, target):
        return remote(tok.at[half], band(source, t), tok_send.at[step], tok_recv.at[step], ctx=target)

    def pass_copy(step, source, core):
        return remote(band(source, core), band(source, core), pass_send.at[step], pass_recv.at[step], tp=1 - t)

    def rank_copy(step, source, target):
        return remote(rank, rank_seq.at[source], rank_send.at[step], rank_recv.at[step], ctx=target)

    for step in range(1, nc):
        token_copy(step - 1, c, ring(c, step, nc)).start()
        rank_copy(step - 1, c, ring(c, step, nc)).start()
    for copy in own:
        copy.wait()

    def arrived(shard):
        regroup(shard, t, rows, cot_line, cot_two, keep_sem, give_send, give_recv)

    arrived(z)
    first = (cot_line, rank_line, small_all)
    line_gather(nz, first, line_send, line_recv, arrived)

    def own_copy(slot):
        return pltpu.make_async_copy(
            cot_send.at[slot, pl.ds(pl.multiple_of(c * most, 16), most)], cot_in.at[c, slot], cot_own.at[slot]
        )

    def send_cotangent():
        number = lax.broadcasted_iota(jnp.int32, (most, block), 0).astype(jnp.float32)
        for slot in range(2):
            for q in range(nc):
                row = rank_line[2 * t + slot, pl.ds(q * nz + z, 1), :]
                hit = jnp.where(number == row, 1.0, 0.0)
                pick[slot, pl.ds(q * most, most), :] = hit.astype(jnp.bfloat16)
        for slot in range(2):
            wait_two(slot, t, rows, cot_line, cot_two, keep_sem, give_recv)
            pick_rows(pick, slot, cot_two, cot_send)
            for step in range(1, nc):
                plane_copy(most, cot_send, cot_in, cot_s, cot_r, slot, step, c, ring(c, step, nc)).start()
            own_copy(slot).start()

    def ignore(shard):
        pass

    partner = nz - 1 - z
    centre = (z == nz // 2 - 1) | (z == nz // 2)
    middle_copy = remote(third.at[:, partner], middle, mid_s, mid_r, fsdp=partner)

    def select_some(step):
        pl.loop(bands * (0, 1, 3)[step] // 4, bands * (1, 3, 4)[step] // 4)(pick_band)
        if step == 2:
            pick_band.close()
            pl.when(centre)(lambda: middle_copy.start())

    line_gather(nz, (w_qkv, w_o), w_send, w_recv, ignore, send_cotangent, select_some)
    for step in range(1, nc):
        source = ring(c, -step, nc)
        token_copy(step - 1, source, source).wait_recv()
        pass_copy(step - 1, source, t).start()
        rank_copy(step - 1, source, source).wait_recv()
    for step in range(1, nc):
        source = ring(c, -step, nc)
        pass_copy(step - 1, source, 1 - t).wait_recv()
        pass_copy(step - 1, source, t).wait_send()
        token_copy(step - 1, c, source).wait_send()
        rank_copy(step - 1, c, source).wait_send()
        for slot in range(2):
            copy = plane_copy(most, cot_send, cot_in, cot_s, cot_r, slot, step, source, source)
            copy.wait_recv()
            copy.wait_send()
    line_sent(nz, first, line_send, line_recv)
    line_sent(nz, (w_qkv, w_o), w_send, w_recv)
    for slot in range(2):
        own_copy(slot).wait()
        wait_given(slot, t, rows, cot_line, cot_two, give_send, give_recv)

    @pl.when(centre)
    def _():
        middle_copy.wait_recv()
        middle_copy.wait_send()


def wait_given(slot, t, rows, line, two, give_send, give_recv):
    band = pl.ds(pl.multiple_of(t * rows, rows), rows)
    remote(line.at[0], two.at[slot, band], give_send.at[slot], give_recv.at[slot], tp=1 - t).wait_send()


def wait_two(slot, t, rows, line, two, keep_sem, give_recv):
    band = pl.ds(pl.multiple_of(t * rows, rows), rows)
    other = pl.ds(pl.multiple_of((1 - t) * rows, rows), rows)
    pltpu.make_async_copy(line.at[0], two.at[slot, band], keep_sem.at[slot]).wait()
    remote(line.at[0], two.at[slot, other], give_recv.at[slot], give_recv.at[slot], tp=1 - t).wait_recv()


def load(tok, cot, wq, wk, wv, wo, small, rank, w_experts, most):
    nz, nc = lax.axis_size("fsdp"), lax.axis_size("ctx")
    block, width = tok.shape
    deep, local = wq.shape[0], wq.shape[1] // nc
    rows = block // 2
    count, ffn = w_experts.shape[2:]
    dma = pltpu.SemaphoreType.DMA
    bf16, f32 = jnp.bfloat16, jnp.float32
    shapes = [
        ((nc * block, width), bf16),
        ((nz, deep, 3 * local), bf16),
        ((nz, local, wo.shape[1]), bf16),
        ((nz,) + small.shape, bf16),
        ((nz,) + rank.shape, f32),
        ((nc,) + rank.shape, f32),
        ((2, nc * most, block), bf16),
        ((nc, 2, most, width), bf16),
        ((nz, deep, ffn), bf16),
        ((2, nz, deep, ffn), bf16),
        ((2, deep, ffn), bf16),
    ]
    hbm = pl.BlockSpec(memory_space=pl.ANY)
    height = 32
    return pl.pallas_call(
        functools.partial(load_kernel, nz, nc),
        out_shape=[jax.ShapeDtypeStruct(shape, kind) for shape, kind in shapes],
        in_specs=[hbm] * 9,
        out_specs=[pl.BlockSpec(memory_space=pltpu.VMEM)] * 7 + [hbm] * 4,
        scratch_shapes=[
            pltpu.VMEM((nz, rows, width), bf16),
            pltpu.VMEM((2, block, width), bf16),
            pltpu.VMEM((2, nc * most, width), bf16),
            dma((9,)),
            dma((2, nz - 1, 3)), dma((2, nz - 1, 3)), dma((2, nz - 1, 2)), dma((2, nz - 1, 2)),
            dma((nc - 1,)), dma((nc - 1,)), dma((nc - 1,)), dma((nc - 1,)), dma((nc - 1,)), dma((nc - 1,)),
            dma((2,)), dma((2,)), dma((2,)), dma((2, nc - 1)), dma((2, nc - 1)), dma((2,)),
            pltpu.VMEM((2, height, 3, count, ffn), bf16),
            pltpu.VMEM((2, nz, height, ffn), bf16),
            pltpu.VMEM((2, 2, nz, height, ffn), bf16),
            dma((2,)), dma((2,)), dma((2,)), dma, dma,
        ],
        compiler_params=pltpu.CompilerParams(
            collective_id=0, has_side_effects=True, vmem_limit_bytes=60 * 2**20
        ),
    )(tok, cot, wq, wk, wv, wo, small, rank, w_experts)


def dispatch_kernel(
    nz, nc, part, tok, gain, router, kept, pick, third, middle,
    residual, normed, probs, x_in, g_in, third_got,
    sib, rs_send, rs_recv, n_line, g_line, n_two, g_two, x_send, g_send,
    sib_s, sib_r, rs_s, rs_r, line_send, line_recv, keep_sem, give_send, give_recv,
    gkeep_sem, ggive_send, ggive_recv, x_s, x_r, g_s, g_r, own_sem,
    third_s, third_r, third_own, mid_own,
):
    z, c, t = places()
    f32, bf16 = jnp.float32, jnp.bfloat16
    rows, width = residual.shape
    most = x_in.shape[2]
    greet(nz, nc, True)
    keep_third = pltpu.make_async_copy(third.at[:, z], third_got.at[:, z], third_own)
    keep_third.start()
    partner = nz - 1 - z
    centre = (z == nz // 2 - 1) | (z == nz // 2)
    keep_middle = pltpu.make_async_copy(middle, third_got.at[:, partner], mid_own)
    pl.when(centre)(lambda: keep_middle.start())

    def still(other):
        return jnp.logical_not(centre & (other == partner))

    def third_copy(kind, step, source, target):
        return remote(
            third.at[kind, target], third_got.at[kind, source], third_s.at[kind, step], third_r.at[kind, step],
            fsdp=target,
        )

    def send_third(kind):
        for step in range(1, nz):
            target = ring(z, step, nz)
            pl.when(still(target))(lambda: third_copy(kind, step - 1, z, target).start())

    def sib_copy(q):
        return remote(part.at[q, 1 - t], sib.at[q], sib_s.at[q], sib_r.at[q], tp=1 - t)

    def rs_copy(step, source, target):
        return remote(rs_send.at[step], rs_recv.at[step], rs_s.at[step], rs_r.at[step], ctx=target)

    for step in range(1, nc + 1):
        sib_copy(ring(c, step, nc)).start()
    chunk = 16
    for step in range(1, nc):
        q = ring(c, step, nc)
        sib_copy(q).wait_recv()

        @pl.loop(0, rows // chunk)
        def _(k):
            at = pl.ds(pl.multiple_of(k * chunk, chunk), chunk)
            rs_send[step - 1, at, :] = (part[q, t, at, :].astype(f32) + sib[q, at, :].astype(f32)).astype(bf16)

        rs_copy(step - 1, c, q).start()

    def own_copy(slot, src, dst, k):
        return pltpu.make_async_copy(
            src.at[slot, pl.ds(pl.multiple_of(c * most, 16), most)], dst.at[c, slot], own_sem.at[k, slot]
        )

    send_third(0)
    sib_copy(c).wait_recv()
    for step in range(1, nc):
        rs_copy(step - 1, c, c).wait_recv()

    @pl.loop(0, rows // chunk)
    def _(k):
        at = pl.ds(pl.multiple_of(k * chunk, chunk), chunk)
        start = pl.ds(pl.multiple_of(t * rows + k * chunk, chunk), chunk)
        total = part[c, t, at, :].astype(f32) + sib[c, at, :].astype(f32)
        for step in range(nc - 1):
            total = total + rs_recv[step, at, :].astype(f32)
        total = total + tok[start, :].astype(f32)
        residual[at, :] = total
        inv = lax.rsqrt(jnp.mean(total * total, -1, keepdims=True) + EPS)
        row = (total * inv * gain[...]).astype(bf16)
        normed[at, :] = row
        n_line[z, at, :] = row

    logits = lax.dot_general(
        normed[...], router[...], (((1,), (1,)), ((), ())), preferred_element_type=f32
    )
    lane = lax.broadcasted_iota(jnp.int32, logits.shape, 1)
    logits = jnp.where(lane < E, logits, -jnp.inf)
    top = jnp.max(logits, -1, keepdims=True)
    raised = jnp.exp(logits - top)
    prob = raised / jnp.sum(raised, -1, keepdims=True)
    probs[...] = prob
    gates = prob * kept[...]
    high = gates.astype(bf16)
    g_line[z, :, pl.ds(0, 128)] = high
    g_line[z, :, pl.ds(128, 128)] = (gates - high.astype(f32)).astype(bf16)

    def arrived(shard):
        regroup(shard, t, rows, n_line, n_two, keep_sem, give_send, give_recv)
        regroup(shard, t, rows, g_line, g_two, gkeep_sem, ggive_send, ggive_recv)

    arrived(z)
    sent = ((x_send, x_in, x_s, x_r), (g_send, g_in, g_s, g_r))

    def near(distance):
        above, below = z + distance, z - distance
        is_above = (above < nz) & (above // 2 == t)
        is_below = (below >= 0) & (below // 2 == t)
        slot = lax.rem(jnp.where(is_above, above, below + 2), 2)

        @pl.when(is_above | is_below)
        def _():
            wait_two(slot, t, rows, n_line, n_two, keep_sem, give_recv)
            wait_two(slot, t, rows, g_line, g_two, gkeep_sem, ggive_recv)
            pick_rows(pick, slot, n_two, x_send)
            pick_rows(pick, slot, g_two, g_send)
            for k, (src, dst, s, r) in enumerate(sent):
                for step in range(1, nc):
                    plane_copy(most, src, dst, s, r, slot, step, c, ring(c, step, nc)).start()
                own_copy(slot, src, dst, k).start()

    line_gather(nz, (n_line, g_line), line_send, line_recv, arrived, None, near)
    near(nz - 1)
    send_third(1)
    line_sent(nz, (n_line, g_line), line_send, line_recv)
    for slot in range(2):
        wait_given(slot, t, rows, n_line, n_two, give_send, give_recv)
        wait_given(slot, t, rows, g_line, g_two, ggive_send, ggive_recv)
        for k, (src, dst, s, r) in enumerate(sent):
            own_copy(slot, src, dst, k).wait()
            for step in range(1, nc):
                source = ring(c, -step, nc)
                copy = plane_copy(most, src, dst, s, r, slot, step, source, source)
                copy.wait_recv()
                copy.wait_send()
    for step in range(1, nc):
        rs_copy(step - 1, c, c).wait_send()
    for step in range(nc):
        sib_copy(step).wait_send()
    for step in range(1, nz):
        source = ring(z, -step, nz)
        for kind in range(2):
            pl.when(still(source))(lambda: third_copy(kind, step - 1, source, source).wait_recv())
            pl.when(still(ring(z, step, nz)))(lambda: third_copy(kind, step - 1, source, source).wait_send())
    keep_third.wait()
    pl.when(centre)(lambda: keep_middle.wait())


def dispatch(part, tok, gain, router, kept, pick, third, middle):
    nz, nc = lax.axis_size("fsdp"), lax.axis_size("ctx")
    rows, width = part.shape[2], part.shape[3]
    block = rows * 2
    most = pick.shape[1] // nc
    dma = pltpu.SemaphoreType.DMA
    bf16, f32 = jnp.bfloat16, jnp.float32
    vmem = pl.BlockSpec(memory_space=pltpu.VMEM)
    hbm = pl.BlockSpec(memory_space=pl.ANY)
    return pl.pallas_call(
        functools.partial(dispatch_kernel, nz, nc),
        out_shape=[
            jax.ShapeDtypeStruct((rows, width), f32),
            jax.ShapeDtypeStruct((rows, width), bf16),
            jax.ShapeDtypeStruct((rows, 128), f32),
            jax.ShapeDtypeStruct((nc, 2, most, width), bf16),
            jax.ShapeDtypeStruct((nc, 2, most, 256), bf16),
            jax.ShapeDtypeStruct(third.shape, bf16),
        ],
        in_specs=[vmem] * 6 + [hbm] * 2,
        out_specs=[vmem] * 3 + [hbm] * 3,
        scratch_shapes=[
            pltpu.VMEM((nc, rows, width), bf16),
            pltpu.VMEM((nc - 1, rows, width), bf16),
            pltpu.VMEM((nc - 1, rows, width), bf16),
            pltpu.VMEM((nz, rows, width), bf16),
            pltpu.VMEM((nz, rows, 256), bf16),
            pltpu.VMEM((2, block, width), bf16),
            pltpu.VMEM((2, block, 256), bf16),
            pltpu.VMEM((2, nc * most, width), bf16),
            pltpu.VMEM((2, nc * most, 256), bf16),
            dma((nc,)), dma((nc,)), dma((nc - 1,)), dma((nc - 1,)),
            dma((2, nz - 1, 2)), dma((2, nz - 1, 2)),
            dma((2,)), dma((2,)), dma((2,)), dma((2,)), dma((2,)), dma((2,)),
            dma((2, nc - 1)), dma((2, nc - 1)), dma((2, nc - 1)), dma((2, nc - 1)),
            dma((2, 2)),
            dma((2, nz - 1)), dma((2, nz - 1)), dma, dma,
        ],
        compiler_params=pltpu.CompilerParams(
            collective_id=1, has_side_effects=True, vmem_limit_bytes=56 * 2**20
        ),
    )(part, tok, gain, router, kept, pick, third, middle)


def experts_kernel(
    nz, nc, x_hbm, cot_hbm, gates, pair_hbm, third_hbm, y_hbm, r_hbm, pair_out, hid_hbm, gg_hbm, gu_hbm,
    x, cot, w, weight, pair, gate, up, out_grad, y, r, hid, gg, gu,
    sem, swap_s, swap_r, out_sem, inner_sem,
):
    z, c, t = places()
    f32, bf16 = jnp.float32, jnp.bfloat16
    width, tall = x.shape[1], x.shape[0]
    deep, ffn = w.shape[3], w.shape[4]
    span = 256
    chunk = 288
    copies = [
        pltpu.make_async_copy(cot_hbm, cot, sem.at[0]),
        pltpu.make_async_copy(pair_hbm, w.at[0, :, 1], sem.at[1]),
        pltpu.make_async_copy(x_hbm, x, sem.at[2]),
        pltpu.make_async_copy(third_hbm.at[0], w.at[0, :, 0], sem.at[3]),
        pltpu.make_async_copy(third_hbm.at[1], w.at[0, :, 2], sem.at[4]),
    ]
    for copy in copies:
        copy.start()
    barrier = pltpu.get_barrier_semaphore()
    pl.semaphore_signal(barrier, inc=1, device_id=dict(tp=1 - t), device_id_type=MESH)
    pl.semaphore_wait(barrier, 1)
    swaps = [
        remote(pair_hbm, w.at[1, :, 1], swap_s.at[0], swap_r.at[0], tp=1 - t),
        remote(third_hbm.at[0], w.at[1, :, 0], swap_s.at[1], swap_r.at[1], tp=1 - t),
        remote(third_hbm.at[1], w.at[1, :, 2], swap_s.at[2], swap_r.at[2], tp=1 - t),
    ]
    for copy in swaps:
        copy.start()
    pair[...] = jnp.zeros_like(pair)
    lane = lax.broadcasted_iota(jnp.int32, (chunk, 256), 1)
    mine = c * nz + z

    @pl.loop(0, tall // chunk)
    def _(m):
        rows = pl.ds(pl.multiple_of(m * chunk, chunk), chunk)
        value = gates[rows, :].astype(f32)
        value = jnp.where((lane == mine) | (lane == mine + 128), value, 0.0)
        weight[rows, :] = jnp.sum(value, 1, keepdims=True)

    for copy in copies[:2]:
        copy.wait()
    per = ffn // span

    def forward(n):
        half, at = n // per, pl.ds(pl.multiple_of(lax.rem(n, per) * span, span), span)
        full = pl.ds(pl.multiple_of(n * span, span), span)

        def times(rows, k):
            return jnp.dot(rows[...], w[half, :, k, :, at].reshape(width, span), preferred_element_type=f32)

        out_grad[...] = times(cot, 1)

        @pl.when(n == 0)
        def _():
            for copy in copies[2:]:
                copy.wait()

        gate[...] = times(x, 0)
        up[...] = times(x, 2)

        @pl.loop(0, tall // chunk)
        def _(m):
            rows = pl.ds(pl.multiple_of(m * chunk, chunk), chunk)
            g, u, o, k = gate[rows, :], up[rows, :], out_grad[rows, :], weight[rows, :]
            sig = 1.0 / (1.0 + jnp.exp(-g))
            silu = g * sig
            hidden = silu * u
            pair[rows, :] += jnp.sum(hidden.astype(bf16).astype(f32) * o, 1, keepdims=True)
            hid[rows, full] = (k * hidden).astype(bf16)
            o = k * o
            gg[rows, full] = (o * u * sig * (1.0 + g * (1.0 - sig))).astype(bf16)
            gu[rows, full] = (o * silu).astype(bf16)

    pl.loop(0, per)(forward)
    for copy in swaps:
        copy.wait_recv()
    pl.loop(per, 2 * per)(forward)

    @pl.loop(0, tall // chunk)
    def _(m):
        rows = pl.ds(pl.multiple_of(m * chunk, chunk), chunk)
        value = pair[rows, :]
        high = value.astype(bf16).astype(f32)
        out = jnp.where(lane == mine, high, jnp.where(lane == mine + 128, value - high, 0.0))
        pair_out[rows, :] = out.astype(bf16)

    inner = [
        pltpu.make_async_copy(src, dst, inner_sem.at[k])
        for k, (src, dst) in enumerate(((hid, hid_hbm), (gg, gg_hbm), (gu, gu_hbm)))
    ]
    for copy in inner:
        copy.start()
    per_deep = deep // span

    def leave(n):
        full = pl.ds(pl.multiple_of(n * span, span), span)
        return (
            pltpu.make_async_copy(y.at[:, full], y_hbm.at[:, full], out_sem.at[0, n]),
            pltpu.make_async_copy(r.at[:, full], r_hbm.at[:, full], out_sem.at[1, n]),
        )

    @pl.loop(0, width // span)
    def _(n):
        zone, at = n // per_deep, pl.ds(pl.multiple_of(lax.rem(n, per_deep) * span, span), span)
        full = pl.ds(pl.multiple_of(n * span, span), span)

        def back(rows, k):
            total = 0.0
            for half in range(2):
                total = total + lax.dot_general(
                    rows[:, pl.ds(half * ffn, ffn)], w[half, zone, k, at, :], (((1,), (1,)), ((), ())),
                    preferred_element_type=f32,
                )
            return total

        y[:, full] = back(hid, 1).astype(bf16)
        r[:, full] = (back(gg, 0) + back(gu, 2)).astype(bf16)
        for copy in leave(n):
            copy.start()

    for n in range(width // span):
        for copy in leave(n):
            copy.wait()
    for copy in inner:
        copy.wait()
    for copy in swaps:
        copy.wait_send()


def experts(x, cot, gates, pair, third):
    bf16, f32 = jnp.bfloat16, jnp.float32
    nz, nc = lax.axis_size("fsdp"), lax.axis_size("ctx")
    tall, width = x.shape
    deep, ffn = third.shape[2:]
    vmem = pl.BlockSpec(memory_space=pltpu.VMEM)
    hbm = pl.BlockSpec(memory_space=pl.ANY)
    inner = jax.ShapeDtypeStruct((tall, 2 * ffn), bf16)
    dma = pltpu.SemaphoreType.DMA
    return pl.pallas_call(
        functools.partial(experts_kernel, nz, nc),
        out_shape=[
            jax.ShapeDtypeStruct((tall, width), bf16),
            jax.ShapeDtypeStruct((tall, width), bf16),
            jax.ShapeDtypeStruct((tall, 256), bf16),
            inner,
            inner,
            inner,
        ],
        in_specs=[hbm, hbm, vmem, hbm, hbm],
        out_specs=[hbm, hbm, vmem, hbm, hbm, hbm],
        scratch_shapes=[
            pltpu.VMEM((tall, width), bf16),
            pltpu.VMEM((tall, width), bf16),
            pltpu.VMEM((2, nz, 3, deep, ffn), bf16),
            pltpu.VMEM((tall, 1), f32),
            pltpu.VMEM((tall, 1), f32),
            pltpu.VMEM((tall, 256), f32),
            pltpu.VMEM((tall, 256), f32),
            pltpu.VMEM((tall, 256), f32),
            pltpu.VMEM((tall, width), bf16),
            pltpu.VMEM((tall, width), bf16),
            pltpu.VMEM((tall, 2 * ffn), bf16),
            pltpu.VMEM((tall, 2 * ffn), bf16),
            pltpu.VMEM((tall, 2 * ffn), bf16),
            dma((5,)), dma((3,)), dma((3,)), dma((2, width // 256)), dma((3,)),
        ],
        compiler_params=pltpu.CompilerParams(
            collective_id=4, has_side_effects=True, vmem_limit_bytes=60 * 2**20
        ),
    )(x, cot, gates, pair, third)


def place_kernel(nz, nc, gate, rest, out):
    tile = rest.shape[1]
    count = nz * nc
    row = lax.broadcasted_iota(jnp.int32, (tile * count, tile * count), 0)
    column = lax.broadcasted_iota(jnp.int32, (tile * count, tile * count), 1)
    expert = lax.rem(row, count)
    hit = column == (lax.rem(expert, nz) * nc + expert // nz) * tile + row // count
    hit = jnp.where(hit, 1.0, 0.0).astype(jnp.bfloat16)
    for k in range(3):
        value = (gate[k] if k < 2 else rest[...]).reshape(count * tile, -1)
        value = jnp.dot(hit, value, preferred_element_type=jnp.float32)
        out[:, k] = value.reshape(tile, count, -1)


def lay_out(gate, rest, nz, nc):
    count, strip, ffn = rest.shape
    tile = 16
    return pl.pallas_call(
        functools.partial(place_kernel, nz, nc),
        grid=(strip // tile,),
        out_shape=jax.ShapeDtypeStruct((strip, 3, count, ffn), jnp.float32),
        in_specs=[
            pl.BlockSpec((2, count, tile, ffn), lambda i: (0, 0, i, 0)),
            pl.BlockSpec((count, tile, ffn), lambda i: (0, i, 0)),
        ],
        out_specs=pl.BlockSpec((tile, 3, count, ffn), lambda i: (i, 0, 0, 0)),
        compiler_params=pltpu.CompilerParams(vmem_limit_bytes=40 * 2**20),
    )(gate, rest)


def collector(nz, nc, pick_t, items, sems):
    z, c, t = places()
    to_s, to_r, own_sem, sib_s, sib_r, line_s, line_r, keep_sem = sems
    rows = items[0][2].shape[1]
    mine_at = pl.ds(pl.multiple_of(t * rows, rows), rows)
    give_at = pl.ds(pl.multiple_of((1 - t) * rows, rows), rows)
    count = len(items)

    def lanes(turn, k):
        wide = items[k][2].shape[-1] // 2
        return pl.ds(turn * wide, wide)

    def to_copy(turn, k, step, source, target):
        src, got = items[k][:2]
        at = lanes(turn, k)
        return remote(
            src.at[target, :, :, at], got.at[source, :, :, at], to_s.at[k, turn, step - 1], to_r.at[k, turn, step - 1],
            ctx=target,
        )

    def own_copy(turn, k):
        src, got = items[k][:2]
        at = lanes(turn, k)
        return pltpu.make_async_copy(src.at[c, :, :, at], got.at[c, :, :, at], own_sem.at[k, turn])

    def sib_copy(turn, k):
        give, sib = items[k][3:5]
        at = lanes(turn, k)
        return remote(give.at[:, :, at], sib.at[:, :, at], sib_s.at[k, turn], sib_r.at[k, turn], tp=1 - t)

    def line_copy(turn, slot, k, half, source, target):
        src = items[k][2 if half == 0 else 4]
        at = lanes(turn, k)
        return remote(
            src.at[slot, :, at], items[k][5].at[source, :, at],
            line_s.at[k, turn, 2 * half + slot], line_r.at[k, turn, source], fsdp=target,
        )

    def keep_copy(turn, slot, k, half):
        src = items[k][2 if half == 0 else 4]
        at = lanes(turn, k)
        return pltpu.make_async_copy(src.at[slot, :, at], items[k][5].at[z, :, at], keep_sem.at[k, turn])

    def goal(slot, half):
        return 2 * (t if half == 0 else 1 - t) + slot

    def forward(turn, k, half):
        for slot in range(2):
            target = goal(slot, half)
            pl.when(target != z)(lambda: line_copy(turn, slot, k, half, z, target).start())
            pl.when(target == z)(lambda: keep_copy(turn, slot, k, half).start())

    def begin(turn):
        for k in range(count):
            for step in range(1, nc):
                to_copy(turn, k, step, c, ring(c, step, nc)).start()
            own_copy(turn, k).start()

    def scatter(turn, slot, k):
        got, mine, give = items[k][1:4]
        wide = mine.shape[-1] // 2
        span = min(wide, 512)
        tall = got.shape[0] * got.shape[2]

        @pl.loop(0, wide // span)
        def _(n):
            at = pl.ds(pl.multiple_of(turn * wide + n * span, span), span)
            pairs = got[:, slot, :, at].reshape(tall, span)
            for picks, out in ((mine_at, mine), (give_at, give)):
                out[slot, :, at] = jnp.dot(
                    pick_t[slot, picks, :], pairs, preferred_element_type=jnp.float32
                ).astype(jnp.bfloat16)

    def process(turn):
        for k in range(count):
            own_copy(turn, k).wait()
            for step in range(1, nc):
                source = ring(c, -step, nc)
                to_copy(turn, k, step, source, c).wait_recv()
            for slot in range(2):
                scatter(turn, slot, k)
            sib_copy(turn, k).start()
            forward(turn, k, 0)
        for k in range(count):
            sib_copy(turn, k).wait_recv()
            forward(turn, k, 1)

    def join():
        for turn in range(2):
            for k in range(count):
                keep_copy(turn, 0, k, 0).wait()
                for step in range(1, nz):
                    line_copy(turn, 0, k, 0, ring(z, -step, nz), z).wait_recv()

    def done():
        for turn in range(2):
            for k in range(count):
                for step in range(1, nc):
                    to_copy(turn, k, step, c, ring(c, step, nc)).wait_send()
                sib_copy(turn, k).wait_send()
                for half in range(2):
                    for slot in range(2):
                        pl.when(goal(slot, half) != z)(
                            lambda: line_copy(turn, slot, k, half, z, goal(slot, half)).wait_send()
                        )

    return begin, process, join, done


def collector_scratch(nz, nc, most, rows, widths):
    dma = pltpu.SemaphoreType.DMA
    bf16 = jnp.bfloat16
    count = len(widths)
    bufs = []
    for w in widths:
        bufs += [pltpu.VMEM((nc, 2, most, w), bf16)]
        bufs += [pltpu.VMEM((2, rows, w), bf16)] * 3
        bufs += [pltpu.VMEM((nz, rows, w), bf16)]
    sems = [
        dma((count, 2, nc - 1)), dma((count, 2, nc - 1)), dma((count, 2)), dma((count, 2)), dma((count, 2)),
        dma((count, 2, 4)), dma((count, 2, nz)), dma((count, 2)),
    ]
    return bufs, sems


def return_kernel(
    nz, nc, r, g, x_hbm, cot_hbm, hid_hbm, gg_hbm, gu_hbm, pick_t, residual, probs, kept, router, gain, cot,
    logits_grad, gain_grad, residual_grad, attn_grad, early_got, rest,
    x, cot_rows, hid, gg, gu, stage, early, early_sib,
    load_sem, keep_sem, give_sem, got_sem, *scratch,
):
    z, c, t = places()
    f32, bf16 = jnp.float32, jnp.bfloat16
    rows, width = residual.shape
    r_line, g_line = scratch[4], scratch[9]
    row_s, row_r, pass_s, pass_r, early_s, early_r, early_own = scratch[18:]
    items = ((r,) + scratch[:5], (g,) + scratch[5:10])
    begin, process, join, done = collector(nz, nc, pick_t, items, scratch[10:18])
    here = z * nc + c
    def keep_early(kind):
        return pltpu.make_async_copy(early.at[kind, here], early_got.at[kind, here], early_own.at[kind])

    loads = [
        pltpu.make_async_copy(src, dst, load_sem.at[k])
        for k, (src, dst) in enumerate(
            ((x_hbm, x), (gg_hbm, gg), (gu_hbm, gu), (cot_hbm, cot_rows), (hid_hbm, hid))
        )
    ]
    for copy in loads:
        copy.start()
    greet(nz, nc, True, True)
    chips = nz * nc
    steps = [(i, j) for i in range(nz) for j in range(nc) if i or j]

    def early_copy(kind, n, source, target, fsdp, ctx):
        return remote(
            early.at[kind, target], early_got.at[kind, source], early_s.at[kind, n], early_r.at[kind, n],
            fsdp=fsdp, ctx=ctx,
        )

    def send_early(kind):
        keep_early(kind).start()
        for n, (i, j) in enumerate(steps):
            zz, cc = ring(z, i, nz), ring(c, j, nc)
            early_copy(kind, n, here, zz * nc + cc, zz, cc).start()

    begin(0)
    begin(1)

    span = 256
    strip, ffn = stage.shape[2], stage.shape[3]
    per = span // strip
    bands = width // span

    def gradients(kind, rows_in, grads):
        def flush(n):
            slot = lax.rem(n, 2)
            at = pl.ds(pl.multiple_of(n * per, per), per)
            return remote(stage.at[slot], early_sib.at[kind, at], give_sem.at[slot], got_sem.at[kind], tp=1 - t)

        @pl.loop(0, bands)
        def _(n):
            full = pl.ds(pl.multiple_of(n * span, span), span)
            slot = lax.rem(n, 2)
            pl.when(n >= 2)(lambda: flush(n - 2).wait_send())
            value = lax.dot_general(
                rows_in[:, full], grads[...], (((0,), (0,)), ((), ())), preferred_element_type=f32
            ).astype(bf16)
            for i in range(per):
                piece = value[i * strip : (i + 1) * strip]
                early[kind, n * per + i] = piece[:, :ffn]
                stage[slot, i] = piece[:, ffn:]
            flush(n).start()

        flush(bands - 2).wait_send()
        flush(bands - 1).wait_send()
        remote(early_sib.at[kind], early_sib.at[kind], got_sem.at[kind], got_sem.at[kind], tp=1 - t).wait_recv()

        @pl.loop(0, chips)
        def _(n):
            early[kind, n] = (early[kind, n].astype(f32) + early_sib[kind, n].astype(f32)).astype(bf16)

    loads[0].wait()
    loads[1].wait()
    gradients(0, x, gg)
    send_early(0)
    for copy in loads[2:]:
        copy.wait()
    gradients(1, x, gu)
    gradients(2, cot_rows, hid)
    keep_rest = pltpu.make_async_copy(early.at[2], rest, keep_sem)
    keep_rest.start()
    for turn in range(2):
        process(turn)
    join()
    pairs = jnp.zeros((rows, 128), f32)
    for source in range(nz):
        pairs = pairs + g_line[source, :, 0:128].astype(f32) + g_line[source, :, 128:256].astype(f32)
    pairs = pairs * kept[...]
    prob = probs[...]
    grad_logits = (prob * (pairs - jnp.sum(prob * pairs, -1, keepdims=True))).astype(bf16)
    logits_grad[...] = grad_logits
    gain_grad[...] = jnp.zeros_like(gain_grad)
    chunk = 16

    @pl.loop(0, rows // chunk)
    def _(k):
        at = pl.ds(pl.multiple_of(k * chunk, chunk), chunk)
        full = pl.ds(pl.multiple_of(t * rows + k * chunk, chunk), chunk)
        res = residual[at, :]
        grad = r_line[0, at, :].astype(f32)
        for source in range(1, nz):
            grad = grad + r_line[source, at, :].astype(f32)
        grad = grad + jnp.dot(logits_grad[at, :], router[...], preferred_element_type=f32)
        inv = lax.rsqrt(jnp.mean(res * res, -1, keepdims=True) + EPS)
        gain_grad[...] += jnp.sum((grad * res * inv).reshape(chunk // 8, 8, width), 0)
        weighted = grad * gain[...]
        inner = jnp.sum(weighted * res, -1, keepdims=True)
        out = cot[full, :].astype(f32) + inv * weighted - res * (inv * inv * inv) * inner / width
        residual_grad[at, :] = out
        attn_grad[c, t, at, :] = out.astype(bf16)

    def row_copy(step, source, target):
        return remote(attn_grad.at[source, t], attn_grad.at[source, t], row_s.at[step], row_r.at[step], ctx=target)

    def pass_copy(step, source, core):
        return remote(attn_grad.at[source, core], attn_grad.at[source, core], pass_s.at[step], pass_r.at[step], tp=1 - t)

    for step in range(1, nc):
        row_copy(step, c, ring(c, step, nc)).start()
    pass_copy(0, c, t).start()
    send_early(1)
    for step in range(1, nc):
        source = ring(c, -step, nc)
        row_copy(step, source, source).wait_recv()
        pass_copy(step, source, t).start()
    for step in range(nc):
        source = ring(c, -step, nc)
        pass_copy(step, source, 1 - t).wait_recv()
        pass_copy(step, source, t).wait_send()
        if step:
            row_copy(step, c, source).wait_send()
    done()
    for kind in range(2):
        for n, (i, j) in enumerate(steps):
            zz, cc = ring(z, -i, nz), ring(c, -j, nc)
            copy = early_copy(kind, n, zz * nc + cc, zz * nc + cc, zz, cc)
            copy.wait_recv()
            copy.wait_send()
        keep_early(kind).wait()
    keep_rest.wait()


def give_back(r, g, x, cot_rows, hid, gg, gu, pick_t, residual, probs, kept, router, gain, cot):
    nz, nc = lax.axis_size("fsdp"), lax.axis_size("ctx")
    rows, width = residual.shape
    dma = pltpu.SemaphoreType.DMA
    bf16, f32 = jnp.bfloat16, jnp.float32
    vmem = pl.BlockSpec(memory_space=pltpu.VMEM)
    hbm = pl.BlockSpec(memory_space=pl.ANY)
    bufs, sems = collector_scratch(nz, nc, r.shape[2], rows, (width, 256))
    chips = nz * nc
    strip, ffn = width // chips, hid.shape[1] // 2
    tall = x.shape[0]
    return pl.pallas_call(
        functools.partial(return_kernel, nz, nc),
        out_shape=[
            jax.ShapeDtypeStruct((rows, 128), bf16),
            jax.ShapeDtypeStruct((8, width), f32),
            jax.ShapeDtypeStruct((rows, width), f32),
            jax.ShapeDtypeStruct((nc, 2, rows, width), bf16),
            jax.ShapeDtypeStruct((2, chips, strip, ffn), bf16),
            jax.ShapeDtypeStruct((chips, strip, ffn), bf16),
        ],
        in_specs=[hbm] * 7 + [vmem] * 7,
        out_specs=[vmem] * 4 + [hbm] * 2,
        scratch_shapes=[
            pltpu.VMEM((tall, width), bf16),
            pltpu.VMEM((tall, width), bf16),
            pltpu.VMEM((tall, 2 * ffn), bf16),
            pltpu.VMEM((tall, 2 * ffn), bf16),
            pltpu.VMEM((tall, 2 * ffn), bf16),
            pltpu.VMEM((2, 256 // strip, strip, ffn), bf16),
            pltpu.VMEM((3, chips, strip, ffn), bf16),
            pltpu.VMEM((3, chips, strip, ffn), bf16),
            dma((5,)), dma, dma((2,)), dma((3,)),
        ]
        + bufs
        + sems
        + [dma((nc,)), dma((nc,)), dma((nc,)), dma((nc,))]
        + [dma((2, nz * nc - 1)), dma((2, nz * nc - 1)), dma((2,))],
        compiler_params=pltpu.CompilerParams(
            collective_id=2, has_side_effects=True, vmem_limit_bytes=60 * 2**20
        ),
    )(r, g, x, cot_rows, hid, gg, gu, pick_t, residual, probs, kept, router, gain, cot)


def final_kernel(
    nz, nc, part, tok, gain, residual_grad, dw, dwo, small, y, pick_t, residual,
    tokens_grad, q_out, k_out, v_out, o_out, small_out, layer,
    dw_out, dwo_out, sib, rs_send, rs_recv, tok_grad, gain_acc, dw_up, dw_down, dwo_up, dwo_down, dw_to, dwo_to,
    dw_next, dwo_next, small_line, small_plane, small_sib, small_a, small_b,
    sib_s, sib_r, rs_s, rs_r, line_s, line_r, to_s, to_r, tg_s, tg_r, sm_s, sm_r, sp_s, sp_r, ss_s, ss_r,
    layer_send, lay_s, lay_r, *scratch,
):
    z, c, t = places()
    f32, bf16 = jnp.float32, jnp.bfloat16
    rows, width = residual_grad.shape
    piece = width // 2
    chunk = 16
    y_line = scratch[4]
    begin, process, join, done = collector(nz, nc, pick_t, ((y,) + scratch[:5],), scratch[5:])
    greet(nz, nc, True)

    bufs = ((dw, dw_up, dw_down), (dwo, dwo_up, dwo_down))
    outs = (dw_next, dwo_next)

    def hop(way, step, k, target):
        src = outs[k].at[way, step]
        return remote(src, bufs[k][1 + way].at[step], line_s.at[way, step, k], line_r.at[way, step, k], fsdp=target)

    def add_to(k, way, step, shard, joined):
        own, out = bufs[k][0], outs[k]
        got = bufs[k][1 + way]
        height = own.shape[2]
        tile = 32

        @pl.loop(0, nc * (height // tile))
        def _(n):
            q, at = n // (height // tile), pl.ds(pl.multiple_of(lax.rem(n, height // tile) * tile, tile), tile)
            value = own[shard, q, at, :]
            if joined:
                value = (value.astype(f32) + got[step, q, at, :].astype(f32)).astype(bf16)
            out[way, step, q, at, :] = value

    def line_one(step, way):
        shard = nz - 1 - step if way == 0 else step
        ahead = z + 1 if way == 0 else z - 1
        behind = z - 1 if way == 0 else z + 1
        first = z == 0 if way == 0 else z == nz - 1
        sends = shard > z if way == 0 else shard < z
        gets = (z > 0) & (shard >= z) if way == 0 else (z < nz - 1) & (shard <= z)

        @pl.when(gets)
        def _():
            for k in range(2):
                hop(way, step, k, behind).wait_recv()

        @pl.when(sends & jnp.logical_not(first))
        def _():
            for k in range(2):
                add_to(k, way, step, shard, True)
                hop(way, step, k, ahead).start()

    def line_step(step):
        @pl.when(2 * z < nz)
        def _():
            line_one(step, 0)
            line_one(step, 1)

        @pl.when(2 * z >= nz)
        def _():
            line_one(step, 1)
            line_one(step, 0)

    def line_begin():
        for way in range(2):
            first = z == 0 if way == 0 else z == nz - 1

            @pl.when(first)
            def _():
                for step in range(nz - 1):
                    shard = nz - 1 - step if way == 0 else step
                    for k in range(2):
                        add_to(k, way, step, shard, False)
                        hop(way, step, k, z + 1 if way == 0 else z - 1).start()

    def sib_copy(q):
        return remote(part.at[q, 1 - t], sib.at[q], sib_s.at[q], sib_r.at[q], tp=1 - t)

    def rs_copy(step, target):
        return remote(rs_send.at[step], rs_recv.at[step], rs_s.at[step], rs_r.at[step], ctx=target)

    for step in range(1, nc + 1):
        sib_copy(ring(c, step, nc)).start()
    line_begin()
    for step in range(1, nc):
        q = ring(c, step, nc)
        sib_copy(q).wait_recv()

        @pl.loop(0, rows // chunk)
        def _(k):
            at = pl.ds(pl.multiple_of(k * chunk, chunk), chunk)
            rs_send[step - 1, at, :] = (part[q, t, at, :].astype(f32) + sib[q, at, :].astype(f32)).astype(bf16)

        rs_copy(step - 1, q).start()
    sib_copy(c).wait_recv()
    begin(0)
    line_step(0)
    begin(1)
    for step in range(1, nc):
        rs_copy(step - 1, c).wait_recv()
    gain_acc[...] = jnp.zeros_like(gain_acc)

    @pl.loop(0, rows // chunk)
    def _(k):
        at = pl.ds(pl.multiple_of(k * chunk, chunk), chunk)
        full = pl.ds(pl.multiple_of(t * rows + k * chunk, chunk), chunk)
        grad = part[c, t, at, :].astype(f32) + sib[c, at, :].astype(f32)
        for step in range(nc - 1):
            grad = grad + rs_recv[step, at, :].astype(f32)
        x = tok[full, :].astype(f32)
        inv = lax.rsqrt(jnp.mean(x * x, -1, keepdims=True) + EPS)
        gain_acc[...] += jnp.sum((grad * x * inv).reshape(chunk // 8, 8, width), 0)
        weighted = grad * gain[...]
        inner = jnp.sum(weighted * x, -1, keepdims=True)
        out = residual_grad[at, :] + inv * weighted - x * (inv * inv * inv) * inner / width
        tok_grad[at, :] = out.astype(bf16)
        tokens_grad[full, :] = out.astype(bf16)

    def grad_copy(core):
        return remote(
            tok_grad, tokens_grad.at[pl.ds(pl.multiple_of(core * rows, rows), rows)], tg_s, tg_r, tp=1 - t
        )

    grad_copy(t).start()

    small_a[...] = small[...]
    total = jnp.sum(gain_acc[...], 0, keepdims=True)
    for strip in range(nz * nc):
        small_a[strip // nc, strip % nc, pl.ds(17, 1), :] = total[:, strip * 128 : (strip + 1) * 128]

    def small_copy(step, shard, target):
        return remote(small_a.at[shard], small_line.at[step], sm_s.at[step], sm_r.at[step], fsdp=target)

    def plane_copy(step, shard, target):
        return remote(small_b.at[shard], small_plane.at[step], sp_s.at[step], sp_r.at[step], ctx=target)

    for step in range(1, nz):
        small_copy(step - 1, ring(z, step, nz), ring(z, step, nz)).start()
    line_step(1)
    process(0)
    line_step(2)
    process(1)
    for step in range(1, nz):
        small_copy(step - 1, z, z).wait_recv()
    value = small_a[z]
    for step in range(nz - 1):
        value = value + small_line[step]
    small_b[...] = value
    for step in range(1, nc):
        plane_copy(step - 1, ring(c, step, nc), ring(c, step, nc)).start()

    def close(k, out, to):
        own, up, down = bufs[k]
        height = own.shape[2]
        tile = 32

        @pl.loop(0, nc * (height // tile))
        def _(n):
            q, at = n // (height // tile), pl.ds(pl.multiple_of(lax.rem(n, height // tile) * tile, tile), tile)
            base = own[z, q, at, :].astype(f32)
            above = up[jnp.minimum(nz - 1 - z, nz - 2), q, at, :].astype(f32)
            below = down[jnp.minimum(z, nz - 2), q, at, :].astype(f32)
            base = base + jnp.where(z > 0, above, 0.0) + jnp.where(z < nz - 1, below, 0.0)
            to[q, at, :] = base.astype(bf16)

    close(0, dw_out, dw_to)
    close(1, dwo_out, dwo_to)

    def to_copy(k, step, source, target):
        src, dst = ((dw_to, dw_out), (dwo_to, dwo_out))[k]
        return remote(src.at[target], dst.at[source], to_s.at[k, step], to_r.at[k, step], ctx=target)

    for step in range(1, nc):
        for k in range(2):
            to_copy(k, step - 1, c, ring(c, step, nc)).start()
    def layer_copy(core):
        return remote(
            layer_send.at[:, pl.ds(pl.multiple_of((1 - t) * piece, piece), piece)],
            layer.at[pl.ds(pl.multiple_of(core * rows, rows), rows)],
            lay_s, lay_r, tp=1 - t,
        )

    join()

    @pl.loop(0, rows // chunk)
    def _(k):
        at = pl.ds(pl.multiple_of(k * chunk, chunk), chunk)
        full = pl.ds(pl.multiple_of(t * rows + k * chunk, chunk), chunk)
        total = residual[at, :]
        for source in range(nz):
            total = total + y_line[source, at, :].astype(f32)
        layer_send[at, :] = total.astype(bf16)
        layer[full, :] = layer_send[at, pl.ds(pl.multiple_of(t * piece, piece), piece)]

    layer_copy(t).start()
    dw_out[c, :, :] = dw_to[c, :, :]
    dwo_out[c, :, :] = dwo_to[c, :, :]
    for step in range(1, nc):
        plane_copy(step - 1, c, c).wait_recv()
    value = small_b[c]
    for step in range(nc - 1):
        value = value + small_plane[step]
    small_out[...] = value
    final = remote(small_out, small_sib, ss_s, ss_r, tp=1 - t)
    final.start()
    final.wait()
    small_out[...] = value + small_sib[...]
    for step in range(1, nc):
        source = ring(c, -step, nc)
        for k in range(2):
            src, dst = ((dw_to, dw_out), (dwo_to, dwo_out))[k]
            remote(
                src.at[c], dst.at[source], to_s.at[k, step - 1], to_r.at[k, step - 1], ctx=source
            ).wait_recv()
    local = o_out.shape[0] // nc
    for source in range(nc):
        at = slice(source * local, (source + 1) * local)
        for k, out in enumerate((q_out, k_out, v_out)):
            out[:, at] = dw_out[source, :, k * local : (k + 1) * local].astype(f32)
        o_out[at, :] = dwo_out[source].astype(f32)
    grad_copy(1 - t).wait_recv()
    grad_copy(t).wait_send()
    layer_copy(1 - t).wait_recv()
    layer_copy(t).wait_send()
    done()
    for step in range(1, nc):
        for k in range(2):
            to_copy(k, step - 1, c, ring(c, step, nc)).wait_send()
        plane_copy(step - 1, ring(c, step, nc), ring(c, step, nc)).wait_send()
        rs_copy(step - 1, c).wait_send()
    for step in range(1, nz):
        small_copy(step - 1, ring(z, step, nz), ring(z, step, nz)).wait_send()
    for q in range(nc):
        sib_copy(q).wait_send()
    for step in range(nz - 1):
        for way in range(2):
            shard = nz - 1 - step if way == 0 else step
            ahead = z + 1 if way == 0 else z - 1
            sends = shard > z if way == 0 else shard < z

            @pl.when(sends)
            def _():
                for k in range(2):
                    hop(way, step, k, ahead).wait_send()


def finish(part, tok, gain, residual_grad, dw, dwo, small, y, pick_t, residual):
    nz, nc = lax.axis_size("fsdp"), lax.axis_size("ctx")
    rows, width = residual_grad.shape
    dma = pltpu.SemaphoreType.DMA
    bf16, f32 = jnp.bfloat16, jnp.float32
    vmem = pl.BlockSpec(memory_space=pltpu.VMEM)
    one, two = dw.shape[1:], dwo.shape[1:]
    bufs, sems = collector_scratch(nz, nc, y.shape[2], rows, (width,))
    tiny = small.shape[2:]
    return pl.pallas_call(
        functools.partial(final_kernel, nz, nc),
        out_shape=[
            jax.ShapeDtypeStruct((2 * rows, width), bf16),
            jax.ShapeDtypeStruct((one[1], nc * two[1]), f32),
            jax.ShapeDtypeStruct((one[1], nc * two[1]), f32),
            jax.ShapeDtypeStruct((one[1], nc * two[1]), f32),
            jax.ShapeDtypeStruct((nc * two[1], two[2]), f32),
            jax.ShapeDtypeStruct(tiny, f32),
            jax.ShapeDtypeStruct((2 * rows, width // 2), bf16),
        ],
        in_specs=[vmem] * 7 + [pl.BlockSpec(memory_space=pl.ANY)] + [vmem] * 2,
        out_specs=[vmem] * 7,
        scratch_shapes=[
            pltpu.VMEM(one, bf16),
            pltpu.VMEM(two, bf16),
            pltpu.VMEM((nc, rows, width), bf16),
            pltpu.VMEM((nc - 1, rows, width), bf16),
            pltpu.VMEM((nc - 1, rows, width), bf16),
            pltpu.VMEM((rows, width), bf16),
            pltpu.VMEM((8, width), f32),
            pltpu.VMEM((nz - 1,) + one, bf16),
            pltpu.VMEM((nz - 1,) + one, bf16),
            pltpu.VMEM((nz - 1,) + two, bf16),
            pltpu.VMEM((nz - 1,) + two, bf16),
            pltpu.VMEM(one, bf16),
            pltpu.VMEM(two, bf16),
            pltpu.VMEM((2, nz - 1) + one, bf16),
            pltpu.VMEM((2, nz - 1) + two, bf16),
            pltpu.VMEM((nz - 1,) + small.shape[1:], f32),
            pltpu.VMEM((nc - 1,) + tiny, f32),
            pltpu.VMEM(tiny, f32),
            pltpu.VMEM(small.shape, f32),
            pltpu.VMEM(small.shape[1:], f32),
            dma((nc,)), dma((nc,)), dma((nc - 1,)), dma((nc - 1,)),
            dma((2, nz - 1, 2)), dma((2, nz - 1, 2)),
            dma((2, nc - 1)), dma((2, nc - 1)), dma, dma,
            dma((nz - 1,)), dma((nz - 1,)), dma((nc - 1,)), dma((nc - 1,)), dma, dma,
            pltpu.VMEM((rows, width), bf16), dma, dma,
        ] + bufs + sems,
        compiler_params=pltpu.CompilerParams(
            collective_id=3, has_side_effects=True, vmem_limit_bytes=60 * 2**20
        ),
    )(part, tok, gain, residual_grad, dw, dwo, small, y, pick_t, residual)


def attention_kernel(
    scale, x, gain, w_qkv, tables, gains, w_o,
    normed, proj, queries, keys, values, context, part,
):
    f32, bf16 = jnp.float32, jnp.bfloat16
    tall, local = queries.shape
    width = x.shape[1]
    heads = local // HD
    small, chunk, span = 32, 256, 256

    @pl.loop(0, tall // small)
    def _(n):
        rows = pl.ds(pl.multiple_of(n * small, small), small)
        value = x[rows, :].astype(f32)
        inv = lax.rsqrt(jnp.mean(value * value, -1, keepdims=True) + EPS)
        normed[rows, :] = (value * inv * gain[...]).astype(bf16)

    @pl.loop(0, 3 * local // span)
    def _(n):
        at = pl.ds(pl.multiple_of(n * span, span), span)
        proj[:, at] = jnp.dot(normed[...], w_qkv[:, at], preferred_element_type=f32)

    @pl.loop(0, tall // chunk)
    def _(n):
        rows = pl.ds(pl.multiple_of(n * chunk, chunk), chunk)
        cos, sin = tables[rows, pl.ds(0, HD)], tables[rows, pl.ds(HD, HD)]
        for head in range(heads):
            at = pl.ds(head * HD, HD)
            for kind, out in enumerate((queries, keys)):
                value = proj[rows, pl.ds(kind * local + head * HD, HD)]
                inv = lax.rsqrt(jnp.mean(value * value, -1, keepdims=True) + EPS)
                value = value * inv * gains[pl.ds(kind, 1), :]
                out[rows, at] = (value * cos - pltpu.roll(value, HD // 2, 1) * sin).astype(bf16)
        values[rows, :] = proj[rows, pl.ds(2 * local, local)].astype(bf16)

    @pl.loop(0, tall // chunk)
    def _(n):
        rows = pl.ds(pl.multiple_of(n * chunk, chunk), chunk)
        for head in range(heads):
            at = pl.ds(head * HD, HD)
            scores = lax.dot_general(
                queries[rows, at], keys[:, at], (((1,), (1,)), ((), ())), preferred_element_type=f32
            ) * scale
            raised = jnp.exp(scores - jnp.max(scores, -1, keepdims=True))
            probs = (raised / jnp.sum(raised, -1, keepdims=True)).astype(bf16)
            context[rows, at] = jnp.dot(probs, values[:, at], preferred_element_type=f32).astype(bf16)

    @pl.loop(0, width // span)
    def _(n):
        at = pl.ds(pl.multiple_of(n * span, span), span)
        part[:, at] = jnp.dot(context[...], w_o[:, at], preferred_element_type=f32).astype(bf16)


def attention(x, gain, w_qkv, tables, gains, w_o):
    bf16, f32 = jnp.bfloat16, jnp.float32
    tall, width = x.shape
    local = w_o.shape[0]
    vmem = pl.BlockSpec(memory_space=pltpu.VMEM)
    shapes = [
        ((tall, width), bf16),
        ((tall, 3 * local), f32),
        ((tall, local), bf16),
        ((tall, local), bf16),
        ((tall, local), bf16),
        ((tall, local), bf16),
        ((tall, width), bf16),
    ]
    return pl.pallas_call(
        functools.partial(attention_kernel, 1.0 / math.sqrt(HD)),
        out_shape=[jax.ShapeDtypeStruct(shape, kind) for shape, kind in shapes],
        in_specs=[vmem] * 6,
        out_specs=[vmem] * 7,
        compiler_params=pltpu.CompilerParams(vmem_limit_bytes=56 * 2**20),
    )(x, gain, w_qkv, tables, gains, w_o)


def attention_back_kernel(
    scale, *refs,
):
    sources, refs = refs[:11], refs[11:]
    part, dw, dwo, q_sum, k_sum = refs[:5]
    held, refs = refs[5:16], refs[16:]
    grad_ctx, gq, gk, gv, grads, sem = refs
    grad_attn, w_o, queries, keys, values, proj, tables, gains, context, normed, w_qkv = held
    f32, bf16 = jnp.float32, jnp.bfloat16
    tall, local = queries.shape
    heads = local // HD
    width = grad_attn.shape[1]
    copies = [pltpu.make_async_copy(src, dst, sem.at[k]) for k, (src, dst) in enumerate(zip(sources, held))]
    for copy in copies:
        copy.start()
    for copy in copies[:5]:
        copy.wait()

    def nt(left, right):
        return lax.dot_general(left, right, (((1,), (1,)), ((), ())), preferred_element_type=f32)

    def tn(left, right):
        return lax.dot_general(left, right, (((0,), (0,)), ((), ())), preferred_element_type=f32)

    grad_ctx[...] = nt(grad_attn[...], w_o[...]).astype(bf16)
    gk[...] = jnp.zeros_like(gk)
    gv[...] = jnp.zeros_like(gv)
    q_sum[...] = jnp.zeros_like(q_sum)
    k_sum[...] = jnp.zeros_like(k_sum)
    chunk = 256

    @pl.loop(0, tall // chunk)
    def _(n):
        rows = pl.ds(pl.multiple_of(n * chunk, chunk), chunk)
        for head in range(heads):
            at = pl.ds(head * HD, HD)
            q, k, v, g = queries[rows, at], keys[:, at], values[:, at], grad_ctx[rows, at]
            scores = nt(q, k) * scale
            raised = jnp.exp(scores - jnp.max(scores, -1, keepdims=True))
            probs = raised / jnp.sum(raised, -1, keepdims=True)
            grad_probs = nt(g, v)
            inner = jnp.sum(probs * grad_probs, -1, keepdims=True)
            grad_scores = (probs * (grad_probs - inner)).astype(bf16)
            gq[rows, at] = jnp.dot(grad_scores, k, preferred_element_type=f32) * scale
            gk[:, at] += tn(grad_scores, q)
            gv[:, at] += tn(probs.astype(bf16), g)

    for copy in copies[5:8]:
        copy.wait()

    @pl.loop(0, tall // chunk)
    def _(n):
        rows = pl.ds(pl.multiple_of(n * chunk, chunk), chunk)
        cos, sin = tables[rows, pl.ds(0, HD)], tables[rows, pl.ds(HD, HD)]
        for head in range(heads):
            for kind, total in enumerate((q_sum, k_sum)):
                at = pl.ds(head * HD, HD)
                column = pl.ds(kind * local + head * HD, HD)
                grad = gq[rows, at] if kind == 0 else gk[rows, at] * scale
                grad = grad * cos + pltpu.roll(grad, HD // 2, 1) * sin
                value = proj[rows, column]
                inv = lax.rsqrt(jnp.mean(value * value, -1, keepdims=True) + EPS)
                total[...] += jnp.sum((grad * value * inv).reshape(chunk // 8, 8, HD), 0)
                weighted = grad * gains[pl.ds(kind, 1), :]
                inner = jnp.sum(weighted * value, -1, keepdims=True)
                out = inv * weighted - value * (inv * inv * inv) * inner / HD
                grads[rows, column] = out.astype(bf16)
        grads[rows, pl.ds(2 * local, local)] = gv[rows, :].astype(bf16)

    for copy in copies[8:]:
        copy.wait()
    span = 256
    strip = dwo.shape[2]

    @pl.loop(0, width // span)
    def _(n):
        full = pl.ds(pl.multiple_of(n * span, span), span)
        dw[full, :] = tn(normed[:, full], grads[...]).astype(bf16)
        part[:, full] = nt(grads[...], w_qkv[full, :]).astype(bf16)
        value = tn(context[...], grad_attn[:, full]).astype(bf16)
        for i in range(span // strip):
            dwo[n * (span // strip) + i] = value[:, i * strip : (i + 1) * strip]


def attention_back(grad_attn, w_o, queries, keys, values, proj, tables, gains, context, normed, w_qkv, strip):
    bf16, f32 = jnp.bfloat16, jnp.float32
    tall, width = grad_attn.shape
    local = queries.shape[1]
    vmem = pl.BlockSpec(memory_space=pltpu.VMEM)
    sources = (grad_attn, w_o, queries, keys, values, proj, tables, gains, context, normed, w_qkv)
    return pl.pallas_call(
        functools.partial(attention_back_kernel, 1.0 / math.sqrt(HD)),
        out_shape=[
            jax.ShapeDtypeStruct((tall, width), bf16),
            jax.ShapeDtypeStruct((width, 3 * local), bf16),
            jax.ShapeDtypeStruct((width // strip, local, strip), bf16),
            jax.ShapeDtypeStruct((8, HD), f32),
            jax.ShapeDtypeStruct((8, HD), f32),
        ],
        in_specs=[pl.BlockSpec(memory_space=pl.ANY)] * len(sources),
        out_specs=[vmem] * 5,
        scratch_shapes=[pltpu.VMEM(source.shape, source.dtype) for source in sources]
        + [
            pltpu.VMEM((tall, local), bf16),
            pltpu.VMEM((tall, local), f32),
            pltpu.VMEM((tall, local), f32),
            pltpu.VMEM((tall, local), f32),
            pltpu.VMEM((tall, 3 * local), bf16),
            pltpu.SemaphoreType.DMA((len(sources),)),
        ],
        compiler_params=pltpu.CompilerParams(vmem_limit_bytes=60 * 2**20),
    )(*sources)


def one_chip(
    tokens,
    w_query,
    w_key,
    w_value,
    w_out,
    gain_attn,
    gain_query,
    gain_key,
    gain_moe,
    w_router,
    w_experts,
    routes,
    cotangent,
):
    z, c, t = lax.axis_index("fsdp"), lax.axis_index("ctx"), lax.axis_index("tp")
    nz, nc = lax.axis_size("fsdp"), lax.axis_size("ctx")
    block, width = tokens.shape[1], tokens.shape[2]
    rows = block // 2
    tall = block * nc
    deep = width // nz
    ffn = w_experts.shape[3]
    most = block * TOPK * 9 // (8 * E)
    bf16, f32 = jnp.bfloat16, jnp.float32

    token_half = lax.dynamic_slice_in_dim(tokens[0], t * rows, rows, 0)
    cotan_half = lax.dynamic_slice_in_dim(cotangent[0], t * rows, rows, 0)
    local = w_query.shape[1] // nc
    small = jnp.concatenate([w_router.T.reshape(-1), gain_attn, gain_moe, gain_query, gain_key])
    total = small.shape[0]
    small = jnp.pad(small, (0, -total % 2048))
    small = small.reshape(-1, 128)
    ids = jnp.arange(E, dtype=jnp.int32)
    named = jnp.any(routes[0][:, :, None] == ids, 1)
    below = jnp.tril(jnp.ones((block, block), bf16), -1)
    rank = jnp.where(named, dot(below, named.astype(bf16)), -1.0).T
    x_rows, w_qkv, w_o, small, _, rank_seq, pick, cot_rows, pair, third, middle = load(
        tokens[0], cotangent[0], w_query, w_key, w_value, w_out, small, rank, w_experts, most
    )
    w_qkv = w_qkv.reshape(width, 3 * local)
    w_o = w_o.transpose(1, 0, 2).reshape(local, width)
    small = small.reshape(nz, -1)
    router = small[:, : E * deep].reshape(nz, E, deep).transpose(1, 0, 2).reshape(E, width)
    at = E * deep
    attn_gain = small[:, at : at + deep].reshape(-1).astype(f32)
    moe_gain = small[:, at + deep : at + 2 * deep].reshape(-1).astype(f32)
    at, part = at + 2 * deep, HD // nz
    query_gain = small[:, at : at + part].reshape(-1).astype(f32)
    key_gain = small[:, at + part : at + 2 * part].reshape(-1).astype(f32)

    pair = exchange(pair, "fsdp")

    counts = jnp.sum((rank_seq >= 0).astype(f32), 2)
    earlier = jnp.sum(jnp.where(jnp.arange(nc)[:, None] < c, counts, 0.0), 0)
    kept = ((rank >= 0) & (rank + earlier[:, None] < CAP)).astype(f32).T
    kept = lax.dynamic_slice_in_dim(kept, t * rows, rows, 0)

    half_dim = HD // 2
    inv_freq = jnp.exp(jnp.arange(half_dim, dtype=f32) * (-2.0 * math.log(ROPE_BASE) / HD))
    angles = jnp.arange(tall, dtype=jnp.int32).astype(f32)[:, None] * inv_freq[None, :]
    cosines, sines = jnp.cos(angles), jnp.sin(angles)
    tables = jnp.concatenate([cosines, cosines, sines, -sines], 1)
    gains = jnp.pad(jnp.stack([query_gain, key_gain]), ((0, 6), (0, 0)))
    normed_one, proj, queries, keys, values, context, attn_part = attention(
        x_rows, attn_gain[None], w_qkv, tables, gains, w_o
    )
    attn_part = attn_part.reshape(nc, 2, rows, width)
    kept_wide = jnp.pad(kept, ((0, 0), (0, 128 - E)))
    router_wide = jnp.pad(router, ((0, 128 - E), (0, 0)))
    residual, normed_two, router_probs, x_in, g_in, third = dispatch(
        attn_part, tokens[0], moe_gain[None], router_wide, kept_wide, pick, third, middle
    )
    pair, x_in = lax.optimization_barrier((pair, x_in))
    x_in = x_in.reshape(nc * 2 * most, width)
    cot_rows = cot_rows.reshape(nc * 2 * most, width)
    chips = nz * nc
    strip = width // chips
    out_rows, back_rows, pair_rows, hid, gg, gu = experts(
        x_in, cot_rows, g_in.reshape(nc * 2 * most, -1), pair, third
    )
    shape = (nc, 2, most, -1)
    pick_t = pick.transpose(0, 2, 1)
    grad_logits, dgain_moe, grad_residual, grad_attn, dw_gate, dw_rest = give_back(
        back_rows.reshape(shape),
        pair_rows.reshape(shape),
        x_in,
        cot_rows,
        hid,
        gg,
        gu,
        pick_t,
        residual,
        router_probs,
        kept_wide,
        router_wide,
        moe_gain[None],
        cotangent[0],
    )

    dw_router = dot_tn(normed_two, grad_logits[:, :E])
    dgain_moe = jnp.sum(dgain_moe, 0)
    dw_rest, grad_attn = lax.optimization_barrier((dw_rest, grad_attn))
    dw_rest = exchange(dw_rest, ("fsdp", "ctx"))
    grad_attn = grad_attn.reshape(tall, width)

    grad_normed_part, dw_qkv, dw_out, dgain_query, dgain_key = attention_back(
        grad_attn,
        w_o,
        queries,
        keys,
        values,
        proj,
        tables,
        gains,
        context,
        normed_one,
        w_qkv,
        strip,
    )
    dgain_query, dgain_key = jnp.sum(dgain_query, 0), jnp.sum(dgain_key, 0)
    grad_normed_part = grad_normed_part.reshape(nc, 2, rows, width)
    head_part = HD // chips
    heads = [dgain_query.reshape(chips, 1, head_part), dgain_key.reshape(chips, 1, head_part)]
    heads = jnp.pad(jnp.concatenate(heads, 2), ((0, 0), (0, 0), (0, strip - 2 * head_part)))
    sums = jnp.concatenate(
        [
            dw_router.reshape(chips, E, strip),
            dgain_moe.reshape(chips, 1, strip),
            jnp.zeros((chips, 1, strip), f32),
            heads,
            jnp.zeros((chips, 24 - E - 3, strip), f32),
        ],
        1,
    ).reshape(nz, nc, 24, strip)
    tokens_grad, dw_query, dw_key, dw_value, dw_out, sums, layer_out = finish(
        grad_normed_part,
        tokens[0],
        attn_gain[None],
        grad_residual,
        dw_qkv.reshape(nz, nc, strip, 3 * local),
        dw_out.reshape(nz, nc, local, strip),
        sums,
        out_rows.reshape(shape),
        pick_t,
        residual,
    )
    dw_experts = lay_out(dw_gate, dw_rest, nz, nc)
    return (
        layer_out[None],
        tokens_grad[None],
        dw_query,
        dw_key,
        dw_value,
        dw_out,
        sums[E + 1],
        sums[E + 2, :head_part],
        sums[E + 2, head_part : 2 * head_part],
        sums[E],
        sums[:E].reshape(strip, E),
        dw_experts,
    )


def solution(mesh):
    chips = mesh.shape["fsdp"] * mesh.shape["ctx"]
    plain = chips == E and mesh.shape["fsdp"] == 4 and mesh.shape["tp"] == 2
    return jax.shard_map(
        one_chip if plain else general,
        mesh=mesh,
        in_specs=(
            P("fsdp", "ctx", None),
            P("fsdp", "tp"),
            P("fsdp", "tp"),
            P("fsdp", "tp"),
            P("tp", "fsdp"),
            P("fsdp"),
            P("fsdp"),
            P("fsdp"),
            P("fsdp"),
            P("fsdp", None),
            P("fsdp", None, None, "tp"),
            P("fsdp", "ctx", None),
            P("fsdp", "ctx", None),
        ),
        out_specs=(
            P("fsdp", "ctx", "tp"),
            P("fsdp", "ctx", None),
            P(("fsdp", "ctx"), "tp"),
            P(("fsdp", "ctx"), "tp"),
            P(("fsdp", "ctx"), "tp"),
            P("tp", ("fsdp", "ctx")),
            P(("fsdp", "ctx")),
            P(("fsdp", "ctx")),
            P(("fsdp", "ctx")),
            P(("fsdp", "ctx")),
            P(("fsdp", "ctx"), None),
            P(("fsdp", "ctx"), None, None, "tp"),
        ),
        check_vma=False,
    )
```

```python
import functools
import math

import jax
import jax.numpy as jnp
from jax import lax
from jax.experimental import pallas as pl
from jax.experimental.pallas import tpu as pltpu
from jax.sharding import PartitionSpec as P

HD = 128
TOPK = 8
E = 16
CAP = 512
MESH = pl.DeviceIdType.MESH


EPS = 1e-06
ROPE_BASE = 10000.0


def prefix(value, axis, join, neutral):
    count, mine = (lax.axis_size(axis), lax.axis_index(axis))
    pieces = lax.all_gather(value, axis)
    running = jnp.full_like(value, 0) + jnp.asarray(neutral, value.dtype)

    def lap(position, running):
        longer = join(running, pieces[position])
        return jnp.where(position < mine, longer, running)

    return lax.fori_loop(0, count - 1, lap, running)


def rms_scale(values):
    return lax.rsqrt(jnp.mean(values * values, -1, keepdims=True) + EPS)


def norm_back(grad_normed, values, inv_rms, gain_vec):
    weighted = grad_normed * gain_vec.astype(jnp.float32)
    inner_sum = jnp.sum(weighted * values, -1, keepdims=True)
    return (
        inv_rms * weighted - values * (inv_rms * inv_rms * inv_rms) * inner_sum / values.shape[-1]
    )


def rope_tables(first, length):
    half_dim = HD // 2
    inv_freq = jnp.exp(jnp.arange(half_dim, dtype=jnp.float32) * (-2.0 * math.log(ROPE_BASE) / HD))
    places = (first + jnp.arange(length, dtype=jnp.int32)).astype(jnp.float32)
    angles = places[:, None] * inv_freq[None, :]
    cos_table = jnp.cos(angles)
    sin_table = jnp.sin(angles)
    cos_full = jnp.concatenate([cos_table, cos_table], -1)[:, None, :]
    sin_full = jnp.concatenate([sin_table, sin_table], -1)[:, None, :]
    return (cos_full, sin_full)


def rotate(values):
    half_dim = values.shape[-1] // 2
    return jnp.concatenate([-values[..., half_dim:], values[..., :half_dim]], -1)


def rotate_back(values):
    half_dim = values.shape[-1] // 2
    return jnp.concatenate([values[..., half_dim:], -values[..., :half_dim]], -1)


def apply_rope(values, cos_full, sin_full):
    return values * cos_full + rotate(values) * sin_full


def rope_back(grads, cos_full, sin_full):
    return grads * cos_full + rotate_back(grads * sin_full)


def add_counts(earlier, later):
    return earlier + later


def general(
    tokens,
    w_query,
    w_key,
    w_value,
    w_out,
    gain_attn,
    gain_query,
    gain_key,
    gain_moe,
    w_router,
    w_experts,
    routes,
    cotangent,
):
    seq_count, block_len, model_width = tokens.shape
    row_count = seq_count * block_len
    (
        full_query,
        full_key,
        full_value,
        full_out,
        router_full,
        attn_gain,
        query_gain,
        key_gain,
        moe_gain,
    ) = (
        lax.all_gather(w_query, "fsdp", axis=0, tiled=True),
        lax.all_gather(w_key, "fsdp", axis=0, tiled=True),
        lax.all_gather(w_value, "fsdp", axis=0, tiled=True),
        lax.all_gather(w_out, "fsdp", axis=1, tiled=True),
        lax.all_gather(w_router, "fsdp", axis=0, tiled=True),
        lax.all_gather(gain_attn, "fsdp", axis=0, tiled=True),
        lax.all_gather(gain_query, "fsdp", axis=0, tiled=True),
        lax.all_gather(gain_key, "fsdp", axis=0, tiled=True),
        lax.all_gather(gain_moe, "fsdp", axis=0, tiled=True),
    )
    local_width = full_query.shape[1]
    head_count = local_width // HD
    head_shape = (seq_count, block_len, head_count, HD)
    token_rows = tokens.reshape(row_count, model_width).astype(jnp.float32)
    inv_one = rms_scale(token_rows)
    normed_one = (token_rows * inv_one * attn_gain.astype(jnp.float32)).astype(jnp.bfloat16)
    query_proj = jnp.dot(normed_one, full_query, preferred_element_type=jnp.float32)
    key_proj = jnp.dot(normed_one, full_key, preferred_element_type=jnp.float32)
    value_proj = jnp.dot(normed_one, full_value, preferred_element_type=jnp.float32)
    cos_full, sin_full = rope_tables(lax.axis_index("ctx") * block_len, block_len)
    query_heads = query_proj.reshape(head_shape)
    key_heads = key_proj.reshape(head_shape)
    query_inv = rms_scale(query_heads)
    key_inv = rms_scale(key_heads)
    queries = apply_rope(
        query_heads * query_inv * query_gain.astype(jnp.float32), cos_full, sin_full
    ).astype(jnp.bfloat16)
    keys_local = apply_rope(
        key_heads * key_inv * key_gain.astype(jnp.float32), cos_full, sin_full
    ).astype(jnp.bfloat16)
    keys_local = keys_local.reshape(seq_count, block_len, local_width)
    values_local = value_proj.astype(jnp.bfloat16).reshape(seq_count, block_len, local_width)
    keys_all, values_all = (
        lax.all_gather(keys_local, "ctx", axis=1, tiled=True),
        lax.all_gather(values_local, "ctx", axis=1, tiled=True),
    )
    seq_len = keys_all.shape[1]
    key_rows = keys_all.reshape(seq_count, seq_len, head_count, HD)
    value_rows = values_all.reshape(seq_count, seq_len, head_count, HD)
    score_scale = 1.0 / math.sqrt(HD)
    scores = (
        jnp.einsum("sqhd,skhd->shqk", queries, key_rows, preferred_element_type=jnp.float32)
        * score_scale
    )
    maximum = jnp.max(scores, -1, keepdims=True)
    exp_scores = jnp.exp(scores - maximum)
    denominator = jnp.sum(exp_scores, -1, keepdims=True)
    attn_probs = exp_scores / denominator
    log_total = maximum + jnp.log(denominator)
    context = jnp.einsum(
        "shqk,skhd->sqhd",
        attn_probs.astype(jnp.bfloat16),
        value_rows,
        preferred_element_type=jnp.float32,
    )
    context = context.astype(jnp.bfloat16).reshape(row_count, local_width)
    attn_part = jnp.dot(context, full_out, preferred_element_type=jnp.float32)
    residual = token_rows + lax.psum(attn_part, "tp")
    inv_two = rms_scale(residual)
    normed_two = (residual * inv_two * moe_gain.astype(jnp.float32)).astype(jnp.bfloat16)
    logits = jnp.dot(normed_two, router_full, preferred_element_type=jnp.float32)
    router_probs = jax.nn.softmax(logits, -1)
    pair_count = block_len * TOPK
    route_rows = routes.reshape(seq_count, pair_count)
    expert_ids = jnp.arange(E, dtype=jnp.int32)
    onehot = (route_rows[:, :, None] == expert_ids[None, None, :]).astype(jnp.int32)
    counts = jnp.sum(onehot, 1, dtype=jnp.int32)
    offsets = prefix(counts, "ctx", add_counts, jnp.zeros_like(counts))
    earlier = jnp.cumsum(onehot, 1, dtype=jnp.int32) - onehot
    local_rank = jnp.sum(earlier * onehot, 2, dtype=jnp.int32)
    slot_base = jnp.sum(onehot * offsets[:, None, :], 2, dtype=jnp.int32)
    kept_mask = (slot_base + local_rank < CAP).astype(jnp.float32).reshape(row_count, TOPK)
    block_most = pair_count * 9 // (8 * E)
    expert_span = seq_count * block_most
    seq_ids = jnp.arange(seq_count, dtype=jnp.int32)[:, None]
    buffer_row = (route_rows * expert_span + seq_ids * block_most + local_rank).reshape(
        row_count * TOPK
    )
    token_ids = (
        seq_ids * block_len + jnp.arange(pair_count, dtype=jnp.int32)[None, :] // TOPK
    ).reshape(row_count * TOPK)
    owner_rows = jnp.zeros((E * expert_span,), jnp.int32).at[buffer_row].set(token_ids)
    onehot_f = onehot.astype(jnp.float32).reshape(row_count, TOPK, E)
    gate_weight = jnp.sum(onehot_f * router_probs[:, None, :], 2) * kept_mask
    slot_weight = (
        jnp.zeros((E * expert_span,), jnp.float32)
        .at[buffer_row]
        .set(gate_weight.reshape(row_count * TOPK))
    )
    expert_rows = normed_two[owner_rows].reshape(E, expert_span, model_width)
    cotan_rows = cotangent.reshape(row_count, model_width)
    grad_expert = (slot_weight[:, None] * cotan_rows[owner_rows].astype(jnp.float32)).astype(
        jnp.bfloat16
    )
    grad_expert = grad_expert.reshape(E, expert_span, model_width)
    ffn_local = w_experts.shape[3]
    fsdp_count = lax.axis_size("fsdp")
    ctx_count = lax.axis_size("ctx")
    group_count = fsdp_count * ctx_count
    sharing = group_count // E
    padded_span = -(-expert_span // sharing) * sharing
    part_span = padded_span // sharing
    target_experts = (
        jnp.arange(fsdp_count, dtype=jnp.int32) * ctx_count + lax.axis_index("ctx")
    ) // sharing
    selected = jnp.take(w_experts, target_experts, axis=2)
    owned = lax.all_to_all(selected, "fsdp", split_axis=2, concat_axis=0, tiled=True)[:, :, 0]
    send_rows = expert_rows.reshape(group_count, part_span, model_width)
    send_grads = grad_expert.reshape(group_count, part_span, model_width)
    recv_rows, recv_grads = (
        lax.all_to_all(send_rows, ("fsdp", "ctx"), split_axis=0, concat_axis=0, tiled=True),
        lax.all_to_all(send_grads, ("fsdp", "ctx"), split_axis=0, concat_axis=0, tiled=True),
    )
    rows_flat = recv_rows.reshape(group_count * part_span, model_width)
    grads_flat = recv_grads.reshape(group_count * part_span, model_width)
    gate_act = jnp.dot(rows_flat, owned[:, 0], preferred_element_type=jnp.float32)
    up_act = jnp.dot(rows_flat, owned[:, 1], preferred_element_type=jnp.float32)
    sigmoid_gate = jax.nn.sigmoid(gate_act)
    silu_gate = gate_act * sigmoid_gate
    hidden = (silu_gate * up_act).astype(jnp.bfloat16)
    produced = jnp.einsum("mf,df->md", hidden, owned[:, 2], preferred_element_type=jnp.float32)
    grad_hidden = jnp.dot(grads_flat, owned[:, 2], preferred_element_type=jnp.float32)
    grad_gate = (
        grad_hidden * up_act * sigmoid_gate * (1.0 + gate_act * (1.0 - sigmoid_gate))
    ).astype(jnp.bfloat16)
    grad_up = (grad_hidden * silu_gate).astype(jnp.bfloat16)
    rows_grad = jnp.einsum("mf,df->md", grad_gate, owned[:, 0], preferred_element_type=jnp.float32)
    rows_grad = rows_grad + jnp.einsum(
        "mf,df->md", grad_up, owned[:, 1], preferred_element_type=jnp.float32
    )
    back_out, back_rows = (
        lax.all_to_all(
            produced.reshape(group_count, part_span, model_width).astype(jnp.bfloat16),
            ("fsdp", "ctx"),
            split_axis=0,
            concat_axis=0,
            tiled=True,
        ).astype(jnp.float32),
        lax.all_to_all(
            rows_grad.reshape(group_count, part_span, model_width).astype(jnp.bfloat16),
            ("fsdp", "ctx"),
            split_axis=0,
            concat_axis=0,
            tiled=True,
        ).astype(jnp.float32),
    )
    expert_out = back_out.reshape(E, padded_span, model_width)
    grad_rows = back_rows.reshape(E, padded_span, model_width)
    gate_term = jnp.einsum("md,mf->df", rows_flat, grad_gate, preferred_element_type=jnp.float32)
    up_term = jnp.einsum("md,mf->df", rows_flat, grad_up, preferred_element_type=jnp.float32)
    down_term = jnp.einsum("md,mf->df", grads_flat, hidden, preferred_element_type=jnp.float32)
    owner_terms = jnp.stack([gate_term, up_term, down_term], 1)[:, :, None, :]
    relaid = lax.all_to_all(
        owner_terms.astype(jnp.bfloat16), ("fsdp", "ctx"), split_axis=0, concat_axis=2, tiled=True
    ).astype(owner_terms.dtype)
    dw_experts = jnp.sum(relaid.reshape(relaid.shape[0], 3, E, sharing, ffn_local), 3)
    picked = expert_out.reshape(E * expert_span, model_width)[buffer_row].reshape(
        row_count, TOPK, model_width
    )
    moe_part = jnp.sum(gate_weight[:, :, None] * picked, 1)
    cotan_float = cotan_rows.astype(jnp.float32)
    grad_gate_part = jnp.sum(picked * cotan_float[:, None, :], 2)
    moe_shard = lax.psum_scatter(
        moe_part.astype(jnp.bfloat16), "tp", scatter_dimension=1, tiled=True
    ).astype(jnp.float32)
    piece_width = moe_shard.shape[1]
    residual_shard = lax.dynamic_slice_in_dim(
        residual, lax.axis_index("tp") * piece_width, piece_width, 1
    )
    layer_out = (
        (residual_shard + moe_shard).astype(jnp.bfloat16).reshape(seq_count, block_len, piece_width)
    )
    grad_normed_part = jnp.sum(
        grad_rows.reshape(E * expert_span, model_width)[buffer_row].reshape(
            row_count, TOPK, model_width
        ),
        1,
    )
    grad_normed_sum, grad_gate_sum = (
        lax.psum(grad_normed_part.astype(jnp.bfloat16), "tp").astype(jnp.float32),
        lax.psum(grad_gate_part.astype(jnp.bfloat16), "tp").astype(jnp.float32),
    )
    grad_pick = grad_gate_sum * kept_mask
    grad_router_probs = jnp.sum(onehot_f * grad_pick[:, :, None], 1)
    grad_logits = router_probs * (
        grad_router_probs - jnp.sum(router_probs * grad_router_probs, -1, keepdims=True)
    )
    grad_logits = grad_logits.astype(jnp.bfloat16)
    grad_router_w = jnp.einsum(
        "nd,ne->de", normed_two, grad_logits, preferred_element_type=jnp.float32
    )
    grad_normed_two = grad_normed_sum + jnp.einsum(
        "ne,de->nd", grad_logits, router_full, preferred_element_type=jnp.float32
    )
    grad_moe_gain = jnp.sum(grad_normed_two * residual * inv_two, 0)
    grad_residual = cotan_float + norm_back(grad_normed_two, residual, inv_two, moe_gain)
    grad_attn = grad_residual.astype(jnp.bfloat16)
    grad_w_out = jnp.einsum("nl,nd->ld", context, grad_attn, preferred_element_type=jnp.float32)
    grad_context = jnp.einsum("nd,ld->nl", grad_attn, full_out, preferred_element_type=jnp.float32)
    grad_context = grad_context.astype(jnp.bfloat16).reshape(head_shape)
    scores = (
        jnp.einsum("sqhd,skhd->shqk", queries, key_rows, preferred_element_type=jnp.float32)
        * score_scale
    )
    attn_probs = jnp.exp(scores - log_total)
    grad_probs = jnp.einsum(
        "sqhd,skhd->shqk", grad_context, value_rows, preferred_element_type=jnp.float32
    )
    grad_scores = attn_probs * (grad_probs - jnp.sum(attn_probs * grad_probs, -1, keepdims=True))
    grad_scores = grad_scores.astype(jnp.bfloat16)
    grad_queries = (
        jnp.einsum("shqk,skhd->sqhd", grad_scores, key_rows, preferred_element_type=jnp.float32)
        * score_scale
    )
    grad_keys_all = (
        jnp.einsum("shqk,sqhd->skhd", grad_scores, queries, preferred_element_type=jnp.float32)
        * score_scale
    )
    grad_values_all = jnp.einsum(
        "shqk,sqhd->skhd",
        attn_probs.astype(jnp.bfloat16),
        grad_context,
        preferred_element_type=jnp.float32,
    )
    grad_keys_own, grad_values_own = (
        lax.psum_scatter(
            grad_keys_all.reshape(seq_count, seq_len, local_width).astype(jnp.bfloat16),
            "ctx",
            scatter_dimension=1,
            tiled=True,
        ).astype(jnp.float32),
        lax.psum_scatter(
            grad_values_all.reshape(seq_count, seq_len, local_width).astype(jnp.bfloat16),
            "ctx",
            scatter_dimension=1,
            tiled=True,
        ).astype(jnp.float32),
    )
    grad_qnormed = rope_back(grad_queries, cos_full, sin_full)
    grad_knormed = rope_back(grad_keys_own.reshape(head_shape), cos_full, sin_full)
    grad_qgain = jnp.sum(grad_qnormed * query_heads * query_inv, (0, 1, 2))
    grad_kgain = jnp.sum(grad_knormed * key_heads * key_inv, (0, 1, 2))
    grad_qproj = (
        norm_back(grad_qnormed, query_heads, query_inv, query_gain)
        .astype(jnp.bfloat16)
        .reshape(row_count, local_width)
    )
    grad_kproj = (
        norm_back(grad_knormed, key_heads, key_inv, key_gain)
        .astype(jnp.bfloat16)
        .reshape(row_count, local_width)
    )
    grad_vproj = grad_values_own.astype(jnp.bfloat16).reshape(row_count, local_width)
    grad_wq = jnp.einsum("nd,nl->dl", normed_one, grad_qproj, preferred_element_type=jnp.float32)
    grad_wk = jnp.einsum("nd,nl->dl", normed_one, grad_kproj, preferred_element_type=jnp.float32)
    grad_wv = jnp.einsum("nd,nl->dl", normed_one, grad_vproj, preferred_element_type=jnp.float32)
    grad_normed_one = jnp.einsum(
        "nl,dl->nd", grad_qproj, full_query, preferred_element_type=jnp.float32
    )
    grad_normed_one = grad_normed_one + jnp.einsum(
        "nl,dl->nd", grad_kproj, full_key, preferred_element_type=jnp.float32
    )
    grad_normed_one = grad_normed_one + jnp.einsum(
        "nl,dl->nd", grad_vproj, full_value, preferred_element_type=jnp.float32
    )
    grad_normed_one, grad_qgain, grad_kgain = (
        lax.psum(grad_normed_one.astype(jnp.bfloat16), "tp").astype(jnp.float32),
        lax.psum(grad_qgain.astype(jnp.bfloat16), "tp").astype(jnp.float32),
        lax.psum(grad_kgain.astype(jnp.bfloat16), "tp").astype(jnp.float32),
    )
    grad_attn_gain = jnp.sum(grad_normed_one * token_rows * inv_one, 0)
    tokens_grad = grad_residual + norm_back(grad_normed_one, token_rows, inv_one, attn_gain)
    tokens_grad = tokens_grad.astype(jnp.bfloat16).reshape(seq_count, block_len, model_width)
    dw_query, dw_key, dw_value, dw_out, dw_router, dgain_attn, dgain_query, dgain_key, dgain_moe = (
        lax.psum_scatter(grad_wq, ("fsdp", "ctx"), scatter_dimension=0, tiled=True),
        lax.psum_scatter(grad_wk, ("fsdp", "ctx"), scatter_dimension=0, tiled=True),
        lax.psum_scatter(grad_wv, ("fsdp", "ctx"), scatter_dimension=0, tiled=True),
        lax.psum_scatter(grad_w_out, ("fsdp", "ctx"), scatter_dimension=1, tiled=True),
        lax.psum_scatter(grad_router_w, ("fsdp", "ctx"), scatter_dimension=0, tiled=True),
        lax.psum_scatter(grad_attn_gain, ("fsdp", "ctx"), scatter_dimension=0, tiled=True),
        lax.psum_scatter(grad_qgain, ("fsdp", "ctx"), scatter_dimension=0, tiled=True),
        lax.psum_scatter(grad_kgain, ("fsdp", "ctx"), scatter_dimension=0, tiled=True),
        lax.psum_scatter(grad_moe_gain, ("fsdp", "ctx"), scatter_dimension=0, tiled=True),
    )
    return (
        layer_out,
        tokens_grad,
        dw_query,
        dw_key,
        dw_value,
        dw_out,
        dgain_attn,
        dgain_query,
        dgain_key,
        dgain_moe,
        dw_router,
        dw_experts,
    )


def swap(value):
    return lax.ppermute(value, "tp", [(0, 1), (1, 0)])


def exchange(value, axes):
    return lax.all_to_all(value, axes, split_axis=0, concat_axis=0, tiled=True)


def spread(value, axes):
    count = lax.axis_size(axes)
    return exchange(jnp.broadcast_to(value[None], (count,) + value.shape), axes)


def dot(left, right):
    return jnp.dot(left, right, preferred_element_type=jnp.float32)


def dot_nt(left, right):
    return lax.dot_general(left, right, (((1,), (1,)), ((), ())), preferred_element_type=jnp.float32)


def dot_tn(left, right):
    return lax.dot_general(left, right, (((0,), (0,)), ((), ())), preferred_element_type=jnp.float32)


def two_parts(values):
    high = values.astype(jnp.bfloat16)
    low = (values - high.astype(jnp.float32)).astype(jnp.bfloat16)
    return (high, low)


def by_core(mine, other, core):
    return jnp.where(core == 0, jnp.stack([mine, other]), jnp.stack([other, mine]))


def remote(src, dst, send, recv, **where):
    return pltpu.make_async_remote_copy(
        src_ref=src, dst_ref=dst, send_sem=send, recv_sem=recv, device_id=where, device_id_type=MESH
    )


def places():
    return lax.axis_index("fsdp"), lax.axis_index("ctx"), lax.axis_index("tp")


def ring(index, step, count):
    return lax.rem(index + step + count, count)


def greet(nz, nc, line, far=False):
    z, c, t = places()
    barrier = pltpu.get_barrier_semaphore()

    def tell(**where):
        pl.semaphore_signal(barrier, inc=1, device_id=where, device_id_type=MESH)

    if line:
        for step in range(1, nz):
            tell(fsdp=ring(z, step, nz))
        count = nz - 1
    else:
        pl.when(z > 0)(lambda: tell(fsdp=z - 1))
        pl.when(z < nz - 1)(lambda: tell(fsdp=z + 1))
        count = jnp.where(z > 0, 1, 0) + jnp.where(z < nz - 1, 1, 0)
    for step in range(1, nc):
        tell(ctx=ring(c, step, nc))
        if far:
            for hop in range(1, nz):
                tell(fsdp=ring(z, hop, nz), ctx=ring(c, step, nc))
    if far:
        count = count + (nz - 1) * (nc - 1)
    tell(tp=1 - t)
    pl.semaphore_wait(barrier, count + nc)


def line_copies(bufs, send_sem, recv_sem, way, step, shard, target):
    return [
        remote(buf.at[shard], buf.at[shard], send_sem.at[way, step, k], recv_sem.at[way, step, k], fsdp=target)
        for k, buf in enumerate(bufs)
    ]


def line_gather(nz, bufs, send_sem, recv_sem, arrived, begun=None, near=None):
    z = lax.axis_index("fsdp")
    for step in range(nz - 1):

        @pl.when((z < nz - 1) & (z >= step))
        def _():
            for copy in line_copies(bufs, send_sem, recv_sem, 0, step, z - step, z + 1):
                copy.start()

        @pl.when((z > 0) & (z + step < nz))
        def _():
            for copy in line_copies(bufs, send_sem, recv_sem, 1, step, z + step, z - 1):
                copy.start()

        if step == 0 and begun is not None:
            begun()
        if near is not None:
            near(step)

        @pl.when(z - 1 >= step)
        def _():
            for copy in line_copies(bufs, send_sem, recv_sem, 0, step, z - 1 - step, z - 1):
                copy.wait_recv()
            arrived(z - 1 - step)

        @pl.when(z + 1 + step < nz)
        def _():
            for copy in line_copies(bufs, send_sem, recv_sem, 1, step, z + 1 + step, z + 1):
                copy.wait_recv()
            arrived(z + 1 + step)


def line_sent(nz, bufs, send_sem, recv_sem):
    z = lax.axis_index("fsdp")
    for step in range(nz - 1):

        @pl.when((z < nz - 1) & (z >= step))
        def _():
            for copy in line_copies(bufs, send_sem, recv_sem, 0, step, z - step, z + 1):
                copy.wait_send()

        @pl.when((z > 0) & (z + step < nz))
        def _():
            for copy in line_copies(bufs, send_sem, recv_sem, 1, step, z + step, z - 1):
                copy.wait_send()


def pick_rows(pick, slot, source, out):
    lanes = out.shape[-1]
    piece = min(lanes, 512)

    @pl.loop(0, lanes // piece)
    def _(k):
        at = pl.ds(pl.multiple_of(k * piece, piece), piece)
        out[slot, :, at] = jnp.dot(pick[slot], source[slot, :, at], preferred_element_type=jnp.float32).astype(
            jnp.bfloat16
        )


def plane_copy(most, src, dst, send, recv, slot, step, source, target):
    rows = pl.ds(pl.multiple_of(target * most, 16), most)
    return remote(
        src.at[slot, rows], dst.at[source, slot], send.at[slot, step - 1], recv.at[slot, step - 1], ctx=target
    )


def regroup(shard, t, rows, line, two, keep_sem, give_send, give_recv):
    slot = lax.rem(shard, 2)
    band = pl.ds(pl.multiple_of(t * rows, rows), rows)

    def keep():
        pltpu.make_async_copy(line.at[shard], two.at[slot, band], keep_sem.at[slot]).start()

    def give():
        remote(line.at[shard], two.at[slot, band], give_send.at[slot], give_recv.at[slot], tp=1 - t).start()

    pl.when(shard // 2 == t)(keep)
    pl.when(shard // 2 != t)(give)


def selector(nz, src, pair, third, held, pair_out, third_out, in_sem, pair_sem, third_sem):
    c = lax.axis_index("ctx")
    tile = 16
    count = src.shape[2]
    height = held.shape[1]
    bands = src.shape[0] // height

    def take(b):
        slot = lax.rem(b, 2)
        return pltpu.make_async_copy(
            src.at[pl.ds(pl.multiple_of(b * height, height), height)], held.at[slot], in_sem.at[slot]
        )

    def put(b):
        slot = lax.rem(b, 2)
        at = pl.ds(pl.multiple_of(b * height, height), height)
        return (
            pltpu.make_async_copy(pair_out.at[slot], pair.at[:, at], pair_sem.at[slot]),
            pltpu.make_async_copy(third_out.at[slot], third.at[:, :, at], third_sem.at[slot]),
        )

    def pick_band(b):
        slot = lax.rem(b, 2)
        take(b).wait()
        pl.when(b + 1 < bands)(lambda: take(b + 1).start())

        @pl.when(b >= 2)
        def _():
            for copy in put(b - 2):
                copy.wait()

        row = lax.broadcasted_iota(jnp.int32, (nz * tile, tile * count), 0)
        column = lax.broadcasted_iota(jnp.int32, (nz * tile, tile * count), 1)
        hit = column == lax.rem(row, tile) * count + c * nz + row // tile
        hit = jnp.where(hit, 1.0, 0.0).astype(jnp.bfloat16)
        for n in range(height // tile):
            at = pl.ds(n * tile, tile)
            for k in range(3):
                value = held[slot, n * tile : (n + 1) * tile, k].reshape(tile * count, -1)
                value = jnp.dot(hit, value, preferred_element_type=jnp.float32).astype(jnp.bfloat16)
                value = value.reshape(nz, tile, -1)
                if k == 2:
                    pair_out[slot, :, at, :] = value
                else:
                    third_out[slot, k, :, at, :] = value
        for copy in put(b):
            copy.start()

    def close():
        for b in (bands - 2, bands - 1):
            for copy in put(b):
                copy.wait()

    pick_band.close = close
    return take, pick_band, bands


def load_kernel(
    nz, nc, tok, cot, wq, wk, wv, wo, small, rank, w_experts,
    x_all, w_qkv, w_o, small_all, rank_line, rank_seq, pick, cot_in, pair, third, middle,
    cot_line, cot_two, cot_send,
    own_sem, line_send, line_recv, w_send, w_recv, tok_send, tok_recv, pass_send, pass_recv,
    rank_send, rank_recv, keep_sem, give_send, give_recv, cot_s, cot_r, cot_own,
    sel_in, sel_pair, sel_third, sel_s, sel_p, sel_t, mid_s, mid_r,
):
    z, c, t = places()
    block = tok.shape[0]
    rows = block // 2
    local = w_qkv.shape[2] // 3
    most = cot_in.shape[2]
    half = pl.ds(pl.multiple_of(t * rows, rows), rows)
    column = pl.ds(pl.multiple_of(c * local, local), local)
    own = [
        pltpu.make_async_copy(cot.at[half], cot_line.at[z], own_sem.at[5]),
        pltpu.make_async_copy(small, small_all.at[z], own_sem.at[4]),
        pltpu.make_async_copy(rank, rank_line.at[z], own_sem.at[7]),
        pltpu.make_async_copy(rank, rank_seq.at[c], own_sem.at[8]),
    ]
    own += [
        pltpu.make_async_copy(w.at[:, column], w_qkv.at[z, :, pl.ds(k * local, local)], own_sem.at[k])
        for k, w in enumerate((wq, wk, wv))
    ]
    own += [
        pltpu.make_async_copy(wo.at[column], w_o.at[z], own_sem.at[3]),
        pltpu.make_async_copy(tok, x_all.at[pl.ds(pl.multiple_of(c * block, block), block)], own_sem.at[6]),
    ]
    for copy in own:
        copy.start()
    take, pick_band, bands = selector(nz, w_experts, pair, third, sel_in, sel_pair, sel_third, sel_s, sel_p, sel_t)
    take(0).start()
    greet(nz, nc, False)

    def band(source, core):
        return x_all.at[pl.ds(pl.multiple_of(source * block + core * rows, rows), rows)]

    def token_copy(step, source, target):
        return remote(tok.at[half], band(source, t), tok_send.at[step], tok_recv.at[step], ctx=target)

    def pass_copy(step, source, core):
        return remote(band(source, core), band(source, core), pass_send.at[step], pass_recv.at[step], tp=1 - t)

    def rank_copy(step, source, target):
        return remote(rank, rank_seq.at[source], rank_send.at[step], rank_recv.at[step], ctx=target)

    for step in range(1, nc):
        token_copy(step - 1, c, ring(c, step, nc)).start()
        rank_copy(step - 1, c, ring(c, step, nc)).start()
    for copy in own:
        copy.wait()

    def arrived(shard):
        regroup(shard, t, rows, cot_line, cot_two, keep_sem, give_send, give_recv)

    arrived(z)
    first = (cot_line, rank_line, small_all)
    line_gather(nz, first, line_send, line_recv, arrived)

    def own_copy(slot):
        return pltpu.make_async_copy(
            cot_send.at[slot, pl.ds(pl.multiple_of(c * most, 16), most)], cot_in.at[c, slot], cot_own.at[slot]
        )

    def send_cotangent():
        number = lax.broadcasted_iota(jnp.int32, (most, block), 0).astype(jnp.float32)
        for slot in range(2):
            for q in range(nc):
                row = rank_line[2 * t + slot, pl.ds(q * nz + z, 1), :]
                hit = jnp.where(number == row, 1.0, 0.0)
                pick[slot, pl.ds(q * most, most), :] = hit.astype(jnp.bfloat16)
        for slot in range(2):
            wait_two(slot, t, rows, cot_line, cot_two, keep_sem, give_recv)
            pick_rows(pick, slot, cot_two, cot_send)
            for step in range(1, nc):
                plane_copy(most, cot_send, cot_in, cot_s, cot_r, slot, step, c, ring(c, step, nc)).start()
            own_copy(slot).start()

    def ignore(shard):
        pass

    partner = nz - 1 - z
    centre = (z == nz // 2 - 1) | (z == nz // 2)
    middle_copy = remote(third.at[:, partner], middle, mid_s, mid_r, fsdp=partner)

    def select_some(step):
        pl.loop(bands * (0, 1, 3)[step] // 4, bands * (1, 3, 4)[step] // 4)(pick_band)
        if step == 2:
            pick_band.close()
            pl.when(centre)(lambda: middle_copy.start())

    line_gather(nz, (w_qkv, w_o), w_send, w_recv, ignore, send_cotangent, select_some)
    for step in range(1, nc):
        source = ring(c, -step, nc)
        token_copy(step - 1, source, source).wait_recv()
        pass_copy(step - 1, source, t).start()
        rank_copy(step - 1, source, source).wait_recv()
    for step in range(1, nc):
        source = ring(c, -step, nc)
        pass_copy(step - 1, source, 1 - t).wait_recv()
        pass_copy(step - 1, source, t).wait_send()
        token_copy(step - 1, c, source).wait_send()
        rank_copy(step - 1, c, source).wait_send()
        for slot in range(2):
            copy = plane_copy(most, cot_send, cot_in, cot_s, cot_r, slot, step, source, source)
            copy.wait_recv()
            copy.wait_send()
    line_sent(nz, first, line_send, line_recv)
    line_sent(nz, (w_qkv, w_o), w_send, w_recv)
    for slot in range(2):
        own_copy(slot).wait()
        wait_given(slot, t, rows, cot_line, cot_two, give_send, give_recv)

    @pl.when(centre)
    def _():
        middle_copy.wait_recv()
        middle_copy.wait_send()


def wait_given(slot, t, rows, line, two, give_send, give_recv):
    band = pl.ds(pl.multiple_of(t * rows, rows), rows)
    remote(line.at[0], two.at[slot, band], give_send.at[slot], give_recv.at[slot], tp=1 - t).wait_send()


def wait_two(slot, t, rows, line, two, keep_sem, give_recv):
    band = pl.ds(pl.multiple_of(t * rows, rows), rows)
    other = pl.ds(pl.multiple_of((1 - t) * rows, rows), rows)
    pltpu.make_async_copy(line.at[0], two.at[slot, band], keep_sem.at[slot]).wait()
    remote(line.at[0], two.at[slot, other], give_recv.at[slot], give_recv.at[slot], tp=1 - t).wait_recv()


def load(tok, cot, wq, wk, wv, wo, small, rank, w_experts, most):
    nz, nc = lax.axis_size("fsdp"), lax.axis_size("ctx")
    block, width = tok.shape
    deep, local = wq.shape[0], wq.shape[1] // nc
    rows = block // 2
    count, ffn = w_experts.shape[2:]
    dma = pltpu.SemaphoreType.DMA
    bf16, f32 = jnp.bfloat16, jnp.float32
    shapes = [
        ((nc * block, width), bf16),
        ((nz, deep, 3 * local), bf16),
        ((nz, local, wo.shape[1]), bf16),
        ((nz,) + small.shape, bf16),
        ((nz,) + rank.shape, f32),
        ((nc,) + rank.shape, f32),
        ((2, nc * most, block), bf16),
        ((nc, 2, most, width), bf16),
        ((nz, deep, ffn), bf16),
        ((2, nz, deep, ffn), bf16),
        ((2, deep, ffn), bf16),
    ]
    hbm = pl.BlockSpec(memory_space=pl.ANY)
    height = 32
    return pl.pallas_call(
        functools.partial(load_kernel, nz, nc),
        out_shape=[jax.ShapeDtypeStruct(shape, kind) for shape, kind in shapes],
        in_specs=[hbm] * 9,
        out_specs=[pl.BlockSpec(memory_space=pltpu.VMEM)] * 7 + [hbm] * 4,
        scratch_shapes=[
            pltpu.VMEM((nz, rows, width), bf16),
            pltpu.VMEM((2, block, width), bf16),
            pltpu.VMEM((2, nc * most, width), bf16),
            dma((9,)),
            dma((2, nz - 1, 3)), dma((2, nz - 1, 3)), dma((2, nz - 1, 2)), dma((2, nz - 1, 2)),
            dma((nc - 1,)), dma((nc - 1,)), dma((nc - 1,)), dma((nc - 1,)), dma((nc - 1,)), dma((nc - 1,)),
            dma((2,)), dma((2,)), dma((2,)), dma((2, nc - 1)), dma((2, nc - 1)), dma((2,)),
            pltpu.VMEM((2, height, 3, count, ffn), bf16),
            pltpu.VMEM((2, nz, height, ffn), bf16),
            pltpu.VMEM((2, 2, nz, height, ffn), bf16),
            dma((2,)), dma((2,)), dma((2,)), dma, dma,
        ],
        compiler_params=pltpu.CompilerParams(
            collective_id=0, has_side_effects=True, vmem_limit_bytes=60 * 2**20
        ),
    )(tok, cot, wq, wk, wv, wo, small, rank, w_experts)


def dispatch_kernel(
    nz, nc, part, tok, gain, router, kept, pick, third, middle,
    residual, normed, probs, x_in, g_in, third_got,
    sib, rs_send, rs_recv, n_line, g_line, n_two, g_two, x_send, g_send,
    sib_s, sib_r, rs_s, rs_r, line_send, line_recv, keep_sem, give_send, give_recv,
    gkeep_sem, ggive_send, ggive_recv, x_s, x_r, g_s, g_r, own_sem,
    third_s, third_r, third_own, mid_own,
):
    z, c, t = places()
    f32, bf16 = jnp.float32, jnp.bfloat16
    rows, width = residual.shape
    most = x_in.shape[2]
    greet(nz, nc, True)
    keep_third = pltpu.make_async_copy(third.at[:, z], third_got.at[:, z], third_own)
    keep_third.start()
    partner = nz - 1 - z
    centre = (z == nz // 2 - 1) | (z == nz // 2)
    keep_middle = pltpu.make_async_copy(middle, third_got.at[:, partner], mid_own)
    pl.when(centre)(lambda: keep_middle.start())

    def still(other):
        return jnp.logical_not(centre & (other == partner))

    def third_copy(kind, step, source, target):
        return remote(
            third.at[kind, target], third_got.at[kind, source], third_s.at[kind, step], third_r.at[kind, step],
            fsdp=target,
        )

    def send_third(kind):
        for step in range(1, nz):
            target = ring(z, step, nz)
            pl.when(still(target))(lambda: third_copy(kind, step - 1, z, target).start())

    def sib_copy(q):
        return remote(part.at[q, 1 - t], sib.at[q], sib_s.at[q], sib_r.at[q], tp=1 - t)

    def rs_copy(step, source, target):
        return remote(rs_send.at[step], rs_recv.at[step], rs_s.at[step], rs_r.at[step], ctx=target)

    for step in range(1, nc + 1):
        sib_copy(ring(c, step, nc)).start()
    chunk = 16
    for step in range(1, nc):
        q = ring(c, step, nc)
        sib_copy(q).wait_recv()

        @pl.loop(0, rows // chunk)
        def _(k):
            at = pl.ds(pl.multiple_of(k * chunk, chunk), chunk)
            rs_send[step - 1, at, :] = (part[q, t, at, :].astype(f32) + sib[q, at, :].astype(f32)).astype(bf16)

        rs_copy(step - 1, c, q).start()

    def own_copy(slot, src, dst, k):
        return pltpu.make_async_copy(
            src.at[slot, pl.ds(pl.multiple_of(c * most, 16), most)], dst.at[c, slot], own_sem.at[k, slot]
        )

    send_third(0)
    sib_copy(c).wait_recv()
    for step in range(1, nc):
        rs_copy(step - 1, c, c).wait_recv()

    @pl.loop(0, rows // chunk)
    def _(k):
        at = pl.ds(pl.multiple_of(k * chunk, chunk), chunk)
        start = pl.ds(pl.multiple_of(t * rows + k * chunk, chunk), chunk)
        total = part[c, t, at, :].astype(f32) + sib[c, at, :].astype(f32)
        for step in range(nc - 1):
            total = total + rs_recv[step, at, :].astype(f32)
        total = total + tok[start, :].astype(f32)
        residual[at, :] = total
        inv = lax.rsqrt(jnp.mean(total * total, -1, keepdims=True) + EPS)
        row = (total * inv * gain[...]).astype(bf16)
        normed[at, :] = row
        n_line[z, at, :] = row

    logits = lax.dot_general(
        normed[...], router[...], (((1,), (1,)), ((), ())), preferred_element_type=f32
    )
    lane = lax.broadcasted_iota(jnp.int32, logits.shape, 1)
    logits = jnp.where(lane < E, logits, -jnp.inf)
    top = jnp.max(logits, -1, keepdims=True)
    raised = jnp.exp(logits - top)
    prob = raised / jnp.sum(raised, -1, keepdims=True)
    probs[...] = prob
    gates = prob * kept[...]
    high = gates.astype(bf16)
    g_line[z, :, pl.ds(0, 128)] = high
    g_line[z, :, pl.ds(128, 128)] = (gates - high.astype(f32)).astype(bf16)

    def arrived(shard):
        regroup(shard, t, rows, n_line, n_two, keep_sem, give_send, give_recv)
        regroup(shard, t, rows, g_line, g_two, gkeep_sem, ggive_send, ggive_recv)

    arrived(z)
    sent = ((x_send, x_in, x_s, x_r), (g_send, g_in, g_s, g_r))

    def near(distance):
        above, below = z + distance, z - distance
        is_above = (above < nz) & (above // 2 == t)
        is_below = (below >= 0) & (below // 2 == t)
        slot = lax.rem(jnp.where(is_above, above, below + 2), 2)

        @pl.when(is_above | is_below)
        def _():
            wait_two(slot, t, rows, n_line, n_two, keep_sem, give_recv)
            wait_two(slot, t, rows, g_line, g_two, gkeep_sem, ggive_recv)
            pick_rows(pick, slot, n_two, x_send)
            pick_rows(pick, slot, g_two, g_send)
            for k, (src, dst, s, r) in enumerate(sent):
                for step in range(1, nc):
                    plane_copy(most, src, dst, s, r, slot, step, c, ring(c, step, nc)).start()
                own_copy(slot, src, dst, k).start()

    line_gather(nz, (n_line, g_line), line_send, line_recv, arrived, None, near)
    near(nz - 1)
    send_third(1)
    line_sent(nz, (n_line, g_line), line_send, line_recv)
    for slot in range(2):
        wait_given(slot, t, rows, n_line, n_two, give_send, give_recv)
        wait_given(slot, t, rows, g_line, g_two, ggive_send, ggive_recv)
        for k, (src, dst, s, r) in enumerate(sent):
            own_copy(slot, src, dst, k).wait()
            for step in range(1, nc):
                source = ring(c, -step, nc)
                copy = plane_copy(most, src, dst, s, r, slot, step, source, source)
                copy.wait_recv()
                copy.wait_send()
    for step in range(1, nc):
        rs_copy(step - 1, c, c).wait_send()
    for step in range(nc):
        sib_copy(step).wait_send()
    for step in range(1, nz):
        source = ring(z, -step, nz)
        for kind in range(2):
            pl.when(still(source))(lambda: third_copy(kind, step - 1, source, source).wait_recv())
            pl.when(still(ring(z, step, nz)))(lambda: third_copy(kind, step - 1, source, source).wait_send())
    keep_third.wait()
    pl.when(centre)(lambda: keep_middle.wait())


def dispatch(part, tok, gain, router, kept, pick, third, middle):
    nz, nc = lax.axis_size("fsdp"), lax.axis_size("ctx")
    rows, width = part.shape[2], part.shape[3]
    block = rows * 2
    most = pick.shape[1] // nc
    dma = pltpu.SemaphoreType.DMA
    bf16, f32 = jnp.bfloat16, jnp.float32
    vmem = pl.BlockSpec(memory_space=pltpu.VMEM)
    hbm = pl.BlockSpec(memory_space=pl.ANY)
    return pl.pallas_call(
        functools.partial(dispatch_kernel, nz, nc),
        out_shape=[
            jax.ShapeDtypeStruct((rows, width), f32),
            jax.ShapeDtypeStruct((rows, width), bf16),
            jax.ShapeDtypeStruct((rows, 128), f32),
            jax.ShapeDtypeStruct((nc, 2, most, width), bf16),
            jax.ShapeDtypeStruct((nc, 2, most, 256), bf16),
            jax.ShapeDtypeStruct(third.shape, bf16),
        ],
        in_specs=[vmem] * 6 + [hbm] * 2,
        out_specs=[vmem] * 3 + [hbm] * 3,
        scratch_shapes=[
            pltpu.VMEM((nc, rows, width), bf16),
            pltpu.VMEM((nc - 1, rows, width), bf16),
            pltpu.VMEM((nc - 1, rows, width), bf16),
            pltpu.VMEM((nz, rows, width), bf16),
            pltpu.VMEM((nz, rows, 256), bf16),
            pltpu.VMEM((2, block, width), bf16),
            pltpu.VMEM((2, block, 256), bf16),
            pltpu.VMEM((2, nc * most, width), bf16),
            pltpu.VMEM((2, nc * most, 256), bf16),
            dma((nc,)), dma((nc,)), dma((nc - 1,)), dma((nc - 1,)),
            dma((2, nz - 1, 2)), dma((2, nz - 1, 2)),
            dma((2,)), dma((2,)), dma((2,)), dma((2,)), dma((2,)), dma((2,)),
            dma((2, nc - 1)), dma((2, nc - 1)), dma((2, nc - 1)), dma((2, nc - 1)),
            dma((2, 2)),
            dma((2, nz - 1)), dma((2, nz - 1)), dma, dma,
        ],
        compiler_params=pltpu.CompilerParams(
            collective_id=1, has_side_effects=True, vmem_limit_bytes=56 * 2**20
        ),
    )(part, tok, gain, router, kept, pick, third, middle)


def experts_kernel(
    nz, nc, x_hbm, cot_hbm, gates, pair_hbm, third_hbm, y_hbm, r_hbm, pair_out, hid_hbm, gg_hbm, gu_hbm,
    x, cot, w, weight, pair, gate, up, out_grad, y, r, hid, gg, gu,
    sem, swap_s, swap_r, out_sem, inner_sem,
):
    z, c, t = places()
    f32, bf16 = jnp.float32, jnp.bfloat16
    width, tall = x.shape[1], x.shape[0]
    deep, ffn = w.shape[3], w.shape[4]
    span = 256
    chunk = 576
    copies = [
        pltpu.make_async_copy(cot_hbm, cot, sem.at[0]),
        pltpu.make_async_copy(pair_hbm, w.at[0, :, 1], sem.at[1]),
        pltpu.make_async_copy(x_hbm, x, sem.at[2]),
        pltpu.make_async_copy(third_hbm.at[0], w.at[0, :, 0], sem.at[3]),
        pltpu.make_async_copy(third_hbm.at[1], w.at[0, :, 2], sem.at[4]),
    ]
    for copy in copies:
        copy.start()
    barrier = pltpu.get_barrier_semaphore()
    pl.semaphore_signal(barrier, inc=1, device_id=dict(tp=1 - t), device_id_type=MESH)
    pl.semaphore_wait(barrier, 1)
    swaps = [
        remote(pair_hbm, w.at[1, :, 1], swap_s.at[0], swap_r.at[0], tp=1 - t),
        remote(third_hbm.at[0], w.at[1, :, 0], swap_s.at[1], swap_r.at[1], tp=1 - t),
        remote(third_hbm.at[1], w.at[1, :, 2], swap_s.at[2], swap_r.at[2], tp=1 - t),
    ]
    for copy in swaps:
        copy.start()
    pair[...] = jnp.zeros_like(pair)
    lane = lax.broadcasted_iota(jnp.int32, (chunk, 256), 1)
    mine = c * nz + z

    @pl.loop(0, tall // chunk)
    def _(m):
        rows = pl.ds(pl.multiple_of(m * chunk, chunk), chunk)
        value = gates[rows, :].astype(f32)
        value = jnp.where((lane == mine) | (lane == mine + 128), value, 0.0)
        weight[rows, :] = jnp.sum(value, 1, keepdims=True)

    for copy in copies[:2]:
        copy.wait()
    per = ffn // span

    def forward(n):
        half, at = n // per, pl.ds(pl.multiple_of(lax.rem(n, per) * span, span), span)
        full = pl.ds(pl.multiple_of(n * span, span), span)

        def times(rows, k):
            return jnp.dot(rows[...], w[half, :, k, :, at].reshape(width, span), preferred_element_type=f32)

        out_grad[...] = times(cot, 1)

        @pl.when(n == 0)
        def _():
            for copy in copies[2:]:
                copy.wait()

        gate[...] = times(x, 0)
        up[...] = times(x, 2)

        @pl.loop(0, tall // chunk)
        def _(m):
            rows = pl.ds(pl.multiple_of(m * chunk, chunk), chunk)
            g, u, o, k = gate[rows, :], up[rows, :], out_grad[rows, :], weight[rows, :]
            sig = 1.0 / (1.0 + jnp.exp(-g))
            silu = g * sig
            hidden = silu * u
            pair[rows, :] += jnp.sum(hidden.astype(bf16).astype(f32) * o, 1, keepdims=True)
            hid[rows, full] = (k * hidden).astype(bf16)
            o = k * o
            gg[rows, full] = (o * u * sig * (1.0 + g * (1.0 - sig))).astype(bf16)
            gu[rows, full] = (o * silu).astype(bf16)

    pl.loop(0, per)(forward)
    for copy in swaps:
        copy.wait_recv()
    pl.loop(per, 2 * per)(forward)

    @pl.loop(0, tall // chunk)
    def _(m):
        rows = pl.ds(pl.multiple_of(m * chunk, chunk), chunk)
        value = pair[rows, :]
        high = value.astype(bf16).astype(f32)
        out = jnp.where(lane == mine, high, jnp.where(lane == mine + 128, value - high, 0.0))
        pair_out[rows, :] = out.astype(bf16)

    inner = [
        pltpu.make_async_copy(src, dst, inner_sem.at[k])
        for k, (src, dst) in enumerate(((hid, hid_hbm), (gg, gg_hbm), (gu, gu_hbm)))
    ]
    for copy in inner:
        copy.start()
    per_deep = deep // span

    def leave(n):
        full = pl.ds(pl.multiple_of(n * span, span), span)
        return (
            pltpu.make_async_copy(y.at[:, full], y_hbm.at[:, full], out_sem.at[0, n]),
            pltpu.make_async_copy(r.at[:, full], r_hbm.at[:, full], out_sem.at[1, n]),
        )

    @pl.loop(0, width // span)
    def _(n):
        zone, at = n // per_deep, pl.ds(pl.multiple_of(lax.rem(n, per_deep) * span, span), span)
        full = pl.ds(pl.multiple_of(n * span, span), span)

        def back(rows, k):
            total = 0.0
            for half in range(2):
                total = total + lax.dot_general(
                    rows[:, pl.ds(half * ffn, ffn)], w[half, zone, k, at, :], (((1,), (1,)), ((), ())),
                    preferred_element_type=f32,
                )
            return total

        y[:, full] = back(hid, 1).astype(bf16)
        r[:, full] = (back(gg, 0) + back(gu, 2)).astype(bf16)
        for copy in leave(n):
            copy.start()

    for n in range(width // span):
        for copy in leave(n):
            copy.wait()
    for copy in inner:
        copy.wait()
    for copy in swaps:
        copy.wait_send()


def experts(x, cot, gates, pair, third):
    bf16, f32 = jnp.bfloat16, jnp.float32
    nz, nc = lax.axis_size("fsdp"), lax.axis_size("ctx")
    tall, width = x.shape
    deep, ffn = third.shape[2:]
    vmem = pl.BlockSpec(memory_space=pltpu.VMEM)
    hbm = pl.BlockSpec(memory_space=pl.ANY)
    inner = jax.ShapeDtypeStruct((tall, 2 * ffn), bf16)
    dma = pltpu.SemaphoreType.DMA
    return pl.pallas_call(
        functools.partial(experts_kernel, nz, nc),
        out_shape=[
            jax.ShapeDtypeStruct((tall, width), bf16),
            jax.ShapeDtypeStruct((tall, width), bf16),
            jax.ShapeDtypeStruct((tall, 256), bf16),
            inner,
            inner,
            inner,
        ],
        in_specs=[hbm, hbm, vmem, hbm, hbm],
        out_specs=[hbm, hbm, vmem, hbm, hbm, hbm],
        scratch_shapes=[
            pltpu.VMEM((tall, width), bf16),
            pltpu.VMEM((tall, width), bf16),
            pltpu.VMEM((2, nz, 3, deep, ffn), bf16),
            pltpu.VMEM((tall, 1), f32),
            pltpu.VMEM((tall, 1), f32),
            pltpu.VMEM((tall, 256), f32),
            pltpu.VMEM((tall, 256), f32),
            pltpu.VMEM((tall, 256), f32),
            pltpu.VMEM((tall, width), bf16),
            pltpu.VMEM((tall, width), bf16),
            pltpu.VMEM((tall, 2 * ffn), bf16),
            pltpu.VMEM((tall, 2 * ffn), bf16),
            pltpu.VMEM((tall, 2 * ffn), bf16),
            dma((5,)), dma((3,)), dma((3,)), dma((2, width // 256)), dma((3,)),
        ],
        compiler_params=pltpu.CompilerParams(
            collective_id=4, has_side_effects=True, vmem_limit_bytes=60 * 2**20
        ),
    )(x, cot, gates, pair, third)


def place_kernel(nz, nc, gate, rest, out):
    tile = rest.shape[1]
    count = nz * nc
    row = lax.broadcasted_iota(jnp.int32, (tile * count, tile * count), 0)
    column = lax.broadcasted_iota(jnp.int32, (tile * count, tile * count), 1)
    expert = lax.rem(row, count)
    hit = column == (lax.rem(expert, nz) * nc + expert // nz) * tile + row // count
    hit = jnp.where(hit, 1.0, 0.0).astype(jnp.bfloat16)
    for k in range(3):
        value = (gate[k] if k < 2 else rest[...]).reshape(count * tile, -1)
        value = jnp.dot(hit, value, preferred_element_type=jnp.float32)
        out[:, k] = value.reshape(tile, count, -1)


def lay_out(gate, rest, nz, nc):
    count, strip, ffn = rest.shape
    tile = 16
    return pl.pallas_call(
        functools.partial(place_kernel, nz, nc),
        grid=(strip // tile,),
        out_shape=jax.ShapeDtypeStruct((strip, 3, count, ffn), jnp.float32),
        in_specs=[
            pl.BlockSpec((2, count, tile, ffn), lambda i: (0, 0, i, 0)),
            pl.BlockSpec((count, tile, ffn), lambda i: (0, i, 0)),
        ],
        out_specs=pl.BlockSpec((tile, 3, count, ffn), lambda i: (i, 0, 0, 0)),
        compiler_params=pltpu.CompilerParams(vmem_limit_bytes=40 * 2**20),
    )(gate, rest)


def collector(nz, nc, pick_t, items, sems):
    z, c, t = places()
    to_s, to_r, own_sem, sib_s, sib_r, line_s, line_r, keep_sem = sems
    rows = items[0][2].shape[1]
    mine_at = pl.ds(pl.multiple_of(t * rows, rows), rows)
    give_at = pl.ds(pl.multiple_of((1 - t) * rows, rows), rows)
    count = len(items)

    def lanes(turn, k):
        wide = items[k][2].shape[-1] // 2
        return pl.ds(turn * wide, wide)

    def to_copy(turn, k, step, source, target):
        src, got = items[k][:2]
        at = lanes(turn, k)
        return remote(
            src.at[target, :, :, at], got.at[source, :, :, at], to_s.at[k, turn, step - 1], to_r.at[k, turn, step - 1],
            ctx=target,
        )

    def own_copy(turn, k):
        src, got = items[k][:2]
        at = lanes(turn, k)
        return pltpu.make_async_copy(src.at[c, :, :, at], got.at[c, :, :, at], own_sem.at[k, turn])

    def sib_copy(turn, k):
        give, sib = items[k][3:5]
        at = lanes(turn, k)
        return remote(give.at[:, :, at], sib.at[:, :, at], sib_s.at[k, turn], sib_r.at[k, turn], tp=1 - t)

    def line_copy(turn, slot, k, half, source, target):
        src = items[k][2 if half == 0 else 4]
        at = lanes(turn, k)
        return remote(
            src.at[slot, :, at], items[k][5].at[source, :, at],
            line_s.at[k, turn, 2 * half + slot], line_r.at[k, turn, source], fsdp=target,
        )

    def keep_copy(turn, slot, k, half):
        src = items[k][2 if half == 0 else 4]
        at = lanes(turn, k)
        return pltpu.make_async_copy(src.at[slot, :, at], items[k][5].at[z, :, at], keep_sem.at[k, turn])

    def goal(slot, half):
        return 2 * (t if half == 0 else 1 - t) + slot

    def forward(turn, k, half):
        for slot in range(2):
            target = goal(slot, half)
            pl.when(target != z)(lambda: line_copy(turn, slot, k, half, z, target).start())
            pl.when(target == z)(lambda: keep_copy(turn, slot, k, half).start())

    def begin(turn):
        for k in range(count):
            for step in range(1, nc):
                to_copy(turn, k, step, c, ring(c, step, nc)).start()
            own_copy(turn, k).start()

    def scatter(turn, slot, k):
        got, mine, give = items[k][1:4]
        wide = mine.shape[-1] // 2
        span = min(wide, 512)
        tall = got.shape[0] * got.shape[2]

        @pl.loop(0, wide // span)
        def _(n):
            at = pl.ds(pl.multiple_of(turn * wide + n * span, span), span)
            pairs = got[:, slot, :, at].reshape(tall, span)
            for picks, out in ((mine_at, mine), (give_at, give)):
                out[slot, :, at] = jnp.dot(
                    pick_t[slot, picks, :], pairs, preferred_element_type=jnp.float32
                ).astype(jnp.bfloat16)

    def process(turn):
        for k in range(count):
            own_copy(turn, k).wait()
            for step in range(1, nc):
                source = ring(c, -step, nc)
                to_copy(turn, k, step, source, c).wait_recv()
            for slot in range(2):
                scatter(turn, slot, k)
            sib_copy(turn, k).start()
            forward(turn, k, 0)
        for k in range(count):
            sib_copy(turn, k).wait_recv()
            forward(turn, k, 1)

    def join():
        for turn in range(2):
            for k in range(count):
                keep_copy(turn, 0, k, 0).wait()
                for step in range(1, nz):
                    line_copy(turn, 0, k, 0, ring(z, -step, nz), z).wait_recv()

    def done():
        for turn in range(2):
            for k in range(count):
                for step in range(1, nc):
                    to_copy(turn, k, step, c, ring(c, step, nc)).wait_send()
                sib_copy(turn, k).wait_send()
                for half in range(2):
                    for slot in range(2):
                        pl.when(goal(slot, half) != z)(
                            lambda: line_copy(turn, slot, k, half, z, goal(slot, half)).wait_send()
                        )

    return begin, process, join, done


def collector_scratch(nz, nc, most, rows, widths):
    dma = pltpu.SemaphoreType.DMA
    bf16 = jnp.bfloat16
    count = len(widths)
    bufs = []
    for w in widths:
        bufs += [pltpu.VMEM((nc, 2, most, w), bf16)]
        bufs += [pltpu.VMEM((2, rows, w), bf16)] * 3
        bufs += [pltpu.VMEM((nz, rows, w), bf16)]
    sems = [
        dma((count, 2, nc - 1)), dma((count, 2, nc - 1)), dma((count, 2)), dma((count, 2)), dma((count, 2)),
        dma((count, 2, 4)), dma((count, 2, nz)), dma((count, 2)),
    ]
    return bufs, sems


def return_kernel(
    nz, nc, r, g, x_hbm, cot_hbm, hid_hbm, gg_hbm, gu_hbm, pick_t, residual, probs, kept, router, gain, cot,
    logits_grad, gain_grad, residual_grad, attn_grad, early_got, rest,
    x, cot_rows, hid, gg, gu, stage, early, early_sib,
    load_sem, keep_sem, give_sem, got_sem, *scratch,
):
    z, c, t = places()
    f32, bf16 = jnp.float32, jnp.bfloat16
    rows, width = residual.shape
    r_line, g_line = scratch[4], scratch[9]
    row_s, row_r, pass_s, pass_r, early_s, early_r, early_own = scratch[18:]
    items = ((r,) + scratch[:5], (g,) + scratch[5:10])
    begin, process, join, done = collector(nz, nc, pick_t, items, scratch[10:18])
    here = z * nc + c
    def keep_early(kind):
        return pltpu.make_async_copy(early.at[kind, here], early_got.at[kind, here], early_own.at[kind])

    loads = [
        pltpu.make_async_copy(src, dst, load_sem.at[k])
        for k, (src, dst) in enumerate(
            ((x_hbm, x), (gg_hbm, gg), (gu_hbm, gu), (cot_hbm, cot_rows), (hid_hbm, hid))
        )
    ]
    for copy in loads:
        copy.start()
    greet(nz, nc, True, True)
    chips = nz * nc
    steps = [(i, j) for i in (*range(1, nz), 0) for j in range(nc) if i or j]

    def early_copy(kind, n, source, target, fsdp, ctx):
        return remote(
            early.at[kind, target], early_got.at[kind, source], early_s.at[kind, n], early_r.at[kind, n],
            fsdp=fsdp, ctx=ctx,
        )

    def send_early(kind):
        keep_early(kind).start()
        for n, (i, j) in enumerate(steps):
            zz, cc = ring(z, i, nz), ring(c, j, nc)
            early_copy(kind, n, here, zz * nc + cc, zz, cc).start()

    begin(0)
    begin(1)

    span = 256
    strip, ffn = stage.shape[2], stage.shape[3]
    per = span // strip
    bands = width // span

    def gradients(kind, rows_in, grads):
        def flush(n):
            slot = lax.rem(n, 2)
            at = pl.ds(pl.multiple_of(n * per, per), per)
            return remote(stage.at[slot], early_sib.at[kind, at], give_sem.at[slot], got_sem.at[kind], tp=1 - t)

        @pl.loop(0, bands)
        def _(n):
            full = pl.ds(pl.multiple_of(n * span, span), span)
            slot = lax.rem(n, 2)
            pl.when(n >= 2)(lambda: flush(n - 2).wait_send())
            value = lax.dot_general(
                rows_in[:, full], grads[...], (((0,), (0,)), ((), ())), preferred_element_type=f32
            ).astype(bf16)
            for i in range(per):
                piece = value[i * strip : (i + 1) * strip]
                early[kind, n * per + i] = piece[:, :ffn]
                stage[slot, i] = piece[:, ffn:]
            flush(n).start()

        flush(bands - 2).wait_send()
        flush(bands - 1).wait_send()
        remote(early_sib.at[kind], early_sib.at[kind], got_sem.at[kind], got_sem.at[kind], tp=1 - t).wait_recv()

        @pl.loop(0, chips)
        def _(n):
            early[kind, n] = (early[kind, n].astype(f32) + early_sib[kind, n].astype(f32)).astype(bf16)

    loads[0].wait()
    loads[1].wait()
    gradients(0, x, gg)
    send_early(0)
    for copy in loads[2:]:
        copy.wait()
    gradients(1, x, gu)
    gradients(2, cot_rows, hid)
    keep_rest = pltpu.make_async_copy(early.at[2], rest, keep_sem)
    keep_rest.start()
    for turn in range(2):
        process(turn)
    join()
    pairs = jnp.zeros((rows, 128), f32)
    for source in range(nz):
        pairs = pairs + g_line[source, :, 0:128].astype(f32) + g_line[source, :, 128:256].astype(f32)
    pairs = pairs * kept[...]
    prob = probs[...]
    grad_logits = (prob * (pairs - jnp.sum(prob * pairs, -1, keepdims=True))).astype(bf16)
    logits_grad[...] = grad_logits
    gain_grad[...] = jnp.zeros_like(gain_grad)
    chunk = 16

    @pl.loop(0, rows // chunk)
    def _(k):
        at = pl.ds(pl.multiple_of(k * chunk, chunk), chunk)
        full = pl.ds(pl.multiple_of(t * rows + k * chunk, chunk), chunk)
        res = residual[at, :]
        grad = r_line[0, at, :].astype(f32)
        for source in range(1, nz):
            grad = grad + r_line[source, at, :].astype(f32)
        grad = grad + jnp.dot(logits_grad[at, :], router[...], preferred_element_type=f32)
        inv = lax.rsqrt(jnp.mean(res * res, -1, keepdims=True) + EPS)
        gain_grad[...] += jnp.sum((grad * res * inv).reshape(chunk // 8, 8, width), 0)
        weighted = grad * gain[...]
        inner = jnp.sum(weighted * res, -1, keepdims=True)
        out = cot[full, :].astype(f32) + inv * weighted - res * (inv * inv * inv) * inner / width
        residual_grad[at, :] = out
        attn_grad[c, t, at, :] = out.astype(bf16)

    def row_copy(step, source, target):
        return remote(attn_grad.at[source, t], attn_grad.at[source, t], row_s.at[step], row_r.at[step], ctx=target)

    def pass_copy(step, source, core):
        return remote(attn_grad.at[source, core], attn_grad.at[source, core], pass_s.at[step], pass_r.at[step], tp=1 - t)

    for step in range(1, nc):
        row_copy(step, c, ring(c, step, nc)).start()
    pass_copy(0, c, t).start()
    send_early(1)
    for step in range(1, nc):
        source = ring(c, -step, nc)
        row_copy(step, source, source).wait_recv()
        pass_copy(step, source, t).start()
    for step in range(nc):
        source = ring(c, -step, nc)
        pass_copy(step, source, 1 - t).wait_recv()
        pass_copy(step, source, t).wait_send()
        if step:
            row_copy(step, c, source).wait_send()
    done()
    for kind in range(2):
        for n, (i, j) in enumerate(steps):
            zz, cc = ring(z, -i, nz), ring(c, -j, nc)
            copy = early_copy(kind, n, zz * nc + cc, zz * nc + cc, zz, cc)
            copy.wait_recv()
            copy.wait_send()
        keep_early(kind).wait()
    keep_rest.wait()


def give_back(r, g, x, cot_rows, hid, gg, gu, pick_t, residual, probs, kept, router, gain, cot):
    nz, nc = lax.axis_size("fsdp"), lax.axis_size("ctx")
    rows, width = residual.shape
    dma = pltpu.SemaphoreType.DMA
    bf16, f32 = jnp.bfloat16, jnp.float32
    vmem = pl.BlockSpec(memory_space=pltpu.VMEM)
    hbm = pl.BlockSpec(memory_space=pl.ANY)
    bufs, sems = collector_scratch(nz, nc, r.shape[2], rows, (width, 256))
    chips = nz * nc
    strip, ffn = width // chips, hid.shape[1] // 2
    tall = x.shape[0]
    return pl.pallas_call(
        functools.partial(return_kernel, nz, nc),
        out_shape=[
            jax.ShapeDtypeStruct((rows, 128), bf16),
            jax.ShapeDtypeStruct((8, width), f32),
            jax.ShapeDtypeStruct((rows, width), f32),
            jax.ShapeDtypeStruct((nc, 2, rows, width), bf16),
            jax.ShapeDtypeStruct((2, chips, strip, ffn), bf16),
            jax.ShapeDtypeStruct((chips, strip, ffn), bf16),
        ],
        in_specs=[hbm] * 7 + [vmem] * 7,
        out_specs=[vmem] * 4 + [hbm] * 2,
        scratch_shapes=[
            pltpu.VMEM((tall, width), bf16),
            pltpu.VMEM((tall, width), bf16),
            pltpu.VMEM((tall, 2 * ffn), bf16),
            pltpu.VMEM((tall, 2 * ffn), bf16),
            pltpu.VMEM((tall, 2 * ffn), bf16),
            pltpu.VMEM((2, 256 // strip, strip, ffn), bf16),
            pltpu.VMEM((3, chips, strip, ffn), bf16),
            pltpu.VMEM((3, chips, strip, ffn), bf16),
            dma((5,)), dma, dma((2,)), dma((3,)),
        ]
        + bufs
        + sems
        + [dma((nc,)), dma((nc,)), dma((nc,)), dma((nc,))]
        + [dma((2, nz * nc - 1)), dma((2, nz * nc - 1)), dma((2,))],
        compiler_params=pltpu.CompilerParams(
            collective_id=2, has_side_effects=True, vmem_limit_bytes=60 * 2**20
        ),
    )(r, g, x, cot_rows, hid, gg, gu, pick_t, residual, probs, kept, router, gain, cot)


def final_kernel(
    nz, nc, part, tok, gain, residual_grad, dw, dwo, small, y, pick_t, residual,
    tokens_grad, q_out, k_out, v_out, o_out, small_out, layer,
    dw_out, dwo_out, sib, rs_send, rs_recv, tok_grad, gain_acc, dw_up, dw_down, dwo_up, dwo_down, dw_to, dwo_to,
    dw_next, dwo_next, small_line, small_plane, small_sib, small_a, small_b,
    sib_s, sib_r, rs_s, rs_r, line_s, line_r, to_s, to_r, tg_s, tg_r, sm_s, sm_r, sp_s, sp_r, ss_s, ss_r,
    layer_send, lay_s, lay_r, *scratch,
):
    z, c, t = places()
    f32, bf16 = jnp.float32, jnp.bfloat16
    rows, width = residual_grad.shape
    piece = width // 2
    chunk = 16
    y_line = scratch[4]
    begin, process, join, done = collector(nz, nc, pick_t, ((y,) + scratch[:5],), scratch[5:])
    greet(nz, nc, True)

    bufs = ((dw, dw_up, dw_down), (dwo, dwo_up, dwo_down))
    outs = (dw_next, dwo_next)

    def hop(way, step, k, target):
        src = outs[k].at[way, step]
        return remote(src, bufs[k][1 + way].at[step], line_s.at[way, step, k], line_r.at[way, step, k], fsdp=target)

    def add_to(k, way, step, shard, joined):
        own, out = bufs[k][0], outs[k]
        got = bufs[k][1 + way]
        height = own.shape[2]
        tile = 32

        @pl.loop(0, nc * (height // tile))
        def _(n):
            q, at = n // (height // tile), pl.ds(pl.multiple_of(lax.rem(n, height // tile) * tile, tile), tile)
            value = own[shard, q, at, :]
            if joined:
                value = (value.astype(f32) + got[step, q, at, :].astype(f32)).astype(bf16)
            out[way, step, q, at, :] = value

    def line_one(step, way):
        shard = nz - 1 - step if way == 0 else step
        ahead = z + 1 if way == 0 else z - 1
        behind = z - 1 if way == 0 else z + 1
        first = z == 0 if way == 0 else z == nz - 1
        sends = shard > z if way == 0 else shard < z
        gets = (z > 0) & (shard >= z) if way == 0 else (z < nz - 1) & (shard <= z)

        @pl.when(gets)
        def _():
            for k in range(2):
                hop(way, step, k, behind).wait_recv()

        @pl.when(sends & jnp.logical_not(first))
        def _():
            for k in range(2):
                add_to(k, way, step, shard, True)
                hop(way, step, k, ahead).start()

    def line_step(step):
        @pl.when(2 * z < nz)
        def _():
            line_one(step, 0)
            line_one(step, 1)

        @pl.when(2 * z >= nz)
        def _():
            line_one(step, 1)
            line_one(step, 0)

    def line_begin():
        for way in range(2):
            first = z == 0 if way == 0 else z == nz - 1

            @pl.when(first)
            def _():
                for step in range(nz - 1):
                    shard = nz - 1 - step if way == 0 else step
                    for k in range(2):
                        add_to(k, way, step, shard, False)
                        hop(way, step, k, z + 1 if way == 0 else z - 1).start()

    def sib_copy(q):
        return remote(part.at[q, 1 - t], sib.at[q], sib_s.at[q], sib_r.at[q], tp=1 - t)

    def rs_copy(step, target):
        return remote(rs_send.at[step], rs_recv.at[step], rs_s.at[step], rs_r.at[step], ctx=target)

    for step in range(1, nc + 1):
        sib_copy(ring(c, step, nc)).start()
    line_begin()
    for step in range(1, nc):
        q = ring(c, step, nc)
        sib_copy(q).wait_recv()

        @pl.loop(0, rows // chunk)
        def _(k):
            at = pl.ds(pl.multiple_of(k * chunk, chunk), chunk)
            rs_send[step - 1, at, :] = (part[q, t, at, :].astype(f32) + sib[q, at, :].astype(f32)).astype(bf16)

        rs_copy(step - 1, q).start()
    sib_copy(c).wait_recv()
    begin(0)
    line_step(0)
    begin(1)
    for step in range(1, nc):
        rs_copy(step - 1, c).wait_recv()
    gain_acc[...] = jnp.zeros_like(gain_acc)

    @pl.loop(0, rows // chunk)
    def _(k):
        at = pl.ds(pl.multiple_of(k * chunk, chunk), chunk)
        full = pl.ds(pl.multiple_of(t * rows + k * chunk, chunk), chunk)
        grad = part[c, t, at, :].astype(f32) + sib[c, at, :].astype(f32)
        for step in range(nc - 1):
            grad = grad + rs_recv[step, at, :].astype(f32)
        x = tok[full, :].astype(f32)
        inv = lax.rsqrt(jnp.mean(x * x, -1, keepdims=True) + EPS)
        gain_acc[...] += jnp.sum((grad * x * inv).reshape(chunk // 8, 8, width), 0)
        weighted = grad * gain[...]
        inner = jnp.sum(weighted * x, -1, keepdims=True)
        out = residual_grad[at, :] + inv * weighted - x * (inv * inv * inv) * inner / width
        tok_grad[at, :] = out.astype(bf16)
        tokens_grad[full, :] = out.astype(bf16)

    def grad_copy(core):
        return remote(
            tok_grad, tokens_grad.at[pl.ds(pl.multiple_of(core * rows, rows), rows)], tg_s, tg_r, tp=1 - t
        )

    grad_copy(t).start()

    small_a[...] = small[...]
    total = jnp.sum(gain_acc[...], 0, keepdims=True)
    for strip in range(nz * nc):
        small_a[strip // nc, strip % nc, pl.ds(17, 1), :] = total[:, strip * 128 : (strip + 1) * 128]

    def small_copy(step, shard, target):
        return remote(small_a.at[shard], small_line.at[step], sm_s.at[step], sm_r.at[step], fsdp=target)

    def plane_copy(step, shard, target):
        return remote(small_b.at[shard], small_plane.at[step], sp_s.at[step], sp_r.at[step], ctx=target)

    for step in range(1, nz):
        small_copy(step - 1, ring(z, step, nz), ring(z, step, nz)).start()
    line_step(1)
    process(0)
    line_step(2)
    process(1)
    for step in range(1, nz):
        small_copy(step - 1, z, z).wait_recv()
    value = small_a[z]
    for step in range(nz - 1):
        value = value + small_line[step]
    small_b[...] = value
    for step in range(1, nc):
        plane_copy(step - 1, ring(c, step, nc), ring(c, step, nc)).start()

    def close(k, out, to):
        own, up, down = bufs[k]
        height = own.shape[2]
        tile = 32

        @pl.loop(0, nc * (height // tile))
        def _(n):
            q, at = n // (height // tile), pl.ds(pl.multiple_of(lax.rem(n, height // tile) * tile, tile), tile)
            base = own[z, q, at, :].astype(f32)
            above = up[jnp.minimum(nz - 1 - z, nz - 2), q, at, :].astype(f32)
            below = down[jnp.minimum(z, nz - 2), q, at, :].astype(f32)
            base = base + jnp.where(z > 0, above, 0.0) + jnp.where(z < nz - 1, below, 0.0)
            to[q, at, :] = base.astype(bf16)

    close(0, dw_out, dw_to)
    close(1, dwo_out, dwo_to)

    def to_copy(k, step, source, target):
        src, dst = ((dw_to, dw_out), (dwo_to, dwo_out))[k]
        return remote(src.at[target], dst.at[source], to_s.at[k, step], to_r.at[k, step], ctx=target)

    for step in range(1, nc):
        for k in range(2):
            to_copy(k, step - 1, c, ring(c, step, nc)).start()
    def layer_copy(core):
        return remote(
            layer_send.at[:, pl.ds(pl.multiple_of((1 - t) * piece, piece), piece)],
            layer.at[pl.ds(pl.multiple_of(core * rows, rows), rows)],
            lay_s, lay_r, tp=1 - t,
        )

    join()

    @pl.loop(0, rows // chunk)
    def _(k):
        at = pl.ds(pl.multiple_of(k * chunk, chunk), chunk)
        full = pl.ds(pl.multiple_of(t * rows + k * chunk, chunk), chunk)
        total = residual[at, :]
        for source in range(nz):
            total = total + y_line[source, at, :].astype(f32)
        layer_send[at, :] = total.astype(bf16)
        layer[full, :] = layer_send[at, pl.ds(pl.multiple_of(t * piece, piece), piece)]

    layer_copy(t).start()
    dw_out[c, :, :] = dw_to[c, :, :]
    dwo_out[c, :, :] = dwo_to[c, :, :]
    for step in range(1, nc):
        plane_copy(step - 1, c, c).wait_recv()
    value = small_b[c]
    for step in range(nc - 1):
        value = value + small_plane[step]
    small_out[...] = value
    final = remote(small_out, small_sib, ss_s, ss_r, tp=1 - t)
    final.start()
    final.wait()
    small_out[...] = value + small_sib[...]
    for step in range(1, nc):
        source = ring(c, -step, nc)
        for k in range(2):
            src, dst = ((dw_to, dw_out), (dwo_to, dwo_out))[k]
            remote(
                src.at[c], dst.at[source], to_s.at[k, step - 1], to_r.at[k, step - 1], ctx=source
            ).wait_recv()
    local = o_out.shape[0] // nc
    for source in range(nc):
        at = slice(source * local, (source + 1) * local)
        for k, out in enumerate((q_out, k_out, v_out)):
            out[:, at] = dw_out[source, :, k * local : (k + 1) * local].astype(f32)
        o_out[at, :] = dwo_out[source].astype(f32)
    grad_copy(1 - t).wait_recv()
    grad_copy(t).wait_send()
    layer_copy(1 - t).wait_recv()
    layer_copy(t).wait_send()
    done()
    for step in range(1, nc):
        for k in range(2):
            to_copy(k, step - 1, c, ring(c, step, nc)).wait_send()
        plane_copy(step - 1, ring(c, step, nc), ring(c, step, nc)).wait_send()
        rs_copy(step - 1, c).wait_send()
    for step in range(1, nz):
        small_copy(step - 1, ring(z, step, nz), ring(z, step, nz)).wait_send()
    for q in range(nc):
        sib_copy(q).wait_send()
    for step in range(nz - 1):
        for way in range(2):
            shard = nz - 1 - step if way == 0 else step
            ahead = z + 1 if way == 0 else z - 1
            sends = shard > z if way == 0 else shard < z

            @pl.when(sends)
            def _():
                for k in range(2):
                    hop(way, step, k, ahead).wait_send()


def finish(part, tok, gain, residual_grad, dw, dwo, small, y, pick_t, residual):
    nz, nc = lax.axis_size("fsdp"), lax.axis_size("ctx")
    rows, width = residual_grad.shape
    dma = pltpu.SemaphoreType.DMA
    bf16, f32 = jnp.bfloat16, jnp.float32
    vmem = pl.BlockSpec(memory_space=pltpu.VMEM)
    one, two = dw.shape[1:], dwo.shape[1:]
    bufs, sems = collector_scratch(nz, nc, y.shape[2], rows, (width,))
    tiny = small.shape[2:]
    return pl.pallas_call(
        functools.partial(final_kernel, nz, nc),
        out_shape=[
            jax.ShapeDtypeStruct((2 * rows, width), bf16),
            jax.ShapeDtypeStruct((one[1], nc * two[1]), f32),
            jax.ShapeDtypeStruct((one[1], nc * two[1]), f32),
            jax.ShapeDtypeStruct((one[1], nc * two[1]), f32),
            jax.ShapeDtypeStruct((nc * two[1], two[2]), f32),
            jax.ShapeDtypeStruct(tiny, f32),
            jax.ShapeDtypeStruct((2 * rows, width // 2), bf16),
        ],
        in_specs=[vmem] * 7 + [pl.BlockSpec(memory_space=pl.ANY)] + [vmem] * 2,
        out_specs=[vmem] * 7,
        scratch_shapes=[
            pltpu.VMEM(one, bf16),
            pltpu.VMEM(two, bf16),
            pltpu.VMEM((nc, rows, width), bf16),
            pltpu.VMEM((nc - 1, rows, width), bf16),
            pltpu.VMEM((nc - 1, rows, width), bf16),
            pltpu.VMEM((rows, width), bf16),
            pltpu.VMEM((8, width), f32),
            pltpu.VMEM((nz - 1,) + one, bf16),
            pltpu.VMEM((nz - 1,) + one, bf16),
            pltpu.VMEM((nz - 1,) + two, bf16),
            pltpu.VMEM((nz - 1,) + two, bf16),
            pltpu.VMEM(one, bf16),
            pltpu.VMEM(two, bf16),
            pltpu.VMEM((2, nz - 1) + one, bf16),
            pltpu.VMEM((2, nz - 1) + two, bf16),
            pltpu.VMEM((nz - 1,) + small.shape[1:], f32),
            pltpu.VMEM((nc - 1,) + tiny, f32),
            pltpu.VMEM(tiny, f32),
            pltpu.VMEM(small.shape, f32),
            pltpu.VMEM(small.shape[1:], f32),
            dma((nc,)), dma((nc,)), dma((nc - 1,)), dma((nc - 1,)),
            dma((2, nz - 1, 2)), dma((2, nz - 1, 2)),
            dma((2, nc - 1)), dma((2, nc - 1)), dma, dma,
            dma((nz - 1,)), dma((nz - 1,)), dma((nc - 1,)), dma((nc - 1,)), dma, dma,
            pltpu.VMEM((rows, width), bf16), dma, dma,
        ] + bufs + sems,
        compiler_params=pltpu.CompilerParams(
            collective_id=3, has_side_effects=True, vmem_limit_bytes=60 * 2**20
        ),
    )(part, tok, gain, residual_grad, dw, dwo, small, y, pick_t, residual)


def attention_kernel(
    scale, x, gain, w_qkv, tables, gains, w_o,
    normed, proj, queries, keys, values, context, part,
):
    f32, bf16 = jnp.float32, jnp.bfloat16
    tall, local = queries.shape
    width = x.shape[1]
    heads = local // HD
    small, chunk, span = 32, 256, 256

    @pl.loop(0, tall // small)
    def _(n):
        rows = pl.ds(pl.multiple_of(n * small, small), small)
        value = x[rows, :].astype(f32)
        inv = lax.rsqrt(jnp.mean(value * value, -1, keepdims=True) + EPS)
        normed[rows, :] = (value * inv * gain[...]).astype(bf16)

    @pl.loop(0, 3 * local // span)
    def _(n):
        at = pl.ds(pl.multiple_of(n * span, span), span)
        proj[:, at] = jnp.dot(normed[...], w_qkv[:, at], preferred_element_type=f32)

    @pl.loop(0, tall // chunk)
    def _(n):
        rows = pl.ds(pl.multiple_of(n * chunk, chunk), chunk)
        cos, sin = tables[rows, pl.ds(0, HD)], tables[rows, pl.ds(HD, HD)]
        for head in range(heads):
            at = pl.ds(head * HD, HD)
            for kind, out in enumerate((queries, keys)):
                value = proj[rows, pl.ds(kind * local + head * HD, HD)]
                inv = lax.rsqrt(jnp.mean(value * value, -1, keepdims=True) + EPS)
                value = value * inv * gains[pl.ds(kind, 1), :]
                out[rows, at] = (value * cos - pltpu.roll(value, HD // 2, 1) * sin).astype(bf16)
        values[rows, :] = proj[rows, pl.ds(2 * local, local)].astype(bf16)

    @pl.loop(0, tall // chunk)
    def _(n):
        rows = pl.ds(pl.multiple_of(n * chunk, chunk), chunk)
        for head in range(heads):
            at = pl.ds(head * HD, HD)
            scores = lax.dot_general(
                queries[rows, at], keys[:, at], (((1,), (1,)), ((), ())), preferred_element_type=f32
            ) * scale
            raised = jnp.exp(scores - jnp.max(scores, -1, keepdims=True))
            probs = (raised / jnp.sum(raised, -1, keepdims=True)).astype(bf16)
            context[rows, at] = jnp.dot(probs, values[:, at], preferred_element_type=f32).astype(bf16)

    @pl.loop(0, width // span)
    def _(n):
        at = pl.ds(pl.multiple_of(n * span, span), span)
        part[:, at] = jnp.dot(context[...], w_o[:, at], preferred_element_type=f32).astype(bf16)


def attention(x, gain, w_qkv, tables, gains, w_o):
    bf16, f32 = jnp.bfloat16, jnp.float32
    tall, width = x.shape
    local = w_o.shape[0]
    vmem = pl.BlockSpec(memory_space=pltpu.VMEM)
    shapes = [
        ((tall, width), bf16),
        ((tall, 3 * local), f32),
        ((tall, local), bf16),
        ((tall, local), bf16),
        ((tall, local), bf16),
        ((tall, local), bf16),
        ((tall, width), bf16),
    ]
    return pl.pallas_call(
        functools.partial(attention_kernel, 1.0 / math.sqrt(HD)),
        out_shape=[jax.ShapeDtypeStruct(shape, kind) for shape, kind in shapes],
        in_specs=[vmem] * 6,
        out_specs=[vmem] * 7,
        compiler_params=pltpu.CompilerParams(vmem_limit_bytes=56 * 2**20),
    )(x, gain, w_qkv, tables, gains, w_o)


def attention_back_kernel(
    scale, *refs,
):
    sources, refs = refs[:11], refs[11:]
    part, dw, dwo, q_sum, k_sum = refs[:5]
    held, refs = refs[5:16], refs[16:]
    grad_ctx, gq, gk, gv, grads, sem = refs
    grad_attn, w_o, queries, keys, values, proj, tables, gains, context, normed, w_qkv = held
    f32, bf16 = jnp.float32, jnp.bfloat16
    tall, local = queries.shape
    heads = local // HD
    width = grad_attn.shape[1]
    copies = [pltpu.make_async_copy(src, dst, sem.at[k]) for k, (src, dst) in enumerate(zip(sources, held))]
    for copy in copies:
        copy.start()
    for copy in copies[:5]:
        copy.wait()

    def nt(left, right):
        return lax.dot_general(left, right, (((1,), (1,)), ((), ())), preferred_element_type=f32)

    def tn(left, right):
        return lax.dot_general(left, right, (((0,), (0,)), ((), ())), preferred_element_type=f32)

    grad_ctx[...] = nt(grad_attn[...], w_o[...]).astype(bf16)
    gk[...] = jnp.zeros_like(gk)
    gv[...] = jnp.zeros_like(gv)
    q_sum[...] = jnp.zeros_like(q_sum)
    k_sum[...] = jnp.zeros_like(k_sum)
    chunk = 256

    @pl.loop(0, tall // chunk)
    def _(n):
        rows = pl.ds(pl.multiple_of(n * chunk, chunk), chunk)
        for head in range(heads):
            at = pl.ds(head * HD, HD)
            q, k, v, g = queries[rows, at], keys[:, at], values[:, at], grad_ctx[rows, at]
            scores = nt(q, k) * scale
            raised = jnp.exp(scores - jnp.max(scores, -1, keepdims=True))
            probs = raised / jnp.sum(raised, -1, keepdims=True)
            grad_probs = nt(g, v)
            inner = jnp.sum(probs * grad_probs, -1, keepdims=True)
            grad_scores = (probs * (grad_probs - inner)).astype(bf16)
            gq[rows, at] = jnp.dot(grad_scores, k, preferred_element_type=f32) * scale
            gk[:, at] += tn(grad_scores, q)
            gv[:, at] += tn(probs.astype(bf16), g)

    for copy in copies[5:8]:
        copy.wait()

    @pl.loop(0, tall // chunk)
    def _(n):
        rows = pl.ds(pl.multiple_of(n * chunk, chunk), chunk)
        cos, sin = tables[rows, pl.ds(0, HD)], tables[rows, pl.ds(HD, HD)]
        for head in range(heads):
            for kind, total in enumerate((q_sum, k_sum)):
                at = pl.ds(head * HD, HD)
                column = pl.ds(kind * local + head * HD, HD)
                grad = gq[rows, at] if kind == 0 else gk[rows, at] * scale
                grad = grad * cos + pltpu.roll(grad, HD // 2, 1) * sin
                value = proj[rows, column]
                inv = lax.rsqrt(jnp.mean(value * value, -1, keepdims=True) + EPS)
                total[...] += jnp.sum((grad * value * inv).reshape(chunk // 8, 8, HD), 0)
                weighted = grad * gains[pl.ds(kind, 1), :]
                inner = jnp.sum(weighted * value, -1, keepdims=True)
                out = inv * weighted - value * (inv * inv * inv) * inner / HD
                grads[rows, column] = out.astype(bf16)
        grads[rows, pl.ds(2 * local, local)] = gv[rows, :].astype(bf16)

    for copy in copies[8:]:
        copy.wait()
    span = 256
    strip = dwo.shape[2]

    @pl.loop(0, width // span)
    def _(n):
        full = pl.ds(pl.multiple_of(n * span, span), span)
        dw[full, :] = tn(normed[:, full], grads[...]).astype(bf16)
        part[:, full] = nt(grads[...], w_qkv[full, :]).astype(bf16)
        value = tn(context[...], grad_attn[:, full]).astype(bf16)
        for i in range(span // strip):
            dwo[n * (span // strip) + i] = value[:, i * strip : (i + 1) * strip]


def attention_back(grad_attn, w_o, queries, keys, values, proj, tables, gains, context, normed, w_qkv, strip):
    bf16, f32 = jnp.bfloat16, jnp.float32
    tall, width = grad_attn.shape
    local = queries.shape[1]
    vmem = pl.BlockSpec(memory_space=pltpu.VMEM)
    sources = (grad_attn, w_o, queries, keys, values, proj, tables, gains, context, normed, w_qkv)
    return pl.pallas_call(
        functools.partial(attention_back_kernel, 1.0 / math.sqrt(HD)),
        out_shape=[
            jax.ShapeDtypeStruct((tall, width), bf16),
            jax.ShapeDtypeStruct((width, 3 * local), bf16),
            jax.ShapeDtypeStruct((width // strip, local, strip), bf16),
            jax.ShapeDtypeStruct((8, HD), f32),
            jax.ShapeDtypeStruct((8, HD), f32),
        ],
        in_specs=[pl.BlockSpec(memory_space=pl.ANY)] * len(sources),
        out_specs=[vmem] * 5,
        scratch_shapes=[pltpu.VMEM(source.shape, source.dtype) for source in sources]
        + [
            pltpu.VMEM((tall, local), bf16),
            pltpu.VMEM((tall, local), f32),
            pltpu.VMEM((tall, local), f32),
            pltpu.VMEM((tall, local), f32),
            pltpu.VMEM((tall, 3 * local), bf16),
            pltpu.SemaphoreType.DMA((len(sources),)),
        ],
        compiler_params=pltpu.CompilerParams(vmem_limit_bytes=60 * 2**20),
    )(*sources)


def one_chip(
    tokens,
    w_query,
    w_key,
    w_value,
    w_out,
    gain_attn,
    gain_query,
    gain_key,
    gain_moe,
    w_router,
    w_experts,
    routes,
    cotangent,
):
    z, c, t = lax.axis_index("fsdp"), lax.axis_index("ctx"), lax.axis_index("tp")
    nz, nc = lax.axis_size("fsdp"), lax.axis_size("ctx")
    block, width = tokens.shape[1], tokens.shape[2]
    rows = block // 2
    tall = block * nc
    deep = width // nz
    ffn = w_experts.shape[3]
    most = block * TOPK * 9 // (8 * E)
    bf16, f32 = jnp.bfloat16, jnp.float32

    token_half = lax.dynamic_slice_in_dim(tokens[0], t * rows, rows, 0)
    cotan_half = lax.dynamic_slice_in_dim(cotangent[0], t * rows, rows, 0)
    local = w_query.shape[1] // nc
    small = jnp.concatenate([w_router.T.reshape(-1), gain_attn, gain_moe, gain_query, gain_key])
    total = small.shape[0]
    small = jnp.pad(small, (0, -total % 2048))
    small = small.reshape(-1, 128)
    ids = jnp.arange(E, dtype=jnp.int32)
    named = jnp.any(routes[0][:, :, None] == ids, 1)
    below = jnp.tril(jnp.ones((block, block), bf16), -1)
    rank = jnp.where(named, dot(below, named.astype(bf16)), -1.0).T
    x_rows, w_qkv, w_o, small, _, rank_seq, pick, cot_rows, pair, third, middle = load(
        tokens[0], cotangent[0], w_query, w_key, w_value, w_out, small, rank, w_experts, most
    )
    w_qkv = w_qkv.reshape(width, 3 * local)
    w_o = w_o.transpose(1, 0, 2).reshape(local, width)
    small = small.reshape(nz, -1)
    router = small[:, : E * deep].reshape(nz, E, deep).transpose(1, 0, 2).reshape(E, width)
    at = E * deep
    attn_gain = small[:, at : at + deep].reshape(-1).astype(f32)
    moe_gain = small[:, at + deep : at + 2 * deep].reshape(-1).astype(f32)
    at, part = at + 2 * deep, HD // nz
    query_gain = small[:, at : at + part].reshape(-1).astype(f32)
    key_gain = small[:, at + part : at + 2 * part].reshape(-1).astype(f32)

    pair = exchange(pair, "fsdp")

    counts = jnp.sum((rank_seq >= 0).astype(f32), 2)
    earlier = jnp.sum(jnp.where(jnp.arange(nc)[:, None] < c, counts, 0.0), 0)
    kept = ((rank >= 0) & (rank + earlier[:, None] < CAP)).astype(f32).T
    kept = lax.dynamic_slice_in_dim(kept, t * rows, rows, 0)

    half_dim = HD // 2
    inv_freq = jnp.exp(jnp.arange(half_dim, dtype=f32) * (-2.0 * math.log(ROPE_BASE) / HD))
    angles = jnp.arange(tall, dtype=jnp.int32).astype(f32)[:, None] * inv_freq[None, :]
    cosines, sines = jnp.cos(angles), jnp.sin(angles)
    tables = jnp.concatenate([cosines, cosines, sines, -sines], 1)
    gains = jnp.pad(jnp.stack([query_gain, key_gain]), ((0, 6), (0, 0)))
    normed_one, proj, queries, keys, values, context, attn_part = attention(
        x_rows, attn_gain[None], w_qkv, tables, gains, w_o
    )
    attn_part = attn_part.reshape(nc, 2, rows, width)
    kept_wide = jnp.pad(kept, ((0, 0), (0, 128 - E)))
    router_wide = jnp.pad(router, ((0, 128 - E), (0, 0)))
    residual, normed_two, router_probs, x_in, g_in, third = dispatch(
        attn_part, tokens[0], moe_gain[None], router_wide, kept_wide, pick, third, middle
    )
    pair, x_in = lax.optimization_barrier((pair, x_in))
    x_in = x_in.reshape(nc * 2 * most, width)
    cot_rows = cot_rows.reshape(nc * 2 * most, width)
    chips = nz * nc
    strip = width // chips
    out_rows, back_rows, pair_rows, hid, gg, gu = experts(
        x_in, cot_rows, g_in.reshape(nc * 2 * most, -1), pair, third
    )
    shape = (nc, 2, most, -1)
    pick_t = pick.transpose(0, 2, 1)
    grad_logits, dgain_moe, grad_residual, grad_attn, dw_gate, dw_rest = give_back(
        back_rows.reshape(shape),
        pair_rows.reshape(shape),
        x_in,
        cot_rows,
        hid,
        gg,
        gu,
        pick_t,
        residual,
        router_probs,
        kept_wide,
        router_wide,
        moe_gain[None],
        cotangent[0],
    )

    dw_router = dot_tn(normed_two, grad_logits[:, :E])
    dgain_moe = jnp.sum(dgain_moe, 0)
    dw_rest, grad_attn = lax.optimization_barrier((dw_rest, grad_attn))
    dw_rest = exchange(dw_rest, ("fsdp", "ctx"))
    grad_attn = grad_attn.reshape(tall, width)

    grad_normed_part, dw_qkv, dw_out, dgain_query, dgain_key = attention_back(
        grad_attn,
        w_o,
        queries,
        keys,
        values,
        proj,
        tables,
        gains,
        context,
        normed_one,
        w_qkv,
        strip,
    )
    dgain_query, dgain_key = jnp.sum(dgain_query, 0), jnp.sum(dgain_key, 0)
    grad_normed_part = grad_normed_part.reshape(nc, 2, rows, width)
    head_part = HD // chips
    heads = [dgain_query.reshape(chips, 1, head_part), dgain_key.reshape(chips, 1, head_part)]
    heads = jnp.pad(jnp.concatenate(heads, 2), ((0, 0), (0, 0), (0, strip - 2 * head_part)))
    sums = jnp.concatenate(
        [
            dw_router.reshape(chips, E, strip),
            dgain_moe.reshape(chips, 1, strip),
            jnp.zeros((chips, 1, strip), f32),
            heads,
            jnp.zeros((chips, 24 - E - 3, strip), f32),
        ],
        1,
    ).reshape(nz, nc, 24, strip)
    tokens_grad, dw_query, dw_key, dw_value, dw_out, sums, layer_out = finish(
        grad_normed_part,
        tokens[0],
        attn_gain[None],
        grad_residual,
        dw_qkv.reshape(nz, nc, strip, 3 * local),
        dw_out.reshape(nz, nc, local, strip),
        sums,
        out_rows.reshape(shape),
        pick_t,
        residual,
    )
    dw_experts = lay_out(dw_gate, dw_rest, nz, nc)
    return (
        layer_out[None],
        tokens_grad[None],
        dw_query,
        dw_key,
        dw_value,
        dw_out,
        sums[E + 1],
        sums[E + 2, :head_part],
        sums[E + 2, head_part : 2 * head_part],
        sums[E],
        sums[:E].reshape(strip, E),
        dw_experts,
    )


def solution(mesh):
    chips = mesh.shape["fsdp"] * mesh.shape["ctx"]
    plain = chips == E and mesh.shape["fsdp"] == 4 and mesh.shape["tp"] == 2
    return jax.shard_map(
        one_chip if plain else general,
        mesh=mesh,
        in_specs=(
            P("fsdp", "ctx", None),
            P("fsdp", "tp"),
            P("fsdp", "tp"),
            P("fsdp", "tp"),
            P("tp", "fsdp"),
            P("fsdp"),
            P("fsdp"),
            P("fsdp"),
            P("fsdp"),
            P("fsdp", None),
            P("fsdp", None, None, "tp"),
            P("fsdp", "ctx", None),
            P("fsdp", "ctx", None),
        ),
        out_specs=(
            P("fsdp", "ctx", "tp"),
            P("fsdp", "ctx", None),
            P(("fsdp", "ctx"), "tp"),
            P(("fsdp", "ctx"), "tp"),
            P(("fsdp", "ctx"), "tp"),
            P("tp", ("fsdp", "ctx")),
            P(("fsdp", "ctx")),
            P(("fsdp", "ctx")),
            P(("fsdp", "ctx")),
            P(("fsdp", "ctx")),
            P(("fsdp", "ctx"), None),
            P(("fsdp", "ctx"), None, None, "tp"),
        ),
        check_vma=False,
    )
```
